32 devices in a mesh: band: 16 (over z, y, core), head: 2 (over x).
Axes of the slice: x: 2, y: 2, z: 4, core: 2. Of those that a mesh axis runs over, the one named last changes fastest.
Arguments:
- block_input: bfloat16 [4096, 1024], P('band'), may hold values from -6 to 6
- out_grad: bfloat16 [4096, 1024], P('band'), may hold values from -6 to 6
- segments: int32 [4096], P('band'), may hold values from 0 to 31, as said below
- lead_steps: int32 [32], replicated, may hold values from 1 to 12
- gain_attn: float32 [1024], replicated, may hold values from 0.1 to 1.9
- shift_attn: float32 [1024], replicated, may hold values from -3 to 3
- lead_weight: float32 [1024], replicated, may hold values from -4 to 4
- query_weight: bfloat16 [1024, 1024], P(None, 'head'), may hold values from -0.1875 to 0.1875
- key_weight: bfloat16 [1024, 1024], P(None, 'head'), may hold values from -0.1875 to 0.1875
- value_weight: bfloat16 [1024, 1024], P(None, 'head'), may hold values from -0.1875 to 0.1875
- output_weight: bfloat16 [1024, 1024], P('head'), may hold values from -0.75 to 0.75
- output_bias: float32 [1024], replicated, may hold values from -3 to 3
- gain_mlp: float32 [1024], replicated, may hold values from 0.1 to 1.9
- shift_mlp: float32 [1024], replicated, may hold values from -3 to 3
- up_weight: bfloat16 [1024, 4096], P(None, 'head'), may hold values from -0.1875 to 0.1875
- up_bias: float32 [4096], P('head'), may hold values from -3 to 3
- down_weight: bfloat16 [4096, 1024], P('head'), may hold values from -0.09375 to 0.09375
- down_bias: float32 [1024], replicated, may hold values from -3 to 3
Outputs:
- block_output: bfloat16 [4096, 1024], P('band')
- input_grad: bfloat16 [4096, 1024], P('band')
- dgain_attn: float32 [1024], replicated
- dshift_attn: float32 [1024], replicated
- dlead_weight: float32 [1024], replicated
- dquery_weight: float32 [1024, 1024], P(None, 'head')
- dkey_weight: float32 [1024, 1024], P(None, 'head')
- dvalue_weight: float32 [1024, 1024], P(None, 'head')
- doutput_weight: float32 [1024, 1024], P('head')
- doutput_bias: float32 [1024], replicated
- dgain_mlp: float32 [1024], replicated
- dshift_mlp: float32 [1024], replicated
- dup_weight: float32 [1024, 4096], P(None, 'head')
- dup_bias: float32 [4096], P('head')
- ddown_weight: float32 [4096, 1024], P('head')
- ddown_bias: float32 [1024], replicated
The draws below stay inside these ranges and needn't reach their ends.
Inputs may be any that keep to these rules, and one draw needn't show every extreme that they name: `segments`: the patches of one crop lie in a run of consecutive latitude bands of 256 patches each; at least one crop covers every band; every crop number occurs.
All inputs are finite; a program needn't handle non-finite values.
Results may differ from the reference program's by a relative error of at most 0.025.
Values may be sent and summed in bfloat16 or wider, within the bound.
No kernel may reach another device: no remote copies, remote signals or barrier semaphores. Data moves between devices by JAX's collectives and lax.ppermute only.
A program may use at most 128 MiB of HBM per device.

```python
import math
import jax
import jax.numpy as jnp
from jax import lax

D = 1024
HEADS = 16
HD = 64
FF = 4096
TOK_DEV = 256
CROPS = 32
SEQ = 4096


def draw_segments(key, part):
    key = jax.random.fold_in(key, 11)
    key_span, key_low, key_whole, key_pick, key_long, key_wide = jax.random.split(key, 6)
    bands = SEQ // TOK_DEV
    reach = max(bands // 4, 1)
    wide_low = max(bands // 2, 1)
    wide_high = max(bands, wide_low + 1)
    crop = jnp.arange(CROPS, dtype=jnp.int32)
    short_span = jax.random.randint(key_span, (CROPS,), 1, reach + 1)
    wide_span = jax.random.randint(key_wide, (CROPS,), wide_low, wide_high)
    whole = jax.random.randint(key_whole, (), 0, CROPS)
    forced = (whole + 1) % CROPS
    is_wide = (jax.random.randint(key_long, (CROPS,), 0, 4) == 0) | (crop == forced)
    span = jnp.where(is_wide, wide_span, short_span)
    lowest = jax.random.randint(key_low, (CROPS,), 0, 1 << 20) % (bands - span + 1)
    span = jnp.where(crop == whole, bands, span)
    lowest = jnp.where(crop == whole, 0, lowest)
    band_of = jnp.arange(SEQ, dtype=jnp.int32) // TOK_DEV
    covers = (band_of[:, None] >= lowest[None, :]) & (band_of[:, None] < lowest[None, :] + span[None, :])
    scores = jax.random.randint(key_pick, (SEQ, CROPS), 0, 1 << 16) * CROPS + crop[None, :]
    scores = jnp.where(covers, scores, -1)
    chosen = jnp.argmax(scores, axis=1).astype(jnp.int32)
    places = lowest * TOK_DEV + crop
    return chosen.at[places].set(crop)


def plant(entries, rng, low, high):
    spot = [jax.random.randint(jax.random.fold_in(rng, axis), (), 0, length) for axis, length in enumerate(entries.shape)]
    widest = entries.shape.index(max(entries.shape))
    neighbour = spot[:widest] + [(spot[widest] + 1) % entries.shape[widest]] + spot[widest + 1:]
    return entries.at[tuple(spot)].set(low).at[tuple(neighbour)].set(high)


def block_scale(stream_key, shape, pieces, smallest, top_value):
    level, own = 1.0, jax.random.fold_in(stream_key, 6)
    for axis_at, shards_of in pieces:
        draws = jnp.exp(jax.random.uniform(jax.random.fold_in(own, axis_at), (shards_of,), jnp.float32, smallest / len(pieces), top_value / len(pieces)))
        level = level * jnp.repeat(draws, shape[axis_at] // shards_of).reshape([-1 if axis == axis_at else 1 for axis in range(len(shape))])
    return level


def scatter_about(stream_key, extent, deviation, bound, cuts=(), kind=jnp.bfloat16):
    values = jax.random.normal(stream_key, extent, jnp.float32) * deviation
    if len(cuts) > 0:
        values = block_scale(stream_key, extent, cuts, -0.22, 0.18) * values
    return jnp.clip(values, min=-bound, max=bound).astype(kind)


def setup_inputs(seed: int = 0) -> dict:
    key_list = jax.random.split(jax.random.key(seed), 19)
    block_input = scatter_about(key_list[0], (SEQ, D), 1.0, 6.0, ((0, 16),))
    out_grad = scatter_about(key_list[1], (SEQ, D), 1.0, 6.0, ((0, 16),))
    segments = draw_segments(jax.random.fold_in(key_list[18], 71), 0)
    lead_steps = plant(jax.random.randint(key_list[3], (CROPS,), 1, 13), jax.random.fold_in(key_list[3], 1), 1, 12).astype(jnp.int32)
    gain_attn = jnp.clip(1.0 + 0.18 * jax.random.normal(key_list[4], (D,), jnp.float32), 0.1, 1.9)
    shift_attn = scatter_about(key_list[5], (D,), 0.5, 3.0, (), jnp.float32)
    lead_weight = scatter_about(key_list[6], (D,), 1.0, 4.0, (), jnp.float32)
    query_weight = scatter_about(key_list[7], (D, D), D ** -0.5, 0.1875, ((1, 2),))
    key_weight = scatter_about(key_list[8], (D, D), D ** -0.5, 0.1875, ((1, 2),))
    value_weight = scatter_about(key_list[9], (D, D), D ** -0.5, 0.1875, ((1, 2),))
    output_weight = scatter_about(key_list[10], (D, D), (D // 16) ** -0.5, 0.75, ((0, 2),))
    output_bias = scatter_about(key_list[11], (D,), 0.5, 3.0, (), jnp.float32)
    gain_mlp = jnp.clip(1.0 + 0.18 * jax.random.normal(key_list[12], (D,), jnp.float32), 0.1, 1.9)
    shift_mlp = scatter_about(key_list[13], (D,), 0.5, 3.0, (), jnp.float32)
    up_weight = scatter_about(key_list[14], (D, FF), D ** -0.5, 0.1875, ((1, 2),))
    up_bias = scatter_about(key_list[15], (FF,), 0.5, 3.0, ((0, 2),), jnp.float32)
    down_weight = scatter_about(key_list[16], (FF, D), FF ** -0.5, 0.09375, ((0, 2),))
    down_bias = scatter_about(key_list[17], (D,), 0.5, 3.0, (), jnp.float32)
    return dict(block_input=block_input, out_grad=out_grad, segments=segments, lead_steps=lead_steps, gain_attn=gain_attn, shift_attn=shift_attn, lead_weight=lead_weight, query_weight=query_weight, key_weight=key_weight, value_weight=value_weight, output_weight=output_weight, output_bias=output_bias, gain_mlp=gain_mlp, shift_mlp=shift_mlp, up_weight=up_weight, up_bias=up_bias, down_weight=down_weight, down_bias=down_bias)


eps = 1e-05
masked_value = -1e+30
highest = lax.Precision.HIGHEST

@jax.custom_vjp
def low(v):
    return lax.optimization_barrier(v.astype(jnp.bfloat16)).astype(jnp.float32)

@jax.custom_vjp
def low_back(v):
    return v

def low_keep(v):
    return (low(v), None)

def low_pass(kept, grad):
    return (grad,)

def back_keep(v):
    return (v, None)

def back_low(kept, grad):
    return (low(grad),)
low.defvjp(low_keep, low_pass)
low_back.defvjp(back_keep, back_low)

def product(first, second):
    return jnp.dot(first, second, precision=highest)

def layer_norm(values, gain, shift):
    centred = values - lax.optimization_barrier(jnp.mean(values, axis=-1, keepdims=True))
    spread = lax.optimization_barrier(jnp.mean(centred * centred, axis=-1, keepdims=True))
    return centred * lax.rsqrt(spread + eps) * gain + shift

def exact_gelu(values):
    return jax.nn.gelu(values, approximate=False)

def forward_pass(segments, lead, block_input, gain_attn, shift_attn, lead_weight, query_weight, key_weight, value_weight, output_weight, output_bias, gain_mlp, shift_mlp, up_weight, up_bias, down_weight, down_bias):
    attn_in = low(layer_norm(block_input, gain_attn, shift_attn) + lead[:, None] * lead_weight[None, :])
    query = low(low_back(product(attn_in, query_weight)))
    keys = low(low_back(product(attn_in, key_weight)))
    values = low(low_back(product(attn_in, value_weight)))
    keys3 = keys.reshape(SEQ, HEADS, HD)
    values3 = values.reshape(SEQ, HEADS, HD)
    stride = math.gcd(SEQ, 256)
    query_blocks = query.reshape(SEQ // stride, stride, HEADS, HD)
    seg_blocks = segments.reshape(SEQ // stride, stride)

    def attend(block):
        query_block, seg_block = block
        scores = jnp.einsum('qhd,khd->hqk', query_block, keys3, precision=highest) * 0.125
        scores = low_back(scores)
        allowed = (seg_block[:, None] == segments[None, :])[None, :, :]
        masked = jnp.where(allowed, scores, masked_value)
        top = lax.optimization_barrier(jnp.max(masked, axis=-1, keepdims=True))
        weights = jnp.where(allowed, jnp.exp(masked - top), 0.0)
        probs = low(weights / lax.optimization_barrier(jnp.sum(weights, axis=-1, keepdims=True)))
        return jnp.einsum('hqk,khd->qhd', probs, values3, precision=highest)
    attn_raw = lax.map(jax.checkpoint(attend), (query_blocks, seg_blocks)).reshape(SEQ, D)
    attn_out = low(low_back(attn_raw))
    hidden = block_input + low_back(product(attn_out, output_weight)) + output_bias
    mlp_in = low(layer_norm(hidden, gain_mlp, shift_mlp))
    upper = low_back(product(mlp_in, up_weight) + up_bias)
    active = low(exact_gelu(upper))
    return hidden + low_back(product(active, down_weight)) + down_bias

def reference(block_input, out_grad, segments, lead_steps, gain_attn, shift_attn, lead_weight, query_weight, key_weight, value_weight, output_weight, output_bias, gain_mlp, shift_mlp, up_weight, up_bias, down_weight, down_bias):
    lead = lead_steps.astype(jnp.float32)[segments] / 12.0
    params = (block_input.astype(jnp.float32), gain_attn, shift_attn, lead_weight, query_weight.astype(jnp.float32), key_weight.astype(jnp.float32), value_weight.astype(jnp.float32), output_weight.astype(jnp.float32), output_bias, gain_mlp, shift_mlp, up_weight.astype(jnp.float32), up_bias, down_weight.astype(jnp.float32), down_bias)

    def closed(*inputs):
        return forward_pass(segments, lead, *inputs)
    output, pullback = jax.vjp(closed, *params)
    grads = pullback(out_grad.astype(jnp.float32))
    return (output.astype(jnp.bfloat16), grads[0].astype(jnp.bfloat16), grads[1], grads[2], grads[3], grads[4], grads[5], grads[6], grads[7], grads[8], grads[9], grads[10], grads[11], grads[12], grads[13], grads[14])
```

```python
import functools

import jax
import jax.numpy as jnp
from jax import lax
from jax.experimental import pallas as pl
from jax.experimental.pallas import tpu as pltpu
from jax.sharding import Mesh, PartitionSpec as P

HD = 64
F32 = jnp.float32
BF16 = jnp.bfloat16
eps = 1e-05
masked_value = -1e30
seg_row = 3 * HD
payload_rows = 3 * HD + 16
vmem_limit = 48 * 2**20


def normalize(values):
    centred = values - jnp.mean(values, axis=-1, keepdims=True)
    inverse = lax.rsqrt(jnp.mean(centred * centred, axis=-1, keepdims=True) + eps)
    return (centred * inverse, inverse)


def normalize_back(grad_unit, unit, inverse):
    return inverse * (
        grad_unit
        - jnp.mean(grad_unit, axis=-1, keepdims=True)
        - unit * jnp.mean(grad_unit * unit, axis=-1, keepdims=True)
    )


def product(first, second, first_axis=1, second_axis=0):
    return lax.dot_general(
        first,
        second,
        (((first_axis,), (second_axis,)), ((), ())),
        preferred_element_type=jnp.float32,
    )


def exact_gelu(values):
    return jax.nn.gelu(values, approximate=False)


def load_keys(pieces, crops, keys, key_t, value_t, value_n):
    start = 0
    for piece in pieces:
        chips, _, patches = piece.shape
        for chip in range(chips):
            crop = lax.broadcasted_iota(jnp.int32, (HD, patches), 0)
            segment = piece[chip, pl.ds(seg_row, 16), :].astype(F32)[:1].astype(jnp.int32)
            mask = jnp.where((crop != segment) & (crop < crops), masked_value, 0.0)
            key = piece[chip, pl.ds(HD, HD), :]
            value = piece[chip, pl.ds(2 * HD, HD), :]
            place = pl.ds(start, patches)
            keys[place, :] = jnp.concatenate([key.astype(F32), mask], axis=0).T.astype(BF16)
            if key_t is not None:
                key_t[:, place] = key
            if value_t is not None:
                value_t[pl.ds(0, HD), place] = value
                value_t[pl.ds(HD, 16), place] = jnp.ones((16, patches), BF16)
            if value_n is not None:
                value_n[place, :] = value.astype(F32).T.astype(BF16)
            start += patches


def masked_query(query_ref):
    query = query_ref[0, pl.ds(0, HD), :].astype(F32) * 0.125
    segment = query_ref[0, pl.ds(seg_row, 16), :].astype(F32)[:1].astype(jnp.int32)
    crop = lax.broadcasted_iota(jnp.int32, query.shape, 0)
    onehot = jnp.where(crop == segment, 1.0, 0.0)
    return jnp.concatenate([query, onehot], axis=0).astype(BF16)


def forward_kernel(crops, step, query_ref, own, other, raw_ref, out_ref, logsum_ref, keys, value_t):
    @pl.when(pl.program_id(0) == 0)
    def _():
        load_keys((own, other), crops, keys, None, value_t, None)

    query = masked_query(query_ref)
    count = query.shape[1]
    top = jnp.full((1, count), masked_value, F32)
    accum = jnp.zeros((HD + 16, count), F32)
    for start in range(0, keys.shape[0], step):
        scores = product(keys[pl.ds(start, step), :], query)
        new_top = jnp.maximum(top, jnp.max(scores, axis=0, keepdims=True))
        weights = jnp.exp(scores - new_top).astype(BF16)
        accum = accum * jnp.exp(top - new_top) + product(value_t[:, pl.ds(start, step)], weights)
        top = new_top
    total = accum[HD : HD + 1]
    raw = accum[:HD] / total
    raw_ref[0] = raw
    out_ref[0] = raw.astype(BF16)
    logsum_ref[0] = top + jnp.log(total)


def backward_kernel(
    crops,
    step,
    query_ref,
    grad_ref,
    raw_ref,
    logsum_ref,
    own,
    other,
    dquery_ref,
    own_ref,
    other_ref,
    keys,
    key_t,
    value_n,
    sums,
):
    group = pl.program_id(0)

    @pl.when(group == 0)
    def _():
        load_keys((own, other), crops, keys, key_t, None, value_n)
        sums[...] = jnp.zeros_like(sums)

    query = masked_query(query_ref)
    grad = grad_ref[0]
    grad_wide = grad.astype(F32)
    delta = jnp.sum(grad_wide * raw_ref[0], axis=0, keepdims=True)
    logsum = logsum_ref[0]
    scaled = query_ref[0, pl.ds(0, HD), :].astype(F32) * 0.125
    zero = jnp.zeros_like(scaled)
    query_side = jnp.concatenate([scaled, zero], axis=0).T.astype(BF16)
    grad_side = jnp.concatenate([zero, grad_wide], axis=0).T.astype(BF16)
    dquery = jnp.zeros_like(scaled)
    for start in range(0, keys.shape[0], step):
        place = pl.ds(start, step)
        probs = jnp.exp(product(keys[place, :], query) - logsum)
        dprobs = product(value_n[place, :], grad)
        dscores = (probs * (dprobs - delta)).astype(BF16)
        sums[place, :] += product(dscores, query_side) + product(probs.astype(BF16), grad_side)
        dquery += product(key_t[:, place], dscores)
    dquery_ref[0] = (dquery * 0.125).astype(BF16)

    @pl.when(group == pl.num_programs(0) - 1)
    def _():
        start = 0
        for target in (own_ref, other_ref):
            chips, _, patches = target.shape
            for chip in range(chips):
                target[chip] = sums[pl.ds(start, patches), :].T.astype(target.dtype)
                start += patches


def key_step(count):
    return 1024 if count % 1024 == 0 else 256


def query_spec(rows, patches):
    return pl.BlockSpec((1, rows, patches), lambda group: (group, 0, 0))


def whole_spec(shape):
    return pl.BlockSpec(shape, lambda group: (0,) * len(shape))


def attention_forward(queries, own, other, crops):
    groups, _, patches = queries.shape
    count = 2 * own.shape[0] * own.shape[2]
    return pl.pallas_call(
        functools.partial(forward_kernel, crops, key_step(count)),
        grid=(groups,),
        in_specs=[
            query_spec(payload_rows, patches),
            whole_spec(own.shape),
            whole_spec(other.shape),
        ],
        out_specs=[query_spec(HD, patches), query_spec(HD, patches), query_spec(1, patches)],
        out_shape=[
            jax.ShapeDtypeStruct((groups, HD, patches), F32),
            jax.ShapeDtypeStruct((groups, HD, patches), BF16),
            jax.ShapeDtypeStruct((groups, 1, patches), F32),
        ],
        scratch_shapes=[pltpu.VMEM((count, 2 * HD), BF16), pltpu.VMEM((HD + 16, count), BF16)],
        compiler_params=pltpu.CompilerParams(vmem_limit_bytes=vmem_limit),
        name="attention_forward",
    )(queries, own, other)


def attention_backward(queries, grads, raw, logsum, own, other, crops):
    groups, _, patches = queries.shape
    count = 2 * own.shape[0] * own.shape[2]
    sums_shape = (own.shape[0], 2 * HD, own.shape[2])
    return pl.pallas_call(
        functools.partial(backward_kernel, crops, key_step(count)),
        grid=(groups,),
        in_specs=[
            query_spec(payload_rows, patches),
            query_spec(HD, patches),
            query_spec(HD, patches),
            query_spec(1, patches),
            whole_spec(own.shape),
            whole_spec(other.shape),
        ],
        out_specs=[query_spec(HD, patches), whole_spec(sums_shape), whole_spec(sums_shape)],
        out_shape=[
            jax.ShapeDtypeStruct((groups, HD, patches), BF16),
            jax.ShapeDtypeStruct(sums_shape, F32),
            jax.ShapeDtypeStruct(sums_shape, BF16),
        ],
        scratch_shapes=[
            pltpu.VMEM((count, 2 * HD), BF16),
            pltpu.VMEM((HD, count), BF16),
            pltpu.VMEM((count, HD), BF16),
            pltpu.VMEM((count, 2 * HD), F32),
        ],
        compiler_params=pltpu.CompilerParams(vmem_limit_bytes=vmem_limit),
        name="attention_backward",
    )(queries, grads, raw, logsum, own, other)


def swap_cores(values):
    return lax.ppermute(values, "core", [(0, 1), (1, 0)])


def to_heads(blocks):
    return lax.all_to_all(blocks, "chip", 0, 0, tiled=True)


def scatter_queries(values, heads, split):
    rows, patches = values.shape[0] // heads, values.shape[1]
    if split == 1:
        return to_heads(values.reshape(heads, rows, patches))
    part = patches // split
    blocks = values.reshape(heads, rows, split, part).transpose(0, 2, 1, 3)
    moved = to_heads(blocks.reshape(heads * split, rows, part))
    width = min(256, moved.shape[0] * part)
    joined = moved.transpose(1, 0, 2).reshape(rows, -1, width)
    return joined.transpose(1, 0, 2)


def gather_queries(values, heads, split, patches):
    rows = values.shape[1]
    if split == 1:
        return to_heads(values).reshape(heads * rows, patches)
    part = patches // split
    joined = values.transpose(1, 0, 2).reshape(rows, heads * split, part)
    moved = to_heads(joined.transpose(1, 0, 2)).reshape(heads, split, rows, part)
    return moved.transpose(0, 2, 1, 3).reshape(heads * rows, patches)


def head_sum(values):
    low = values.astype(BF16)
    if lax.axis_size("head") == 2:
        return low.astype(F32) + lax.ppermute(low, "head", [(0, 1), (1, 0)]).astype(F32)
    return lax.psum(low, "head").astype(F32)


def band_sum(values):
    values = values + swap_cores(values)
    chips, reach = lax.axis_size("chip"), 1
    while reach < chips:
        pairs = [(chip, chip ^ reach) for chip in range(chips)]
        values = values + lax.ppermute(values, "chip", pairs)
        reach *= 2
    return values


def local(
    block_input,
    out_grad,
    segments,
    lead_steps,
    gain_attn,
    shift_attn,
    lead_weight,
    query_weight,
    key_weight,
    value_weight,
    output_weight,
    output_bias,
    gain_mlp,
    shift_mlp,
    up_weight,
    up_bias,
    down_weight,
    down_bias,
):
    rows = block_input.shape[0]
    heads = query_weight.shape[1] // HD
    width = heads * HD
    chips = lax.axis_size("chip")
    split = chips // heads
    crops = lead_steps.shape[0]
    inputs = block_input.astype(F32)
    unit_attn, inverse_attn = normalize(inputs)
    onehot = (segments[:, None] == jnp.arange(crops, dtype=jnp.int32)[None, :]).astype(F32)
    lead = jnp.sum(onehot * lead_steps.astype(F32)[None, :], axis=1) / 12.0
    attn_in = (unit_attn * gain_attn + shift_attn + lead[:, None] * lead_weight).astype(BF16)
    query, key, value = (
        product(weight, attn_in, 0, 1).astype(BF16).reshape(heads, HD, rows)
        for weight in (query_weight, key_weight, value_weight)
    )
    crop_rows = jnp.broadcast_to(segments.astype(BF16), (heads, 16, rows))
    payload = jnp.concatenate([query, key, value, crop_rows], axis=1)
    if split == 1:
        own = to_heads(payload)
        queries = own
    else:
        queries = scatter_queries(payload.reshape(-1, rows), heads, split)
        own = to_heads(jnp.repeat(payload, split, axis=0))
    other = swap_cores(own)
    raw, out, logsum = attention_forward(queries, own, other, crops)
    attn_out = gather_queries(out, heads, split, rows)
    branch = head_sum(product(attn_out, output_weight, 0, 0))
    hidden = inputs + branch + output_bias
    unit_mlp, inverse_mlp = normalize(hidden)
    mlp_in = (unit_mlp * gain_mlp + shift_mlp).astype(BF16)
    upper = product(mlp_in, up_weight) + up_bias
    active, gelu_back = jax.vjp(exact_gelu, upper)
    active_low = active.astype(BF16)
    d_active = product(out_grad, down_weight, 1, 1)
    d_upper = gelu_back(d_active)[0].astype(BF16)
    d_mlp = head_sum(product(d_upper, up_weight, 1, 1))
    mlp_out = head_sum(product(active_low, down_weight))
    block_output = (hidden + mlp_out + down_bias).astype(BF16)
    grad_out = out_grad.astype(F32)
    ddown_weight = product(active_low, out_grad, 0, 0)
    dup_weight = product(mlp_in, d_upper, 0, 0)
    d_hidden = grad_out + normalize_back(d_mlp * gain_mlp, unit_mlp, inverse_mlp)
    d_branch = d_hidden.astype(BF16)
    doutput_weight = product(attn_out, d_branch)
    d_attn = product(output_weight, d_branch, 1, 1).astype(BF16)
    grads = scatter_queries(d_attn, heads, split)
    dquery, own_sums, other_sums = attention_backward(
        queries, grads, raw, logsum, own, other, crops
    )
    key_value = (own_sums + swap_cores(other_sums).astype(F32)).astype(BF16)
    if split == 1:
        moved = to_heads(jnp.concatenate([dquery, key_value], axis=1))
        dquery, dkey, dvalue = (
            moved[:, at * HD : at * HD + HD].reshape(width, rows) for at in range(3)
        )
    else:
        dquery = gather_queries(dquery, heads, split, rows)
        moved = to_heads(key_value).reshape(heads, split, 2 * HD, rows).astype(F32)
        moved = jnp.sum(moved, axis=1).astype(BF16)
        dkey, dvalue = (moved[:, at * HD : at * HD + HD].reshape(width, rows) for at in range(2))
    dquery_weight, dkey_weight, dvalue_weight = (
        product(attn_in, grad, 0, 1) for grad in (dquery, dkey, dvalue)
    )
    d_in = head_sum(
        product(dquery, query_weight, 0, 1)
        + product(dkey, key_weight, 0, 1)
        + product(dvalue, value_weight, 0, 1)
    )
    input_grad = (d_hidden + normalize_back(d_in * gain_attn, unit_attn, inverse_attn)).astype(
        BF16
    )
    small = band_sum(
        jnp.stack(
            [
                jnp.sum(d_in * unit_attn, axis=0),
                jnp.sum(d_in, axis=0),
                jnp.sum(lead[:, None] * d_in, axis=0),
                jnp.sum(d_hidden, axis=0),
                jnp.sum(d_mlp * unit_mlp, axis=0),
                jnp.sum(d_mlp, axis=0),
                jnp.sum(grad_out, axis=0),
            ]
        )
    )
    dup_bias = band_sum(jnp.sum(d_upper.astype(F32), axis=0))
    large = [
        lax.psum(grad.astype(BF16), ("chip", "core")).astype(F32)
        for grad in (
            dquery_weight,
            dkey_weight,
            dvalue_weight,
            doutput_weight,
            dup_weight,
            ddown_weight,
        )
    ]
    return (
        block_output,
        input_grad,
        small[0],
        small[1],
        small[2],
        large[0],
        large[1],
        large[2],
        large[3],
        small[3],
        small[4],
        small[5],
        large[4],
        dup_bias,
        large[5],
        small[6],
    )


def solution(mesh):
    bands, halves = mesh.shape["band"], mesh.shape["head"]
    inner = Mesh(mesh.devices.reshape(bands // 2, 2, halves), ("chip", "core", "head"))
    band = ("chip", "core")
    rows, columns, split_rows = P(band, None), P(None, "head"), P("head", None)
    return jax.shard_map(
        local,
        mesh=inner,
        in_specs=(
            rows,
            rows,
            P(band),
            P(),
            P(),
            P(),
            P(),
            columns,
            columns,
            columns,
            split_rows,
            P(),
            P(),
            P(),
            columns,
            P("head"),
            split_rows,
            P(),
        ),
        out_specs=(
            rows,
            rows,
            P(),
            P(),
            P(),
            columns,
            columns,
            columns,
            split_rows,
            P(),
            P(),
            P(),
            columns,
            P("head"),
            split_rows,
            P(),
        ),
        check_vma=False,
    )
```

```python
import functools

import jax
import jax.numpy as jnp
from jax import lax
from jax.experimental import pallas as pl
from jax.experimental.pallas import tpu as pltpu
from jax.sharding import Mesh, PartitionSpec as P

HD = 64
F32 = jnp.float32
BF16 = jnp.bfloat16
eps = 1e-05
masked_value = -1e30
seg_row = 3 * HD
payload_rows = 3 * HD + 16
vmem_limit = 48 * 2**20


def normalize(values):
    centred = values - jnp.mean(values, axis=-1, keepdims=True)
    inverse = lax.rsqrt(jnp.mean(centred * centred, axis=-1, keepdims=True) + eps)
    return (centred * inverse, inverse)


def normalize_back(grad_unit, unit, inverse):
    return inverse * (
        grad_unit
        - jnp.mean(grad_unit, axis=-1, keepdims=True)
        - unit * jnp.mean(grad_unit * unit, axis=-1, keepdims=True)
    )


def product(first, second, first_axis=1, second_axis=0):
    return lax.dot_general(
        first,
        second,
        (((first_axis,), (second_axis,)), ((), ())),
        preferred_element_type=jnp.float32,
    )


def exact_gelu(values):
    return jax.nn.gelu(values, approximate=False)


def load_keys(pieces, crops, keys, key_t, value_t, value_n):
    start = 0
    for piece in pieces:
        chips, _, patches = piece.shape
        for chip in range(chips):
            crop = lax.broadcasted_iota(jnp.int32, (HD, patches), 0)
            segment = piece[chip, pl.ds(seg_row, 16), :].astype(F32)[:1].astype(jnp.int32)
            mask = jnp.where((crop != segment) & (crop < crops), masked_value, 0.0)
            key = piece[chip, pl.ds(HD, HD), :]
            value = piece[chip, pl.ds(2 * HD, HD), :]
            place = pl.ds(start, patches)
            keys[place, :] = jnp.concatenate([key.astype(F32), mask], axis=0).T.astype(BF16)
            if key_t is not None:
                key_t[:, place] = key
            if value_t is not None:
                value_t[pl.ds(0, HD), place] = value
                value_t[pl.ds(HD, 16), place] = jnp.ones((16, patches), BF16)
            if value_n is not None:
                value_n[place, :] = value.astype(F32).T.astype(BF16)
            start += patches


def masked_query(query_ref):
    query = query_ref[0, pl.ds(0, HD), :].astype(F32) * 0.125
    segment = query_ref[0, pl.ds(seg_row, 16), :].astype(F32)[:1].astype(jnp.int32)
    crop = lax.broadcasted_iota(jnp.int32, query.shape, 0)
    onehot = jnp.where(crop == segment, 1.0, 0.0)
    return jnp.concatenate([query, onehot], axis=0).astype(BF16)


def forward_kernel(crops, step, query_ref, own, other, raw_ref, out_ref, logsum_ref, keys, value_t):
    @pl.when(pl.program_id(0) == 0)
    def _():
        load_keys((own, other), crops, keys, None, value_t, None)

    query = masked_query(query_ref)
    count = query.shape[1]
    top = jnp.full((1, count), masked_value, F32)
    accum = jnp.zeros((HD + 16, count), F32)
    for start in range(0, keys.shape[0], step):
        scores = product(keys[pl.ds(start, step), :], query)
        new_top = jnp.maximum(top, jnp.max(scores, axis=0, keepdims=True))
        weights = jnp.exp(scores - new_top).astype(BF16)
        accum = accum * jnp.exp(top - new_top) + product(value_t[:, pl.ds(start, step)], weights)
        top = new_top
    total = accum[HD : HD + 1]
    raw = accum[:HD] / total
    raw_ref[0] = raw
    out_ref[0] = raw.astype(BF16)
    logsum_ref[0] = top + jnp.log(total)


def backward_kernel(
    crops,
    query_ref,
    grad_ref,
    raw_ref,
    logsum_ref,
    before_ref,
    piece,
    dquery_ref,
    sums_ref,
    keys,
    key_t,
    value_n,
    sums,
):
    group = pl.program_id(0)

    @pl.when(group == 0)
    def _():
        load_keys((piece,), crops, keys, key_t, None, value_n)
        sums[...] = jnp.zeros_like(sums)

    query = masked_query(query_ref)
    grad = grad_ref[0]
    grad_wide = grad.astype(F32)
    delta = jnp.sum(grad_wide * raw_ref[0], axis=0, keepdims=True)
    scaled = query_ref[0, pl.ds(0, HD), :].astype(F32) * 0.125
    zero = jnp.zeros_like(scaled)
    query_side = jnp.concatenate([scaled, zero], axis=0).T.astype(BF16)
    grad_side = jnp.concatenate([zero, grad_wide], axis=0).T.astype(BF16)
    probs = jnp.exp(product(keys[...], query) - logsum_ref[0])
    dprobs = product(value_n[...], grad)
    dscores = (probs * (dprobs - delta)).astype(BF16)
    sums[...] += product(dscores, query_side) + product(probs.astype(BF16), grad_side)
    dquery = product(key_t[...], dscores) * 0.125
    if before_ref is not None:
        dquery = before_ref[0] + dquery
    dquery_ref[0] = dquery.astype(dquery_ref.dtype)

    @pl.when(group == pl.num_programs(0) - 1)
    def _():
        chips, _, patches = sums_ref.shape
        for chip in range(chips):
            sums_ref[chip] = sums[pl.ds(chip * patches, patches), :].T.astype(sums_ref.dtype)


def key_step(count):
    return 1024 if count % 1024 == 0 else 256


def query_spec(rows, patches):
    return pl.BlockSpec((1, rows, patches), lambda group: (group, 0, 0))


def whole_spec(shape):
    return pl.BlockSpec(shape, lambda group: (0,) * len(shape))


def attention_forward(queries, own, other, crops):
    groups, _, patches = queries.shape
    count = 2 * own.shape[0] * own.shape[2]
    return pl.pallas_call(
        functools.partial(forward_kernel, crops, key_step(count)),
        grid=(groups,),
        in_specs=[
            query_spec(payload_rows, patches),
            whole_spec(own.shape),
            whole_spec(other.shape),
        ],
        out_specs=[query_spec(HD, patches), query_spec(HD, patches), query_spec(1, patches)],
        out_shape=[
            jax.ShapeDtypeStruct((groups, HD, patches), F32),
            jax.ShapeDtypeStruct((groups, HD, patches), BF16),
            jax.ShapeDtypeStruct((groups, 1, patches), F32),
        ],
        scratch_shapes=[pltpu.VMEM((count, 2 * HD), BF16), pltpu.VMEM((HD + 16, count), BF16)],
        compiler_params=pltpu.CompilerParams(vmem_limit_bytes=vmem_limit),
        cost_estimate=pl.CostEstimate(
            flops=groups * patches * count * 2 * 1024,
            bytes_accessed=4 * 2**20,
            transcendentals=groups * patches * count,
        ),
        name="attention_forward",
    )(queries, own, other)


def backward_piece(queries, grads, raw, logsum, before, keys, index, pieces, crops, sums_type, last):
    groups, _, patches = queries.shape
    chips = keys.shape[0] // pieces
    count = chips * keys.shape[2]
    sums_shape = (chips, 2 * HD, keys.shape[2])
    earlier = [] if before is None else [before]
    body = functools.partial(backward_kernel, crops)
    if before is None:
        body = lambda *refs: backward_kernel(crops, *refs[:4], None, *refs[4:])
    return pl.pallas_call(
        body,
        grid=(groups,),
        in_specs=[
            query_spec(payload_rows, patches),
            query_spec(HD, patches),
            query_spec(HD, patches),
            query_spec(1, patches),
        ]
        + [query_spec(HD, patches)] * len(earlier)
        + [pl.BlockSpec((chips,) + keys.shape[1:], lambda group: (index, 0, 0))],
        out_specs=[query_spec(HD, patches), whole_spec(sums_shape)],
        out_shape=[
            jax.ShapeDtypeStruct((groups, HD, patches), BF16 if last else F32),
            jax.ShapeDtypeStruct(sums_shape, sums_type),
        ],
        scratch_shapes=[
            pltpu.VMEM((count, 2 * HD), BF16),
            pltpu.VMEM((HD, count), BF16),
            pltpu.VMEM((count, HD), BF16),
            pltpu.VMEM((count, 2 * HD), F32),
        ],
        compiler_params=pltpu.CompilerParams(vmem_limit_bytes=vmem_limit),
        cost_estimate=pl.CostEstimate(
            flops=groups * patches * count * 2 * 2048,
            bytes_accessed=4 * 2**20,
            transcendentals=groups * patches * count,
        ),
        name="attention_backward",
    )(queries, grads, raw, logsum, *earlier, keys)


def swap_cores(values):
    return lax.ppermute(values, "core", [(0, 1), (1, 0)])


def to_heads(blocks):
    return lax.all_to_all(blocks, "chip", 0, 0, tiled=True)


def scatter_queries(values, heads, split):
    rows, patches = values.shape[0] // heads, values.shape[1]
    if split == 1:
        return to_heads(values.reshape(heads, rows, patches))
    part = patches // split
    blocks = values.reshape(heads, rows, split, part).transpose(0, 2, 1, 3)
    moved = to_heads(blocks.reshape(heads * split, rows, part))
    width = min(256, moved.shape[0] * part)
    joined = moved.transpose(1, 0, 2).reshape(rows, -1, width)
    return joined.transpose(1, 0, 2)


def gather_queries(values, heads, split, patches):
    rows = values.shape[1]
    if split == 1:
        return to_heads(values).reshape(heads * rows, patches)
    part = patches // split
    joined = values.transpose(1, 0, 2).reshape(rows, heads * split, part)
    moved = to_heads(joined.transpose(1, 0, 2)).reshape(heads, split, rows, part)
    return moved.transpose(0, 2, 1, 3).reshape(heads * rows, patches)


def ring_position():
    chips, chip = lax.axis_size("chip"), lax.axis_index("chip")
    return jnp.where(chip % 2 == 0, chip // 2, chips - 1 - chip // 2)


def ring_pairs(direction):
    chips = lax.axis_size("chip")
    order = list(range(0, chips, 2)) + list(range(chips - 1, 0, -2))
    return [(order[at], order[(at + direction) % chips]) for at in range(chips)]


def ring_sum(partial, direction):
    chips, place, pairs = lax.axis_size("chip"), ring_position(), ring_pairs(direction)
    rows = partial.shape[0] // chips

    def block(step):
        index = lax.rem(place + (chips - direction * step) % chips, chips)
        return lax.dynamic_slice_in_dim(partial, index * rows, rows, 0)

    travel = block(1).astype(BF16)
    for step in range(2, chips + 1):
        travel = (lax.ppermute(travel, "chip", pairs).astype(F32) + block(step)).astype(BF16)
    blocks = [travel]
    for _ in range(chips - 1):
        blocks.append(lax.ppermute(blocks[-1], "chip", pairs))
    return blocks


def assemble_kernel(cuts, _, *refs):
    inputs, outputs = refs[: -len(cuts)], refs[-len(cuts) :]
    for at, block in enumerate(inputs):

        @pl.when(pl.program_id(0) == at)
        def _(block=block):
            for output, cut in zip(outputs, cuts):
                output[...] = block[:, cut].astype(F32)


def assemble(blocks, direction, axis, count=1):
    chips, place, core = lax.axis_size("chip"), ring_position(), lax.axis_index("core")
    steps = jnp.arange(chips, dtype=jnp.int32)
    index = lax.rem(place + (chips - direction * steps) % chips, chips)
    index = jnp.concatenate([index, index])
    side = jnp.concatenate([jnp.full((chips,), core), jnp.full((chips,), 1 - core)])
    if axis == 0:
        order = jnp.stack([side * chips + index, jnp.zeros_like(index)])
    else:
        order = jnp.stack([index, side])
    rows, columns = blocks[0].shape
    columns //= count
    shape = (2 * chips * rows, columns) if axis == 0 else (chips * rows, 2 * columns)
    cuts = [slice(at * columns, at * columns + columns) for at in range(count)]
    blocks = blocks + [swap_cores(block) for block in blocks]
    if rows % 8 or columns % 128:
        outputs = [jnp.zeros(shape, F32)] * count
        for at, block in enumerate(blocks):
            start = (order[0, at] * rows, order[1, at] * columns)
            outputs = [
                lax.dynamic_update_slice(output, block[:, cut].astype(F32), start)
                for output, cut in zip(outputs, cuts)
            ]
        return outputs
    return pl.pallas_call(
        functools.partial(assemble_kernel, cuts),
        grid_spec=pltpu.PrefetchScalarGridSpec(
            num_scalar_prefetch=1,
            grid=(2 * chips,),
            in_specs=[pl.BlockSpec(blocks[0].shape, lambda at, order: (0, 0))] * (2 * chips),
            out_specs=[pl.BlockSpec((rows, columns), lambda at, order: (order[0, at], order[1, at]))]
            * count,
        ),
        out_shape=[jax.ShapeDtypeStruct(shape, F32)] * count,
        compiler_params=pltpu.CompilerParams(vmem_limit_bytes=vmem_limit),
        name="assemble",
    )(order.astype(jnp.int32), *blocks)


def core_half(values, axis, side):
    size = values.shape[axis] // 2
    return lax.dynamic_slice_in_dim(values, side * size, size, axis)


def share_halves(values, axis):
    core = lax.axis_index("core")
    return core_half(values, axis, core), swap_cores(core_half(values, axis, 1 - core))


def head_sum(values):
    low = values.astype(BF16)
    if lax.axis_size("head") == 2:
        return low.astype(F32) + lax.ppermute(low, "head", [(0, 1), (1, 0)]).astype(F32)
    return lax.psum(low, "head").astype(F32)


def whole_head_sum(values):
    if lax.axis_size("head") == 2:
        return values + lax.ppermute(values, "head", [(0, 1), (1, 0)])
    return lax.psum(values, "head")


def band_sum(values):
    values = values + swap_cores(values)
    chips, reach = lax.axis_size("chip"), 1
    while reach < chips:
        pairs = [(chip, chip ^ reach) for chip in range(chips)]
        values = values + lax.ppermute(values, "chip", pairs)
        reach *= 2
    return values


def local(
    block_input,
    out_grad,
    segments,
    lead_steps,
    gain_attn,
    shift_attn,
    lead_weight,
    query_weight,
    key_weight,
    value_weight,
    output_weight,
    output_bias,
    gain_mlp,
    shift_mlp,
    up_weight,
    up_bias,
    down_weight,
    down_bias,
):
    rows = block_input.shape[0]
    heads = query_weight.shape[1] // HD
    width = heads * HD
    chips = lax.axis_size("chip")
    split = chips // heads
    crops = lead_steps.shape[0]
    inputs = block_input.astype(F32)
    unit_attn, inverse_attn = normalize(inputs)
    onehot = (segments[:, None] == jnp.arange(crops, dtype=jnp.int32)[None, :]).astype(F32)
    lead = jnp.sum(onehot * lead_steps.astype(F32)[None, :], axis=1) / 12.0
    attn_in = (unit_attn * gain_attn + shift_attn + lead[:, None] * lead_weight).astype(BF16)
    query, key, value = (
        product(weight, attn_in, 0, 1).astype(BF16).reshape(heads, HD, rows)
        for weight in (query_weight, key_weight, value_weight)
    )
    crop_rows = jnp.broadcast_to(segments.astype(BF16), (heads, 16, rows))
    payload = jnp.concatenate([query, key, value, crop_rows], axis=1)
    if split == 1:
        own = to_heads(payload)
        queries = own
    else:
        queries = scatter_queries(payload.reshape(-1, rows), heads, split)
        own = to_heads(jnp.repeat(payload, split, axis=0))
    other = swap_cores(own)
    raw, out, logsum = attention_forward(queries, own, other, crops)
    attn_out = gather_queries(out, heads, split, rows)
    branch = head_sum(product(attn_out, output_weight, 0, 0))
    hidden = inputs + branch + output_bias
    unit_mlp, inverse_mlp = normalize(hidden)
    mlp_in = (unit_mlp * gain_mlp + shift_mlp).astype(BF16)
    upper = product(mlp_in, up_weight) + up_bias
    active, gelu_back = jax.vjp(exact_gelu, upper)
    active_low = active.astype(BF16)
    d_active = product(out_grad, down_weight, 1, 1)
    d_upper = gelu_back(d_active)[0].astype(BF16)
    d_mlp = head_sum(product(d_upper, up_weight, 1, 1))
    mlp_part, d_mlp = lax.optimization_barrier(
        (product(active_low, down_weight).astype(BF16), d_mlp)
    )
    mlp_out = head_sum(mlp_part)
    block_output = (hidden + mlp_out + down_bias).astype(BF16)
    grad_out = out_grad.astype(F32)
    grad_far, mlp_in_far, attn_in_far = (swap_cores(v) for v in (out_grad, mlp_in, attn_in))
    active_near, active_far = share_halves(active_low, 1)
    upper_near, upper_far = share_halves(d_upper, 1)
    ddown = ring_sum(product(active_near, out_grad, 0, 0) + product(active_far, grad_far, 0, 0), 1)
    dup = ring_sum(product(mlp_in, upper_near, 0, 0) + product(mlp_in_far, upper_far, 0, 0), -1)
    d_hidden = grad_out + normalize_back(d_mlp * gain_mlp, unit_mlp, inverse_mlp)
    d_branch = d_hidden.astype(BF16)
    out_near, out_far = share_halves(attn_out, 0)
    doutput = ring_sum(product(out_near, d_branch) + product(out_far, swap_cores(d_branch)), -1)
    d_attn = product(output_weight, d_branch, 1, 1).astype(BF16)
    grads = scatter_queries(d_attn, heads, split)
    pieces = 2
    dquery = None
    far_sums, near_sums = [], []
    for keys, sums, sums_type in ((other, far_sums, BF16), (own, near_sums, F32)):
        for index in range(pieces):
            last = keys is own and index == pieces - 1
            dquery, piece = backward_piece(
                queries, grads, raw, logsum, dquery, keys, index, pieces, crops, sums_type, last
            )
            sums.append(piece)
    key_value = jnp.concatenate(
        [
            (near + swap_cores(far).astype(F32)).astype(BF16)
            for near, far in zip(near_sums, far_sums)
        ]
    )
    if split == 1:
        moved = to_heads(jnp.concatenate([dquery, key_value], axis=1))
        dquery, dkey, dvalue = (
            moved[:, at * HD : at * HD + HD].reshape(width, rows) for at in range(3)
        )
    else:
        dquery = gather_queries(dquery, heads, split, rows)
        moved = to_heads(key_value).reshape(heads, split, 2 * HD, rows).astype(F32)
        moved = jnp.sum(moved, axis=1).astype(BF16)
        dkey, dvalue = (moved[:, at * HD : at * HD + HD].reshape(width, rows) for at in range(2))
    d_part = (
        product(dquery, query_weight, 0, 1)
        + product(dkey, key_weight, 0, 1)
        + product(dvalue, value_weight, 0, 1)
    )
    near, far = zip(*(share_halves(grad, 0) for grad in (dquery, dkey, dvalue)))
    dquery_weight, dkey_weight, dvalue_weight = (
        product(attn_in, one, 0, 1) + product(attn_in_far, two, 0, 1)
        for one, two in zip(near, far)
    )
    dquery_key = ring_sum(jnp.concatenate([dquery_weight, dkey_weight], axis=1), 1)
    dvalue_blocks = ring_sum(dvalue_weight, -1)
    d_in = head_sum(d_part)
    input_grad = (d_hidden + normalize_back(d_in * gain_attn, unit_attn, inverse_attn)).astype(
        BF16
    )
    ends = band_sum(
        whole_head_sum(
            jnp.stack(
                [
                    jnp.sum(d_part * unit_attn, axis=0),
                    jnp.sum(d_part, axis=0),
                    jnp.sum(lead[:, None] * d_part, axis=0),
                ]
            )
        )
    )
    small = band_sum(
        jnp.stack(
            [
                jnp.sum(d_hidden, axis=0),
                jnp.sum(d_mlp * unit_mlp, axis=0),
                jnp.sum(d_mlp, axis=0),
                jnp.sum(grad_out, axis=0),
            ]
        )
    )
    dup_bias = band_sum(jnp.sum(d_upper.astype(F32), axis=0))
    (ddown_weight,) = assemble(ddown, 1, 0)
    (dup_weight,) = assemble(dup, -1, 1)
    (doutput_weight,) = assemble(doutput, -1, 0)
    dquery_weight, dkey_weight = assemble(dquery_key, 1, 1, 2)
    (dvalue_weight,) = assemble(dvalue_blocks, -1, 1)
    return (
        block_output,
        input_grad,
        ends[0],
        ends[1],
        ends[2],
        dquery_weight,
        dkey_weight,
        dvalue_weight,
        doutput_weight,
        small[0],
        small[1],
        small[2],
        dup_weight,
        dup_bias,
        ddown_weight,
        small[3],
    )


def solution(mesh):
    bands, halves = mesh.shape["band"], mesh.shape["head"]
    inner = Mesh(mesh.devices.reshape(bands // 2, 2, halves), ("chip", "core", "head"))
    band = ("chip", "core")
    rows, columns, split_rows = P(band, None), P(None, "head"), P("head", None)
    return jax.shard_map(
        local,
        mesh=inner,
        in_specs=(
            rows,
            rows,
            P(band),
            P(),
            P(),
            P(),
            P(),
            columns,
            columns,
            columns,
            split_rows,
            P(),
            P(),
            P(),
            columns,
            P("head"),
            split_rows,
            P(),
        ),
        out_specs=(
            rows,
            rows,
            P(),
            P(),
            P(),
            columns,
            columns,
            columns,
            split_rows,
            P(),
            P(),
            P(),
            columns,
            P("head"),
            split_rows,
            P(),
        ),
        check_vma=False,
    )
```

```python
import functools

import jax
import jax.numpy as jnp
from jax import lax
from jax.experimental import pallas as pl
from jax.experimental.pallas import tpu as pltpu
from jax.sharding import Mesh, PartitionSpec as P

HD = 64
F32 = jnp.float32
BF16 = jnp.bfloat16
eps = 1e-05
masked_value = -1e30
seg_row = 3 * HD
payload_rows = 3 * HD + 16
vmem_limit = 48 * 2**20


def normalize(values):
    centred = values - jnp.mean(values, axis=-1, keepdims=True)
    inverse = lax.rsqrt(jnp.mean(centred * centred, axis=-1, keepdims=True) + eps)
    return (centred * inverse, inverse)


def normalize_back(grad_unit, unit, inverse):
    return inverse * (
        grad_unit
        - jnp.mean(grad_unit, axis=-1, keepdims=True)
        - unit * jnp.mean(grad_unit * unit, axis=-1, keepdims=True)
    )


def product(first, second, first_axis=1, second_axis=0):
    return lax.dot_general(
        first,
        second,
        (((first_axis,), (second_axis,)), ((), ())),
        preferred_element_type=jnp.float32,
    )


def exact_gelu(values):
    return jax.nn.gelu(values, approximate=False)


def load_keys(pieces, crops, keys, key_t, value_t, value_n):
    start = 0
    for piece in pieces:
        chips, _, patches = piece.shape
        for chip in range(chips):
            crop = lax.broadcasted_iota(jnp.int32, (HD, patches), 0)
            segment = piece[chip, pl.ds(seg_row, 16), :].astype(F32)[:1].astype(jnp.int32)
            mask = jnp.where((crop != segment) & (crop < crops), masked_value, 0.0)
            key = piece[chip, pl.ds(HD, HD), :]
            value = piece[chip, pl.ds(2 * HD, HD), :]
            place = pl.ds(start, patches)
            keys[place, :] = jnp.concatenate([key.astype(F32), mask], axis=0).T.astype(BF16)
            if key_t is not None:
                key_t[:, place] = key
            if value_t is not None:
                value_t[pl.ds(0, HD), place] = value
                value_t[pl.ds(HD, 16), place] = jnp.ones((16, patches), BF16)
            if value_n is not None:
                value_n[place, :] = value.astype(F32).T.astype(BF16)
            start += patches


def masked_query(query_ref):
    query = query_ref[0, pl.ds(0, HD), :].astype(F32) * 0.125
    segment = query_ref[0, pl.ds(seg_row, 16), :].astype(F32)[:1].astype(jnp.int32)
    crop = lax.broadcasted_iota(jnp.int32, query.shape, 0)
    onehot = jnp.where(crop == segment, 1.0, 0.0)
    return jnp.concatenate([query, onehot], axis=0).astype(BF16)


def forward_kernel(crops, step, query_ref, own, other, raw_ref, out_ref, logsum_ref, keys, value_t):
    @pl.when(pl.program_id(0) == 0)
    def _():
        load_keys((own, other), crops, keys, None, value_t, None)

    query = masked_query(query_ref)
    count = query.shape[1]
    top = jnp.full((1, count), masked_value, F32)
    accum = jnp.zeros((HD + 16, count), F32)
    for start in range(0, keys.shape[0], step):
        scores = product(keys[pl.ds(start, step), :], query)
        new_top = jnp.maximum(top, jnp.max(scores, axis=0, keepdims=True))
        weights = jnp.exp(scores - new_top).astype(BF16)
        accum = accum * jnp.exp(top - new_top) + product(value_t[:, pl.ds(start, step)], weights)
        top = new_top
    total = accum[HD : HD + 1]
    raw = accum[:HD] / total
    raw_ref[0] = raw
    out_ref[0] = raw.astype(BF16)
    logsum_ref[0] = top + jnp.log(total)


def backward_kernel(
    crops,
    query_ref,
    grad_ref,
    raw_ref,
    logsum_ref,
    before_ref,
    piece,
    dquery_ref,
    sums_ref,
    keys,
    key_t,
    value_n,
    sums,
):
    group = pl.program_id(0)

    @pl.when(group == 0)
    def _():
        load_keys((piece,), crops, keys, key_t, None, value_n)
        sums[...] = jnp.zeros_like(sums)

    query = masked_query(query_ref)
    grad = grad_ref[0]
    grad_wide = grad.astype(F32)
    delta = jnp.sum(grad_wide * raw_ref[0], axis=0, keepdims=True)
    scaled = query_ref[0, pl.ds(0, HD), :].astype(F32) * 0.125
    zero = jnp.zeros_like(scaled)
    query_side = jnp.concatenate([scaled, zero], axis=0).T.astype(BF16)
    grad_side = jnp.concatenate([zero, grad_wide], axis=0).T.astype(BF16)
    probs = jnp.exp(product(keys[...], query) - logsum_ref[0])
    dprobs = product(value_n[...], grad)
    dscores = (probs * (dprobs - delta)).astype(BF16)
    sums[...] += product(dscores, query_side) + product(probs.astype(BF16), grad_side)
    dquery = product(key_t[...], dscores) * 0.125
    if before_ref is not None:
        dquery = before_ref[0] + dquery
    dquery_ref[0] = dquery.astype(dquery_ref.dtype)

    @pl.when(group == pl.num_programs(0) - 1)
    def _():
        chips, _, patches = sums_ref.shape
        for chip in range(chips):
            sums_ref[chip] = sums[pl.ds(chip * patches, patches), :].T.astype(sums_ref.dtype)


def key_step(count):
    return 1024 if count % 1024 == 0 else 256


def query_spec(rows, patches):
    return pl.BlockSpec((1, rows, patches), lambda group: (group, 0, 0))


def whole_spec(shape):
    return pl.BlockSpec(shape, lambda group: (0,) * len(shape))


def attention_forward(queries, own, other, crops):
    groups, _, patches = queries.shape
    count = 2 * own.shape[0] * own.shape[2]
    return pl.pallas_call(
        functools.partial(forward_kernel, crops, key_step(count)),
        grid=(groups,),
        in_specs=[
            query_spec(payload_rows, patches),
            whole_spec(own.shape),
            whole_spec(other.shape),
        ],
        out_specs=[query_spec(HD, patches), query_spec(HD, patches), query_spec(1, patches)],
        out_shape=[
            jax.ShapeDtypeStruct((groups, HD, patches), F32),
            jax.ShapeDtypeStruct((groups, HD, patches), BF16),
            jax.ShapeDtypeStruct((groups, 1, patches), F32),
        ],
        scratch_shapes=[pltpu.VMEM((count, 2 * HD), BF16), pltpu.VMEM((HD + 16, count), BF16)],
        compiler_params=pltpu.CompilerParams(vmem_limit_bytes=vmem_limit),
        cost_estimate=pl.CostEstimate(
            flops=groups * patches * count * 2 * 1024,
            bytes_accessed=4 * 2**20,
            transcendentals=groups * patches * count,
        ),
        name="attention_forward",
    )(queries, own, other)


def backward_piece(queries, grads, raw, logsum, before, keys, index, pieces, crops, sums_type, last):
    groups, _, patches = queries.shape
    chips = keys.shape[0] // pieces
    count = chips * keys.shape[2]
    sums_shape = (chips, 2 * HD, keys.shape[2])
    earlier = [] if before is None else [before]
    body = functools.partial(backward_kernel, crops)
    if before is None:
        body = lambda *refs: backward_kernel(crops, *refs[:4], None, *refs[4:])
    return pl.pallas_call(
        body,
        grid=(groups,),
        in_specs=[
            query_spec(payload_rows, patches),
            query_spec(HD, patches),
            query_spec(HD, patches),
            query_spec(1, patches),
        ]
        + [query_spec(HD, patches)] * len(earlier)
        + [pl.BlockSpec((chips,) + keys.shape[1:], lambda group: (index, 0, 0))],
        out_specs=[query_spec(HD, patches), whole_spec(sums_shape)],
        out_shape=[
            jax.ShapeDtypeStruct((groups, HD, patches), BF16 if last else F32),
            jax.ShapeDtypeStruct(sums_shape, sums_type),
        ],
        scratch_shapes=[
            pltpu.VMEM((count, 2 * HD), BF16),
            pltpu.VMEM((HD, count), BF16),
            pltpu.VMEM((count, HD), BF16),
            pltpu.VMEM((count, 2 * HD), F32),
        ],
        compiler_params=pltpu.CompilerParams(vmem_limit_bytes=vmem_limit),
        cost_estimate=pl.CostEstimate(
            flops=groups * patches * count * 2 * 2048,
            bytes_accessed=4 * 2**20,
            transcendentals=groups * patches * count,
        ),
        name="attention_backward",
    )(queries, grads, raw, logsum, *earlier, keys)


def swap_cores(values):
    return lax.ppermute(values, "core", [(0, 1), (1, 0)])


def to_heads(blocks):
    return lax.all_to_all(blocks, "chip", 0, 0, tiled=True)


def scatter_queries(values, heads, split):
    rows, patches = values.shape[0] // heads, values.shape[1]
    if split == 1:
        return to_heads(values.reshape(heads, rows, patches))
    part = patches // split
    blocks = values.reshape(heads, rows, split, part).transpose(0, 2, 1, 3)
    moved = to_heads(blocks.reshape(heads * split, rows, part))
    width = min(256, moved.shape[0] * part)
    joined = moved.transpose(1, 0, 2).reshape(rows, -1, width)
    return joined.transpose(1, 0, 2)


def gather_queries(values, heads, split, patches):
    rows = values.shape[1]
    if split == 1:
        return to_heads(values).reshape(heads * rows, patches)
    part = patches // split
    joined = values.transpose(1, 0, 2).reshape(rows, heads * split, part)
    moved = to_heads(joined.transpose(1, 0, 2)).reshape(heads, split, rows, part)
    return moved.transpose(0, 2, 1, 3).reshape(heads * rows, patches)


def ring_position():
    chips, chip = lax.axis_size("chip"), lax.axis_index("chip")
    return jnp.where(chip % 2 == 0, chip // 2, chips - 1 - chip // 2)


def ring_pairs(direction):
    chips = lax.axis_size("chip")
    order = list(range(0, chips, 2)) + list(range(chips - 1, 0, -2))
    return [(order[at], order[(at + direction) % chips]) for at in range(chips)]


class Ring:
    def __init__(self, partial, direction):
        self.chips = lax.axis_size("chip")
        self.partial, self.direction = partial, direction
        self.rows = partial.shape[0] // self.chips
        self.step, self.near, self.far = 1, [], []
        self.pending = [self.send(self.block(1).astype(BF16))]

    def index(self, step):
        ahead = (self.chips - self.direction * step) % self.chips
        return lax.rem(ring_position() + ahead, self.chips)

    def block(self, step):
        return lax.dynamic_slice_in_dim(
            self.partial, self.index(step) * self.rows, self.rows, 0
        )

    def send(self, block):
        return lax.ppermute(block, "chip", ring_pairs(self.direction))

    def advance(self, arrived):
        self.step += 1
        if len(arrived) > 1 or self.step == 2 * self.chips:
            self.far.append(arrived[-1])
        block, self.pending = arrived[0], []
        if self.step <= self.chips:
            block = (block.astype(F32) + self.block(self.step)).astype(BF16)
        if self.step < 2 * self.chips - 1:
            self.pending.append(self.send(block))
        if self.chips <= self.step < 2 * self.chips:
            self.near.append(block)
            self.pending.append(swap_cores(block))


def visit(rings, values):
    pending, values = lax.optimization_barrier(([ring.pending for ring in rings], values))
    for ring, arrived in zip(rings, pending):
        if arrived:
            ring.advance(arrived)
    return values


def place_kernel(_, *refs):
    refs = refs[-6:]
    for side in range(2):

        @pl.when(pl.program_id(0) == side)
        def _(side=side):
            refs[4][...] = refs[side][...].astype(F32)
            refs[5][...] = refs[2 + side][...].astype(F32)


def place(outputs, down, up, at):
    tall, wide = down.near[at].shape, up.near[at].shape
    chips, core = down.chips, lax.axis_index("core")
    blocks = [down.near[at], down.far[at], up.near[at], up.far[at]]
    shapes = [(2 * chips * tall[0], tall[1]), (chips * wide[0], 2 * wide[1])]
    order = jnp.stack([down.index(at), up.index(at), core]).astype(jnp.int32)

    def side(at, order):
        return jnp.where(at == 0, order[2], 1 - order[2])

    return pl.pallas_call(
        place_kernel,
        grid_spec=pltpu.PrefetchScalarGridSpec(
            num_scalar_prefetch=1,
            grid=(2,),
            in_specs=[pl.BlockSpec(memory_space=pl.ANY)] * len(outputs)
            + [pl.BlockSpec(block.shape, lambda at, order: (0, 0)) for block in blocks],
            out_specs=[
                pl.BlockSpec(tall, lambda at, order: (side(at, order) * chips + order[0], 0)),
                pl.BlockSpec(wide, lambda at, order: (order[1], side(at, order))),
            ],
        ),
        out_shape=[jax.ShapeDtypeStruct(shape, F32) for shape in shapes],
        input_output_aliases={1 + at: at for at in range(len(outputs))},
        compiler_params=pltpu.CompilerParams(vmem_limit_bytes=vmem_limit),
        name="place",
    )(order, *outputs, *blocks)


def place_all(down, up):
    outputs = []
    for at in range(down.chips):
        outputs = place(outputs, down, up, at)
    return outputs


def core_half(values, axis, side):
    size = values.shape[axis] // 2
    return lax.dynamic_slice_in_dim(values, side * size, size, axis)


def share_halves(values, axis):
    core = lax.axis_index("core")
    return core_half(values, axis, core), swap_cores(core_half(values, axis, 1 - core))


def head_sum(values):
    low = values.astype(BF16)
    if lax.axis_size("head") == 2:
        return low.astype(F32) + lax.ppermute(low, "head", [(0, 1), (1, 0)]).astype(F32)
    return lax.psum(low, "head").astype(F32)


def whole_head_sum(values):
    if lax.axis_size("head") == 2:
        return values + lax.ppermute(values, "head", [(0, 1), (1, 0)])
    return lax.psum(values, "head")


def ring_position():
    chips, chip = lax.axis_size("chip"), lax.axis_index("chip")
    return jnp.where(chip % 2 == 0, chip // 2, chips - 1 - chip // 2)


def ring_pairs(direction):
    chips = lax.axis_size("chip")
    order = list(range(0, chips, 2)) + list(range(chips - 1, 0, -2))
    return [(order[at], order[(at + direction) % chips]) for at in range(chips)]


class Ring:
    def __init__(self, partial, direction):
        self.chips = lax.axis_size("chip")
        self.partial, self.direction = partial, direction
        self.rows = partial.shape[0] // self.chips
        self.step, self.near, self.far = 1, [], []
        self.pending = [self.send(self.block(1).astype(BF16))]

    def index(self, step):
        ahead = (self.chips - self.direction * step) % self.chips
        return lax.rem(ring_position() + ahead, self.chips)

    def block(self, step):
        return lax.dynamic_slice_in_dim(
            self.partial, self.index(step) * self.rows, self.rows, 0
        )

    def send(self, block):
        return lax.ppermute(block, "chip", ring_pairs(self.direction))

    def advance(self, arrived):
        self.step += 1
        if len(arrived) > 1 or self.step == 2 * self.chips:
            self.far.append(arrived[-1])
        block, self.pending = arrived[0], []
        if self.step <= self.chips:
            block = (block.astype(F32) + self.block(self.step)).astype(BF16)
        if self.step < 2 * self.chips - 1:
            self.pending.append(self.send(block))
        if self.chips <= self.step < 2 * self.chips:
            self.near.append(block)
            self.pending.append(swap_cores(block))


def visit(rings, values):
    pending, values = lax.optimization_barrier(([ring.pending for ring in rings], values))
    for ring, arrived in zip(rings, pending):
        if arrived:
            ring.advance(arrived)
    return values


def place_kernel(_, *refs):
    refs = refs[-6:]
    for side in range(2):

        @pl.when(pl.program_id(0) == side)
        def _(side=side):
            refs[4][...] = refs[side][...].astype(F32)
            refs[5][...] = refs[2 + side][...].astype(F32)


def place(outputs, down, up, at):
    tall, wide = down.near[at].shape, up.near[at].shape
    chips, core = down.chips, lax.axis_index("core")
    blocks = [down.near[at], down.far[at], up.near[at], up.far[at]]
    shapes = [(2 * chips * tall[0], tall[1]), (chips * wide[0], 2 * wide[1])]
    order = jnp.stack([down.index(at), up.index(at), core]).astype(jnp.int32)

    def side(at, order):
        return jnp.where(at == 0, order[2], 1 - order[2])

    return pl.pallas_call(
        place_kernel,
        grid_spec=pltpu.PrefetchScalarGridSpec(
            num_scalar_prefetch=1,
            grid=(2,),
            in_specs=[pl.BlockSpec(memory_space=pl.ANY)] * len(outputs)
            + [pl.BlockSpec(block.shape, lambda at, order: (0, 0)) for block in blocks],
            out_specs=[
                pl.BlockSpec(tall, lambda at, order: (side(at, order) * chips + order[0], 0)),
                pl.BlockSpec(wide, lambda at, order: (order[1], side(at, order))),
            ],
        ),
        out_shape=[jax.ShapeDtypeStruct(shape, F32) for shape in shapes],
        input_output_aliases={1 + at: at for at in range(len(outputs))},
        compiler_params=pltpu.CompilerParams(vmem_limit_bytes=vmem_limit),
        name="place",
    )(order, *outputs, *blocks)


def place_all(down, up):
    outputs = []
    for at in range(down.chips):
        outputs = place(outputs, down, up, at)
    return outputs


def core_half(values, axis, side):
    size = values.shape[axis] // 2
    return lax.dynamic_slice_in_dim(values, side * size, size, axis)


def share_halves(values, axis):
    core = lax.axis_index("core")
    return core_half(values, axis, core), swap_cores(core_half(values, axis, 1 - core))


def head_sum(values):
    low = values.astype(BF16)
    if lax.axis_size("head") == 2:
        return low.astype(F32) + lax.ppermute(low, "head", [(0, 1), (1, 0)]).astype(F32)
    return lax.psum(low, "head").astype(F32)


def whole_head_sum(values):
    if lax.axis_size("head") == 2:
        return values + lax.ppermute(values, "head", [(0, 1), (1, 0)])
    return lax.psum(values, "head")


def band_sum(values):
    values = values + swap_cores(values)
    chips, reach = lax.axis_size("chip"), 1
    while reach < chips:
        pairs = [(chip, chip ^ reach) for chip in range(chips)]
        values = values + lax.ppermute(values, "chip", pairs)
        reach *= 2
    return values


def local(
    block_input,
    out_grad,
    segments,
    lead_steps,
    gain_attn,
    shift_attn,
    lead_weight,
    query_weight,
    key_weight,
    value_weight,
    output_weight,
    output_bias,
    gain_mlp,
    shift_mlp,
    up_weight,
    up_bias,
    down_weight,
    down_bias,
):
    rows = block_input.shape[0]
    heads = query_weight.shape[1] // HD
    width = heads * HD
    chips = lax.axis_size("chip")
    split = chips // heads
    crops = lead_steps.shape[0]
    inputs = block_input.astype(F32)
    unit_attn, inverse_attn = normalize(inputs)
    onehot = (segments[:, None] == jnp.arange(crops, dtype=jnp.int32)[None, :]).astype(F32)
    lead = jnp.sum(onehot * lead_steps.astype(F32)[None, :], axis=1) / 12.0
    attn_in = (unit_attn * gain_attn + shift_attn + lead[:, None] * lead_weight).astype(BF16)
    query, key, value = (
        product(weight, attn_in, 0, 1).astype(BF16).reshape(heads, HD, rows)
        for weight in (query_weight, key_weight, value_weight)
    )
    crop_rows = jnp.broadcast_to(segments.astype(BF16), (heads, 16, rows))
    payload = jnp.concatenate([query, key, value, crop_rows], axis=1)
    if split == 1:
        own = to_heads(payload)
        queries = own
    else:
        queries = scatter_queries(payload.reshape(-1, rows), heads, split)
        own = to_heads(jnp.repeat(payload, split, axis=0))
    other = swap_cores(own)
    if split == 1:
        attn_in_all, other = lax.optimization_barrier((attn_in, other))
        attn_in_all = lax.all_gather(attn_in_all, "chip", axis=0)
    raw, out, logsum = attention_forward(queries, own, other, crops)
    attn_out = gather_queries(out, heads, split, rows)
    branch = head_sum(product(attn_out, output_weight, 0, 0))
    hidden = inputs + branch + output_bias
    unit_mlp, inverse_mlp = normalize(hidden)
    mlp_in = (unit_mlp * gain_mlp + shift_mlp).astype(BF16)
    upper = product(mlp_in, up_weight) + up_bias
    active, gelu_back = jax.vjp(exact_gelu, upper)
    active_low = active.astype(BF16)
    d_active = product(out_grad, down_weight, 1, 1)
    d_upper = gelu_back(d_active)[0].astype(BF16)
    d_mlp = head_sum(product(d_upper, up_weight, 1, 1))
    grad_out = out_grad.astype(F32)
    grad_far, mlp_in_far = swap_cores(out_grad), swap_cores(mlp_in)
    active_near, active_far = share_halves(active_low, 1)
    upper_near, upper_far = share_halves(d_upper, 1)
    down = Ring(product(active_near, out_grad, 0, 0) + product(active_far, grad_far, 0, 0), 1)
    up = Ring(product(mlp_in, upper_near, 0, 0) + product(mlp_in_far, upper_far, 0, 0), -1)
    rings = (down, up)
    d_mlp = visit(rings, d_mlp)
    mlp_part, d_mlp = lax.optimization_barrier(
        (product(active_low, down_weight).astype(BF16), d_mlp)
    )
    mlp_out = head_sum(mlp_part)
    d_hidden = grad_out + normalize_back(d_mlp * gain_mlp, unit_mlp, inverse_mlp)
    d_branch = d_hidden.astype(BF16)
    d_attn = product(output_weight, d_branch, 1, 1).astype(BF16)
    d_attn = visit(rings, d_attn)
    grads = scatter_queries(d_attn, heads, split)
    pieces = 2
    dquery = None
    far_sums, near_sums = [], []
    for keys, sums, sums_type in ((other, far_sums, BF16), (own, near_sums, F32)):
        for index in range(pieces):
            grads, dquery = visit(rings, (grads, dquery))
            last = keys is own and index == pieces - 1
            dquery, piece = backward_piece(
                queries, grads, raw, logsum, dquery, keys, index, pieces, crops, sums_type, last
            )
            sums.append(piece)
    key_value = jnp.concatenate(
        [
            (near + swap_cores(far).astype(F32)).astype(BF16)
            for near, far in zip(near_sums, far_sums)
        ]
    )
    small = jnp.concatenate(
        [
            jnp.stack(
                [
                    jnp.sum(d_hidden, axis=0),
                    jnp.sum(d_mlp * unit_mlp, axis=0),
                    jnp.sum(d_mlp, axis=0),
                    jnp.sum(grad_out, axis=0),
                ]
            ).reshape(-1),
            jnp.sum(d_upper.astype(F32), axis=0),
        ]
    )
    lines = -(-small.shape[0] // (16 * d_branch.shape[1])) * 16
    small = jnp.pad(small, (0, lines * d_branch.shape[1] - small.shape[0])).astype(BF16)
    later = lax.psum(
        jnp.concatenate(
            [product(attn_out, d_branch).astype(BF16), small.reshape(lines, -1)], axis=0
        ),
        ("chip", "core"),
    ).astype(F32)
    doutput_weight, small = later[:width], later[width:].reshape(-1)
    model = d_branch.shape[1]
    dup_bias = small[4 * model : 4 * model + d_upper.shape[1]]
    if split == 1:
        head_grads = visit(rings, jnp.concatenate([dquery, key_value], axis=1))
        moved = to_heads(head_grads)
        dquery, dkey, dvalue = (
            moved[:, at * HD : at * HD + HD].reshape(width, rows) for at in range(3)
        )
    else:
        dquery = gather_queries(dquery, heads, split, rows)
        moved = to_heads(key_value).reshape(heads, split, 2 * HD, rows).astype(F32)
        moved = jnp.sum(moved, axis=1).astype(BF16)
        dkey, dvalue = (moved[:, at * HD : at * HD + HD].reshape(width, rows) for at in range(2))
        dquery, dkey, dvalue = visit(rings, (dquery, dkey, dvalue))
    d_part = (
        product(dquery, query_weight, 0, 1)
        + product(dkey, key_weight, 0, 1)
        + product(dvalue, value_weight, 0, 1)
    )
    if split == 1:
        projections = lax.dot_general(
            head_grads, attn_in_all, (((0, 2), (0, 1)), ((), ())), preferred_element_type=F32
        ).astype(BF16)
        near, far = share_halves(projections, 0)
        projections = (near.astype(F32) + far.astype(F32)).astype(BF16)
        d_part, projections = visit(rings, (d_part, projections))
        projections = lax.all_gather(projections, ("chip", "core"), axis=0, tiled=True)
        projections = projections.reshape(heads, 3, HD, model)
        projections = [
            projections[:, at].reshape(width, model).T.astype(F32) for at in range(3)
        ]
    else:
        projections = [
            lax.psum(product(attn_in, grad, 0, 1).astype(BF16), ("chip", "core")).astype(F32)
            for grad in (dquery, dkey, dvalue)
        ]
    d_in = head_sum(d_part)
    ends = jnp.stack(
        [
            jnp.sum(d_part * unit_attn, axis=0),
            jnp.sum(d_part, axis=0),
            jnp.sum(lead[:, None] * d_part, axis=0),
        ]
    )
    ends = visit(rings, ends)
    ends = whole_head_sum(ends)
    ends = visit(rings, ends)
    ends = ends + swap_cores(ends)
    reach = 1
    while reach < chips:
        ends = visit(rings, ends)
        pairs = [(chip, chip ^ reach) for chip in range(chips)]
        ends = ends + lax.ppermute(ends, "chip", pairs)
        reach *= 2
    input_grad = (d_hidden + normalize_back(d_in * gain_attn, unit_attn, inverse_attn)).astype(
        BF16
    )
    while any(ring.pending for ring in rings):
        visit(rings, ())
    ddown_weight, dup_weight = place_all(down, up)
    block_output = (hidden + mlp_out + down_bias).astype(BF16)
    return (
        block_output,
        input_grad,
        ends[0],
        ends[1],
        ends[2],
        *projections,
        doutput_weight,
        *(small[at * model : at * model + model] for at in range(3)),
        dup_weight,
        dup_bias,
        ddown_weight,
        small[3 * model : 4 * model],
    )


def solution(mesh):
    bands, halves = mesh.shape["band"], mesh.shape["head"]
    inner = Mesh(mesh.devices.reshape(bands // 2, 2, halves), ("chip", "core", "head"))
    band = ("chip", "core")
    rows, columns, split_rows = P(band, None), P(None, "head"), P("head", None)
    return jax.shard_map(
        local,
        mesh=inner,
        in_specs=(
            rows,
            rows,
            P(band),
            P(),
            P(),
            P(),
            P(),
            columns,
            columns,
            columns,
            split_rows,
            P(),
            P(),
            P(),
            columns,
            P("head"),
            split_rows,
            P(),
        ),
        out_specs=(
            rows,
            rows,
            P(),
            P(),
            P(),
            columns,
            columns,
            columns,
            split_rows,
            P(),
            P(),
            P(),
            columns,
            P("head"),
            split_rows,
            P(),
        ),
        check_vma=False,
    )
```

```python
import functools

import jax
import jax.numpy as jnp
from jax import lax
from jax.experimental import pallas as pl
from jax.experimental.pallas import tpu as pltpu
from jax.sharding import Mesh, PartitionSpec as P

HD = 64
F32 = jnp.float32
BF16 = jnp.bfloat16
eps = 1e-05
masked_value = -1e30
seg_row = 3 * HD
payload_rows = 3 * HD + 16
vmem_limit = 48 * 2**20


def normalize(values):
    centred = values - jnp.mean(values, axis=-1, keepdims=True)
    inverse = lax.rsqrt(jnp.mean(centred * centred, axis=-1, keepdims=True) + eps)
    return (centred * inverse, inverse)


def normalize_back(grad_unit, unit, inverse):
    return inverse * (
        grad_unit
        - jnp.mean(grad_unit, axis=-1, keepdims=True)
        - unit * jnp.mean(grad_unit * unit, axis=-1, keepdims=True)
    )


def product(first, second, first_axis=1, second_axis=0):
    return lax.dot_general(
        first,
        second,
        (((first_axis,), (second_axis,)), ((), ())),
        preferred_element_type=jnp.float32,
    )


def exact_gelu(values):
    return jax.nn.gelu(values, approximate=False)


def load_keys(pieces, crops, keys, key_t, value_t, value_n):
    start = 0
    for piece in pieces:
        chips, _, patches = piece.shape
        for chip in range(chips):
            crop = lax.broadcasted_iota(jnp.int32, (HD, patches), 0)
            segment = piece[chip, pl.ds(seg_row, 16), :].astype(F32)[:1].astype(jnp.int32)
            mask = jnp.where((crop != segment) & (crop < crops), masked_value, 0.0)
            key = piece[chip, pl.ds(HD, HD), :]
            value = piece[chip, pl.ds(2 * HD, HD), :]
            place = pl.ds(start, patches)
            keys[place, :] = jnp.concatenate([key.astype(F32), mask], axis=0).T.astype(BF16)
            if key_t is not None:
                key_t[:, place] = key
            if value_t is not None:
                value_t[pl.ds(0, HD), place] = value
                value_t[pl.ds(HD, 16), place] = jnp.ones((16, patches), BF16)
            if value_n is not None:
                value_n[place, :] = value.astype(F32).T.astype(BF16)
            start += patches


def masked_query(query_ref):
    query = query_ref[0, pl.ds(0, HD), :].astype(F32) * 0.125
    segment = query_ref[0, pl.ds(seg_row, 16), :].astype(F32)[:1].astype(jnp.int32)
    crop = lax.broadcasted_iota(jnp.int32, query.shape, 0)
    onehot = jnp.where(crop == segment, 1.0, 0.0)
    return jnp.concatenate([query, onehot], axis=0).astype(BF16)


def forward_kernel(crops, step, query_ref, own, other, raw_ref, out_ref, logsum_ref, keys, value_t):
    @pl.when(pl.program_id(0) == 0)
    def _():
        load_keys((own, other), crops, keys, None, value_t, None)

    query = masked_query(query_ref)
    count = query.shape[1]
    top = jnp.full((1, count), masked_value, F32)
    accum = jnp.zeros((HD + 16, count), F32)
    for start in range(0, keys.shape[0], step):
        scores = product(keys[pl.ds(start, step), :], query)
        new_top = jnp.maximum(top, jnp.max(scores, axis=0, keepdims=True))
        weights = jnp.exp(scores - new_top).astype(BF16)
        accum = accum * jnp.exp(top - new_top) + product(value_t[:, pl.ds(start, step)], weights)
        top = new_top
    total = accum[HD : HD + 1]
    raw = accum[:HD] / total
    raw_ref[0] = raw
    out_ref[0] = raw.astype(BF16)
    logsum_ref[0] = top + jnp.log(total)


def backward_kernel(
    crops,
    query_ref,
    grad_ref,
    raw_ref,
    logsum_ref,
    before_ref,
    piece,
    dquery_ref,
    sums_ref,
    keys,
    key_t,
    value_n,
    sums,
):
    group = pl.program_id(0)

    @pl.when(group == 0)
    def _():
        load_keys((piece,), crops, keys, key_t, None, value_n)
        sums[...] = jnp.zeros_like(sums)

    query = masked_query(query_ref)
    grad = grad_ref[0]
    grad_wide = grad.astype(F32)
    delta = jnp.sum(grad_wide * raw_ref[0], axis=0, keepdims=True)
    scaled = query_ref[0, pl.ds(0, HD), :].astype(F32) * 0.125
    zero = jnp.zeros_like(scaled)
    query_side = jnp.concatenate([scaled, zero], axis=0).T.astype(BF16)
    grad_side = jnp.concatenate([zero, grad_wide], axis=0).T.astype(BF16)
    probs = jnp.exp(product(keys[...], query) - logsum_ref[0])
    dprobs = product(value_n[...], grad)
    dscores = (probs * (dprobs - delta)).astype(BF16)
    sums[...] += product(dscores, query_side) + product(probs.astype(BF16), grad_side)
    dquery = product(key_t[...], dscores) * 0.125
    if before_ref is not None:
        dquery = before_ref[0] + dquery
    dquery_ref[0] = dquery.astype(dquery_ref.dtype)

    @pl.when(group == pl.num_programs(0) - 1)
    def _():
        chips, _, patches = sums_ref.shape
        for chip in range(chips):
            sums_ref[chip] = sums[pl.ds(chip * patches, patches), :].T.astype(sums_ref.dtype)


def key_step(count):
    return 1024 if count % 1024 == 0 else 256


def query_spec(rows, patches):
    return pl.BlockSpec((1, rows, patches), lambda group: (group, 0, 0))


def whole_spec(shape):
    return pl.BlockSpec(shape, lambda group: (0,) * len(shape))


def attention_forward(queries, own, other, crops):
    groups, _, patches = queries.shape
    count = 2 * own.shape[0] * own.shape[2]
    return pl.pallas_call(
        functools.partial(forward_kernel, crops, key_step(count)),
        grid=(groups,),
        in_specs=[
            query_spec(payload_rows, patches),
            whole_spec(own.shape),
            whole_spec(other.shape),
        ],
        out_specs=[query_spec(HD, patches), query_spec(HD, patches), query_spec(1, patches)],
        out_shape=[
            jax.ShapeDtypeStruct((groups, HD, patches), F32),
            jax.ShapeDtypeStruct((groups, HD, patches), BF16),
            jax.ShapeDtypeStruct((groups, 1, patches), F32),
        ],
        scratch_shapes=[pltpu.VMEM((count, 2 * HD), BF16), pltpu.VMEM((HD + 16, count), BF16)],
        compiler_params=pltpu.CompilerParams(vmem_limit_bytes=vmem_limit),
        cost_estimate=pl.CostEstimate(
            flops=groups * patches * count * 2 * 1024,
            bytes_accessed=4 * 2**20,
            transcendentals=groups * patches * count,
        ),
        name="attention_forward",
    )(queries, own, other)


def backward_piece(queries, grads, raw, logsum, before, keys, index, pieces, crops, sums_type, last):
    groups, _, patches = queries.shape
    chips = keys.shape[0] // pieces
    count = chips * keys.shape[2]
    sums_shape = (chips, 2 * HD, keys.shape[2])
    earlier = [] if before is None else [before]
    body = functools.partial(backward_kernel, crops)
    if before is None:
        body = lambda *refs: backward_kernel(crops, *refs[:4], None, *refs[4:])
    return pl.pallas_call(
        body,
        grid=(groups,),
        in_specs=[
            query_spec(payload_rows, patches),
            query_spec(HD, patches),
            query_spec(HD, patches),
            query_spec(1, patches),
        ]
        + [query_spec(HD, patches)] * len(earlier)
        + [pl.BlockSpec((chips,) + keys.shape[1:], lambda group: (index, 0, 0))],
        out_specs=[query_spec(HD, patches), whole_spec(sums_shape)],
        out_shape=[
            jax.ShapeDtypeStruct((groups, HD, patches), BF16 if last else F32),
            jax.ShapeDtypeStruct(sums_shape, sums_type),
        ],
        scratch_shapes=[
            pltpu.VMEM((count, 2 * HD), BF16),
            pltpu.VMEM((HD, count), BF16),
            pltpu.VMEM((count, HD), BF16),
            pltpu.VMEM((count, 2 * HD), F32),
        ],
        compiler_params=pltpu.CompilerParams(vmem_limit_bytes=vmem_limit),
        cost_estimate=pl.CostEstimate(
            flops=groups * patches * count * 2 * 2048,
            bytes_accessed=4 * 2**20,
            transcendentals=groups * patches * count,
        ),
        name="attention_backward",
    )(queries, grads, raw, logsum, *earlier, keys)


def swap_cores(values):
    return lax.ppermute(values, "core", [(0, 1), (1, 0)])


def to_heads(blocks):
    return lax.all_to_all(blocks, "chip", 0, 0, tiled=True)


def scatter_queries(values, heads, split):
    rows, patches = values.shape[0] // heads, values.shape[1]
    if split == 1:
        return to_heads(values.reshape(heads, rows, patches))
    part = patches // split
    blocks = values.reshape(heads, rows, split, part).transpose(0, 2, 1, 3)
    moved = to_heads(blocks.reshape(heads * split, rows, part))
    width = min(256, moved.shape[0] * part)
    joined = moved.transpose(1, 0, 2).reshape(rows, -1, width)
    return joined.transpose(1, 0, 2)


def gather_queries(values, heads, split, patches):
    rows = values.shape[1]
    if split == 1:
        return to_heads(values).reshape(heads * rows, patches)
    part = patches // split
    joined = values.transpose(1, 0, 2).reshape(rows, heads * split, part)
    moved = to_heads(joined.transpose(1, 0, 2)).reshape(heads, split, rows, part)
    return moved.transpose(0, 2, 1, 3).reshape(heads * rows, patches)


def ring_position():
    chips, chip = lax.axis_size("chip"), lax.axis_index("chip")
    return jnp.where(chip % 2 == 0, chip // 2, chips - 1 - chip // 2)


def ring_pairs(direction):
    chips = lax.axis_size("chip")
    order = list(range(0, chips, 2)) + list(range(chips - 1, 0, -2))
    return [(order[at], order[(at + direction) % chips]) for at in range(chips)]


def add_kernel(_, *refs):
    half = len(refs) // 2
    for partial, arrived, output in zip(refs[:2], refs[2:4], refs[4:]) if half == 3 else ():
        output[...] = (arrived[...].astype(F32) + partial[...]).astype(BF16)
    for partial, output in zip(refs[:2], refs[2:]) if half == 2 else ():
        output[...] = partial[...].astype(BF16)


def place_kernel(_, *refs):
    refs = refs[-6:]
    for side in range(2):

        @pl.when(pl.program_id(0) == side)
        def _(side=side):
            refs[4][...] = refs[side][...].astype(F32)
            refs[5][...] = refs[2 + side][...].astype(F32)


class Rings:
    def __init__(self, down, up):
        self.chips, self.partials, self.directions = lax.axis_size("chip"), (down, up), (1, -1)
        self.shapes = [(array.shape[0] // self.chips, array.shape[1]) for array in (down, up)]
        self.step, self.outputs, self.near = 1, [], None
        self.swapping = []
        self.pending = self.send(self.add(()))

    def index(self, step):
        place = ring_position()
        ahead = [(self.chips - direction * step) % self.chips for direction in self.directions]
        return jnp.stack([lax.rem(place + steps, self.chips) for steps in ahead]).astype(jnp.int32)

    def add(self, arrived):
        def local_block(which):
            return pl.BlockSpec(self.shapes[which], lambda at, order: (order[which], 0))

        whole = [pl.BlockSpec(shape, lambda at, order: (0, 0)) for shape in self.shapes]
        return pl.pallas_call(
            add_kernel,
            grid_spec=pltpu.PrefetchScalarGridSpec(
                num_scalar_prefetch=1,
                grid=(1,),
                in_specs=[local_block(0), local_block(1)] + (whole if arrived else []),
                out_specs=whole,
            ),
            out_shape=[jax.ShapeDtypeStruct(shape, BF16) for shape in self.shapes],
            compiler_params=pltpu.CompilerParams(vmem_limit_bytes=vmem_limit),
            name="ring_add",
        )(self.index(self.step), *self.partials, *arrived)

    def send(self, blocks):
        return [
            lax.ppermute(block, "chip", ring_pairs(direction))
            for block, direction in zip(blocks, self.directions)
        ]

    def place(self, near, far, step):
        (tall, columns), (rows, wide) = self.shapes
        chips, core = self.chips, lax.axis_index("core")
        order = jnp.concatenate([self.index(step), core[None].astype(jnp.int32)])
        blocks = [near[0], far[0], near[1], far[1]]

        def side(at, order):
            return jnp.where(at == 0, order[2], 1 - order[2])

        return pl.pallas_call(
            place_kernel,
            grid_spec=pltpu.PrefetchScalarGridSpec(
                num_scalar_prefetch=1,
                grid=(2,),
                in_specs=[pl.BlockSpec(memory_space=pl.ANY)] * len(self.outputs)
                + [pl.BlockSpec(block.shape, lambda at, order: (0, 0)) for block in blocks],
                out_specs=[
                    pl.BlockSpec((tall, columns), lambda at, order: (side(at, order) * chips + order[0], 0)),
                    pl.BlockSpec((rows, wide), lambda at, order: (order[1], side(at, order))),
                ],
            ),
            out_shape=[
                jax.ShapeDtypeStruct((2 * chips * tall, columns), F32),
                jax.ShapeDtypeStruct((chips * rows, 2 * wide), F32),
            ],
            input_output_aliases={1 + at: at for at in range(len(self.outputs))},
            compiler_params=pltpu.CompilerParams(vmem_limit_bytes=vmem_limit),
            name="place",
        )(order, *self.outputs, *blocks)

    def visit(self, values):
        self.pending, self.swapping, self.outputs, values = lax.optimization_barrier(
            (self.pending, self.swapping, self.outputs, values)
        )
        if self.swapping:
            self.outputs = self.place(self.near, self.swapping, self.step - self.chips)
            self.swapping = []
        if self.pending:
            self.step += 1
            blocks, self.pending = self.pending, []
            if self.step <= self.chips:
                blocks = self.add(blocks)
            if self.step < 2 * self.chips - 1:
                self.pending = self.send(blocks)
            if self.step >= self.chips:
                self.near = blocks
                self.swapping = [swap_cores(block) for block in blocks]
        return values

    def finish(self):
        while self.pending or self.swapping:
            self.visit(())
        return self.outputs


def core_half(values, axis, side):
    size = values.shape[axis] // 2
    return lax.dynamic_slice_in_dim(values, side * size, size, axis)


def share_halves(values, axis):
    core = lax.axis_index("core")
    return core_half(values, axis, core), swap_cores(core_half(values, axis, 1 - core))


def head_sum(values):
    low = values.astype(BF16)
    if lax.axis_size("head") == 2:
        return low.astype(F32) + lax.ppermute(low, "head", [(0, 1), (1, 0)]).astype(F32)
    return lax.psum(low, "head").astype(F32)


def whole_head_sum(values):
    if lax.axis_size("head") == 2:
        return values + lax.ppermute(values, "head", [(0, 1), (1, 0)])
    return lax.psum(values, "head")


def ring_position():
    chips, chip = lax.axis_size("chip"), lax.axis_index("chip")
    return jnp.where(chip % 2 == 0, chip // 2, chips - 1 - chip // 2)


def ring_pairs(direction):
    chips = lax.axis_size("chip")
    order = list(range(0, chips, 2)) + list(range(chips - 1, 0, -2))
    return [(order[at], order[(at + direction) % chips]) for at in range(chips)]


class Ring:
    def __init__(self, partial, direction):
        self.chips = lax.axis_size("chip")
        self.partial, self.direction = partial, direction
        self.rows = partial.shape[0] // self.chips
        self.step, self.near, self.far = 1, [], []
        self.pending = [self.send(self.block(1).astype(BF16))]

    def index(self, step):
        ahead = (self.chips - self.direction * step) % self.chips
        return lax.rem(ring_position() + ahead, self.chips)

    def block(self, step):
        return lax.dynamic_slice_in_dim(
            self.partial, self.index(step) * self.rows, self.rows, 0
        )

    def send(self, block):
        return lax.ppermute(block, "chip", ring_pairs(self.direction))

    def advance(self, arrived):
        self.step += 1
        if len(arrived) > 1 or self.step == 2 * self.chips:
            self.far.append(arrived[-1])
        block, self.pending = arrived[0], []
        if self.step <= self.chips:
            block = (block.astype(F32) + self.block(self.step)).astype(BF16)
        if self.step < 2 * self.chips - 1:
            self.pending.append(self.send(block))
        if self.chips <= self.step < 2 * self.chips:
            self.near.append(block)
            self.pending.append(swap_cores(block))


def visit(rings, values):
    pending, values = lax.optimization_barrier(([ring.pending for ring in rings], values))
    for ring, arrived in zip(rings, pending):
        if arrived:
            ring.advance(arrived)
    return values


def place_kernel(_, *refs):
    refs = refs[-6:]
    for side in range(2):

        @pl.when(pl.program_id(0) == side)
        def _(side=side):
            refs[4][...] = refs[side][...].astype(F32)
            refs[5][...] = refs[2 + side][...].astype(F32)


def place(outputs, down, up, at):
    tall, wide = down.near[at].shape, up.near[at].shape
    chips, core = down.chips, lax.axis_index("core")
    blocks = [down.near[at], down.far[at], up.near[at], up.far[at]]
    shapes = [(2 * chips * tall[0], tall[1]), (chips * wide[0], 2 * wide[1])]
    order = jnp.stack([down.index(at), up.index(at), core]).astype(jnp.int32)

    def side(at, order):
        return jnp.where(at == 0, order[2], 1 - order[2])

    return pl.pallas_call(
        place_kernel,
        grid_spec=pltpu.PrefetchScalarGridSpec(
            num_scalar_prefetch=1,
            grid=(2,),
            in_specs=[pl.BlockSpec(memory_space=pl.ANY)] * len(outputs)
            + [pl.BlockSpec(block.shape, lambda at, order: (0, 0)) for block in blocks],
            out_specs=[
                pl.BlockSpec(tall, lambda at, order: (side(at, order) * chips + order[0], 0)),
                pl.BlockSpec(wide, lambda at, order: (order[1], side(at, order))),
            ],
        ),
        out_shape=[jax.ShapeDtypeStruct(shape, F32) for shape in shapes],
        input_output_aliases={1 + at: at for at in range(len(outputs))},
        compiler_params=pltpu.CompilerParams(vmem_limit_bytes=vmem_limit),
        name="place",
    )(order, *outputs, *blocks)


def place_all(down, up):
    outputs = []
    for at in range(down.chips):
        outputs = place(outputs, down, up, at)
    return outputs


def core_half(values, axis, side):
    size = values.shape[axis] // 2
    return lax.dynamic_slice_in_dim(values, side * size, size, axis)


def share_halves(values, axis):
    core = lax.axis_index("core")
    return core_half(values, axis, core), swap_cores(core_half(values, axis, 1 - core))


def head_sum(values):
    low = values.astype(BF16)
    if lax.axis_size("head") == 2:
        return low.astype(F32) + lax.ppermute(low, "head", [(0, 1), (1, 0)]).astype(F32)
    return lax.psum(low, "head").astype(F32)


def whole_head_sum(values):
    if lax.axis_size("head") == 2:
        return values + lax.ppermute(values, "head", [(0, 1), (1, 0)])
    return lax.psum(values, "head")


def band_sum(values):
    values = values + swap_cores(values)
    chips, reach = lax.axis_size("chip"), 1
    while reach < chips:
        pairs = [(chip, chip ^ reach) for chip in range(chips)]
        values = values + lax.ppermute(values, "chip", pairs)
        reach *= 2
    return values


def local(
    block_input,
    out_grad,
    segments,
    lead_steps,
    gain_attn,
    shift_attn,
    lead_weight,
    query_weight,
    key_weight,
    value_weight,
    output_weight,
    output_bias,
    gain_mlp,
    shift_mlp,
    up_weight,
    up_bias,
    down_weight,
    down_bias,
):
    rows = block_input.shape[0]
    heads = query_weight.shape[1] // HD
    width = heads * HD
    chips = lax.axis_size("chip")
    split = chips // heads
    crops = lead_steps.shape[0]
    inputs = block_input.astype(F32)
    unit_attn, inverse_attn = normalize(inputs)
    onehot = (segments[:, None] == jnp.arange(crops, dtype=jnp.int32)[None, :]).astype(F32)
    lead = jnp.sum(onehot * lead_steps.astype(F32)[None, :], axis=1) / 12.0
    attn_in = (unit_attn * gain_attn + shift_attn + lead[:, None] * lead_weight).astype(BF16)
    query, key, value = (
        product(weight, attn_in, 0, 1).astype(BF16).reshape(heads, HD, rows)
        for weight in (query_weight, key_weight, value_weight)
    )
    crop_rows = jnp.broadcast_to(segments.astype(BF16), (heads, 16, rows))
    payload = jnp.concatenate([query, key, value, crop_rows], axis=1)
    if split == 1:
        own = to_heads(payload)
        queries = own
    else:
        queries = scatter_queries(payload.reshape(-1, rows), heads, split)
        own = to_heads(jnp.repeat(payload, split, axis=0))
    other = swap_cores(own)
    if split == 1:
        attn_in_all, other = lax.optimization_barrier((attn_in, other))
        attn_in_all = lax.all_gather(attn_in_all, "chip", axis=0)
    raw, out, logsum = attention_forward(queries, own, other, crops)
    attn_out = gather_queries(out, heads, split, rows)
    branch = head_sum(product(attn_out, output_weight, 0, 0))
    hidden = inputs + branch + output_bias
    unit_mlp, inverse_mlp = normalize(hidden)
    mlp_in = (unit_mlp * gain_mlp + shift_mlp).astype(BF16)
    upper = product(mlp_in, up_weight) + up_bias
    active, gelu_back = jax.vjp(exact_gelu, upper)
    active_low = active.astype(BF16)
    d_active = product(out_grad, down_weight, 1, 1)
    d_upper = gelu_back(d_active)[0].astype(BF16)
    d_mlp = head_sum(product(d_upper, up_weight, 1, 1))
    grad_out = out_grad.astype(F32)
    grad_far, mlp_in_far = swap_cores(out_grad), swap_cores(mlp_in)
    active_near, active_far = share_halves(active_low, 1)
    upper_near, upper_far = share_halves(d_upper, 1)
    rings = Rings(
        product(active_near, out_grad, 0, 0) + product(active_far, grad_far, 0, 0),
        product(mlp_in, upper_near, 0, 0) + product(mlp_in_far, upper_far, 0, 0),
    )
    d_mlp = rings.visit(d_mlp)
    mlp_part, d_mlp = lax.optimization_barrier(
        (product(active_low, down_weight).astype(BF16), d_mlp)
    )
    mlp_out = head_sum(mlp_part)
    d_hidden = grad_out + normalize_back(d_mlp * gain_mlp, unit_mlp, inverse_mlp)
    d_branch = d_hidden.astype(BF16)
    d_attn = product(output_weight, d_branch, 1, 1).astype(BF16)
    d_attn = rings.visit(d_attn)
    grads = scatter_queries(d_attn, heads, split)
    small = jnp.concatenate(
        [
            jnp.sum(d_hidden, axis=0),
            jnp.sum(d_mlp * unit_mlp, axis=0),
            jnp.sum(d_mlp, axis=0),
            jnp.sum(grad_out, axis=0),
            jnp.sum(d_upper.astype(F32), axis=0),
        ]
    )
    model = d_branch.shape[1]
    lines = small.shape[0] // chips
    small = jnp.pad(small.reshape(chips, 1, lines), ((0, 0), (0, 7), (0, model - lines)))
    out_near, out_far = share_halves(attn_out, 0)
    doutput = product(out_near, d_branch) + product(out_far, swap_cores(d_branch))
    doutput = jnp.concatenate([doutput.reshape(chips, -1, model), small], axis=1).astype(BF16)
    pieces = 2
    dquery = None
    far_sums, near_sums = [], []
    for keys, sums, sums_type in ((other, far_sums, BF16), (own, near_sums, F32)):
        for index in range(pieces):
            if keys is own and index == 0:
                doutput = to_heads(doutput)
            last = keys is own and index == pieces - 1
            if not last:
                grads, dquery, doutput = rings.visit((grads, dquery, doutput))
            else:
                grads, dquery, doutput, mlp_out = rings.visit((grads, dquery, doutput, mlp_out))
                doutput = jnp.sum(doutput.astype(F32), axis=0).astype(BF16)
                block_output = (hidden + mlp_out + down_bias).astype(BF16)
            dquery, piece = backward_piece(
                queries, grads, raw, logsum, dquery, keys, index, pieces, crops, sums_type, last
            )
            sums.append(piece)
    key_value = jnp.concatenate(
        [
            (near + swap_cores(far).astype(F32)).astype(BF16)
            for near, far in zip(near_sums, far_sums)
        ]
    )
    if split == 1:
        head_grads = rings.visit(jnp.concatenate([dquery, key_value], axis=1))
        moved = to_heads(head_grads)
        dquery, dkey, dvalue = (
            moved[:, at * HD : at * HD + HD].reshape(width, rows) for at in range(3)
        )
    else:
        dquery = gather_queries(dquery, heads, split, rows)
        moved = to_heads(key_value).reshape(heads, split, 2 * HD, rows).astype(F32)
        moved = jnp.sum(moved, axis=1).astype(BF16)
        dkey, dvalue = (moved[:, at * HD : at * HD + HD].reshape(width, rows) for at in range(2))
        dquery, dkey, dvalue = rings.visit((dquery, dkey, dvalue))
    d_part = (
        product(dquery, query_weight, 0, 1)
        + product(dkey, key_weight, 0, 1)
        + product(dvalue, value_weight, 0, 1)
    )
    if split == 1:
        projections = lax.dot_general(
            head_grads, attn_in_all, (((0, 2), (0, 1)), ((), ())), preferred_element_type=F32
        ).astype(BF16)
        near, far = share_halves(projections, 0)
        projections = (near.astype(F32) + far.astype(F32)).astype(BF16)
        size = projections.shape[0]
        blocks = jnp.concatenate([projections, doutput], axis=0)
        d_part, blocks = rings.visit((d_part, blocks))
    else:
        size, blocks = 0, doutput
        projections = [
            lax.psum(product(attn_in, grad, 0, 1).astype(BF16), ("chip", "core")).astype(F32)
            for grad in (dquery, dkey, dvalue)
        ]
    blocks = lax.all_gather(blocks, ("chip", "core"), axis=0)
    d_in = head_sum(d_part)
    ends = jnp.stack(
        [
            jnp.sum(d_part * unit_attn, axis=0),
            jnp.sum(d_part, axis=0),
            jnp.sum(lead[:, None] * d_part, axis=0),
        ]
    )
    ends = whole_head_sum(ends)
    ends = rings.visit(ends)
    ends = ends + swap_cores(ends)
    reach = 1
    while reach < chips:
        ends = rings.visit(ends)
        pairs = [(chip, chip ^ reach) for chip in range(chips)]
        ends = ends + lax.ppermute(ends, "chip", pairs)
        reach *= 2
    input_grad = (d_hidden + normalize_back(d_in * gain_attn, unit_attn, inverse_attn)).astype(
        BF16
    )
    ddown_weight, dup_weight = rings.finish()
    if split == 1:
        projections = blocks[:, :size].reshape(heads, 3, HD, model)
        projections = [
            projections[:, at].reshape(width, model).T.astype(F32) for at in range(3)
        ]
    blocks = blocks.reshape(chips, 2, -1, model)[:, :, size:]
    doutput_weight = (
        blocks[:, :, :-8].transpose(1, 0, 2, 3).reshape(width, model).astype(F32)
    )
    small = jnp.sum(blocks[:, :, -8, :lines].astype(F32), axis=1).reshape(-1)
    dup_bias = small[4 * model :]
    small = [small[at * model : at * model + model] for at in range(4)]
    return (
        block_output,
        input_grad,
        ends[0],
        ends[1],
        ends[2],
        *projections,
        doutput_weight,
        *small[:3],
        dup_weight,
        dup_bias,
        ddown_weight,
        small[3],
    )


def solution(mesh):
    bands, halves = mesh.shape["band"], mesh.shape["head"]
    inner = Mesh(mesh.devices.reshape(bands // 2, 2, halves), ("chip", "core", "head"))
    band = ("chip", "core")
    rows, columns, split_rows = P(band, None), P(None, "head"), P("head", None)
    return jax.shard_map(
        local,
        mesh=inner,
        in_specs=(
            rows,
            rows,
            P(band),
            P(),
            P(),
            P(),
            P(),
            columns,
            columns,
            columns,
            split_rows,
            P(),
            P(),
            P(),
            columns,
            P("head"),
            split_rows,
            P(),
        ),
        out_specs=(
            rows,
            rows,
            P(),
            P(),
            P(),
            columns,
            columns,
            columns,
            split_rows,
            P(),
            P(),
            P(),
            columns,
            P("head"),
            split_rows,
            P(),
        ),
        check_vma=False,
    )
```

```python
import functools
import math

import jax
import jax.numpy as jnp
from jax import lax
from jax.experimental import pallas as pl
from jax.experimental.pallas import tpu as pltpu
from jax.sharding import Mesh, PartitionSpec as P

HD = 64
F32 = jnp.float32
BF16 = jnp.bfloat16
eps = 1e-05
masked_value = -1e30
seg_row = 3 * HD
payload_rows = 3 * HD + 16
small_rows = 8
params = pltpu.CompilerParams(vmem_limit_bytes=56 * 2**20)


def normalize(values):
    centred = values - jnp.mean(values, axis=-1, keepdims=True)
    inverse = lax.rsqrt(jnp.mean(centred * centred, axis=-1, keepdims=True) + eps)
    return (centred * inverse, inverse)


def normalize_back(grad_unit, unit, inverse):
    return inverse * (
        grad_unit
        - jnp.mean(grad_unit, axis=-1, keepdims=True)
        - unit * jnp.mean(grad_unit * unit, axis=-1, keepdims=True)
    )


def product(first, second, first_axis=1, second_axis=0):
    return lax.dot_general(
        first,
        second,
        (((first_axis,), (second_axis,)), ((), ())),
        preferred_element_type=jnp.float32,
    )


def struct(shape, dtype):
    return jax.ShapeDtypeStruct(shape, dtype)


def whole_spec(shape):
    return pl.BlockSpec(shape, lambda *at: (0,) * len(shape))


def cost(flops, size, exps=0):
    return pl.CostEstimate(flops=flops, bytes_accessed=size, transcendentals=exps)


def project_kernel(
    input_ref, segment_ref, steps_ref, gain, shift, lead_weight, *refs
):
    weights, (payload_ref, attn_in_ref) = refs[:3], refs[3:]
    rows = input_ref.shape[0]

    @pl.when(pl.program_id(0) == 0)
    def _():
        unit, _ = normalize(input_ref[...].astype(F32))
        crops = steps_ref.shape[0]
        crop = lax.broadcasted_iota(jnp.int32, (crops, rows), 0)
        onehot = jnp.where(crop == segment_ref[...], 1.0, 0.0)
        lead = product(onehot, steps_ref[...].astype(F32), 0, 0)[:, :1] / 12.0
        attn_in = unit * gain[...] + shift[...] + lead * lead_weight[...]
        attn_in_ref[...] = attn_in.astype(BF16)

    for at, weight in enumerate(weights):
        part = product(attn_in_ref[...], weight[...]).T.astype(BF16)
        for head in range(2):
            payload_ref[head, pl.ds(at * HD, HD), :] = part[head * HD : head * HD + HD]
    segment = jnp.broadcast_to(segment_ref[...].astype(F32), (16, rows)).astype(BF16)
    for head in range(2):
        payload_ref[head, pl.ds(seg_row, 16), :] = segment


def project(block_input, segments, lead_steps, gain, shift, lead_weight, weights):
    rows, model = block_input.shape
    heads = weights[0].shape[1] // HD
    steps = jnp.broadcast_to(lead_steps[:, None], (lead_steps.shape[0], 128))
    line = whole_spec((1, model))
    column = pl.BlockSpec((model, 2 * HD), lambda at: (0, at))
    return pl.pallas_call(
        project_kernel,
        grid=(heads // 2,),
        in_specs=[whole_spec(block_input.shape), whole_spec((1, rows)), whole_spec(steps.shape)]
        + [line] * 3
        + [column] * 3,
        out_specs=[
            pl.BlockSpec((2, payload_rows, rows), lambda at: (at, 0, 0)),
            whole_spec((rows, model)),
        ],
        out_shape=[struct((heads, payload_rows, rows), BF16), struct((rows, model), BF16)],
        compiler_params=params,
        cost_estimate=cost(2 * rows * model * 3 * heads * HD, 8 * 2**20),
        name="project",
    )(block_input, segments[None], steps, gain[None], shift[None], lead_weight[None], *weights)


def mlp_kernel(count, input_ref, grad_ref, *refs):
    branches, refs = refs[:count], refs[count:]
    output_bias, gain, shift, up_weight, up_bias, down_weight = refs[:6]
    wide_ref, mlp_in_ref, hidden_ref, bias_ref, forward_ref, back_ref, forward, back = refs[6:]
    at = pl.program_id(0)

    @pl.when(at == 0)
    def _():
        hidden = input_ref[...].astype(F32) + output_bias[...]
        for branch in branches:
            hidden += branch[...].astype(F32)
        hidden_ref[...] = hidden
        unit, _ = normalize(hidden)
        mlp_in_ref[...] = (unit * gain[...] + shift[...]).astype(BF16)
        forward[...] = jnp.zeros_like(forward)
        back[...] = jnp.zeros_like(back)

    upper = product(mlp_in_ref[...], up_weight[...]) + up_bias[...]
    share = 0.5 + 0.5 * lax.erf(upper * math.sqrt(0.5))
    slope = share + upper * (jnp.exp(upper * upper * -0.5) * (1.0 / math.sqrt(2.0 * math.pi)))
    active = (upper * share).astype(BF16)
    d_active = product(grad_ref[...], down_weight[...], 1, 1)
    d_upper = (d_active * slope).astype(BF16)
    wide_ref[0] = active
    wide_ref[1] = d_upper
    bias_ref[...] = jnp.sum(d_upper.astype(F32), axis=0, keepdims=True)
    forward[...] += product(active, down_weight[...])
    back[...] += product(d_upper, up_weight[...], 1, 1)

    @pl.when(at == pl.num_programs(0) - 1)
    def _():
        forward_ref[...] = forward[...].astype(BF16)
        back_ref[...] = back[...].astype(BF16)


def mlp(block_input, out_grad, branches, output_bias, gain, shift, up_weight, up_bias, down_weight):
    rows, model = block_input.shape
    units = up_weight.shape[1]
    step = math.gcd(units, 512)
    tile, line = whole_spec((rows, model)), whole_spec((1, model))
    return pl.pallas_call(
        functools.partial(mlp_kernel, len(branches)),
        grid=(units // step,),
        in_specs=[tile] * (2 + len(branches))
        + [line] * 3
        + [
            pl.BlockSpec((model, step), lambda at: (0, at)),
            pl.BlockSpec((1, step), lambda at: (0, at)),
            pl.BlockSpec((step, model), lambda at: (at, 0)),
        ],
        out_specs=[
            pl.BlockSpec((2, rows, step), lambda at: (0, 0, at)),
            tile,
            tile,
            pl.BlockSpec((1, step), lambda at: (0, at)),
            tile,
            tile,
        ],
        out_shape=[
            struct((2, rows, units), BF16),
            struct((rows, model), BF16),
            struct((rows, model), F32),
            struct((1, units), F32),
            struct((rows, model), BF16),
            struct((rows, model), BF16),
        ],
        scratch_shapes=[pltpu.VMEM((rows, model), F32)] * 2,
        compiler_params=params,
        cost_estimate=cost(8 * rows * model * units, 16 * 2**20, 2 * rows * units),
        name="mlp",
    )(
        block_input,
        out_grad,
        *branches,
        output_bias[None],
        gain[None],
        shift[None],
        up_weight,
        up_bias[None],
        down_weight,
    )


def middle_kernel(count, hidden_ref, grad_ref, *refs):
    parts, refs = refs[:count], refs[count:]
    gain, output_weight, d_hidden_ref, d_branch_ref, d_attn_ref, sums_ref = refs
    unit, inverse = normalize(hidden_ref[...])
    d_mlp = parts[0][...].astype(F32)
    for part in parts[1:]:
        d_mlp += part[...].astype(F32)
    grad = grad_ref[...].astype(F32)
    d_hidden = grad + normalize_back(d_mlp * gain[...], unit, inverse)
    d_hidden_ref[...] = d_hidden
    d_branch = d_hidden.astype(BF16)
    d_branch_ref[...] = d_branch
    d_attn_ref[...] = product(output_weight[...], d_branch, 1, 1).astype(BF16)
    for at, values in enumerate((d_hidden, d_mlp * unit, d_mlp, grad)):
        sums_ref[pl.ds(at, 1), :] = jnp.sum(values, axis=0, keepdims=True)


def middle(hidden, out_grad, parts, gain, output_weight):
    rows, model = hidden.shape
    width = output_weight.shape[0]
    return pl.pallas_call(
        functools.partial(middle_kernel, len(parts)),
        out_shape=[
            struct((rows, model), F32),
            struct((rows, model), BF16),
            struct((width, rows), BF16),
            struct((4, model), F32),
        ],
        compiler_params=params,
        cost_estimate=cost(2 * rows * model * width, 6 * 2**20),
        name="middle",
    )(hidden, out_grad, *parts, gain[None], output_weight)


def load_keys(pieces, crops, keys, key_t, value_t, value_n):
    start = 0
    for piece in pieces:
        chips, _, patches = piece.shape
        for chip in range(chips):
            crop = lax.broadcasted_iota(jnp.int32, (HD, patches), 0)
            segment = piece[chip, pl.ds(seg_row, 16), :].astype(F32)[:1].astype(jnp.int32)
            mask = jnp.where((crop != segment) & (crop < crops), masked_value, 0.0)
            key = piece[chip, pl.ds(HD, HD), :]
            value = piece[chip, pl.ds(2 * HD, HD), :]
            place = pl.ds(start, patches)
            keys[place, :] = jnp.concatenate([key.astype(F32), mask], axis=0).T.astype(BF16)
            if key_t is not None:
                key_t[:, place] = key
            if value_t is not None:
                value_t[pl.ds(0, HD), place] = value
                value_t[pl.ds(HD, 16), place] = jnp.ones((16, patches), BF16)
            if value_n is not None:
                value_n[place, :] = value.astype(F32).T.astype(BF16)
            start += patches


def masked_query(query_ref):
    query = query_ref[0, pl.ds(0, HD), :].astype(F32) * 0.125
    segment = query_ref[0, pl.ds(seg_row, 16), :].astype(F32)[:1].astype(jnp.int32)
    crop = lax.broadcasted_iota(jnp.int32, query.shape, 0)
    onehot = jnp.where(crop == segment, 1.0, 0.0)
    return jnp.concatenate([query, onehot], axis=0).astype(BF16)


def forward_kernel(crops, step, query_ref, own, other, raw_ref, out_ref, logsum_ref, keys, value_t):
    @pl.when(pl.program_id(0) == 0)
    def _():
        load_keys((own, other), crops, keys, None, value_t, None)

    query = masked_query(query_ref)
    count = query.shape[1]
    top = jnp.full((1, count), masked_value, F32)
    accum = jnp.zeros((HD + 16, count), F32)
    for start in range(0, keys.shape[0], step):
        scores = product(keys[pl.ds(start, step), :], query)
        new_top = jnp.maximum(top, jnp.max(scores, axis=0, keepdims=True))
        weights = jnp.exp(scores - new_top).astype(BF16)
        accum = accum * jnp.exp(top - new_top) + product(value_t[:, pl.ds(start, step)], weights)
        top = new_top
    total = accum[HD : HD + 1]
    raw = accum[:HD] / total
    raw_ref[0] = raw
    out_ref[0] = raw.astype(BF16)
    logsum_ref[0] = top + jnp.log(total)


def backward_kernel(
    crops,
    before,
    query_ref,
    grad_ref,
    raw_ref,
    logsum_ref,
    *refs,
):
    before_refs, (piece, dquery_ref, sums_ref, keys, key_t, value_n, sums) = (
        refs[:before],
        refs[before:],
    )
    group = pl.program_id(0)

    @pl.when(group == 0)
    def _():
        load_keys((piece,), crops, keys, key_t, None, value_n)
        sums[...] = jnp.zeros_like(sums)

    query = masked_query(query_ref)
    grad = grad_ref[0]
    grad_wide = grad.astype(F32)
    delta = jnp.sum(grad_wide * raw_ref[0], axis=0, keepdims=True)
    scaled = query_ref[0, pl.ds(0, HD), :].astype(F32) * 0.125
    zero = jnp.zeros_like(scaled)
    query_side = jnp.concatenate([scaled, zero], axis=0).T.astype(BF16)
    grad_side = jnp.concatenate([zero, grad_wide], axis=0).T.astype(BF16)
    probs = jnp.exp(product(keys[...], query) - logsum_ref[0])
    dprobs = product(value_n[...], grad)
    dscores = (probs * (dprobs - delta)).astype(BF16)
    sums[...] += product(dscores, query_side) + product(probs.astype(BF16), grad_side)
    dquery = product(key_t[...], dscores) * 0.125
    for ref in before_refs:
        dquery = ref[0] + dquery
    dquery_ref[0] = dquery.astype(dquery_ref.dtype)

    @pl.when(group == pl.num_programs(0) - 1)
    def _():
        chips, _, patches = sums_ref.shape
        for chip in range(chips):
            sums_ref[chip] = sums[pl.ds(chip * patches, patches), :].T.astype(sums_ref.dtype)


def key_step(count):
    return 1024 if count % 1024 == 0 else 256


def query_spec(rows, patches):
    return pl.BlockSpec((1, rows, patches), lambda group: (group, 0, 0))


def attention_forward(queries, own, other, crops):
    groups, _, patches = queries.shape
    count = 2 * own.shape[0] * own.shape[2]
    return pl.pallas_call(
        functools.partial(forward_kernel, crops, key_step(count)),
        grid=(groups,),
        in_specs=[
            query_spec(payload_rows, patches),
            whole_spec(own.shape),
            whole_spec(other.shape),
        ],
        out_specs=[query_spec(HD, patches), query_spec(HD, patches), query_spec(1, patches)],
        out_shape=[
            struct((groups, HD, patches), F32),
            struct((groups, HD, patches), BF16),
            struct((groups, 1, patches), F32),
        ],
        scratch_shapes=[pltpu.VMEM((count, 2 * HD), BF16), pltpu.VMEM((HD + 16, count), BF16)],
        compiler_params=params,
        cost_estimate=cost(
            groups * patches * count * 4096, 4 * 2**20, groups * patches * count
        ),
        name="attention_forward",
    )(queries, own, other)


def backward_piece(queries, grads, raw, logsum, before, keys, index, pieces, crops, sums_type, last):
    groups, _, patches = queries.shape
    chips = keys.shape[0] // pieces
    count = chips * keys.shape[2]
    sums_shape = (chips, 2 * HD, keys.shape[2])
    return pl.pallas_call(
        functools.partial(backward_kernel, crops, len(before)),
        grid=(groups,),
        in_specs=[
            query_spec(payload_rows, patches),
            query_spec(HD, patches),
            query_spec(HD, patches),
            query_spec(1, patches),
        ]
        + [query_spec(HD, patches)] * len(before)
        + [pl.BlockSpec((chips,) + keys.shape[1:], lambda group: (index, 0, 0))],
        out_specs=[query_spec(HD, patches), whole_spec(sums_shape)],
        out_shape=[
            struct((groups, HD, patches), BF16 if last else F32),
            struct(sums_shape, sums_type),
        ],
        scratch_shapes=[
            pltpu.VMEM((count, 2 * HD), BF16),
            pltpu.VMEM((HD, count), BF16),
            pltpu.VMEM((count, HD), BF16),
            pltpu.VMEM((count, 2 * HD), F32),
        ],
        compiler_params=params,
        cost_estimate=cost(
            groups * patches * count * 4096, 4 * 2**20, groups * patches * count
        ),
        name="attention_backward",
    )(queries, grads, raw, logsum, *before, keys)


def swap_cores(values):
    return lax.ppermute(values, "core", [(0, 1), (1, 0)])


def to_heads(blocks):
    return lax.all_to_all(blocks, "chip", 0, 0, tiled=True)


def scatter_queries(values, heads, split):
    rows, patches = values.shape[0] // heads, values.shape[1]
    if split == 1:
        return to_heads(values.reshape(heads, rows, patches))
    part = patches // split
    blocks = values.reshape(heads, rows, split, part).transpose(0, 2, 1, 3)
    moved = to_heads(blocks.reshape(heads * split, rows, part))
    width = min(256, moved.shape[0] * part)
    joined = moved.transpose(1, 0, 2).reshape(rows, -1, width)
    return joined.transpose(1, 0, 2)


def gather_queries(values, heads, split, patches):
    rows = values.shape[1]
    if split == 1:
        return to_heads(values).reshape(heads * rows, patches)
    part = patches // split
    joined = values.transpose(1, 0, 2).reshape(rows, heads * split, part)
    moved = to_heads(joined.transpose(1, 0, 2)).reshape(heads, split, rows, part)
    return moved.transpose(0, 2, 1, 3).reshape(heads * rows, patches)


def across_heads(part):
    if lax.axis_size("head") == 2:
        return [part, lax.ppermute(part, "head", [(0, 1), (1, 0)])]
    return [lax.psum(part, "head")]


def ring_position():
    chips, chip = lax.axis_size("chip"), lax.axis_index("chip")
    return jnp.where(chip % 2 == 0, chip // 2, chips - 1 - chip // 2)


def ring_order():
    chips = lax.axis_size("chip")
    return list(range(0, chips, 2)) + list(range(chips - 1, 0, -2))


def ring_pairs(direction):
    order = ring_order()
    return [(order[at], order[(at + direction) % len(order)]) for at in range(len(order))]


def visit(streams, values):
    states, values = lax.optimization_barrier(([stream.state for stream in streams], values))
    for stream, state in zip(streams, states):
        stream.state = state
        stream.advance()
    return values


class Gather:
    def __init__(self, block):
        self.chips = lax.axis_size("chip")
        self.blocks = [(0, block)]
        self.step = 0
        self.state = []
        self.send([block, block])

    def send(self, arrived):
        self.step += 1
        reach = [self.chips // 2, (self.chips - 1) // 2]
        self.state = [
            lax.ppermute(block, "chip", ring_pairs(direction))
            for block, direction, steps in zip(arrived, (1, -1), reach)
            if self.step <= steps
        ]

    def advance(self):
        arrived = self.state
        for block, direction in zip(arrived, (-1, 1)):
            self.blocks.append((direction * self.step, block))
        self.send(arrived)

    def order(self):
        table = jnp.array(ring_order(), jnp.int32)
        steps = jnp.array([step for step, _ in self.blocks], jnp.int32)
        return table[(ring_position() + steps + self.chips) % self.chips]


def partial_kernel(core, grad, mlp_in, wide, grad_far, mlp_in_far, wide_far, out_ref):
    is_down = core[0] == 0

    @pl.when(is_down)
    def _():
        out_ref[...] = (
            product(wide[0], grad[...], 0, 0) + product(wide_far[...], grad_far[...], 0, 0)
        ).astype(BF16)

    @pl.when(jnp.logical_not(is_down))
    def _():
        out_ref[...] = (
            product(mlp_in[...], wide[0], 0, 0) + product(mlp_in_far[...], wide_far[...], 0, 0)
        ).astype(BF16)


def weight_partial(core, grad, mlp_in, wide, grad_far, mlp_in_far, wide_far):
    rows, model = grad.shape
    units = wide.shape[2]
    half = units // 2
    tile = whole_spec((rows, model))
    if model != half:
        down = product(wide[0], grad, 0, 0) + product(wide_far, grad_far, 0, 0)
        down = down.reshape(2, half, model).transpose(1, 0, 2).reshape(model, units)
        up = product(mlp_in, wide[1], 0, 0) + product(mlp_in_far, wide_far, 0, 0)
        return jnp.where(core == 0, down, up).astype(BF16)
    return pl.pallas_call(
        partial_kernel,
        grid_spec=pltpu.PrefetchScalarGridSpec(
            num_scalar_prefetch=1,
            grid=(2,),
            in_specs=[
                tile,
                tile,
                pl.BlockSpec((1, rows, half), lambda at, core: (core[0], 0, at)),
                tile,
                tile,
                pl.BlockSpec((rows, half), lambda at, core: (0, at)),
            ],
            out_specs=pl.BlockSpec((model, half), lambda at, core: (0, at)),
        ),
        out_shape=struct((model, units), BF16),
        compiler_params=params,
        cost_estimate=cost(4 * rows * model * units, 12 * 2**20),
        name="weight_partial",
    )(core[None], grad, mlp_in, wide, grad_far, mlp_in_far, wide_far)


def add_kernel(_, partial, arrived, output):
    output[...] = (arrived[...].astype(F32) + partial[...].astype(F32)).astype(BF16)


def place_kernel(order, *refs):
    near, far, down, up = refs[-4:]
    half = down.shape[2]

    def put(first, second):
        for side in range(2):
            down[side] = first[:, pl.ds(side * half, half)].astype(F32)
        up[...] = second[...].astype(F32)

    pl.when(order[2] == 0)(lambda: put(near, far))
    pl.when(order[2] != 0)(lambda: put(far, near))


class Ring:
    def __init__(self, partial, core):
        self.chips, self.partial, self.core = lax.axis_size("chip"), partial, core
        self.shape = (partial.shape[0] // self.chips, partial.shape[1])
        self.step, self.near = 1, None
        order, count = ring_order(), self.chips
        self.pairs = []
        for at in range(count):
            self.pairs.append((2 * order[at], 2 * order[(at + 1) % count]))
            self.pairs.append((2 * order[at] + 1, 2 * order[(at - 1) % count] + 1))
        block = lax.dynamic_slice_in_dim(partial, self.index() * self.shape[0], self.shape[0], 0)
        self.state = (self.send(block), [], [])

    def index(self, direction=None):
        if direction is None:
            direction = 1 - 2 * self.core
        return lax.rem(ring_position() + self.chips * 2 - direction * self.step, self.chips)

    def send(self, block):
        return [lax.ppermute(block, ("chip", "core"), self.pairs)]

    def add(self, block):
        whole = pl.BlockSpec(self.shape, lambda at, order: (0, 0))
        return pl.pallas_call(
            add_kernel,
            grid_spec=pltpu.PrefetchScalarGridSpec(
                num_scalar_prefetch=1,
                grid=(1,),
                in_specs=[pl.BlockSpec(self.shape, lambda at, order: (order[0], 0)), whole],
                out_specs=whole,
            ),
            out_shape=struct(self.shape, BF16),
            compiler_params=params,
            name="ring_add",
        )(self.index()[None].astype(jnp.int32), self.partial, block)

    def place(self, far, outputs):
        rows, columns = self.shape
        half = columns // 2
        order = jnp.stack([self.index(1), self.index(-1), self.core]).astype(jnp.int32)
        block = pl.BlockSpec(self.shape, lambda at, order: (0, 0))
        return pl.pallas_call(
            place_kernel,
            grid_spec=pltpu.PrefetchScalarGridSpec(
                num_scalar_prefetch=1,
                grid=(1,),
                in_specs=[pl.BlockSpec(memory_space=pl.ANY)] * len(outputs) + [block] * 2,
                out_specs=[
                    pl.BlockSpec((2, rows, half), lambda at, order: (0, order[0], 0)),
                    pl.BlockSpec((rows, columns), lambda at, order: (order[1], 0)),
                ],
            ),
            out_shape=[
                struct((2, self.chips * rows, half), F32),
                struct((self.chips * rows, columns), F32),
            ],
            input_output_aliases={1 + at: at for at in range(len(outputs))},
            compiler_params=params,
            name="place",
        )(order, *outputs, self.near, far)

    def advance(self):
        flying, swapped, outputs = self.state
        if swapped:
            outputs = self.place(swapped[0], outputs)
            swapped = []
        if flying:
            self.step += 1
            block, flying = flying[0], []
            if self.step <= self.chips:
                block = self.add(block)
            if self.step < 2 * self.chips - 1:
                flying = self.send(block)
            if self.step >= self.chips:
                self.near = block
                swapped = [swap_cores(block)]
        self.state = (flying, swapped, outputs)

    def busy(self):
        return bool(self.state[0] or self.state[1])


class Doubling:
    def __init__(self, values):
        chips = lax.axis_size("chip")
        self.moves = [lambda v: swap_cores(v)]
        reach = 1
        while reach < chips:
            pairs = [(chip, chip ^ reach) for chip in range(chips)]
            self.moves.append(functools.partial(lax.ppermute, axis_name="chip", perm=pairs))
            reach *= 2
        parts = across_heads(values)
        self.state = (parts[0], parts[1:])

    def advance(self):
        values, arrived = self.state
        for part in arrived:
            values = values + part
        self.state = (values, [self.moves.pop(0)(values)] if self.moves else [])

    def busy(self):
        return bool(self.state[1])


def head_gradient_kernel(count, order, query_ref, key_value_ref, *refs):
    blocks, (out_ref, accum) = refs[:count], refs[count:]
    at = pl.program_id(0)

    @pl.when(at == 0)
    def _():
        accum[...] = jnp.zeros_like(accum)

    grads = jnp.concatenate([query_ref[0], key_value_ref[0]], axis=0)
    for index, block in enumerate(blocks):

        @pl.when(at == index)
        def _(block=block):
            accum[...] += product(grads, block[...])

    @pl.when(at == count - 1)
    def _():
        out_ref[...] = accum[...].astype(BF16)


def head_gradient(dquery, key_value, inputs):
    count, rows, patches = dquery.shape
    blocks = [block for _, block in inputs.blocks]
    model = blocks[0].shape[1]
    return pl.pallas_call(
        functools.partial(head_gradient_kernel, count),
        grid_spec=pltpu.PrefetchScalarGridSpec(
            num_scalar_prefetch=1,
            grid=(count,),
            in_specs=[
                pl.BlockSpec((1, rows, patches), lambda at, order: (order[at], 0, 0)),
                pl.BlockSpec((1, 2 * rows, patches), lambda at, order: (order[at], 0, 0)),
            ]
            + [pl.BlockSpec((patches, model), lambda at, order: (0, 0))] * count,
            out_specs=pl.BlockSpec((3 * rows, model), lambda at, order: (0, 0)),
            scratch_shapes=[pltpu.VMEM((3 * rows, model), F32)],
        ),
        out_shape=struct((3 * rows, model), BF16),
        compiler_params=params,
        cost_estimate=cost(6 * rows * count * patches * model, 6 * 2**20),
        name="head_gradient",
    )(inputs.order(), dquery, key_value, *blocks)


def layout_kernel(count, size, order, *refs):
    near, far, outputs, (held,) = (
        refs[:count],
        refs[count : 2 * count],
        refs[2 * count : 2 * count + 3],
        refs[2 * count + 3 :],
    )
    at = pl.program_id(0)

    @pl.when(at == 0)
    def _():
        core = order[count]
        for index in range(count):
            head = order[index]
            for side, blocks in ((core, near), (1 - core, far)):
                held[head, side] = blocks[index][pl.ds(0, size), :]

    pair = [
        jnp.concatenate([held[2 * at + head, 0], held[2 * at + head, 1]], axis=0)
        for head in range(2)
    ]
    for index, output in enumerate(outputs):
        rows = [part[index * HD : index * HD + HD] for part in pair]
        output[...] = jnp.concatenate(rows, axis=0).astype(F32).T


def projection_outputs(gathered, far, core, size):
    count = gathered.chips
    blocks = [block for _, block in gathered.blocks]
    rows, model = blocks[0].shape
    order = jnp.concatenate([gathered.order(), core[None].astype(jnp.int32)])
    return pl.pallas_call(
        functools.partial(layout_kernel, count, size),
        grid_spec=pltpu.PrefetchScalarGridSpec(
            num_scalar_prefetch=1,
            grid=(count // 2,),
            in_specs=[pl.BlockSpec((rows, model), lambda at, order: (0, 0))] * (2 * count),
            out_specs=[pl.BlockSpec((model, 2 * HD), lambda at, order: (0, at))] * 3,
            scratch_shapes=[pltpu.VMEM((count, 2, size, model), BF16)],
        ),
        out_shape=[struct((model, count * HD), F32)] * 3,
        compiler_params=params,
        name="projection_outputs",
    )(order, *blocks, *far)


def core_half(values, axis, side):
    size = values.shape[axis] // 2
    return lax.dynamic_slice_in_dim(values, side * size, size, axis)


def share_halves(values, axis):
    core = lax.axis_index("core")
    return core_half(values, axis, core), swap_cores(core_half(values, axis, 1 - core))


def local(
    block_input,
    out_grad,
    segments,
    lead_steps,
    gain_attn,
    shift_attn,
    lead_weight,
    query_weight,
    key_weight,
    value_weight,
    output_weight,
    output_bias,
    gain_mlp,
    shift_mlp,
    up_weight,
    up_bias,
    down_weight,
    down_bias,
):
    rows, model = block_input.shape
    heads = query_weight.shape[1] // HD
    width = heads * HD
    chips, core = lax.axis_size("chip"), lax.axis_index("core")
    split = chips // heads
    crops = lead_steps.shape[0]
    weights = (query_weight, key_weight, value_weight)
    payload, attn_in = project(
        block_input, segments, lead_steps, gain_attn, shift_attn, lead_weight, weights
    )
    if split == 1:
        own = to_heads(payload)
        queries = own
    else:
        queries = scatter_queries(payload.reshape(-1, rows), heads, split)
        own = to_heads(jnp.repeat(payload, split, axis=0))
    own, attn_in = lax.optimization_barrier((own, attn_in))
    inputs = Gather(attn_in)
    grad_far = swap_cores(out_grad)
    raw, out, logsum = attention_forward(queries, own, swap_cores(own), crops)
    other = swap_cores(own)
    attn_out = gather_queries(out, heads, split, rows)
    attn_out = visit([inputs], attn_out)
    branches = across_heads(product(attn_out, output_weight, 0, 0).astype(BF16))
    branches = visit([inputs], branches)
    wide, mlp_in, hidden, dup_bias, mlp_part, d_mlp_part = mlp(
        block_input,
        out_grad,
        branches,
        output_bias,
        gain_mlp,
        shift_mlp,
        up_weight,
        up_bias,
        down_weight,
    )
    wide, mlp_in, d_mlp_part = visit([inputs], (wide, mlp_in, d_mlp_part))
    d_mlp = across_heads(d_mlp_part)
    mlp_in_far = swap_cores(mlp_in)
    wide_far = swap_cores(lax.dynamic_index_in_dim(wide, 1 - core, 0, keepdims=False))
    ring = Ring(
        weight_partial(core, out_grad, mlp_in, wide, grad_far, mlp_in_far, wide_far), core
    )
    d_mlp = visit([ring, inputs], d_mlp)
    mlp_part, d_mlp = lax.optimization_barrier((mlp_part, d_mlp))
    mlp_out = across_heads(mlp_part)
    d_hidden, d_branch, d_attn, sums = middle(hidden, out_grad, d_mlp, gain_mlp, output_weight)
    d_branch_far = swap_cores(d_branch)
    d_attn = visit([ring], d_attn)
    grads = scatter_queries(d_attn, heads, split)
    small = jnp.concatenate([sums.reshape(-1), dup_bias[0]])
    lines = small.shape[0] // chips
    small = jnp.pad(
        small.reshape(chips, 1, lines), ((0, 0), (0, small_rows - 1), (0, model - lines))
    )
    out_near, out_far = share_halves(attn_out, 0)
    doutput = product(out_near, d_branch) + product(out_far, d_branch_far)
    doutput = jnp.concatenate([doutput.reshape(chips, -1, model), small], axis=1).astype(BF16)
    pieces = 2
    dquery = []
    far_sums, near_sums = [], []
    for keys, piece_sums, sums_type in ((other, far_sums, BF16), (own, near_sums, F32)):
        for index in range(pieces):
            if keys is own and index == 0:
                doutput = to_heads(doutput)
            last = keys is own and index == pieces - 1
            if not last:
                grads, dquery, doutput = visit([ring], (grads, dquery, doutput))
            else:
                grads, dquery, doutput, mlp_out = visit([ring], (grads, dquery, doutput, mlp_out))
                doutput = jnp.sum(doutput.astype(F32), axis=0).astype(BF16)
                block_output = hidden + down_bias
                for part in mlp_out:
                    block_output += part.astype(F32)
                block_output = block_output.astype(BF16)
            *dquery, piece = backward_piece(
                queries, grads, raw, logsum, dquery, keys, index, pieces, crops, sums_type, last
            )
            piece_sums.append(piece)
    (dquery,) = dquery
    key_value = jnp.concatenate(
        [
            (near + swap_cores(far).astype(F32)).astype(BF16)
            for near, far in zip(near_sums, far_sums)
        ]
    )
    if split == 1:
        dquery, key_value = visit([ring], (dquery, key_value))
        moved = to_heads(jnp.concatenate([dquery, key_value], axis=1))
        projections = head_gradient(dquery, key_value, inputs)
        near, far = share_halves(projections, 0)
        projections = (near.astype(F32) + far.astype(F32)).astype(BF16)
        size = projections.shape[0]
        blocks = jnp.concatenate([projections, doutput], axis=0)
        dquery, dkey, dvalue = (
            moved[:, at * HD : at * HD + HD].reshape(width, rows) for at in range(3)
        )
    else:
        dquery = gather_queries(dquery, heads, split, rows)
        moved = to_heads(key_value).reshape(heads, split, 2 * HD, rows).astype(F32)
        moved = jnp.sum(moved, axis=1).astype(BF16)
        dkey, dvalue = (moved[:, at * HD : at * HD + HD].reshape(width, rows) for at in range(2))
        size, blocks = 0, doutput
        projections = [
            lax.psum(product(attn_in, grad, 0, 1).astype(BF16), ("chip", "core")).astype(F32)
            for grad in (dquery, dkey, dvalue)
        ]
    dquery, dkey, dvalue, blocks = visit([ring], (dquery, dkey, dvalue, blocks))
    gathered = Gather(blocks)
    d_part = (
        product(dquery, query_weight, 0, 1)
        + product(dkey, key_weight, 0, 1)
        + product(dvalue, value_weight, 0, 1)
    )
    unit_attn, inverse_attn = normalize(block_input.astype(F32))
    onehot = (segments[:, None] == jnp.arange(crops, dtype=jnp.int32)[None, :]).astype(F32)
    lead = jnp.sum(onehot * lead_steps.astype(F32)[None, :], axis=1) / 12.0
    ends = Doubling(
        jnp.stack(
            [
                jnp.sum(d_part * unit_attn, axis=0),
                jnp.sum(d_part, axis=0),
                jnp.sum(lead[:, None] * d_part, axis=0),
            ]
        )
    )
    d_in = across_heads(d_part.astype(BF16))
    d_in = visit([ring, gathered, ends], d_in)
    d_in = functools.reduce(jnp.add, (part.astype(F32) for part in d_in))
    input_grad = (d_hidden + normalize_back(d_in * gain_attn, unit_attn, inverse_attn)).astype(
        BF16
    )
    while ring.busy() or gathered.state or ends.busy():
        visit([ring, gathered, ends], ())
    ddown_weight, dup_weight = ring.state[2]
    ddown_weight = ddown_weight.reshape(-1, model)
    ends = ends.state[0]
    far = [swap_cores(block) for _, block in gathered.blocks]
    if split == 1:
        projections = projection_outputs(gathered, far, core, size)
    position = jnp.argsort(gathered.order())
    blocks = jnp.stack(
        [jnp.stack([block[size:] for _, block in gathered.blocks]), jnp.stack([block[size:] for block in far])]
    )
    blocks = jnp.take(jnp.where(core == 0, blocks, blocks[::-1]), position, axis=1)
    doutput_weight = blocks[:, :, :-small_rows].reshape(width, model).astype(F32)
    small = jnp.sum(blocks[:, :, -small_rows, :lines].astype(F32), axis=0).reshape(-1)
    dup_bias = small[4 * model :]
    small = [small[at * model : at * model + model] for at in range(4)]
    return (
        block_output,
        input_grad,
        ends[0],
        ends[1],
        ends[2],
        *projections,
        doutput_weight,
        *small[:3],
        dup_weight,
        dup_bias,
        ddown_weight,
        small[3],
    )


def solution(mesh):
    bands, halves = mesh.shape["band"], mesh.shape["head"]
    inner = Mesh(mesh.devices.reshape(bands // 2, 2, halves), ("chip", "core", "head"))
    band = ("chip", "core")
    rows, columns, split_rows = P(band, None), P(None, "head"), P("head", None)
    return jax.shard_map(
        local,
        mesh=inner,
        in_specs=(
            rows,
            rows,
            P(band),
            P(),
            P(),
            P(),
            P(),
            columns,
            columns,
            columns,
            split_rows,
            P(),
            P(),
            P(),
            columns,
            P("head"),
            split_rows,
            P(),
        ),
        out_specs=(
            rows,
            rows,
            P(),
            P(),
            P(),
            columns,
            columns,
            columns,
            split_rows,
            P(),
            P(),
            P(),
            columns,
            P("head"),
            split_rows,
            P(),
        ),
        check_vma=False,
    )
```

```python
import functools
import math

import jax
import jax.numpy as jnp
from jax import lax
from jax.experimental import pallas as pl
from jax.experimental.pallas import tpu as pltpu
from jax.sharding import Mesh, PartitionSpec as P

HD = 64
F32 = jnp.float32
BF16 = jnp.bfloat16
eps = 1e-05
masked_value = -1e30
seg_row = 3 * HD
payload_rows = 3 * HD + 16
small_rows = 8
params = pltpu.CompilerParams(vmem_limit_bytes=32 * 2**20)
streaming = pltpu.CompilerParams(vmem_limit_bytes=60 * 2**20)


def normalize(values):
    centred = values - jnp.mean(values, axis=-1, keepdims=True)
    inverse = lax.rsqrt(jnp.mean(centred * centred, axis=-1, keepdims=True) + eps)
    return (centred * inverse, inverse)


def normalize_back(grad_unit, unit, inverse):
    return inverse * (
        grad_unit
        - jnp.mean(grad_unit, axis=-1, keepdims=True)
        - unit * jnp.mean(grad_unit * unit, axis=-1, keepdims=True)
    )


def product(first, second, first_axis=1, second_axis=0):
    return lax.dot_general(
        first,
        second,
        (((first_axis,), (second_axis,)), ((), ())),
        preferred_element_type=jnp.float32,
    )


def struct(shape, dtype):
    return jax.ShapeDtypeStruct(shape, dtype)


def whole_spec(shape):
    return pl.BlockSpec(shape, lambda *at: (0,) * len(shape))


def cost(flops, size, exps=0):
    return pl.CostEstimate(flops=flops, bytes_accessed=size, transcendentals=exps)


def project_kernel(
    input_ref, segment_ref, steps_ref, gain, shift, lead_weight, *refs
):
    weights, (payload_ref, attn_in_ref) = refs[:3], refs[3:]
    rows = input_ref.shape[0]

    @pl.when(pl.program_id(0) == 0)
    def _():
        unit, _ = normalize(input_ref[...].astype(F32))
        crops = steps_ref.shape[0]
        crop = lax.broadcasted_iota(jnp.int32, (crops, rows), 0)
        onehot = jnp.where(crop == segment_ref[...], 1.0, 0.0)
        lead = product(onehot, steps_ref[...].astype(F32), 0, 0)[:, :1] / 12.0
        attn_in = unit * gain[...] + shift[...] + lead * lead_weight[...]
        attn_in_ref[...] = attn_in.astype(BF16)

    for at, weight in enumerate(weights):
        part = product(attn_in_ref[...], weight[...]).T.astype(BF16)
        for head in range(2):
            payload_ref[head, pl.ds(at * HD, HD), :] = part[head * HD : head * HD + HD]
    segment = jnp.broadcast_to(segment_ref[...].astype(F32), (16, rows)).astype(BF16)
    for head in range(2):
        payload_ref[head, pl.ds(seg_row, 16), :] = segment


def project(block_input, segments, lead_steps, gain, shift, lead_weight, weights):
    rows, model = block_input.shape
    heads = weights[0].shape[1] // HD
    steps = jnp.broadcast_to(lead_steps[:, None], (lead_steps.shape[0], 128))
    line = whole_spec((1, model))
    column = pl.BlockSpec((model, 2 * HD), lambda at: (0, at))
    return pl.pallas_call(
        project_kernel,
        grid=(heads // 2,),
        in_specs=[whole_spec(block_input.shape), whole_spec((1, rows)), whole_spec(steps.shape)]
        + [line] * 3
        + [column] * 3,
        out_specs=[
            pl.BlockSpec((2, payload_rows, rows), lambda at: (at, 0, 0)),
            whole_spec((rows, model)),
        ],
        out_shape=[struct((heads, payload_rows, rows), BF16), struct((rows, model), BF16)],
        compiler_params=params,
        cost_estimate=cost(2 * rows * model * 3 * heads * HD, 8 * 2**20),
        name="project",
    )(block_input, segments[None], steps, gain[None], shift[None], lead_weight[None], *weights)


def mlp_kernel(count, input_ref, grad_ref, *refs):
    branches, refs = refs[:count], refs[count:]
    output_bias, gain, shift, up_weight, up_bias, down_weight = refs[:6]
    wide_ref, mlp_in_ref, hidden_ref, bias_ref, forward_ref, back_ref, forward, back = refs[6:]
    at = pl.program_id(0)

    @pl.when(at == 0)
    def _():
        hidden = input_ref[...].astype(F32) + output_bias[...]
        for branch in branches:
            hidden += branch[...].astype(F32)
        hidden_ref[...] = hidden
        unit, _ = normalize(hidden)
        mlp_in_ref[...] = (unit * gain[...] + shift[...]).astype(BF16)
        forward[...] = jnp.zeros_like(forward)
        back[...] = jnp.zeros_like(back)

    upper = product(mlp_in_ref[...], up_weight[...]) + up_bias[...]
    share = 0.5 + 0.5 * lax.erf(upper * math.sqrt(0.5))
    slope = share + upper * (jnp.exp(upper * upper * -0.5) * (1.0 / math.sqrt(2.0 * math.pi)))
    active = (upper * share).astype(BF16)
    d_active = product(grad_ref[...], down_weight[...], 1, 1)
    d_upper = (d_active * slope).astype(BF16)
    wide_ref[0] = active
    wide_ref[1] = d_upper
    bias_ref[...] = jnp.sum(d_upper.astype(F32), axis=0, keepdims=True)
    forward[...] += product(active, down_weight[...])
    back[...] += product(d_upper, up_weight[...], 1, 1)

    @pl.when(at == pl.num_programs(0) - 1)
    def _():
        forward_ref[...] = forward[...].astype(BF16)
        back_ref[...] = back[...].astype(BF16)


def mlp(block_input, out_grad, branches, output_bias, gain, shift, up_weight, up_bias, down_weight):
    rows, model = block_input.shape
    units = up_weight.shape[1]
    step = math.gcd(units, 512)
    tile, line = whole_spec((rows, model)), whole_spec((1, model))
    return pl.pallas_call(
        functools.partial(mlp_kernel, len(branches)),
        grid=(units // step,),
        in_specs=[tile] * (2 + len(branches))
        + [line] * 3
        + [
            pl.BlockSpec((model, step), lambda at: (0, at)),
            pl.BlockSpec((1, step), lambda at: (0, at)),
            pl.BlockSpec((step, model), lambda at: (at, 0)),
        ],
        out_specs=[
            pl.BlockSpec((2, rows, step), lambda at: (0, 0, at)),
            tile,
            tile,
            pl.BlockSpec((1, step), lambda at: (0, at)),
            tile,
            tile,
        ],
        out_shape=[
            struct((2, rows, units), BF16),
            struct((rows, model), BF16),
            struct((rows, model), F32),
            struct((1, units), F32),
            struct((rows, model), BF16),
            struct((rows, model), BF16),
        ],
        scratch_shapes=[pltpu.VMEM((rows, model), F32)] * 2,
        compiler_params=params,
        cost_estimate=cost(8 * rows * model * units, 16 * 2**20, 2 * rows * units),
        name="mlp",
    )(
        block_input,
        out_grad,
        *branches,
        output_bias[None],
        gain[None],
        shift[None],
        up_weight,
        up_bias[None],
        down_weight,
    )


def middle_kernel(count, hidden_ref, grad_ref, *refs):
    parts, refs = refs[:count], refs[count:]
    gain, output_weight, d_hidden_ref, d_branch_ref, d_attn_ref, sums_ref = refs
    unit, inverse = normalize(hidden_ref[...])
    d_mlp = parts[0][...].astype(F32)
    for part in parts[1:]:
        d_mlp += part[...].astype(F32)
    grad = grad_ref[...].astype(F32)
    d_hidden = grad + normalize_back(d_mlp * gain[...], unit, inverse)
    d_hidden_ref[...] = d_hidden
    d_branch = d_hidden.astype(BF16)
    d_branch_ref[...] = d_branch
    d_attn_ref[...] = product(output_weight[...], d_branch, 1, 1).astype(BF16)
    for at, values in enumerate((d_hidden, d_mlp * unit, d_mlp, grad)):
        sums_ref[pl.ds(at, 1), :] = jnp.sum(values, axis=0, keepdims=True)


def middle(hidden, out_grad, parts, gain, output_weight):
    rows, model = hidden.shape
    width = output_weight.shape[0]
    return pl.pallas_call(
        functools.partial(middle_kernel, len(parts)),
        out_shape=[
            struct((rows, model), F32),
            struct((rows, model), BF16),
            struct((width, rows), BF16),
            struct((4, model), F32),
        ],
        compiler_params=params,
        cost_estimate=cost(2 * rows * model * width, 6 * 2**20),
        name="middle",
    )(hidden, out_grad, *parts, gain[None], output_weight)


def load_keys(pieces, crops, keys, key_t, value_t, value_n):
    start = 0
    for piece in pieces:
        chips, _, patches = piece.shape
        for chip in range(chips):
            crop = lax.broadcasted_iota(jnp.int32, (HD, patches), 0)
            segment = piece[chip, pl.ds(seg_row, 16), :].astype(F32)[:1].astype(jnp.int32)
            mask = jnp.where((crop != segment) & (crop < crops), masked_value, 0.0)
            key = piece[chip, pl.ds(HD, HD), :]
            value = piece[chip, pl.ds(2 * HD, HD), :]
            place = pl.ds(start, patches)
            keys[place, :] = jnp.concatenate([key.astype(F32), mask], axis=0).T.astype(BF16)
            if key_t is not None:
                key_t[:, place] = key
            if value_t is not None:
                value_t[pl.ds(0, HD), place] = value
                value_t[pl.ds(HD, 16), place] = jnp.ones((16, patches), BF16)
            if value_n is not None:
                value_n[place, :] = value.astype(F32).T.astype(BF16)
            start += patches


def masked_query(query_ref):
    query = query_ref[0, pl.ds(0, HD), :].astype(F32) * 0.125
    segment = query_ref[0, pl.ds(seg_row, 16), :].astype(F32)[:1].astype(jnp.int32)
    crop = lax.broadcasted_iota(jnp.int32, query.shape, 0)
    onehot = jnp.where(crop == segment, 1.0, 0.0)
    return jnp.concatenate([query, onehot], axis=0).astype(BF16)


def forward_kernel(crops, step, query_ref, own, other, raw_ref, out_ref, logsum_ref, keys, value_t):
    @pl.when(pl.program_id(0) == 0)
    def _():
        load_keys((own, other), crops, keys, None, value_t, None)

    query = masked_query(query_ref)
    count = query.shape[1]
    top = jnp.full((1, count), masked_value, F32)
    accum = jnp.zeros((HD + 16, count), F32)
    for start in range(0, keys.shape[0], step):
        scores = product(keys[pl.ds(start, step), :], query)
        new_top = jnp.maximum(top, jnp.max(scores, axis=0, keepdims=True))
        weights = jnp.exp(scores - new_top).astype(BF16)
        accum = accum * jnp.exp(top - new_top) + product(value_t[:, pl.ds(start, step)], weights)
        top = new_top
    total = accum[HD : HD + 1]
    raw = accum[:HD] / total
    raw_ref[0] = raw
    out_ref[0] = raw.astype(BF16)
    logsum_ref[0] = top + jnp.log(total)


def backward_kernel(
    crops,
    before,
    query_ref,
    grad_ref,
    raw_ref,
    logsum_ref,
    *refs,
):
    before_refs, refs = refs[:before], refs[before:]
    piece, (dquery_ref, sums_ref, keys, key_t, value_n, sums) = refs[0], refs[-6:]
    group = pl.program_id(0)

    @pl.when(group == 0)
    def _():
        load_keys((piece,), crops, keys, key_t, None, value_n)
        sums[...] = jnp.zeros_like(sums)

    query = masked_query(query_ref)
    grad = grad_ref[0]
    grad_wide = grad.astype(F32)
    delta = jnp.sum(grad_wide * raw_ref[0], axis=0, keepdims=True)
    scaled = query_ref[0, pl.ds(0, HD), :].astype(F32) * 0.125
    zero = jnp.zeros_like(scaled)
    query_side = jnp.concatenate([scaled, zero], axis=0).T.astype(BF16)
    grad_side = jnp.concatenate([zero, grad_wide], axis=0).T.astype(BF16)
    probs = jnp.exp(product(keys[...], query) - logsum_ref[0])
    dprobs = product(value_n[...], grad)
    dscores = (probs * (dprobs - delta)).astype(BF16)
    sums[...] += product(dscores, query_side) + product(probs.astype(BF16), grad_side)
    dquery = product(key_t[...], dscores) * 0.125
    for ref in before_refs:
        dquery = ref[0] + dquery
    dquery_ref[0] = dquery.astype(dquery_ref.dtype)

    @pl.when(group == pl.num_programs(0) - 1)
    def _():
        chips, _, patches = sums_ref.shape
        for chip in range(chips):
            sums_ref[chip] = sums[pl.ds(chip * patches, patches), :].T.astype(sums_ref.dtype)


def key_step(count):
    return 1024 if count % 1024 == 0 else 256


def query_spec(rows, patches):
    return pl.BlockSpec((1, rows, patches), lambda group: (group, 0, 0))


def attention_forward(queries, own, other, crops):
    groups, _, patches = queries.shape
    count = 2 * own.shape[0] * own.shape[2]
    return pl.pallas_call(
        functools.partial(forward_kernel, crops, key_step(count)),
        grid=(groups,),
        in_specs=[
            query_spec(payload_rows, patches),
            whole_spec(own.shape),
            whole_spec(other.shape),
        ],
        out_specs=[query_spec(HD, patches), query_spec(HD, patches), query_spec(1, patches)],
        out_shape=[
            struct((groups, HD, patches), F32),
            struct((groups, HD, patches), BF16),
            struct((groups, 1, patches), F32),
        ],
        scratch_shapes=[pltpu.VMEM((count, 2 * HD), BF16), pltpu.VMEM((HD + 16, count), BF16)],
        compiler_params=params,
        cost_estimate=cost(
            groups * patches * count * 4096, 4 * 2**20, groups * patches * count
        ),
        name="attention_forward",
    )(queries, own, other)


def backward_piece(queries, grads, raw, logsum, before, keys, earlier, index, pieces, crops, dtypes):
    groups, _, patches = queries.shape
    chips = keys.shape[0] // pieces
    count = chips * keys.shape[2]
    sums_shape = (chips, 2 * HD, keys.shape[2])
    return pl.pallas_call(
        functools.partial(backward_kernel, crops, len(before)),
        grid=(groups,),
        in_specs=[
            query_spec(payload_rows, patches),
            query_spec(HD, patches),
            query_spec(HD, patches),
            query_spec(1, patches),
        ]
        + [query_spec(HD, patches)] * len(before)
        + [pl.BlockSpec((chips,) + keys.shape[1:], lambda group: (index, 0, 0))]
        + [pl.BlockSpec(memory_space=pl.ANY)] * len(earlier),
        out_specs=[
            query_spec(HD, patches),
            pl.BlockSpec(sums_shape, lambda group: (index, 0, 0)),
        ],
        out_shape=[
            struct((groups, HD, patches), dtypes[0]),
            struct((keys.shape[0],) + sums_shape[1:], dtypes[1]),
        ],
        input_output_aliases={5 + len(before): 1} if earlier else {},
        scratch_shapes=[
            pltpu.VMEM((count, 2 * HD), BF16),
            pltpu.VMEM((HD, count), BF16),
            pltpu.VMEM((count, HD), BF16),
            pltpu.VMEM((count, 2 * HD), F32),
        ],
        compiler_params=params,
        cost_estimate=cost(
            groups * patches * count * 4096, 4 * 2**20, groups * patches * count
        ),
        name="attention_backward",
    )(queries, grads, raw, logsum, *before, keys, *earlier)


def swap_cores(values):
    return lax.ppermute(values, "core", [(0, 1), (1, 0)])


def to_heads(blocks):
    return lax.all_to_all(blocks, "chip", 0, 0, tiled=True)


def scatter_queries(values, heads, split):
    rows, patches = values.shape[0] // heads, values.shape[1]
    if split == 1:
        return to_heads(values.reshape(heads, rows, patches))
    part = patches // split
    blocks = values.reshape(heads, rows, split, part).transpose(0, 2, 1, 3)
    moved = to_heads(blocks.reshape(heads * split, rows, part))
    width = min(256, moved.shape[0] * part)
    joined = moved.transpose(1, 0, 2).reshape(rows, -1, width)
    return joined.transpose(1, 0, 2)


def gather_queries(values, heads, split, patches):
    rows = values.shape[1]
    if split == 1:
        return to_heads(values).reshape(heads * rows, patches)
    part = patches // split
    joined = values.transpose(1, 0, 2).reshape(rows, heads * split, part)
    moved = to_heads(joined.transpose(1, 0, 2)).reshape(heads, split, rows, part)
    return moved.transpose(0, 2, 1, 3).reshape(heads * rows, patches)


def across_heads(part):
    if lax.axis_size("head") == 2:
        return [part, lax.ppermute(part, "head", [(0, 1), (1, 0)])]
    return [lax.psum(part, "head")]


def ring_position():
    chips, chip = lax.axis_size("chip"), lax.axis_index("chip")
    return jnp.where(chip % 2 == 0, chip // 2, chips - 1 - chip // 2)


def ring_order():
    chips = lax.axis_size("chip")
    return list(range(0, chips, 2)) + list(range(chips - 1, 0, -2))


def ring_pairs(direction):
    order = ring_order()
    return [(order[at], order[(at + direction) % len(order)]) for at in range(len(order))]


def visit(streams, values):
    states, values = lax.optimization_barrier(([stream.state for stream in streams], values))
    for stream, state in zip(streams, states):
        stream.state = state
        stream.advance()
    return values


class Gather:
    def __init__(self, block):
        self.chips = lax.axis_size("chip")
        self.blocks = [(0, block)]
        self.step = 0
        self.state = []
        self.send([block, block])

    def send(self, arrived):
        self.step += 1
        reach = [self.chips // 2, (self.chips - 1) // 2]
        self.state = [
            lax.ppermute(block, "chip", ring_pairs(direction))
            for block, direction, steps in zip(arrived, (1, -1), reach)
            if self.step <= steps
        ]

    def advance(self):
        arrived = self.state
        for block, direction in zip(arrived, (-1, 1)):
            self.blocks.append((direction * self.step, block))
        self.send(arrived)

    def order(self):
        table = jnp.array(ring_order(), jnp.int32)
        steps = jnp.array([step for step, _ in self.blocks], jnp.int32)
        return table[(ring_position() + steps + self.chips) % self.chips]


def partial_kernel(core, grad, mlp_in, wide, grad_far, mlp_in_far, wide_far, out_ref):
    is_down = core[0] == 0

    @pl.when(is_down)
    def _():
        out_ref[...] = (
            product(wide[0], grad[...], 0, 0) + product(wide_far[...], grad_far[...], 0, 0)
        ).astype(BF16)

    @pl.when(jnp.logical_not(is_down))
    def _():
        out_ref[...] = (
            product(mlp_in[...], wide[0], 0, 0) + product(mlp_in_far[...], wide_far[...], 0, 0)
        ).astype(BF16)


def weight_partial(core, grad, mlp_in, wide, grad_far, mlp_in_far, wide_far):
    rows, model = grad.shape
    units = wide.shape[2]
    half = units // 2
    tile = whole_spec((rows, model))
    if model != half:
        down = product(wide[0], grad, 0, 0) + product(wide_far, grad_far, 0, 0)
        down = down.reshape(2, half, model).transpose(1, 0, 2).reshape(model, units)
        up = product(mlp_in, wide[1], 0, 0) + product(mlp_in_far, wide_far, 0, 0)
        return jnp.where(core == 0, down, up).astype(BF16)
    return pl.pallas_call(
        partial_kernel,
        grid_spec=pltpu.PrefetchScalarGridSpec(
            num_scalar_prefetch=1,
            grid=(2,),
            in_specs=[
                tile,
                tile,
                pl.BlockSpec((1, rows, half), lambda at, core: (core[0], 0, at)),
                tile,
                tile,
                pl.BlockSpec((rows, half), lambda at, core: (0, at)),
            ],
            out_specs=pl.BlockSpec((model, half), lambda at, core: (0, at)),
        ),
        out_shape=struct((model, units), BF16),
        compiler_params=streaming,
        cost_estimate=cost(4 * rows * model * units, 12 * 2**20),
        name="weight_partial",
    )(core[None], grad, mlp_in, wide, grad_far, mlp_in_far, wide_far)


def add_kernel(_, partial, arrived, output):
    output[...] = (arrived[...].astype(F32) + partial[...].astype(F32)).astype(BF16)


def place_kernel(order, *refs):
    near, far, down, up = refs[-4:]
    half = down.shape[2]

    def put(first, second):
        for side in range(2):
            down[side] = first[:, pl.ds(side * half, half)].astype(F32)
        up[...] = second[...].astype(F32)

    pl.when(order[2] == 0)(lambda: put(near, far))
    pl.when(order[2] != 0)(lambda: put(far, near))


class Ring:
    def __init__(self, partial, core):
        self.chips, self.partial, self.core = lax.axis_size("chip"), partial, core
        self.shape = (partial.shape[0] // self.chips, partial.shape[1])
        self.step, self.near = 1, None
        order, count = ring_order(), self.chips
        self.pairs = []
        for at in range(count):
            self.pairs.append((2 * order[at], 2 * order[(at + 1) % count]))
            self.pairs.append((2 * order[at] + 1, 2 * order[(at - 1) % count] + 1))
        block = lax.dynamic_slice_in_dim(partial, self.index() * self.shape[0], self.shape[0], 0)
        self.state = (self.send(block), [], [])

    def index(self, direction=None):
        if direction is None:
            direction = 1 - 2 * self.core
        return lax.rem(ring_position() + self.chips * 2 - direction * self.step, self.chips)

    def send(self, block):
        return [lax.ppermute(block, ("chip", "core"), self.pairs)]

    def add(self, block):
        whole = pl.BlockSpec(self.shape, lambda at, order: (0, 0))
        return pl.pallas_call(
            add_kernel,
            grid_spec=pltpu.PrefetchScalarGridSpec(
                num_scalar_prefetch=1,
                grid=(1,),
                in_specs=[pl.BlockSpec(self.shape, lambda at, order: (order[0], 0)), whole],
                out_specs=whole,
            ),
            out_shape=struct(self.shape, BF16),
            compiler_params=streaming,
            name="ring_add",
        )(self.index()[None].astype(jnp.int32), self.partial, block)

    def place(self, far, outputs):
        rows, columns = self.shape
        half = columns // 2
        order = jnp.stack([self.index(1), self.index(-1), self.core]).astype(jnp.int32)
        block = pl.BlockSpec(self.shape, lambda at, order: (0, 0))
        return pl.pallas_call(
            place_kernel,
            grid_spec=pltpu.PrefetchScalarGridSpec(
                num_scalar_prefetch=1,
                grid=(1,),
                in_specs=[pl.BlockSpec(memory_space=pl.ANY)] * len(outputs) + [block] * 2,
                out_specs=[
                    pl.BlockSpec((2, rows, half), lambda at, order: (0, order[0], 0)),
                    pl.BlockSpec((rows, columns), lambda at, order: (order[1], 0)),
                ],
            ),
            out_shape=[
                struct((2, self.chips * rows, half), F32),
                struct((self.chips * rows, columns), F32),
            ],
            input_output_aliases={1 + at: at for at in range(len(outputs))},
            compiler_params=streaming,
            name="place",
        )(order, *outputs, self.near, far)

    def advance(self):
        flying, swapped, outputs = self.state
        if swapped:
            outputs = self.place(swapped[0], outputs)
            swapped = []
        if flying:
            self.step += 1
            block, flying = flying[0], []
            if self.step <= self.chips:
                block = self.add(block)
            if self.step < 2 * self.chips - 1:
                flying = self.send(block)
            if self.step >= self.chips:
                self.near = block
                swapped = [swap_cores(block)]
        self.state = (flying, swapped, outputs)

    def busy(self):
        return bool(self.state[0] or self.state[1])


class Doubling:
    def __init__(self, values):
        chips = lax.axis_size("chip")
        self.moves = [lambda v: swap_cores(v)]
        reach = 1
        while reach < chips:
            pairs = [(chip, chip ^ reach) for chip in range(chips)]
            self.moves.append(functools.partial(lax.ppermute, axis_name="chip", perm=pairs))
            reach *= 2
        parts = across_heads(values)
        self.state = (parts[0], parts[1:])

    def advance(self):
        values, arrived = self.state
        for part in arrived:
            values = values + part
        self.state = (values, [self.moves.pop(0)(values)] if self.moves else [])

    def busy(self):
        return bool(self.state[1])


def head_gradient_kernel(count, order, query_ref, key_value_ref, *refs):
    blocks, (out_ref, accum) = refs[:count], refs[count:]
    at = pl.program_id(0)

    @pl.when(at == 0)
    def _():
        accum[...] = jnp.zeros_like(accum)

    grads = jnp.concatenate([query_ref[0], key_value_ref[0]], axis=0)
    for index, block in enumerate(blocks):

        @pl.when(at == index)
        def _(block=block):
            accum[...] += product(grads, block[...])

    @pl.when(at == count - 1)
    def _():
        out_ref[...] = accum[...].astype(BF16)


def head_gradient(dquery, key_value, inputs):
    count, rows, patches = dquery.shape
    blocks = [block for _, block in inputs.blocks]
    model = blocks[0].shape[1]
    return pl.pallas_call(
        functools.partial(head_gradient_kernel, count),
        grid_spec=pltpu.PrefetchScalarGridSpec(
            num_scalar_prefetch=1,
            grid=(count,),
            in_specs=[
                pl.BlockSpec((1, rows, patches), lambda at, order: (order[at], 0, 0)),
                pl.BlockSpec((1, 2 * rows, patches), lambda at, order: (order[at], 0, 0)),
            ]
            + [pl.BlockSpec((patches, model), lambda at, order: (0, 0))] * count,
            out_specs=pl.BlockSpec((3 * rows, model), lambda at, order: (0, 0)),
            scratch_shapes=[pltpu.VMEM((3 * rows, model), F32)],
        ),
        out_shape=struct((3 * rows, model), BF16),
        compiler_params=streaming,
        cost_estimate=cost(6 * rows * count * patches * model, 6 * 2**20),
        name="head_gradient",
    )(inputs.order(), dquery, key_value, *blocks)


def layout_kernel(count, size, order, *refs):
    near, far, outputs, (held,) = (
        refs[:count],
        refs[count : 2 * count],
        refs[2 * count : 2 * count + 3],
        refs[2 * count + 3 :],
    )
    at = pl.program_id(0)

    @pl.when(at == 0)
    def _():
        core = order[count]
        for index in range(count):
            head = order[index]
            for side, blocks in ((core, near), (1 - core, far)):
                held[head, side] = blocks[index][pl.ds(0, size), :]

    pair = [
        jnp.concatenate([held[2 * at + head, 0], held[2 * at + head, 1]], axis=0)
        for head in range(2)
    ]
    for index, output in enumerate(outputs):
        rows = [part[index * HD : index * HD + HD] for part in pair]
        output[...] = jnp.concatenate(rows, axis=0).astype(F32).T


def projection_outputs(gathered, far, core, size):
    count = gathered.chips
    blocks = [block for _, block in gathered.blocks]
    rows, model = blocks[0].shape
    order = jnp.concatenate([gathered.order(), core[None].astype(jnp.int32)])
    return pl.pallas_call(
        functools.partial(layout_kernel, count, size),
        grid_spec=pltpu.PrefetchScalarGridSpec(
            num_scalar_prefetch=1,
            grid=(count // 2,),
            in_specs=[pl.BlockSpec((rows, model), lambda at, order: (0, 0))] * (2 * count),
            out_specs=[pl.BlockSpec((model, 2 * HD), lambda at, order: (0, at))] * 3,
            scratch_shapes=[pltpu.VMEM((count, 2, size, model), BF16)],
        ),
        out_shape=[struct((model, count * HD), F32)] * 3,
        compiler_params=streaming,
        name="projection_outputs",
    )(order, *blocks, *far)


def core_half(values, axis, side):
    size = values.shape[axis] // 2
    return lax.dynamic_slice_in_dim(values, side * size, size, axis)


def share_halves(values, axis):
    core = lax.axis_index("core")
    return core_half(values, axis, core), swap_cores(core_half(values, axis, 1 - core))


def local(
    block_input,
    out_grad,
    segments,
    lead_steps,
    gain_attn,
    shift_attn,
    lead_weight,
    query_weight,
    key_weight,
    value_weight,
    output_weight,
    output_bias,
    gain_mlp,
    shift_mlp,
    up_weight,
    up_bias,
    down_weight,
    down_bias,
):
    rows, model = block_input.shape
    heads = query_weight.shape[1] // HD
    width = heads * HD
    chips, core = lax.axis_size("chip"), lax.axis_index("core")
    split = chips // heads
    crops = lead_steps.shape[0]
    weights = (query_weight, key_weight, value_weight)
    payload, attn_in = project(
        block_input, segments, lead_steps, gain_attn, shift_attn, lead_weight, weights
    )
    if split == 1:
        own = to_heads(payload)
        queries = own
    else:
        queries = scatter_queries(payload.reshape(-1, rows), heads, split)
        own = to_heads(jnp.repeat(payload, split, axis=0))
    own, attn_in = lax.optimization_barrier((own, attn_in))
    inputs = Gather(attn_in)
    grad_far = swap_cores(out_grad)
    raw, out, logsum = attention_forward(queries, own, swap_cores(own), crops)
    other = swap_cores(own)
    attn_out = gather_queries(out, heads, split, rows)
    attn_out = visit([inputs], attn_out)
    branches = across_heads(product(attn_out, output_weight, 0, 0).astype(BF16))
    branches = visit([inputs], branches)
    wide, mlp_in, hidden, dup_bias, mlp_part, d_mlp_part = mlp(
        block_input,
        out_grad,
        branches,
        output_bias,
        gain_mlp,
        shift_mlp,
        up_weight,
        up_bias,
        down_weight,
    )
    d_mlp = across_heads(d_mlp_part)
    (wide, mlp_in), d_mlp_part = lax.optimization_barrier(((wide, mlp_in), d_mlp_part))
    wide, mlp_in = visit([inputs], (wide, mlp_in))
    mlp_in_far = swap_cores(mlp_in)
    wide_far = swap_cores(lax.dynamic_index_in_dim(wide, 1 - core, 0, keepdims=False))
    ring = Ring(
        weight_partial(core, out_grad, mlp_in, wide, grad_far, mlp_in_far, wide_far), core
    )
    d_mlp = visit([ring, inputs], d_mlp)
    mlp_part, d_mlp = lax.optimization_barrier((mlp_part, d_mlp))
    mlp_out = across_heads(mlp_part)
    d_hidden, d_branch, d_attn, sums = middle(hidden, out_grad, d_mlp, gain_mlp, output_weight)
    d_branch_far = swap_cores(d_branch)
    grads = scatter_queries(d_attn, heads, split)
    small = jnp.concatenate([sums.reshape(-1), dup_bias[0]])
    lines = small.shape[0] // chips
    small = jnp.pad(
        small.reshape(chips, 1, lines), ((0, 0), (0, small_rows - 1), (0, model - lines))
    )
    out_near, out_far = share_halves(attn_out, 0)
    doutput = product(out_near, d_branch) + product(out_far, d_branch_far)
    doutput = jnp.concatenate([doutput.reshape(chips, -1, model), small], axis=1).astype(BF16)
    pieces = math.gcd(chips, 4)
    dquery, sums = [], {}
    for keys, dtype in ((other, BF16), (own, F32)):
        piece_sums = []
        for index in range(pieces):
            last = keys is own and index == pieces - 1
            if keys is own and index == 0:
                grads, dquery, doutput = visit([ring], (grads, dquery, doutput))
                far_sums = swap_cores(sums)
                doutput = to_heads(doutput)
            elif not last:
                grads, dquery = visit([ring], (grads, dquery))
            else:
                grads, dquery, doutput, mlp_out = visit([ring], (grads, dquery, doutput, mlp_out))
                doutput = jnp.sum(doutput.astype(F32), axis=0).astype(BF16)
                block_output = hidden + down_bias
                for part in mlp_out:
                    block_output += part.astype(F32)
                block_output = block_output.astype(BF16)
            dtypes = (BF16 if last else F32, dtype)
            *dquery, sums = backward_piece(
                queries, grads, raw, logsum, dquery, keys, piece_sums, index, pieces, crops, dtypes
            )
            piece_sums = [sums]
    (dquery,) = dquery
    key_value = (sums + far_sums.astype(F32)).astype(BF16)
    if split == 1:
        dquery, key_value = visit([ring], (dquery, key_value))
        moved = to_heads(jnp.concatenate([dquery, key_value], axis=1))
        projections = head_gradient(dquery, key_value, inputs)
        near, far = share_halves(projections, 0)
        projections = (near.astype(F32) + far.astype(F32)).astype(BF16)
        size = projections.shape[0]
        blocks = jnp.concatenate([projections, doutput], axis=0)
        dquery, dkey, dvalue = (
            moved[:, at * HD : at * HD + HD].reshape(width, rows) for at in range(3)
        )
    else:
        dquery = gather_queries(dquery, heads, split, rows)
        moved = to_heads(key_value).reshape(heads, split, 2 * HD, rows).astype(F32)
        moved = jnp.sum(moved, axis=1).astype(BF16)
        dkey, dvalue = (moved[:, at * HD : at * HD + HD].reshape(width, rows) for at in range(2))
        size, blocks = 0, doutput
        projections = [
            lax.psum(product(attn_in, grad, 0, 1).astype(BF16), ("chip", "core")).astype(F32)
            for grad in (dquery, dkey, dvalue)
        ]
    dquery, dkey, dvalue, blocks = visit([ring], (dquery, dkey, dvalue, blocks))
    gathered = Gather(blocks)
    d_part = (
        product(dquery, query_weight, 0, 1)
        + product(dkey, key_weight, 0, 1)
        + product(dvalue, value_weight, 0, 1)
    )
    unit_attn, inverse_attn = normalize(block_input.astype(F32))
    onehot = (segments[:, None] == jnp.arange(crops, dtype=jnp.int32)[None, :]).astype(F32)
    lead = jnp.sum(onehot * lead_steps.astype(F32)[None, :], axis=1) / 12.0
    ends = Doubling(
        jnp.stack(
            [
                jnp.sum(d_part * unit_attn, axis=0),
                jnp.sum(d_part, axis=0),
                jnp.sum(lead[:, None] * d_part, axis=0),
            ]
        )
    )
    d_in = across_heads(d_part.astype(BF16))
    d_in = visit([ring, gathered, ends], d_in)
    d_in = functools.reduce(jnp.add, (part.astype(F32) for part in d_in))
    input_grad = (d_hidden + normalize_back(d_in * gain_attn, unit_attn, inverse_attn)).astype(
        BF16
    )
    while ring.busy() or gathered.state or ends.busy():
        visit([ring, gathered, ends], ())
    ddown_weight, dup_weight = ring.state[2]
    ddown_weight = ddown_weight.reshape(-1, model)
    ends = ends.state[0]
    far = [swap_cores(block) for _, block in gathered.blocks]
    if split == 1:
        projections = projection_outputs(gathered, far, core, size)
    position = jnp.argsort(gathered.order())
    blocks = jnp.stack(
        [jnp.stack([block[size:] for _, block in gathered.blocks]), jnp.stack([block[size:] for block in far])]
    )
    blocks = jnp.take(jnp.where(core == 0, blocks, blocks[::-1]), position, axis=1)
    doutput_weight = blocks[:, :, :-small_rows].reshape(width, model).astype(F32)
    small = jnp.sum(blocks[:, :, -small_rows, :lines].astype(F32), axis=0).reshape(-1)
    dup_bias = small[4 * model :]
    small = [small[at * model : at * model + model] for at in range(4)]
    return (
        block_output,
        input_grad,
        ends[0],
        ends[1],
        ends[2],
        *projections,
        doutput_weight,
        *small[:3],
        dup_weight,
        dup_bias,
        ddown_weight,
        small[3],
    )


def solution(mesh):
    bands, halves = mesh.shape["band"], mesh.shape["head"]
    inner = Mesh(mesh.devices.reshape(bands // 2, 2, halves), ("chip", "core", "head"))
    band = ("chip", "core")
    rows, columns, split_rows = P(band, None), P(None, "head"), P("head", None)
    return jax.shard_map(
        local,
        mesh=inner,
        in_specs=(
            rows,
            rows,
            P(band),
            P(),
            P(),
            P(),
            P(),
            columns,
            columns,
            columns,
            split_rows,
            P(),
            P(),
            P(),
            columns,
            P("head"),
            split_rows,
            P(),
        ),
        out_specs=(
            rows,
            rows,
            P(),
            P(),
            P(),
            columns,
            columns,
            columns,
            split_rows,
            P(),
            P(),
            P(),
            columns,
            P("head"),
            split_rows,
            P(),
        ),
        check_vma=False,
    )
```

```python
import functools
import math

import jax
import jax.numpy as jnp
from jax import lax
from jax.experimental import pallas as pl
from jax.experimental.pallas import tpu as pltpu
from jax.sharding import Mesh, PartitionSpec as P

HD = 64
F32 = jnp.float32
BF16 = jnp.bfloat16
eps = 1e-05
masked_value = -1e30
seg_row = 3 * HD
payload_rows = 3 * HD + 16
small_rows = 8
params = pltpu.CompilerParams(vmem_limit_bytes=48 * 2**20)
streaming = pltpu.CompilerParams(vmem_limit_bytes=60 * 2**20)


def normalize(values):
    centred = values - jnp.mean(values, axis=-1, keepdims=True)
    inverse = lax.rsqrt(jnp.mean(centred * centred, axis=-1, keepdims=True) + eps)
    return (centred * inverse, inverse)


def normalize_back(grad_unit, unit, inverse):
    return inverse * (
        grad_unit
        - jnp.mean(grad_unit, axis=-1, keepdims=True)
        - unit * jnp.mean(grad_unit * unit, axis=-1, keepdims=True)
    )


def product(first, second, first_axis=1, second_axis=0):
    return lax.dot_general(
        first,
        second,
        (((first_axis,), (second_axis,)), ((), ())),
        preferred_element_type=jnp.float32,
    )


def struct(shape, dtype):
    return jax.ShapeDtypeStruct(shape, dtype)


def whole_spec(shape):
    return pl.BlockSpec(shape, lambda *at: (0,) * len(shape))


def cost(flops, size, exps=0):
    return pl.CostEstimate(flops=flops, bytes_accessed=size, transcendentals=exps)


def project_kernel(
    input_ref, segment_ref, steps_ref, gain, shift, lead_weight, *refs
):
    weights, (payload_ref, attn_in_ref) = refs[:3], refs[3:]
    rows = input_ref.shape[0]

    @pl.when(pl.program_id(0) == 0)
    def _():
        unit, _ = normalize(input_ref[...].astype(F32))
        crops = steps_ref.shape[0]
        crop = lax.broadcasted_iota(jnp.int32, (crops, rows), 0)
        onehot = jnp.where(crop == segment_ref[...], 1.0, 0.0)
        lead = product(onehot, steps_ref[...].astype(F32), 0, 0)[:, :1] / 12.0
        attn_in = unit * gain[...] + shift[...] + lead * lead_weight[...]
        attn_in_ref[...] = attn_in.astype(BF16)

    for at, weight in enumerate(weights):
        part = product(attn_in_ref[...], weight[...]).T.astype(BF16)
        for head in range(2):
            payload_ref[head, pl.ds(at * HD, HD), :] = part[head * HD : head * HD + HD]
    segment = jnp.broadcast_to(segment_ref[...].astype(F32), (16, rows)).astype(BF16)
    for head in range(2):
        payload_ref[head, pl.ds(seg_row, 16), :] = segment


def project(block_input, segments, lead_steps, gain, shift, lead_weight, weights):
    rows, model = block_input.shape
    heads = weights[0].shape[1] // HD
    steps = jnp.broadcast_to(lead_steps[:, None], (lead_steps.shape[0], 128))
    line = whole_spec((1, model))
    column = pl.BlockSpec((model, 2 * HD), lambda at: (0, at))
    return pl.pallas_call(
        project_kernel,
        grid=(heads // 2,),
        in_specs=[whole_spec(block_input.shape), whole_spec((1, rows)), whole_spec(steps.shape)]
        + [line] * 3
        + [column] * 3,
        out_specs=[
            pl.BlockSpec((2, payload_rows, rows), lambda at: (at, 0, 0)),
            whole_spec((rows, model)),
        ],
        out_shape=[struct((heads, payload_rows, rows), BF16), struct((rows, model), BF16)],
        compiler_params=streaming,
        cost_estimate=cost(2 * rows * model * 3 * heads * HD, 8 * 2**20),
        name="project",
    )(block_input, segments[None], steps, gain[None], shift[None], lead_weight[None], *weights)


def mlp_kernel(count, input_ref, grad_ref, *refs):
    branches, refs = refs[:count], refs[count:]
    output_bias, gain, shift, up_weight, up_bias, down_weight = refs[:6]
    wide_ref, mlp_in_ref, hidden_ref, bias_ref, forward_ref, back_ref, forward, back = refs[6:]
    at = pl.program_id(0)

    @pl.when(at == 0)
    def _():
        hidden = input_ref[...].astype(F32) + output_bias[...]
        for branch in branches:
            hidden += branch[...].astype(F32)
        hidden_ref[...] = hidden
        unit, _ = normalize(hidden)
        mlp_in_ref[...] = (unit * gain[...] + shift[...]).astype(BF16)
        forward[...] = jnp.zeros_like(forward)
        back[...] = jnp.zeros_like(back)

    upper = product(mlp_in_ref[...], up_weight[...]) + up_bias[...]
    share = 0.5 + 0.5 * lax.erf(upper * math.sqrt(0.5))
    slope = share + upper * (jnp.exp(upper * upper * -0.5) * (1.0 / math.sqrt(2.0 * math.pi)))
    active = (upper * share).astype(BF16)
    d_active = product(grad_ref[...], down_weight[...], 1, 1)
    d_upper = (d_active * slope).astype(BF16)
    wide_ref[0] = active
    wide_ref[1] = d_upper
    bias_ref[...] = jnp.sum(d_upper.astype(F32), axis=0, keepdims=True)
    forward[...] += product(active, down_weight[...])
    back[...] += product(d_upper, up_weight[...], 1, 1)

    @pl.when(at == pl.num_programs(0) - 1)
    def _():
        forward_ref[...] = forward[...].astype(BF16)
        back_ref[...] = back[...].astype(BF16)


def mlp(block_input, out_grad, branches, output_bias, gain, shift, up_weight, up_bias, down_weight):
    rows, model = block_input.shape
    units = up_weight.shape[1]
    step = math.gcd(units, 256)
    tile, line = whole_spec((rows, model)), whole_spec((1, model))
    return pl.pallas_call(
        functools.partial(mlp_kernel, len(branches)),
        grid=(units // step,),
        in_specs=[tile] * (2 + len(branches))
        + [line] * 3
        + [
            pl.BlockSpec((model, step), lambda at: (0, at)),
            pl.BlockSpec((1, step), lambda at: (0, at)),
            pl.BlockSpec((step, model), lambda at: (at, 0)),
        ],
        out_specs=[
            pl.BlockSpec((2, rows, step), lambda at: (0, 0, at)),
            tile,
            tile,
            pl.BlockSpec((1, step), lambda at: (0, at)),
            tile,
            tile,
        ],
        out_shape=[
            struct((2, rows, units), BF16),
            struct((rows, model), BF16),
            struct((rows, model), F32),
            struct((1, units), F32),
            struct((rows, model), BF16),
            struct((rows, model), BF16),
        ],
        scratch_shapes=[pltpu.VMEM((rows, model), F32)] * 2,
        compiler_params=streaming,
        cost_estimate=cost(8 * rows * model * units, 16 * 2**20, 2 * rows * units),
        name="mlp",
    )(
        block_input,
        out_grad,
        *branches,
        output_bias[None],
        gain[None],
        shift[None],
        up_weight,
        up_bias[None],
        down_weight,
    )


def middle_kernel(count, hidden_ref, grad_ref, *refs):
    parts, refs = refs[:count], refs[count:]
    gain, output_weight, d_hidden_ref, d_branch_ref, d_attn_ref, sums_ref = refs
    unit, inverse = normalize(hidden_ref[...])
    d_mlp = parts[0][...].astype(F32)
    for part in parts[1:]:
        d_mlp += part[...].astype(F32)
    grad = grad_ref[...].astype(F32)
    d_hidden = grad + normalize_back(d_mlp * gain[...], unit, inverse)
    d_hidden_ref[...] = d_hidden
    d_branch = d_hidden.astype(BF16)
    d_branch_ref[...] = d_branch
    d_attn_ref[...] = product(output_weight[...], d_branch, 1, 1).astype(BF16)
    for at, values in enumerate((d_hidden, d_mlp * unit, d_mlp, grad)):
        sums_ref[pl.ds(at, 1), :] = jnp.sum(values, axis=0, keepdims=True)


def middle(hidden, out_grad, parts, gain, output_weight):
    rows, model = hidden.shape
    width = output_weight.shape[0]
    return pl.pallas_call(
        functools.partial(middle_kernel, len(parts)),
        out_shape=[
            struct((rows, model), F32),
            struct((rows, model), BF16),
            struct((width, rows), BF16),
            struct((4, model), F32),
        ],
        compiler_params=streaming,
        cost_estimate=cost(2 * rows * model * width, 6 * 2**20),
        name="middle",
    )(hidden, out_grad, *parts, gain[None], output_weight)


def load_keys(pieces, crops, keys, key_t, value_t, value_n):
    start = 0
    for piece in pieces:
        chips, _, patches = piece.shape
        for chip in range(chips):
            crop = lax.broadcasted_iota(jnp.int32, (HD, patches), 0)
            segment = piece[chip, pl.ds(seg_row, 16), :].astype(F32)[:1].astype(jnp.int32)
            mask = jnp.where((crop != segment) & (crop < crops), masked_value, 0.0)
            key = piece[chip, pl.ds(HD, HD), :]
            value = piece[chip, pl.ds(2 * HD, HD), :]
            place = pl.ds(start, patches)
            keys[place, :] = jnp.concatenate([key.astype(F32), mask], axis=0).T.astype(BF16)
            if key_t is not None:
                key_t[:, place] = key
            if value_t is not None:
                value_t[pl.ds(0, HD), place] = value
                value_t[pl.ds(HD, 16), place] = jnp.ones((16, patches), BF16)
            if value_n is not None:
                value_n[place, :] = value.astype(F32).T.astype(BF16)
            start += patches


def masked_query(query_ref):
    query = query_ref[0, pl.ds(0, HD), :].astype(F32) * 0.125
    segment = query_ref[0, pl.ds(seg_row, 16), :].astype(F32)[:1].astype(jnp.int32)
    crop = lax.broadcasted_iota(jnp.int32, query.shape, 0)
    onehot = jnp.where(crop == segment, 1.0, 0.0)
    return jnp.concatenate([query, onehot], axis=0).astype(BF16)


def forward_kernel(crops, step, query_ref, own, other, raw_ref, out_ref, logsum_ref, keys, value_t):
    @pl.when(pl.program_id(0) == 0)
    def _():
        load_keys((own, other), crops, keys, None, value_t, None)

    query = masked_query(query_ref)
    count = query.shape[1]
    top = jnp.full((1, count), masked_value, F32)
    accum = jnp.zeros((HD + 16, count), F32)
    for start in range(0, keys.shape[0], step):
        scores = product(keys[pl.ds(start, step), :], query)
        new_top = jnp.maximum(top, jnp.max(scores, axis=0, keepdims=True))
        weights = jnp.exp(scores - new_top).astype(BF16)
        accum = accum * jnp.exp(top - new_top) + product(value_t[:, pl.ds(start, step)], weights)
        top = new_top
    total = accum[HD : HD + 1]
    raw = accum[:HD] / total
    raw_ref[0] = raw
    out_ref[0] = raw.astype(BF16)
    logsum_ref[0] = top + jnp.log(total)


def backward_kernel(
    crops,
    before,
    query_ref,
    grad_ref,
    raw_ref,
    logsum_ref,
    *refs,
):
    before_refs, refs = refs[:before], refs[before:]
    piece, (dquery_ref, sums_ref, keys, key_t, value_n, sums) = refs[0], refs[-6:]
    group = pl.program_id(0)

    @pl.when(group == 0)
    def _():
        load_keys((piece,), crops, keys, key_t, None, value_n)
        sums[...] = jnp.zeros_like(sums)

    query = masked_query(query_ref)
    grad = grad_ref[0]
    grad_wide = grad.astype(F32)
    delta = jnp.sum(grad_wide * raw_ref[0], axis=0, keepdims=True)
    scaled = query_ref[0, pl.ds(0, HD), :].astype(F32) * 0.125
    zero = jnp.zeros_like(scaled)
    query_side = jnp.concatenate([scaled, zero], axis=0).T.astype(BF16)
    grad_side = jnp.concatenate([zero, grad_wide], axis=0).T.astype(BF16)
    probs = jnp.exp(product(keys[...], query) - logsum_ref[0])
    dprobs = product(value_n[...], grad)
    dscores = (probs * (dprobs - delta)).astype(BF16)
    sums[...] += product(dscores, query_side) + product(probs.astype(BF16), grad_side)
    dquery = product(key_t[...], dscores) * 0.125
    for ref in before_refs:
        dquery = ref[0] + dquery
    dquery_ref[0] = dquery.astype(dquery_ref.dtype)

    @pl.when(group == pl.num_programs(0) - 1)
    def _():
        chips, _, patches = sums_ref.shape
        for chip in range(chips):
            sums_ref[chip] = sums[pl.ds(chip * patches, patches), :].T.astype(sums_ref.dtype)


def key_step(count):
    return 1024 if count % 1024 == 0 else 256


def query_spec(rows, patches):
    return pl.BlockSpec((1, rows, patches), lambda group: (group, 0, 0))


def attention_forward(queries, own, other, crops):
    groups, _, patches = queries.shape
    count = 2 * own.shape[0] * own.shape[2]
    return pl.pallas_call(
        functools.partial(forward_kernel, crops, key_step(count)),
        grid=(groups,),
        in_specs=[
            query_spec(payload_rows, patches),
            whole_spec(own.shape),
            whole_spec(other.shape),
        ],
        out_specs=[query_spec(HD, patches), query_spec(HD, patches), query_spec(1, patches)],
        out_shape=[
            struct((groups, HD, patches), F32),
            struct((groups, HD, patches), BF16),
            struct((groups, 1, patches), F32),
        ],
        scratch_shapes=[pltpu.VMEM((count, 2 * HD), BF16), pltpu.VMEM((HD + 16, count), BF16)],
        compiler_params=params,
        cost_estimate=cost(
            groups * patches * count * 4096, 4 * 2**20, groups * patches * count
        ),
        name="attention_forward",
    )(queries, own, other)


def backward_piece(queries, grads, raw, logsum, before, keys, earlier, index, pieces, crops, dtypes):
    groups, _, patches = queries.shape
    chips = keys.shape[0] // pieces
    count = chips * keys.shape[2]
    sums_shape = (chips, 2 * HD, keys.shape[2])
    return pl.pallas_call(
        functools.partial(backward_kernel, crops, len(before)),
        grid=(groups,),
        in_specs=[
            query_spec(payload_rows, patches),
            query_spec(HD, patches),
            query_spec(HD, patches),
            query_spec(1, patches),
        ]
        + [query_spec(HD, patches)] * len(before)
        + [pl.BlockSpec((chips,) + keys.shape[1:], lambda group: (index, 0, 0))]
        + [pl.BlockSpec(memory_space=pl.ANY)] * len(earlier),
        out_specs=[
            query_spec(HD, patches),
            pl.BlockSpec(sums_shape, lambda group: (index, 0, 0)),
        ],
        out_shape=[
            struct((groups, HD, patches), dtypes[0]),
            struct((keys.shape[0],) + sums_shape[1:], dtypes[1]),
        ],
        input_output_aliases={5 + len(before): 1} if earlier else {},
        scratch_shapes=[
            pltpu.VMEM((count, 2 * HD), BF16),
            pltpu.VMEM((HD, count), BF16),
            pltpu.VMEM((count, HD), BF16),
            pltpu.VMEM((count, 2 * HD), F32),
        ],
        compiler_params=params,
        cost_estimate=cost(
            groups * patches * count * 4096, 4 * 2**20, groups * patches * count
        ),
        name="attention_backward",
    )(queries, grads, raw, logsum, *before, keys, *earlier)


def swap_cores(values):
    return lax.ppermute(values, "core", [(0, 1), (1, 0)])


def to_heads(blocks):
    return lax.all_to_all(blocks, "chip", 0, 0, tiled=True)


def scatter_queries(values, heads, split):
    rows, patches = values.shape[0] // heads, values.shape[1]
    if split == 1:
        return to_heads(values.reshape(heads, rows, patches))
    part = patches // split
    blocks = values.reshape(heads, rows, split, part).transpose(0, 2, 1, 3)
    moved = to_heads(blocks.reshape(heads * split, rows, part))
    width = min(256, moved.shape[0] * part)
    joined = moved.transpose(1, 0, 2).reshape(rows, -1, width)
    return joined.transpose(1, 0, 2)


def gather_queries(values, heads, split, patches):
    rows = values.shape[1]
    if split == 1:
        return to_heads(values).reshape(heads * rows, patches)
    part = patches // split
    joined = values.transpose(1, 0, 2).reshape(rows, heads * split, part)
    moved = to_heads(joined.transpose(1, 0, 2)).reshape(heads, split, rows, part)
    return moved.transpose(0, 2, 1, 3).reshape(heads * rows, patches)


def across_heads(part):
    if lax.axis_size("head") == 2:
        return [part, lax.ppermute(part, "head", [(0, 1), (1, 0)])]
    return [lax.psum(part, "head")]


def ring_pairs(direction):
    chips = lax.axis_size("chip")
    order = list(range(0, chips, 2)) + list(range(chips - 1, 0, -2))
    return [(order[at], order[(at + direction) % chips]) for at in range(chips)]


def ring_table():
    chips, chip = lax.axis_size("chip"), lax.axis_index("chip")
    place = jnp.where(chip % 2 == 0, chip // 2, chips - 1 - chip // 2)
    steps = jnp.arange(2 * chips + 1, dtype=jnp.int32)
    places = (place + steps) % chips
    there = jnp.where(places < chips // 2, 2 * places, 2 * (chips - 1 - places) + 1)
    table = jnp.where(steps < chips, places, there)
    return jnp.where(steps == 2 * chips, lax.axis_index("core"), table).astype(jnp.int32)


def visit(streams, values):
    states, values = lax.optimization_barrier(([stream.state for stream in streams], values))
    for stream, state in zip(streams, states):
        stream.state = state
        stream.advance()
    return values


class Gather:
    def __init__(self, block, swap=False, take=None):
        self.chips, self.swap, self.take = lax.axis_size("chip"), swap, take
        self.blocks, self.pairs, self.count = [], [], 0
        self.state = ([], [], [])
        self.send([(0, block)], [block, block], [])

    def send(self, new, sides, outputs):
        self.blocks += new
        self.new = new
        self.count += 1
        reach = (self.chips // 2, (self.chips - 1) // 2)
        flying = [
            lax.ppermute(block, "chip", ring_pairs(direction))
            for block, direction, steps in zip(sides, (1, -1), reach)
            if self.count <= steps
        ]
        self.state = (flying, [swap_cores(block) for _, block in new] if self.swap else [], outputs)

    def advance(self):
        arrived, swapped, outputs = self.state
        pairs = [(step, near, far) for (step, near), far in zip(self.new, swapped)]
        self.pairs += pairs
        if self.take and pairs:
            outputs = self.take(outputs, pairs)
        new = [(side * self.count, block) for block, side in zip(arrived, (-1, 1))]
        self.send(new, arrived, outputs)

    def busy(self):
        return bool(self.state[0] or self.state[1])


def partial_kernel(core, grad, mlp_in, wide, grad_far, mlp_in_far, wide_far, out_ref):
    is_down = core[0] == 0

    @pl.when(is_down)
    def _():
        out_ref[...] = (
            product(wide[0], grad[...], 0, 0) + product(wide_far[...], grad_far[...], 0, 0)
        ).astype(BF16)

    @pl.when(jnp.logical_not(is_down))
    def _():
        out_ref[...] = (
            product(mlp_in[...], wide[0], 0, 0) + product(mlp_in_far[...], wide_far[...], 0, 0)
        ).astype(BF16)


def weight_partial(core, grad, mlp_in, wide, grad_far, mlp_in_far, wide_far):
    rows, model = grad.shape
    units = wide.shape[2]
    half = units // 2
    tile = whole_spec((rows, model))
    if model != half:
        down = product(wide[0], grad, 0, 0) + product(wide_far, grad_far, 0, 0)
        down = down.reshape(2, half, model).transpose(1, 0, 2).reshape(model, units)
        up = product(mlp_in, wide[1], 0, 0) + product(mlp_in_far, wide_far, 0, 0)
        return jnp.where(core == 0, down, up).astype(BF16)
    return pl.pallas_call(
        partial_kernel,
        grid_spec=pltpu.PrefetchScalarGridSpec(
            num_scalar_prefetch=1,
            grid=(2,),
            in_specs=[
                tile,
                tile,
                pl.BlockSpec((1, rows, half), lambda at, core: (core[0], 0, at)),
                tile,
                tile,
                pl.BlockSpec((rows, half), lambda at, core: (0, at)),
            ],
            out_specs=pl.BlockSpec((model, half), lambda at, core: (0, at)),
        ),
        out_shape=struct((model, units), BF16),
        compiler_params=streaming,
        cost_estimate=cost(4 * rows * model * units, 12 * 2**20),
        name="weight_partial",
    )(core[None], grad, mlp_in, wide, grad_far, mlp_in_far, wide_far)


class Reduce:
    def __init__(self, partial, table):
        self.chips, self.partial, self.table = lax.axis_size("chip"), partial, table
        self.shape = (partial.shape[0] // self.chips, partial.shape[1])
        self.reach = (self.chips // 2, (self.chips - 1) // 2)
        self.count, self.gather = 0, None
        self.send([self.block(self.reach[0]), self.block(-self.reach[1])], [])

    def block(self, step):
        start = self.table[step % self.chips] * self.shape[0]
        return lax.dynamic_slice_in_dim(self.partial, start, self.shape[0], 0)

    def send(self, sides, held):
        self.count += 1
        flying = [
            lax.ppermute(block, "chip", ring_pairs(direction))
            for block, direction in zip(sides, (1, -1))
        ]
        self.state = (flying, held)

    def advance(self):
        if self.gather:
            self.gather.state = self.state
            self.gather.advance()
            self.state = self.gather.state
            return
        arrived, held = self.state
        sums, done = [], self.count == self.reach[0]
        for block, reach, side in zip(arrived, self.reach, (1, -1)):
            left = reach - self.count
            if left > 0 or done:
                parts = held if done else []
                sums.append(self.add([block] + parts, side * left))
            else:
                held = [block]
        if done:
            self.gather = Gather(sums[0], True, self.place)
            self.state = self.gather.state
        else:
            self.send(sums, held)

    def add(self, parts, step):
        total = self.block(step).astype(F32)
        for part in parts:
            total += part.astype(F32)
        return total.astype(BF16)

    def place(self, outputs, pairs):
        rows, columns = self.shape
        half, chips = columns // 2, self.chips
        first = pairs[0][0] % chips
        stride = pairs[-1][0] % chips - first
        block = pl.BlockSpec(self.shape, lambda at, table: (0, 0))
        return pl.pallas_call(
            functools.partial(place_kernel, len(pairs)),
            grid_spec=pltpu.PrefetchScalarGridSpec(
                num_scalar_prefetch=1,
                grid=(len(pairs),),
                in_specs=[pl.BlockSpec(memory_space=pl.ANY)] * len(outputs)
                + [block] * (2 * len(pairs)),
                out_specs=[
                    pl.BlockSpec((2, rows, half), lambda at, table: (0, table[first + at * stride], 0)),
                    pl.BlockSpec((rows, columns), lambda at, table: (table[first + at * stride], 0)),
                ],
            ),
            out_shape=[
                struct((2, chips * rows, half), F32),
                struct((chips * rows, columns), F32),
            ],
            input_output_aliases={1 + at: at for at in range(len(outputs))},
            compiler_params=streaming,
            cost_estimate=cost(0, 2 * 2**20),
            name="place",
        )(self.table, *outputs, *[pair[1] for pair in pairs], *[pair[2] for pair in pairs])

    def busy(self):
        return self.gather is None or self.gather.busy()


def place_kernel(count, table, *refs):
    nears, fars, (down, up) = refs[-2 - 2 * count : -2 - count], refs[-2 - count : -2], refs[-2:]
    half = down.shape[2]
    core = table[table.shape[0] - 1]

    def put(first, second):
        for side in range(2):
            down[side] = first[:, pl.ds(side * half, half)].astype(F32)
        up[...] = second[...].astype(F32)

    for at, (near, far) in enumerate(zip(nears, fars)):
        here = pl.program_id(0) == at
        pl.when(here & (core == 0))(functools.partial(put, near, far))
        pl.when(here & (core != 0))(functools.partial(put, far, near))


def head_gradient_kernel(steps, table, query_ref, key_value_ref, *refs):
    blocks, out_ref = refs[:-1], refs[-1]
    chips = len(blocks)
    total = jnp.zeros(out_ref.shape, F32)
    for step, block in zip(steps, blocks):
        chip = table[chips + step % chips]
        grads = jnp.concatenate([query_ref[chip], key_value_ref[chip]], axis=0)
        total += product(grads, block[...])
    out_ref[...] = total.astype(BF16)


def head_gradient(dquery, key_value, inputs, table):
    count, rows, patches = dquery.shape
    steps, blocks = zip(*inputs.blocks)
    model = blocks[0].shape[1]
    step = math.gcd(model, 256)
    return pl.pallas_call(
        functools.partial(head_gradient_kernel, steps),
        grid_spec=pltpu.PrefetchScalarGridSpec(
            num_scalar_prefetch=1,
            grid=(model // step,),
            in_specs=[
                pl.BlockSpec(dquery.shape, lambda at, table: (0, 0, 0)),
                pl.BlockSpec(key_value.shape, lambda at, table: (0, 0, 0)),
            ]
            + [pl.BlockSpec((patches, step), lambda at, table: (0, at))] * count,
            out_specs=pl.BlockSpec((3 * rows, step), lambda at, table: (0, at)),
        ),
        out_shape=struct((3 * rows, model), BF16),
        compiler_params=streaming,
        cost_estimate=cost(6 * rows * count * patches * model, 6 * 2**20),
        name="head_gradient",
    )(table, dquery, key_value, *blocks)


def layout_kernel(steps, size, extra, table, *refs):
    count = len(steps)
    nears, fars, outputs, output_ref, small_ref, held = (
        refs[:count],
        refs[count : 2 * count],
        refs[2 * count : 2 * count + 3],
        refs[2 * count + 3],
        refs[2 * count + 4],
        refs[2 * count + 5],
    )
    at = pl.program_id(0)

    @pl.when(at == 0)
    def _():
        core = table[2 * count]
        for step, near, far in zip(steps, nears, fars):
            chip = table[count + step % count]
            for side, block in ((core, near), (1 - core, far)):
                held[chip, side] = block[pl.ds(0, size), :]
                output_ref[side, chip] = block[pl.ds(size, extra), :].astype(F32)
                small_ref[side, chip] = block[pl.ds(size + extra, small_rows), :].astype(F32)

    pair = [
        jnp.concatenate([held[2 * at + head, 0], held[2 * at + head, 1]], axis=0)
        for head in range(2)
    ]
    for index, output in enumerate(outputs):
        rows = [part[index * HD : index * HD + HD] for part in pair]
        output[...] = jnp.concatenate(rows, axis=0).astype(F32).T


def final_layout(pairs, size, table):
    count = len(pairs)
    steps, nears, fars = zip(*pairs)
    rows, model = nears[0].shape
    extra = rows - size - small_rows
    return pl.pallas_call(
        functools.partial(layout_kernel, steps, size, extra),
        grid_spec=pltpu.PrefetchScalarGridSpec(
            num_scalar_prefetch=1,
            grid=(count // 2,),
            in_specs=[pl.BlockSpec((rows, model), lambda at, table: (0, 0))] * (2 * count),
            out_specs=[pl.BlockSpec((model, 2 * HD), lambda at, table: (0, at))] * 3
            + [
                pl.BlockSpec((2, count, extra, model), lambda at, table: (0, 0, 0, 0)),
                pl.BlockSpec((2, count, small_rows, model), lambda at, table: (0, 0, 0, 0)),
            ],
            scratch_shapes=[pltpu.VMEM((count, 2, size, model), BF16)],
        ),
        out_shape=[struct((model, count * HD), F32)] * 3
        + [
            struct((2, count, extra, model), F32),
            struct((2, count, small_rows, model), F32),
        ],
        compiler_params=streaming,
        name="final_layout",
    )(table, *nears, *fars)


def core_half(values, axis, side):
    size = values.shape[axis] // 2
    return lax.dynamic_slice_in_dim(values, side * size, size, axis)


def share_halves(values, axis):
    core = lax.axis_index("core")
    return core_half(values, axis, core), swap_cores(core_half(values, axis, 1 - core))


def local(
    block_input,
    out_grad,
    segments,
    lead_steps,
    gain_attn,
    shift_attn,
    lead_weight,
    query_weight,
    key_weight,
    value_weight,
    output_weight,
    output_bias,
    gain_mlp,
    shift_mlp,
    up_weight,
    up_bias,
    down_weight,
    down_bias,
):
    rows, model = block_input.shape
    heads = query_weight.shape[1] // HD
    width = heads * HD
    chips, core = lax.axis_size("chip"), lax.axis_index("core")
    split = chips // heads
    crops = lead_steps.shape[0]
    table = ring_table()
    weights = (query_weight, key_weight, value_weight)
    payload, attn_in = project(
        block_input, segments, lead_steps, gain_attn, shift_attn, lead_weight, weights
    )
    if split == 1:
        own = to_heads(payload)
        queries = own
    else:
        queries = scatter_queries(payload.reshape(-1, rows), heads, split)
        own = to_heads(jnp.repeat(payload, split, axis=0))
    own, attn_in = lax.optimization_barrier((own, attn_in))
    inputs = Gather(attn_in)
    grad_far = swap_cores(out_grad)
    raw, out, logsum = attention_forward(queries, own, swap_cores(own), crops)
    other = swap_cores(own)
    attn_out = gather_queries(out, heads, split, rows)
    attn_out = visit([inputs], attn_out)
    branches = across_heads(product(attn_out, output_weight, 0, 0).astype(BF16))
    branches = visit([inputs], branches)
    wide, mlp_in, hidden, dup_bias, mlp_part, d_mlp_part = mlp(
        block_input,
        out_grad,
        branches,
        output_bias,
        gain_mlp,
        shift_mlp,
        up_weight,
        up_bias,
        down_weight,
    )
    d_mlp = across_heads(d_mlp_part)
    (wide, mlp_in), d_mlp_part = lax.optimization_barrier(((wide, mlp_in), d_mlp_part))
    wide, mlp_in = visit([inputs], (wide, mlp_in))
    mlp_in_far = swap_cores(mlp_in)
    wide_far = swap_cores(lax.dynamic_index_in_dim(wide, 1 - core, 0, keepdims=False))
    ring = Reduce(
        weight_partial(core, out_grad, mlp_in, wide, grad_far, mlp_in_far, wide_far), table
    )
    d_mlp = visit([ring, inputs], d_mlp)
    mlp_part, d_mlp = lax.optimization_barrier((mlp_part, d_mlp))
    mlp_out = across_heads(mlp_part)
    d_hidden, d_branch, d_attn, sums = middle(hidden, out_grad, d_mlp, gain_mlp, output_weight)
    d_branch_far = swap_cores(d_branch)
    grads = scatter_queries(d_attn, heads, split)
    small = jnp.concatenate([sums.reshape(-1), dup_bias[0]])
    lines = small.shape[0] // chips
    small = jnp.pad(
        small.reshape(chips, 1, lines), ((0, 0), (0, small_rows - 1), (0, model - lines))
    )
    out_near, out_far = share_halves(attn_out, 0)
    doutput = product(out_near, d_branch) + product(out_far, d_branch_far)
    doutput = jnp.concatenate([doutput.reshape(chips, -1, model), small], axis=1).astype(BF16)
    pieces = 2
    dquery, sums = [], {}
    for keys, dtype in ((other, BF16), (own, F32)):
        piece_sums = []
        for index in range(pieces):
            last = keys is own and index == pieces - 1
            if keys is own and index == 0:
                grads, dquery, doutput = visit([ring], (grads, dquery, doutput))
                far_sums = swap_cores(sums)
                doutput = to_heads(doutput)
            elif not last:
                grads, dquery = visit([ring], (grads, dquery))
            else:
                grads, dquery, doutput, mlp_out = visit([ring], (grads, dquery, doutput, mlp_out))
                doutput = jnp.sum(doutput.astype(F32), axis=0).astype(BF16)
                block_output = hidden + down_bias
                for part in mlp_out:
                    block_output += part.astype(F32)
                block_output = block_output.astype(BF16)
            dtypes = (BF16 if last else F32, dtype)
            *dquery, sums = backward_piece(
                queries, grads, raw, logsum, dquery, keys, piece_sums, index, pieces, crops, dtypes
            )
            piece_sums = [sums]
    (dquery,) = dquery
    key_value = (sums + far_sums.astype(F32)).astype(BF16)
    if split == 1:
        dquery, key_value = visit([ring], (dquery, key_value))
        moved = to_heads(jnp.concatenate([dquery, key_value], axis=1))
        projections = head_gradient(dquery, key_value, inputs, table)
        near, far = share_halves(projections, 0)
        projections = (near.astype(F32) + far.astype(F32)).astype(BF16)
        size = projections.shape[0]
        blocks = jnp.concatenate([projections, doutput], axis=0)
        dquery, dkey, dvalue = (
            moved[:, at * HD : at * HD + HD].reshape(width, rows) for at in range(3)
        )
    else:
        dquery = gather_queries(dquery, heads, split, rows)
        moved = to_heads(key_value).reshape(heads, split, 2 * HD, rows).astype(F32)
        moved = jnp.sum(moved, axis=1).astype(BF16)
        dkey, dvalue = (moved[:, at * HD : at * HD + HD].reshape(width, rows) for at in range(2))
        size, blocks = 0, doutput
        projections = [
            lax.psum(product(attn_in, grad, 0, 1).astype(BF16), ("chip", "core")).astype(F32)
            for grad in (dquery, dkey, dvalue)
        ]
    dquery, dkey, dvalue, blocks = visit([ring], (dquery, dkey, dvalue, blocks))
    gathered = Gather(blocks, True)
    d_part = (
        product(dquery, query_weight, 0, 1)
        + product(dkey, key_weight, 0, 1)
        + product(dvalue, value_weight, 0, 1)
    )
    d_in = across_heads(d_part.astype(BF16))
    unit_attn, inverse_attn = normalize(block_input.astype(F32))
    onehot = (segments[:, None] == jnp.arange(crops, dtype=jnp.int32)[None, :]).astype(F32)
    lead = jnp.sum(onehot * lead_steps.astype(F32)[None, :], axis=1) / 12.0
    ends = jnp.stack(
        [
            jnp.sum(d_part * unit_attn, axis=0),
            jnp.sum(d_part, axis=0),
            jnp.sum(lead[:, None] * d_part, axis=0),
        ]
    )
    ends = jnp.pad(ends.reshape(-1, 128), ((0, -ends.size // 128 % 16), (0, 0))).astype(BF16)
    everyone = ("chip", "core", "head")
    ends = jnp.broadcast_to(ends, (lax.axis_size(everyone),) + ends.shape)
    ends = lax.all_to_all(ends, everyone, 0, 0, tiled=True)
    d_in = visit([ring, gathered], d_in)
    d_in = functools.reduce(jnp.add, (part.astype(F32) for part in d_in))
    input_grad = (d_hidden + normalize_back(d_in * gain_attn, unit_attn, inverse_attn)).astype(
        BF16
    )
    input_grad, ends = visit([ring, gathered], (input_grad, ends))
    while ring.busy() or gathered.busy():
        visit([ring, gathered], ())
    ends = jnp.sum(ends.astype(F32), axis=0).reshape(-1)[: 3 * model].reshape(3, model)
    ddown_weight, dup_weight = ring.state[2]
    ddown_weight = ddown_weight.reshape(-1, model)
    if split == 1:
        *projections, doutput_weight, small = final_layout(gathered.pairs, size, table)
        doutput_weight = doutput_weight.reshape(width, model)
        small = small[:, :, 0, :lines]
    else:
        blocks = jnp.zeros((2, chips) + blocks.shape, F32)
        for step, near, far in gathered.pairs:
            for side, block in ((core, near), (1 - core, far)):
                start = (side, table[chips + step % chips], 0, 0)
                block = block[None, None].astype(F32)
                blocks = lax.dynamic_update_slice(blocks, block, start)
        doutput_weight = blocks[:, :, :-small_rows].reshape(width, model)
        small = blocks[:, :, -small_rows, :lines]
    small = jnp.sum(small, axis=0).reshape(-1)
    dup_bias = small[4 * model :]
    small = [small[at * model : at * model + model] for at in range(4)]
    return (
        block_output,
        input_grad,
        ends[0],
        ends[1],
        ends[2],
        *projections,
        doutput_weight,
        *small[:3],
        dup_weight,
        dup_bias,
        ddown_weight,
        small[3],
    )


def solution(mesh):
    bands, halves = mesh.shape["band"], mesh.shape["head"]
    inner = Mesh(mesh.devices.reshape(bands // 2, 2, halves), ("chip", "core", "head"))
    band = ("chip", "core")
    rows, columns, split_rows = P(band, None), P(None, "head"), P("head", None)
    return jax.shard_map(
        local,
        mesh=inner,
        in_specs=(
            rows,
            rows,
            P(band),
            P(),
            P(),
            P(),
            P(),
            columns,
            columns,
            columns,
            split_rows,
            P(),
            P(),
            P(),
            columns,
            P("head"),
            split_rows,
            P(),
        ),
        out_specs=(
            rows,
            rows,
            P(),
            P(),
            P(),
            columns,
            columns,
            columns,
            split_rows,
            P(),
            P(),
            P(),
            columns,
            P("head"),
            split_rows,
            P(),
        ),
        check_vma=False,
    )
```

```python
import functools
import math

import jax
import jax.numpy as jnp
from jax import lax
from jax.experimental import pallas as pl
from jax.experimental.pallas import tpu as pltpu
from jax.sharding import Mesh, PartitionSpec as P

HD = 64
F32 = jnp.float32
BF16 = jnp.bfloat16
eps = 1e-05
masked_value = -1e30
seg_row = 3 * HD
payload_rows = 3 * HD + 16
small_rows = 8
params = pltpu.CompilerParams(vmem_limit_bytes=48 * 2**20)
streaming = pltpu.CompilerParams(vmem_limit_bytes=60 * 2**20)


def normalize(values):
    centred = values - jnp.mean(values, axis=-1, keepdims=True)
    inverse = lax.rsqrt(jnp.mean(centred * centred, axis=-1, keepdims=True) + eps)
    return (centred * inverse, inverse)


def normalize_back(grad_unit, unit, inverse):
    return inverse * (
        grad_unit
        - jnp.mean(grad_unit, axis=-1, keepdims=True)
        - unit * jnp.mean(grad_unit * unit, axis=-1, keepdims=True)
    )


def product(first, second, first_axis=1, second_axis=0):
    return lax.dot_general(
        first,
        second,
        (((first_axis,), (second_axis,)), ((), ())),
        preferred_element_type=jnp.float32,
    )


def struct(shape, dtype):
    return jax.ShapeDtypeStruct(shape, dtype)


def whole_spec(shape):
    return pl.BlockSpec(shape, lambda *at: (0,) * len(shape))


def cost(flops, size, exps=0):
    return pl.CostEstimate(flops=flops, bytes_accessed=size, transcendentals=exps)


def project_kernel(
    input_ref, segment_ref, steps_ref, gain, shift, lead_weight, *refs
):
    weights, (payload_ref, attn_in_ref) = refs[:3], refs[3:]
    rows = input_ref.shape[0]

    @pl.when(pl.program_id(0) == 0)
    def _():
        unit, _ = normalize(input_ref[...].astype(F32))
        crops = steps_ref.shape[0]
        crop = lax.broadcasted_iota(jnp.int32, (crops, rows), 0)
        steps = jnp.zeros((crops, rows), jnp.int32)
        for at in range(crops):
            steps = jnp.where(crop == at, steps_ref[at], steps)
        steps = jnp.where(crop == segment_ref[...], steps, 0).astype(F32)
        lead = product(steps, jnp.ones((crops, 128), F32), 0, 0)[:, :1] / 12.0
        attn_in = unit * gain[...] + shift[...] + lead * lead_weight[...]
        attn_in_ref[...] = attn_in.astype(BF16)

    for at, weight in enumerate(weights):
        part = product(attn_in_ref[...], weight[...]).T.astype(BF16)
        for head in range(2):
            payload_ref[head, pl.ds(at * HD, HD), :] = part[head * HD : head * HD + HD]
    segment = jnp.broadcast_to(segment_ref[...].astype(F32), (16, rows)).astype(BF16)
    for head in range(2):
        payload_ref[head, pl.ds(seg_row, 16), :] = segment


def project(block_input, segments, lead_steps, gain, shift, lead_weight, weights):
    rows, model = block_input.shape
    heads = weights[0].shape[1] // HD
    line = whole_spec((1, model))
    column = pl.BlockSpec((model, 2 * HD), lambda at: (0, at))
    return pl.pallas_call(
        project_kernel,
        grid=(heads // 2,),
        in_specs=[whole_spec(block_input.shape), whole_spec((1, rows)), pl.BlockSpec(memory_space=pltpu.SMEM)]
        + [line] * 3
        + [column] * 3,
        out_specs=[
            pl.BlockSpec((2, payload_rows, rows), lambda at: (at, 0, 0)),
            whole_spec((rows, model)),
        ],
        out_shape=[struct((heads, payload_rows, rows), BF16), struct((rows, model), BF16)],
        compiler_params=streaming,
        cost_estimate=cost(2 * rows * model * 3 * heads * HD, 8 * 2**20),
        name="project",
    )(block_input, segments[None], lead_steps, gain[None], shift[None], lead_weight[None], *weights)


def mlp_kernel(count, core_ref, input_ref, grad_ref, *refs):
    branches, refs = refs[:count], refs[count:]
    output_bias, gain, shift, up_weight, up_bias, down_weight = refs[:6]
    keep_ref, give_ref, keep_in_ref, give_in_ref, hidden_ref, bias_ref, forward_ref, back_ref = refs[
        6:14
    ]
    mlp_in_ref, forward, back = refs[14:]
    at = pl.program_id(0)
    is_down = core_ref[core_ref.shape[0] - 1] == 0

    @pl.when(at == 0)
    def _():
        hidden = input_ref[...].astype(F32) + output_bias[...]
        for branch in branches:
            hidden += branch[...].astype(F32)
        hidden_ref[...] = hidden
        unit, _ = normalize(hidden)
        mlp_in = (unit * gain[...] + shift[...]).astype(BF16)
        mlp_in_ref[...] = mlp_in
        keep_in_ref[...] = jnp.where(is_down, grad_ref[...], mlp_in)
        give_in_ref[...] = jnp.where(is_down, mlp_in, grad_ref[...])
        forward[...] = jnp.zeros_like(forward)
        back[...] = jnp.zeros_like(back)

    upper = product(mlp_in_ref[...], up_weight[...]) + up_bias[...]
    share = 0.5 + 0.5 * lax.erf(upper * math.sqrt(0.5))
    slope = share + upper * (jnp.exp(upper * upper * -0.5) * (1.0 / math.sqrt(2.0 * math.pi)))
    active = (upper * share).astype(BF16)
    d_active = product(grad_ref[...], down_weight[...], 1, 1)
    d_upper = (d_active * slope).astype(BF16)
    keep_ref[...] = jnp.where(is_down, active, d_upper)
    give_ref[...] = jnp.where(is_down, d_upper, active)
    bias_ref[...] = jnp.sum(d_upper.astype(F32), axis=0, keepdims=True)
    forward[...] += product(active, down_weight[...])
    back[...] += product(d_upper, up_weight[...], 1, 1)

    @pl.when(at == pl.num_programs(0) - 1)
    def _():
        forward_ref[...] = forward[...].astype(BF16)
        back_ref[...] = back[...].astype(BF16)


def mlp(
    table, block_input, out_grad, branches, output_bias, gain, shift, up_weight, up_bias, down_weight
):
    rows, model = block_input.shape
    units = up_weight.shape[1]
    step = math.gcd(units, 512)
    tile, line = whole_spec((rows, model)), whole_spec((1, model))
    wide = pl.BlockSpec((rows, step), lambda at, table: (0, at))
    bias = pl.BlockSpec((1, step), lambda at, table: (0, at))
    return pl.pallas_call(
        functools.partial(mlp_kernel, len(branches)),
        grid_spec=pltpu.PrefetchScalarGridSpec(
            num_scalar_prefetch=1,
            grid=(units // step,),
            in_specs=[tile] * (2 + len(branches))
            + [line] * 3
            + [
                pl.BlockSpec((model, step), lambda at, table: (0, at)),
                bias,
                pl.BlockSpec((step, model), lambda at, table: (at, 0)),
            ],
            out_specs=[wide, wide, tile, tile, tile, bias, tile, tile],
            scratch_shapes=[pltpu.VMEM((rows, model), BF16)]
            + [pltpu.VMEM((rows, model), F32)] * 2,
        ),
        out_shape=[struct((rows, units), BF16)] * 2
        + [struct((rows, model), BF16)] * 2
        + [
            struct((rows, model), F32),
            struct((1, units), F32),
            struct((rows, model), BF16),
            struct((rows, model), BF16),
        ],
        compiler_params=streaming,
        cost_estimate=cost(8 * rows * model * units, 16 * 2**20, 2 * rows * units),
        name="mlp",
    )(
        table,
        block_input,
        out_grad,
        *branches,
        output_bias[None],
        gain[None],
        shift[None],
        up_weight,
        up_bias[None],
        down_weight,
    )


def middle_kernel(count, hidden_ref, grad_ref, *refs):
    parts, refs = refs[:count], refs[count:]
    gain, output_weight, d_hidden_ref, d_branch_ref, d_attn_ref, sums_ref = refs
    unit, inverse = normalize(hidden_ref[...])
    d_mlp = parts[0][...].astype(F32)
    for part in parts[1:]:
        d_mlp += part[...].astype(F32)
    grad = grad_ref[...].astype(F32)
    d_hidden = grad + normalize_back(d_mlp * gain[...], unit, inverse)
    d_hidden_ref[...] = d_hidden
    d_branch = d_hidden.astype(BF16)
    d_branch_ref[...] = d_branch
    d_attn_ref[...] = product(output_weight[...], d_branch, 1, 1).astype(BF16)
    for at, values in enumerate((d_hidden, d_mlp * unit, d_mlp, grad)):
        sums_ref[pl.ds(at, 1), :] = jnp.sum(values, axis=0, keepdims=True)


def middle(hidden, out_grad, parts, gain, output_weight):
    rows, model = hidden.shape
    width = output_weight.shape[0]
    return pl.pallas_call(
        functools.partial(middle_kernel, len(parts)),
        out_shape=[
            struct((rows, model), F32),
            struct((rows, model), BF16),
            struct((width, rows), BF16),
            struct((4, model), F32),
        ],
        compiler_params=streaming,
        cost_estimate=cost(2 * rows * model * width, 6 * 2**20),
        name="middle",
    )(hidden, out_grad, *parts, gain[None], output_weight)


def mask_rows(piece, chip, crops):
    crop = lax.broadcasted_iota(jnp.int32, (HD, piece.shape[2]), 0)
    segment = piece[chip, pl.ds(seg_row, 16), :].astype(F32)[:1].astype(jnp.int32)
    return jnp.where((crop != segment) & (crop < crops), masked_value, 0.0)


def load_keys(piece, crops, keys, key_t, value_n):
    chips, _, patches = piece.shape
    for chip in range(chips):
        key = piece[chip, pl.ds(HD, HD), :]
        value = piece[chip, pl.ds(2 * HD, HD), :]
        place = pl.ds(chip * patches, patches)
        both = jnp.concatenate([key.astype(F32), mask_rows(piece, chip, crops)], axis=0)
        keys[place, :] = both.T.astype(BF16)
        key_t[:, place] = key
        value_n[place, :] = value.astype(F32).T.astype(BF16)


def masked_query(query_ref, dtype=BF16):
    query = query_ref[0, pl.ds(0, HD), :].astype(F32) * 0.125
    segment = query_ref[0, pl.ds(seg_row, 16), :].astype(F32)[:1].astype(jnp.int32)
    crop = lax.broadcasted_iota(jnp.int32, query.shape, 0)
    onehot = jnp.where(crop == segment, 1.0, 0.0)
    return jnp.concatenate([query, onehot], axis=0).astype(dtype)


def forward_kernel(
    crops, step, query_ref, own, other, raw_ref, out_ref, logsum_ref, key_t, value_n, scores
):
    @pl.when(pl.program_id(0) == 0)
    def _():
        start = 0
        for piece in (own, other):
            chips, _, patches = piece.shape
            for chip in range(chips):
                place = pl.ds(start, patches)
                key = piece[chip, pl.ds(HD, HD), :].astype(F32)
                key_t[:, place] = jnp.concatenate([key, mask_rows(piece, chip, crops)], axis=0).astype(BF16)
                value = piece[chip, pl.ds(2 * HD, HD), :].astype(F32)
                value = jnp.concatenate([value, jnp.ones_like(value)], axis=0)
                value_n[place, :] = value.T.astype(BF16)
                start += patches

    query = masked_query(query_ref, F32).T.astype(BF16)
    count = query.shape[0]
    top = jnp.full((count, 128), masked_value, F32)
    for start in range(0, key_t.shape[1], step):
        block = product(query, key_t[:, pl.ds(start, step)])
        scores[:, pl.ds(start, step)] = block
        for at in range(0, step, 128):
            top = jnp.maximum(top, block[:, at : at + 128])
    top = jnp.max(top, axis=1, keepdims=True)
    accum = jnp.zeros((count, 2 * HD), F32)
    for start in range(0, key_t.shape[1], step):
        weights = jnp.exp(scores[:, pl.ds(start, step)] - top).astype(BF16)
        accum += product(weights, value_n[pl.ds(start, step), :])
    accum = accum.T
    total = accum[HD : HD + 1]
    raw = accum[:HD] / total
    raw_ref[0] = raw
    out_ref[0] = raw.astype(BF16)
    top = jnp.broadcast_to(top, (count, 128)).T[:1]
    logsum_ref[0] = top + jnp.log(total)


def backward_kernel(
    crops,
    before,
    query_ref,
    grad_ref,
    raw_ref,
    logsum_ref,
    *refs,
):
    before_refs, refs = refs[:before], refs[before:]
    piece, (dquery_ref, sums_ref, keys, key_t, value_n, sums) = refs[0], refs[-6:]
    group = pl.program_id(0)

    @pl.when(group == 0)
    def _():
        load_keys(piece, crops, keys, key_t, value_n)
        sums[...] = jnp.zeros_like(sums)

    query = masked_query(query_ref)
    grad = grad_ref[0]
    grad_wide = grad.astype(F32)
    delta = jnp.sum(grad_wide * raw_ref[0], axis=0, keepdims=True)
    scaled = query_ref[0, pl.ds(0, HD), :].astype(F32) * 0.125
    zero = jnp.zeros_like(scaled)
    query_side = jnp.concatenate([scaled, zero], axis=0).T.astype(BF16)
    grad_side = jnp.concatenate([zero, grad_wide], axis=0).T.astype(BF16)
    probs = jnp.exp(product(keys[...], query) - logsum_ref[0])
    dprobs = product(value_n[...], grad)
    dscores = (probs * (dprobs - delta)).astype(BF16)
    sums[...] += product(dscores, query_side) + product(probs.astype(BF16), grad_side)
    dquery = product(key_t[...], dscores) * 0.125
    for ref in before_refs:
        dquery = ref[0] + dquery
    dquery_ref[0] = dquery.astype(dquery_ref.dtype)

    @pl.when(group == pl.num_programs(0) - 1)
    def _():
        chips, _, patches = sums_ref.shape
        for chip in range(chips):
            sums_ref[chip] = sums[pl.ds(chip * patches, patches), :].T.astype(sums_ref.dtype)


def key_step(count):
    return 1024 if count % 1024 == 0 else 256


def query_spec(rows, patches):
    return pl.BlockSpec((1, rows, patches), lambda group: (group, 0, 0))


def attention_forward(queries, own, other, crops):
    groups, _, patches = queries.shape
    count = 2 * own.shape[0] * own.shape[2]
    return pl.pallas_call(
        functools.partial(forward_kernel, crops, key_step(count)),
        grid=(groups,),
        in_specs=[
            query_spec(payload_rows, patches),
            whole_spec(own.shape),
            whole_spec(other.shape),
        ],
        out_specs=[query_spec(HD, patches), query_spec(HD, patches), query_spec(1, patches)],
        out_shape=[
            struct((groups, HD, patches), F32),
            struct((groups, HD, patches), BF16),
            struct((groups, 1, patches), F32),
        ],
        scratch_shapes=[
            pltpu.VMEM((2 * HD, count), BF16),
            pltpu.VMEM((count, 2 * HD), BF16),
            pltpu.VMEM((patches, count), F32),
        ],
        compiler_params=streaming,
        cost_estimate=cost(
            groups * patches * count * 4096, 4 * 2**20, groups * patches * count
        ),
        name="attention_forward",
    )(queries, own, other)


def backward_piece(queries, grads, raw, logsum, before, keys, earlier, index, pieces, crops, dtypes):
    groups, _, patches = queries.shape
    chips = keys.shape[0] // pieces
    count = chips * keys.shape[2]
    sums_shape = (chips, 2 * HD, keys.shape[2])
    return pl.pallas_call(
        functools.partial(backward_kernel, crops, len(before)),
        grid=(groups,),
        in_specs=[
            query_spec(payload_rows, patches),
            query_spec(HD, patches),
            query_spec(HD, patches),
            query_spec(1, patches),
        ]
        + [query_spec(HD, patches)] * len(before)
        + [pl.BlockSpec((chips,) + keys.shape[1:], lambda group: (index, 0, 0))]
        + [pl.BlockSpec(memory_space=pl.ANY)] * len(earlier),
        out_specs=[
            query_spec(HD, patches),
            pl.BlockSpec(sums_shape, lambda group: (index, 0, 0)),
        ],
        out_shape=[
            struct((groups, HD, patches), dtypes[0]),
            struct((keys.shape[0],) + sums_shape[1:], dtypes[1]),
        ],
        input_output_aliases={5 + len(before): 1} if earlier else {},
        scratch_shapes=[
            pltpu.VMEM((count, 2 * HD), BF16),
            pltpu.VMEM((HD, count), BF16),
            pltpu.VMEM((count, HD), BF16),
            pltpu.VMEM((count, 2 * HD), F32),
        ],
        compiler_params=params,
        cost_estimate=cost(
            groups * patches * count * 4096, 4 * 2**20, groups * patches * count
        ),
        name="attention_backward",
    )(queries, grads, raw, logsum, *before, keys, *earlier)


def swap_cores(values):
    return lax.ppermute(values, "core", [(0, 1), (1, 0)])


def to_heads(blocks):
    return lax.all_to_all(blocks, "chip", 0, 0, tiled=True)


def scatter_queries(values, heads, split):
    rows, patches = values.shape[0] // heads, values.shape[1]
    if split == 1:
        return to_heads(values.reshape(heads, rows, patches))
    part = patches // split
    blocks = values.reshape(heads, rows, split, part).transpose(0, 2, 1, 3)
    moved = to_heads(blocks.reshape(heads * split, rows, part))
    width = min(256, moved.shape[0] * part)
    joined = moved.transpose(1, 0, 2).reshape(rows, -1, width)
    return joined.transpose(1, 0, 2)


def gather_queries(values, heads, split, patches):
    rows = values.shape[1]
    if split == 1:
        return to_heads(values).reshape(heads * rows, patches)
    part = patches // split
    joined = values.transpose(1, 0, 2).reshape(rows, heads * split, part)
    moved = to_heads(joined.transpose(1, 0, 2)).reshape(heads, split, rows, part)
    return moved.transpose(0, 2, 1, 3).reshape(heads * rows, patches)


def across_heads(part):
    if lax.axis_size("head") == 2:
        return [part, lax.ppermute(part, "head", [(0, 1), (1, 0)])]
    return [lax.psum(part, "head")]


def ring_pairs(direction):
    chips = lax.axis_size("chip")
    order = list(range(0, chips, 2)) + list(range(chips - 1, 0, -2))
    return [(order[at], order[(at + direction) % chips]) for at in range(chips)]


def ring_table():
    chips, chip = lax.axis_size("chip"), lax.axis_index("chip")
    place = jnp.where(chip % 2 == 0, chip // 2, chips - 1 - chip // 2)
    steps = jnp.arange(2 * chips + 1, dtype=jnp.int32)
    places = (place + steps) % chips
    there = jnp.where(places < chips // 2, 2 * places, 2 * (chips - 1 - places) + 1)
    table = jnp.where(steps < chips, places, there)
    return jnp.where(steps == 2 * chips, lax.axis_index("core"), table).astype(jnp.int32)


def visit(streams, values):
    states, values = lax.optimization_barrier(([stream.state for stream in streams], values))
    for stream, state in zip(streams, states):
        stream.state = state
        stream.advance()
    return values


class Gather:
    def __init__(self, block, swap=False, take=None):
        self.chips, self.swap, self.take = lax.axis_size("chip"), swap, take
        self.blocks, self.pairs, self.count = [], [], 0
        self.state = ([], [], [])
        self.send([(0, block)], [block, block], [])

    def send(self, new, sides, outputs):
        self.blocks += new
        self.new = new
        self.count += 1
        reach = (self.chips // 2, (self.chips - 1) // 2)
        flying = [
            lax.ppermute(block, "chip", ring_pairs(direction))
            for block, direction, steps in zip(sides, (1, -1), reach)
            if self.count <= steps
        ]
        self.state = (flying, [swap_cores(block) for _, block in new] if self.swap else [], outputs)

    def advance(self):
        arrived, swapped, outputs = self.state
        pairs = [(step, near, far) for (step, near), far in zip(self.new, swapped)]
        self.pairs += pairs
        if self.take and pairs:
            outputs = self.take(outputs, pairs)
        new = [(side * self.count, block) for block, side in zip(arrived, (-1, 1))]
        self.send(new, arrived, outputs)

    def busy(self):
        return bool(self.state[0] or self.state[1])


def add_kernel(counts, _, *refs):
    outputs, refs = refs[-len(counts) :], list(refs[: -len(counts)])
    keep_in, far_in = refs.pop(0), refs.pop(0)
    for count, output in zip(counts, outputs):
        near, far = refs.pop(0), refs.pop(0)
        total = product(near[...], keep_in[...], 0, 0) + product(far[...], far_in[...], 0, 0)
        for _ in range(count):
            total += refs.pop(0)[...].astype(F32)
        output[...] = total.astype(BF16)


class Reduce:
    def __init__(self, keep, far, keep_in, far_in, table):
        self.chips, self.table = lax.axis_size("chip"), table
        self.operands, self.sides = (keep, far), (keep_in, far_in)
        self.units = keep.shape[1] // self.chips
        self.tiled = self.units % 128 == 0
        self.reach = (self.chips // 2, (self.chips - 1) // 2)
        self.count, self.gather = 0, None
        self.send(self.add([(self.reach[0], []), (-self.reach[1], [])]), [])

    def send(self, sides, held):
        self.count += 1
        flying = [
            lax.ppermute(block, "chip", ring_pairs(direction))
            for block, direction in zip(sides, (1, -1))
        ]
        self.state = (flying, held)

    def advance(self):
        if self.gather:
            self.gather.state = self.state
            self.gather.advance()
            self.state = self.gather.state
            return
        arrived, held = self.state
        wanted, done = [], self.count == self.reach[0]
        for block, reach, side in zip(arrived, self.reach, (1, -1)):
            left = reach - self.count
            if left > 0 or done:
                wanted.append((side * left, [block] + held))
            else:
                held = [block]
        if done:
            self.gather = Gather(self.add(wanted)[0], True, self.place)
            self.state = self.gather.state
        else:
            self.send(self.add([(step, parts[:1]) for step, parts in wanted]), held)

    def add(self, wanted):
        (rows, model), units, chips = self.sides[0].shape, self.units, self.chips
        if not self.tiled:
            sums = []
            for step, parts in wanted:
                start = self.table[step % chips] * units
                total = functools.reduce(jnp.add, (part.astype(F32) for part in parts), 0.0)
                for operand, side in zip(self.operands, self.sides):
                    block = lax.dynamic_slice_in_dim(operand, start, units, 1)
                    total += product(block, side, 0, 0)
                sums.append(total.astype(BF16))
            return sums
        side = pl.BlockSpec((rows, model), lambda at, table: (0, 0))
        whole = pl.BlockSpec((units, model), lambda at, table: (0, 0))
        specs, arrays = [side] * 2, list(self.sides)
        for step, parts in wanted:
            block = pl.BlockSpec(
                (rows, units), lambda at, table, step=step % chips: (0, table[step])
            )
            specs += [block] * 2 + [whole] * len(parts)
            arrays += list(self.operands) + parts
        return pl.pallas_call(
            functools.partial(add_kernel, [len(parts) for _, parts in wanted]),
            grid_spec=pltpu.PrefetchScalarGridSpec(
                num_scalar_prefetch=1,
                grid=(1,),
                in_specs=specs,
                out_specs=[whole] * len(wanted),
            ),
            out_shape=[struct((units, model), BF16)] * len(wanted),
            compiler_params=streaming,
            cost_estimate=cost(4 * rows * units * model * len(wanted), 4 * 2**20),
            name="ring_add",
        )(self.table, *arrays)

    def place(self, outputs, pairs):
        units, chips, model = self.units, self.chips, self.sides[0].shape[1]
        shapes = [struct((chips * units, model), F32), struct((model, chips * units), F32)]
        if not self.tiled:
            outputs = outputs or [jnp.zeros(shape.shape, F32) for shape in shapes]
            down, up = outputs
            is_down = self.table[2 * chips] == 0
            for step, near, far in pairs:
                start = self.table[step % chips] * units
                first = jnp.where(is_down, near, far).astype(F32)
                second = jnp.where(is_down, far, near).astype(F32).T
                down = lax.dynamic_update_slice_in_dim(down, first, start, 0)
                up = lax.dynamic_update_slice_in_dim(up, second, start, 1)
            return [down, up]
        first = pairs[0][0] % chips
        stride = pairs[-1][0] % chips - first
        block = pl.BlockSpec((units, model), lambda at, table: (0, 0))
        return pl.pallas_call(
            functools.partial(place_kernel, len(pairs)),
            grid_spec=pltpu.PrefetchScalarGridSpec(
                num_scalar_prefetch=1,
                grid=(len(pairs),),
                in_specs=[pl.BlockSpec(memory_space=pl.ANY)] * len(outputs)
                + [block] * (2 * len(pairs)),
                out_specs=[
                    pl.BlockSpec((units, model), lambda at, table: (table[first + at * stride], 0)),
                    pl.BlockSpec((model, units), lambda at, table: (0, table[first + at * stride])),
                ],
            ),
            out_shape=shapes,
            input_output_aliases={1 + at: at for at in range(len(outputs))},
            compiler_params=streaming,
            cost_estimate=cost(0, 2 * 2**20),
            name="place",
        )(self.table, *outputs, *[pair[1] for pair in pairs], *[pair[2] for pair in pairs])

    def busy(self):
        return self.gather is None or self.gather.busy()


def place_kernel(count, table, *refs):
    nears, fars, (down, up) = refs[-2 - 2 * count : -2 - count], refs[-2 - count : -2], refs[-2:]
    core = table[table.shape[0] - 1]

    def put(first, second):
        down[...] = first[...].astype(F32)
        up[...] = second[...].astype(F32).T

    for at, (near, far) in enumerate(zip(nears, fars)):
        here = pl.program_id(0) == at
        pl.when(here & (core == 0))(functools.partial(put, near, far))
        pl.when(here & (core != 0))(functools.partial(put, far, near))


def head_gradient_kernel(steps, table, query_ref, key_value_ref, *refs):
    blocks, out_ref = refs[:-1], refs[-1]
    chips = len(blocks)
    total = jnp.zeros(out_ref.shape, F32)
    for step, block in zip(steps, blocks):
        chip = table[chips + step % chips]
        grads = jnp.concatenate([query_ref[chip], key_value_ref[chip]], axis=0)
        total += product(grads, block[...])
    out_ref[...] = total.astype(BF16)


def head_gradient(dquery, key_value, inputs, table):
    count, rows, patches = dquery.shape
    steps, blocks = zip(*inputs.blocks)
    model = blocks[0].shape[1]
    step = math.gcd(model, 256)
    return pl.pallas_call(
        functools.partial(head_gradient_kernel, steps),
        grid_spec=pltpu.PrefetchScalarGridSpec(
            num_scalar_prefetch=1,
            grid=(model // step,),
            in_specs=[
                pl.BlockSpec(dquery.shape, lambda at, table: (0, 0, 0)),
                pl.BlockSpec(key_value.shape, lambda at, table: (0, 0, 0)),
            ]
            + [pl.BlockSpec((patches, step), lambda at, table: (0, at))] * count,
            out_specs=pl.BlockSpec((3 * rows, step), lambda at, table: (0, at)),
        ),
        out_shape=struct((3 * rows, model), BF16),
        compiler_params=streaming,
        cost_estimate=cost(6 * rows * count * patches * model, 6 * 2**20),
        name="head_gradient",
    )(table, dquery, key_value, *blocks)


def layout_kernel(steps, size, extra, table, *refs):
    count = len(steps)
    nears, fars, outputs, output_ref, small_ref, held = (
        refs[:count],
        refs[count : 2 * count],
        refs[2 * count : 2 * count + 3],
        refs[2 * count + 3],
        refs[2 * count + 4],
        refs[2 * count + 5],
    )
    at = pl.program_id(0)

    @pl.when(at == 0)
    def _():
        core = table[2 * count]
        for step, near, far in zip(steps, nears, fars):
            chip = table[count + step % count]
            for side, block in ((core, near), (1 - core, far)):
                held[chip, side] = block[pl.ds(0, size), :]
                output_ref[side, chip] = block[pl.ds(size, extra), :].astype(F32)
                small_ref[side, chip] = block[pl.ds(size + extra, small_rows), :].astype(F32)

    pair = [
        jnp.concatenate([held[2 * at + head, 0], held[2 * at + head, 1]], axis=0)
        for head in range(2)
    ]
    for index, output in enumerate(outputs):
        rows = [part[index * HD : index * HD + HD] for part in pair]
        output[...] = jnp.concatenate(rows, axis=0).astype(F32).T


def final_layout(pairs, size, table):
    count = len(pairs)
    steps, nears, fars = zip(*pairs)
    rows, model = nears[0].shape
    extra = rows - size - small_rows
    return pl.pallas_call(
        functools.partial(layout_kernel, steps, size, extra),
        grid_spec=pltpu.PrefetchScalarGridSpec(
            num_scalar_prefetch=1,
            grid=(count // 2,),
            in_specs=[pl.BlockSpec((rows, model), lambda at, table: (0, 0))] * (2 * count),
            out_specs=[pl.BlockSpec((model, 2 * HD), lambda at, table: (0, at))] * 3
            + [
                pl.BlockSpec((2, count, extra, model), lambda at, table: (0, 0, 0, 0)),
                pl.BlockSpec((2, count, small_rows, model), lambda at, table: (0, 0, 0, 0)),
            ],
            scratch_shapes=[pltpu.VMEM((count, 2, size, model), BF16)],
        ),
        out_shape=[struct((model, count * HD), F32)] * 3
        + [
            struct((2, count, extra, model), F32),
            struct((2, count, small_rows, model), F32),
        ],
        compiler_params=streaming,
        name="final_layout",
    )(table, *nears, *fars)


def core_half(values, axis, side):
    size = values.shape[axis] // 2
    return lax.dynamic_slice_in_dim(values, side * size, size, axis)


def share_halves(values, axis):
    core = lax.axis_index("core")
    return core_half(values, axis, core), swap_cores(core_half(values, axis, 1 - core))


def local(
    block_input,
    out_grad,
    segments,
    lead_steps,
    gain_attn,
    shift_attn,
    lead_weight,
    query_weight,
    key_weight,
    value_weight,
    output_weight,
    output_bias,
    gain_mlp,
    shift_mlp,
    up_weight,
    up_bias,
    down_weight,
    down_bias,
):
    rows, model = block_input.shape
    heads = query_weight.shape[1] // HD
    width = heads * HD
    chips, core = lax.axis_size("chip"), lax.axis_index("core")
    split = chips // heads
    crops = lead_steps.shape[0]
    table = ring_table()
    weights = (query_weight, key_weight, value_weight)
    payload, attn_in = project(
        block_input, segments, lead_steps, gain_attn, shift_attn, lead_weight, weights
    )
    if split == 1:
        own = to_heads(payload)
        queries = own
    else:
        queries = scatter_queries(payload.reshape(-1, rows), heads, split)
        own = to_heads(jnp.repeat(payload, split, axis=0))
    own, attn_in = lax.optimization_barrier((own, attn_in))
    inputs = Gather(attn_in)
    raw, out, logsum = attention_forward(queries, own, swap_cores(own), crops)
    other = swap_cores(own)
    attn_out = gather_queries(out, heads, split, rows)
    attn_out = visit([inputs], attn_out)
    branches = across_heads(product(attn_out, output_weight, 0, 0).astype(BF16))
    branches = visit([inputs], branches)
    keep, give, keep_in, give_in, hidden, dup_bias, mlp_part, d_mlp_part = mlp(
        table,
        block_input,
        out_grad,
        branches,
        output_bias,
        gain_mlp,
        shift_mlp,
        up_weight,
        up_bias,
        down_weight,
    )
    d_mlp = across_heads(d_mlp_part)
    ring = Reduce(keep, swap_cores(give), keep_in, swap_cores(give_in), table)
    mlp_part, d_mlp = lax.optimization_barrier((mlp_part, d_mlp))
    mlp_out = across_heads(mlp_part)
    d_hidden, d_branch, d_attn, sums = middle(hidden, out_grad, d_mlp, gain_mlp, output_weight)
    grads = scatter_queries(d_attn, heads, split)
    d_branch = visit([ring, inputs], d_branch)
    out_near, out_far = share_halves(attn_out, 0)
    doutput = product(out_near, d_branch) + product(out_far, swap_cores(d_branch))
    doutput = doutput.astype(BF16).reshape(chips, -1, model)
    pieces = 2
    dquery, turn = [], 0
    for keys, dtype in ((other, BF16), (own, F32)):
        piece_sums = []
        for index in range(pieces):
            last = keys is own and index == pieces - 1
            if turn == 1:
                grads, dquery, piece_sums = visit([ring, inputs], (grads, dquery, piece_sums))
            if turn == 2:
                far_sums = swap_cores(far_sums)
                doutput, dquery = lax.optimization_barrier((doutput, dquery))
                doutput = to_heads(doutput)
            if turn == 3:
                grads, dquery, piece_sums, mlp_out = visit(
                    [ring], (grads, dquery, piece_sums, mlp_out)
                )
                block_output = hidden + down_bias
                for part in mlp_out:
                    block_output += part.astype(F32)
                block_output = block_output.astype(BF16)
            dtypes = (BF16 if last else F32, dtype)
            *dquery, piece = backward_piece(
                queries, grads, raw, logsum, dquery, keys, piece_sums, index, pieces, crops, dtypes
            )
            piece_sums = [piece]
            turn += 1
        if keys is other:
            far_sums = piece
    (dquery,) = dquery
    key_value = (piece + far_sums.astype(F32)).astype(BF16)
    doutput, key_value = lax.optimization_barrier((doutput, key_value))
    doutput = jnp.sum(doutput.astype(F32), axis=0)
    small = jnp.concatenate([sums.reshape(-1), dup_bias[0]])
    small = jnp.pad(small, (0, small_rows * model - small.shape[0])).reshape(small_rows, model)
    doutput = jnp.concatenate([doutput, small], axis=0).astype(BF16)
    if split == 1:
        moved = to_heads(jnp.concatenate([dquery, key_value], axis=1))
        projections = head_gradient(dquery, key_value, inputs, table)
        near, far = share_halves(projections, 0)
        projections = (near.astype(F32) + far.astype(F32)).astype(BF16)
        size = projections.shape[0]
        blocks = jnp.concatenate([projections, doutput], axis=0)
        dquery, dkey, dvalue = (
            moved[:, at * HD : at * HD + HD].reshape(width, rows) for at in range(3)
        )
    else:
        dquery = gather_queries(dquery, heads, split, rows)
        moved = to_heads(key_value).reshape(heads, split, 2 * HD, rows).astype(F32)
        moved = jnp.sum(moved, axis=1).astype(BF16)
        dkey, dvalue = (moved[:, at * HD : at * HD + HD].reshape(width, rows) for at in range(2))
        size, blocks = 0, doutput
        projections = [
            lax.psum(product(attn_in, grad, 0, 1).astype(BF16), ("chip", "core")).astype(F32)
            for grad in (dquery, dkey, dvalue)
        ]
    while inputs.busy():
        visit([inputs], ())
    gathered = Gather(blocks, True)
    visit([ring], blocks)
    d_part = (
        product(dquery, query_weight, 0, 1)
        + product(dkey, key_weight, 0, 1)
        + product(dvalue, value_weight, 0, 1)
    )
    d_in = across_heads(d_part.astype(BF16))
    unit_attn, inverse_attn = normalize(block_input.astype(F32))
    onehot = (segments[:, None] == jnp.arange(crops, dtype=jnp.int32)[None, :]).astype(F32)
    lead = jnp.sum(onehot * lead_steps.astype(F32)[None, :], axis=1) / 12.0
    ends = jnp.stack(
        [
            jnp.sum(d_part * unit_attn, axis=0),
            jnp.sum(d_part, axis=0),
            jnp.sum(lead[:, None] * d_part, axis=0),
        ]
    )
    ends = jnp.pad(ends.reshape(-1, 128), ((0, -ends.size // 128 % 16), (0, 0))).astype(BF16)
    everyone = ("chip", "core", "head")
    ends = jnp.broadcast_to(ends, (lax.axis_size(everyone),) + ends.shape)
    ends = lax.all_to_all(ends, everyone, 0, 0, tiled=True)
    d_in = visit([ring, gathered], d_in)
    d_in = functools.reduce(jnp.add, (part.astype(F32) for part in d_in))
    input_grad = (d_hidden + normalize_back(d_in * gain_attn, unit_attn, inverse_attn)).astype(
        BF16
    )
    input_grad, ends = visit([ring, gathered], (input_grad, ends))
    while ring.busy() or gathered.busy():
        visit([ring, gathered], ())
    ends = jnp.sum(ends.astype(F32), axis=0).reshape(-1)[: 3 * model].reshape(3, model)
    ddown_weight, dup_weight = ring.state[2]
    if split == 1:
        *projections, doutput_weight, small = final_layout(gathered.pairs, size, table)
        doutput_weight = doutput_weight.reshape(width, model)
    else:
        blocks = jnp.zeros((2, chips) + blocks.shape, F32)
        for step, near, far in gathered.pairs:
            for side, block in ((core, near), (1 - core, far)):
                start = (side, table[chips + step % chips], 0, 0)
                block = block[None, None].astype(F32)
                blocks = lax.dynamic_update_slice(blocks, block, start)
        doutput_weight = blocks[:, :, :-small_rows].reshape(width, model)
        small = blocks[:, :, -small_rows:]
    small = jnp.sum(small, axis=(0, 1))
    dup_bias = small[4:].reshape(-1)[: dup_bias.shape[1]]
    return (
        block_output,
        input_grad,
        ends[0],
        ends[1],
        ends[2],
        *projections,
        doutput_weight,
        *small[:3],
        dup_weight,
        dup_bias,
        ddown_weight,
        small[3],
    )


def solution(mesh):
    bands, halves = mesh.shape["band"], mesh.shape["head"]
    inner = Mesh(mesh.devices.reshape(bands // 2, 2, halves), ("chip", "core", "head"))
    band = ("chip", "core")
    rows, columns, split_rows = P(band, None), P(None, "head"), P("head", None)
    return jax.shard_map(
        local,
        mesh=inner,
        in_specs=(
            rows,
            rows,
            P(band),
            P(),
            P(),
            P(),
            P(),
            columns,
            columns,
            columns,
            split_rows,
            P(),
            P(),
            P(),
            columns,
            P("head"),
            split_rows,
            P(),
        ),
        out_specs=(
            rows,
            rows,
            P(),
            P(),
            P(),
            columns,
            columns,
            columns,
            split_rows,
            P(),
            P(),
            P(),
            columns,
            P("head"),
            split_rows,
            P(),
        ),
        check_vma=False,
    )
```

```python
import functools
import math

import jax
import jax.numpy as jnp
from jax import lax
from jax.experimental import pallas as pl
from jax.experimental.pallas import tpu as pltpu
from jax.sharding import Mesh, PartitionSpec as P

HD = 64
F32 = jnp.float32
BF16 = jnp.bfloat16
eps = 1e-05
masked_value = -1e30
seg_row = 3 * HD
payload_rows = 3 * HD + 16
small_rows = 8
params = pltpu.CompilerParams(vmem_limit_bytes=48 * 2**20)
streaming = pltpu.CompilerParams(vmem_limit_bytes=60 * 2**20)


def normalize(values):
    centred = values - jnp.mean(values, axis=-1, keepdims=True)
    inverse = lax.rsqrt(jnp.mean(centred * centred, axis=-1, keepdims=True) + eps)
    return (centred * inverse, inverse)


def normalize_back(grad_unit, unit, inverse):
    return inverse * (
        grad_unit
        - jnp.mean(grad_unit, axis=-1, keepdims=True)
        - unit * jnp.mean(grad_unit * unit, axis=-1, keepdims=True)
    )


def product(first, second, first_axis=1, second_axis=0):
    return lax.dot_general(
        first,
        second,
        (((first_axis,), (second_axis,)), ((), ())),
        preferred_element_type=jnp.float32,
    )


def struct(shape, dtype):
    return jax.ShapeDtypeStruct(shape, dtype)


def whole_spec(shape):
    return pl.BlockSpec(shape, lambda *at: (0,) * len(shape))


light = pl.CostEstimate(flops=1, bytes_accessed=1, transcendentals=0)


def project_kernel(
    input_ref, segment_ref, steps_ref, gain, shift, lead_weight, *refs
):
    weights, (payload_ref, attn_in_ref) = refs[:3], refs[3:]
    rows = input_ref.shape[0]

    @pl.when(pl.program_id(0) == 0)
    def _():
        unit, _ = normalize(input_ref[...].astype(F32))
        crops = steps_ref.shape[0]
        crop = lax.broadcasted_iota(jnp.int32, (crops, rows), 0)
        steps = jnp.zeros((crops, rows), jnp.int32)
        for at in range(crops):
            steps = jnp.where(crop == at, steps_ref[at], steps)
        steps = jnp.where(crop == segment_ref[...], steps, 0).astype(F32)
        lead = product(steps, jnp.ones((crops, 128), F32), 0, 0)[:, :1] / 12.0
        attn_in = unit * gain[...] + shift[...] + lead * lead_weight[...]
        attn_in_ref[...] = attn_in.astype(BF16)

    for at, weight in enumerate(weights):
        part = product(attn_in_ref[...], weight[...]).T.astype(BF16)
        for head in range(2):
            payload_ref[head, pl.ds(at * HD, HD), :] = part[head * HD : head * HD + HD]
    segment = jnp.broadcast_to(segment_ref[...].astype(F32), (16, rows)).astype(BF16)
    for head in range(2):
        payload_ref[head, pl.ds(seg_row, 16), :] = segment


def project(block_input, segments, lead_steps, gain, shift, lead_weight, weights):
    rows, model = block_input.shape
    heads = weights[0].shape[1] // HD
    line = whole_spec((1, model))
    column = pl.BlockSpec((model, 2 * HD), lambda at: (0, at))
    return pl.pallas_call(
        project_kernel,
        grid=(heads // 2,),
        in_specs=[whole_spec(block_input.shape), whole_spec((1, rows)), pl.BlockSpec(memory_space=pltpu.SMEM)]
        + [line] * 3
        + [column] * 3,
        out_specs=[
            pl.BlockSpec((2, payload_rows, rows), lambda at: (at, 0, 0)),
            whole_spec((rows, model)),
        ],
        out_shape=[struct((heads, payload_rows, rows), BF16), struct((rows, model), BF16)],
        compiler_params=streaming,
        cost_estimate=light,
        name="project",
    )(block_input, segments[None], lead_steps, gain[None], shift[None], lead_weight[None], *weights)


def mlp_kernel(count, core_ref, input_ref, grad_ref, *refs):
    branches, refs = refs[:count], refs[count:]
    output_bias, gain, shift, up_weight, up_bias, down_weight = refs[:6]
    keep_ref, give_ref, keep_in_ref, give_in_ref, hidden_ref, bias_ref, forward_ref, back_ref = refs[
        6:14
    ]
    mlp_in_ref, forward, back = refs[14:]
    at = pl.program_id(0)
    is_down = core_ref[core_ref.shape[0] - 1] == 0

    @pl.when(at == 0)
    def _():
        hidden = input_ref[...].astype(F32) + output_bias[...]
        for branch in branches:
            hidden += branch[...].astype(F32)
        hidden_ref[...] = hidden
        unit, _ = normalize(hidden)
        mlp_in = (unit * gain[...] + shift[...]).astype(BF16)
        mlp_in_ref[...] = mlp_in
        keep_in_ref[...] = jnp.where(is_down, grad_ref[...], mlp_in)
        give_in_ref[...] = jnp.where(is_down, mlp_in, grad_ref[...])
        forward[...] = jnp.zeros_like(forward)
        back[...] = jnp.zeros_like(back)

    upper = product(mlp_in_ref[...], up_weight[...]) + up_bias[...]
    share = 0.5 + 0.5 * lax.erf(upper * math.sqrt(0.5))
    slope = share + upper * (jnp.exp(upper * upper * -0.5) * (1.0 / math.sqrt(2.0 * math.pi)))
    active = (upper * share).astype(BF16)
    d_active = product(grad_ref[...], down_weight[...], 1, 1)
    d_upper = (d_active * slope).astype(BF16)
    keep_ref[...] = jnp.where(is_down, active, d_upper)
    give_ref[...] = jnp.where(is_down, d_upper, active)
    bias_ref[...] = jnp.sum(d_upper.astype(F32), axis=0, keepdims=True)
    forward[...] += product(active, down_weight[...])
    back[...] += product(d_upper, up_weight[...], 1, 1)

    @pl.when(at == pl.num_programs(0) - 1)
    def _():
        forward_ref[...] = forward[...].astype(BF16)
        back_ref[...] = back[...].astype(BF16)


def mlp(
    table, block_input, out_grad, branches, output_bias, gain, shift, up_weight, up_bias, down_weight
):
    rows, model = block_input.shape
    units = up_weight.shape[1]
    step = math.gcd(units, 512)
    tile, line = whole_spec((rows, model)), whole_spec((1, model))
    wide = pl.BlockSpec((rows, step), lambda at, table: (0, at))
    bias = pl.BlockSpec((1, step), lambda at, table: (0, at))
    return pl.pallas_call(
        functools.partial(mlp_kernel, len(branches)),
        grid_spec=pltpu.PrefetchScalarGridSpec(
            num_scalar_prefetch=1,
            grid=(units // step,),
            in_specs=[tile] * (2 + len(branches))
            + [line] * 3
            + [
                pl.BlockSpec((model, step), lambda at, table: (0, at)),
                bias,
                pl.BlockSpec((step, model), lambda at, table: (at, 0)),
            ],
            out_specs=[wide, wide, tile, tile, tile, bias, tile, tile],
            scratch_shapes=[pltpu.VMEM((rows, model), BF16)]
            + [pltpu.VMEM((rows, model), F32)] * 2,
        ),
        out_shape=[struct((rows, units), BF16)] * 2
        + [struct((rows, model), BF16)] * 2
        + [
            struct((rows, model), F32),
            struct((1, units), F32),
            struct((rows, model), BF16),
            struct((rows, model), BF16),
        ],
        compiler_params=streaming,
        cost_estimate=light,
        name="mlp",
    )(
        table,
        block_input,
        out_grad,
        *branches,
        output_bias[None],
        gain[None],
        shift[None],
        up_weight,
        up_bias[None],
        down_weight,
    )


def middle_kernel(count, hidden_ref, grad_ref, *refs):
    parts, refs = refs[:count], refs[count:]
    gain, output_weight, d_hidden_ref, d_branch_ref, d_attn_ref, sums_ref = refs
    unit, inverse = normalize(hidden_ref[...])
    d_mlp = parts[0][...].astype(F32)
    for part in parts[1:]:
        d_mlp += part[...].astype(F32)
    grad = grad_ref[...].astype(F32)
    d_hidden = grad + normalize_back(d_mlp * gain[...], unit, inverse)
    d_hidden_ref[...] = d_hidden
    d_branch = d_hidden.astype(BF16)
    d_branch_ref[...] = d_branch
    d_attn_ref[...] = product(output_weight[...], d_branch, 1, 1).astype(BF16)
    for at, values in enumerate((d_hidden, d_mlp * unit, d_mlp, grad)):
        sums_ref[pl.ds(at, 1), :] = jnp.sum(values, axis=0, keepdims=True)


def middle(hidden, out_grad, parts, gain, output_weight):
    rows, model = hidden.shape
    width = output_weight.shape[0]
    return pl.pallas_call(
        functools.partial(middle_kernel, len(parts)),
        out_shape=[
            struct((rows, model), F32),
            struct((rows, model), BF16),
            struct((width, rows), BF16),
            struct((4, model), F32),
        ],
        compiler_params=streaming,
        cost_estimate=light,
        name="middle",
    )(hidden, out_grad, *parts, gain[None], output_weight)


def mask_rows(piece, chip, crops):
    crop = lax.broadcasted_iota(jnp.int32, (HD, piece.shape[2]), 0)
    segment = piece[chip, pl.ds(seg_row, 16), :].astype(F32)[:1].astype(jnp.int32)
    return jnp.where((crop != segment) & (crop < crops), masked_value, 0.0)


def load_keys(piece, crops, keys, key_t, value_n):
    chips, _, patches = piece.shape
    for chip in range(chips):
        key = piece[chip, pl.ds(HD, HD), :]
        value = piece[chip, pl.ds(2 * HD, HD), :]
        place = pl.ds(chip * patches, patches)
        both = jnp.concatenate([key.astype(F32), mask_rows(piece, chip, crops)], axis=0)
        keys[place, :] = both.T.astype(BF16)
        key_t[:, place] = key
        value_n[place, :] = value.astype(F32).T.astype(BF16)


def masked_query(query_ref, dtype=BF16):
    query = query_ref[0, pl.ds(0, HD), :].astype(F32) * 0.125
    segment = query_ref[0, pl.ds(seg_row, 16), :].astype(F32)[:1].astype(jnp.int32)
    crop = lax.broadcasted_iota(jnp.int32, query.shape, 0)
    onehot = jnp.where(crop == segment, 1.0, 0.0)
    return jnp.concatenate([query, onehot], axis=0).astype(dtype)


def forward_kernel(
    crops, step, query_ref, own, other, raw_ref, out_ref, logsum_ref, key_t, value_n, scores
):
    @pl.when(pl.program_id(0) == 0)
    def _():
        start = 0
        for piece in (own, other):
            chips, _, patches = piece.shape
            for chip in range(chips):
                place = pl.ds(start, patches)
                key = piece[chip, pl.ds(HD, HD), :].astype(F32)
                key_t[:, place] = jnp.concatenate([key, mask_rows(piece, chip, crops)], axis=0).astype(BF16)
                value = piece[chip, pl.ds(2 * HD, HD), :].astype(F32)
                value = jnp.concatenate([value, jnp.ones_like(value)], axis=0)
                value_n[place, :] = value.T.astype(BF16)
                start += patches

    query = masked_query(query_ref, F32).T.astype(BF16)
    count = query.shape[0]
    top = jnp.full((count, 128), masked_value, F32)
    for start in range(0, key_t.shape[1], step):
        block = product(query, key_t[:, pl.ds(start, step)])
        scores[:, pl.ds(start, step)] = block
        for at in range(0, step, 128):
            top = jnp.maximum(top, block[:, at : at + 128])
    top = jnp.max(top, axis=1, keepdims=True)
    accum = jnp.zeros((count, 2 * HD), F32)
    for start in range(0, key_t.shape[1], step):
        weights = jnp.exp(scores[:, pl.ds(start, step)] - top).astype(BF16)
        accum += product(weights, value_n[pl.ds(start, step), :])
    accum = accum.T
    total = accum[HD : HD + 1]
    raw = accum[:HD] / total
    raw_ref[0] = raw
    out_ref[0] = raw.astype(BF16)
    top = jnp.broadcast_to(top, (count, 128)).T[:1]
    logsum_ref[0] = top + jnp.log(total)


def backward_kernel(
    crops,
    before,
    query_ref,
    grad_ref,
    raw_ref,
    logsum_ref,
    *refs,
):
    before_refs, refs = refs[:before], refs[before:]
    piece, (dquery_ref, sums_ref, keys, key_t, value_n, sums) = refs[0], refs[-6:]
    group = pl.program_id(0)

    @pl.when(group == 0)
    def _():
        load_keys(piece, crops, keys, key_t, value_n)
        sums[...] = jnp.zeros_like(sums)

    query = masked_query(query_ref)
    grad = grad_ref[0]
    grad_wide = grad.astype(F32)
    delta = jnp.sum(grad_wide * raw_ref[0], axis=0, keepdims=True)
    scaled = query_ref[0, pl.ds(0, HD), :].astype(F32) * 0.125
    zero = jnp.zeros_like(scaled)
    query_side = jnp.concatenate([scaled, zero], axis=0).T.astype(BF16)
    grad_side = jnp.concatenate([zero, grad_wide], axis=0).T.astype(BF16)
    probs = jnp.exp(product(keys[...], query) - logsum_ref[0])
    dprobs = product(value_n[...], grad)
    dscores = (probs * (dprobs - delta)).astype(BF16)
    sums[...] += product(dscores, query_side) + product(probs.astype(BF16), grad_side)
    dquery = product(key_t[...], dscores) * 0.125
    for ref in before_refs:
        dquery = ref[0] + dquery
    dquery_ref[0] = dquery.astype(dquery_ref.dtype)

    @pl.when(group == pl.num_programs(0) - 1)
    def _():
        chips, _, patches = sums_ref.shape
        for chip in range(chips):
            sums_ref[chip] = sums[pl.ds(chip * patches, patches), :].T.astype(sums_ref.dtype)


def key_step(count):
    return 1024 if count % 1024 == 0 else 256


def query_spec(rows, patches):
    return pl.BlockSpec((1, rows, patches), lambda group: (group, 0, 0))


def attention_forward(queries, own, other, crops):
    groups, _, patches = queries.shape
    count = 2 * own.shape[0] * own.shape[2]
    return pl.pallas_call(
        functools.partial(forward_kernel, crops, key_step(count)),
        grid=(groups,),
        in_specs=[
            query_spec(payload_rows, patches),
            whole_spec(own.shape),
            whole_spec(other.shape),
        ],
        out_specs=[query_spec(HD, patches), query_spec(HD, patches), query_spec(1, patches)],
        out_shape=[
            struct((groups, HD, patches), F32),
            struct((groups, HD, patches), BF16),
            struct((groups, 1, patches), F32),
        ],
        scratch_shapes=[
            pltpu.VMEM((2 * HD, count), BF16),
            pltpu.VMEM((count, 2 * HD), BF16),
            pltpu.VMEM((patches, count), F32),
        ],
        compiler_params=streaming,
        cost_estimate=light,
        name="attention_forward",
    )(queries, own, other)


def backward_piece(queries, grads, raw, logsum, before, keys, earlier, index, pieces, crops, dtypes):
    groups, _, patches = queries.shape
    chips = keys.shape[0] // pieces
    count = chips * keys.shape[2]
    sums_shape = (chips, 2 * HD, keys.shape[2])
    return pl.pallas_call(
        functools.partial(backward_kernel, crops, len(before)),
        grid=(groups,),
        in_specs=[
            query_spec(payload_rows, patches),
            query_spec(HD, patches),
            query_spec(HD, patches),
            query_spec(1, patches),
        ]
        + [query_spec(HD, patches)] * len(before)
        + [pl.BlockSpec((chips,) + keys.shape[1:], lambda group: (index, 0, 0))]
        + [pl.BlockSpec(memory_space=pl.ANY)] * len(earlier),
        out_specs=[
            query_spec(HD, patches),
            pl.BlockSpec(sums_shape, lambda group: (index, 0, 0)),
        ],
        out_shape=[
            struct((groups, HD, patches), dtypes[0]),
            struct((keys.shape[0],) + sums_shape[1:], dtypes[1]),
        ],
        input_output_aliases={5 + len(before): 1} if earlier else {},
        scratch_shapes=[
            pltpu.VMEM((count, 2 * HD), BF16),
            pltpu.VMEM((HD, count), BF16),
            pltpu.VMEM((count, HD), BF16),
            pltpu.VMEM((count, 2 * HD), F32),
        ],
        compiler_params=params,
        cost_estimate=light,
        name="attention_backward",
    )(queries, grads, raw, logsum, *before, keys, *earlier)


def swap_cores(values):
    return lax.ppermute(values, "core", [(0, 1), (1, 0)])


def to_heads(blocks):
    return lax.all_to_all(blocks, "chip", 0, 0, tiled=True)


def scatter_queries(values, heads, split):
    rows, patches = values.shape[0] // heads, values.shape[1]
    if split == 1:
        return to_heads(values.reshape(heads, rows, patches))
    part = patches // split
    blocks = values.reshape(heads, rows, split, part).transpose(0, 2, 1, 3)
    moved = to_heads(blocks.reshape(heads * split, rows, part))
    width = min(256, moved.shape[0] * part)
    joined = moved.transpose(1, 0, 2).reshape(rows, -1, width)
    return joined.transpose(1, 0, 2)


def gather_queries(values, heads, split, patches):
    rows = values.shape[1]
    if split == 1:
        return to_heads(values).reshape(heads * rows, patches)
    part = patches // split
    joined = values.transpose(1, 0, 2).reshape(rows, heads * split, part)
    moved = to_heads(joined.transpose(1, 0, 2)).reshape(heads, split, rows, part)
    return moved.transpose(0, 2, 1, 3).reshape(heads * rows, patches)


def across_heads(part):
    if lax.axis_size("head") == 2:
        return [part, lax.ppermute(part, "head", [(0, 1), (1, 0)])]
    return [lax.psum(part, "head")]


def ring_pairs(direction):
    chips = lax.axis_size("chip")
    order = list(range(0, chips, 2)) + list(range(chips - 1, 0, -2))
    return [(order[at], order[(at + direction) % chips]) for at in range(chips)]


def ring_table():
    chips, chip = lax.axis_size("chip"), lax.axis_index("chip")
    place = jnp.where(chip % 2 == 0, chip // 2, chips - 1 - chip // 2)
    steps = jnp.arange(2 * chips + 1, dtype=jnp.int32)
    places = (place + steps) % chips
    there = jnp.where(places < chips // 2, 2 * places, 2 * (chips - 1 - places) + 1)
    table = jnp.where(steps < chips, places, there)
    return jnp.where(steps == 2 * chips, lax.axis_index("core"), table).astype(jnp.int32)


def visit(streams, values):
    states, values = lax.optimization_barrier(([stream.state for stream in streams], values))
    for stream, state in zip(streams, states):
        stream.advance(state)
    ready, values = lax.optimization_barrier(([stream.ready for stream in streams], values))
    for stream, blocks in zip(streams, ready):
        stream.send(blocks)
    return values


class Gather:
    def __init__(self, block, swap=False, take=None):
        self.chips, self.swap, self.take = lax.axis_size("chip"), swap, take
        self.blocks, self.pairs, self.count = [], [], 0
        self.new, self.outputs = [0], []
        self.ready = [block]

    def send(self, ready):
        new = list(zip(self.new, ready))
        self.blocks += new
        self.new = new
        self.count += 1
        sides = ready if len(ready) > 1 else ready * 2
        reach = (self.chips // 2, (self.chips - 1) // 2)
        flying = [
            lax.ppermute(block, "chip", ring_pairs(direction))
            for block, direction, steps in zip(sides, (1, -1), reach)
            if self.count <= steps
        ]
        self.state = (flying, [swap_cores(block) for block in ready] if self.swap else [], self.outputs)

    def advance(self, state):
        self.ready, swapped, self.outputs = state
        pairs = [(step, near, far) for (step, near), far in zip(self.new, swapped)]
        self.pairs += pairs
        if self.take and pairs:
            self.outputs = self.take(self.outputs, pairs)
        self.new = [side * self.count for side in (-1, 1)][: len(self.ready)]

    def busy(self):
        return bool(self.state[0] or self.state[1])


def add_kernel(counts, _, *refs):
    outputs, refs = refs[-len(counts) :], list(refs[: -len(counts)])
    keep_in, far_in = refs.pop(0), refs.pop(0)
    for count, output in zip(counts, outputs):
        near, far = refs.pop(0), refs.pop(0)
        total = product(near[...], keep_in[...], 0, 0) + product(far[...], far_in[...], 0, 0)
        for _ in range(count):
            total += refs.pop(0)[...].astype(F32)
        output[...] = total.astype(BF16)


class Reduce:
    def __init__(self, keep, far, keep_in, far_in, table):
        self.chips, self.table = lax.axis_size("chip"), table
        self.operands, self.sides = (keep, far), (keep_in, far_in)
        self.units = keep.shape[1] // self.chips
        self.tiled = self.units % 128 == 0
        self.reach = (self.chips // 2, (self.chips - 1) // 2)
        self.count, self.gather, self.held = 0, None, []
        self.send(self.add([(self.reach[0], []), (-self.reach[1], [])]))

    def send(self, ready):
        if self.gather:
            self.gather.send(ready)
            self.state = self.gather.state
            return
        self.count += 1
        flying = [
            lax.ppermute(block, "chip", ring_pairs(direction))
            for block, direction in zip(ready, (1, -1))
        ]
        self.state = (flying, self.held)

    def advance(self, state):
        if self.gather:
            self.gather.advance(state)
            self.ready = self.gather.ready
            return
        arrived, self.held = state
        wanted, done = [], self.count == self.reach[0]
        for block, reach, side in zip(arrived, self.reach, (1, -1)):
            left = reach - self.count
            if left > 0:
                wanted.append((side * left, [block]))
            elif done:
                wanted.append((0, [block] + self.held))
            else:
                self.held = [block]
        self.ready = self.add(wanted)
        if done:
            self.gather = Gather(self.ready[0], True, self.place)

    def add(self, wanted):
        (rows, model), units, chips = self.sides[0].shape, self.units, self.chips
        if not self.tiled:
            sums = []
            for step, parts in wanted:
                start = self.table[step % chips] * units
                total = functools.reduce(jnp.add, (part.astype(F32) for part in parts), 0.0)
                for operand, side in zip(self.operands, self.sides):
                    block = lax.dynamic_slice_in_dim(operand, start, units, 1)
                    total += product(block, side, 0, 0)
                sums.append(total.astype(BF16))
            return sums
        side = pl.BlockSpec((rows, model), lambda at, table: (0, 0))
        whole = pl.BlockSpec((units, model), lambda at, table: (0, 0))
        specs, arrays = [side] * 2, list(self.sides)
        for step, parts in wanted:
            block = pl.BlockSpec(
                (rows, units), lambda at, table, step=step % chips: (0, table[step])
            )
            specs += [block] * 2 + [whole] * len(parts)
            arrays += list(self.operands) + parts
        return pl.pallas_call(
            functools.partial(add_kernel, [len(parts) for _, parts in wanted]),
            grid_spec=pltpu.PrefetchScalarGridSpec(
                num_scalar_prefetch=1,
                grid=(1,),
                in_specs=specs,
                out_specs=[whole] * len(wanted),
            ),
            out_shape=[struct((units, model), BF16)] * len(wanted),
            compiler_params=streaming,
            cost_estimate=light,
            name="ring_add",
        )(self.table, *arrays)

    def place(self, outputs, pairs):
        units, chips, model = self.units, self.chips, self.sides[0].shape[1]
        shapes = [struct((chips * units, model), F32), struct((model, chips * units), F32)]
        if not self.tiled:
            outputs = outputs or [jnp.zeros(shape.shape, F32) for shape in shapes]
            down, up = outputs
            is_down = self.table[2 * chips] == 0
            for step, near, far in pairs:
                start = self.table[step % chips] * units
                first = jnp.where(is_down, near, far).astype(F32)
                second = jnp.where(is_down, far, near).astype(F32).T
                down = lax.dynamic_update_slice_in_dim(down, first, start, 0)
                up = lax.dynamic_update_slice_in_dim(up, second, start, 1)
            return [down, up]
        first = pairs[0][0] % chips
        stride = pairs[-1][0] % chips - first
        block = pl.BlockSpec((units, model), lambda at, table: (0, 0))
        return pl.pallas_call(
            functools.partial(place_kernel, len(pairs)),
            grid_spec=pltpu.PrefetchScalarGridSpec(
                num_scalar_prefetch=1,
                grid=(len(pairs),),
                in_specs=[pl.BlockSpec(memory_space=pl.ANY)] * len(outputs)
                + [block] * (2 * len(pairs)),
                out_specs=[
                    pl.BlockSpec((units, model), lambda at, table: (table[first + at * stride], 0)),
                    pl.BlockSpec((model, units), lambda at, table: (0, table[first + at * stride])),
                ],
            ),
            out_shape=shapes,
            input_output_aliases={1 + at: at for at in range(len(outputs))},
            compiler_params=streaming,
            cost_estimate=light,
            name="place",
        )(self.table, *outputs, *[pair[1] for pair in pairs], *[pair[2] for pair in pairs])

    def busy(self):
        return self.gather is None or self.gather.busy()


def place_kernel(count, table, *refs):
    nears, fars, (down, up) = refs[-2 - 2 * count : -2 - count], refs[-2 - count : -2], refs[-2:]
    core = table[table.shape[0] - 1]

    def put(first, second):
        down[...] = first[...].astype(F32)
        up[...] = second[...].astype(F32).T

    for at, (near, far) in enumerate(zip(nears, fars)):
        here = pl.program_id(0) == at
        pl.when(here & (core == 0))(functools.partial(put, near, far))
        pl.when(here & (core != 0))(functools.partial(put, far, near))


def head_gradient_kernel(steps, table, query_ref, key_value_ref, *refs):
    blocks, out_ref = refs[:-1], refs[-1]
    chips = len(blocks)
    total = jnp.zeros(out_ref.shape, F32)
    for step, block in zip(steps, blocks):
        chip = table[chips + step % chips]
        grads = jnp.concatenate([query_ref[chip], key_value_ref[chip]], axis=0)
        total += product(grads, block[...])
    out_ref[...] = total.astype(BF16)


def head_gradient(dquery, key_value, inputs, table):
    count, rows, patches = dquery.shape
    steps, blocks = zip(*inputs.blocks)
    model = blocks[0].shape[1]
    step = math.gcd(model, 256)
    return pl.pallas_call(
        functools.partial(head_gradient_kernel, steps),
        grid_spec=pltpu.PrefetchScalarGridSpec(
            num_scalar_prefetch=1,
            grid=(model // step,),
            in_specs=[
                pl.BlockSpec(dquery.shape, lambda at, table: (0, 0, 0)),
                pl.BlockSpec(key_value.shape, lambda at, table: (0, 0, 0)),
            ]
            + [pl.BlockSpec((patches, step), lambda at, table: (0, at))] * count,
            out_specs=pl.BlockSpec((3 * rows, step), lambda at, table: (0, at)),
        ),
        out_shape=struct((3 * rows, model), BF16),
        compiler_params=streaming,
        cost_estimate=light,
        name="head_gradient",
    )(table, dquery, key_value, *blocks)


def layout_kernel(steps, size, extra, table, *refs):
    count = len(steps)
    nears, fars, outputs, output_ref, small_ref, held = (
        refs[:count],
        refs[count : 2 * count],
        refs[2 * count : 2 * count + 3],
        refs[2 * count + 3],
        refs[2 * count + 4],
        refs[2 * count + 5],
    )
    at = pl.program_id(0)

    @pl.when(at == 0)
    def _():
        core = table[2 * count]
        for step, near, far in zip(steps, nears, fars):
            chip = table[count + step % count]
            for side, block in ((core, near), (1 - core, far)):
                held[chip, side] = block[pl.ds(0, size), :]
                output_ref[side, chip] = block[pl.ds(size, extra), :].astype(F32)
                small_ref[side, chip] = block[pl.ds(size + extra, small_rows), :].astype(F32)

    pair = [
        jnp.concatenate([held[2 * at + head, 0], held[2 * at + head, 1]], axis=0)
        for head in range(2)
    ]
    for index, output in enumerate(outputs):
        rows = [part[index * HD : index * HD + HD] for part in pair]
        output[...] = jnp.concatenate(rows, axis=0).astype(F32).T


def final_layout(pairs, size, table):
    count = len(pairs)
    steps, nears, fars = zip(*pairs)
    rows, model = nears[0].shape
    extra = rows - size - small_rows
    return pl.pallas_call(
        functools.partial(layout_kernel, steps, size, extra),
        grid_spec=pltpu.PrefetchScalarGridSpec(
            num_scalar_prefetch=1,
            grid=(count // 2,),
            in_specs=[pl.BlockSpec((rows, model), lambda at, table: (0, 0))] * (2 * count),
            out_specs=[pl.BlockSpec((model, 2 * HD), lambda at, table: (0, at))] * 3
            + [
                pl.BlockSpec((2, count, extra, model), lambda at, table: (0, 0, 0, 0)),
                pl.BlockSpec((2, count, small_rows, model), lambda at, table: (0, 0, 0, 0)),
            ],
            scratch_shapes=[pltpu.VMEM((count, 2, size, model), BF16)],
        ),
        out_shape=[struct((model, count * HD), F32)] * 3
        + [
            struct((2, count, extra, model), F32),
            struct((2, count, small_rows, model), F32),
        ],
        compiler_params=streaming,
        cost_estimate=light,
        name="final_layout",
    )(table, *nears, *fars)


def core_half(values, axis, side):
    size = values.shape[axis] // 2
    return lax.dynamic_slice_in_dim(values, side * size, size, axis)


def share_halves(values, axis):
    core = lax.axis_index("core")
    return core_half(values, axis, core), swap_cores(core_half(values, axis, 1 - core))


def local(
    block_input,
    out_grad,
    segments,
    lead_steps,
    gain_attn,
    shift_attn,
    lead_weight,
    query_weight,
    key_weight,
    value_weight,
    output_weight,
    output_bias,
    gain_mlp,
    shift_mlp,
    up_weight,
    up_bias,
    down_weight,
    down_bias,
):
    rows, model = block_input.shape
    heads = query_weight.shape[1] // HD
    width = heads * HD
    chips, core = lax.axis_size("chip"), lax.axis_index("core")
    split = chips // heads
    crops = lead_steps.shape[0]
    table = ring_table()
    weights = (query_weight, key_weight, value_weight)
    payload, attn_in = project(
        block_input, segments, lead_steps, gain_attn, shift_attn, lead_weight, weights
    )
    if split == 1:
        own = to_heads(payload)
        queries = own
    else:
        queries = scatter_queries(payload.reshape(-1, rows), heads, split)
        own = to_heads(jnp.repeat(payload, split, axis=0))
    own, attn_in = lax.optimization_barrier((own, attn_in))
    inputs = Gather(attn_in)
    inputs.send(inputs.ready)
    raw, out, logsum = attention_forward(queries, own, swap_cores(own), crops)
    other = swap_cores(own)
    attn_out = gather_queries(out, heads, split, rows)
    attn_out = visit([inputs], attn_out)
    branches = across_heads(product(attn_out, output_weight, 0, 0).astype(BF16))
    branches = visit([inputs], branches)
    keep, give, keep_in, give_in, hidden, dup_bias, mlp_part, d_mlp_part = mlp(
        table,
        block_input,
        out_grad,
        branches,
        output_bias,
        gain_mlp,
        shift_mlp,
        up_weight,
        up_bias,
        down_weight,
    )
    d_mlp = across_heads(d_mlp_part)
    ring = Reduce(keep, swap_cores(give), keep_in, swap_cores(give_in), table)
    mlp_part, d_mlp = lax.optimization_barrier((mlp_part, d_mlp))
    mlp_out = across_heads(mlp_part)
    d_hidden, d_branch, d_attn, sums = middle(hidden, out_grad, d_mlp, gain_mlp, output_weight)
    grads = scatter_queries(d_attn, heads, split)
    d_branch = visit([ring, inputs], d_branch)
    out_near, out_far = share_halves(attn_out, 0)
    doutput = product(out_near, d_branch) + product(out_far, swap_cores(d_branch))
    doutput = doutput.astype(BF16).reshape(chips, -1, model)
    pieces = 2
    dquery, turn = [], 0
    for keys, dtype in ((other, BF16), (own, F32)):
        piece_sums = []
        for index in range(pieces):
            last = keys is own and index == pieces - 1
            if turn == 1:
                grads, dquery, piece_sums = visit([ring, inputs], (grads, dquery, piece_sums))
            if turn == 2:
                far_sums = swap_cores(far_sums)
                doutput, dquery = lax.optimization_barrier((doutput, dquery))
                doutput = to_heads(doutput)
            if turn == 3:
                grads, dquery, piece_sums, mlp_out = visit(
                    [ring], (grads, dquery, piece_sums, mlp_out)
                )
                block_output = hidden + down_bias
                for part in mlp_out:
                    block_output += part.astype(F32)
                block_output = block_output.astype(BF16)
            dtypes = (BF16 if last else F32, dtype)
            *dquery, piece = backward_piece(
                queries, grads, raw, logsum, dquery, keys, piece_sums, index, pieces, crops, dtypes
            )
            piece_sums = [piece]
            turn += 1
        if keys is other:
            far_sums = piece
    (dquery,) = dquery
    key_value = (piece + far_sums.astype(F32)).astype(BF16)
    doutput, key_value = lax.optimization_barrier((doutput, key_value))
    doutput = jnp.sum(doutput.astype(F32), axis=0)
    small = jnp.concatenate([sums.reshape(-1), dup_bias[0]])
    small = jnp.pad(small, (0, small_rows * model - small.shape[0])).reshape(small_rows, model)
    doutput = jnp.concatenate([doutput, small], axis=0).astype(BF16)
    if split == 1:
        moved = to_heads(jnp.concatenate([dquery, key_value], axis=1))
        projections = head_gradient(dquery, key_value, inputs, table)
        near, far = share_halves(projections, 0)
        projections = (near.astype(F32) + far.astype(F32)).astype(BF16)
        size = projections.shape[0]
        blocks = jnp.concatenate([projections, doutput], axis=0)
        dquery, dkey, dvalue = (
            moved[:, at * HD : at * HD + HD].reshape(width, rows) for at in range(3)
        )
    else:
        dquery = gather_queries(dquery, heads, split, rows)
        moved = to_heads(key_value).reshape(heads, split, 2 * HD, rows).astype(F32)
        moved = jnp.sum(moved, axis=1).astype(BF16)
        dkey, dvalue = (moved[:, at * HD : at * HD + HD].reshape(width, rows) for at in range(2))
        size, blocks = 0, doutput
        projections = [
            lax.psum(product(attn_in, grad, 0, 1).astype(BF16), ("chip", "core")).astype(F32)
            for grad in (dquery, dkey, dvalue)
        ]
    while inputs.busy():
        visit([inputs], ())
    blocks = visit([ring], blocks)
    gathered = Gather(blocks, True)
    gathered.send(gathered.ready)
    d_part = (
        product(dquery, query_weight, 0, 1)
        + product(dkey, key_weight, 0, 1)
        + product(dvalue, value_weight, 0, 1)
    )
    d_in = across_heads(d_part.astype(BF16))
    unit_attn, inverse_attn = normalize(block_input.astype(F32))
    onehot = (segments[:, None] == jnp.arange(crops, dtype=jnp.int32)[None, :]).astype(F32)
    lead = jnp.sum(onehot * lead_steps.astype(F32)[None, :], axis=1) / 12.0
    ends = jnp.stack(
        [
            jnp.sum(d_part * unit_attn, axis=0),
            jnp.sum(d_part, axis=0),
            jnp.sum(lead[:, None] * d_part, axis=0),
        ]
    )
    ends = jnp.pad(ends.reshape(-1, 128), ((0, -ends.size // 128 % 16), (0, 0))).astype(BF16)
    everyone = ("chip", "core", "head")
    ends = jnp.broadcast_to(ends, (lax.axis_size(everyone),) + ends.shape)
    ends = lax.all_to_all(ends, everyone, 0, 0, tiled=True)
    visit([ring, gathered], ())
    d_in = visit([ring, gathered], d_in)
    d_in = functools.reduce(jnp.add, (part.astype(F32) for part in d_in))
    input_grad = (d_hidden + normalize_back(d_in * gain_attn, unit_attn, inverse_attn)).astype(
        BF16
    )
    while ring.busy() or gathered.busy():
        visit([ring, gathered], ())
    ends = jnp.sum(ends.astype(F32), axis=0).reshape(-1)[: 3 * model].reshape(3, model)
    ddown_weight, dup_weight = ring.state[2]
    if split == 1:
        *projections, doutput_weight, small = final_layout(gathered.pairs, size, table)
        doutput_weight = doutput_weight.reshape(width, model)
    else:
        blocks = jnp.zeros((2, chips) + blocks.shape, F32)
        for step, near, far in gathered.pairs:
            for side, block in ((core, near), (1 - core, far)):
                start = (side, table[chips + step % chips], 0, 0)
                block = block[None, None].astype(F32)
                blocks = lax.dynamic_update_slice(blocks, block, start)
        doutput_weight = blocks[:, :, :-small_rows].reshape(width, model)
        small = blocks[:, :, -small_rows:]
    small = jnp.sum(small, axis=(0, 1))
    dup_bias = small[4:].reshape(-1)[: dup_bias.shape[1]]
    return (
        block_output,
        input_grad,
        ends[0],
        ends[1],
        ends[2],
        *projections,
        doutput_weight,
        *small[:3],
        dup_weight,
        dup_bias,
        ddown_weight,
        small[3],
    )


def solution(mesh):
    bands, halves = mesh.shape["band"], mesh.shape["head"]
    inner = Mesh(mesh.devices.reshape(bands // 2, 2, halves), ("chip", "core", "head"))
    band = ("chip", "core")
    rows, columns, split_rows = P(band, None), P(None, "head"), P("head", None)
    return jax.shard_map(
        local,
        mesh=inner,
        in_specs=(
            rows,
            rows,
            P(band),
            P(),
            P(),
            P(),
            P(),
            columns,
            columns,
            columns,
            split_rows,
            P(),
            P(),
            P(),
            columns,
            P("head"),
            split_rows,
            P(),
        ),
        out_specs=(
            rows,
            rows,
            P(),
            P(),
            P(),
            columns,
            columns,
            columns,
            split_rows,
            P(),
            P(),
            P(),
            columns,
            P("head"),
            split_rows,
            P(),
        ),
        check_vma=False,
    )
```

```python
import functools
import math

import jax
import jax.numpy as jnp
from jax import lax
from jax.experimental import pallas as pl
from jax.experimental.pallas import tpu as pltpu
from jax.sharding import Mesh, PartitionSpec as P

HD = 64
F32 = jnp.float32
BF16 = jnp.bfloat16
eps = 1e-05
masked_value = -1e30
seg_row = 3 * HD
payload_rows = 3 * HD + 16
small_rows = 8
params = pltpu.CompilerParams(vmem_limit_bytes=48 * 2**20)
streaming = pltpu.CompilerParams(vmem_limit_bytes=60 * 2**20)


def normalize(values):
    centred = values - jnp.mean(values, axis=-1, keepdims=True)
    inverse = lax.rsqrt(jnp.mean(centred * centred, axis=-1, keepdims=True) + eps)
    return (centred * inverse, inverse)


def normalize_back(grad_unit, unit, inverse):
    return inverse * (
        grad_unit
        - jnp.mean(grad_unit, axis=-1, keepdims=True)
        - unit * jnp.mean(grad_unit * unit, axis=-1, keepdims=True)
    )


def product(first, second, first_axis=1, second_axis=0):
    return lax.dot_general(
        first,
        second,
        (((first_axis,), (second_axis,)), ((), ())),
        preferred_element_type=jnp.float32,
    )


def struct(shape, dtype):
    return jax.ShapeDtypeStruct(shape, dtype)


def whole_spec(shape):
    return pl.BlockSpec(shape, lambda *at: (0,) * len(shape))


light = pl.CostEstimate(flops=1, bytes_accessed=1, transcendentals=0)


def project_kernel(
    input_ref, segment_ref, steps_ref, gain, shift, lead_weight, *refs
):
    weights, (payload_ref, attn_in_ref) = refs[:3], refs[3:]
    rows = input_ref.shape[0]

    @pl.when(pl.program_id(0) == 0)
    def _():
        unit, _ = normalize(input_ref[...].astype(F32))
        crops = steps_ref.shape[0]
        crop = lax.broadcasted_iota(jnp.int32, (crops, rows), 0)
        steps = jnp.zeros((crops, rows), jnp.int32)
        for at in range(crops):
            steps = jnp.where(crop == at, steps_ref[at], steps)
        steps = jnp.where(crop == segment_ref[...], steps, 0).astype(F32)
        lead = product(steps, jnp.ones((crops, 128), F32), 0, 0)[:, :1] / 12.0
        attn_in = unit * gain[...] + shift[...] + lead * lead_weight[...]
        attn_in_ref[...] = attn_in.astype(BF16)

    for at, weight in enumerate(weights):
        part = product(attn_in_ref[...], weight[...]).T.astype(BF16)
        for head in range(2):
            payload_ref[head, pl.ds(at * HD, HD), :] = part[head * HD : head * HD + HD]
    segment = jnp.broadcast_to(segment_ref[...].astype(F32), (16, rows)).astype(BF16)
    for head in range(2):
        payload_ref[head, pl.ds(seg_row, 16), :] = segment


def project(block_input, segments, lead_steps, gain, shift, lead_weight, weights):
    rows, model = block_input.shape
    heads = weights[0].shape[1] // HD
    line = whole_spec((1, model))
    column = pl.BlockSpec((model, 2 * HD), lambda at: (0, at))
    return pl.pallas_call(
        project_kernel,
        grid=(heads // 2,),
        in_specs=[whole_spec(block_input.shape), whole_spec((1, rows)), pl.BlockSpec(memory_space=pltpu.SMEM)]
        + [line] * 3
        + [column] * 3,
        out_specs=[
            pl.BlockSpec((2, payload_rows, rows), lambda at: (at, 0, 0)),
            whole_spec((rows, model)),
        ],
        out_shape=[struct((heads, payload_rows, rows), BF16), struct((rows, model), BF16)],
        compiler_params=streaming,
        cost_estimate=light,
        name="project",
    )(block_input, segments[None], lead_steps, gain[None], shift[None], lead_weight[None], *weights)


def mlp_kernel(count, core_ref, input_ref, grad_ref, *refs):
    branches, refs = refs[:count], refs[count:]
    output_bias, gain, shift, up_weight, up_bias, down_weight = refs[:6]
    keep_ref, give_ref, keep_in_ref, give_in_ref, hidden_ref, bias_ref, forward_ref, back_ref = refs[
        6:14
    ]
    mlp_in_ref, forward, back = refs[14:]
    at = pl.program_id(0)
    is_down = core_ref[core_ref.shape[0] - 2] == 0

    @pl.when(at == 0)
    def _():
        hidden = input_ref[...].astype(F32) + output_bias[...]
        for branch in branches:
            hidden += branch[...].astype(F32)
        hidden_ref[...] = hidden
        unit, _ = normalize(hidden)
        mlp_in = (unit * gain[...] + shift[...]).astype(BF16)
        mlp_in_ref[...] = mlp_in
        keep_in_ref[...] = jnp.where(is_down, grad_ref[...], mlp_in)
        give_in_ref[...] = jnp.where(is_down, mlp_in, grad_ref[...])
        forward[...] = jnp.zeros_like(forward)
        back[...] = jnp.zeros_like(back)

    upper = product(mlp_in_ref[...], up_weight[...]) + up_bias[...]
    share = 0.5 + 0.5 * lax.erf(upper * math.sqrt(0.5))
    slope = share + upper * (jnp.exp(upper * upper * -0.5) * (1.0 / math.sqrt(2.0 * math.pi)))
    active = (upper * share).astype(BF16)
    d_active = product(grad_ref[...], down_weight[...], 1, 1)
    d_upper = (d_active * slope).astype(BF16)
    keep_ref[...] = jnp.where(is_down, active, d_upper)
    give_ref[...] = jnp.where(is_down, d_upper, active)
    bias_ref[...] = jnp.sum(d_upper.astype(F32), axis=0, keepdims=True)
    forward[...] += product(active, down_weight[...])
    back[...] += product(d_upper, up_weight[...], 1, 1)

    @pl.when(at == pl.num_programs(0) - 1)
    def _():
        forward_ref[...] = forward[...].astype(BF16)
        back_ref[...] = back[...].astype(BF16)


def mlp(
    table, block_input, out_grad, branches, output_bias, gain, shift, up_weight, up_bias, down_weight
):
    rows, model = block_input.shape
    units = up_weight.shape[1]
    step = math.gcd(units, 512)
    tile, line = whole_spec((rows, model)), whole_spec((1, model))
    wide = pl.BlockSpec((rows, step), lambda at, table: (0, at))
    bias = pl.BlockSpec((1, step), lambda at, table: (0, at))
    return pl.pallas_call(
        functools.partial(mlp_kernel, len(branches)),
        grid_spec=pltpu.PrefetchScalarGridSpec(
            num_scalar_prefetch=1,
            grid=(units // step,),
            in_specs=[tile] * (2 + len(branches))
            + [line] * 3
            + [
                pl.BlockSpec((model, step), lambda at, table: (0, at)),
                bias,
                pl.BlockSpec((step, model), lambda at, table: (at, 0)),
            ],
            out_specs=[wide, wide, tile, tile, tile, bias, tile, tile],
            scratch_shapes=[pltpu.VMEM((rows, model), BF16)]
            + [pltpu.VMEM((rows, model), F32)] * 2,
        ),
        out_shape=[struct((rows, units), BF16)] * 2
        + [struct((rows, model), BF16)] * 2
        + [
            struct((rows, model), F32),
            struct((1, units), F32),
            struct((rows, model), BF16),
            struct((rows, model), BF16),
        ],
        compiler_params=streaming,
        cost_estimate=light,
        name="mlp",
    )(
        table,
        block_input,
        out_grad,
        *branches,
        output_bias[None],
        gain[None],
        shift[None],
        up_weight,
        up_bias[None],
        down_weight,
    )


def middle_kernel(count, hidden_ref, grad_ref, *refs):
    parts, refs = refs[:count], refs[count:]
    gain, output_weight, d_hidden_ref, d_branch_ref, d_attn_ref, sums_ref = refs
    unit, inverse = normalize(hidden_ref[...])
    d_mlp = parts[0][...].astype(F32)
    for part in parts[1:]:
        d_mlp += part[...].astype(F32)
    grad = grad_ref[...].astype(F32)
    d_hidden = grad + normalize_back(d_mlp * gain[...], unit, inverse)
    d_hidden_ref[...] = d_hidden
    d_branch = d_hidden.astype(BF16)
    d_branch_ref[...] = d_branch
    d_attn_ref[...] = product(output_weight[...], d_branch, 1, 1).astype(BF16)
    for at, values in enumerate((d_hidden, d_mlp * unit, d_mlp, grad)):
        sums_ref[pl.ds(at, 1), :] = jnp.sum(values, axis=0, keepdims=True)


def middle(hidden, out_grad, parts, gain, output_weight):
    rows, model = hidden.shape
    width = output_weight.shape[0]
    return pl.pallas_call(
        functools.partial(middle_kernel, len(parts)),
        out_shape=[
            struct((rows, model), F32),
            struct((rows, model), BF16),
            struct((width, rows), BF16),
            struct((4, model), F32),
        ],
        compiler_params=streaming,
        cost_estimate=light,
        name="middle",
    )(hidden, out_grad, *parts, gain[None], output_weight)


def mask_rows(piece, chip, crops):
    crop = lax.broadcasted_iota(jnp.int32, (HD, piece.shape[2]), 0)
    segment = piece[chip, pl.ds(seg_row, 16), :].astype(F32)[:1].astype(jnp.int32)
    return jnp.where((crop != segment) & (crop < crops), masked_value, 0.0)


def load_keys(piece, crops, keys, key_t, value_n):
    chips, _, patches = piece.shape
    for chip in range(chips):
        key = piece[chip, pl.ds(HD, HD), :]
        value = piece[chip, pl.ds(2 * HD, HD), :]
        place = pl.ds(chip * patches, patches)
        both = jnp.concatenate([key.astype(F32), mask_rows(piece, chip, crops)], axis=0)
        keys[place, :] = both.T.astype(BF16)
        key_t[:, place] = key
        value_n[place, :] = value.astype(F32).T.astype(BF16)


def masked_query(query_ref, dtype=BF16):
    query = query_ref[0, pl.ds(0, HD), :].astype(F32) * 0.125
    segment = query_ref[0, pl.ds(seg_row, 16), :].astype(F32)[:1].astype(jnp.int32)
    crop = lax.broadcasted_iota(jnp.int32, query.shape, 0)
    onehot = jnp.where(crop == segment, 1.0, 0.0)
    return jnp.concatenate([query, onehot], axis=0).astype(dtype)


def forward_kernel(
    crops, step, query_ref, own, other, raw_ref, out_ref, logsum_ref, key_t, value_n, scores
):
    @pl.when(pl.program_id(0) == 0)
    def _():
        start = 0
        for piece in (own, other):
            chips, _, patches = piece.shape
            for chip in range(chips):
                place = pl.ds(start, patches)
                key = piece[chip, pl.ds(HD, HD), :].astype(F32)
                key_t[:, place] = jnp.concatenate([key, mask_rows(piece, chip, crops)], axis=0).astype(BF16)
                value = piece[chip, pl.ds(2 * HD, HD), :].astype(F32)
                value = jnp.concatenate([value, jnp.ones_like(value)], axis=0)
                value_n[place, :] = value.T.astype(BF16)
                start += patches

    query = masked_query(query_ref, F32).T.astype(BF16)
    count = query.shape[0]
    top = jnp.full((count, 128), masked_value, F32)
    for start in range(0, key_t.shape[1], step):
        block = product(query, key_t[:, pl.ds(start, step)])
        scores[:, pl.ds(start, step)] = block
        for at in range(0, step, 128):
            top = jnp.maximum(top, block[:, at : at + 128])
    top = jnp.max(top, axis=1, keepdims=True)
    accum = jnp.zeros((count, 2 * HD), F32)
    for start in range(0, key_t.shape[1], step):
        weights = jnp.exp(scores[:, pl.ds(start, step)] - top).astype(BF16)
        accum += product(weights, value_n[pl.ds(start, step), :])
    accum = accum.T
    total = accum[HD : HD + 1]
    raw = accum[:HD] / total
    raw_ref[0] = raw
    out_ref[0] = raw.astype(BF16)
    top = jnp.broadcast_to(top, (count, 128)).T[:1]
    logsum_ref[0] = top + jnp.log(total)


def backward_kernel(
    crops,
    before,
    query_ref,
    grad_ref,
    raw_ref,
    logsum_ref,
    *refs,
):
    before_refs, refs = refs[:before], refs[before:]
    piece, (dquery_ref, sums_ref, keys, key_t, value_n, sums) = refs[0], refs[-6:]
    group = pl.program_id(0)

    @pl.when(group == 0)
    def _():
        load_keys(piece, crops, keys, key_t, value_n)
        sums[...] = jnp.zeros_like(sums)

    query = masked_query(query_ref)
    grad = grad_ref[0]
    grad_wide = grad.astype(F32)
    delta = jnp.sum(grad_wide * raw_ref[0], axis=0, keepdims=True)
    scaled = query_ref[0, pl.ds(0, HD), :].astype(F32) * 0.125
    zero = jnp.zeros_like(scaled)
    query_side = jnp.concatenate([scaled, zero], axis=0).T.astype(BF16)
    grad_side = jnp.concatenate([zero, grad_wide], axis=0).T.astype(BF16)
    probs = jnp.exp(product(keys[...], query) - logsum_ref[0])
    dprobs = product(value_n[...], grad)
    dscores = (probs * (dprobs - delta)).astype(BF16)
    sums[...] += product(dscores, query_side) + product(probs.astype(BF16), grad_side)
    dquery = product(key_t[...], dscores) * 0.125
    for ref in before_refs:
        dquery = ref[0] + dquery
    dquery_ref[0] = dquery.astype(dquery_ref.dtype)

    @pl.when(group == pl.num_programs(0) - 1)
    def _():
        chips, _, patches = sums_ref.shape
        for chip in range(chips):
            sums_ref[chip] = sums[pl.ds(chip * patches, patches), :].T.astype(sums_ref.dtype)


def key_step(count):
    return 1024 if count % 1024 == 0 else 256


def query_spec(rows, patches):
    return pl.BlockSpec((1, rows, patches), lambda group: (group, 0, 0))


def attention_forward(queries, own, other, crops):
    groups, _, patches = queries.shape
    count = 2 * own.shape[0] * own.shape[2]
    return pl.pallas_call(
        functools.partial(forward_kernel, crops, key_step(count)),
        grid=(groups,),
        in_specs=[
            query_spec(payload_rows, patches),
            whole_spec(own.shape),
            whole_spec(other.shape),
        ],
        out_specs=[query_spec(HD, patches), query_spec(HD, patches), query_spec(1, patches)],
        out_shape=[
            struct((groups, HD, patches), F32),
            struct((groups, HD, patches), BF16),
            struct((groups, 1, patches), F32),
        ],
        scratch_shapes=[
            pltpu.VMEM((2 * HD, count), BF16),
            pltpu.VMEM((count, 2 * HD), BF16),
            pltpu.VMEM((patches, count), F32),
        ],
        compiler_params=streaming,
        cost_estimate=light,
        name="attention_forward",
    )(queries, own, other)


def backward_piece(queries, grads, raw, logsum, before, keys, earlier, index, pieces, crops, dtypes):
    groups, _, patches = queries.shape
    chips = keys.shape[0] // pieces
    count = chips * keys.shape[2]
    sums_shape = (chips, 2 * HD, keys.shape[2])
    return pl.pallas_call(
        functools.partial(backward_kernel, crops, len(before)),
        grid=(groups,),
        in_specs=[
            query_spec(payload_rows, patches),
            query_spec(HD, patches),
            query_spec(HD, patches),
            query_spec(1, patches),
        ]
        + [query_spec(HD, patches)] * len(before)
        + [pl.BlockSpec((chips,) + keys.shape[1:], lambda group: (index, 0, 0))]
        + [pl.BlockSpec(memory_space=pl.ANY)] * len(earlier),
        out_specs=[
            query_spec(HD, patches),
            pl.BlockSpec(sums_shape, lambda group: (index, 0, 0)),
        ],
        out_shape=[
            struct((groups, HD, patches), dtypes[0]),
            struct((keys.shape[0],) + sums_shape[1:], dtypes[1]),
        ],
        input_output_aliases={5 + len(before): 1} if earlier else {},
        scratch_shapes=[
            pltpu.VMEM((count, 2 * HD), BF16),
            pltpu.VMEM((HD, count), BF16),
            pltpu.VMEM((count, HD), BF16),
            pltpu.VMEM((count, 2 * HD), F32),
        ],
        compiler_params=params,
        cost_estimate=light,
        name="attention_backward",
    )(queries, grads, raw, logsum, *before, keys, *earlier)


def swap_cores(values):
    return lax.ppermute(values, "core", [(0, 1), (1, 0)])


def to_heads(blocks):
    return lax.all_to_all(blocks, "chip", 0, 0, tiled=True)


def scatter_queries(values, heads, split):
    rows, patches = values.shape[0] // heads, values.shape[1]
    if split == 1:
        return to_heads(values.reshape(heads, rows, patches))
    part = patches // split
    blocks = values.reshape(heads, rows, split, part).transpose(0, 2, 1, 3)
    moved = to_heads(blocks.reshape(heads * split, rows, part))
    width = min(256, moved.shape[0] * part)
    joined = moved.transpose(1, 0, 2).reshape(rows, -1, width)
    return joined.transpose(1, 0, 2)


def gather_queries(values, heads, split, patches):
    rows = values.shape[1]
    if split == 1:
        return to_heads(values).reshape(heads * rows, patches)
    part = patches // split
    joined = values.transpose(1, 0, 2).reshape(rows, heads * split, part)
    moved = to_heads(joined.transpose(1, 0, 2)).reshape(heads, split, rows, part)
    return moved.transpose(0, 2, 1, 3).reshape(heads * rows, patches)


def across_heads(part):
    if lax.axis_size("head") == 2:
        return [part, lax.ppermute(part, "head", [(0, 1), (1, 0)])]
    return [lax.psum(part, "head")]


def ring_pairs(direction):
    chips = lax.axis_size("chip")
    order = list(range(0, chips, 2)) + list(range(chips - 1, 0, -2))
    return [(order[at], order[(at + direction) % chips]) for at in range(chips)]


def ring_table():
    chips, chip = lax.axis_size("chip"), lax.axis_index("chip")
    place = jnp.where(chip % 2 == 0, chip // 2, chips - 1 - chip // 2)
    steps = jnp.arange(2 * chips + 2, dtype=jnp.int32)
    places = (place + steps) % chips
    there = jnp.where(places < chips // 2, 2 * places, 2 * (chips - 1 - places) + 1)
    table = jnp.where(steps < chips, places, there)
    table = jnp.where(steps == 2 * chips, lax.axis_index("core"), table)
    return jnp.where(steps == 2 * chips + 1, lax.axis_index("head"), table).astype(jnp.int32)


def visit(streams, values):
    states, values = lax.optimization_barrier(([stream.state for stream in streams], values))
    for stream, state in zip(streams, states):
        stream.advance(state)
    ready, values = lax.optimization_barrier(([stream.ready for stream in streams], values))
    for stream, blocks in zip(streams, ready):
        stream.send(blocks)
    return values


class Gather:
    def __init__(self, block, swap=False, take=None):
        self.reach, self.swap, self.take = lax.axis_size("chip") // 2, swap, take
        self.blocks, self.pairs, self.count = [], [], 0
        self.new, self.outputs = [0], []
        self.ready = [block]

    def send(self, ready):
        new = list(zip(self.new, ready))
        self.blocks += new
        self.new = new
        self.count += 1
        sides = ready if len(ready) > 1 else ready * 2
        if self.count == self.reach:
            half = ready[0].shape[1] // 2
            sides = [sides[0][:, :half], sides[1][:, half:]]
        flying = []
        if self.count <= self.reach:
            flying = [
                lax.ppermute(block, "chip", ring_pairs(direction))
                for block, direction in zip(sides, (1, -1))
            ]
        swapped = [swap_cores(block) for block in ready] if self.swap else []
        self.state = (flying, swapped, self.outputs)

    def advance(self, state):
        arrived, swapped, self.outputs = state
        pairs = [(step, near, far) for (step, near), far in zip(self.new, swapped)]
        self.pairs += pairs
        if self.take and pairs:
            self.outputs = self.take(self.outputs, pairs)
        self.new = [-self.count, self.count]
        if arrived and self.count == self.reach:
            arrived, self.new = [jnp.concatenate(arrived, axis=1)], [self.count]
        self.ready = arrived

    def busy(self):
        return bool(self.state[0] or self.state[1])


def add_kernel(wanted, _, *refs):
    outputs, refs = refs[-len(wanted) :], list(refs[: -len(wanted)])
    keep_in, far_in = refs.pop(0), refs.pop(0)
    for starts, output in zip(wanted, outputs):
        near, far = refs.pop(0), refs.pop(0)
        total = product(near[...], keep_in[...], 0, 0) + product(far[...], far_in[...], 0, 0)
        output[...] = total.astype(BF16)
        arrived = [refs.pop(0) for _ in starts]
        for start in sorted(set(starts)):
            parts = [part for part, at in zip(arrived, starts) if at == start]
            columns = slice(start, start + parts[0].shape[1])
            summed = total[:, columns]
            for part in parts:
                summed += part[...].astype(F32)
            output[:, columns] = summed.astype(BF16)


class Reduce:
    def __init__(self, keep, far, keep_in, far_in, table):
        self.chips, self.table = lax.axis_size("chip"), table
        self.operands, self.sides = (keep, far), (keep_in, far_in)
        self.units = keep.shape[1] // self.chips
        self.tiled = self.units % 128 == 0
        self.left, self.gather = self.chips // 2, None
        (block,) = self.add([(self.left, [])])
        half = block.shape[1] // 2
        self.send([block[:, :half], block[:, half:]])

    def send(self, ready):
        if self.gather:
            self.gather.send(ready)
            self.state = self.gather.state
            return
        self.left -= 1
        self.state = [
            lax.ppermute(block, "chip", ring_pairs(direction))
            for block, direction in zip(ready, (1, -1))
        ]

    def advance(self, state):
        if self.gather:
            self.gather.advance(state)
            self.ready = self.gather.ready
            return
        half = self.sides[0].shape[1] // 2
        ahead, behind = state
        first = 0 if ahead.shape[1] != half else half
        if self.left:
            wanted = [(self.left, [(ahead, 0)]), (-self.left, [(behind, first)])]
        else:
            wanted = [(0, [(ahead, 0), (behind, first)])]
        self.ready = self.add(wanted)
        if not self.left:
            self.gather = Gather(self.ready[0], True, self.place)

    def add(self, wanted):
        (rows, model), units, chips = self.sides[0].shape, self.units, self.chips
        if not self.tiled:
            sums = []
            for step, parts in wanted:
                start = self.table[step % chips] * units
                total = jnp.zeros((units, model), F32)
                for operand, side in zip(self.operands, self.sides):
                    block = lax.dynamic_slice_in_dim(operand, start, units, 1)
                    total += product(block, side, 0, 0)
                for part, start in parts:
                    total = total.at[:, start : start + part.shape[1]].add(part.astype(F32))
                sums.append(total.astype(BF16))
            return sums
        side = pl.BlockSpec((rows, model), lambda at, table: (0, 0))
        whole = pl.BlockSpec((units, model), lambda at, table: (0, 0))
        specs, arrays = [side] * 2, list(self.sides)
        for step, parts in wanted:
            block = pl.BlockSpec(
                (rows, units), lambda at, table, step=step % chips: (0, table[step])
            )
            specs += [block] * 2
            specs += [pl.BlockSpec(part.shape, lambda at, table: (0, 0)) for part, _ in parts]
            arrays += list(self.operands) + [part for part, _ in parts]
        return pl.pallas_call(
            functools.partial(add_kernel, [[start for _, start in parts] for _, parts in wanted]),
            grid_spec=pltpu.PrefetchScalarGridSpec(
                num_scalar_prefetch=1,
                grid=(1,),
                in_specs=specs,
                out_specs=[whole] * len(wanted),
            ),
            out_shape=[struct((units, model), BF16)] * len(wanted),
            compiler_params=streaming,
            cost_estimate=light,
            name="ring_add",
        )(self.table, *arrays)

    def place(self, outputs, pairs):
        units, chips, model = self.units, self.chips, self.sides[0].shape[1]
        shapes = [struct((chips * units, model), F32), struct((model, chips * units), F32)]
        if not self.tiled:
            outputs = outputs or [jnp.zeros(shape.shape, F32) for shape in shapes]
            down, up = outputs
            is_down = self.table[2 * chips] == 0
            for step, near, far in pairs:
                start = self.table[step % chips] * units
                first = jnp.where(is_down, near, far).astype(F32)
                second = jnp.where(is_down, far, near).astype(F32).T
                down = lax.dynamic_update_slice_in_dim(down, first, start, 0)
                up = lax.dynamic_update_slice_in_dim(up, second, start, 1)
            return [down, up]
        first = pairs[0][0] % chips
        stride = pairs[-1][0] % chips - first
        block = pl.BlockSpec((units, model), lambda at, table: (0, 0))
        return pl.pallas_call(
            functools.partial(place_kernel, len(pairs)),
            grid_spec=pltpu.PrefetchScalarGridSpec(
                num_scalar_prefetch=1,
                grid=(len(pairs),),
                in_specs=[pl.BlockSpec(memory_space=pl.ANY)] * len(outputs)
                + [block] * (2 * len(pairs)),
                out_specs=[
                    pl.BlockSpec((units, model), lambda at, table: (table[first + at * stride], 0)),
                    pl.BlockSpec((model, units), lambda at, table: (0, table[first + at * stride])),
                ],
            ),
            out_shape=shapes,
            input_output_aliases={1 + at: at for at in range(len(outputs))},
            compiler_params=streaming,
            cost_estimate=light,
            name="place",
        )(self.table, *outputs, *[pair[1] for pair in pairs], *[pair[2] for pair in pairs])

    def busy(self):
        return self.gather is None or self.gather.busy()


def place_kernel(count, table, *refs):
    nears, fars, (down, up) = refs[-2 - 2 * count : -2 - count], refs[-2 - count : -2], refs[-2:]
    core = table[table.shape[0] - 2]

    def put(first, second):
        down[...] = first[...].astype(F32)
        up[...] = second[...].astype(F32).T

    for at, (near, far) in enumerate(zip(nears, fars)):
        here = pl.program_id(0) == at
        pl.when(here & (core == 0))(functools.partial(put, near, far))
        pl.when(here & (core != 0))(functools.partial(put, far, near))


def head_gradient_kernel(steps, chips, table, query_ref, key_value_ref, *refs):
    parts, out_ref = refs[:-1], refs[-1]
    patches = query_ref.shape[2]
    for at, part in enumerate(parts):

        @pl.when(pl.program_id(0) == at)
        def _(part=part):
            total = jnp.zeros(out_ref.shape, F32)
            for index, step in enumerate(steps):
                chip = table[chips + step % chips]
                grads = jnp.concatenate([query_ref[chip], key_value_ref[chip]], axis=0)
                total += product(grads, part[pl.ds(index * patches, patches), :])
            out_ref[...] = total.astype(BF16)


def head_gradient(dquery, key_value, parts, steps, table):
    chips, rows, _ = dquery.shape
    columns = parts[0].shape[1]

    def column(at, table):
        mine = table[2 * chips + 1] if len(parts) > 1 else 0
        return (0, jnp.where(at == 0, mine, 1 - mine))

    return pl.pallas_call(
        functools.partial(head_gradient_kernel, steps, chips),
        grid_spec=pltpu.PrefetchScalarGridSpec(
            num_scalar_prefetch=1,
            grid=(len(parts),),
            in_specs=[
                pl.BlockSpec(array.shape, lambda at, table, rank=array.ndim: (0,) * rank)
                for array in (dquery, key_value, *parts)
            ],
            out_specs=pl.BlockSpec((3 * rows, columns), column),
        ),
        out_shape=struct((3 * rows, columns * len(parts)), BF16),
        compiler_params=streaming,
        cost_estimate=light,
        name="head_gradient",
    )(table, dquery, key_value, *parts)


def layout_kernel(steps, size, extra, table, *refs):
    count = len(steps)
    nears, fars, outputs, output_ref, small_ref, held = (
        refs[:count],
        refs[count : 2 * count],
        refs[2 * count : 2 * count + 3],
        refs[2 * count + 3],
        refs[2 * count + 4],
        refs[2 * count + 5],
    )
    at = pl.program_id(0)

    @pl.when(at == 0)
    def _():
        core = table[2 * count]
        for step, near, far in zip(steps, nears, fars):
            chip = table[count + step % count]
            for side, block in ((core, near), (1 - core, far)):
                held[chip, side] = block[pl.ds(0, size), :]
                output_ref[side, chip] = block[pl.ds(size, extra), :].astype(F32)
                small_ref[side, chip] = block[pl.ds(size + extra, small_rows), :].astype(F32)

    pair = [
        jnp.concatenate([held[2 * at + head, 0], held[2 * at + head, 1]], axis=0)
        for head in range(2)
    ]
    for index, output in enumerate(outputs):
        rows = [part[index * HD : index * HD + HD] for part in pair]
        output[...] = jnp.concatenate(rows, axis=0).astype(F32).T


def final_layout(pairs, size, table):
    count = len(pairs)
    steps, nears, fars = zip(*pairs)
    rows, model = nears[0].shape
    extra = rows - size - small_rows
    return pl.pallas_call(
        functools.partial(layout_kernel, steps, size, extra),
        grid_spec=pltpu.PrefetchScalarGridSpec(
            num_scalar_prefetch=1,
            grid=(count // 2,),
            in_specs=[pl.BlockSpec((rows, model), lambda at, table: (0, 0))] * (2 * count),
            out_specs=[pl.BlockSpec((model, 2 * HD), lambda at, table: (0, at))] * 3
            + [
                pl.BlockSpec((2, count, extra, model), lambda at, table: (0, 0, 0, 0)),
                pl.BlockSpec((2, count, small_rows, model), lambda at, table: (0, 0, 0, 0)),
            ],
            scratch_shapes=[pltpu.VMEM((count, 2, size, model), BF16)],
        ),
        out_shape=[struct((model, count * HD), F32)] * 3
        + [
            struct((2, count, extra, model), F32),
            struct((2, count, small_rows, model), F32),
        ],
        compiler_params=streaming,
        cost_estimate=light,
        name="final_layout",
    )(table, *nears, *fars)


def core_half(values, axis, side):
    size = values.shape[axis] // 2
    return lax.dynamic_slice_in_dim(values, side * size, size, axis)


def share_halves(values, axis):
    core = lax.axis_index("core")
    return core_half(values, axis, core), swap_cores(core_half(values, axis, 1 - core))


def local(
    block_input,
    out_grad,
    segments,
    lead_steps,
    gain_attn,
    shift_attn,
    lead_weight,
    query_weight,
    key_weight,
    value_weight,
    output_weight,
    output_bias,
    gain_mlp,
    shift_mlp,
    up_weight,
    up_bias,
    down_weight,
    down_bias,
):
    rows, model = block_input.shape
    heads = query_weight.shape[1] // HD
    width = heads * HD
    chips, core = lax.axis_size("chip"), lax.axis_index("core")
    split = chips // heads
    crops = lead_steps.shape[0]
    table = ring_table()
    weights = (query_weight, key_weight, value_weight)
    payload, attn_in = project(
        block_input, segments, lead_steps, gain_attn, shift_attn, lead_weight, weights
    )
    if split == 1:
        own = to_heads(payload)
        queries = own
    else:
        queries = scatter_queries(payload.reshape(-1, rows), heads, split)
        own = to_heads(jnp.repeat(payload, split, axis=0))
    own, attn_in = lax.optimization_barrier((own, attn_in))
    cut = model // 2 if lax.axis_size("head") == 2 else model
    inputs = Gather(
        lax.dynamic_slice_in_dim(attn_in, lax.axis_index("head") * cut % model, cut, 1)
    )
    inputs.send(inputs.ready)
    other = swap_cores(own)
    raw, out, logsum = attention_forward(queries, own, other, crops)
    out = visit([inputs], out)
    attn_out = gather_queries(out, heads, split, rows)
    attn_out = visit([inputs], attn_out)
    branches = across_heads(product(attn_out, output_weight, 0, 0).astype(BF16))
    branches = visit([inputs], branches)
    keep, give, keep_in, give_in, hidden, dup_bias, mlp_part, d_mlp_part = mlp(
        table,
        block_input,
        out_grad,
        branches,
        output_bias,
        gain_mlp,
        shift_mlp,
        up_weight,
        up_bias,
        down_weight,
    )
    keep, give, keep_in, give_in, d_mlp_part = visit(
        [inputs], (keep, give, keep_in, give_in, d_mlp_part)
    )
    d_mlp = across_heads(d_mlp_part)
    ring = Reduce(keep, swap_cores(give), keep_in, swap_cores(give_in), table)
    while inputs.busy():
        visit([inputs], ())
    steps, inputs = zip(*inputs.blocks)
    inputs = jnp.concatenate(inputs, axis=0)
    mlp_part, inputs, d_mlp = lax.optimization_barrier((mlp_part, inputs, d_mlp))
    parts = [inputs]
    if cut != model:
        parts = across_heads(inputs)
    d_hidden, d_branch, d_attn, sums = middle(hidden, out_grad, d_mlp, gain_mlp, output_weight)
    grads = scatter_queries(d_attn, heads, split)
    d_branch, mlp_part = visit([ring], (d_branch, mlp_part))
    mlp_out = across_heads(mlp_part)
    out_near, out_far = share_halves(attn_out, 0)
    doutput = product(out_near, d_branch) + product(out_far, swap_cores(d_branch))
    doutput = to_heads(doutput.astype(BF16).reshape(chips, -1, model))
    *dquery, far_sums = backward_piece(
        queries, grads, raw, logsum, [], other, [], 0, 1, crops, (F32, BF16)
    )
    grads, dquery, far_sums = visit([ring], (grads, dquery, far_sums))
    far_sums = swap_cores(far_sums)
    *dquery, near_sums = backward_piece(
        queries, grads, raw, logsum, dquery, own, [], 0, 1, crops, (BF16, F32)
    )
    near_sums, dquery, mlp_out = visit([ring], (near_sums, dquery, mlp_out))
    block_output = hidden + down_bias
    for part in mlp_out:
        block_output += part.astype(F32)
    block_output = block_output.astype(BF16)
    (dquery,) = dquery
    key_value = (near_sums + far_sums.astype(F32)).astype(BF16)
    doutput, key_value = lax.optimization_barrier((doutput, key_value))
    doutput = jnp.sum(doutput.astype(F32), axis=0)
    small = jnp.concatenate([sums.reshape(-1), dup_bias[0]])
    small = jnp.pad(small, (0, small_rows * model - small.shape[0])).reshape(small_rows, model)
    doutput = jnp.concatenate([doutput, small], axis=0).astype(BF16)
    if split == 1:
        moved = to_heads(jnp.concatenate([dquery, key_value], axis=1))
        projections = head_gradient(dquery, key_value, parts, steps, table)
        near, far = share_halves(projections, 0)
        projections = (near.astype(F32) + far.astype(F32)).astype(BF16)
        size = projections.shape[0]
        blocks = jnp.concatenate([projections, doutput], axis=0)
        dquery, dkey, dvalue = (
            moved[:, at * HD : at * HD + HD].reshape(width, rows) for at in range(3)
        )
    else:
        dquery = gather_queries(dquery, heads, split, rows)
        moved = to_heads(key_value).reshape(heads, split, 2 * HD, rows).astype(F32)
        moved = jnp.sum(moved, axis=1).astype(BF16)
        dkey, dvalue = (moved[:, at * HD : at * HD + HD].reshape(width, rows) for at in range(2))
        size, blocks = 0, doutput
        projections = [
            lax.psum(product(attn_in, grad, 0, 1).astype(BF16), ("chip", "core")).astype(F32)
            for grad in (dquery, dkey, dvalue)
        ]
    gathered = Gather(blocks, True)
    gathered.send(gathered.ready)
    visit([ring], blocks)
    d_part = (
        product(dquery, query_weight, 0, 1)
        + product(dkey, key_weight, 0, 1)
        + product(dvalue, value_weight, 0, 1)
    )
    d_part = visit([ring, gathered], d_part)
    d_in = across_heads(d_part.astype(BF16))
    unit_attn, inverse_attn = normalize(block_input.astype(F32))
    onehot = (segments[:, None] == jnp.arange(crops, dtype=jnp.int32)[None, :]).astype(F32)
    lead = jnp.sum(onehot * lead_steps.astype(F32)[None, :], axis=1) / 12.0
    ends = jnp.stack(
        [
            jnp.sum(d_part * unit_attn, axis=0),
            jnp.sum(d_part, axis=0),
            jnp.sum(lead[:, None] * d_part, axis=0),
        ]
    )
    ends = jnp.pad(ends.reshape(-1, 128), ((0, -ends.size // 128 % 16), (0, 0))).astype(BF16)
    everyone = ("chip", "core", "head")
    ends = jnp.broadcast_to(ends, (lax.axis_size(everyone),) + ends.shape)
    ends = lax.all_to_all(ends, everyone, 0, 0, tiled=True)
    visit([ring, gathered], ())
    d_in = visit([ring, gathered], d_in)
    d_in = functools.reduce(jnp.add, (part.astype(F32) for part in d_in))
    input_grad = (d_hidden + normalize_back(d_in * gain_attn, unit_attn, inverse_attn)).astype(
        BF16
    )
    while gathered.busy():
        visit([gathered], ())
    ends = jnp.sum(ends.astype(F32), axis=0).reshape(-1)[: 3 * model].reshape(3, model)
    if split == 1:
        layout = final_layout(gathered.pairs, size, table)
        *projections, doutput_weight, small = visit([ring], layout)
        doutput_weight = doutput_weight.reshape(width, model)
    while ring.busy():
        visit([ring], ())
    ddown_weight, dup_weight = ring.state[2]
    if split != 1:
        blocks = jnp.zeros((2, chips) + blocks.shape, F32)
        for step, near, far in gathered.pairs:
            for side, block in ((core, near), (1 - core, far)):
                start = (side, table[chips + step % chips], 0, 0)
                block = block[None, None].astype(F32)
                blocks = lax.dynamic_update_slice(blocks, block, start)
        doutput_weight = blocks[:, :, :-small_rows].reshape(width, model)
        small = blocks[:, :, -small_rows:]
    small = jnp.sum(small, axis=(0, 1))
    dup_bias = small[4:].reshape(-1)[: dup_bias.shape[1]]
    return (
        block_output,
        input_grad,
        ends[0],
        ends[1],
        ends[2],
        *projections,
        doutput_weight,
        *small[:3],
        dup_weight,
        dup_bias,
        ddown_weight,
        small[3],
    )


def solution(mesh):
    bands, halves = mesh.shape["band"], mesh.shape["head"]
    inner = Mesh(mesh.devices.reshape(bands // 2, 2, halves), ("chip", "core", "head"))
    band = ("chip", "core")
    rows, columns, split_rows = P(band, None), P(None, "head"), P("head", None)
    return jax.shard_map(
        local,
        mesh=inner,
        in_specs=(
            rows,
            rows,
            P(band),
            P(),
            P(),
            P(),
            P(),
            columns,
            columns,
            columns,
            split_rows,
            P(),
            P(),
            P(),
            columns,
            P("head"),
            split_rows,
            P(),
        ),
        out_specs=(
            rows,
            rows,
            P(),
            P(),
            P(),
            columns,
            columns,
            columns,
            split_rows,
            P(),
            P(),
            P(),
            columns,
            P("head"),
            split_rows,
            P(),
        ),
        check_vma=False,
    )
```

```python
import functools
import math

import jax
import jax.numpy as jnp
from jax import lax
from jax.experimental import pallas as pl
from jax.experimental.pallas import tpu as pltpu
from jax.sharding import Mesh, PartitionSpec as P

HD = 64
F32 = jnp.float32
BF16 = jnp.bfloat16
eps = 1e-05
masked_value = -1e30
seg_row = 3 * HD
payload_rows = 3 * HD + 16
small_rows = 16
params = pltpu.CompilerParams(vmem_limit_bytes=48 * 2**20)
streaming = pltpu.CompilerParams(vmem_limit_bytes=60 * 2**20)


def normalize(values):
    centred = values - jnp.mean(values, axis=-1, keepdims=True)
    inverse = lax.rsqrt(jnp.mean(centred * centred, axis=-1, keepdims=True) + eps)
    return (centred * inverse, inverse)


def normalize_back(grad_unit, unit, inverse):
    return inverse * (
        grad_unit
        - jnp.mean(grad_unit, axis=-1, keepdims=True)
        - unit * jnp.mean(grad_unit * unit, axis=-1, keepdims=True)
    )


def product(first, second, first_axis=1, second_axis=0):
    return lax.dot_general(
        first,
        second,
        (((first_axis,), (second_axis,)), ((), ())),
        preferred_element_type=jnp.float32,
    )


def struct(shape, dtype):
    return jax.ShapeDtypeStruct(shape, dtype)


def whole_spec(shape):
    return pl.BlockSpec(shape, lambda *at: (0,) * len(shape))


light = pl.CostEstimate(flops=1, bytes_accessed=1, transcendentals=0)


def project_kernel(
    table, input_ref, segment_ref, steps_ref, gain, shift, lead_weight, *refs
):
    weights, (payload_ref, attn_in_ref, cut_ref) = refs[:3], refs[3:]
    rows = input_ref.shape[0]

    @pl.when(pl.program_id(0) == 0)
    def _():
        unit, _ = normalize(input_ref[...].astype(F32))
        crops = steps_ref.shape[0]
        crop = lax.broadcasted_iota(jnp.int32, (crops, rows), 0)
        steps = jnp.zeros((crops, rows), jnp.int32)
        for at in range(crops):
            steps = jnp.where(crop == at, steps_ref[at], steps)
        steps = jnp.where(crop == segment_ref[...], steps, 0).astype(F32)
        lead = product(steps, jnp.ones((crops, 128), F32), 0, 0)[:, :1] / 12.0
        attn_in = unit * gain[...] + shift[...] + lead * lead_weight[...]
        attn_in = attn_in.astype(BF16)
        attn_in_ref[...] = attn_in
        columns = cut_ref.shape[1]
        first = table[table.shape[0] - 1] % (attn_in.shape[1] // columns) == 0
        cut_ref[...] = jnp.where(first, attn_in[:, :columns], attn_in[:, -columns:])

    for at, weight in enumerate(weights):
        part = product(attn_in_ref[...], weight[...]).T.astype(BF16)
        for head in range(2):
            payload_ref[head, pl.ds(at * HD, HD), :] = part[head * HD : head * HD + HD]
    segment = jnp.broadcast_to(segment_ref[...].astype(F32), (16, rows)).astype(BF16)
    for head in range(2):
        payload_ref[head, pl.ds(seg_row, 16), :] = segment


def project(table, cut, block_input, segments, lead_steps, gain, shift, lead_weight, weights):
    rows, model = block_input.shape
    heads = weights[0].shape[1] // HD
    line = whole_spec((1, model))
    column = pl.BlockSpec((model, 2 * HD), lambda at, table: (0, at))
    return pl.pallas_call(
        project_kernel,
        grid_spec=pltpu.PrefetchScalarGridSpec(
            num_scalar_prefetch=1,
            grid=(heads // 2,),
            in_specs=[
                whole_spec(block_input.shape),
                whole_spec((1, rows)),
                pl.BlockSpec(memory_space=pltpu.SMEM),
            ]
            + [line] * 3
            + [column] * 3,
            out_specs=[
                pl.BlockSpec((2, payload_rows, rows), lambda at, table: (at, 0, 0)),
                whole_spec((rows, model)),
                whole_spec((rows, cut)),
            ],
        ),
        out_shape=[
            struct((heads, payload_rows, rows), BF16),
            struct((rows, model), BF16),
            struct((rows, cut), BF16),
        ],
        compiler_params=streaming,
        cost_estimate=light,
        name="project",
    )(table, block_input, segments[None], lead_steps, gain[None], shift[None], lead_weight[None], *weights)


def mlp_kernel(count, core_ref, input_ref, grad_ref, *refs):
    branches, refs = refs[:count], refs[count:]
    output_bias, gain, shift, up_weight, up_bias, down_weight = refs[:6]
    keep_ref, give_ref, keep_in_ref, give_in_ref, hidden_ref, bias_ref, forward_ref, back_ref = refs[
        6:14
    ]
    mlp_in_ref, forward, back = refs[14:]
    at = pl.program_id(0)
    is_down = core_ref[core_ref.shape[0] - 2] == 0

    @pl.when(at == 0)
    def _():
        hidden = input_ref[...].astype(F32) + output_bias[...]
        for branch in branches:
            hidden += branch[...].astype(F32)
        hidden_ref[...] = hidden
        unit, _ = normalize(hidden)
        mlp_in = (unit * gain[...] + shift[...]).astype(BF16)
        mlp_in_ref[...] = mlp_in
        keep_in_ref[...] = jnp.where(is_down, grad_ref[...], mlp_in)
        give_in_ref[...] = jnp.where(is_down, mlp_in, grad_ref[...])
        forward[...] = jnp.zeros_like(forward)
        back[...] = jnp.zeros_like(back)

    upper = product(mlp_in_ref[...], up_weight[...]) + up_bias[...]
    share = 0.5 + 0.5 * lax.erf(upper * math.sqrt(0.5))
    slope = share + upper * (jnp.exp(upper * upper * -0.5) * (1.0 / math.sqrt(2.0 * math.pi)))
    active = (upper * share).astype(BF16)
    d_active = product(grad_ref[...], down_weight[...], 1, 1)
    d_upper = (d_active * slope).astype(BF16)
    keep_ref[...] = jnp.where(is_down, active, d_upper)
    give_ref[...] = jnp.where(is_down, d_upper, active)
    bias_ref[...] = jnp.sum(d_upper.astype(F32), axis=0, keepdims=True)
    forward[...] += product(active, down_weight[...])
    back[...] += product(d_upper, up_weight[...], 1, 1)

    @pl.when(at == pl.num_programs(0) - 1)
    def _():
        forward_ref[...] = forward[...].astype(BF16)
        back_ref[...] = back[...].astype(BF16)


def mlp(
    table, block_input, out_grad, branches, output_bias, gain, shift, up_weight, up_bias, down_weight
):
    rows, model = block_input.shape
    units = up_weight.shape[1]
    step = math.gcd(units, 512)
    tile, line = whole_spec((rows, model)), whole_spec((1, model))
    wide = pl.BlockSpec((rows, step), lambda at, table: (0, at))
    bias = pl.BlockSpec((1, step), lambda at, table: (0, at))
    return pl.pallas_call(
        functools.partial(mlp_kernel, len(branches)),
        grid_spec=pltpu.PrefetchScalarGridSpec(
            num_scalar_prefetch=1,
            grid=(units // step,),
            in_specs=[tile] * (2 + len(branches))
            + [line] * 3
            + [
                pl.BlockSpec((model, step), lambda at, table: (0, at)),
                bias,
                pl.BlockSpec((step, model), lambda at, table: (at, 0)),
            ],
            out_specs=[wide, wide, tile, tile, tile, bias, tile, tile],
            scratch_shapes=[pltpu.VMEM((rows, model), BF16)]
            + [pltpu.VMEM((rows, model), F32)] * 2,
        ),
        out_shape=[struct((rows, units), BF16)] * 2
        + [struct((rows, model), BF16)] * 2
        + [
            struct((rows, model), F32),
            struct((1, units), F32),
            struct((rows, model), BF16),
            struct((rows, model), BF16),
        ],
        compiler_params=streaming,
        cost_estimate=light,
        name="mlp",
    )(
        table,
        block_input,
        out_grad,
        *branches,
        output_bias[None],
        gain[None],
        shift[None],
        up_weight,
        up_bias[None],
        down_weight,
    )


def middle_kernel(count, hidden_ref, grad_ref, *refs):
    parts, refs = refs[:count], refs[count:]
    gain, output_weight, d_hidden_ref, d_branch_ref, d_attn_ref, sums_ref = refs
    unit, inverse = normalize(hidden_ref[...])
    d_mlp = parts[0][...].astype(F32)
    for part in parts[1:]:
        d_mlp += part[...].astype(F32)
    grad = grad_ref[...].astype(F32)
    d_hidden = grad + normalize_back(d_mlp * gain[...], unit, inverse)
    d_hidden_ref[...] = d_hidden
    d_branch = d_hidden.astype(BF16)
    d_branch_ref[...] = d_branch
    d_attn_ref[...] = product(output_weight[...], d_branch, 1, 1).astype(BF16)
    for at, values in enumerate((d_hidden, d_mlp * unit, d_mlp, grad)):
        sums_ref[pl.ds(at, 1), :] = jnp.sum(values, axis=0, keepdims=True)


def middle(hidden, out_grad, parts, gain, output_weight):
    rows, model = hidden.shape
    width = output_weight.shape[0]
    return pl.pallas_call(
        functools.partial(middle_kernel, len(parts)),
        out_shape=[
            struct((rows, model), F32),
            struct((rows, model), BF16),
            struct((width, rows), BF16),
            struct((4, model), F32),
        ],
        compiler_params=streaming,
        cost_estimate=light,
        name="middle",
    )(hidden, out_grad, *parts, gain[None], output_weight)


def mask_rows(piece, chip, crops):
    crop = lax.broadcasted_iota(jnp.int32, (HD, piece.shape[2]), 0)
    segment = piece[chip, pl.ds(seg_row, 16), :].astype(F32)[:1].astype(jnp.int32)
    return jnp.where((crop != segment) & (crop < crops), masked_value, 0.0)


def load_keys(piece, crops, keys, key_t, value_n):
    chips, _, patches = piece.shape
    for chip in range(chips):
        key = piece[chip, pl.ds(HD, HD), :]
        value = piece[chip, pl.ds(2 * HD, HD), :]
        place = pl.ds(chip * patches, patches)
        both = jnp.concatenate([key.astype(F32), mask_rows(piece, chip, crops)], axis=0)
        keys[place, :] = both.T.astype(BF16)
        key_t[:, place] = key
        value_n[place, :] = value.astype(F32).T.astype(BF16)


def masked_query(query_ref, dtype=BF16):
    query = query_ref[0, pl.ds(0, HD), :].astype(F32) * 0.125
    segment = query_ref[0, pl.ds(seg_row, 16), :].astype(F32)[:1].astype(jnp.int32)
    crop = lax.broadcasted_iota(jnp.int32, query.shape, 0)
    onehot = jnp.where(crop == segment, 1.0, 0.0)
    return jnp.concatenate([query, onehot], axis=0).astype(dtype)


def forward_kernel(
    crops, step, query_ref, own, other, raw_ref, out_ref, logsum_ref, key_t, value_n, scores
):
    @pl.when(pl.program_id(0) == 0)
    def _():
        start = 0
        for piece in (own, other):
            chips, _, patches = piece.shape
            for chip in range(chips):
                place = pl.ds(start, patches)
                key = piece[chip, pl.ds(HD, HD), :].astype(F32)
                key_t[:, place] = jnp.concatenate([key, mask_rows(piece, chip, crops)], axis=0).astype(BF16)
                value = piece[chip, pl.ds(2 * HD, HD), :].astype(F32)
                value = jnp.concatenate([value, jnp.ones_like(value)], axis=0)
                value_n[place, :] = value.T.astype(BF16)
                start += patches

    query = masked_query(query_ref, F32).T.astype(BF16)
    count = query.shape[0]
    top = jnp.full((count, 128), masked_value, F32)
    for start in range(0, key_t.shape[1], step):
        block = product(query, key_t[:, pl.ds(start, step)])
        scores[:, pl.ds(start, step)] = block
        for at in range(0, step, 128):
            top = jnp.maximum(top, block[:, at : at + 128])
    top = jnp.max(top, axis=1, keepdims=True)
    accum = jnp.zeros((count, 2 * HD), F32)
    for start in range(0, key_t.shape[1], step):
        weights = jnp.exp(scores[:, pl.ds(start, step)] - top).astype(BF16)
        accum += product(weights, value_n[pl.ds(start, step), :])
    accum = accum.T
    total = accum[HD : HD + 1]
    raw = accum[:HD] / total
    raw_ref[0] = raw
    out_ref[0] = raw.astype(BF16)
    top = jnp.broadcast_to(top, (count, 128)).T[:1]
    logsum_ref[0] = top + jnp.log(total)


def backward_kernel(
    crops,
    before,
    query_ref,
    grad_ref,
    raw_ref,
    logsum_ref,
    *refs,
):
    before_refs, refs = refs[:before], refs[before:]
    piece, (dquery_ref, sums_ref, keys, key_t, value_n, sums) = refs[0], refs[-6:]
    group = pl.program_id(0)

    @pl.when(group == 0)
    def _():
        load_keys(piece, crops, keys, key_t, value_n)
        sums[...] = jnp.zeros_like(sums)

    query = masked_query(query_ref)
    grad = grad_ref[0]
    grad_wide = grad.astype(F32)
    delta = jnp.sum(grad_wide * raw_ref[0], axis=0, keepdims=True)
    scaled = query_ref[0, pl.ds(0, HD), :].astype(F32) * 0.125
    zero = jnp.zeros_like(scaled)
    query_side = jnp.concatenate([scaled, zero], axis=0).T.astype(BF16)
    grad_side = jnp.concatenate([zero, grad_wide], axis=0).T.astype(BF16)
    probs = jnp.exp(product(keys[...], query) - logsum_ref[0])
    dprobs = product(value_n[...], grad)
    dscores = (probs * (dprobs - delta)).astype(BF16)
    sums[...] += product(dscores, query_side) + product(probs.astype(BF16), grad_side)
    dquery = product(key_t[...], dscores) * 0.125
    for ref in before_refs:
        dquery = ref[0] + dquery
    dquery_ref[0] = dquery.astype(dquery_ref.dtype)

    @pl.when(group == pl.num_programs(0) - 1)
    def _():
        chips, _, patches = sums_ref.shape
        for chip in range(chips):
            sums_ref[chip] = sums[pl.ds(chip * patches, patches), :].T.astype(sums_ref.dtype)


def key_step(count):
    return 1024 if count % 1024 == 0 else 256


def query_spec(rows, patches):
    return pl.BlockSpec((1, rows, patches), lambda group: (group, 0, 0))


def attention_forward(queries, own, other, crops):
    groups, _, patches = queries.shape
    count = 2 * own.shape[0] * own.shape[2]
    return pl.pallas_call(
        functools.partial(forward_kernel, crops, key_step(count)),
        grid=(groups,),
        in_specs=[
            query_spec(payload_rows, patches),
            whole_spec(own.shape),
            whole_spec(other.shape),
        ],
        out_specs=[query_spec(HD, patches), query_spec(HD, patches), query_spec(1, patches)],
        out_shape=[
            struct((groups, HD, patches), F32),
            struct((groups, HD, patches), BF16),
            struct((groups, 1, patches), F32),
        ],
        scratch_shapes=[
            pltpu.VMEM((2 * HD, count), BF16),
            pltpu.VMEM((count, 2 * HD), BF16),
            pltpu.VMEM((patches, count), F32),
        ],
        compiler_params=streaming,
        cost_estimate=light,
        name="attention_forward",
    )(queries, own, other)


def backward_piece(queries, grads, raw, logsum, before, keys, earlier, index, pieces, crops, dtypes):
    groups, _, patches = queries.shape
    chips = keys.shape[0] // pieces
    count = chips * keys.shape[2]
    sums_shape = (chips, 2 * HD, keys.shape[2])
    return pl.pallas_call(
        functools.partial(backward_kernel, crops, len(before)),
        grid=(groups,),
        in_specs=[
            query_spec(payload_rows, patches),
            query_spec(HD, patches),
            query_spec(HD, patches),
            query_spec(1, patches),
        ]
        + [query_spec(HD, patches)] * len(before)
        + [pl.BlockSpec((chips,) + keys.shape[1:], lambda group: (index, 0, 0))]
        + [pl.BlockSpec(memory_space=pl.ANY)] * len(earlier),
        out_specs=[
            query_spec(HD, patches),
            pl.BlockSpec(sums_shape, lambda group: (index, 0, 0)),
        ],
        out_shape=[
            struct((groups, HD, patches), dtypes[0]),
            struct((keys.shape[0],) + sums_shape[1:], dtypes[1]),
        ],
        input_output_aliases={5 + len(before): 1} if earlier else {},
        scratch_shapes=[
            pltpu.VMEM((count, 2 * HD), BF16),
            pltpu.VMEM((HD, count), BF16),
            pltpu.VMEM((count, HD), BF16),
            pltpu.VMEM((count, 2 * HD), F32),
        ],
        compiler_params=params,
        cost_estimate=light,
        name="attention_backward",
    )(queries, grads, raw, logsum, *before, keys, *earlier)


def swap_cores(values):
    return lax.ppermute(values, "core", [(0, 1), (1, 0)])


def to_heads(blocks):
    return lax.all_to_all(blocks, "chip", 0, 0, tiled=True)


def scatter_queries(values, heads, split):
    rows, patches = values.shape[0] // heads, values.shape[1]
    if split == 1:
        return to_heads(values.reshape(heads, rows, patches))
    part = patches // split
    blocks = values.reshape(heads, rows, split, part).transpose(0, 2, 1, 3)
    moved = to_heads(blocks.reshape(heads * split, rows, part))
    width = min(256, moved.shape[0] * part)
    joined = moved.transpose(1, 0, 2).reshape(rows, -1, width)
    return joined.transpose(1, 0, 2)


def gather_queries(values, heads, split, patches):
    rows = values.shape[1]
    if split == 1:
        return to_heads(values).reshape(heads * rows, patches)
    part = patches // split
    joined = values.transpose(1, 0, 2).reshape(rows, heads * split, part)
    moved = to_heads(joined.transpose(1, 0, 2)).reshape(heads, split, rows, part)
    return moved.transpose(0, 2, 1, 3).reshape(heads * rows, patches)


def across_heads(part):
    if lax.axis_size("head") == 2:
        return [part, lax.ppermute(part, "head", [(0, 1), (1, 0)])]
    return [lax.psum(part, "head")]


def ring_pairs(direction):
    chips = lax.axis_size("chip")
    order = list(range(0, chips, 2)) + list(range(chips - 1, 0, -2))
    return [(order[at], order[(at + direction) % chips]) for at in range(chips)]


def ring_table():
    chips, chip = lax.axis_size("chip"), lax.axis_index("chip")
    place = jnp.where(chip % 2 == 0, chip // 2, chips - 1 - chip // 2)
    steps = jnp.arange(2 * chips + 2, dtype=jnp.int32)
    places = (place + steps) % chips
    there = jnp.where(places < chips // 2, 2 * places, 2 * (chips - 1 - places) + 1)
    table = jnp.where(steps < chips, places, there)
    table = jnp.where(steps == 2 * chips, lax.axis_index("core"), table)
    return jnp.where(steps == 2 * chips + 1, lax.axis_index("head"), table).astype(jnp.int32)


def visit(streams, values):
    states, values = lax.optimization_barrier(([stream.state for stream in streams], values))
    for stream, state in zip(streams, states):
        stream.advance(state)
    ready, values = lax.optimization_barrier(([stream.ready for stream in streams], values))
    for stream, blocks in zip(streams, ready):
        stream.send(blocks)
    return values


def join_kernel(*refs):
    start = 0
    for block in refs[:-1]:
        refs[-1][pl.ds(start, block.shape[0]), :] = block[...]
        start += block.shape[0]


def join(blocks):
    rows = sum(block.shape[0] for block in blocks)
    return pl.pallas_call(
        join_kernel,
        out_shape=struct((rows, blocks[0].shape[1]), blocks[0].dtype),
        compiler_params=streaming,
        name="join",
    )(*blocks)


def halves_kernel(left, right, left_ref, right_ref):
    left_ref[...] = left[...]
    right_ref[...] = right[...]


def halves(left, right):
    rows, columns = left.shape
    if rows % 16 or columns % 256:
        return [left[:, : columns // 2], right[:, columns // 2 :]]
    out = pl.BlockSpec((rows, columns // 2), lambda at: (0, 0))
    return pl.pallas_call(
        halves_kernel,
        grid=(1,),
        in_specs=[out, pl.BlockSpec((rows, columns // 2), lambda at: (0, 1))],
        out_specs=[out, out],
        out_shape=[struct((rows, columns // 2), left.dtype)] * 2,
        compiler_params=streaming,
        name="halves",
    )(left, right)


class Gather:
    def __init__(self, block, swap=False, take=None):
        self.reach, self.swap, self.take = lax.axis_size("chip") // 2, swap, take
        self.blocks, self.pairs, self.count = [], [], 0
        self.new, self.outputs = [0], []
        self.ready = [block]

    def send(self, ready):
        new = list(zip(self.new, ready))
        self.blocks += new
        self.new = new
        self.count += 1
        sides = ready if len(ready) > 1 else ready * 2
        if self.count == self.reach:
            sides = halves(*sides)
        flying = []
        if self.count <= self.reach:
            flying = [
                lax.ppermute(block, "chip", ring_pairs(direction))
                for block, direction in zip(sides, (1, -1))
            ]
        swapped = [swap_cores(block) for block in ready] if self.swap else []
        self.state = (flying, swapped, self.outputs)

    def advance(self, state):
        arrived, swapped, self.outputs = state
        pairs = [(step, near, far) for (step, near), far in zip(self.new, swapped)]
        self.pairs += pairs
        if self.take and pairs:
            self.outputs = self.take(self.outputs, pairs)
        self.new = [-self.count, self.count]
        if arrived and self.count == self.reach:
            arrived, self.new = [jnp.concatenate(arrived, axis=1)], [self.count]
        self.ready = arrived

    def busy(self):
        return bool(self.state[0] or self.state[1])


def add_kernel(wanted, _, *refs):
    outputs, refs = refs[-len(wanted) :], list(refs[: -len(wanted)])
    keep_in, far_in = refs.pop(0), refs.pop(0)
    for starts, output in zip(wanted, outputs):
        near, far = refs.pop(0), refs.pop(0)
        total = product(near[...], keep_in[...], 0, 0) + product(far[...], far_in[...], 0, 0)
        output[...] = total.astype(BF16)
        arrived = [refs.pop(0) for _ in starts]
        for start in sorted(set(starts)):
            parts = [part for part, at in zip(arrived, starts) if at == start]
            columns = slice(start, start + parts[0].shape[1])
            summed = total[:, columns]
            for part in parts:
                summed += part[...].astype(F32)
            output[:, columns] = summed.astype(BF16)


class Reduce:
    def __init__(self, keep, far, keep_in, far_in, table):
        self.chips, self.table = lax.axis_size("chip"), table
        self.operands, self.sides = (keep, far), (keep_in, far_in)
        self.units = keep.shape[1] // self.chips
        self.tiled = self.units % 128 == 0
        self.left, self.rest = self.chips // 2, None
        (block,) = self.add([(self.left, [])])
        self.send(halves(block, block))

    def send(self, ready):
        self.left -= 1
        self.state = [
            lax.ppermute(block, "chip", ring_pairs(direction))
            for block, direction in zip(ready, (1, -1))
        ]

    def advance(self, state):
        half = self.sides[0].shape[1] // 2
        ahead, behind = state
        first = 0 if ahead.shape[1] != half else half
        self.ready = self.add([(self.left, [(ahead, 0)]), (-self.left, [(behind, first)])])

    def finish(self, values):
        (ahead, behind), values = lax.optimization_barrier((self.state, values))
        (total,) = self.add([(0, [(ahead, 0), (behind, 0)])])
        return total, values

    def add(self, wanted):
        (rows, model), units, chips = self.sides[0].shape, self.units, self.chips
        if not self.tiled:
            sums = []
            for step, parts in wanted:
                start = self.table[step % chips] * units
                total = jnp.zeros((units, model), F32)
                for operand, side in zip(self.operands, self.sides):
                    block = lax.dynamic_slice_in_dim(operand, start, units, 1)
                    total += product(block, side, 0, 0)
                for part, start in parts:
                    total = total.at[:, start : start + part.shape[1]].add(part.astype(F32))
                sums.append(total.astype(BF16))
            return sums
        side = pl.BlockSpec((rows, model), lambda at, table: (0, 0))
        whole = pl.BlockSpec((units, model), lambda at, table: (0, 0))
        specs, arrays = [side] * 2, list(self.sides)
        for step, parts in wanted:
            block = pl.BlockSpec(
                (rows, units), lambda at, table, step=step % chips: (0, table[step])
            )
            specs += [block] * 2
            specs += [pl.BlockSpec(part.shape, lambda at, table: (0, 0)) for part, _ in parts]
            arrays += list(self.operands) + [part for part, _ in parts]
        return pl.pallas_call(
            functools.partial(add_kernel, [[start for _, start in parts] for _, parts in wanted]),
            grid_spec=pltpu.PrefetchScalarGridSpec(
                num_scalar_prefetch=1,
                grid=(1,),
                in_specs=specs,
                out_specs=[whole] * len(wanted),
            ),
            out_shape=[struct((units, model), BF16)] * len(wanted),
            compiler_params=streaming,
            cost_estimate=light,
            name="ring_add",
        )(self.table, *arrays)

    def place(self, outputs, pairs):
        units, chips, model = self.units, self.chips, self.sides[0].shape[1]
        shapes = [struct((chips * units, model), F32), struct((model, chips * units), F32)]
        if not self.tiled:
            outputs = outputs or [jnp.zeros(shape.shape, F32) for shape in shapes]
            down, up = outputs
            is_down = self.table[2 * chips] == 0
            for step, near, far in pairs:
                start = self.table[step % chips] * units
                near, far = near[:units], far[:units]
                first = jnp.where(is_down, near, far).astype(F32)
                second = jnp.where(is_down, far, near).astype(F32).T
                down = lax.dynamic_update_slice_in_dim(down, first, start, 0)
                up = lax.dynamic_update_slice_in_dim(up, second, start, 1)
            return [down, up]
        first = pairs[0][0] % chips
        stride = pairs[-1][0] % chips - first
        block = pl.BlockSpec((units, model), lambda at, table: (0, 0))
        return pl.pallas_call(
            functools.partial(place_kernel, len(pairs)),
            grid_spec=pltpu.PrefetchScalarGridSpec(
                num_scalar_prefetch=1,
                grid=(len(pairs),),
                in_specs=[pl.BlockSpec(memory_space=pl.ANY)] * len(outputs)
                + [block] * (2 * len(pairs)),
                out_specs=[
                    pl.BlockSpec((units, model), lambda at, table: (table[first + at * stride], 0)),
                    pl.BlockSpec((model, units), lambda at, table: (0, table[first + at * stride])),
                ],
            ),
            out_shape=shapes,
            input_output_aliases={1 + at: at for at in range(len(outputs))},
            compiler_params=streaming,
            cost_estimate=light,
            name="place",
        )(self.table, *outputs, *[pair[1] for pair in pairs], *[pair[2] for pair in pairs])


def place_kernel(count, table, *refs):
    nears, fars, (down, up) = refs[-2 - 2 * count : -2 - count], refs[-2 - count : -2], refs[-2:]
    core = table[table.shape[0] - 2]

    def put(first, second):
        down[...] = first[...].astype(F32)
        up[...] = second[...].astype(F32).T

    for at, (near, far) in enumerate(zip(nears, fars)):
        here = pl.program_id(0) == at
        pl.when(here & (core == 0))(functools.partial(put, near, far))
        pl.when(here & (core != 0))(functools.partial(put, far, near))


def head_gradient_kernel(steps, chips, table, query_ref, key_value_ref, *refs):
    parts, out_ref = refs[:-1], refs[-1]
    patches = query_ref.shape[2]
    for at, part in enumerate(parts):

        @pl.when(pl.program_id(0) == at)
        def _(part=part):
            total = jnp.zeros(out_ref.shape, F32)
            for index, step in enumerate(steps):
                chip = table[chips + step % chips]
                grads = jnp.concatenate([query_ref[chip], key_value_ref[chip]], axis=0)
                total += product(grads, part[pl.ds(index * patches, patches), :])
            out_ref[...] = total.astype(BF16)


def head_gradient(dquery, key_value, parts, steps, table):
    chips, rows, _ = dquery.shape
    columns = parts[0].shape[1]

    def column(at, table):
        mine = table[2 * chips + 1] if len(parts) > 1 else 0
        return (0, jnp.where(at == 0, mine, 1 - mine))

    return pl.pallas_call(
        functools.partial(head_gradient_kernel, steps, chips),
        grid_spec=pltpu.PrefetchScalarGridSpec(
            num_scalar_prefetch=1,
            grid=(len(parts),),
            in_specs=[
                pl.BlockSpec(array.shape, lambda at, table, rank=array.ndim: (0,) * rank)
                for array in (dquery, key_value, *parts)
            ],
            out_specs=pl.BlockSpec((3 * rows, columns), column),
        ),
        out_shape=struct((3 * rows, columns * len(parts)), BF16),
        compiler_params=streaming,
        cost_estimate=light,
        name="head_gradient",
    )(table, dquery, key_value, *parts)


def layout_kernel(steps, size, extra, table, *refs):
    count = len(steps)
    blocks, refs = refs[: 4 * count], refs[4 * count :]
    nears = list(zip(blocks[:count], blocks[2 * count : 3 * count]))
    fars = list(zip(blocks[count : 2 * count], blocks[3 * count :]))
    outputs, (output_ref, small_ref, held) = refs[:3], refs[3:]
    at = pl.program_id(0)

    @pl.when(at == 0)
    def _():
        core = table[2 * count]
        for step, near, far in zip(steps, nears, fars):
            chip = table[count + step % count]
            for side, (block, small) in ((core, near), (1 - core, far)):
                held[chip, side] = block[pl.ds(0, size), :]
                output_ref[side, chip] = block[pl.ds(size, extra), :].astype(F32)
                small_ref[side, chip] = small[...].astype(F32)

    pair = [
        jnp.concatenate([held[2 * at + head, 0], held[2 * at + head, 1]], axis=0)
        for head in range(2)
    ]
    for index, output in enumerate(outputs):
        rows = [part[index * HD : index * HD + HD] for part in pair]
        output[...] = jnp.concatenate(rows, axis=0).astype(F32).T


def final_layout(pairs, start, size, table):
    count = len(pairs)
    steps, nears, fars = zip(*pairs)
    rows, model = nears[0].shape
    extra = rows - start - size - small_rows
    part = pl.BlockSpec((size + extra, model), lambda at, table: (start // (size + extra), 0))
    last = pl.BlockSpec((small_rows, model), lambda at, table: (rows // small_rows - 1, 0))
    return pl.pallas_call(
        functools.partial(layout_kernel, steps, size, extra),
        grid_spec=pltpu.PrefetchScalarGridSpec(
            num_scalar_prefetch=1,
            grid=(count // 2,),
            in_specs=[part] * (2 * count) + [last] * (2 * count),
            out_specs=[pl.BlockSpec((model, 2 * HD), lambda at, table: (0, at))] * 3
            + [
                pl.BlockSpec((2, count, extra, model), lambda at, table: (0, 0, 0, 0)),
                pl.BlockSpec((2, count, small_rows, model), lambda at, table: (0, 0, 0, 0)),
            ],
            scratch_shapes=[pltpu.VMEM((count, 2, size, model), BF16)],
        ),
        out_shape=[struct((model, count * HD), F32)] * 3
        + [
            struct((2, count, extra, model), F32),
            struct((2, count, small_rows, model), F32),
        ],
        compiler_params=streaming,
        cost_estimate=light,
        name="final_layout",
    )(table, *nears, *fars, *nears, *fars)


def core_half(values, axis, side):
    size = values.shape[axis] // 2
    return lax.dynamic_slice_in_dim(values, side * size, size, axis)


def share_halves(values, axis):
    core = lax.axis_index("core")
    return core_half(values, axis, core), swap_cores(core_half(values, axis, 1 - core))


def local(
    block_input,
    out_grad,
    segments,
    lead_steps,
    gain_attn,
    shift_attn,
    lead_weight,
    query_weight,
    key_weight,
    value_weight,
    output_weight,
    output_bias,
    gain_mlp,
    shift_mlp,
    up_weight,
    up_bias,
    down_weight,
    down_bias,
):
    rows, model = block_input.shape
    heads = query_weight.shape[1] // HD
    width = heads * HD
    chips, core = lax.axis_size("chip"), lax.axis_index("core")
    split = chips // heads
    crops = lead_steps.shape[0]
    table = ring_table()
    weights = (query_weight, key_weight, value_weight)
    cut = model // 2 if lax.axis_size("head") == 2 else model
    payload, attn_in, attn_in_cut = project(
        table, cut, block_input, segments, lead_steps, gain_attn, shift_attn, lead_weight, weights
    )
    if split == 1:
        own = to_heads(payload)
        queries = own
    else:
        queries = scatter_queries(payload.reshape(-1, rows), heads, split)
        own = to_heads(jnp.repeat(payload, split, axis=0))
    own, attn_in_cut = lax.optimization_barrier((own, attn_in_cut))
    inputs = Gather(attn_in_cut)
    inputs.send(inputs.ready)
    other = swap_cores(own)
    raw, out, logsum = attention_forward(queries, own, other, crops)
    out = visit([inputs], out)
    attn_out = gather_queries(out, heads, split, rows)
    attn_out = visit([inputs], attn_out)
    branches = across_heads(product(attn_out, output_weight, 0, 0).astype(BF16))
    branches = visit([inputs], branches)
    keep, give, keep_in, give_in, hidden, dup_bias, mlp_part, d_mlp_part = mlp(
        table,
        block_input,
        out_grad,
        branches,
        output_bias,
        gain_mlp,
        shift_mlp,
        up_weight,
        up_bias,
        down_weight,
    )
    keep, give, keep_in, give_in, d_mlp_part = visit(
        [inputs], (keep, give, keep_in, give_in, d_mlp_part)
    )
    d_mlp = across_heads(d_mlp_part)
    ring = Reduce(keep, swap_cores(give), keep_in, swap_cores(give_in), table)
    while inputs.busy():
        visit([inputs], ())
    steps, inputs = zip(*inputs.blocks)
    inputs = join(inputs)
    mlp_part, inputs, d_mlp = lax.optimization_barrier((mlp_part, inputs, d_mlp))
    parts = [inputs]
    if cut != model:
        parts = across_heads(inputs)
    d_hidden, d_branch, d_attn, sums = middle(hidden, out_grad, d_mlp, gain_mlp, output_weight)
    grads = scatter_queries(d_attn, heads, split)
    d_branch, mlp_part = visit([ring], (d_branch, mlp_part))
    mlp_out = across_heads(mlp_part)
    out_near, out_far = share_halves(attn_out, 0)
    doutput = product(out_near, d_branch) + product(out_far, swap_cores(d_branch))
    doutput = to_heads(doutput.astype(BF16).reshape(chips, -1, model))
    grads = visit([ring], grads)
    *dquery, far_sums = backward_piece(
        queries, grads, raw, logsum, [], other, [], 0, 1, crops, (F32, BF16)
    )
    grads, dquery, far_sums = visit([ring], (grads, dquery, far_sums))
    far_sums = swap_cores(far_sums)
    *dquery, near_sums = backward_piece(
        queries, grads, raw, logsum, dquery, own, [], 0, 1, crops, (BF16, F32)
    )
    (dquery,) = dquery
    key_value = (near_sums + far_sums.astype(F32)).astype(BF16)
    doutput, key_value = lax.optimization_barrier((doutput, key_value))
    doutput = jnp.sum(doutput.astype(F32), axis=0)
    small = jnp.concatenate([sums.reshape(-1), dup_bias[0]])
    small = jnp.pad(small, (0, small_rows * model - small.shape[0])).reshape(small_rows, model)
    doutput = jnp.concatenate([doutput, small], axis=0).astype(BF16)
    if split == 1:
        moved = to_heads(jnp.concatenate([dquery, key_value], axis=1))
        projections = head_gradient(dquery, key_value, parts, steps, table)
        near, far = share_halves(projections, 0)
        projections = (near.astype(F32) + far.astype(F32)).astype(BF16)
        size = projections.shape[0]
        blocks = jnp.concatenate([projections, doutput], axis=0)
        dquery, dkey, dvalue = (
            moved[:, at * HD : at * HD + HD].reshape(width, rows) for at in range(3)
        )
    else:
        dquery = gather_queries(dquery, heads, split, rows)
        moved = to_heads(key_value).reshape(heads, split, 2 * HD, rows).astype(F32)
        moved = jnp.sum(moved, axis=1).astype(BF16)
        dkey, dvalue = (moved[:, at * HD : at * HD + HD].reshape(width, rows) for at in range(2))
        size, blocks = 0, doutput
        projections = [
            lax.psum(product(attn_in, grad, 0, 1).astype(BF16), ("chip", "core")).astype(F32)
            for grad in (dquery, dkey, dvalue)
        ]
    total, blocks = ring.finish(blocks)
    start = total.shape[0]
    gathered = Gather(jnp.concatenate([total, blocks], axis=0), True, ring.place)
    gathered.send(gathered.ready)
    d_part = (
        product(dquery, query_weight, 0, 1)
        + product(dkey, key_weight, 0, 1)
        + product(dvalue, value_weight, 0, 1)
    )
    d_part = visit([gathered], d_part)
    d_in = across_heads(d_part.astype(BF16))
    unit_attn, inverse_attn = normalize(block_input.astype(F32))
    onehot = (segments[:, None] == jnp.arange(crops, dtype=jnp.int32)[None, :]).astype(F32)
    lead = jnp.sum(onehot * lead_steps.astype(F32)[None, :], axis=1) / 12.0
    ends = jnp.stack(
        [
            jnp.sum(d_part * unit_attn, axis=0),
            jnp.sum(d_part, axis=0),
            jnp.sum(lead[:, None] * d_part, axis=0),
        ]
    )
    ends = jnp.pad(ends.reshape(-1, 128), ((0, -ends.size // 128 % 16), (0, 0))).astype(BF16)
    everyone = ("chip", "core", "head")
    ends = jnp.broadcast_to(ends, (lax.axis_size(everyone),) + ends.shape)
    ends = lax.all_to_all(ends, everyone, 0, 0, tiled=True)
    visit([gathered], ())
    d_in, mlp_out = visit([gathered], (d_in, mlp_out))
    block_output = hidden + down_bias
    for part in mlp_out:
        block_output += part.astype(F32)
    block_output = block_output.astype(BF16)
    d_in = functools.reduce(jnp.add, (part.astype(F32) for part in d_in))
    input_grad = (d_hidden + normalize_back(d_in * gain_attn, unit_attn, inverse_attn)).astype(
        BF16
    )
    while gathered.busy():
        visit([gathered], ())
    ddown_weight, dup_weight = gathered.outputs
    ends = jnp.sum(ends.astype(F32), axis=0).reshape(-1)[: 3 * model].reshape(3, model)
    if split == 1:
        *projections, doutput_weight, small = final_layout(gathered.pairs, start, size, table)
        doutput_weight = doutput_weight.reshape(width, model)
    if split != 1:
        blocks = jnp.zeros((2, chips) + blocks.shape, F32)
        for step, near, far in gathered.pairs:
            for side, block in ((core, near[start:]), (1 - core, far[start:])):
                at = (side, table[chips + step % chips], 0, 0)
                block = block[None, None].astype(F32)
                blocks = lax.dynamic_update_slice(blocks, block, at)
        doutput_weight = blocks[:, :, :-small_rows].reshape(width, model)
        small = blocks[:, :, -small_rows:]
    small = jnp.sum(small, axis=(0, 1))
    dup_bias = small[4:].reshape(-1)[: dup_bias.shape[1]]
    return (
        block_output,
        input_grad,
        ends[0],
        ends[1],
        ends[2],
        *projections,
        doutput_weight,
        *small[:3],
        dup_weight,
        dup_bias,
        ddown_weight,
        small[3],
    )


def solution(mesh):
    bands, halves = mesh.shape["band"], mesh.shape["head"]
    inner = Mesh(mesh.devices.reshape(bands // 2, 2, halves), ("chip", "core", "head"))
    band = ("chip", "core")
    rows, columns, split_rows = P(band, None), P(None, "head"), P("head", None)
    return jax.shard_map(
        local,
        mesh=inner,
        in_specs=(
            rows,
            rows,
            P(band),
            P(),
            P(),
            P(),
            P(),
            columns,
            columns,
            columns,
            split_rows,
            P(),
            P(),
            P(),
            columns,
            P("head"),
            split_rows,
            P(),
        ),
        out_specs=(
            rows,
            rows,
            P(),
            P(),
            P(),
            columns,
            columns,
            columns,
            split_rows,
            P(),
            P(),
            P(),
            columns,
            P("head"),
            split_rows,
            P(),
        ),
        check_vma=False,
    )
```

```python
import functools
import math

import jax
import jax.numpy as jnp
from jax import lax
from jax.experimental import pallas as pl
from jax.experimental.pallas import tpu as pltpu
from jax.sharding import Mesh, PartitionSpec as P

HD = 64
F32 = jnp.float32
BF16 = jnp.bfloat16
eps = 1e-05
masked_value = -1e30
seg_row = 3 * HD
payload_rows = 3 * HD + 16
small_rows = 16
params = pltpu.CompilerParams(vmem_limit_bytes=48 * 2**20)
streaming = pltpu.CompilerParams(vmem_limit_bytes=60 * 2**20)


def normalize(values):
    centred = values - jnp.mean(values, axis=-1, keepdims=True)
    inverse = lax.rsqrt(jnp.mean(centred * centred, axis=-1, keepdims=True) + eps)
    return (centred * inverse, inverse)


def normalize_back(grad_unit, unit, inverse):
    return inverse * (
        grad_unit
        - jnp.mean(grad_unit, axis=-1, keepdims=True)
        - unit * jnp.mean(grad_unit * unit, axis=-1, keepdims=True)
    )


def product(first, second, first_axis=1, second_axis=0):
    return lax.dot_general(
        first,
        second,
        (((first_axis,), (second_axis,)), ((), ())),
        preferred_element_type=jnp.float32,
    )


def struct(shape, dtype):
    return jax.ShapeDtypeStruct(shape, dtype)


def whole_spec(shape):
    return pl.BlockSpec(shape, lambda *at: (0,) * len(shape))


light = pl.CostEstimate(flops=1, bytes_accessed=1, transcendentals=0)


def project_kernel(
    table, input_ref, segment_ref, steps_ref, gain, shift, lead_weight, *refs
):
    weights, (payload_ref, attn_in_ref, cut_ref) = refs[:3], refs[3:]
    rows = input_ref.shape[0]

    @pl.when(pl.program_id(0) == 0)
    def _():
        unit, _ = normalize(input_ref[...].astype(F32))
        crops = steps_ref.shape[0]
        crop = lax.broadcasted_iota(jnp.int32, (crops, rows), 0)
        steps = jnp.zeros((crops, rows), jnp.int32)
        for at in range(crops):
            steps = jnp.where(crop == at, steps_ref[at], steps)
        steps = jnp.where(crop == segment_ref[...], steps, 0).astype(F32)
        lead = product(steps, jnp.ones((crops, 128), F32), 0, 0)[:, :1] / 12.0
        attn_in = unit * gain[...] + shift[...] + lead * lead_weight[...]
        attn_in = attn_in.astype(BF16)
        attn_in_ref[...] = attn_in
        columns = cut_ref.shape[1]
        first = table[table.shape[0] - 1] % (attn_in.shape[1] // columns) == 0
        cut_ref[...] = jnp.where(first, attn_in[:, :columns], attn_in[:, -columns:])

    for at, weight in enumerate(weights):
        part = product(attn_in_ref[...], weight[...]).T.astype(BF16)
        for head in range(2):
            payload_ref[head, pl.ds(at * HD, HD), :] = part[head * HD : head * HD + HD]
    segment = jnp.broadcast_to(segment_ref[...].astype(F32), (16, rows)).astype(BF16)
    for head in range(2):
        payload_ref[head, pl.ds(seg_row, 16), :] = segment


def project(table, cut, block_input, segments, lead_steps, gain, shift, lead_weight, weights):
    rows, model = block_input.shape
    heads = weights[0].shape[1] // HD
    line = whole_spec((1, model))
    column = pl.BlockSpec((model, 2 * HD), lambda at, table: (0, at))
    return pl.pallas_call(
        project_kernel,
        grid_spec=pltpu.PrefetchScalarGridSpec(
            num_scalar_prefetch=1,
            grid=(heads // 2,),
            in_specs=[
                whole_spec(block_input.shape),
                whole_spec((1, rows)),
                pl.BlockSpec(memory_space=pltpu.SMEM),
            ]
            + [line] * 3
            + [column] * 3,
            out_specs=[
                pl.BlockSpec((2, payload_rows, rows), lambda at, table: (at, 0, 0)),
                whole_spec((rows, model)),
                whole_spec((rows, cut)),
            ],
        ),
        out_shape=[
            struct((heads, payload_rows, rows), BF16),
            struct((rows, model), BF16),
            struct((rows, cut), BF16),
        ],
        compiler_params=streaming,
        cost_estimate=light,
        name="project",
    )(table, block_input, segments[None], lead_steps, gain[None], shift[None], lead_weight[None], *weights)


def mlp_kernel(count, core_ref, input_ref, grad_ref, *refs):
    branches, refs = refs[:count], refs[count:]
    output_bias, gain, shift, up_weight, up_bias, down_weight = refs[:6]
    keep_ref, give_ref, keep_in_ref, give_in_ref, hidden_ref, bias_ref, forward_ref, back_ref = refs[
        6:14
    ]
    mlp_in_ref, forward, back = refs[14:]
    at = pl.program_id(0)
    is_down = core_ref[core_ref.shape[0] - 2] == 0

    @pl.when(at == 0)
    def _():
        hidden = input_ref[...].astype(F32) + output_bias[...]
        for branch in branches:
            hidden += branch[...].astype(F32)
        hidden_ref[...] = hidden
        unit, _ = normalize(hidden)
        mlp_in = (unit * gain[...] + shift[...]).astype(BF16)
        mlp_in_ref[...] = mlp_in
        keep_in_ref[...] = jnp.where(is_down, grad_ref[...], mlp_in)
        give_in_ref[...] = jnp.where(is_down, mlp_in, grad_ref[...])
        forward[...] = jnp.zeros_like(forward)
        back[...] = jnp.zeros_like(back)

    upper = product(mlp_in_ref[...], up_weight[...]) + up_bias[...]
    share = 0.5 + 0.5 * lax.erf(upper * math.sqrt(0.5))
    slope = share + upper * (jnp.exp(upper * upper * -0.5) * (1.0 / math.sqrt(2.0 * math.pi)))
    active = (upper * share).astype(BF16)
    d_active = product(grad_ref[...], down_weight[...], 1, 1)
    d_upper = (d_active * slope).astype(BF16)
    keep_ref[...] = jnp.where(is_down, active, d_upper)
    give_ref[...] = jnp.where(is_down, d_upper, active)
    bias_ref[...] = jnp.sum(d_upper.astype(F32), axis=0, keepdims=True)
    forward[...] += product(active, down_weight[...])
    back[...] += product(d_upper, up_weight[...], 1, 1)

    @pl.when(at == pl.num_programs(0) - 1)
    def _():
        forward_ref[...] = forward[...].astype(BF16)
        back_ref[...] = back[...].astype(BF16)


def mlp(
    table, block_input, out_grad, branches, output_bias, gain, shift, up_weight, up_bias, down_weight
):
    rows, model = block_input.shape
    units = up_weight.shape[1]
    step = math.gcd(units, 512)
    tile, line = whole_spec((rows, model)), whole_spec((1, model))
    wide = pl.BlockSpec((rows, step), lambda at, table: (0, at))
    bias = pl.BlockSpec((1, step), lambda at, table: (0, at))
    return pl.pallas_call(
        functools.partial(mlp_kernel, len(branches)),
        grid_spec=pltpu.PrefetchScalarGridSpec(
            num_scalar_prefetch=1,
            grid=(units // step,),
            in_specs=[tile] * (2 + len(branches))
            + [line] * 3
            + [
                pl.BlockSpec((model, step), lambda at, table: (0, at)),
                bias,
                pl.BlockSpec((step, model), lambda at, table: (at, 0)),
            ],
            out_specs=[wide, wide, tile, tile, tile, bias, tile, tile],
            scratch_shapes=[pltpu.VMEM((rows, model), BF16)]
            + [pltpu.VMEM((rows, model), F32)] * 2,
        ),
        out_shape=[struct((rows, units), BF16)] * 2
        + [struct((rows, model), BF16)] * 2
        + [
            struct((rows, model), F32),
            struct((1, units), F32),
            struct((rows, model), BF16),
            struct((rows, model), BF16),
        ],
        compiler_params=streaming,
        cost_estimate=light,
        name="mlp",
    )(
        table,
        block_input,
        out_grad,
        *branches,
        output_bias[None],
        gain[None],
        shift[None],
        up_weight,
        up_bias[None],
        down_weight,
    )


def middle_kernel(count, hidden_ref, grad_ref, *refs):
    parts, refs = refs[:count], refs[count:]
    gain, output_weight, d_hidden_ref, d_branch_ref, d_attn_ref, sums_ref = refs
    unit, inverse = normalize(hidden_ref[...])
    d_mlp = parts[0][...].astype(F32)
    for part in parts[1:]:
        d_mlp += part[...].astype(F32)
    grad = grad_ref[...].astype(F32)
    d_hidden = grad + normalize_back(d_mlp * gain[...], unit, inverse)
    d_hidden_ref[...] = d_hidden
    d_branch = d_hidden.astype(BF16)
    d_branch_ref[...] = d_branch
    d_attn_ref[...] = product(output_weight[...], d_branch, 1, 1).astype(BF16)
    for at, values in enumerate((d_hidden, d_mlp * unit, d_mlp, grad)):
        sums_ref[pl.ds(at, 1), :] = jnp.sum(values, axis=0, keepdims=True)


def middle(hidden, out_grad, parts, gain, output_weight):
    rows, model = hidden.shape
    width = output_weight.shape[0]
    return pl.pallas_call(
        functools.partial(middle_kernel, len(parts)),
        out_shape=[
            struct((rows, model), F32),
            struct((rows, model), BF16),
            struct((width, rows), BF16),
            struct((4, model), F32),
        ],
        compiler_params=streaming,
        cost_estimate=light,
        name="middle",
    )(hidden, out_grad, *parts, gain[None], output_weight)


def mask_rows(piece, chip, crops):
    crop = lax.broadcasted_iota(jnp.int32, (HD, piece.shape[2]), 0)
    segment = piece[chip, pl.ds(seg_row, 16), :].astype(F32)[:1].astype(jnp.int32)
    return jnp.where((crop != segment) & (crop < crops), masked_value, 0.0)


def load_keys(piece, crops, keys, key_t, value_n):
    chips, _, patches = piece.shape
    for chip in range(chips):
        key = piece[chip, pl.ds(HD, HD), :]
        value = piece[chip, pl.ds(2 * HD, HD), :]
        place = pl.ds(chip * patches, patches)
        both = jnp.concatenate([key.astype(F32), mask_rows(piece, chip, crops)], axis=0)
        keys[place, :] = both.T.astype(BF16)
        key_t[:, place] = key
        value_n[place, :] = value.astype(F32).T.astype(BF16)


def masked_query(query_ref, dtype=BF16):
    query = query_ref[0, pl.ds(0, HD), :].astype(F32) * 0.125
    segment = query_ref[0, pl.ds(seg_row, 16), :].astype(F32)[:1].astype(jnp.int32)
    crop = lax.broadcasted_iota(jnp.int32, query.shape, 0)
    onehot = jnp.where(crop == segment, 1.0, 0.0)
    return jnp.concatenate([query, onehot], axis=0).astype(dtype)


def forward_kernel(
    crops, step, query_ref, own, other, raw_ref, out_ref, logsum_ref, key_t, value_n, scores
):
    @pl.when(pl.program_id(0) == 0)
    def _():
        start = 0
        for piece in (own, other):
            chips, _, patches = piece.shape
            for chip in range(chips):
                place = pl.ds(start, patches)
                key = piece[chip, pl.ds(HD, HD), :].astype(F32)
                key_t[:, place] = jnp.concatenate([key, mask_rows(piece, chip, crops)], axis=0).astype(BF16)
                value = piece[chip, pl.ds(2 * HD, HD), :].astype(F32)
                value = jnp.concatenate([value, jnp.ones_like(value)], axis=0)
                value_n[place, :] = value.T.astype(BF16)
                start += patches

    query = masked_query(query_ref, F32).T.astype(BF16)
    count = query.shape[0]
    top = jnp.full((count, 128), masked_value, F32)
    for start in range(0, key_t.shape[1], step):
        block = product(query, key_t[:, pl.ds(start, step)])
        scores[:, pl.ds(start, step)] = block
        for at in range(0, step, 128):
            top = jnp.maximum(top, block[:, at : at + 128])
    top = jnp.max(top, axis=1, keepdims=True)
    accum = jnp.zeros((count, 2 * HD), F32)
    for start in range(0, key_t.shape[1], step):
        weights = jnp.exp(scores[:, pl.ds(start, step)] - top).astype(BF16)
        accum += product(weights, value_n[pl.ds(start, step), :])
    accum = accum.T
    total = accum[HD : HD + 1]
    raw = accum[:HD] / total
    raw_ref[0] = raw
    out_ref[0] = raw.astype(BF16)
    top = jnp.broadcast_to(top, (count, 128)).T[:1]
    logsum_ref[0] = top + jnp.log(total)


def backward_kernel(
    crops,
    before,
    query_ref,
    grad_ref,
    raw_ref,
    logsum_ref,
    *refs,
):
    before_refs, refs = refs[:before], refs[before:]
    piece, (dquery_ref, sums_ref, keys, key_t, value_n, sums) = refs[0], refs[-6:]
    group = pl.program_id(0)

    @pl.when(group == 0)
    def _():
        load_keys(piece, crops, keys, key_t, value_n)
        sums[...] = jnp.zeros_like(sums)

    query = masked_query(query_ref)
    grad = grad_ref[0]
    grad_wide = grad.astype(F32)
    delta = jnp.sum(grad_wide * raw_ref[0], axis=0, keepdims=True)
    scaled = query_ref[0, pl.ds(0, HD), :].astype(F32) * 0.125
    zero = jnp.zeros_like(scaled)
    query_side = jnp.concatenate([scaled, zero], axis=0).T.astype(BF16)
    grad_side = jnp.concatenate([zero, grad_wide], axis=0).T.astype(BF16)
    probs = jnp.exp(product(keys[...], query) - logsum_ref[0])
    dprobs = product(value_n[...], grad)
    dscores = (probs * (dprobs - delta)).astype(BF16)
    sums[...] += product(dscores, query_side) + product(probs.astype(BF16), grad_side)
    dquery = product(key_t[...], dscores) * 0.125
    for ref in before_refs:
        dquery = ref[0] + dquery
    dquery_ref[0] = dquery.astype(dquery_ref.dtype)

    @pl.when(group == pl.num_programs(0) - 1)
    def _():
        chips, _, patches = sums_ref.shape
        for chip in range(chips):
            sums_ref[chip] = sums[pl.ds(chip * patches, patches), :].T.astype(sums_ref.dtype)


def key_step(count):
    return 1024 if count % 1024 == 0 else 256


def query_spec(rows, patches):
    return pl.BlockSpec((1, rows, patches), lambda group: (group, 0, 0))


def attention_forward(queries, own, other, crops):
    groups, _, patches = queries.shape
    count = 2 * own.shape[0] * own.shape[2]
    return pl.pallas_call(
        functools.partial(forward_kernel, crops, key_step(count)),
        grid=(groups,),
        in_specs=[
            query_spec(payload_rows, patches),
            whole_spec(own.shape),
            whole_spec(other.shape),
        ],
        out_specs=[query_spec(HD, patches), query_spec(HD, patches), query_spec(1, patches)],
        out_shape=[
            struct((groups, HD, patches), F32),
            struct((groups, HD, patches), BF16),
            struct((groups, 1, patches), F32),
        ],
        scratch_shapes=[
            pltpu.VMEM((2 * HD, count), BF16),
            pltpu.VMEM((count, 2 * HD), BF16),
            pltpu.VMEM((patches, count), F32),
        ],
        compiler_params=streaming,
        cost_estimate=light,
        name="attention_forward",
    )(queries, own, other)


def backward_piece(queries, grads, raw, logsum, before, keys, earlier, index, pieces, crops, dtypes):
    groups, _, patches = queries.shape
    chips = keys.shape[0] // pieces
    count = chips * keys.shape[2]
    sums_shape = (chips, 2 * HD, keys.shape[2])
    return pl.pallas_call(
        functools.partial(backward_kernel, crops, len(before)),
        grid=(groups,),
        in_specs=[
            query_spec(payload_rows, patches),
            query_spec(HD, patches),
            query_spec(HD, patches),
            query_spec(1, patches),
        ]
        + [query_spec(HD, patches)] * len(before)
        + [pl.BlockSpec((chips,) + keys.shape[1:], lambda group: (index, 0, 0))]
        + [pl.BlockSpec(memory_space=pl.ANY)] * len(earlier),
        out_specs=[
            query_spec(HD, patches),
            pl.BlockSpec(sums_shape, lambda group: (index, 0, 0)),
        ],
        out_shape=[
            struct((groups, HD, patches), dtypes[0]),
            struct((keys.shape[0],) + sums_shape[1:], dtypes[1]),
        ],
        input_output_aliases={5 + len(before): 1} if earlier else {},
        scratch_shapes=[
            pltpu.VMEM((count, 2 * HD), BF16),
            pltpu.VMEM((HD, count), BF16),
            pltpu.VMEM((count, HD), BF16),
            pltpu.VMEM((count, 2 * HD), F32),
        ],
        compiler_params=params,
        cost_estimate=light,
        name="attention_backward",
    )(queries, grads, raw, logsum, *before, keys, *earlier)


def swap_cores(values):
    return lax.ppermute(values, "core", [(0, 1), (1, 0)])


def to_heads(blocks):
    return lax.all_to_all(blocks, "chip", 0, 0, tiled=True)


def scatter_queries(values, heads, split):
    rows, patches = values.shape[0] // heads, values.shape[1]
    if split == 1:
        return to_heads(values.reshape(heads, rows, patches))
    part = patches // split
    blocks = values.reshape(heads, rows, split, part).transpose(0, 2, 1, 3)
    moved = to_heads(blocks.reshape(heads * split, rows, part))
    width = min(256, moved.shape[0] * part)
    joined = moved.transpose(1, 0, 2).reshape(rows, -1, width)
    return joined.transpose(1, 0, 2)


def gather_queries(values, heads, split, patches):
    rows = values.shape[1]
    if split == 1:
        return to_heads(values).reshape(heads * rows, patches)
    part = patches // split
    joined = values.transpose(1, 0, 2).reshape(rows, heads * split, part)
    moved = to_heads(joined.transpose(1, 0, 2)).reshape(heads, split, rows, part)
    return moved.transpose(0, 2, 1, 3).reshape(heads * rows, patches)


def across_heads(part):
    if lax.axis_size("head") == 2:
        return [part, lax.ppermute(part, "head", [(0, 1), (1, 0)])]
    return [lax.psum(part, "head")]


def ring_pairs(direction):
    chips = lax.axis_size("chip")
    order = list(range(0, chips, 2)) + list(range(chips - 1, 0, -2))
    return [(order[at], order[(at + direction) % chips]) for at in range(chips)]


def ring_table():
    chips, chip = lax.axis_size("chip"), lax.axis_index("chip")
    place = jnp.where(chip % 2 == 0, chip // 2, chips - 1 - chip // 2)
    steps = jnp.arange(2 * chips + 2, dtype=jnp.int32)
    places = (place + steps) % chips
    there = jnp.where(places < chips // 2, 2 * places, 2 * (chips - 1 - places) + 1)
    table = jnp.where(steps < chips, places, there)
    table = jnp.where(steps == 2 * chips, lax.axis_index("core"), table)
    return jnp.where(steps == 2 * chips + 1, lax.axis_index("head"), table).astype(jnp.int32)


def visit(streams, values):
    states, values = lax.optimization_barrier(([stream.state for stream in streams], values))
    for stream, state in zip(streams, states):
        stream.advance(state)
    ready, values = lax.optimization_barrier(([stream.ready for stream in streams], values))
    for stream, blocks in zip(streams, ready):
        stream.send(blocks)
    return values


def join_kernel(*refs):
    start = 0
    for block in refs[:-1]:
        refs[-1][pl.ds(start, block.shape[0]), :] = block[...]
        start += block.shape[0]


def join(blocks):
    rows = sum(block.shape[0] for block in blocks)
    return pl.pallas_call(
        join_kernel,
        out_shape=struct((rows, blocks[0].shape[1]), blocks[0].dtype),
        compiler_params=streaming,
        name="join",
    )(*blocks)


def halves_kernel(left, right, left_ref, right_ref):
    left_ref[...] = left[...]
    right_ref[...] = right[...]


def halves(left, right):
    rows, columns = left.shape
    if rows % 16 or columns % 256:
        return [left[:, : columns // 2], right[:, columns // 2 :]]
    out = pl.BlockSpec((rows, columns // 2), lambda at: (0, 0))
    return pl.pallas_call(
        halves_kernel,
        grid=(1,),
        in_specs=[out, pl.BlockSpec((rows, columns // 2), lambda at: (0, 1))],
        out_specs=[out, out],
        out_shape=[struct((rows, columns // 2), left.dtype)] * 2,
        compiler_params=streaming,
        name="halves",
    )(left, right)


class Gather:
    def __init__(self, block, swap=False, take=None):
        self.reach, self.swap, self.take = lax.axis_size("chip") // 2, swap, take
        self.blocks, self.pairs, self.count = [], [], 0
        self.new, self.outputs = [0], []
        self.ready = [block]

    def send(self, ready):
        new = list(zip(self.new, ready))
        self.blocks += new
        self.new = new
        self.count += 1
        sides = ready if len(ready) > 1 else ready * 2
        if self.count == self.reach:
            sides = halves(*sides)
        flying = []
        if self.count <= self.reach:
            flying = [
                lax.ppermute(block, "chip", ring_pairs(direction))
                for block, direction in zip(sides, (1, -1))
            ]
        if self.swap and ready:
            pairs = [(step, block, swap_cores(block)) for step, block in new]
            self.pairs += pairs
            self.outputs = self.take(self.outputs, pairs)
        self.state = (flying, self.outputs)

    def advance(self, state):
        arrived, self.outputs = state
        self.new = [-self.count, self.count]
        if arrived and self.count == self.reach:
            arrived, self.new = [jnp.concatenate(arrived, axis=1)], [self.count]
        self.ready = arrived

    def busy(self):
        return bool(self.state[0])


def add_kernel(wanted, count, _, *refs):
    outputs, refs = refs[-count:], list(refs[:-count])
    keep_in, far_in = refs.pop(0), refs.pop(0)
    for starts, output in zip(wanted, outputs):
        near, far = refs.pop(0), refs.pop(0)
        total = product(near[...], keep_in[...], 0, 0) + product(far[...], far_in[...], 0, 0)
        if len(outputs) > len(wanted):
            for at, output in enumerate(outputs):
                columns = output.shape[1]
                output[...] = total[:, at * columns : at * columns + columns].astype(BF16)
            return
        output[...] = total.astype(BF16)
        arrived = [refs.pop(0) for _ in starts]
        for start in sorted(set(starts)):
            parts = [part for part, at in zip(arrived, starts) if at == start]
            columns = slice(start, start + parts[0].shape[1])
            summed = total[:, columns]
            for part in parts:
                summed += part[...].astype(F32)
            output[:, columns] = summed.astype(BF16)


class Reduce:
    def __init__(self, keep, far, keep_in, far_in, table):
        self.chips, self.table = lax.axis_size("chip"), table
        self.operands, self.sides = (keep, far), (keep_in, far_in)
        self.units = keep.shape[1] // self.chips
        self.tiled = self.units % 128 == 0
        self.left, self.rest = self.chips // 2, None
        blocks = self.add([(self.left, [])], True)
        self.send(blocks if len(blocks) > 1 else halves(blocks[0], blocks[0]))

    def send(self, ready):
        self.left -= 1
        self.state = [
            lax.ppermute(block, "chip", ring_pairs(direction))
            for block, direction in zip(ready, (1, -1))
        ]

    def advance(self, state):
        half = self.sides[0].shape[1] // 2
        ahead, behind = state
        first = 0 if ahead.shape[1] != half else half
        self.ready = self.add([(self.left, [(ahead, 0)]), (-self.left, [(behind, first)])])

    def arrive(self, values):
        self.state, values = lax.optimization_barrier((self.state, values))
        return values

    def finish(self):
        ahead, behind = self.state
        return self.add([(0, [(ahead, 0), (behind, 0)])])[0]

    def add(self, wanted, split=False):
        (rows, model), units, chips = self.sides[0].shape, self.units, self.chips
        if not self.tiled:
            sums = []
            for step, parts in wanted:
                start = self.table[step % chips] * units
                total = jnp.zeros((units, model), F32)
                for operand, side in zip(self.operands, self.sides):
                    block = lax.dynamic_slice_in_dim(operand, start, units, 1)
                    total += product(block, side, 0, 0)
                for part, start in parts:
                    total = total.at[:, start : start + part.shape[1]].add(part.astype(F32))
                sums.append(total.astype(BF16))
            return sums
        side = pl.BlockSpec((rows, model), lambda at, table: (0, 0))
        whole = pl.BlockSpec((units, model), lambda at, table: (0, 0))
        specs, arrays = [side] * 2, list(self.sides)
        for step, parts in wanted:
            block = pl.BlockSpec(
                (rows, units), lambda at, table, step=step % chips: (0, table[step])
            )
            specs += [block] * 2
            specs += [pl.BlockSpec(part.shape, lambda at, table: (0, 0)) for part, _ in parts]
            arrays += list(self.operands) + [part for part, _ in parts]
        starts = [[start for _, start in parts] for _, parts in wanted]
        shapes = [struct((units, model), BF16)] * len(wanted)
        if split:
            shapes = [struct((units, model // 2), BF16)] * 2
        return pl.pallas_call(
            functools.partial(add_kernel, starts, len(shapes)),
            grid_spec=pltpu.PrefetchScalarGridSpec(
                num_scalar_prefetch=1,
                grid=(1,),
                in_specs=specs,
                out_specs=[pl.BlockSpec(shape.shape, lambda at, table: (0, 0)) for shape in shapes],
            ),
            out_shape=shapes,
            compiler_params=streaming,
            cost_estimate=light,
            name="ring_add",
        )(self.table, *arrays)

    def place(self, outputs, pairs):
        units, chips, model = self.units, self.chips, self.sides[0].shape[1]
        size, extra = self.size, self.extra
        shapes = [struct((chips * units, model), F32), struct((model, chips * units), F32)]
        if not self.tiled:
            outputs = outputs or [jnp.zeros(shape.shape, F32) for shape in shapes]
            down, up = outputs
            is_down = self.table[2 * chips] == 0
            for step, near, far in pairs:
                start = self.table[step % chips] * units
                near, far = near[:units], far[:units]
                first = jnp.where(is_down, near, far).astype(F32)
                second = jnp.where(is_down, far, near).astype(F32).T
                down = lax.dynamic_update_slice_in_dim(down, first, start, 0)
                up = lax.dynamic_update_slice_in_dim(up, second, start, 1)
            return [down, up]
        first = pairs[0][0] % chips
        stride = pairs[-1][0] % chips - first
        block = pl.BlockSpec(pairs[0][1].shape, lambda at, table: (0, 0))

        def place(at, table):
            return table[first + at * stride]

        def chip(at, table):
            return table[chips + first + at * stride]

        return pl.pallas_call(
            functools.partial(place_kernel, len(pairs), (units, size, extra)),
            grid_spec=pltpu.PrefetchScalarGridSpec(
                num_scalar_prefetch=1,
                grid=(len(pairs),),
                in_specs=[pl.BlockSpec(memory_space=pl.ANY)] * len(outputs)
                + [block] * (2 * len(pairs)),
                out_specs=[
                    pl.BlockSpec((units, model), lambda at, table: (place(at, table), 0)),
                    pl.BlockSpec((model, units), lambda at, table: (0, place(at, table))),
                    pl.BlockSpec((1, 2, size, model), lambda at, table: (chip(at, table), 0, 0, 0)),
                    pl.BlockSpec((2, 1, extra, model), lambda at, table: (0, chip(at, table), 0, 0)),
                    pl.BlockSpec(
                        (1, 2, small_rows, model), lambda at, table: (chip(at, table), 0, 0, 0)
                    ),
                ],
            ),
            out_shape=shapes
            + [
                struct((chips, 2, size, model), BF16),
                struct((2, chips, extra, model), F32),
                struct((chips, 2, small_rows, model), F32),
            ],
            input_output_aliases={1 + at: at for at in range(len(outputs))},
            compiler_params=streaming,
            cost_estimate=light,
            name="place",
        )(self.table, *outputs, *[pair[1] for pair in pairs], *[pair[2] for pair in pairs])


def place_kernel(count, sizes, table, *refs):
    blocks, (down, up, projections, weight, small) = refs[-5 - 2 * count : -5], refs[-5:]
    core = table[table.shape[0] - 2]
    units, size, extra = sizes
    rows = [pl.ds(0, units), pl.ds(units, size), pl.ds(units + size, extra)]
    rows.append(pl.ds(units + size + extra, small_rows))

    def put(first, second):
        down[...] = first[rows[0], :].astype(F32)
        up[...] = second[rows[0], :].astype(F32).T
        for side, block in ((0, first), (1, second)):
            projections[0, side] = block[rows[1], :]
            weight[side, 0] = block[rows[2], :].astype(F32)
            small[0, side] = block[rows[3], :].astype(F32)

    for at in range(count):
        near, far = blocks[at], blocks[count + at]
        here = pl.program_id(0) == at
        pl.when(here & (core == 0))(functools.partial(put, near, far))
        pl.when(here & (core != 0))(functools.partial(put, far, near))


def head_gradient_kernel(steps, chips, table, query_ref, key_value_ref, *refs):
    parts, out_ref = refs[:-1], refs[-1]
    patches = query_ref.shape[2]
    for at, part in enumerate(parts):

        @pl.when(pl.program_id(0) == at)
        def _(part=part):
            total = jnp.zeros(out_ref.shape, F32)
            for index, step in enumerate(steps):
                chip = table[chips + step % chips]
                grads = jnp.concatenate([query_ref[chip], key_value_ref[chip]], axis=0)
                total += product(grads, part[pl.ds(index * patches, patches), :])
            out_ref[...] = total.astype(BF16)


def head_gradient(dquery, key_value, parts, steps, table):
    chips, rows, _ = dquery.shape
    columns = parts[0].shape[1]

    def column(at, table):
        mine = table[2 * chips + 1] if len(parts) > 1 else 0
        return (0, jnp.where(at == 0, mine, 1 - mine))

    return pl.pallas_call(
        functools.partial(head_gradient_kernel, steps, chips),
        grid_spec=pltpu.PrefetchScalarGridSpec(
            num_scalar_prefetch=1,
            grid=(len(parts),),
            in_specs=[
                pl.BlockSpec(array.shape, lambda at, table, rank=array.ndim: (0,) * rank)
                for array in (dquery, key_value, *parts)
            ],
            out_specs=pl.BlockSpec((3 * rows, columns), column),
        ),
        out_shape=struct((3 * rows, columns * len(parts)), BF16),
        compiler_params=streaming,
        cost_estimate=light,
        name="head_gradient",
    )(table, dquery, key_value, *parts)


def layout_kernel(held, *outputs):
    pair = [jnp.concatenate([held[head, 0], held[head, 1]], axis=0) for head in range(2)]
    for index, output in enumerate(outputs):
        rows = [part[index * HD : index * HD + HD] for part in pair]
        output[...] = jnp.concatenate(rows, axis=0).astype(F32).T


def final_layout(held):
    count, _, size, model = held.shape
    return pl.pallas_call(
        layout_kernel,
        grid=(count // 2,),
        in_specs=[pl.BlockSpec((2, 2, size, model), lambda at: (at, 0, 0, 0))],
        out_specs=[pl.BlockSpec((model, 2 * HD), lambda at: (0, at))] * 3,
        out_shape=[struct((model, count * HD), F32)] * 3,
        compiler_params=streaming,
        cost_estimate=light,
        name="final_layout",
    )(held)


def core_half(values, axis, side):
    size = values.shape[axis] // 2
    return lax.dynamic_slice_in_dim(values, side * size, size, axis)


def share_halves(values, axis):
    core = lax.axis_index("core")
    return core_half(values, axis, core), swap_cores(core_half(values, axis, 1 - core))


def local(
    block_input,
    out_grad,
    segments,
    lead_steps,
    gain_attn,
    shift_attn,
    lead_weight,
    query_weight,
    key_weight,
    value_weight,
    output_weight,
    output_bias,
    gain_mlp,
    shift_mlp,
    up_weight,
    up_bias,
    down_weight,
    down_bias,
):
    rows, model = block_input.shape
    heads = query_weight.shape[1] // HD
    width = heads * HD
    chips, core = lax.axis_size("chip"), lax.axis_index("core")
    split = chips // heads
    crops = lead_steps.shape[0]
    table = ring_table()
    weights = (query_weight, key_weight, value_weight)
    cut = model // 2 if lax.axis_size("head") == 2 else model
    payload, attn_in, attn_in_cut = project(
        table, cut, block_input, segments, lead_steps, gain_attn, shift_attn, lead_weight, weights
    )
    if split == 1:
        own = to_heads(payload)
        queries = own
    else:
        queries = scatter_queries(payload.reshape(-1, rows), heads, split)
        own = to_heads(jnp.repeat(payload, split, axis=0))
    own, attn_in_cut = lax.optimization_barrier((own, attn_in_cut))
    inputs = Gather(attn_in_cut)
    inputs.send(inputs.ready)
    other = swap_cores(own)
    raw, out, logsum = attention_forward(queries, own, other, crops)
    out = visit([inputs], out)
    attn_out = gather_queries(out, heads, split, rows)
    attn_out = visit([inputs], attn_out)
    branches = across_heads(product(attn_out, output_weight, 0, 0).astype(BF16))
    keep, give, keep_in, give_in, hidden, dup_bias, mlp_part, d_mlp_part = mlp(
        table,
        block_input,
        out_grad,
        branches,
        output_bias,
        gain_mlp,
        shift_mlp,
        up_weight,
        up_bias,
        down_weight,
    )
    keep, give, keep_in, give_in, d_mlp_part = visit(
        [inputs], (keep, give, keep_in, give_in, d_mlp_part)
    )
    d_mlp = across_heads(d_mlp_part)
    ring = Reduce(keep, swap_cores(give), keep_in, swap_cores(give_in), table)
    mlp_part, d_mlp = lax.optimization_barrier((mlp_part, d_mlp))
    d_hidden, d_branch, d_attn, sums = middle(hidden, out_grad, d_mlp, gain_mlp, output_weight)
    grads = scatter_queries(d_attn, heads, split)
    d_branch, mlp_part = visit([ring, inputs], (d_branch, mlp_part))
    while inputs.busy():
        visit([inputs], ())
    mlp_out = across_heads(mlp_part)
    steps, inputs = zip(*inputs.blocks)
    parts = [join(inputs)]
    if cut != model:
        parts = across_heads(parts[0])
    out_near, out_far = share_halves(attn_out, 0)
    doutput = product(out_near, d_branch) + product(out_far, swap_cores(d_branch))
    doutput = to_heads(doutput.astype(BF16).reshape(chips, -1, model))
    grads = visit([ring], grads)
    *dquery, far_sums = backward_piece(
        queries, grads, raw, logsum, [], other, [], 0, 1, crops, (F32, BF16)
    )
    grads, dquery, far_sums = visit([ring], (grads, dquery, far_sums))
    far_sums = swap_cores(far_sums)
    *dquery, near_sums = backward_piece(
        queries, grads, raw, logsum, dquery, own, [], 0, 1, crops, (BF16, F32)
    )
    near_sums, dquery = ring.arrive((near_sums, dquery))
    (dquery,) = dquery
    key_value = (near_sums + far_sums.astype(F32)).astype(BF16)
    doutput, key_value = lax.optimization_barrier((doutput, key_value))
    doutput = jnp.sum(doutput.astype(F32), axis=0)
    small = jnp.concatenate([sums.reshape(-1), dup_bias[0]])
    small = jnp.pad(small, (0, small_rows * model - small.shape[0])).reshape(small_rows, model)
    doutput = jnp.concatenate([doutput, small], axis=0).astype(BF16)
    if split == 1:
        moved = to_heads(jnp.concatenate([dquery, key_value], axis=1))
        projections = head_gradient(dquery, key_value, parts, steps, table)
        near, far = share_halves(projections, 0)
        projections = (near.astype(F32) + far.astype(F32)).astype(BF16)
        size = projections.shape[0]
        blocks = jnp.concatenate([projections, doutput], axis=0)
        dquery, dkey, dvalue = (
            moved[:, at * HD : at * HD + HD].reshape(width, rows) for at in range(3)
        )
    else:
        dquery = gather_queries(dquery, heads, split, rows)
        moved = to_heads(key_value).reshape(heads, split, 2 * HD, rows).astype(F32)
        moved = jnp.sum(moved, axis=1).astype(BF16)
        dkey, dvalue = (moved[:, at * HD : at * HD + HD].reshape(width, rows) for at in range(2))
        size, blocks = 0, doutput
        projections = [
            lax.psum(product(attn_in, grad, 0, 1).astype(BF16), ("chip", "core")).astype(F32)
            for grad in (dquery, dkey, dvalue)
        ]
    total = ring.finish()
    start = total.shape[0]
    ring.size, ring.extra = size, blocks.shape[0] - size - small_rows
    gathered = Gather(jnp.concatenate([total, blocks], axis=0), True, ring.place)
    gathered.send(gathered.ready)
    d_part = (
        product(dquery, query_weight, 0, 1)
        + product(dkey, key_weight, 0, 1)
        + product(dvalue, value_weight, 0, 1)
    )
    d_part = visit([gathered], d_part)
    d_in = across_heads(d_part.astype(BF16))
    unit_attn, inverse_attn = normalize(block_input.astype(F32))
    onehot = (segments[:, None] == jnp.arange(crops, dtype=jnp.int32)[None, :]).astype(F32)
    lead = jnp.sum(onehot * lead_steps.astype(F32)[None, :], axis=1) / 12.0
    ends = jnp.stack(
        [
            jnp.sum(d_part * unit_attn, axis=0),
            jnp.sum(d_part, axis=0),
            jnp.sum(lead[:, None] * d_part, axis=0),
        ]
    )
    ends = jnp.pad(ends.reshape(-1, 128), ((0, -ends.size // 128 % 16), (0, 0))).astype(BF16)
    everyone = ("chip", "core", "head")
    ends = jnp.broadcast_to(ends, (lax.axis_size(everyone),) + ends.shape)
    ends = lax.all_to_all(ends, everyone, 0, 0, tiled=True)
    visit([gathered], ())
    d_in, mlp_out = visit([gathered], (d_in, mlp_out))
    block_output = hidden + down_bias
    for part in mlp_out:
        block_output += part.astype(F32)
    block_output = block_output.astype(BF16)
    d_in = functools.reduce(jnp.add, (part.astype(F32) for part in d_in))
    input_grad = (d_hidden + normalize_back(d_in * gain_attn, unit_attn, inverse_attn)).astype(
        BF16
    )
    while gathered.busy():
        visit([gathered], ())
    ddown_weight, dup_weight, *rest = gathered.outputs
    ends = jnp.sum(ends.astype(F32), axis=0).reshape(-1)[: 3 * model].reshape(3, model)
    if split == 1:
        held, doutput_weight, small = rest
        projections = final_layout(held)
        doutput_weight = doutput_weight.reshape(width, model)
    if split != 1:
        blocks = jnp.zeros((2, chips) + blocks.shape, F32)
        for step, near, far in gathered.pairs:
            for side, block in ((core, near[start:]), (1 - core, far[start:])):
                at = (side, table[chips + step % chips], 0, 0)
                block = block[None, None].astype(F32)
                blocks = lax.dynamic_update_slice(blocks, block, at)
        doutput_weight = blocks[:, :, :-small_rows].reshape(width, model)
        small = blocks[:, :, -small_rows:]
    small = jnp.sum(small, axis=(0, 1))
    dup_bias = small[4:].reshape(-1)[: dup_bias.shape[1]]
    return (
        block_output,
        input_grad,
        ends[0],
        ends[1],
        ends[2],
        *projections,
        doutput_weight,
        *small[:3],
        dup_weight,
        dup_bias,
        ddown_weight,
        small[3],
    )


def solution(mesh):
    bands, halves = mesh.shape["band"], mesh.shape["head"]
    inner = Mesh(mesh.devices.reshape(bands // 2, 2, halves), ("chip", "core", "head"))
    band = ("chip", "core")
    rows, columns, split_rows = P(band, None), P(None, "head"), P("head", None)
    return jax.shard_map(
        local,
        mesh=inner,
        in_specs=(
            rows,
            rows,
            P(band),
            P(),
            P(),
            P(),
            P(),
            columns,
            columns,
            columns,
            split_rows,
            P(),
            P(),
            P(),
            columns,
            P("head"),
            split_rows,
            P(),
        ),
        out_specs=(
            rows,
            rows,
            P(),
            P(),
            P(),
            columns,
            columns,
            columns,
            split_rows,
            P(),
            P(),
            P(),
            columns,
            P("head"),
            split_rows,
            P(),
        ),
        check_vma=False,
    )
```

```python
import functools
import math

import jax
import jax.numpy as jnp
from jax import lax
from jax.experimental import pallas as pl
from jax.experimental.pallas import tpu as pltpu
from jax.sharding import Mesh, PartitionSpec as P

HD = 64
F32 = jnp.float32
BF16 = jnp.bfloat16
eps = 1e-05
masked_value = -1e30
seg_row = 3 * HD
payload_rows = 3 * HD + 16
small_rows = 16
params = pltpu.CompilerParams(vmem_limit_bytes=48 * 2**20)
streaming = pltpu.CompilerParams(vmem_limit_bytes=60 * 2**20)


def normalize(values):
    centred = values - jnp.mean(values, axis=-1, keepdims=True)
    inverse = lax.rsqrt(jnp.mean(centred * centred, axis=-1, keepdims=True) + eps)
    return (centred * inverse, inverse)


def normalize_back(grad_unit, unit, inverse):
    return inverse * (
        grad_unit
        - jnp.mean(grad_unit, axis=-1, keepdims=True)
        - unit * jnp.mean(grad_unit * unit, axis=-1, keepdims=True)
    )


def product(first, second, first_axis=1, second_axis=0):
    return lax.dot_general(
        first,
        second,
        (((first_axis,), (second_axis,)), ((), ())),
        preferred_element_type=jnp.float32,
    )


def struct(shape, dtype):
    return jax.ShapeDtypeStruct(shape, dtype)


def whole_spec(shape):
    return pl.BlockSpec(shape, lambda *at: (0,) * len(shape))


light = pl.CostEstimate(flops=1, bytes_accessed=1, transcendentals=0)


def project_kernel(
    table, input_ref, segment_ref, steps_ref, gain, shift, lead_weight, *refs
):
    weights, (payload_ref, attn_in_ref, cut_ref) = refs[:3], refs[3:]
    rows = input_ref.shape[0]

    @pl.when(pl.program_id(0) == 0)
    def _():
        unit, _ = normalize(input_ref[...].astype(F32))
        crops = steps_ref.shape[0]
        crop = lax.broadcasted_iota(jnp.int32, (crops, rows), 0)
        steps = jnp.zeros((crops, rows), jnp.int32)
        for at in range(crops):
            steps = jnp.where(crop == at, steps_ref[at], steps)
        steps = jnp.where(crop == segment_ref[...], steps, 0).astype(F32)
        lead = product(steps, jnp.ones((crops, 128), F32), 0, 0)[:, :1] / 12.0
        attn_in = unit * gain[...] + shift[...] + lead * lead_weight[...]
        attn_in = attn_in.astype(BF16)
        attn_in_ref[...] = attn_in
        columns = cut_ref.shape[1]
        first = table[table.shape[0] - 1] % (attn_in.shape[1] // columns) == 0
        cut_ref[...] = jnp.where(first, attn_in[:, :columns], attn_in[:, -columns:])

    for at, weight in enumerate(weights):
        part = product(attn_in_ref[...], weight[...]).T.astype(BF16)
        for head in range(2):
            payload_ref[head, pl.ds(at * HD, HD), :] = part[head * HD : head * HD + HD]
    segment = jnp.broadcast_to(segment_ref[...].astype(F32), (16, rows)).astype(BF16)
    for head in range(2):
        payload_ref[head, pl.ds(seg_row, 16), :] = segment


def project(table, cut, block_input, segments, lead_steps, gain, shift, lead_weight, weights):
    rows, model = block_input.shape
    heads = weights[0].shape[1] // HD
    line = whole_spec((1, model))
    column = pl.BlockSpec((model, 2 * HD), lambda at, table: (0, at))
    return pl.pallas_call(
        project_kernel,
        grid_spec=pltpu.PrefetchScalarGridSpec(
            num_scalar_prefetch=1,
            grid=(heads // 2,),
            in_specs=[
                whole_spec(block_input.shape),
                whole_spec((1, rows)),
                pl.BlockSpec(memory_space=pltpu.SMEM),
            ]
            + [line] * 3
            + [column] * 3,
            out_specs=[
                pl.BlockSpec((2, payload_rows, rows), lambda at, table: (at, 0, 0)),
                whole_spec((rows, model)),
                whole_spec((rows, cut)),
            ],
        ),
        out_shape=[
            struct((heads, payload_rows, rows), BF16),
            struct((rows, model), BF16),
            struct((rows, cut), BF16),
        ],
        compiler_params=streaming,
        cost_estimate=light,
        name="project",
    )(table, block_input, segments[None], lead_steps, gain[None], shift[None], lead_weight[None], *weights)


def mlp_kernel(count, core_ref, input_ref, grad_ref, *refs):
    branches, refs = refs[:count], refs[count:]
    output_bias, gain, shift, up_weight, up_bias, down_weight = refs[:6]
    keep_ref, give_ref, keep_in_ref, give_in_ref, hidden_ref, bias_ref, forward_ref, back_ref = refs[
        6:14
    ]
    mlp_in_ref, forward, back = refs[14:]
    at = pl.program_id(0)
    is_down = core_ref[core_ref.shape[0] - 2] == 0

    @pl.when(at == 0)
    def _():
        hidden = input_ref[...].astype(F32) + output_bias[...]
        for branch in branches:
            hidden += branch[...].astype(F32)
        hidden_ref[...] = hidden
        unit, _ = normalize(hidden)
        mlp_in = (unit * gain[...] + shift[...]).astype(BF16)
        mlp_in_ref[...] = mlp_in
        keep_in_ref[...] = jnp.where(is_down, grad_ref[...], mlp_in)
        give_in_ref[...] = jnp.where(is_down, mlp_in, grad_ref[...])
        forward[...] = jnp.zeros_like(forward)
        back[...] = jnp.zeros_like(back)

    upper = product(mlp_in_ref[...], up_weight[...]) + up_bias[...]
    share = 0.5 + 0.5 * lax.erf(upper * math.sqrt(0.5))
    slope = share + upper * (jnp.exp(upper * upper * -0.5) * (1.0 / math.sqrt(2.0 * math.pi)))
    active = (upper * share).astype(BF16)
    d_active = product(grad_ref[...], down_weight[...], 1, 1)
    d_upper = (d_active * slope).astype(BF16)
    keep_ref[...] = jnp.where(is_down, active, d_upper)
    give_ref[...] = jnp.where(is_down, d_upper, active)
    bias_ref[...] = jnp.sum(d_upper.astype(F32), axis=0, keepdims=True)
    forward[...] += product(active, down_weight[...])
    back[...] += product(d_upper, up_weight[...], 1, 1)

    @pl.when(at == pl.num_programs(0) - 1)
    def _():
        forward_ref[...] = forward[...].astype(BF16)
        back_ref[...] = back[...].astype(BF16)


def mlp(
    table, block_input, out_grad, branches, output_bias, gain, shift, up_weight, up_bias, down_weight
):
    rows, model = block_input.shape
    units = up_weight.shape[1]
    step = math.gcd(units, 512)
    tile, line = whole_spec((rows, model)), whole_spec((1, model))
    wide = pl.BlockSpec((rows, step), lambda at, table: (0, at))
    bias = pl.BlockSpec((1, step), lambda at, table: (0, at))
    return pl.pallas_call(
        functools.partial(mlp_kernel, len(branches)),
        grid_spec=pltpu.PrefetchScalarGridSpec(
            num_scalar_prefetch=1,
            grid=(units // step,),
            in_specs=[tile] * (2 + len(branches))
            + [line] * 3
            + [
                pl.BlockSpec((model, step), lambda at, table: (0, at)),
                bias,
                pl.BlockSpec((step, model), lambda at, table: (at, 0)),
            ],
            out_specs=[wide, wide, tile, tile, tile, bias, tile, tile],
            scratch_shapes=[pltpu.VMEM((rows, model), BF16)]
            + [pltpu.VMEM((rows, model), F32)] * 2,
        ),
        out_shape=[struct((rows, units), BF16)] * 2
        + [struct((rows, model), BF16)] * 2
        + [
            struct((rows, model), F32),
            struct((1, units), F32),
            struct((rows, model), BF16),
            struct((rows, model), BF16),
        ],
        compiler_params=streaming,
        cost_estimate=light,
        name="mlp",
    )(
        table,
        block_input,
        out_grad,
        *branches,
        output_bias[None],
        gain[None],
        shift[None],
        up_weight,
        up_bias[None],
        down_weight,
    )


def middle_kernel(count, hidden_ref, grad_ref, *refs):
    parts, refs = refs[:count], refs[count:]
    gain, output_weight, d_hidden_ref, d_branch_ref, d_attn_ref, sums_ref = refs
    unit, inverse = normalize(hidden_ref[...])
    d_mlp = parts[0][...].astype(F32)
    for part in parts[1:]:
        d_mlp += part[...].astype(F32)
    grad = grad_ref[...].astype(F32)
    d_hidden = grad + normalize_back(d_mlp * gain[...], unit, inverse)
    d_hidden_ref[...] = d_hidden
    d_branch = d_hidden.astype(BF16)
    d_branch_ref[...] = d_branch
    d_attn_ref[...] = product(output_weight[...], d_branch, 1, 1).astype(BF16)
    for at, values in enumerate((d_hidden, d_mlp * unit, d_mlp, grad)):
        sums_ref[pl.ds(at, 1), :] = jnp.sum(values, axis=0, keepdims=True)


def middle(hidden, out_grad, parts, gain, output_weight):
    rows, model = hidden.shape
    width = output_weight.shape[0]
    return pl.pallas_call(
        functools.partial(middle_kernel, len(parts)),
        out_shape=[
            struct((rows, model), F32),
            struct((rows, model), BF16),
            struct((width, rows), BF16),
            struct((4, model), F32),
        ],
        compiler_params=streaming,
        cost_estimate=light,
        name="middle",
    )(hidden, out_grad, *parts, gain[None], output_weight)


def mask_rows(piece, chip, crops):
    crop = lax.broadcasted_iota(jnp.int32, (HD, piece.shape[2]), 0)
    segment = piece[chip, pl.ds(seg_row, 16), :].astype(F32)[:1].astype(jnp.int32)
    return jnp.where((crop != segment) & (crop < crops), masked_value, 0.0)


def load_keys(piece, crops, keys, key_t, value_n):
    chips, _, patches = piece.shape
    for chip in range(chips):
        key = piece[chip, pl.ds(HD, HD), :]
        value = piece[chip, pl.ds(2 * HD, HD), :]
        place = pl.ds(chip * patches, patches)
        both = jnp.concatenate([key.astype(F32), mask_rows(piece, chip, crops)], axis=0)
        keys[place, :] = both.T.astype(BF16)
        key_t[:, place] = key
        value_n[place, :] = value.astype(F32).T.astype(BF16)


def masked_query(query_ref, dtype=BF16):
    query = query_ref[0, pl.ds(0, HD), :].astype(F32) * 0.125
    segment = query_ref[0, pl.ds(seg_row, 16), :].astype(F32)[:1].astype(jnp.int32)
    crop = lax.broadcasted_iota(jnp.int32, query.shape, 0)
    onehot = jnp.where(crop == segment, 1.0, 0.0)
    return jnp.concatenate([query, onehot], axis=0).astype(dtype)


def forward_kernel(
    crops, step, query_ref, own, other, raw_ref, out_ref, logsum_ref, key_t, value_n, scores
):
    @pl.when(pl.program_id(0) == 0)
    def _():
        start = 0
        for piece in (own, other):
            chips, _, patches = piece.shape
            for chip in range(chips):
                place = pl.ds(start, patches)
                key = piece[chip, pl.ds(HD, HD), :].astype(F32)
                key_t[:, place] = jnp.concatenate([key, mask_rows(piece, chip, crops)], axis=0).astype(BF16)
                value = piece[chip, pl.ds(2 * HD, HD), :].astype(F32)
                value = jnp.concatenate([value, jnp.ones_like(value)], axis=0)
                value_n[place, :] = value.T.astype(BF16)
                start += patches

    query = masked_query(query_ref, F32).T.astype(BF16)
    count = query.shape[0]
    top = jnp.full((count, 128), masked_value, F32)
    for start in range(0, key_t.shape[1], step):
        block = product(query, key_t[:, pl.ds(start, step)])
        scores[:, pl.ds(start, step)] = block
        for at in range(0, step, 128):
            top = jnp.maximum(top, block[:, at : at + 128])
    top = jnp.max(top, axis=1, keepdims=True)
    accum = jnp.zeros((count, 2 * HD), F32)
    for start in range(0, key_t.shape[1], step):
        weights = jnp.exp(scores[:, pl.ds(start, step)] - top).astype(BF16)
        accum += product(weights, value_n[pl.ds(start, step), :])
    accum = accum.T
    total = accum[HD : HD + 1]
    raw = accum[:HD] / total
    raw_ref[0] = raw
    out_ref[0] = raw.astype(BF16)
    top = jnp.broadcast_to(top, (count, 128)).T[:1]
    logsum_ref[0] = top + jnp.log(total)


def backward_kernel(
    crops,
    before,
    query_ref,
    grad_ref,
    raw_ref,
    logsum_ref,
    *refs,
):
    before_refs, refs = refs[:before], refs[before:]
    piece, (dquery_ref, sums_ref, keys, key_t, value_n, sums) = refs[0], refs[-6:]
    group = pl.program_id(0)

    @pl.when(group == 0)
    def _():
        load_keys(piece, crops, keys, key_t, value_n)
        sums[...] = jnp.zeros_like(sums)

    query = masked_query(query_ref)
    grad = grad_ref[0]
    grad_wide = grad.astype(F32)
    delta = jnp.sum(grad_wide * raw_ref[0], axis=0, keepdims=True)
    scaled = query_ref[0, pl.ds(0, HD), :].astype(F32) * 0.125
    zero = jnp.zeros_like(scaled)
    query_side = jnp.concatenate([scaled, zero], axis=0).T.astype(BF16)
    grad_side = jnp.concatenate([zero, grad_wide], axis=0).T.astype(BF16)
    probs = jnp.exp(product(keys[...], query) - logsum_ref[0])
    dprobs = product(value_n[...], grad)
    dscores = (probs * (dprobs - delta)).astype(BF16)
    sums[...] += product(dscores, query_side) + product(probs.astype(BF16), grad_side)
    dquery = product(key_t[...], dscores) * 0.125
    for ref in before_refs:
        dquery = ref[0] + dquery
    dquery_ref[0] = dquery.astype(dquery_ref.dtype)

    @pl.when(group == pl.num_programs(0) - 1)
    def _():
        chips, _, patches = sums_ref.shape
        for chip in range(chips):
            sums_ref[chip] = sums[pl.ds(chip * patches, patches), :].T.astype(sums_ref.dtype)


def key_step(count):
    return 1024 if count % 1024 == 0 else 256


def query_spec(rows, patches):
    return pl.BlockSpec((1, rows, patches), lambda group: (group, 0, 0))


def attention_forward(queries, own, other, crops):
    groups, _, patches = queries.shape
    count = 2 * own.shape[0] * own.shape[2]
    return pl.pallas_call(
        functools.partial(forward_kernel, crops, key_step(count)),
        grid=(groups,),
        in_specs=[
            query_spec(payload_rows, patches),
            whole_spec(own.shape),
            whole_spec(other.shape),
        ],
        out_specs=[query_spec(HD, patches), query_spec(HD, patches), query_spec(1, patches)],
        out_shape=[
            struct((groups, HD, patches), F32),
            struct((groups, HD, patches), BF16),
            struct((groups, 1, patches), F32),
        ],
        scratch_shapes=[
            pltpu.VMEM((2 * HD, count), BF16),
            pltpu.VMEM((count, 2 * HD), BF16),
            pltpu.VMEM((patches, count), F32),
        ],
        compiler_params=streaming,
        cost_estimate=light,
        name="attention_forward",
    )(queries, own, other)


def backward_piece(queries, grads, raw, logsum, before, keys, earlier, index, pieces, crops, dtypes):
    groups, _, patches = queries.shape
    chips = keys.shape[0] // pieces
    count = chips * keys.shape[2]
    sums_shape = (chips, 2 * HD, keys.shape[2])
    return pl.pallas_call(
        functools.partial(backward_kernel, crops, len(before)),
        grid=(groups,),
        in_specs=[
            query_spec(payload_rows, patches),
            query_spec(HD, patches),
            query_spec(HD, patches),
            query_spec(1, patches),
        ]
        + [query_spec(HD, patches)] * len(before)
        + [pl.BlockSpec((chips,) + keys.shape[1:], lambda group: (index, 0, 0))]
        + [pl.BlockSpec(memory_space=pl.ANY)] * len(earlier),
        out_specs=[
            query_spec(HD, patches),
            pl.BlockSpec(sums_shape, lambda group: (index, 0, 0)),
        ],
        out_shape=[
            struct((groups, HD, patches), dtypes[0]),
            struct((keys.shape[0],) + sums_shape[1:], dtypes[1]),
        ],
        input_output_aliases={5 + len(before): 1} if earlier else {},
        scratch_shapes=[
            pltpu.VMEM((count, 2 * HD), BF16),
            pltpu.VMEM((HD, count), BF16),
            pltpu.VMEM((count, HD), BF16),
            pltpu.VMEM((count, 2 * HD), F32),
        ],
        compiler_params=params,
        cost_estimate=light,
        name="attention_backward",
    )(queries, grads, raw, logsum, *before, keys, *earlier)


def swap_cores(values):
    return lax.ppermute(values, "core", [(0, 1), (1, 0)])


def to_heads(blocks):
    return lax.all_to_all(blocks, "chip", 0, 0, tiled=True)


def scatter_queries(values, heads, split):
    rows, patches = values.shape[0] // heads, values.shape[1]
    if split == 1:
        return to_heads(values.reshape(heads, rows, patches))
    part = patches // split
    blocks = values.reshape(heads, rows, split, part).transpose(0, 2, 1, 3)
    moved = to_heads(blocks.reshape(heads * split, rows, part))
    width = min(256, moved.shape[0] * part)
    joined = moved.transpose(1, 0, 2).reshape(rows, -1, width)
    return joined.transpose(1, 0, 2)


def gather_queries(values, heads, split, patches):
    rows = values.shape[1]
    if split == 1:
        return to_heads(values).reshape(heads * rows, patches)
    part = patches // split
    joined = values.transpose(1, 0, 2).reshape(rows, heads * split, part)
    moved = to_heads(joined.transpose(1, 0, 2)).reshape(heads, split, rows, part)
    return moved.transpose(0, 2, 1, 3).reshape(heads * rows, patches)


def across_heads(part):
    if lax.axis_size("head") == 2:
        return [part, lax.ppermute(part, "head", [(0, 1), (1, 0)])]
    return [lax.psum(part, "head")]


def ring_pairs(direction):
    chips = lax.axis_size("chip")
    order = list(range(0, chips, 2)) + list(range(chips - 1, 0, -2))
    return [(order[at], order[(at + direction) % chips]) for at in range(chips)]


def ring_table():
    chips, chip = lax.axis_size("chip"), lax.axis_index("chip")
    place = jnp.where(chip % 2 == 0, chip // 2, chips - 1 - chip // 2)
    steps = jnp.arange(2 * chips + 2, dtype=jnp.int32)
    places = (place + steps) % chips
    there = jnp.where(places < chips // 2, 2 * places, 2 * (chips - 1 - places) + 1)
    table = jnp.where(steps < chips, places, there)
    table = jnp.where(steps == 2 * chips, lax.axis_index("core"), table)
    return jnp.where(steps == 2 * chips + 1, lax.axis_index("head"), table).astype(jnp.int32)


def visit(streams, values):
    states, values = lax.optimization_barrier(([stream.state for stream in streams], values))
    for stream, state in zip(streams, states):
        stream.advance(state)
    ready, values = lax.optimization_barrier(([stream.ready for stream in streams], values))
    for stream, blocks in zip(streams, ready):
        stream.send(blocks)
    return values


def join_kernel(*refs):
    start = 0
    for block in refs[:-1]:
        refs[-1][pl.ds(start, block.shape[0]), :] = block[...]
        start += block.shape[0]


def join(blocks):
    rows = sum(block.shape[0] for block in blocks)
    return pl.pallas_call(
        join_kernel,
        out_shape=struct((rows, blocks[0].shape[1]), blocks[0].dtype),
        compiler_params=streaming,
        name="join",
    )(*blocks)


def halves_kernel(left, right, left_ref, right_ref):
    left_ref[...] = left[...]
    right_ref[...] = right[...]


def halves(left, right):
    rows, columns = left.shape
    if rows % 16 or columns % 256:
        return [left[:, : columns // 2], right[:, columns // 2 :]]
    out = pl.BlockSpec((rows, columns // 2), lambda at: (0, 0))
    return pl.pallas_call(
        halves_kernel,
        grid=(1,),
        in_specs=[out, pl.BlockSpec((rows, columns // 2), lambda at: (0, 1))],
        out_specs=[out, out],
        out_shape=[struct((rows, columns // 2), left.dtype)] * 2,
        compiler_params=streaming,
        name="halves",
    )(left, right)


class Gather:
    def __init__(self, block, swap=False, take=None):
        self.reach, self.swap, self.take = lax.axis_size("chip") // 2, swap, take
        self.blocks, self.pairs, self.count = [], [], 0
        self.new, self.outputs = [0], []
        self.ready = [block]

    def send(self, ready):
        new = list(zip(self.new, ready))
        self.blocks += new
        self.new = new
        self.count += 1
        sides = ready if len(ready) > 1 else ready * 2
        if self.count == self.reach:
            sides = halves(*sides)
        flying = []
        if self.count <= self.reach:
            flying = [
                lax.ppermute(block, "chip", ring_pairs(direction))
                for block, direction in zip(sides, (1, -1))
            ]
        if self.swap and ready:
            pairs = [(step, block, swap_cores(block)) for step, block in new]
            self.pairs += pairs
            self.outputs = self.take(self.outputs, pairs)
        self.state = (flying, self.outputs)

    def advance(self, state):
        arrived, self.outputs = state
        self.new = [-self.count, self.count]
        if arrived and self.count == self.reach:
            arrived, self.new = [jnp.concatenate(arrived, axis=1)], [self.count]
        self.ready = arrived

    def busy(self):
        return bool(self.state[0])


def add_kernel(wanted, count, _, *refs):
    outputs, refs = refs[-count:], list(refs[:-count])
    keep_in, far_in = refs.pop(0), refs.pop(0)
    for starts, output in zip(wanted, outputs):
        near, far = refs.pop(0), refs.pop(0)
        total = product(near[...], keep_in[...], 0, 0) + product(far[...], far_in[...], 0, 0)
        if len(outputs) > len(wanted):
            for at, output in enumerate(outputs):
                columns = output.shape[1]
                output[...] = total[:, at * columns : at * columns + columns].astype(BF16)
            return
        output[...] = total.astype(BF16)
        arrived = [refs.pop(0) for _ in starts]
        for start in sorted(set(starts)):
            parts = [part for part, at in zip(arrived, starts) if at == start]
            columns = slice(start, start + parts[0].shape[1])
            summed = total[:, columns]
            for part in parts:
                summed += part[...].astype(F32)
            output[:, columns] = summed.astype(BF16)


class Reduce:
    def __init__(self, keep, far, keep_in, far_in, table):
        self.chips, self.table = lax.axis_size("chip"), table
        self.operands, self.sides = (keep, far), (keep_in, far_in)
        self.units = keep.shape[1] // self.chips
        self.tiled = self.units % 128 == 0
        self.left, self.rest = self.chips // 2, None
        blocks = self.add([(self.left, [])], True)
        self.send(blocks if len(blocks) > 1 else halves(blocks[0], blocks[0]))

    def send(self, ready):
        self.left -= 1
        self.state = [
            lax.ppermute(block, "chip", ring_pairs(direction))
            for block, direction in zip(ready, (1, -1))
        ]

    def advance(self, state):
        half = self.sides[0].shape[1] // 2
        ahead, behind = state
        first = 0 if ahead.shape[1] != half else half
        self.ready = self.add([(self.left, [(ahead, 0)]), (-self.left, [(behind, first)])])

    def arrive(self, values):
        self.state, values = lax.optimization_barrier((self.state, values))
        return values

    def finish(self):
        ahead, behind = self.state
        return self.add([(0, [(ahead, 0), (behind, 0)])])[0]

    def add(self, wanted, split=False):
        (rows, model), units, chips = self.sides[0].shape, self.units, self.chips
        if not self.tiled:
            sums = []
            for step, parts in wanted:
                start = self.table[step % chips] * units
                total = jnp.zeros((units, model), F32)
                for operand, side in zip(self.operands, self.sides):
                    block = lax.dynamic_slice_in_dim(operand, start, units, 1)
                    total += product(block, side, 0, 0)
                for part, start in parts:
                    total = total.at[:, start : start + part.shape[1]].add(part.astype(F32))
                sums.append(total.astype(BF16))
            return sums
        side = pl.BlockSpec((rows, model), lambda at, table: (0, 0))
        whole = pl.BlockSpec((units, model), lambda at, table: (0, 0))
        specs, arrays = [side] * 2, list(self.sides)
        for step, parts in wanted:
            block = pl.BlockSpec(
                (rows, units), lambda at, table, step=step % chips: (0, table[step])
            )
            specs += [block] * 2
            specs += [pl.BlockSpec(part.shape, lambda at, table: (0, 0)) for part, _ in parts]
            arrays += list(self.operands) + [part for part, _ in parts]
        starts = [[start for _, start in parts] for _, parts in wanted]
        shapes = [struct((units, model), BF16)] * len(wanted)
        if split:
            shapes = [struct((units, model // 2), BF16)] * 2
        return pl.pallas_call(
            functools.partial(add_kernel, starts, len(shapes)),
            grid_spec=pltpu.PrefetchScalarGridSpec(
                num_scalar_prefetch=1,
                grid=(1,),
                in_specs=specs,
                out_specs=[pl.BlockSpec(shape.shape, lambda at, table: (0, 0)) for shape in shapes],
            ),
            out_shape=shapes,
            compiler_params=streaming,
            cost_estimate=light,
            name="ring_add",
        )(self.table, *arrays)

    def place(self, outputs, pairs):
        units, chips, model = self.units, self.chips, self.sides[0].shape[1]
        size, extra = self.size, self.extra
        shapes = [struct((chips * units, model), F32), struct((model, chips * units), F32)]
        if not self.tiled:
            outputs = outputs or [jnp.zeros(shape.shape, F32) for shape in shapes]
            down, up = outputs
            is_down = self.table[2 * chips] == 0
            for step, near, far in pairs:
                start = self.table[step % chips] * units
                near, far = near[:units], far[:units]
                first = jnp.where(is_down, near, far).astype(F32)
                second = jnp.where(is_down, far, near).astype(F32).T
                down = lax.dynamic_update_slice_in_dim(down, first, start, 0)
                up = lax.dynamic_update_slice_in_dim(up, second, start, 1)
            return [down, up]
        first = pairs[0][0] % chips
        stride = pairs[-1][0] % chips - first
        block = pl.BlockSpec(pairs[0][1].shape, lambda at, table: (0, 0))

        def place(at, table):
            return table[first + at * stride]

        def chip(at, table):
            return table[chips + first + at * stride]

        return pl.pallas_call(
            functools.partial(place_kernel, len(pairs), (units, size, extra)),
            grid_spec=pltpu.PrefetchScalarGridSpec(
                num_scalar_prefetch=1,
                grid=(len(pairs),),
                in_specs=[pl.BlockSpec(memory_space=pl.ANY)] * len(outputs)
                + [block] * (2 * len(pairs)),
                out_specs=[
                    pl.BlockSpec((units, model), lambda at, table: (place(at, table), 0)),
                    pl.BlockSpec((model, units), lambda at, table: (0, place(at, table))),
                    pl.BlockSpec((1, 2, size, model), lambda at, table: (chip(at, table), 0, 0, 0)),
                    pl.BlockSpec((2, 1, extra, model), lambda at, table: (0, chip(at, table), 0, 0)),
                    pl.BlockSpec(
                        (1, 2, small_rows, model), lambda at, table: (chip(at, table), 0, 0, 0)
                    ),
                ],
            ),
            out_shape=shapes
            + [
                struct((chips, 2, size, model), BF16),
                struct((2, chips, extra, model), F32),
                struct((chips, 2, small_rows, model), F32),
            ],
            input_output_aliases={1 + at: at for at in range(len(outputs))},
            compiler_params=streaming,
            cost_estimate=light,
            name="place",
        )(self.table, *outputs, *[pair[1] for pair in pairs], *[pair[2] for pair in pairs])


def place_kernel(count, sizes, table, *refs):
    blocks, (down, up, projections, weight, small) = refs[-5 - 2 * count : -5], refs[-5:]
    core = table[table.shape[0] - 2]
    units, size, extra = sizes
    rows = [pl.ds(0, units), pl.ds(units, size), pl.ds(units + size, extra)]
    rows.append(pl.ds(units + size + extra, small_rows))

    def put(first, second):
        down[...] = first[rows[0], :].astype(F32)
        up[...] = second[rows[0], :].astype(F32).T
        for side, block in ((0, first), (1, second)):
            projections[0, side] = block[rows[1], :]
            weight[side, 0] = block[rows[2], :].astype(F32)
            small[0, side] = block[rows[3], :].astype(F32)

    for at in range(count):
        near, far = blocks[at], blocks[count + at]
        here = pl.program_id(0) == at
        pl.when(here & (core == 0))(functools.partial(put, near, far))
        pl.when(here & (core != 0))(functools.partial(put, far, near))


def head_gradient_kernel(steps, chips, table, query_ref, key_value_ref, *refs):
    parts, out_ref = refs[:-1], refs[-1]
    patches = query_ref.shape[2]
    for at, part in enumerate(parts):

        @pl.when(pl.program_id(0) == at)
        def _(part=part):
            total = jnp.zeros(out_ref.shape, F32)
            for index, step in enumerate(steps):
                chip = table[chips + step % chips]
                grads = jnp.concatenate([query_ref[chip], key_value_ref[chip]], axis=0)
                total += product(grads, part[pl.ds(index * patches, patches), :])
            out_ref[...] = total.astype(BF16)


def head_gradient(dquery, key_value, parts, steps, table):
    chips, rows, _ = dquery.shape
    columns = parts[0].shape[1]

    def column(at, table):
        mine = table[2 * chips + 1] if len(parts) > 1 else 0
        return (0, jnp.where(at == 0, mine, 1 - mine))

    return pl.pallas_call(
        functools.partial(head_gradient_kernel, steps, chips),
        grid_spec=pltpu.PrefetchScalarGridSpec(
            num_scalar_prefetch=1,
            grid=(len(parts),),
            in_specs=[
                pl.BlockSpec(array.shape, lambda at, table, rank=array.ndim: (0,) * rank)
                for array in (dquery, key_value, *parts)
            ],
            out_specs=pl.BlockSpec((3 * rows, columns), column),
        ),
        out_shape=struct((3 * rows, columns * len(parts)), BF16),
        compiler_params=streaming,
        cost_estimate=light,
        name="head_gradient",
    )(table, dquery, key_value, *parts)


def layout_kernel(held, *outputs):
    pair = [jnp.concatenate([held[head, 0], held[head, 1]], axis=0) for head in range(2)]
    for index, output in enumerate(outputs):
        rows = [part[index * HD : index * HD + HD] for part in pair]
        output[...] = jnp.concatenate(rows, axis=0).astype(F32).T


def final_layout(held):
    count, _, size, model = held.shape
    return pl.pallas_call(
        layout_kernel,
        grid=(count // 2,),
        in_specs=[pl.BlockSpec((2, 2, size, model), lambda at: (at, 0, 0, 0))],
        out_specs=[pl.BlockSpec((model, 2 * HD), lambda at: (0, at))] * 3,
        out_shape=[struct((model, count * HD), F32)] * 3,
        compiler_params=streaming,
        cost_estimate=light,
        name="final_layout",
    )(held)


def core_half(values, axis, side):
    size = values.shape[axis] // 2
    return lax.dynamic_slice_in_dim(values, side * size, size, axis)


def share_halves(values, axis):
    core = lax.axis_index("core")
    return core_half(values, axis, core), swap_cores(core_half(values, axis, 1 - core))


def local(
    block_input,
    out_grad,
    segments,
    lead_steps,
    gain_attn,
    shift_attn,
    lead_weight,
    query_weight,
    key_weight,
    value_weight,
    output_weight,
    output_bias,
    gain_mlp,
    shift_mlp,
    up_weight,
    up_bias,
    down_weight,
    down_bias,
):
    rows, model = block_input.shape
    heads = query_weight.shape[1] // HD
    width = heads * HD
    chips, core = lax.axis_size("chip"), lax.axis_index("core")
    split = chips // heads
    crops = lead_steps.shape[0]
    table = ring_table()
    weights = (query_weight, key_weight, value_weight)
    cut = model // 2 if lax.axis_size("head") == 2 else model
    payload, attn_in, attn_in_cut = project(
        table, cut, block_input, segments, lead_steps, gain_attn, shift_attn, lead_weight, weights
    )
    if split == 1:
        own = to_heads(payload)
        queries = own
    else:
        queries = scatter_queries(payload.reshape(-1, rows), heads, split)
        own = to_heads(jnp.repeat(payload, split, axis=0))
    own, attn_in_cut = lax.optimization_barrier((own, attn_in_cut))
    inputs = Gather(attn_in_cut)
    inputs.send(inputs.ready)
    other = swap_cores(own)
    raw, out, logsum = attention_forward(queries, own, other, crops)
    attn_out = gather_queries(out, heads, split, rows)
    attn_out = visit([inputs], attn_out)
    visit([inputs], ())
    branches = across_heads(product(attn_out, output_weight, 0, 0).astype(BF16))
    keep, give, keep_in, give_in, hidden, dup_bias, mlp_part, d_mlp_part = mlp(
        table,
        block_input,
        out_grad,
        branches,
        output_bias,
        gain_mlp,
        shift_mlp,
        up_weight,
        up_bias,
        down_weight,
    )
    keep, give, keep_in, give_in, d_mlp_part = visit(
        [inputs], (keep, give, keep_in, give_in, d_mlp_part)
    )
    d_mlp = across_heads(d_mlp_part)
    ring = Reduce(keep, swap_cores(give), keep_in, swap_cores(give_in), table)
    mlp_part, d_mlp = lax.optimization_barrier((mlp_part, d_mlp))
    d_hidden, d_branch, d_attn, sums = middle(hidden, out_grad, d_mlp, gain_mlp, output_weight)
    grads = scatter_queries(d_attn, heads, split)
    d_branch, mlp_part = visit([ring, inputs], (d_branch, mlp_part))
    while inputs.busy():
        visit([inputs], ())
    mlp_out = across_heads(mlp_part)
    steps, inputs = zip(*inputs.blocks)
    parts = [join(inputs)]
    if cut != model:
        parts = across_heads(parts[0])
    out_near, out_far = share_halves(attn_out, 0)
    doutput = product(out_near, d_branch) + product(out_far, swap_cores(d_branch))
    doutput = doutput.astype(BF16).reshape(chips, -1, model)
    grads, doutput = visit([ring], (grads, doutput))
    doutput = to_heads(doutput)
    *dquery, far_sums = backward_piece(
        queries, grads, raw, logsum, [], other, [], 0, 1, crops, (F32, BF16)
    )
    grads, dquery, far_sums = visit([ring], (grads, dquery, far_sums))
    far_sums = swap_cores(far_sums)
    *dquery, near_sums = backward_piece(
        queries, grads, raw, logsum, dquery, own, [], 0, 1, crops, (BF16, F32)
    )
    near_sums, dquery = ring.arrive((near_sums, dquery))
    (dquery,) = dquery
    key_value = (near_sums + far_sums.astype(F32)).astype(BF16)
    doutput, key_value = lax.optimization_barrier((doutput, key_value))
    doutput = jnp.sum(doutput.astype(F32), axis=0)
    small = jnp.concatenate([sums.reshape(-1), dup_bias[0]])
    small = jnp.pad(small, (0, small_rows * model - small.shape[0])).reshape(small_rows, model)
    doutput = jnp.concatenate([doutput, small], axis=0).astype(BF16)
    if split == 1:
        moved = to_heads(jnp.concatenate([dquery, key_value], axis=1))
        projections = head_gradient(dquery, key_value, parts, steps, table)
        near, far = share_halves(projections, 0)
        projections = (near.astype(F32) + far.astype(F32)).astype(BF16)
        size = projections.shape[0]
        blocks = jnp.concatenate([projections, doutput], axis=0)
        dquery, dkey, dvalue = (
            moved[:, at * HD : at * HD + HD].reshape(width, rows) for at in range(3)
        )
    else:
        dquery = gather_queries(dquery, heads, split, rows)
        moved = to_heads(key_value).reshape(heads, split, 2 * HD, rows).astype(F32)
        moved = jnp.sum(moved, axis=1).astype(BF16)
        dkey, dvalue = (moved[:, at * HD : at * HD + HD].reshape(width, rows) for at in range(2))
        size, blocks = 0, doutput
        projections = [
            lax.psum(product(attn_in, grad, 0, 1).astype(BF16), ("chip", "core")).astype(F32)
            for grad in (dquery, dkey, dvalue)
        ]
    blocks, mlp_out = lax.optimization_barrier((blocks, mlp_out))
    block_output = hidden + down_bias
    for part in mlp_out:
        block_output += part.astype(F32)
    block_output = block_output.astype(BF16)
    total = ring.finish()
    start = total.shape[0]
    ring.size, ring.extra = size, blocks.shape[0] - size - small_rows
    gathered = Gather(jnp.concatenate([total, blocks], axis=0), True, ring.place)
    gathered.send(gathered.ready)
    d_part = (
        product(dquery, query_weight, 0, 1)
        + product(dkey, key_weight, 0, 1)
        + product(dvalue, value_weight, 0, 1)
    )
    d_in = across_heads(d_part.astype(BF16))
    unit_attn, inverse_attn = normalize(block_input.astype(F32))
    onehot = (segments[:, None] == jnp.arange(crops, dtype=jnp.int32)[None, :]).astype(F32)
    lead = jnp.sum(onehot * lead_steps.astype(F32)[None, :], axis=1) / 12.0
    ends = jnp.stack(
        [
            jnp.sum(d_part * unit_attn, axis=0),
            jnp.sum(d_part, axis=0),
            jnp.sum(lead[:, None] * d_part, axis=0),
        ]
    )
    ends = jnp.pad(ends.reshape(-1, 128), ((0, -ends.size // 128 % 16), (0, 0))).astype(BF16)
    everyone = ("chip", "core", "head")
    ends = jnp.broadcast_to(ends, (lax.axis_size(everyone),) + ends.shape)
    ends = lax.all_to_all(ends, everyone, 0, 0, tiled=True)
    visit([gathered], d_part)
    d_in, block_output = visit([gathered], (d_in, block_output))
    ends = visit([gathered], ends)
    ends = jnp.sum(ends.astype(F32), axis=0).reshape(-1)[: 3 * model].reshape(3, model)
    d_in = functools.reduce(jnp.add, (part.astype(F32) for part in d_in))
    input_grad = (d_hidden + normalize_back(d_in * gain_attn, unit_attn, inverse_attn)).astype(
        BF16
    )
    while gathered.busy():
        ends, input_grad = visit([gathered], (ends, input_grad))
    ddown_weight, dup_weight, *rest = gathered.outputs
    if split == 1:
        held, doutput_weight, small = rest
        projections = final_layout(held)
        doutput_weight = doutput_weight.reshape(width, model)
    if split != 1:
        blocks = jnp.zeros((2, chips) + blocks.shape, F32)
        for step, near, far in gathered.pairs:
            for side, block in ((core, near[start:]), (1 - core, far[start:])):
                at = (side, table[chips + step % chips], 0, 0)
                block = block[None, None].astype(F32)
                blocks = lax.dynamic_update_slice(blocks, block, at)
        doutput_weight = blocks[:, :, :-small_rows].reshape(width, model)
        small = blocks[:, :, -small_rows:]
    small = jnp.sum(small, axis=(0, 1))
    dup_bias = small[4:].reshape(-1)[: dup_bias.shape[1]]
    return (
        block_output,
        input_grad,
        ends[0],
        ends[1],
        ends[2],
        *projections,
        doutput_weight,
        *small[:3],
        dup_weight,
        dup_bias,
        ddown_weight,
        small[3],
    )


def solution(mesh):
    bands, halves = mesh.shape["band"], mesh.shape["head"]
    inner = Mesh(mesh.devices.reshape(bands // 2, 2, halves), ("chip", "core", "head"))
    band = ("chip", "core")
    rows, columns, split_rows = P(band, None), P(None, "head"), P("head", None)
    return jax.shard_map(
        local,
        mesh=inner,
        in_specs=(
            rows,
            rows,
            P(band),
            P(),
            P(),
            P(),
            P(),
            columns,
            columns,
            columns,
            split_rows,
            P(),
            P(),
            P(),
            columns,
            P("head"),
            split_rows,
            P(),
        ),
        out_specs=(
            rows,
            rows,
            P(),
            P(),
            P(),
            columns,
            columns,
            columns,
            split_rows,
            P(),
            P(),
            P(),
            columns,
            P("head"),
            split_rows,
            P(),
        ),
        check_vma=False,
    )
```

```python
import functools
import math

import jax
import jax.numpy as jnp
from jax import lax
from jax.experimental import pallas as pl
from jax.experimental.pallas import tpu as pltpu
from jax.sharding import Mesh, PartitionSpec as P

HD = 64
F32 = jnp.float32
BF16 = jnp.bfloat16
eps = 1e-05
masked_value = -1e30
seg_row = 3 * HD
payload_rows = 3 * HD + 16
small_rows = 16
params = pltpu.CompilerParams(vmem_limit_bytes=48 * 2**20)
streaming = pltpu.CompilerParams(vmem_limit_bytes=60 * 2**20)


def normalize(values):
    centred = values - jnp.mean(values, axis=-1, keepdims=True)
    inverse = lax.rsqrt(jnp.mean(centred * centred, axis=-1, keepdims=True) + eps)
    return (centred * inverse, inverse)


def normalize_back(grad_unit, unit, inverse):
    return inverse * (
        grad_unit
        - jnp.mean(grad_unit, axis=-1, keepdims=True)
        - unit * jnp.mean(grad_unit * unit, axis=-1, keepdims=True)
    )


def product(first, second, first_axis=1, second_axis=0):
    return lax.dot_general(
        first,
        second,
        (((first_axis,), (second_axis,)), ((), ())),
        preferred_element_type=jnp.float32,
    )


def struct(shape, dtype):
    return jax.ShapeDtypeStruct(shape, dtype)


def whole_spec(shape):
    return pl.BlockSpec(shape, lambda *at: (0,) * len(shape))


light = pl.CostEstimate(flops=1, bytes_accessed=1, transcendentals=0)


def project_kernel(
    table, input_ref, segment_ref, steps_ref, gain, shift, lead_weight, *refs
):
    weights, (payload_ref, attn_in_ref, cut_ref) = refs[:3], refs[3:]
    rows = input_ref.shape[0]

    @pl.when(pl.program_id(0) == 0)
    def _():
        unit, _ = normalize(input_ref[...].astype(F32))
        crops = steps_ref.shape[0]
        crop = lax.broadcasted_iota(jnp.int32, (crops, rows), 0)
        steps = jnp.zeros((crops, rows), jnp.int32)
        for at in range(crops):
            steps = jnp.where(crop == at, steps_ref[at], steps)
        steps = jnp.where(crop == segment_ref[...], steps, 0).astype(F32)
        lead = product(steps, jnp.ones((crops, 128), F32), 0, 0)[:, :1] / 12.0
        attn_in = unit * gain[...] + shift[...] + lead * lead_weight[...]
        attn_in = attn_in.astype(BF16)
        attn_in_ref[...] = attn_in
        columns = cut_ref.shape[1]
        first = table[table.shape[0] - 1] % (attn_in.shape[1] // columns) == 0
        cut_ref[...] = jnp.where(first, attn_in[:, :columns], attn_in[:, -columns:])

    for at, weight in enumerate(weights):
        part = product(attn_in_ref[...], weight[...]).T.astype(BF16)
        for head in range(2):
            payload_ref[head, pl.ds(at * HD, HD), :] = part[head * HD : head * HD + HD]
    segment = jnp.broadcast_to(segment_ref[...].astype(F32), (16, rows)).astype(BF16)
    for head in range(2):
        payload_ref[head, pl.ds(seg_row, 16), :] = segment


def project(table, cut, block_input, segments, lead_steps, gain, shift, lead_weight, weights):
    rows, model = block_input.shape
    heads = weights[0].shape[1] // HD
    line = whole_spec((1, model))
    column = pl.BlockSpec((model, 2 * HD), lambda at, table: (0, at))
    return pl.pallas_call(
        project_kernel,
        grid_spec=pltpu.PrefetchScalarGridSpec(
            num_scalar_prefetch=1,
            grid=(heads // 2,),
            in_specs=[
                whole_spec(block_input.shape),
                whole_spec((1, rows)),
                pl.BlockSpec(memory_space=pltpu.SMEM),
            ]
            + [line] * 3
            + [column] * 3,
            out_specs=[
                pl.BlockSpec((2, payload_rows, rows), lambda at, table: (at, 0, 0)),
                whole_spec((rows, model)),
                whole_spec((rows, cut)),
            ],
        ),
        out_shape=[
            struct((heads, payload_rows, rows), BF16),
            struct((rows, model), BF16),
            struct((rows, cut), BF16),
        ],
        compiler_params=streaming,
        cost_estimate=light,
        name="project",
    )(table, block_input, segments[None], lead_steps, gain[None], shift[None], lead_weight[None], *weights)


def mlp_kernel(count, core_ref, input_ref, grad_ref, *refs):
    branches, refs = refs[:count], refs[count:]
    output_bias, gain, shift, up_weight, up_bias, down_weight = refs[:6]
    keep_ref, give_ref, keep_in_ref, give_in_ref, hidden_ref, bias_ref, forward_ref, back_ref = refs[
        6:14
    ]
    mlp_in_ref, forward, back = refs[14:]
    at = pl.program_id(0)
    is_down = core_ref[core_ref.shape[0] - 2] == 0

    @pl.when(at == 0)
    def _():
        hidden = input_ref[...].astype(F32) + output_bias[...]
        for branch in branches:
            hidden += branch[...].astype(F32)
        hidden_ref[...] = hidden
        unit, _ = normalize(hidden)
        mlp_in = (unit * gain[...] + shift[...]).astype(BF16)
        mlp_in_ref[...] = mlp_in
        keep_in_ref[...] = jnp.where(is_down, grad_ref[...], mlp_in)
        give_in_ref[...] = jnp.where(is_down, mlp_in, grad_ref[...])
        forward[...] = jnp.zeros_like(forward)
        back[...] = jnp.zeros_like(back)

    upper = product(mlp_in_ref[...], up_weight[...]) + up_bias[...]
    share = 0.5 + 0.5 * lax.erf(upper * math.sqrt(0.5))
    slope = share + upper * (jnp.exp(upper * upper * -0.5) * (1.0 / math.sqrt(2.0 * math.pi)))
    active = (upper * share).astype(BF16)
    d_active = product(grad_ref[...], down_weight[...], 1, 1)
    d_upper = (d_active * slope).astype(BF16)
    keep_ref[...] = jnp.where(is_down, active, d_upper)
    give_ref[...] = jnp.where(is_down, d_upper, active)
    bias_ref[...] = jnp.sum(d_upper.astype(F32), axis=0, keepdims=True)
    forward[...] += product(active, down_weight[...])
    back[...] += product(d_upper, up_weight[...], 1, 1)

    @pl.when(at == pl.num_programs(0) - 1)
    def _():
        forward_ref[...] = forward[...].astype(BF16)
        back_ref[...] = back[...].astype(BF16)


def mlp(
    table, block_input, out_grad, branches, output_bias, gain, shift, up_weight, up_bias, down_weight
):
    rows, model = block_input.shape
    units = up_weight.shape[1]
    step = math.gcd(units, 512)
    tile, line = whole_spec((rows, model)), whole_spec((1, model))
    wide = pl.BlockSpec((rows, step), lambda at, table: (0, at))
    bias = pl.BlockSpec((1, step), lambda at, table: (0, at))
    return pl.pallas_call(
        functools.partial(mlp_kernel, len(branches)),
        grid_spec=pltpu.PrefetchScalarGridSpec(
            num_scalar_prefetch=1,
            grid=(units // step,),
            in_specs=[tile] * (2 + len(branches))
            + [line] * 3
            + [
                pl.BlockSpec((model, step), lambda at, table: (0, at)),
                bias,
                pl.BlockSpec((step, model), lambda at, table: (at, 0)),
            ],
            out_specs=[wide, wide, tile, tile, tile, bias, tile, tile],
            scratch_shapes=[pltpu.VMEM((rows, model), BF16)]
            + [pltpu.VMEM((rows, model), F32)] * 2,
        ),
        out_shape=[struct((rows, units), BF16)] * 2
        + [struct((rows, model), BF16)] * 2
        + [
            struct((rows, model), F32),
            struct((1, units), F32),
            struct((rows, model), BF16),
            struct((rows, model), BF16),
        ],
        compiler_params=streaming,
        cost_estimate=light,
        name="mlp",
    )(
        table,
        block_input,
        out_grad,
        *branches,
        output_bias[None],
        gain[None],
        shift[None],
        up_weight,
        up_bias[None],
        down_weight,
    )


def middle_kernel(count, hidden_ref, grad_ref, *refs):
    parts, refs = refs[:count], refs[count:]
    gain, output_weight, d_hidden_ref, d_branch_ref, d_attn_ref, sums_ref = refs
    unit, inverse = normalize(hidden_ref[...])
    d_mlp = parts[0][...].astype(F32)
    for part in parts[1:]:
        d_mlp += part[...].astype(F32)
    grad = grad_ref[...].astype(F32)
    d_hidden = grad + normalize_back(d_mlp * gain[...], unit, inverse)
    d_hidden_ref[...] = d_hidden
    d_branch = d_hidden.astype(BF16)
    d_branch_ref[...] = d_branch
    d_attn_ref[...] = product(output_weight[...], d_branch, 1, 1).astype(BF16)
    for at, values in enumerate((d_hidden, d_mlp * unit, d_mlp, grad)):
        sums_ref[pl.ds(at, 1), :] = jnp.sum(values, axis=0, keepdims=True)


def middle(hidden, out_grad, parts, gain, output_weight):
    rows, model = hidden.shape
    width = output_weight.shape[0]
    return pl.pallas_call(
        functools.partial(middle_kernel, len(parts)),
        out_shape=[
            struct((rows, model), F32),
            struct((rows, model), BF16),
            struct((width, rows), BF16),
            struct((4, model), F32),
        ],
        compiler_params=streaming,
        cost_estimate=light,
        name="middle",
    )(hidden, out_grad, *parts, gain[None], output_weight)


def mask_rows(piece, chip, crops):
    crop = lax.broadcasted_iota(jnp.int32, (HD, piece.shape[2]), 0)
    segment = piece[chip, pl.ds(seg_row, 16), :].astype(F32)[:1].astype(jnp.int32)
    return jnp.where((crop != segment) & (crop < crops), masked_value, 0.0)


def load_keys(piece, crops, keys, key_t, value_n):
    chips, _, patches = piece.shape
    for chip in range(chips):
        key = piece[chip, pl.ds(HD, HD), :]
        value = piece[chip, pl.ds(2 * HD, HD), :]
        place = pl.ds(chip * patches, patches)
        both = jnp.concatenate([key.astype(F32), mask_rows(piece, chip, crops)], axis=0)
        keys[place, :] = both.T.astype(BF16)
        key_t[:, place] = key
        value_n[place, :] = value.astype(F32).T.astype(BF16)


def masked_query(query_ref, dtype=BF16):
    query = query_ref[0, pl.ds(0, HD), :].astype(F32) * 0.125
    segment = query_ref[0, pl.ds(seg_row, 16), :].astype(F32)[:1].astype(jnp.int32)
    crop = lax.broadcasted_iota(jnp.int32, query.shape, 0)
    onehot = jnp.where(crop == segment, 1.0, 0.0)
    return jnp.concatenate([query, onehot], axis=0).astype(dtype)


def forward_kernel(
    crops, step, query_ref, own, other, raw_ref, out_ref, logsum_ref, key_t, value_n, scores
):
    @pl.when(pl.program_id(0) == 0)
    def _():
        start = 0
        for piece in (own, other):
            chips, _, patches = piece.shape
            for chip in range(chips):
                place = pl.ds(start, patches)
                key = piece[chip, pl.ds(HD, HD), :].astype(F32)
                key_t[:, place] = jnp.concatenate([key, mask_rows(piece, chip, crops)], axis=0).astype(BF16)
                value = piece[chip, pl.ds(2 * HD, HD), :].astype(F32)
                value = jnp.concatenate([value, jnp.ones_like(value)], axis=0)
                value_n[place, :] = value.T.astype(BF16)
                start += patches

    query = masked_query(query_ref, F32).T.astype(BF16)
    count = query.shape[0]
    top = jnp.full((count, 128), masked_value, F32)
    for start in range(0, key_t.shape[1], step):
        block = product(query, key_t[:, pl.ds(start, step)])
        scores[:, pl.ds(start, step)] = block
        for at in range(0, step, 128):
            top = jnp.maximum(top, block[:, at : at + 128])
    top = jnp.max(top, axis=1, keepdims=True)
    accum = jnp.zeros((count, 2 * HD), F32)
    for start in range(0, key_t.shape[1], step):
        weights = jnp.exp(scores[:, pl.ds(start, step)] - top).astype(BF16)
        accum += product(weights, value_n[pl.ds(start, step), :])
    accum = accum.T
    total = accum[HD : HD + 1]
    raw = accum[:HD] / total
    raw_ref[0] = raw
    out_ref[0] = raw.astype(BF16)
    top = jnp.broadcast_to(top, (count, 128)).T[:1]
    logsum_ref[0] = top + jnp.log(total)


def backward_kernel(
    crops,
    before,
    query_ref,
    grad_ref,
    raw_ref,
    logsum_ref,
    *refs,
):
    before_refs, refs = refs[:before], refs[before:]
    piece, (dquery_ref, sums_ref, keys, key_t, value_n, sums) = refs[0], refs[-6:]
    group = pl.program_id(0)

    @pl.when(group == 0)
    def _():
        load_keys(piece, crops, keys, key_t, value_n)
        sums[...] = jnp.zeros_like(sums)

    query = masked_query(query_ref)
    grad = grad_ref[0]
    grad_wide = grad.astype(F32)
    delta = jnp.sum(grad_wide * raw_ref[0], axis=0, keepdims=True)
    scaled = query_ref[0, pl.ds(0, HD), :].astype(F32) * 0.125
    zero = jnp.zeros_like(scaled)
    query_side = jnp.concatenate([scaled, zero], axis=0).T.astype(BF16)
    grad_side = jnp.concatenate([zero, grad_wide], axis=0).T.astype(BF16)
    probs = jnp.exp(product(keys[...], query) - logsum_ref[0])
    dprobs = product(value_n[...], grad)
    dscores = (probs * (dprobs - delta)).astype(BF16)
    sums[...] += product(dscores, query_side) + product(probs.astype(BF16), grad_side)
    dquery = product(key_t[...], dscores) * 0.125
    for ref in before_refs:
        dquery = ref[0] + dquery
    dquery_ref[0] = dquery.astype(dquery_ref.dtype)

    @pl.when(group == pl.num_programs(0) - 1)
    def _():
        chips, _, patches = sums_ref.shape
        for chip in range(chips):
            sums_ref[chip] = sums[pl.ds(chip * patches, patches), :].T.astype(sums_ref.dtype)


def key_step(count):
    return 1024 if count % 1024 == 0 else 256


def query_spec(rows, patches):
    return pl.BlockSpec((1, rows, patches), lambda group: (group, 0, 0))


def attention_forward(queries, own, other, crops):
    groups, _, patches = queries.shape
    count = 2 * own.shape[0] * own.shape[2]
    return pl.pallas_call(
        functools.partial(forward_kernel, crops, key_step(count)),
        grid=(groups,),
        in_specs=[
            query_spec(payload_rows, patches),
            whole_spec(own.shape),
            whole_spec(other.shape),
        ],
        out_specs=[query_spec(HD, patches), query_spec(HD, patches), query_spec(1, patches)],
        out_shape=[
            struct((groups, HD, patches), F32),
            struct((groups, HD, patches), BF16),
            struct((groups, 1, patches), F32),
        ],
        scratch_shapes=[
            pltpu.VMEM((2 * HD, count), BF16),
            pltpu.VMEM((count, 2 * HD), BF16),
            pltpu.VMEM((patches, count), F32),
        ],
        compiler_params=streaming,
        cost_estimate=light,
        name="attention_forward",
    )(queries, own, other)


def backward_piece(queries, grads, raw, logsum, before, keys, earlier, index, pieces, crops, dtypes):
    groups, _, patches = queries.shape
    chips = keys.shape[0] // pieces
    count = chips * keys.shape[2]
    sums_shape = (chips, 2 * HD, keys.shape[2])
    return pl.pallas_call(
        functools.partial(backward_kernel, crops, len(before)),
        grid=(groups,),
        in_specs=[
            query_spec(payload_rows, patches),
            query_spec(HD, patches),
            query_spec(HD, patches),
            query_spec(1, patches),
        ]
        + [query_spec(HD, patches)] * len(before)
        + [pl.BlockSpec((chips,) + keys.shape[1:], lambda group: (index, 0, 0))]
        + [pl.BlockSpec(memory_space=pl.ANY)] * len(earlier),
        out_specs=[
            query_spec(HD, patches),
            pl.BlockSpec(sums_shape, lambda group: (index, 0, 0)),
        ],
        out_shape=[
            struct((groups, HD, patches), dtypes[0]),
            struct((keys.shape[0],) + sums_shape[1:], dtypes[1]),
        ],
        input_output_aliases={5 + len(before): 1} if earlier else {},
        scratch_shapes=[
            pltpu.VMEM((count, 2 * HD), BF16),
            pltpu.VMEM((HD, count), BF16),
            pltpu.VMEM((count, HD), BF16),
            pltpu.VMEM((count, 2 * HD), F32),
        ],
        compiler_params=params,
        cost_estimate=light,
        name="attention_backward",
    )(queries, grads, raw, logsum, *before, keys, *earlier)


def swap_cores(values):
    return lax.ppermute(values, "core", [(0, 1), (1, 0)])


def to_heads(blocks):
    return lax.all_to_all(blocks, "chip", 0, 0, tiled=True)


def scatter_queries(values, heads, split):
    rows, patches = values.shape[0] // heads, values.shape[1]
    if split == 1:
        return to_heads(values.reshape(heads, rows, patches))
    part = patches // split
    blocks = values.reshape(heads, rows, split, part).transpose(0, 2, 1, 3)
    moved = to_heads(blocks.reshape(heads * split, rows, part))
    width = min(256, moved.shape[0] * part)
    joined = moved.transpose(1, 0, 2).reshape(rows, -1, width)
    return joined.transpose(1, 0, 2)


def gather_queries(values, heads, split, patches):
    rows = values.shape[1]
    if split == 1:
        return to_heads(values).reshape(heads * rows, patches)
    part = patches // split
    joined = values.transpose(1, 0, 2).reshape(rows, heads * split, part)
    moved = to_heads(joined.transpose(1, 0, 2)).reshape(heads, split, rows, part)
    return moved.transpose(0, 2, 1, 3).reshape(heads * rows, patches)


def across_heads(part):
    if lax.axis_size("head") == 2:
        return [part, lax.ppermute(part, "head", [(0, 1), (1, 0)])]
    return [lax.psum(part, "head")]


def ring_pairs(direction):
    chips = lax.axis_size("chip")
    order = list(range(0, chips, 2)) + list(range(chips - 1, 0, -2))
    return [(order[at], order[(at + direction) % chips]) for at in range(chips)]


def ring_table():
    chips, chip = lax.axis_size("chip"), lax.axis_index("chip")
    place = jnp.where(chip % 2 == 0, chip // 2, chips - 1 - chip // 2)
    steps = jnp.arange(2 * chips + 2, dtype=jnp.int32)
    places = (place + steps) % chips
    there = jnp.where(places < chips // 2, 2 * places, 2 * (chips - 1 - places) + 1)
    table = jnp.where(steps < chips, places, there)
    table = jnp.where(steps == 2 * chips, lax.axis_index("core"), table)
    return jnp.where(steps == 2 * chips + 1, lax.axis_index("head"), table).astype(jnp.int32)


def visit(streams, values):
    states, values = lax.optimization_barrier(([stream.state for stream in streams], values))
    for stream, state in zip(streams, states):
        stream.advance(state)
    ready, values = lax.optimization_barrier(([stream.ready for stream in streams], values))
    for stream, blocks in zip(streams, ready):
        stream.send(blocks)
    return values


def join_kernel(*refs):
    start = 0
    for block in refs[:-1]:
        refs[-1][pl.ds(start, block.shape[0]), :] = block[...]
        start += block.shape[0]


def join(blocks):
    rows = sum(block.shape[0] for block in blocks)
    return pl.pallas_call(
        join_kernel,
        out_shape=struct((rows, blocks[0].shape[1]), blocks[0].dtype),
        compiler_params=streaming,
        name="join",
    )(*blocks)


def halves_kernel(left, right, left_ref, right_ref):
    left_ref[...] = left[...]
    right_ref[...] = right[...]


def halves(left, right):
    rows, columns = left.shape
    if rows % 16 or columns % 256:
        return [left[:, : columns // 2], right[:, columns // 2 :]]
    out = pl.BlockSpec((rows, columns // 2), lambda at: (0, 0))
    return pl.pallas_call(
        halves_kernel,
        grid=(1,),
        in_specs=[out, pl.BlockSpec((rows, columns // 2), lambda at: (0, 1))],
        out_specs=[out, out],
        out_shape=[struct((rows, columns // 2), left.dtype)] * 2,
        compiler_params=streaming,
        name="halves",
    )(left, right)


class Gather:
    def __init__(self, block, swap=False, take=None):
        self.reach, self.swap, self.take = lax.axis_size("chip") // 2, swap, take
        self.blocks, self.pairs, self.count = [], [], 0
        self.new, self.outputs = [0], []
        self.ready = [block]

    def send(self, ready):
        new = list(zip(self.new, ready))
        self.blocks += new
        self.new = new
        self.count += 1
        sides = ready if len(ready) > 1 else ready * 2
        if self.count == self.reach:
            sides = halves(*sides)
        flying = []
        if self.count <= self.reach:
            flying = [
                lax.ppermute(block, "chip", ring_pairs(direction))
                for block, direction in zip(sides, (1, -1))
            ]
        if self.swap and ready:
            pairs = [(step, block, swap_cores(block)) for step, block in new]
            self.pairs += pairs
            self.outputs = self.take(self.outputs, pairs)
        self.state = (flying, self.outputs)

    def advance(self, state):
        arrived, self.outputs = state
        self.new = [-self.count, self.count]
        if arrived and self.count == self.reach:
            arrived, self.new = [jnp.concatenate(arrived, axis=1)], [self.count]
        self.ready = arrived

    def busy(self):
        return bool(self.state[0])


def add_kernel(wanted, count, _, *refs):
    outputs, refs = refs[-count:], list(refs[:-count])
    keep_in, far_in = refs.pop(0), refs.pop(0)
    for starts, output in zip(wanted, outputs):
        near, far = refs.pop(0), refs.pop(0)
        total = product(near[...], keep_in[...], 0, 0) + product(far[...], far_in[...], 0, 0)
        if len(outputs) > len(wanted):
            for at, output in enumerate(outputs):
                columns = output.shape[1]
                output[...] = total[:, at * columns : at * columns + columns].astype(BF16)
            return
        output[...] = total.astype(BF16)
        arrived = [refs.pop(0) for _ in starts]
        for start in sorted(set(starts)):
            parts = [part for part, at in zip(arrived, starts) if at == start]
            columns = slice(start, start + parts[0].shape[1])
            summed = total[:, columns]
            for part in parts:
                summed += part[...].astype(F32)
            output[:, columns] = summed.astype(BF16)


class Reduce:
    def __init__(self, keep, far, keep_in, far_in, table):
        self.chips, self.table = lax.axis_size("chip"), table
        self.operands, self.sides = (keep, far), (keep_in, far_in)
        self.units = keep.shape[1] // self.chips
        self.tiled = self.units % 128 == 0
        self.left, self.rest = self.chips // 2, None
        blocks = self.add([(self.left, [])], True)
        self.send(blocks if len(blocks) > 1 else halves(blocks[0], blocks[0]))

    def send(self, ready):
        self.left -= 1
        self.state = [
            lax.ppermute(block, "chip", ring_pairs(direction))
            for block, direction in zip(ready, (1, -1))
        ]

    def advance(self, state):
        half = self.sides[0].shape[1] // 2
        ahead, behind = state
        first = 0 if ahead.shape[1] != half else half
        self.ready = self.add([(self.left, [(ahead, 0)]), (-self.left, [(behind, first)])])

    def arrive(self, values):
        self.state, values = lax.optimization_barrier((self.state, values))
        return values

    def finish(self):
        ahead, behind = self.state
        return self.add([(0, [(ahead, 0), (behind, 0)])])[0]

    def add(self, wanted, split=False):
        (rows, model), units, chips = self.sides[0].shape, self.units, self.chips
        if not self.tiled:
            sums = []
            for step, parts in wanted:
                start = self.table[step % chips] * units
                total = jnp.zeros((units, model), F32)
                for operand, side in zip(self.operands, self.sides):
                    block = lax.dynamic_slice_in_dim(operand, start, units, 1)
                    total += product(block, side, 0, 0)
                for part, start in parts:
                    total = total.at[:, start : start + part.shape[1]].add(part.astype(F32))
                sums.append(total.astype(BF16))
            return sums
        side = pl.BlockSpec((rows, model), lambda at, table: (0, 0))
        whole = pl.BlockSpec((units, model), lambda at, table: (0, 0))
        specs, arrays = [side] * 2, list(self.sides)
        for step, parts in wanted:
            block = pl.BlockSpec(
                (rows, units), lambda at, table, step=step % chips: (0, table[step])
            )
            specs += [block] * 2
            specs += [pl.BlockSpec(part.shape, lambda at, table: (0, 0)) for part, _ in parts]
            arrays += list(self.operands) + [part for part, _ in parts]
        starts = [[start for _, start in parts] for _, parts in wanted]
        shapes = [struct((units, model), BF16)] * len(wanted)
        if split:
            shapes = [struct((units, model // 2), BF16)] * 2
        return pl.pallas_call(
            functools.partial(add_kernel, starts, len(shapes)),
            grid_spec=pltpu.PrefetchScalarGridSpec(
                num_scalar_prefetch=1,
                grid=(1,),
                in_specs=specs,
                out_specs=[pl.BlockSpec(shape.shape, lambda at, table: (0, 0)) for shape in shapes],
            ),
            out_shape=shapes,
            compiler_params=streaming,
            cost_estimate=light,
            name="ring_add",
        )(self.table, *arrays)

    def place(self, outputs, pairs):
        units, chips, model = self.units, self.chips, self.sides[0].shape[1]
        size, extra = self.size, self.extra
        shapes = [struct((chips * units, model), F32), struct((model, chips * units), F32)]
        if not self.tiled:
            outputs = outputs or [jnp.zeros(shape.shape, F32) for shape in shapes]
            down, up = outputs
            is_down = self.table[2 * chips] == 0
            for step, near, far in pairs:
                start = self.table[step % chips] * units
                near, far = near[:units], far[:units]
                first = jnp.where(is_down, near, far).astype(F32)
                second = jnp.where(is_down, far, near).astype(F32).T
                down = lax.dynamic_update_slice_in_dim(down, first, start, 0)
                up = lax.dynamic_update_slice_in_dim(up, second, start, 1)
            return [down, up]
        first = pairs[0][0] % chips
        stride = pairs[-1][0] % chips - first
        block = pl.BlockSpec(pairs[0][1].shape, lambda at, table: (0, 0))

        def place(at, table):
            return table[first + at * stride]

        def chip(at, table):
            return table[chips + first + at * stride]

        column = pl.BlockSpec(
            (model, 2 * HD), lambda at, table: (0, lax.div(chip(at, table), 2))
        )
        columns = [column] * (3 if outputs else 0)
        heads = [[first, first + stride][at] + chips for at in range(len(pairs))]
        return pl.pallas_call(
            functools.partial(place_kernel, heads, (units, size, extra)),
            grid_spec=pltpu.PrefetchScalarGridSpec(
                num_scalar_prefetch=1,
                grid=(len(pairs),),
                in_specs=[pl.BlockSpec(memory_space=pl.ANY)] * (len(outputs) - len(columns))
                + columns
                + [block] * (2 * len(pairs)),
                out_specs=[
                    pl.BlockSpec((units, model), lambda at, table: (place(at, table), 0)),
                    pl.BlockSpec((model, units), lambda at, table: (0, place(at, table))),
                    pl.BlockSpec((2, 1, extra, model), lambda at, table: (0, chip(at, table), 0, 0)),
                    pl.BlockSpec(
                        (1, 2, small_rows, model), lambda at, table: (chip(at, table), 0, 0, 0)
                    ),
                ]
                + [column] * 3,
            ),
            out_shape=shapes
            + [
                struct((2, chips, extra, model), F32),
                struct((chips, 2, small_rows, model), F32),
            ]
            + [struct((model, chips * HD), F32)] * 3,
            input_output_aliases={1 + at: at for at in range(len(outputs))},
            compiler_params=streaming,
            cost_estimate=light,
            name="place",
        )(self.table, *outputs, *[pair[1] for pair in pairs], *[pair[2] for pair in pairs])


def place_kernel(heads, sizes, table, *refs):
    count = len(heads)
    refs, (down, up, weight, small), projections = refs[:-7], refs[-7:-3], refs[-3:]
    blocks, refs = refs[-2 * count :], refs[: -2 * count]
    core = table[table.shape[0] - 2]
    units, size, extra = sizes
    rows = [pl.ds(0, units), pl.ds(units, size), pl.ds(units + size, extra)]
    rows.append(pl.ds(units + size + extra, small_rows))

    def put(first, second, head):
        down[...] = first[rows[0], :].astype(F32)
        up[...] = second[rows[0], :].astype(F32).T
        for side, block in ((0, first), (1, second)):
            weight[side, 0] = block[rows[2], :].astype(F32)
            small[0, side] = block[rows[3], :].astype(F32)
        both = jnp.concatenate([first[rows[1], :], second[rows[1], :]], axis=0)
        for at, output in enumerate(projections):
            part = both[at * HD : at * HD + HD].astype(F32)
            part = jnp.concatenate([part, part], axis=0).T
            if refs:
                mine = lax.broadcasted_iota(jnp.int32, part.shape, 1) // HD == head % 2
                part = jnp.where(mine, part, refs[at - 3][...])
            output[...] = part

    for at in range(count):
        near, far, head = blocks[at], blocks[count + at], table[heads[at]]
        here = pl.program_id(0) == at
        pl.when(here & (core == 0))(functools.partial(put, near, far, head))
        pl.when(here & (core != 0))(functools.partial(put, far, near, head))


def head_gradient_kernel(steps, chips, table, query_ref, key_value_ref, *refs):
    parts, out_ref = refs[:-1], refs[-1]
    patches = query_ref.shape[2]
    for at, part in enumerate(parts):

        @pl.when(pl.program_id(0) == at)
        def _(part=part):
            total = jnp.zeros(out_ref.shape, F32)
            for index, step in enumerate(steps):
                chip = table[chips + step % chips]
                grads = jnp.concatenate([query_ref[chip], key_value_ref[chip]], axis=0)
                total += product(grads, part[pl.ds(index * patches, patches), :])
            out_ref[...] = total.astype(BF16)


def head_gradient(dquery, key_value, parts, steps, table):
    chips, rows, _ = dquery.shape
    columns = parts[0].shape[1]

    def column(at, table):
        mine = table[2 * chips + 1] if len(parts) > 1 else 0
        return (0, jnp.where(at == 0, mine, 1 - mine))

    return pl.pallas_call(
        functools.partial(head_gradient_kernel, steps, chips),
        grid_spec=pltpu.PrefetchScalarGridSpec(
            num_scalar_prefetch=1,
            grid=(len(parts),),
            in_specs=[
                pl.BlockSpec(array.shape, lambda at, table, rank=array.ndim: (0,) * rank)
                for array in (dquery, key_value, *parts)
            ],
            out_specs=pl.BlockSpec((3 * rows, columns), column),
        ),
        out_shape=struct((3 * rows, columns * len(parts)), BF16),
        compiler_params=streaming,
        cost_estimate=light,
        name="head_gradient",
    )(table, dquery, key_value, *parts)


def core_half(values, axis, side):
    size = values.shape[axis] // 2
    return lax.dynamic_slice_in_dim(values, side * size, size, axis)


def share_halves(values, axis):
    core = lax.axis_index("core")
    return core_half(values, axis, core), swap_cores(core_half(values, axis, 1 - core))


def local(
    block_input,
    out_grad,
    segments,
    lead_steps,
    gain_attn,
    shift_attn,
    lead_weight,
    query_weight,
    key_weight,
    value_weight,
    output_weight,
    output_bias,
    gain_mlp,
    shift_mlp,
    up_weight,
    up_bias,
    down_weight,
    down_bias,
):
    rows, model = block_input.shape
    heads = query_weight.shape[1] // HD
    width = heads * HD
    chips, core = lax.axis_size("chip"), lax.axis_index("core")
    split = chips // heads
    crops = lead_steps.shape[0]
    table = ring_table()
    weights = (query_weight, key_weight, value_weight)
    cut = model // 2 if lax.axis_size("head") == 2 else model
    payload, attn_in, attn_in_cut = project(
        table, cut, block_input, segments, lead_steps, gain_attn, shift_attn, lead_weight, weights
    )
    if split == 1:
        own = to_heads(payload)
        queries = own
    else:
        queries = scatter_queries(payload.reshape(-1, rows), heads, split)
        own = to_heads(jnp.repeat(payload, split, axis=0))
    own, attn_in_cut = lax.optimization_barrier((own, attn_in_cut))
    inputs = Gather(attn_in_cut)
    inputs.send(inputs.ready)
    other = swap_cores(own)
    raw, out, logsum = attention_forward(queries, own, other, crops)
    inputs.state, out = lax.optimization_barrier((inputs.state, out))
    attn_out = gather_queries(out, heads, split, rows)
    attn_out = visit([inputs], attn_out)
    branches = across_heads(product(attn_out, output_weight, 0, 0).astype(BF16))
    visit([inputs], ())
    keep, give, keep_in, give_in, hidden, dup_bias, mlp_part, d_mlp_part = mlp(
        table,
        block_input,
        out_grad,
        branches,
        output_bias,
        gain_mlp,
        shift_mlp,
        up_weight,
        up_bias,
        down_weight,
    )
    keep, give, keep_in, give_in, d_mlp_part = visit(
        [inputs], (keep, give, keep_in, give_in, d_mlp_part)
    )
    d_mlp = across_heads(d_mlp_part)
    ring = Reduce(keep, swap_cores(give), keep_in, swap_cores(give_in), table)
    mlp_part, d_mlp = lax.optimization_barrier((mlp_part, d_mlp))
    d_hidden, d_branch, d_attn, sums = middle(hidden, out_grad, d_mlp, gain_mlp, output_weight)
    grads = scatter_queries(d_attn, heads, split)
    d_branch, mlp_part = visit([ring, inputs], (d_branch, mlp_part))
    while inputs.busy():
        visit([inputs], ())
    mlp_out = across_heads(mlp_part)
    steps, inputs = zip(*inputs.blocks)
    parts = [join(inputs)]
    if cut != model:
        parts = across_heads(parts[0])
    out_near, out_far = share_halves(attn_out, 0)
    doutput = product(out_near, d_branch) + product(out_far, swap_cores(d_branch))
    doutput = doutput.astype(BF16).reshape(chips, -1, model)
    doutput = to_heads(doutput)
    *dquery, far_sums = backward_piece(
        queries, grads, raw, logsum, [], other, [], 0, 1, crops, (F32, BF16)
    )
    grads, dquery, far_sums, doutput = visit([ring], (grads, dquery, far_sums, doutput))
    far_sums = swap_cores(far_sums)
    *dquery, near_sums = backward_piece(
        queries, grads, raw, logsum, dquery, own, [], 0, 1, crops, (BF16, F32)
    )
    near_sums, dquery = visit([ring], (near_sums, dquery))
    (dquery,) = dquery
    key_value = (near_sums + far_sums.astype(F32)).astype(BF16)
    doutput, key_value = lax.optimization_barrier((doutput, key_value))
    doutput = jnp.sum(doutput.astype(F32), axis=0)
    small = jnp.concatenate([sums.reshape(-1), dup_bias[0]])
    small = jnp.pad(small, (0, small_rows * model - small.shape[0])).reshape(small_rows, model)
    doutput = jnp.concatenate([doutput, small], axis=0).astype(BF16)
    if split == 1:
        moved = to_heads(jnp.concatenate([dquery, key_value], axis=1))
        projections = head_gradient(dquery, key_value, parts, steps, table)
        near, far = share_halves(projections, 0)
        projections = (near.astype(F32) + far.astype(F32)).astype(BF16)
        size = projections.shape[0]
        blocks = jnp.concatenate([projections, doutput], axis=0)
        dquery, dkey, dvalue = (
            moved[:, at * HD : at * HD + HD].reshape(width, rows) for at in range(3)
        )
    else:
        dquery = gather_queries(dquery, heads, split, rows)
        moved = to_heads(key_value).reshape(heads, split, 2 * HD, rows).astype(F32)
        moved = jnp.sum(moved, axis=1).astype(BF16)
        dkey, dvalue = (moved[:, at * HD : at * HD + HD].reshape(width, rows) for at in range(2))
        size, blocks = 0, doutput
        projections = [
            lax.psum(product(attn_in, grad, 0, 1).astype(BF16), ("chip", "core")).astype(F32)
            for grad in (dquery, dkey, dvalue)
        ]
    blocks = ring.arrive(blocks)
    total = ring.finish()
    start = total.shape[0]
    ring.size, ring.extra = size, blocks.shape[0] - size - small_rows
    gathered = Gather(jnp.concatenate([total, blocks], axis=0), True, ring.place)
    gathered.send(gathered.ready)
    d_part = (
        product(dquery, query_weight, 0, 1)
        + product(dkey, key_weight, 0, 1)
        + product(dvalue, value_weight, 0, 1)
    )
    d_in = across_heads(d_part.astype(BF16))
    unit_attn, inverse_attn = normalize(block_input.astype(F32))
    onehot = (segments[:, None] == jnp.arange(crops, dtype=jnp.int32)[None, :]).astype(F32)
    lead = jnp.sum(onehot * lead_steps.astype(F32)[None, :], axis=1) / 12.0
    ends = jnp.stack(
        [
            jnp.sum(d_part * unit_attn, axis=0),
            jnp.sum(d_part, axis=0),
            jnp.sum(lead[:, None] * d_part, axis=0),
        ]
    )
    ends = jnp.pad(ends.reshape(-1, 128), ((0, -ends.size // 128 % 16), (0, 0))).astype(BF16)
    everyone = ("chip", "core", "head")
    ends = jnp.broadcast_to(ends, (lax.axis_size(everyone),) + ends.shape)
    ends = lax.all_to_all(ends, everyone, 0, 0, tiled=True)
    _, mlp_out = visit([gathered], (d_part, mlp_out))
    block_output = hidden + down_bias
    for part in mlp_out:
        block_output += part.astype(F32)
    block_output = block_output.astype(BF16)
    d_in, block_output = visit([gathered], (d_in, block_output))
    visit([gathered], ())
    d_in = functools.reduce(jnp.add, (part.astype(F32) for part in d_in))
    input_grad = (d_hidden + normalize_back(d_in * gain_attn, unit_attn, inverse_attn)).astype(
        BF16
    )
    while gathered.busy():
        input_grad = visit([gathered], input_grad)
    ddown_weight, dup_weight, *rest = gathered.outputs
    ends = jnp.sum(ends.astype(F32), axis=0).reshape(-1)[: 3 * model].reshape(3, model)
    if split == 1:
        doutput_weight, small, *projections = rest
        doutput_weight = doutput_weight.reshape(width, model)
    if split != 1:
        blocks = jnp.zeros((2, chips) + blocks.shape, F32)
        for step, near, far in gathered.pairs:
            for side, block in ((core, near[start:]), (1 - core, far[start:])):
                at = (side, table[chips + step % chips], 0, 0)
                block = block[None, None].astype(F32)
                blocks = lax.dynamic_update_slice(blocks, block, at)
        doutput_weight = blocks[:, :, :-small_rows].reshape(width, model)
        small = blocks[:, :, -small_rows:]
    small = jnp.sum(small, axis=(0, 1))
    dup_bias = small[4:].reshape(-1)[: dup_bias.shape[1]]
    return (
        block_output,
        input_grad,
        ends[0],
        ends[1],
        ends[2],
        *projections,
        doutput_weight,
        *small[:3],
        dup_weight,
        dup_bias,
        ddown_weight,
        small[3],
    )


def solution(mesh):
    bands, halves = mesh.shape["band"], mesh.shape["head"]
    inner = Mesh(mesh.devices.reshape(bands // 2, 2, halves), ("chip", "core", "head"))
    band = ("chip", "core")
    rows, columns, split_rows = P(band, None), P(None, "head"), P("head", None)
    return jax.shard_map(
        local,
        mesh=inner,
        in_specs=(
            rows,
            rows,
            P(band),
            P(),
            P(),
            P(),
            P(),
            columns,
            columns,
            columns,
            split_rows,
            P(),
            P(),
            P(),
            columns,
            P("head"),
            split_rows,
            P(),
        ),
        out_specs=(
            rows,
            rows,
            P(),
            P(),
            P(),
            columns,
            columns,
            columns,
            split_rows,
            P(),
            P(),
            P(),
            columns,
            P("head"),
            split_rows,
            P(),
        ),
        check_vma=False,
    )
```

```python
import functools
import math

import jax
import jax.numpy as jnp
from jax import lax
from jax.experimental import pallas as pl
from jax.experimental.pallas import tpu as pltpu
from jax.sharding import Mesh, PartitionSpec as P

HD = 64
F32 = jnp.float32
BF16 = jnp.bfloat16
eps = 1e-05
masked_value = -1e30
seg_row = 3 * HD
payload_rows = 3 * HD + 16
small_rows = 16
params = pltpu.CompilerParams(vmem_limit_bytes=48 * 2**20)
streaming = pltpu.CompilerParams(vmem_limit_bytes=60 * 2**20)


def normalize(values):
    centred = values - jnp.mean(values, axis=-1, keepdims=True)
    inverse = lax.rsqrt(jnp.mean(centred * centred, axis=-1, keepdims=True) + eps)
    return (centred * inverse, inverse)


def normalize_back(grad_unit, unit, inverse):
    return inverse * (
        grad_unit
        - jnp.mean(grad_unit, axis=-1, keepdims=True)
        - unit * jnp.mean(grad_unit * unit, axis=-1, keepdims=True)
    )


def product(first, second, first_axis=1, second_axis=0):
    return lax.dot_general(
        first,
        second,
        (((first_axis,), (second_axis,)), ((), ())),
        preferred_element_type=jnp.float32,
    )


def struct(shape, dtype):
    return jax.ShapeDtypeStruct(shape, dtype)


def whole_spec(shape):
    return pl.BlockSpec(shape, lambda *at: (0,) * len(shape))


light = pl.CostEstimate(flops=1, bytes_accessed=1, transcendentals=0)


def project_kernel(
    table, input_ref, segment_ref, steps_ref, gain, shift, lead_weight, *refs
):
    weights, (payload_ref, attn_in_ref, cut_ref) = refs[:3], refs[3:]
    rows = input_ref.shape[0]

    @pl.when(pl.program_id(0) == 0)
    def _():
        unit, _ = normalize(input_ref[...].astype(F32))
        crops = steps_ref.shape[0]
        crop = lax.broadcasted_iota(jnp.int32, (crops, rows), 0)
        steps = jnp.zeros((crops, rows), jnp.int32)
        for at in range(crops):
            steps = jnp.where(crop == at, steps_ref[at], steps)
        steps = jnp.where(crop == segment_ref[...], steps, 0).astype(F32)
        lead = product(steps, jnp.ones((crops, 128), F32), 0, 0)[:, :1] / 12.0
        attn_in = unit * gain[...] + shift[...] + lead * lead_weight[...]
        attn_in = attn_in.astype(BF16)
        attn_in_ref[...] = attn_in
        columns = cut_ref.shape[1]
        first = table[table.shape[0] - 1] % (attn_in.shape[1] // columns) == 0
        cut_ref[...] = jnp.where(first, attn_in[:, :columns], attn_in[:, -columns:])

    for at, weight in enumerate(weights):
        part = product(attn_in_ref[...], weight[...]).T.astype(BF16)
        for head in range(2):
            payload_ref[head, pl.ds(at * HD, HD), :] = part[head * HD : head * HD + HD]
    segment = jnp.broadcast_to(segment_ref[...].astype(F32), (16, rows)).astype(BF16)
    for head in range(2):
        payload_ref[head, pl.ds(seg_row, 16), :] = segment


def project(table, cut, block_input, segments, lead_steps, gain, shift, lead_weight, weights):
    rows, model = block_input.shape
    heads = weights[0].shape[1] // HD
    line = whole_spec((1, model))
    column = pl.BlockSpec((model, 2 * HD), lambda at, table: (0, at))
    return pl.pallas_call(
        project_kernel,
        grid_spec=pltpu.PrefetchScalarGridSpec(
            num_scalar_prefetch=1,
            grid=(heads // 2,),
            in_specs=[
                whole_spec(block_input.shape),
                whole_spec((1, rows)),
                pl.BlockSpec(memory_space=pltpu.SMEM),
            ]
            + [line] * 3
            + [column] * 3,
            out_specs=[
                pl.BlockSpec((2, payload_rows, rows), lambda at, table: (at, 0, 0)),
                whole_spec((rows, model)),
                whole_spec((rows, cut)),
            ],
        ),
        out_shape=[
            struct((heads, payload_rows, rows), BF16),
            struct((rows, model), BF16),
            struct((rows, cut), BF16),
        ],
        compiler_params=streaming,
        cost_estimate=light,
        name="project",
    )(table, block_input, segments[None], lead_steps, gain[None], shift[None], lead_weight[None], *weights)


def mlp_kernel(count, core_ref, input_ref, grad_ref, *refs):
    branches, refs = refs[:count], refs[count:]
    output_bias, gain, shift, up_weight, up_bias, down_weight = refs[:6]
    keep_ref, give_ref, keep_in_ref, give_in_ref, hidden_ref, bias_ref, forward_ref, back_ref = refs[
        6:14
    ]
    mlp_in_ref, forward, back = refs[14:]
    at = pl.program_id(0)
    is_down = core_ref[core_ref.shape[0] - 2] == 0

    @pl.when(at == 0)
    def _():
        hidden = input_ref[...].astype(F32) + output_bias[...]
        for branch in branches:
            hidden += branch[...].astype(F32)
        hidden_ref[...] = hidden
        unit, _ = normalize(hidden)
        mlp_in = (unit * gain[...] + shift[...]).astype(BF16)
        mlp_in_ref[...] = mlp_in
        keep_in_ref[...] = jnp.where(is_down, grad_ref[...], mlp_in)
        give_in_ref[...] = jnp.where(is_down, mlp_in, grad_ref[...])
        forward[...] = jnp.zeros_like(forward)
        back[...] = jnp.zeros_like(back)

    upper = product(mlp_in_ref[...], up_weight[...]) + up_bias[...]
    share = 0.5 + 0.5 * lax.erf(upper * math.sqrt(0.5))
    slope = share + upper * (jnp.exp(upper * upper * -0.5) * (1.0 / math.sqrt(2.0 * math.pi)))
    active = (upper * share).astype(BF16)
    d_active = product(grad_ref[...], down_weight[...], 1, 1)
    d_upper = (d_active * slope).astype(BF16)
    keep_ref[...] = jnp.where(is_down, active, d_upper)
    give_ref[...] = jnp.where(is_down, d_upper, active)
    bias_ref[...] = jnp.sum(d_upper.astype(F32), axis=0, keepdims=True)
    forward[...] += product(active, down_weight[...])
    back[...] += product(d_upper, up_weight[...], 1, 1)

    @pl.when(at == pl.num_programs(0) - 1)
    def _():
        forward_ref[...] = forward[...].astype(BF16)
        back_ref[...] = back[...].astype(BF16)


def mlp(
    table, block_input, out_grad, branches, output_bias, gain, shift, up_weight, up_bias, down_weight
):
    rows, model = block_input.shape
    units = up_weight.shape[1]
    step = math.gcd(units, 512)
    tile, line = whole_spec((rows, model)), whole_spec((1, model))
    wide = pl.BlockSpec((rows, step), lambda at, table: (0, at))
    bias = pl.BlockSpec((1, step), lambda at, table: (0, at))
    return pl.pallas_call(
        functools.partial(mlp_kernel, len(branches)),
        grid_spec=pltpu.PrefetchScalarGridSpec(
            num_scalar_prefetch=1,
            grid=(units // step,),
            in_specs=[tile] * (2 + len(branches))
            + [line] * 3
            + [
                pl.BlockSpec((model, step), lambda at, table: (0, at)),
                bias,
                pl.BlockSpec((step, model), lambda at, table: (at, 0)),
            ],
            out_specs=[wide, wide, tile, tile, tile, bias, tile, tile],
            scratch_shapes=[pltpu.VMEM((rows, model), BF16)]
            + [pltpu.VMEM((rows, model), F32)] * 2,
        ),
        out_shape=[struct((rows, units), BF16)] * 2
        + [struct((rows, model), BF16)] * 2
        + [
            struct((rows, model), F32),
            struct((1, units), F32),
            struct((rows, model), BF16),
            struct((rows, model), BF16),
        ],
        compiler_params=streaming,
        cost_estimate=light,
        name="mlp",
    )(
        table,
        block_input,
        out_grad,
        *branches,
        output_bias[None],
        gain[None],
        shift[None],
        up_weight,
        up_bias[None],
        down_weight,
    )


def middle_kernel(count, hidden_ref, grad_ref, *refs):
    parts, refs = refs[:count], refs[count:]
    gain, output_weight, d_hidden_ref, d_branch_ref, d_attn_ref, sums_ref = refs
    unit, inverse = normalize(hidden_ref[...])
    d_mlp = parts[0][...].astype(F32)
    for part in parts[1:]:
        d_mlp += part[...].astype(F32)
    grad = grad_ref[...].astype(F32)
    d_hidden = grad + normalize_back(d_mlp * gain[...], unit, inverse)
    d_hidden_ref[...] = d_hidden
    d_branch = d_hidden.astype(BF16)
    d_branch_ref[...] = d_branch
    d_attn_ref[...] = product(output_weight[...], d_branch, 1, 1).astype(BF16)
    for at, values in enumerate((d_hidden, d_mlp * unit, d_mlp, grad)):
        sums_ref[pl.ds(at, 1), :] = jnp.sum(values, axis=0, keepdims=True)


def middle(hidden, out_grad, parts, gain, output_weight):
    rows, model = hidden.shape
    width = output_weight.shape[0]
    return pl.pallas_call(
        functools.partial(middle_kernel, len(parts)),
        out_shape=[
            struct((rows, model), F32),
            struct((rows, model), BF16),
            struct((width, rows), BF16),
            struct((4, model), F32),
        ],
        compiler_params=streaming,
        cost_estimate=light,
        name="middle",
    )(hidden, out_grad, *parts, gain[None], output_weight)


def mask_rows(piece, chip, crops):
    crop = lax.broadcasted_iota(jnp.int32, (HD, piece.shape[2]), 0)
    segment = piece[chip, pl.ds(seg_row, 16), :].astype(F32)[:1].astype(jnp.int32)
    return jnp.where((crop != segment) & (crop < crops), masked_value, 0.0)


def load_keys(piece, crops, keys, key_t, value_n):
    chips, _, patches = piece.shape
    for chip in range(chips):
        key = piece[chip, pl.ds(HD, HD), :]
        value = piece[chip, pl.ds(2 * HD, HD), :]
        place = pl.ds(chip * patches, patches)
        both = jnp.concatenate([key.astype(F32), mask_rows(piece, chip, crops)], axis=0)
        keys[place, :] = both.T.astype(BF16)
        key_t[:, place] = key
        value_n[place, :] = value.astype(F32).T.astype(BF16)


def masked_query(query_ref, dtype=BF16):
    query = query_ref[0, pl.ds(0, HD), :].astype(F32) * 0.125
    segment = query_ref[0, pl.ds(seg_row, 16), :].astype(F32)[:1].astype(jnp.int32)
    crop = lax.broadcasted_iota(jnp.int32, query.shape, 0)
    onehot = jnp.where(crop == segment, 1.0, 0.0)
    return jnp.concatenate([query, onehot], axis=0).astype(dtype)


def forward_kernel(
    crops, step, query_ref, own, other, raw_ref, out_ref, logsum_ref, key_t, value_n, scores
):
    @pl.when(pl.program_id(0) == 0)
    def _():
        start = 0
        for piece in (own, other):
            chips, _, patches = piece.shape
            for chip in range(chips):
                place = pl.ds(start, patches)
                key = piece[chip, pl.ds(HD, HD), :].astype(F32)
                key_t[:, place] = jnp.concatenate([key, mask_rows(piece, chip, crops)], axis=0).astype(BF16)
                value = piece[chip, pl.ds(2 * HD, HD), :].astype(F32)
                value = jnp.concatenate([value, jnp.ones_like(value)], axis=0)
                value_n[place, :] = value.T.astype(BF16)
                start += patches

    query = masked_query(query_ref, F32).T.astype(BF16)
    count = query.shape[0]
    top = jnp.full((count, 128), masked_value, F32)
    for start in range(0, key_t.shape[1], step):
        block = product(query, key_t[:, pl.ds(start, step)])
        scores[:, pl.ds(start, step)] = block
        for at in range(0, step, 128):
            top = jnp.maximum(top, block[:, at : at + 128])
    top = jnp.max(top, axis=1, keepdims=True)
    accum = jnp.zeros((count, 2 * HD), F32)
    for start in range(0, key_t.shape[1], step):
        weights = jnp.exp(scores[:, pl.ds(start, step)] - top).astype(BF16)
        accum += product(weights, value_n[pl.ds(start, step), :])
    accum = accum.T
    total = accum[HD : HD + 1]
    raw = accum[:HD] / total
    raw_ref[0] = raw
    out_ref[0] = raw.astype(BF16)
    top = jnp.broadcast_to(top, (count, 128)).T[:1]
    logsum_ref[0] = top + jnp.log(total)


def backward_kernel(
    crops,
    before,
    query_ref,
    grad_ref,
    raw_ref,
    logsum_ref,
    *refs,
):
    before_refs, refs = refs[:before], refs[before:]
    piece, (dquery_ref, sums_ref, keys, key_t, value_n, sums) = refs[0], refs[-6:]
    group = pl.program_id(0)

    @pl.when(group == 0)
    def _():
        load_keys(piece, crops, keys, key_t, value_n)
        sums[...] = jnp.zeros_like(sums)

    query = masked_query(query_ref)
    grad = grad_ref[0]
    grad_wide = grad.astype(F32)
    delta = jnp.sum(grad_wide * raw_ref[0], axis=0, keepdims=True)
    scaled = query_ref[0, pl.ds(0, HD), :].astype(F32) * 0.125
    zero = jnp.zeros_like(scaled)
    query_side = jnp.concatenate([scaled, zero], axis=0).T.astype(BF16)
    grad_side = jnp.concatenate([zero, grad_wide], axis=0).T.astype(BF16)
    probs = jnp.exp(product(keys[...], query) - logsum_ref[0])
    dprobs = product(value_n[...], grad)
    dscores = (probs * (dprobs - delta)).astype(BF16)
    sums[...] += product(dscores, query_side) + product(probs.astype(BF16), grad_side)
    dquery = product(key_t[...], dscores) * 0.125
    for ref in before_refs:
        dquery = ref[0] + dquery
    dquery_ref[0] = dquery.astype(dquery_ref.dtype)

    @pl.when(group == pl.num_programs(0) - 1)
    def _():
        chips, _, patches = sums_ref.shape
        for chip in range(chips):
            sums_ref[chip] = sums[pl.ds(chip * patches, patches), :].T.astype(sums_ref.dtype)


def key_step(count):
    return 1024 if count % 1024 == 0 else 256


def query_spec(rows, patches):
    return pl.BlockSpec((1, rows, patches), lambda group: (group, 0, 0))


def attention_forward(queries, own, other, crops):
    groups, _, patches = queries.shape
    count = 2 * own.shape[0] * own.shape[2]
    return pl.pallas_call(
        functools.partial(forward_kernel, crops, key_step(count)),
        grid=(groups,),
        in_specs=[
            query_spec(payload_rows, patches),
            whole_spec(own.shape),
            whole_spec(other.shape),
        ],
        out_specs=[query_spec(HD, patches), query_spec(HD, patches), query_spec(1, patches)],
        out_shape=[
            struct((groups, HD, patches), F32),
            struct((groups, HD, patches), BF16),
            struct((groups, 1, patches), F32),
        ],
        scratch_shapes=[
            pltpu.VMEM((2 * HD, count), BF16),
            pltpu.VMEM((count, 2 * HD), BF16),
            pltpu.VMEM((patches, count), F32),
        ],
        compiler_params=streaming,
        cost_estimate=light,
        name="attention_forward",
    )(queries, own, other)


def backward_piece(queries, grads, raw, logsum, before, keys, earlier, index, pieces, crops, dtypes):
    groups, _, patches = queries.shape
    chips = keys.shape[0] // pieces
    count = chips * keys.shape[2]
    sums_shape = (chips, 2 * HD, keys.shape[2])
    return pl.pallas_call(
        functools.partial(backward_kernel, crops, len(before)),
        grid=(groups,),
        in_specs=[
            query_spec(payload_rows, patches),
            query_spec(HD, patches),
            query_spec(HD, patches),
            query_spec(1, patches),
        ]
        + [query_spec(HD, patches)] * len(before)
        + [pl.BlockSpec((chips,) + keys.shape[1:], lambda group: (index, 0, 0))]
        + [pl.BlockSpec(memory_space=pl.ANY)] * len(earlier),
        out_specs=[
            query_spec(HD, patches),
            pl.BlockSpec(sums_shape, lambda group: (index, 0, 0)),
        ],
        out_shape=[
            struct((groups, HD, patches), dtypes[0]),
            struct((keys.shape[0],) + sums_shape[1:], dtypes[1]),
        ],
        input_output_aliases={5 + len(before): 1} if earlier else {},
        scratch_shapes=[
            pltpu.VMEM((count, 2 * HD), BF16),
            pltpu.VMEM((HD, count), BF16),
            pltpu.VMEM((count, HD), BF16),
            pltpu.VMEM((count, 2 * HD), F32),
        ],
        compiler_params=params,
        cost_estimate=light,
        name="attention_backward",
    )(queries, grads, raw, logsum, *before, keys, *earlier)


def swap_cores(values):
    return lax.ppermute(values, "core", [(0, 1), (1, 0)])


def to_heads(blocks):
    return lax.all_to_all(blocks, "chip", 0, 0, tiled=True)


def scatter_queries(values, heads, split):
    rows, patches = values.shape[0] // heads, values.shape[1]
    if split == 1:
        return to_heads(values.reshape(heads, rows, patches))
    part = patches // split
    blocks = values.reshape(heads, rows, split, part).transpose(0, 2, 1, 3)
    moved = to_heads(blocks.reshape(heads * split, rows, part))
    width = min(256, moved.shape[0] * part)
    joined = moved.transpose(1, 0, 2).reshape(rows, -1, width)
    return joined.transpose(1, 0, 2)


def gather_queries(values, heads, split, patches):
    rows = values.shape[1]
    if split == 1:
        return to_heads(values).reshape(heads * rows, patches)
    part = patches // split
    joined = values.transpose(1, 0, 2).reshape(rows, heads * split, part)
    moved = to_heads(joined.transpose(1, 0, 2)).reshape(heads, split, rows, part)
    return moved.transpose(0, 2, 1, 3).reshape(heads * rows, patches)


def across_heads(part):
    if lax.axis_size("head") == 2:
        return [part, lax.ppermute(part, "head", [(0, 1), (1, 0)])]
    return [lax.psum(part, "head")]


def ring_pairs(direction):
    chips = lax.axis_size("chip")
    order = list(range(0, chips, 2)) + list(range(chips - 1, 0, -2))
    return [(order[at], order[(at + direction) % chips]) for at in range(chips)]


def ring_table():
    chips, chip = lax.axis_size("chip"), lax.axis_index("chip")
    place = jnp.where(chip % 2 == 0, chip // 2, chips - 1 - chip // 2)
    steps = jnp.arange(2 * chips + 2, dtype=jnp.int32)
    places = (place + steps) % chips
    there = jnp.where(places < chips // 2, 2 * places, 2 * (chips - 1 - places) + 1)
    table = jnp.where(steps < chips, places, there)
    table = jnp.where(steps == 2 * chips, lax.axis_index("core"), table)
    return jnp.where(steps == 2 * chips + 1, lax.axis_index("head"), table).astype(jnp.int32)


def visit(streams, values):
    states, values = lax.optimization_barrier(([stream.state for stream in streams], values))
    for stream, state in zip(streams, states):
        stream.advance(state)
    ready, values = lax.optimization_barrier(([stream.ready for stream in streams], values))
    for stream, blocks in zip(streams, ready):
        stream.send(blocks)
    return values


def join_kernel(*refs):
    start = 0
    for block in refs[:-1]:
        refs[-1][pl.ds(start, block.shape[0]), :] = block[...]
        start += block.shape[0]


def join(blocks):
    rows = sum(block.shape[0] for block in blocks)
    return pl.pallas_call(
        join_kernel,
        out_shape=struct((rows, blocks[0].shape[1]), blocks[0].dtype),
        compiler_params=streaming,
        name="join",
    )(*blocks)


def halves_kernel(left, right, left_ref, right_ref):
    left_ref[...] = left[...]
    right_ref[...] = right[...]


def halves(left, right):
    rows, columns = left.shape
    if rows % 16 or columns % 256:
        return [left[:, : columns // 2], right[:, columns // 2 :]]
    out = pl.BlockSpec((rows, columns // 2), lambda at: (0, 0))
    return pl.pallas_call(
        halves_kernel,
        grid=(1,),
        in_specs=[out, pl.BlockSpec((rows, columns // 2), lambda at: (0, 1))],
        out_specs=[out, out],
        out_shape=[struct((rows, columns // 2), left.dtype)] * 2,
        compiler_params=streaming,
        name="halves",
    )(left, right)


class Gather:
    def __init__(self, block, swap=False, take=None):
        self.reach, self.swap, self.take = lax.axis_size("chip") // 2, swap, take
        self.blocks, self.pairs, self.count = [], [], 0
        self.new, self.outputs = [0], []
        self.ready = [block]

    def send(self, ready):
        new = list(zip(self.new, ready))
        self.blocks += new
        self.new = new
        self.count += 1
        sides = ready if len(ready) > 1 else ready * 2
        if self.count == self.reach:
            sides = halves(*sides)
        flying = []
        if self.count <= self.reach:
            flying = [
                lax.ppermute(block, "chip", ring_pairs(direction))
                for block, direction in zip(sides, (1, -1))
            ]
        if self.swap and ready:
            pairs = [(step, block, swap_cores(block)) for step, block in new]
            self.pairs += pairs
            self.outputs = self.take(self.outputs, pairs)
        self.state = (flying, self.outputs)

    def advance(self, state):
        arrived, self.outputs = state
        self.new = [-self.count, self.count]
        if arrived and self.count == self.reach:
            arrived, self.new = [jnp.concatenate(arrived, axis=1)], [self.count]
        self.ready = arrived

    def busy(self):
        return bool(self.state[0])


def add_kernel(wanted, count, _, *refs):
    outputs, refs = refs[-count:], list(refs[:-count])
    keep_in, far_in = refs.pop(0), refs.pop(0)
    for starts, output in zip(wanted, outputs):
        near, far = refs.pop(0), refs.pop(0)
        total = product(near[...], keep_in[...], 0, 0) + product(far[...], far_in[...], 0, 0)
        if len(outputs) > len(wanted):
            for at, output in enumerate(outputs):
                columns = output.shape[1]
                output[...] = total[:, at * columns : at * columns + columns].astype(BF16)
            return
        output[...] = total.astype(BF16)
        arrived = [refs.pop(0) for _ in starts]
        for start in sorted(set(starts)):
            parts = [part for part, at in zip(arrived, starts) if at == start]
            columns = slice(start, start + parts[0].shape[1])
            summed = total[:, columns]
            for part in parts:
                summed += part[...].astype(F32)
            output[:, columns] = summed.astype(BF16)


class Reduce:
    def __init__(self, keep, far, keep_in, far_in, table):
        self.chips, self.table = lax.axis_size("chip"), table
        self.operands, self.sides = (keep, far), (keep_in, far_in)
        self.units = keep.shape[1] // self.chips
        self.tiled = self.units % 128 == 0
        self.left, self.rest = self.chips // 2, None
        blocks = self.add([(self.left, [])], True)
        self.send(blocks if len(blocks) > 1 else halves(blocks[0], blocks[0]))

    def send(self, ready):
        self.left -= 1
        self.state = [
            lax.ppermute(block, "chip", ring_pairs(direction))
            for block, direction in zip(ready, (1, -1))
        ]

    def advance(self, state):
        half = self.sides[0].shape[1] // 2
        ahead, behind = state
        first = 0 if ahead.shape[1] != half else half
        self.ready = self.add([(self.left, [(ahead, 0)]), (-self.left, [(behind, first)])])

    def arrive(self, values):
        self.state, values = lax.optimization_barrier((self.state, values))
        return values

    def finish(self):
        ahead, behind = self.state
        return self.add([(0, [(ahead, 0), (behind, 0)])])[0]

    def add(self, wanted, split=False):
        (rows, model), units, chips = self.sides[0].shape, self.units, self.chips
        if not self.tiled:
            sums = []
            for step, parts in wanted:
                start = self.table[step % chips] * units
                total = jnp.zeros((units, model), F32)
                for operand, side in zip(self.operands, self.sides):
                    block = lax.dynamic_slice_in_dim(operand, start, units, 1)
                    total += product(block, side, 0, 0)
                for part, start in parts:
                    total = total.at[:, start : start + part.shape[1]].add(part.astype(F32))
                sums.append(total.astype(BF16))
            return sums
        side = pl.BlockSpec((rows, model), lambda at, table: (0, 0))
        whole = pl.BlockSpec((units, model), lambda at, table: (0, 0))
        specs, arrays = [side] * 2, list(self.sides)
        for step, parts in wanted:
            block = pl.BlockSpec(
                (rows, units), lambda at, table, step=step % chips: (0, table[step])
            )
            specs += [block] * 2
            specs += [pl.BlockSpec(part.shape, lambda at, table: (0, 0)) for part, _ in parts]
            arrays += list(self.operands) + [part for part, _ in parts]
        starts = [[start for _, start in parts] for _, parts in wanted]
        shapes = [struct((units, model), BF16)] * len(wanted)
        if split:
            shapes = [struct((units, model // 2), BF16)] * 2
        return pl.pallas_call(
            functools.partial(add_kernel, starts, len(shapes)),
            grid_spec=pltpu.PrefetchScalarGridSpec(
                num_scalar_prefetch=1,
                grid=(1,),
                in_specs=specs,
                out_specs=[pl.BlockSpec(shape.shape, lambda at, table: (0, 0)) for shape in shapes],
            ),
            out_shape=shapes,
            compiler_params=streaming,
            cost_estimate=light,
            name="ring_add",
        )(self.table, *arrays)

    def place(self, outputs, pairs):
        units, chips, model = self.units, self.chips, self.sides[0].shape[1]
        size, extra = self.size, self.extra
        shapes = [struct((chips * units, model), F32), struct((model, chips * units), F32)]
        if not self.tiled:
            outputs = outputs or [jnp.zeros(shape.shape, F32) for shape in shapes]
            down, up = outputs
            is_down = self.table[2 * chips] == 0
            for step, near, far in pairs:
                start = self.table[step % chips] * units
                near, far = near[:units], far[:units]
                first = jnp.where(is_down, near, far).astype(F32)
                second = jnp.where(is_down, far, near).astype(F32).T
                down = lax.dynamic_update_slice_in_dim(down, first, start, 0)
                up = lax.dynamic_update_slice_in_dim(up, second, start, 1)
            return [down, up]
        first = pairs[0][0] % chips
        stride = pairs[-1][0] % chips - first
        block = pl.BlockSpec(pairs[0][1].shape, lambda at, table: (0, 0))

        def place(at, table):
            return table[first + at * stride]

        def chip(at, table):
            return table[chips + first + at * stride]

        column = pl.BlockSpec(
            (model, 2 * HD), lambda at, table: (0, lax.div(chip(at, table), 2))
        )
        columns = [column] * (3 if outputs else 0)
        heads = [[first, first + stride][at] + chips for at in range(len(pairs))]
        return pl.pallas_call(
            functools.partial(place_kernel, heads, (units, size, extra)),
            grid_spec=pltpu.PrefetchScalarGridSpec(
                num_scalar_prefetch=1,
                grid=(len(pairs),),
                in_specs=[pl.BlockSpec(memory_space=pl.ANY)] * (len(outputs) - len(columns))
                + columns
                + [block] * (2 * len(pairs)),
                out_specs=[
                    pl.BlockSpec((units, model), lambda at, table: (place(at, table), 0)),
                    pl.BlockSpec((model, units), lambda at, table: (0, place(at, table))),
                    pl.BlockSpec((2, 1, extra, model), lambda at, table: (0, chip(at, table), 0, 0)),
                    pl.BlockSpec(
                        (1, 2, small_rows, model), lambda at, table: (chip(at, table), 0, 0, 0)
                    ),
                ]
                + [column] * 3,
            ),
            out_shape=shapes
            + [
                struct((2, chips, extra, model), F32),
                struct((chips, 2, small_rows, model), F32),
            ]
            + [struct((model, chips * HD), F32)] * 3,
            input_output_aliases={1 + at: at for at in range(len(outputs))},
            compiler_params=streaming,
            cost_estimate=light,
            name="place",
        )(self.table, *outputs, *[pair[1] for pair in pairs], *[pair[2] for pair in pairs])


def place_kernel(heads, sizes, table, *refs):
    count = len(heads)
    refs, (down, up, weight, small), projections = refs[:-7], refs[-7:-3], refs[-3:]
    blocks, refs = refs[-2 * count :], refs[: -2 * count]
    core = table[table.shape[0] - 2]
    units, size, extra = sizes
    rows = [pl.ds(0, units), pl.ds(units, size), pl.ds(units + size, extra)]
    rows.append(pl.ds(units + size + extra, small_rows))

    def put(first, second, head):
        down[...] = first[rows[0], :].astype(F32)
        up[...] = second[rows[0], :].astype(F32).T
        for side, block in ((0, first), (1, second)):
            weight[side, 0] = block[rows[2], :].astype(F32)
            small[0, side] = block[rows[3], :].astype(F32)
        both = jnp.concatenate([first[rows[1], :], second[rows[1], :]], axis=0)
        for at, output in enumerate(projections):
            part = both[at * HD : at * HD + HD].astype(F32)
            part = jnp.concatenate([part, part], axis=0).T
            if refs:
                mine = lax.broadcasted_iota(jnp.int32, part.shape, 1) // HD == head % 2
                part = jnp.where(mine, part, refs[at - 3][...])
            output[...] = part

    for at in range(count):
        near, far, head = blocks[at], blocks[count + at], table[heads[at]]
        here = pl.program_id(0) == at
        pl.when(here & (core == 0))(functools.partial(put, near, far, head))
        pl.when(here & (core != 0))(functools.partial(put, far, near, head))


def head_gradient_kernel(steps, chips, table, query_ref, key_value_ref, *refs):
    parts, out_ref = refs[:-1], refs[-1]
    patches = query_ref.shape[2]
    for at, part in enumerate(parts):

        @pl.when(pl.program_id(0) == at)
        def _(part=part):
            total = jnp.zeros(out_ref.shape, F32)
            for index, step in enumerate(steps):
                chip = table[chips + step % chips]
                grads = jnp.concatenate([query_ref[chip], key_value_ref[chip]], axis=0)
                total += product(grads, part[pl.ds(index * patches, patches), :])
            out_ref[...] = total.astype(BF16)


def head_gradient(dquery, key_value, parts, steps, table):
    chips, rows, _ = dquery.shape
    columns = parts[0].shape[1]

    def column(at, table):
        mine = table[2 * chips + 1] if len(parts) > 1 else 0
        return (0, jnp.where(at == 0, mine, 1 - mine))

    return pl.pallas_call(
        functools.partial(head_gradient_kernel, steps, chips),
        grid_spec=pltpu.PrefetchScalarGridSpec(
            num_scalar_prefetch=1,
            grid=(len(parts),),
            in_specs=[
                pl.BlockSpec(array.shape, lambda at, table, rank=array.ndim: (0,) * rank)
                for array in (dquery, key_value, *parts)
            ],
            out_specs=pl.BlockSpec((3 * rows, columns), column),
        ),
        out_shape=struct((3 * rows, columns * len(parts)), BF16),
        compiler_params=streaming,
        cost_estimate=light,
        name="head_gradient",
    )(table, dquery, key_value, *parts)


def core_half(values, axis, side):
    size = values.shape[axis] // 2
    return lax.dynamic_slice_in_dim(values, side * size, size, axis)


def share_halves(values, axis):
    core = lax.axis_index("core")
    return core_half(values, axis, core), swap_cores(core_half(values, axis, 1 - core))


def local(
    block_input,
    out_grad,
    segments,
    lead_steps,
    gain_attn,
    shift_attn,
    lead_weight,
    query_weight,
    key_weight,
    value_weight,
    output_weight,
    output_bias,
    gain_mlp,
    shift_mlp,
    up_weight,
    up_bias,
    down_weight,
    down_bias,
):
    rows, model = block_input.shape
    heads = query_weight.shape[1] // HD
    width = heads * HD
    chips, core = lax.axis_size("chip"), lax.axis_index("core")
    split = chips // heads
    crops = lead_steps.shape[0]
    table = ring_table()
    weights = (query_weight, key_weight, value_weight)
    cut = model // 2 if lax.axis_size("head") == 2 else model
    payload, attn_in, attn_in_cut = project(
        table, cut, block_input, segments, lead_steps, gain_attn, shift_attn, lead_weight, weights
    )
    if split == 1:
        own = to_heads(payload)
        queries = own
    else:
        queries = scatter_queries(payload.reshape(-1, rows), heads, split)
        own = to_heads(jnp.repeat(payload, split, axis=0))
    own, attn_in_cut = lax.optimization_barrier((own, attn_in_cut))
    inputs = Gather(attn_in_cut)
    inputs.send(inputs.ready)
    other = swap_cores(own)
    raw, out, logsum = attention_forward(queries, own, other, crops)
    inputs.state, out = lax.optimization_barrier((inputs.state, out))
    attn_out = gather_queries(out, heads, split, rows)
    attn_out = visit([inputs], attn_out)
    branches = across_heads(product(attn_out, output_weight, 0, 0).astype(BF16))
    visit([inputs], ())
    keep, give, keep_in, give_in, hidden, dup_bias, mlp_part, d_mlp_part = mlp(
        table,
        block_input,
        out_grad,
        branches,
        output_bias,
        gain_mlp,
        shift_mlp,
        up_weight,
        up_bias,
        down_weight,
    )
    keep, give, keep_in, give_in, d_mlp_part = visit(
        [inputs], (keep, give, keep_in, give_in, d_mlp_part)
    )
    d_mlp = across_heads(d_mlp_part)
    ring = Reduce(keep, swap_cores(give), keep_in, swap_cores(give_in), table)
    mlp_part, d_mlp = lax.optimization_barrier((mlp_part, d_mlp))
    d_hidden, d_branch, d_attn, sums = middle(hidden, out_grad, d_mlp, gain_mlp, output_weight)
    grads = scatter_queries(d_attn, heads, split)
    d_branch, mlp_part = visit([ring, inputs], (d_branch, mlp_part))
    while inputs.busy():
        visit([inputs], ())
    mlp_out = across_heads(mlp_part)
    steps, inputs = zip(*inputs.blocks)
    parts = [join(inputs)]
    if cut != model:
        parts = across_heads(parts[0])
    out_near, out_far = share_halves(attn_out, 0)
    doutput = product(out_near, d_branch) + product(out_far, swap_cores(d_branch))
    doutput = doutput.astype(BF16).reshape(chips, -1, model)
    grads, doutput = visit([ring], (grads, doutput))
    doutput = to_heads(doutput)
    *dquery, far_sums = backward_piece(
        queries, grads, raw, logsum, [], other, [], 0, 1, crops, (F32, BF16)
    )
    grads, dquery, far_sums = visit([ring], (grads, dquery, far_sums))
    far_sums = swap_cores(far_sums)
    *dquery, near_sums = backward_piece(
        queries, grads, raw, logsum, dquery, own, [], 0, 1, crops, (BF16, F32)
    )
    near_sums, dquery = ring.arrive((near_sums, dquery))
    (dquery,) = dquery
    key_value = (near_sums + far_sums.astype(F32)).astype(BF16)
    doutput, key_value = lax.optimization_barrier((doutput, key_value))
    doutput = jnp.sum(doutput.astype(F32), axis=0)
    small = jnp.concatenate([sums.reshape(-1), dup_bias[0]])
    small = jnp.pad(small, (0, small_rows * model - small.shape[0])).reshape(small_rows, model)
    doutput = jnp.concatenate([doutput, small], axis=0).astype(BF16)
    if split == 1:
        moved = to_heads(jnp.concatenate([dquery, key_value], axis=1))
        projections = head_gradient(dquery, key_value, parts, steps, table)
        near, far = share_halves(projections, 0)
        projections = (near.astype(F32) + far.astype(F32)).astype(BF16)
        size = projections.shape[0]
        blocks = jnp.concatenate([projections, doutput], axis=0)
        dquery, dkey, dvalue = (
            moved[:, at * HD : at * HD + HD].reshape(width, rows) for at in range(3)
        )
    else:
        dquery = gather_queries(dquery, heads, split, rows)
        moved = to_heads(key_value).reshape(heads, split, 2 * HD, rows).astype(F32)
        moved = jnp.sum(moved, axis=1).astype(BF16)
        dkey, dvalue = (moved[:, at * HD : at * HD + HD].reshape(width, rows) for at in range(2))
        size, blocks = 0, doutput
        projections = [
            lax.psum(product(attn_in, grad, 0, 1).astype(BF16), ("chip", "core")).astype(F32)
            for grad in (dquery, dkey, dvalue)
        ]
    total = ring.finish()
    start = total.shape[0]
    ring.size, ring.extra = size, blocks.shape[0] - size - small_rows
    gathered = Gather(jnp.concatenate([total, blocks], axis=0), True, ring.place)
    gathered.send(gathered.ready)
    d_part = (
        product(dquery, query_weight, 0, 1)
        + product(dkey, key_weight, 0, 1)
        + product(dvalue, value_weight, 0, 1)
    )
    d_in = across_heads(d_part.astype(BF16))
    unit_attn, inverse_attn = normalize(block_input.astype(F32))
    onehot = (segments[:, None] == jnp.arange(crops, dtype=jnp.int32)[None, :]).astype(F32)
    lead = jnp.sum(onehot * lead_steps.astype(F32)[None, :], axis=1) / 12.0
    ends = jnp.stack(
        [
            jnp.sum(d_part * unit_attn, axis=0),
            jnp.sum(d_part, axis=0),
            jnp.sum(lead[:, None] * d_part, axis=0),
        ]
    )
    ends = jnp.pad(ends.reshape(-1, 128), ((0, -ends.size // 128 % 16), (0, 0))).astype(BF16)
    everyone = ("chip", "core", "head")
    ends = jnp.broadcast_to(ends, (lax.axis_size(everyone),) + ends.shape)
    ends = lax.all_to_all(ends, everyone, 0, 0, tiled=True)
    ends = visit([gathered], ends)
    ends = jnp.sum(ends.astype(F32), axis=0).reshape(-1)[: 3 * model].reshape(3, model)
    ends, mlp_out = visit([gathered], (ends, mlp_out))
    block_output = hidden + down_bias
    for part in mlp_out:
        block_output += part.astype(F32)
    block_output = block_output.astype(BF16)
    d_in, block_output = visit([gathered], (d_in, block_output))
    d_in = functools.reduce(jnp.add, (part.astype(F32) for part in d_in))
    input_grad = (d_hidden + normalize_back(d_in * gain_attn, unit_attn, inverse_attn)).astype(
        BF16
    )
    while gathered.busy():
        input_grad = visit([gathered], input_grad)
    ddown_weight, dup_weight, *rest = gathered.outputs
    if split == 1:
        doutput_weight, small, *projections = rest
        doutput_weight = doutput_weight.reshape(width, model)
    if split != 1:
        blocks = jnp.zeros((2, chips) + blocks.shape, F32)
        for step, near, far in gathered.pairs:
            for side, block in ((core, near[start:]), (1 - core, far[start:])):
                at = (side, table[chips + step % chips], 0, 0)
                block = block[None, None].astype(F32)
                blocks = lax.dynamic_update_slice(blocks, block, at)
        doutput_weight = blocks[:, :, :-small_rows].reshape(width, model)
        small = blocks[:, :, -small_rows:]
    small = jnp.sum(small, axis=(0, 1))
    dup_bias = small[4:].reshape(-1)[: dup_bias.shape[1]]
    return (
        block_output,
        input_grad,
        ends[0],
        ends[1],
        ends[2],
        *projections,
        doutput_weight,
        *small[:3],
        dup_weight,
        dup_bias,
        ddown_weight,
        small[3],
    )


def solution(mesh):
    bands, halves = mesh.shape["band"], mesh.shape["head"]
    inner = Mesh(mesh.devices.reshape(bands // 2, 2, halves), ("chip", "core", "head"))
    band = ("chip", "core")
    rows, columns, split_rows = P(band, None), P(None, "head"), P("head", None)
    return jax.shard_map(
        local,
        mesh=inner,
        in_specs=(
            rows,
            rows,
            P(band),
            P(),
            P(),
            P(),
            P(),
            columns,
            columns,
            columns,
            split_rows,
            P(),
            P(),
            P(),
            columns,
            P("head"),
            split_rows,
            P(),
        ),
        out_specs=(
            rows,
            rows,
            P(),
            P(),
            P(),
            columns,
            columns,
            columns,
            split_rows,
            P(),
            P(),
            P(),
            columns,
            P("head"),
            split_rows,
            P(),
        ),
        check_vma=False,
    )
```

```python
import functools
import math

import jax
import jax.numpy as jnp
from jax import lax
from jax.experimental import pallas as pl
from jax.experimental.pallas import tpu as pltpu
from jax.sharding import Mesh, PartitionSpec as P

HD = 64
F32 = jnp.float32
BF16 = jnp.bfloat16
eps = 1e-05
masked_value = -1e30
seg_row = 3 * HD
payload_rows = 3 * HD + 16
small_rows = 16
params = pltpu.CompilerParams(vmem_limit_bytes=48 * 2**20)
streaming = pltpu.CompilerParams(vmem_limit_bytes=60 * 2**20)


def normalize(values):
    centred = values - jnp.mean(values, axis=-1, keepdims=True)
    inverse = lax.rsqrt(jnp.mean(centred * centred, axis=-1, keepdims=True) + eps)
    return (centred * inverse, inverse)


def normalize_back(grad_unit, unit, inverse):
    return inverse * (
        grad_unit
        - jnp.mean(grad_unit, axis=-1, keepdims=True)
        - unit * jnp.mean(grad_unit * unit, axis=-1, keepdims=True)
    )


def product(first, second, first_axis=1, second_axis=0):
    return lax.dot_general(
        first,
        second,
        (((first_axis,), (second_axis,)), ((), ())),
        preferred_element_type=jnp.float32,
    )


def struct(shape, dtype):
    return jax.ShapeDtypeStruct(shape, dtype)


def whole_spec(shape):
    return pl.BlockSpec(shape, lambda *at: (0,) * len(shape))


light = pl.CostEstimate(flops=1, bytes_accessed=1, transcendentals=0)


def project_kernel(
    table, input_ref, segment_ref, steps_ref, gain, shift, lead_weight, *refs
):
    weights, (payload_ref, attn_in_ref, cut_ref) = refs[:3], refs[3:]
    rows = input_ref.shape[0]

    @pl.when(pl.program_id(0) == 0)
    def _():
        unit, _ = normalize(input_ref[...].astype(F32))
        crops = steps_ref.shape[0]
        crop = lax.broadcasted_iota(jnp.int32, (crops, rows), 0)
        steps = jnp.zeros((crops, rows), jnp.int32)
        for at in range(crops):
            steps = jnp.where(crop == at, steps_ref[at], steps)
        steps = jnp.where(crop == segment_ref[...], steps, 0).astype(F32)
        lead = product(steps, jnp.ones((crops, 128), F32), 0, 0)[:, :1] / 12.0
        attn_in = unit * gain[...] + shift[...] + lead * lead_weight[...]
        attn_in = attn_in.astype(BF16)
        attn_in_ref[...] = attn_in
        columns = cut_ref.shape[1]
        first = table[table.shape[0] - 1] % (attn_in.shape[1] // columns) == 0
        cut_ref[...] = jnp.where(first, attn_in[:, :columns], attn_in[:, -columns:])

    for at, weight in enumerate(weights):
        part = product(attn_in_ref[...], weight[...]).T.astype(BF16)
        for head in range(2):
            payload_ref[head, pl.ds(at * HD, HD), :] = part[head * HD : head * HD + HD]
    segment = jnp.broadcast_to(segment_ref[...].astype(F32), (16, rows)).astype(BF16)
    for head in range(2):
        payload_ref[head, pl.ds(seg_row, 16), :] = segment


def project(table, cut, block_input, segments, lead_steps, gain, shift, lead_weight, weights):
    rows, model = block_input.shape
    heads = weights[0].shape[1] // HD
    line = whole_spec((1, model))
    column = pl.BlockSpec((model, 2 * HD), lambda at, table: (0, at))
    return pl.pallas_call(
        project_kernel,
        grid_spec=pltpu.PrefetchScalarGridSpec(
            num_scalar_prefetch=1,
            grid=(heads // 2,),
            in_specs=[
                whole_spec(block_input.shape),
                whole_spec((1, rows)),
                pl.BlockSpec(memory_space=pltpu.SMEM),
            ]
            + [line] * 3
            + [column] * 3,
            out_specs=[
                pl.BlockSpec((2, payload_rows, rows), lambda at, table: (at, 0, 0)),
                whole_spec((rows, model)),
                whole_spec((rows, cut)),
            ],
        ),
        out_shape=[
            struct((heads, payload_rows, rows), BF16),
            struct((rows, model), BF16),
            struct((rows, cut), BF16),
        ],
        compiler_params=streaming,
        cost_estimate=light,
        name="project",
    )(table, block_input, segments[None], lead_steps, gain[None], shift[None], lead_weight[None], *weights)


def mlp_kernel(count, core_ref, input_ref, grad_ref, *refs):
    branches, refs = refs[:count], refs[count:]
    output_bias, gain, shift, up_weight, up_bias, down_weight = refs[:6]
    keep_ref, give_ref, keep_in_ref, give_in_ref, hidden_ref, bias_ref, forward_ref, back_ref = refs[
        6:14
    ]
    mlp_in_ref, forward, back = refs[14:]
    at = pl.program_id(0)
    is_down = core_ref[core_ref.shape[0] - 2] == 0

    @pl.when(at == 0)
    def _():
        hidden = input_ref[...].astype(F32) + output_bias[...]
        for branch in branches:
            hidden += branch[...].astype(F32)
        hidden_ref[...] = hidden
        unit, _ = normalize(hidden)
        mlp_in = (unit * gain[...] + shift[...]).astype(BF16)
        mlp_in_ref[...] = mlp_in
        keep_in_ref[...] = jnp.where(is_down, grad_ref[...], mlp_in)
        give_in_ref[...] = jnp.where(is_down, mlp_in, grad_ref[...])
        forward[...] = jnp.zeros_like(forward)
        back[...] = jnp.zeros_like(back)

    upper = product(mlp_in_ref[...], up_weight[...]) + up_bias[...]
    share = 0.5 + 0.5 * lax.erf(upper * math.sqrt(0.5))
    slope = share + upper * (jnp.exp(upper * upper * -0.5) * (1.0 / math.sqrt(2.0 * math.pi)))
    active = (upper * share).astype(BF16)
    d_active = product(grad_ref[...], down_weight[...], 1, 1)
    d_upper = (d_active * slope).astype(BF16)
    keep_ref[...] = jnp.where(is_down, active, d_upper)
    give_ref[...] = jnp.where(is_down, d_upper, active)
    bias_ref[...] = jnp.sum(d_upper.astype(F32), axis=0, keepdims=True)
    forward[...] += product(active, down_weight[...])
    back[...] += product(d_upper, up_weight[...], 1, 1)

    @pl.when(at == pl.num_programs(0) - 1)
    def _():
        forward_ref[...] = forward[...].astype(BF16)
        back_ref[...] = back[...].astype(BF16)


def mlp(
    table, block_input, out_grad, branches, output_bias, gain, shift, up_weight, up_bias, down_weight
):
    rows, model = block_input.shape
    units = up_weight.shape[1]
    step = math.gcd(units, 512)
    tile, line = whole_spec((rows, model)), whole_spec((1, model))
    wide = pl.BlockSpec((rows, step), lambda at, table: (0, at))
    bias = pl.BlockSpec((1, step), lambda at, table: (0, at))
    return pl.pallas_call(
        functools.partial(mlp_kernel, len(branches)),
        grid_spec=pltpu.PrefetchScalarGridSpec(
            num_scalar_prefetch=1,
            grid=(units // step,),
            in_specs=[tile] * (2 + len(branches))
            + [line] * 3
            + [
                pl.BlockSpec((model, step), lambda at, table: (0, at)),
                bias,
                pl.BlockSpec((step, model), lambda at, table: (at, 0)),
            ],
            out_specs=[wide, wide, tile, tile, tile, bias, tile, tile],
            scratch_shapes=[pltpu.VMEM((rows, model), BF16)]
            + [pltpu.VMEM((rows, model), F32)] * 2,
        ),
        out_shape=[struct((rows, units), BF16)] * 2
        + [struct((rows, model), BF16)] * 2
        + [
            struct((rows, model), F32),
            struct((1, units), F32),
            struct((rows, model), BF16),
            struct((rows, model), BF16),
        ],
        compiler_params=streaming,
        cost_estimate=light,
        name="mlp",
    )(
        table,
        block_input,
        out_grad,
        *branches,
        output_bias[None],
        gain[None],
        shift[None],
        up_weight,
        up_bias[None],
        down_weight,
    )


def middle_kernel(count, hidden_ref, grad_ref, *refs):
    parts, refs = refs[:count], refs[count:]
    gain, output_weight, d_hidden_ref, d_branch_ref, d_attn_ref, sums_ref = refs
    unit, inverse = normalize(hidden_ref[...])
    d_mlp = parts[0][...].astype(F32)
    for part in parts[1:]:
        d_mlp += part[...].astype(F32)
    grad = grad_ref[...].astype(F32)
    d_hidden = grad + normalize_back(d_mlp * gain[...], unit, inverse)
    d_hidden_ref[...] = d_hidden
    d_branch = d_hidden.astype(BF16)
    d_branch_ref[...] = d_branch
    d_attn_ref[...] = product(output_weight[...], d_branch, 1, 1).astype(BF16)
    for at, values in enumerate((d_hidden, d_mlp * unit, d_mlp, grad)):
        sums_ref[pl.ds(at, 1), :] = jnp.sum(values, axis=0, keepdims=True)


def middle(hidden, out_grad, parts, gain, output_weight):
    rows, model = hidden.shape
    width = output_weight.shape[0]
    return pl.pallas_call(
        functools.partial(middle_kernel, len(parts)),
        out_shape=[
            struct((rows, model), F32),
            struct((rows, model), BF16),
            struct((width, rows), BF16),
            struct((4, model), F32),
        ],
        compiler_params=streaming,
        cost_estimate=light,
        name="middle",
    )(hidden, out_grad, *parts, gain[None], output_weight)


def mask_rows(piece, chip, crops):
    crop = lax.broadcasted_iota(jnp.int32, (HD, piece.shape[2]), 0)
    segment = piece[chip, pl.ds(seg_row, 16), :].astype(F32)[:1].astype(jnp.int32)
    return jnp.where((crop != segment) & (crop < crops), masked_value, 0.0)


def load_keys(piece, crops, keys, key_t, value_n):
    chips, _, patches = piece.shape
    for chip in range(chips):
        key = piece[chip, pl.ds(HD, HD), :]
        value = piece[chip, pl.ds(2 * HD, HD), :]
        place = pl.ds(chip * patches, patches)
        both = jnp.concatenate([key.astype(F32), mask_rows(piece, chip, crops)], axis=0)
        keys[place, :] = both.T.astype(BF16)
        key_t[:, place] = key
        value_n[place, :] = value.astype(F32).T.astype(BF16)


def masked_query(query_ref, dtype=BF16):
    query = query_ref[0, pl.ds(0, HD), :].astype(F32) * 0.125
    segment = query_ref[0, pl.ds(seg_row, 16), :].astype(F32)[:1].astype(jnp.int32)
    crop = lax.broadcasted_iota(jnp.int32, query.shape, 0)
    onehot = jnp.where(crop == segment, 1.0, 0.0)
    return jnp.concatenate([query, onehot], axis=0).astype(dtype)


def forward_kernel(
    crops, step, query_ref, own, other, raw_ref, out_ref, logsum_ref, key_t, value_n, scores
):
    @pl.when(pl.program_id(0) == 0)
    def _():
        start = 0
        for piece in (own, other):
            chips, _, patches = piece.shape
            for chip in range(chips):
                place = pl.ds(start, patches)
                key = piece[chip, pl.ds(HD, HD), :].astype(F32)
                key_t[:, place] = jnp.concatenate([key, mask_rows(piece, chip, crops)], axis=0).astype(BF16)
                value = piece[chip, pl.ds(2 * HD, HD), :].astype(F32)
                value = jnp.concatenate([value, jnp.ones_like(value)], axis=0)
                value_n[place, :] = value.T.astype(BF16)
                start += patches

    query = masked_query(query_ref, F32).T.astype(BF16)
    count = query.shape[0]
    top = jnp.full((count, 128), masked_value, F32)
    for start in range(0, key_t.shape[1], step):
        block = product(query, key_t[:, pl.ds(start, step)])
        scores[:, pl.ds(start, step)] = block
        for at in range(0, step, 128):
            top = jnp.maximum(top, block[:, at : at + 128])
    top = jnp.max(top, axis=1, keepdims=True)
    accum = jnp.zeros((count, 2 * HD), F32)
    for start in range(0, key_t.shape[1], step):
        weights = jnp.exp(scores[:, pl.ds(start, step)] - top).astype(BF16)
        accum += product(weights, value_n[pl.ds(start, step), :])
    accum = accum.T
    total = accum[HD : HD + 1]
    raw = accum[:HD] / total
    raw_ref[0] = raw
    out_ref[0] = raw.astype(BF16)
    top = jnp.broadcast_to(top, (count, 128)).T[:1]
    logsum_ref[0] = top + jnp.log(total)


def backward_kernel(
    crops,
    before,
    query_ref,
    grad_ref,
    raw_ref,
    logsum_ref,
    *refs,
):
    before_refs, refs = refs[:before], refs[before:]
    piece, (dquery_ref, sums_ref, keys, key_t, value_n, sums) = refs[0], refs[-6:]
    group = pl.program_id(0)

    @pl.when(group == 0)
    def _():
        load_keys(piece, crops, keys, key_t, value_n)
        sums[...] = jnp.zeros_like(sums)

    query = masked_query(query_ref)
    grad = grad_ref[0]
    grad_wide = grad.astype(F32)
    delta = jnp.sum(grad_wide * raw_ref[0], axis=0, keepdims=True)
    scaled = query_ref[0, pl.ds(0, HD), :].astype(F32) * 0.125
    zero = jnp.zeros_like(scaled)
    query_side = jnp.concatenate([scaled, zero], axis=0).T.astype(BF16)
    grad_side = jnp.concatenate([zero, grad_wide], axis=0).T.astype(BF16)
    probs = jnp.exp(product(keys[...], query) - logsum_ref[0])
    dprobs = product(value_n[...], grad)
    dscores = (probs * (dprobs - delta)).astype(BF16)
    sums[...] += product(dscores, query_side) + product(probs.astype(BF16), grad_side)
    dquery = product(key_t[...], dscores) * 0.125
    for ref in before_refs:
        dquery = ref[0] + dquery
    dquery_ref[0] = dquery.astype(dquery_ref.dtype)

    @pl.when(group == pl.num_programs(0) - 1)
    def _():
        chips, _, patches = sums_ref.shape
        for chip in range(chips):
            sums_ref[chip] = sums[pl.ds(chip * patches, patches), :].T.astype(sums_ref.dtype)


def key_step(count):
    return 1024 if count % 1024 == 0 else 256


def query_spec(rows, patches):
    return pl.BlockSpec((1, rows, patches), lambda group: (group, 0, 0))


def attention_forward(queries, own, other, crops):
    groups, _, patches = queries.shape
    count = 2 * own.shape[0] * own.shape[2]
    return pl.pallas_call(
        functools.partial(forward_kernel, crops, key_step(count)),
        grid=(groups,),
        in_specs=[
            query_spec(payload_rows, patches),
            whole_spec(own.shape),
            whole_spec(other.shape),
        ],
        out_specs=[query_spec(HD, patches), query_spec(HD, patches), query_spec(1, patches)],
        out_shape=[
            struct((groups, HD, patches), F32),
            struct((groups, HD, patches), BF16),
            struct((groups, 1, patches), F32),
        ],
        scratch_shapes=[
            pltpu.VMEM((2 * HD, count), BF16),
            pltpu.VMEM((count, 2 * HD), BF16),
            pltpu.VMEM((patches, count), F32),
        ],
        compiler_params=streaming,
        cost_estimate=light,
        name="attention_forward",
    )(queries, own, other)


def backward_piece(queries, grads, raw, logsum, before, keys, earlier, index, pieces, crops, dtypes):
    groups, _, patches = queries.shape
    chips = keys.shape[0] // pieces
    count = chips * keys.shape[2]
    sums_shape = (chips, 2 * HD, keys.shape[2])
    return pl.pallas_call(
        functools.partial(backward_kernel, crops, len(before)),
        grid=(groups,),
        in_specs=[
            query_spec(payload_rows, patches),
            query_spec(HD, patches),
            query_spec(HD, patches),
            query_spec(1, patches),
        ]
        + [query_spec(HD, patches)] * len(before)
        + [pl.BlockSpec((chips,) + keys.shape[1:], lambda group: (index, 0, 0))]
        + [pl.BlockSpec(memory_space=pl.ANY)] * len(earlier),
        out_specs=[
            query_spec(HD, patches),
            pl.BlockSpec(sums_shape, lambda group: (index, 0, 0)),
        ],
        out_shape=[
            struct((groups, HD, patches), dtypes[0]),
            struct((keys.shape[0],) + sums_shape[1:], dtypes[1]),
        ],
        input_output_aliases={5 + len(before): 1} if earlier else {},
        scratch_shapes=[
            pltpu.VMEM((count, 2 * HD), BF16),
            pltpu.VMEM((HD, count), BF16),
            pltpu.VMEM((count, HD), BF16),
            pltpu.VMEM((count, 2 * HD), F32),
        ],
        compiler_params=params,
        cost_estimate=light,
        name="attention_backward",
    )(queries, grads, raw, logsum, *before, keys, *earlier)


def swap_cores(values):
    return lax.ppermute(values, "core", [(0, 1), (1, 0)])


def to_heads(blocks):
    return lax.all_to_all(blocks, "chip", 0, 0, tiled=True)


def scatter_queries(values, heads, split):
    rows, patches = values.shape[0] // heads, values.shape[1]
    if split == 1:
        return to_heads(values.reshape(heads, rows, patches))
    part = patches // split
    blocks = values.reshape(heads, rows, split, part).transpose(0, 2, 1, 3)
    moved = to_heads(blocks.reshape(heads * split, rows, part))
    width = min(256, moved.shape[0] * part)
    joined = moved.transpose(1, 0, 2).reshape(rows, -1, width)
    return joined.transpose(1, 0, 2)


def gather_queries(values, heads, split, patches):
    rows = values.shape[1]
    if split == 1:
        return to_heads(values).reshape(heads * rows, patches)
    part = patches // split
    joined = values.transpose(1, 0, 2).reshape(rows, heads * split, part)
    moved = to_heads(joined.transpose(1, 0, 2)).reshape(heads, split, rows, part)
    return moved.transpose(0, 2, 1, 3).reshape(heads * rows, patches)


def across_heads(part):
    if lax.axis_size("head") == 2:
        return [part, lax.ppermute(part, "head", [(0, 1), (1, 0)])]
    return [lax.psum(part, "head")]


def ring_pairs(direction):
    chips = lax.axis_size("chip")
    order = list(range(0, chips, 2)) + list(range(chips - 1, 0, -2))
    return [(order[at], order[(at + direction) % chips]) for at in range(chips)]


def ring_table():
    chips, chip = lax.axis_size("chip"), lax.axis_index("chip")
    place = jnp.where(chip % 2 == 0, chip // 2, chips - 1 - chip // 2)
    steps = jnp.arange(2 * chips + 2, dtype=jnp.int32)
    places = (place + steps) % chips
    there = jnp.where(places < chips // 2, 2 * places, 2 * (chips - 1 - places) + 1)
    table = jnp.where(steps < chips, places, there)
    table = jnp.where(steps == 2 * chips, lax.axis_index("core"), table)
    return jnp.where(steps == 2 * chips + 1, lax.axis_index("head"), table).astype(jnp.int32)


def visit(streams, values):
    states, values = lax.optimization_barrier(([stream.state for stream in streams], values))
    for stream, state in zip(streams, states):
        stream.advance(state)
    ready, values = lax.optimization_barrier(([stream.ready for stream in streams], values))
    for stream, blocks in zip(streams, ready):
        stream.send(blocks)
    return values


def pieces_of(block):
    return list(block) if isinstance(block, tuple) else [block]


def whole_block(block):
    return jnp.concatenate(pieces_of(block), axis=1)


def join_kernel(counts, *refs):
    output, refs, start = refs[-1], list(refs[:-1]), 0
    for count in counts:
        column = 0
        for _ in range(count):
            piece = refs.pop(0)
            rows, columns = piece.shape
            output[pl.ds(start, rows), pl.ds(column, columns)] = piece[...]
            column += columns
        start += rows


def join(blocks):
    blocks = [pieces_of(block) for block in blocks]
    rows = sum(block[0].shape[0] for block in blocks)
    columns = sum(piece.shape[1] for piece in blocks[0])
    return pl.pallas_call(
        functools.partial(join_kernel, [len(block) for block in blocks]),
        out_shape=struct((rows, columns), blocks[0][0].dtype),
        compiler_params=streaming,
        name="join",
    )(*[piece for block in blocks for piece in block])


def halves_kernel(left, right, left_ref, right_ref):
    left_ref[...] = left[...]
    right_ref[...] = right[...]


def halves(left, right):
    rows, columns = left.shape
    if rows % 16 or columns % 256:
        return [left[:, : columns // 2], right[:, columns // 2 :]]
    out = pl.BlockSpec((rows, columns // 2), lambda at: (0, 0))
    return pl.pallas_call(
        halves_kernel,
        grid=(1,),
        in_specs=[out, pl.BlockSpec((rows, columns // 2), lambda at: (0, 1))],
        out_specs=[out, out],
        out_shape=[struct((rows, columns // 2), left.dtype)] * 2,
        compiler_params=streaming,
        name="halves",
    )(left, right)


class Gather:
    def __init__(self, block, swap=False, take=None):
        self.reach, self.swap, self.take = lax.axis_size("chip") // 2, swap, take
        self.blocks, self.pairs, self.count = [], [], 0
        self.new, self.outputs = [0], []
        self.ready = [block]

    def send(self, ready):
        if len(self.new) < len(ready):
            ready = [tuple(ready)]
        new = list(zip(self.new, ready))
        self.blocks += new
        self.new = new
        self.count += 1
        sides = ready if len(ready) > 1 else ready * 2
        if self.count == self.reach:
            sides = halves(*sides)
        flying = []
        if self.count <= self.reach:
            flying = [
                lax.ppermute(block, "chip", ring_pairs(direction))
                for block, direction in zip(sides, (1, -1))
            ]
        if self.swap and ready:
            pairs = [(step, block, jax.tree.map(swap_cores, block)) for step, block in new]
            self.pairs += pairs
            self.outputs = self.take(self.outputs, pairs)
        self.state = (flying, self.outputs)

    def advance(self, state):
        arrived, self.outputs = state
        self.new = [-self.count, self.count]
        if self.count == self.reach:
            self.new = [self.count]
        self.ready = arrived

    def busy(self):
        return bool(self.state[0])


def add_kernel(wanted, count, _, *refs):
    outputs, refs = refs[-count:], list(refs[:-count])
    keep_in, far_in = refs.pop(0), refs.pop(0)
    for starts, output in zip(wanted, outputs):
        near, far = refs.pop(0), refs.pop(0)
        total = product(near[...], keep_in[...], 0, 0) + product(far[...], far_in[...], 0, 0)
        if len(outputs) > len(wanted):
            for at, output in enumerate(outputs):
                columns = output.shape[1]
                output[...] = total[:, at * columns : at * columns + columns].astype(BF16)
            return
        output[...] = total.astype(BF16)
        arrived = [refs.pop(0) for _ in starts]
        for start in sorted(set(starts)):
            parts = [part for part, at in zip(arrived, starts) if at == start]
            columns = slice(start, start + parts[0].shape[1])
            summed = total[:, columns]
            for part in parts:
                summed += part[...].astype(F32)
            output[:, columns] = summed.astype(BF16)


class Reduce:
    def __init__(self, keep, far, keep_in, far_in, table):
        self.chips, self.table = lax.axis_size("chip"), table
        self.operands, self.sides = (keep, far), (keep_in, far_in)
        self.units = keep.shape[1] // self.chips
        self.tiled = self.units % 128 == 0
        self.left, self.rest = self.chips // 2, None
        blocks = self.add([(self.left, [])], True)
        self.send(blocks if len(blocks) > 1 else halves(blocks[0], blocks[0]))

    def send(self, ready):
        self.left -= 1
        self.state = [
            lax.ppermute(block, "chip", ring_pairs(direction))
            for block, direction in zip(ready, (1, -1))
        ]

    def advance(self, state):
        half = self.sides[0].shape[1] // 2
        ahead, behind = state
        first = 0 if ahead.shape[1] != half else half
        self.ready = self.add([(self.left, [(ahead, 0)]), (-self.left, [(behind, first)])])

    def arrive(self, values):
        self.state, values = lax.optimization_barrier((self.state, values))
        return values

    def finish(self):
        ahead, behind = self.state
        return self.add([(0, [(ahead, 0), (behind, 0)])])[0]

    def add(self, wanted, split=False):
        (rows, model), units, chips = self.sides[0].shape, self.units, self.chips
        if not self.tiled:
            sums = []
            for step, parts in wanted:
                start = self.table[step % chips] * units
                total = jnp.zeros((units, model), F32)
                for operand, side in zip(self.operands, self.sides):
                    block = lax.dynamic_slice_in_dim(operand, start, units, 1)
                    total += product(block, side, 0, 0)
                for part, start in parts:
                    total = total.at[:, start : start + part.shape[1]].add(part.astype(F32))
                sums.append(total.astype(BF16))
            return sums
        side = pl.BlockSpec((rows, model), lambda at, table: (0, 0))
        whole = pl.BlockSpec((units, model), lambda at, table: (0, 0))
        specs, arrays = [side] * 2, list(self.sides)
        for step, parts in wanted:
            block = pl.BlockSpec(
                (rows, units), lambda at, table, step=step % chips: (0, table[step])
            )
            specs += [block] * 2
            specs += [pl.BlockSpec(part.shape, lambda at, table: (0, 0)) for part, _ in parts]
            arrays += list(self.operands) + [part for part, _ in parts]
        starts = [[start for _, start in parts] for _, parts in wanted]
        shapes = [struct((units, model), BF16)] * len(wanted)
        if split:
            shapes = [struct((units, model // 2), BF16)] * 2
        return pl.pallas_call(
            functools.partial(add_kernel, starts, len(shapes)),
            grid_spec=pltpu.PrefetchScalarGridSpec(
                num_scalar_prefetch=1,
                grid=(1,),
                in_specs=specs,
                out_specs=[pl.BlockSpec(shape.shape, lambda at, table: (0, 0)) for shape in shapes],
            ),
            out_shape=shapes,
            compiler_params=streaming,
            cost_estimate=light,
            name="ring_add",
        )(self.table, *arrays)

    def place(self, outputs, pairs):
        units, chips, model = self.units, self.chips, self.sides[0].shape[1]
        size, extra = self.size, self.extra
        shapes = [struct((chips * units, model), F32), struct((model, chips * units), F32)]
        if not self.tiled:
            outputs = outputs or [jnp.zeros(shape.shape, F32) for shape in shapes]
            down, up = outputs
            is_down = self.table[2 * chips] == 0
            for step, near, far in pairs:
                start = self.table[step % chips] * units
                near, far = whole_block(near)[:units], whole_block(far)[:units]
                first = jnp.where(is_down, near, far).astype(F32)
                second = jnp.where(is_down, far, near).astype(F32).T
                down = lax.dynamic_update_slice_in_dim(down, first, start, 0)
                up = lax.dynamic_update_slice_in_dim(up, second, start, 1)
            return [down, up]
        first = pairs[0][0] % chips
        stride = pairs[-1][0] % chips - first
        blocks = [pieces_of(pair[1]) + pieces_of(pair[2]) for pair in pairs]
        flat = [piece for block in blocks for piece in block]

        def place(at, table):
            return table[first + at * stride]

        def chip(at, table):
            return table[chips + first + at * stride]

        column = pl.BlockSpec(
            (model, 2 * HD), lambda at, table: (0, lax.div(chip(at, table), 2))
        )
        columns = [column] * (3 if outputs else 0)
        heads = [[first, first + stride][at] + chips for at in range(len(pairs))]
        return pl.pallas_call(
            functools.partial(place_kernel, heads, len(blocks[0]) // 2, (units, size, extra)),
            grid_spec=pltpu.PrefetchScalarGridSpec(
                num_scalar_prefetch=1,
                grid=(len(pairs),),
                in_specs=[pl.BlockSpec(memory_space=pl.ANY)] * (len(outputs) - len(columns))
                + columns
                + [pl.BlockSpec(piece.shape, lambda at, table: (0, 0)) for piece in flat],
                out_specs=[
                    pl.BlockSpec((units, model), lambda at, table: (place(at, table), 0)),
                    pl.BlockSpec((model, units), lambda at, table: (0, place(at, table))),
                    pl.BlockSpec((2, 1, extra, model), lambda at, table: (0, chip(at, table), 0, 0)),
                    pl.BlockSpec(
                        (1, 2, small_rows, model), lambda at, table: (chip(at, table), 0, 0, 0)
                    ),
                ]
                + [column] * 3,
            ),
            out_shape=shapes
            + [
                struct((2, chips, extra, model), F32),
                struct((chips, 2, small_rows, model), F32),
            ]
            + [struct((model, chips * HD), F32)] * 3,
            input_output_aliases={1 + at: at for at in range(len(outputs))},
            compiler_params=streaming,
            cost_estimate=light,
            name="place",
        )(self.table, *outputs, *flat)


def place_kernel(heads, width, sizes, table, *refs):
    count = len(heads)
    refs, (down, up, weight, small), projections = refs[:-7], refs[-7:-3], refs[-3:]
    blocks, refs = refs[-2 * width * count :], refs[: -2 * width * count]
    core = table[table.shape[0] - 2]
    units, size, extra = sizes
    rows = [pl.ds(0, units), pl.ds(units, size), pl.ds(units + size, extra)]
    rows.append(pl.ds(units + size + extra, small_rows))

    def read(block, which):
        return jnp.concatenate([piece[rows[which], :] for piece in block], axis=1)

    def put(first, second, head):
        down[...] = read(first, 0).astype(F32)
        up[...] = read(second, 0).astype(F32).T
        for side, block in ((0, first), (1, second)):
            weight[side, 0] = read(block, 2).astype(F32)
            small[0, side] = read(block, 3).astype(F32)
        both = jnp.concatenate([read(first, 1), read(second, 1)], axis=0)
        for at, output in enumerate(projections):
            part = both[at * HD : at * HD + HD].astype(F32)
            part = jnp.concatenate([part, part], axis=0).T
            if refs:
                mine = lax.broadcasted_iota(jnp.int32, part.shape, 1) // HD == head % 2
                part = jnp.where(mine, part, refs[at - 3][...])
            output[...] = part

    for at in range(count):
        near, far = (
            blocks[(2 * at + side) * width : (2 * at + side + 1) * width] for side in range(2)
        )
        head = table[heads[at]]
        here = pl.program_id(0) == at
        pl.when(here & (core == 0))(functools.partial(put, near, far, head))
        pl.when(here & (core != 0))(functools.partial(put, far, near, head))


def head_gradient_kernel(steps, chips, table, query_ref, key_value_ref, *refs):
    parts, out_ref = refs[:-1], refs[-1]
    patches = query_ref.shape[2]
    for at, part in enumerate(parts):

        @pl.when(pl.program_id(0) == at)
        def _(part=part):
            total = jnp.zeros(out_ref.shape, F32)
            for index, step in enumerate(steps):
                chip = table[chips + step % chips]
                grads = jnp.concatenate([query_ref[chip], key_value_ref[chip]], axis=0)
                total += product(grads, part[pl.ds(index * patches, patches), :])
            out_ref[...] = total.astype(BF16)


def head_gradient(dquery, key_value, parts, steps, table):
    chips, rows, _ = dquery.shape
    columns = parts[0].shape[1]

    def column(at, table):
        mine = table[2 * chips + 1] if len(parts) > 1 else 0
        return (0, jnp.where(at == 0, mine, 1 - mine))

    return pl.pallas_call(
        functools.partial(head_gradient_kernel, steps, chips),
        grid_spec=pltpu.PrefetchScalarGridSpec(
            num_scalar_prefetch=1,
            grid=(len(parts),),
            in_specs=[
                pl.BlockSpec(array.shape, lambda at, table, rank=array.ndim: (0,) * rank)
                for array in (dquery, key_value, *parts)
            ],
            out_specs=pl.BlockSpec((3 * rows, columns), column),
        ),
        out_shape=struct((3 * rows, columns * len(parts)), BF16),
        compiler_params=streaming,
        cost_estimate=light,
        name="head_gradient",
    )(table, dquery, key_value, *parts)


def core_half(values, axis, side):
    size = values.shape[axis] // 2
    return lax.dynamic_slice_in_dim(values, side * size, size, axis)


def share_halves(values, axis):
    core = lax.axis_index("core")
    return core_half(values, axis, core), swap_cores(core_half(values, axis, 1 - core))


def local(
    block_input,
    out_grad,
    segments,
    lead_steps,
    gain_attn,
    shift_attn,
    lead_weight,
    query_weight,
    key_weight,
    value_weight,
    output_weight,
    output_bias,
    gain_mlp,
    shift_mlp,
    up_weight,
    up_bias,
    down_weight,
    down_bias,
):
    rows, model = block_input.shape
    heads = query_weight.shape[1] // HD
    width = heads * HD
    chips, core = lax.axis_size("chip"), lax.axis_index("core")
    split = chips // heads
    crops = lead_steps.shape[0]
    table = ring_table()
    weights = (query_weight, key_weight, value_weight)
    cut = model // 2 if lax.axis_size("head") == 2 else model
    payload, attn_in, attn_in_cut = project(
        table, cut, block_input, segments, lead_steps, gain_attn, shift_attn, lead_weight, weights
    )
    if split == 1:
        own = to_heads(payload)
        queries = own
    else:
        queries = scatter_queries(payload.reshape(-1, rows), heads, split)
        own = to_heads(jnp.repeat(payload, split, axis=0))
    own, attn_in_cut = lax.optimization_barrier((own, attn_in_cut))
    inputs = Gather(attn_in_cut)
    inputs.send(inputs.ready)
    other = swap_cores(own)
    raw, out, logsum = attention_forward(queries, own, other, crops)
    inputs.state, out = lax.optimization_barrier((inputs.state, out))
    attn_out = gather_queries(out, heads, split, rows)
    attn_out = visit([inputs], attn_out)
    branches = across_heads(product(attn_out, output_weight, 0, 0).astype(BF16))
    visit([inputs], ())
    keep, give, keep_in, give_in, hidden, dup_bias, mlp_part, d_mlp_part = mlp(
        table,
        block_input,
        out_grad,
        branches,
        output_bias,
        gain_mlp,
        shift_mlp,
        up_weight,
        up_bias,
        down_weight,
    )
    keep, give, keep_in, give_in, d_mlp_part = visit(
        [inputs], (keep, give, keep_in, give_in, d_mlp_part)
    )
    d_mlp = across_heads(d_mlp_part)
    ring = Reduce(keep, swap_cores(give), keep_in, swap_cores(give_in), table)
    mlp_part, d_mlp = lax.optimization_barrier((mlp_part, d_mlp))
    d_hidden, d_branch, d_attn, sums = middle(hidden, out_grad, d_mlp, gain_mlp, output_weight)
    grads = scatter_queries(d_attn, heads, split)
    d_branch, mlp_part = visit([ring, inputs], (d_branch, mlp_part))
    while inputs.busy():
        visit([inputs], ())
    mlp_out = across_heads(mlp_part)
    out_near, out_far = share_halves(attn_out, 0)
    doutput = product(out_near, d_branch) + product(out_far, swap_cores(d_branch))
    doutput = doutput.astype(BF16).reshape(chips, -1, model)
    doutput = to_heads(doutput)
    steps, inputs = zip(*inputs.blocks)
    inputs = join(inputs)
    parts = across_heads(inputs) if cut != model else [inputs]
    grads, doutput, _ = visit([ring], (grads, doutput, inputs))
    *dquery, far_sums = backward_piece(
        queries, grads, raw, logsum, [], other, [], 0, 1, crops, (F32, BF16)
    )
    grads, dquery, far_sums = visit([ring], (grads, dquery, far_sums))
    far_sums = swap_cores(far_sums)
    *dquery, near_sums = backward_piece(
        queries, grads, raw, logsum, dquery, own, [], 0, 1, crops, (BF16, F32)
    )
    near_sums, dquery = ring.arrive((near_sums, dquery))
    (dquery,) = dquery
    key_value = (near_sums + far_sums.astype(F32)).astype(BF16)
    doutput, key_value = lax.optimization_barrier((doutput, key_value))
    doutput = jnp.sum(doutput.astype(F32), axis=0)
    small = jnp.concatenate([sums.reshape(-1), dup_bias[0]])
    small = jnp.pad(small, (0, small_rows * model - small.shape[0])).reshape(small_rows, model)
    doutput = jnp.concatenate([doutput, small], axis=0).astype(BF16)
    if split == 1:
        moved = to_heads(jnp.concatenate([dquery, key_value], axis=1))
        projections = head_gradient(dquery, key_value, parts, steps, table)
        near, far = share_halves(projections, 0)
        projections = (near.astype(F32) + far.astype(F32)).astype(BF16)
        size = projections.shape[0]
        blocks = jnp.concatenate([projections, doutput], axis=0)
        dquery, dkey, dvalue = (
            moved[:, at * HD : at * HD + HD].reshape(width, rows) for at in range(3)
        )
    else:
        dquery = gather_queries(dquery, heads, split, rows)
        moved = to_heads(key_value).reshape(heads, split, 2 * HD, rows).astype(F32)
        moved = jnp.sum(moved, axis=1).astype(BF16)
        dkey, dvalue = (moved[:, at * HD : at * HD + HD].reshape(width, rows) for at in range(2))
        size, blocks = 0, doutput
        projections = [
            lax.psum(product(attn_in, grad, 0, 1).astype(BF16), ("chip", "core")).astype(F32)
            for grad in (dquery, dkey, dvalue)
        ]
    total = ring.finish()
    start = total.shape[0]
    ring.size, ring.extra = size, blocks.shape[0] - size - small_rows
    gathered = Gather(jnp.concatenate([total, blocks], axis=0), True, ring.place)
    gathered.send(gathered.ready)
    d_part = (
        product(dquery, query_weight, 0, 1)
        + product(dkey, key_weight, 0, 1)
        + product(dvalue, value_weight, 0, 1)
    )
    d_in = across_heads(d_part.astype(BF16))
    unit_attn, inverse_attn = normalize(block_input.astype(F32))
    onehot = (segments[:, None] == jnp.arange(crops, dtype=jnp.int32)[None, :]).astype(F32)
    lead = jnp.sum(onehot * lead_steps.astype(F32)[None, :], axis=1) / 12.0
    ends = jnp.stack(
        [
            jnp.sum(d_part * unit_attn, axis=0),
            jnp.sum(d_part, axis=0),
            jnp.sum(lead[:, None] * d_part, axis=0),
        ]
    )
    ends = ends.reshape(-1, 128)
    ends = functools.reduce(jnp.add, across_heads(ends))
    ends = ends + swap_cores(ends)
    moves = [chips >> (at + 1) for at in range(chips.bit_length() - 1)][::-1]

    def step_ends(ends):
        if not moves:
            return [ends]
        reach = moves.pop(0)
        pairs = [(chip, chip ^ reach) for chip in range(chips)]
        return [ends, lax.ppermute(ends, "chip", pairs)]

    ends = step_ends(visit([gathered], ends))
    ends, mlp_out = visit([gathered], (ends, mlp_out))
    ends = step_ends(functools.reduce(jnp.add, ends))
    block_output = hidden + down_bias
    for part in mlp_out:
        block_output += part.astype(F32)
    block_output = block_output.astype(BF16)
    d_in, block_output, ends = visit([gathered], (d_in, block_output, ends))
    ends = step_ends(functools.reduce(jnp.add, ends))
    d_in = functools.reduce(jnp.add, (part.astype(F32) for part in d_in))
    input_grad = (d_hidden + normalize_back(d_in * gain_attn, unit_attn, inverse_attn)).astype(
        BF16
    )
    while gathered.busy() or moves:
        input_grad, ends = visit([gathered], (input_grad, ends))
        ends = step_ends(functools.reduce(jnp.add, ends))
    ends = functools.reduce(jnp.add, ends).reshape(3, model)
    ddown_weight, dup_weight, *rest = gathered.outputs
    if split == 1:
        doutput_weight, small, *projections = rest
        doutput_weight = doutput_weight.reshape(width, model)
    if split != 1:
        blocks = jnp.zeros((2, chips) + blocks.shape, F32)
        for step, near, far in gathered.pairs:
            for side, block in ((core, near), (1 - core, far)):
                at = (side, table[chips + step % chips], 0, 0)
                block = whole_block(block)[None, None, start:].astype(F32)
                blocks = lax.dynamic_update_slice(blocks, block, at)
        doutput_weight = blocks[:, :, :-small_rows].reshape(width, model)
        small = blocks[:, :, -small_rows:]
    small = jnp.sum(small, axis=(0, 1))
    dup_bias = small[4:].reshape(-1)[: dup_bias.shape[1]]
    return (
        block_output,
        input_grad,
        ends[0],
        ends[1],
        ends[2],
        *projections,
        doutput_weight,
        *small[:3],
        dup_weight,
        dup_bias,
        ddown_weight,
        small[3],
    )


def solution(mesh):
    bands, halves = mesh.shape["band"], mesh.shape["head"]
    inner = Mesh(mesh.devices.reshape(bands // 2, 2, halves), ("chip", "core", "head"))
    band = ("chip", "core")
    rows, columns, split_rows = P(band, None), P(None, "head"), P("head", None)
    return jax.shard_map(
        local,
        mesh=inner,
        in_specs=(
            rows,
            rows,
            P(band),
            P(),
            P(),
            P(),
            P(),
            columns,
            columns,
            columns,
            split_rows,
            P(),
            P(),
            P(),
            columns,
            P("head"),
            split_rows,
            P(),
        ),
        out_specs=(
            rows,
            rows,
            P(),
            P(),
            P(),
            columns,
            columns,
            columns,
            split_rows,
            P(),
            P(),
            P(),
            columns,
            P("head"),
            split_rows,
            P(),
        ),
        check_vma=False,
    )
```

```python
import functools
import math

import jax
import jax.numpy as jnp
from jax import lax
from jax.experimental import pallas as pl
from jax.experimental.pallas import tpu as pltpu
from jax.sharding import Mesh, PartitionSpec as P

HD = 64
F32 = jnp.float32
BF16 = jnp.bfloat16
eps = 1e-05
masked_value = -1e30
seg_row = 3 * HD
payload_rows = 3 * HD + 16
small_rows = 16
params = pltpu.CompilerParams(vmem_limit_bytes=48 * 2**20)
streaming = pltpu.CompilerParams(vmem_limit_bytes=60 * 2**20)


def normalize(values):
    centred = values - jnp.mean(values, axis=-1, keepdims=True)
    inverse = lax.rsqrt(jnp.mean(centred * centred, axis=-1, keepdims=True) + eps)
    return (centred * inverse, inverse)


def normalize_back(grad_unit, unit, inverse):
    return inverse * (
        grad_unit
        - jnp.mean(grad_unit, axis=-1, keepdims=True)
        - unit * jnp.mean(grad_unit * unit, axis=-1, keepdims=True)
    )


def product(first, second, first_axis=1, second_axis=0):
    return lax.dot_general(
        first,
        second,
        (((first_axis,), (second_axis,)), ((), ())),
        preferred_element_type=jnp.float32,
    )


def struct(shape, dtype):
    return jax.ShapeDtypeStruct(shape, dtype)


def whole_spec(shape):
    return pl.BlockSpec(shape, lambda *at: (0,) * len(shape))


light = pl.CostEstimate(flops=1, bytes_accessed=1, transcendentals=0)


def project_kernel(
    table, input_ref, segment_ref, steps_ref, gain, shift, lead_weight, *refs
):
    weights, (payload_ref, attn_in_ref, cut_ref) = refs[:3], refs[3:]
    rows = input_ref.shape[0]

    @pl.when(pl.program_id(0) == 0)
    def _():
        unit, _ = normalize(input_ref[...].astype(F32))
        crops = steps_ref.shape[0]
        crop = lax.broadcasted_iota(jnp.int32, (crops, rows), 0)
        steps = jnp.zeros((crops, rows), jnp.int32)
        for at in range(crops):
            steps = jnp.where(crop == at, steps_ref[at], steps)
        steps = jnp.where(crop == segment_ref[...], steps, 0).astype(F32)
        lead = product(steps, jnp.ones((crops, 128), F32), 0, 0)[:, :1] / 12.0
        attn_in = unit * gain[...] + shift[...] + lead * lead_weight[...]
        attn_in = attn_in.astype(BF16)
        attn_in_ref[...] = attn_in
        columns = cut_ref.shape[1]
        first = table[table.shape[0] - 1] % (attn_in.shape[1] // columns) == 0
        cut_ref[...] = jnp.where(first, attn_in[:, :columns], attn_in[:, -columns:])

    for at, weight in enumerate(weights):
        part = product(attn_in_ref[...], weight[...]).T.astype(BF16)
        for head in range(2):
            payload_ref[head, pl.ds(at * HD, HD), :] = part[head * HD : head * HD + HD]
    segment = jnp.broadcast_to(segment_ref[...].astype(F32), (16, rows)).astype(BF16)
    for head in range(2):
        payload_ref[head, pl.ds(seg_row, 16), :] = segment


def project(table, cut, block_input, segments, lead_steps, gain, shift, lead_weight, weights):
    rows, model = block_input.shape
    heads = weights[0].shape[1] // HD
    line = whole_spec((1, model))
    column = pl.BlockSpec((model, 2 * HD), lambda at, table: (0, at))
    return pl.pallas_call(
        project_kernel,
        grid_spec=pltpu.PrefetchScalarGridSpec(
            num_scalar_prefetch=1,
            grid=(heads // 2,),
            in_specs=[
                whole_spec(block_input.shape),
                whole_spec((1, rows)),
                pl.BlockSpec(memory_space=pltpu.SMEM),
            ]
            + [line] * 3
            + [column] * 3,
            out_specs=[
                pl.BlockSpec((2, payload_rows, rows), lambda at, table: (at, 0, 0)),
                whole_spec((rows, model)),
                whole_spec((rows, cut)),
            ],
        ),
        out_shape=[
            struct((heads, payload_rows, rows), BF16),
            struct((rows, model), BF16),
            struct((rows, cut), BF16),
        ],
        compiler_params=streaming,
        cost_estimate=light,
        name="project",
    )(table, block_input, segments[None], lead_steps, gain[None], shift[None], lead_weight[None], *weights)


def mlp_kernel(count, core_ref, input_ref, grad_ref, *refs):
    branches, refs = refs[:count], refs[count:]
    output_bias, gain, shift, up_weight, up_bias, down_weight = refs[:6]
    keep_ref, give_ref, keep_in_ref, give_in_ref, hidden_ref, bias_ref, forward_ref, back_ref = refs[
        6:14
    ]
    mlp_in_ref, forward, back = refs[14:]
    at = pl.program_id(0)
    is_down = core_ref[core_ref.shape[0] - 2] == 0

    @pl.when(at == 0)
    def _():
        hidden = input_ref[...].astype(F32) + output_bias[...]
        for branch in branches:
            hidden += branch[...].astype(F32)
        hidden_ref[...] = hidden
        unit, _ = normalize(hidden)
        mlp_in = (unit * gain[...] + shift[...]).astype(BF16)
        mlp_in_ref[...] = mlp_in
        keep_in_ref[...] = jnp.where(is_down, grad_ref[...], mlp_in)
        give_in_ref[...] = jnp.where(is_down, mlp_in, grad_ref[...])
        forward[...] = jnp.zeros_like(forward)
        back[...] = jnp.zeros_like(back)

    upper = product(mlp_in_ref[...], up_weight[...]) + up_bias[...]
    share = 0.5 + 0.5 * lax.erf(upper * math.sqrt(0.5))
    slope = share + upper * (jnp.exp(upper * upper * -0.5) * (1.0 / math.sqrt(2.0 * math.pi)))
    active = (upper * share).astype(BF16)
    d_active = product(grad_ref[...], down_weight[...], 1, 1)
    d_upper = (d_active * slope).astype(BF16)
    keep_ref[...] = jnp.where(is_down, active, d_upper)
    give_ref[...] = jnp.where(is_down, d_upper, active)
    bias_ref[...] = jnp.sum(d_upper.astype(F32), axis=0, keepdims=True)
    forward[...] += product(active, down_weight[...])
    back[...] += product(d_upper, up_weight[...], 1, 1)

    @pl.when(at == pl.num_programs(0) - 1)
    def _():
        forward_ref[...] = forward[...].astype(BF16)
        back_ref[...] = back[...].astype(BF16)


def mlp(
    table, block_input, out_grad, branches, output_bias, gain, shift, up_weight, up_bias, down_weight
):
    rows, model = block_input.shape
    units = up_weight.shape[1]
    step = math.gcd(units, 512)
    tile, line = whole_spec((rows, model)), whole_spec((1, model))
    wide = pl.BlockSpec((rows, step), lambda at, table: (0, at))
    bias = pl.BlockSpec((1, step), lambda at, table: (0, at))
    return pl.pallas_call(
        functools.partial(mlp_kernel, len(branches)),
        grid_spec=pltpu.PrefetchScalarGridSpec(
            num_scalar_prefetch=1,
            grid=(units // step,),
            in_specs=[tile] * (2 + len(branches))
            + [line] * 3
            + [
                pl.BlockSpec((model, step), lambda at, table: (0, at)),
                bias,
                pl.BlockSpec((step, model), lambda at, table: (at, 0)),
            ],
            out_specs=[wide, wide, tile, tile, tile, bias, tile, tile],
            scratch_shapes=[pltpu.VMEM((rows, model), BF16)]
            + [pltpu.VMEM((rows, model), F32)] * 2,
        ),
        out_shape=[struct((rows, units), BF16)] * 2
        + [struct((rows, model), BF16)] * 2
        + [
            struct((rows, model), F32),
            struct((1, units), F32),
            struct((rows, model), BF16),
            struct((rows, model), BF16),
        ],
        compiler_params=streaming,
        cost_estimate=light,
        name="mlp",
    )(
        table,
        block_input,
        out_grad,
        *branches,
        output_bias[None],
        gain[None],
        shift[None],
        up_weight,
        up_bias[None],
        down_weight,
    )


def middle_kernel(count, hidden_ref, grad_ref, *refs):
    parts, refs = refs[:count], refs[count:]
    gain, output_weight, d_hidden_ref, d_branch_ref, d_attn_ref, sums_ref = refs
    unit, inverse = normalize(hidden_ref[...])
    d_mlp = parts[0][...].astype(F32)
    for part in parts[1:]:
        d_mlp += part[...].astype(F32)
    grad = grad_ref[...].astype(F32)
    d_hidden = grad + normalize_back(d_mlp * gain[...], unit, inverse)
    d_hidden_ref[...] = d_hidden
    d_branch = d_hidden.astype(BF16)
    d_branch_ref[...] = d_branch
    d_attn_ref[...] = product(output_weight[...], d_branch, 1, 1).astype(BF16)
    for at, values in enumerate((d_hidden, d_mlp * unit, d_mlp, grad)):
        sums_ref[pl.ds(at, 1), :] = jnp.sum(values, axis=0, keepdims=True)


def middle(hidden, out_grad, parts, gain, output_weight):
    rows, model = hidden.shape
    width = output_weight.shape[0]
    return pl.pallas_call(
        functools.partial(middle_kernel, len(parts)),
        out_shape=[
            struct((rows, model), F32),
            struct((rows, model), BF16),
            struct((width, rows), BF16),
            struct((4, model), F32),
        ],
        compiler_params=streaming,
        cost_estimate=light,
        name="middle",
    )(hidden, out_grad, *parts, gain[None], output_weight)


def mask_rows(piece, chip, crops):
    crop = lax.broadcasted_iota(jnp.int32, (HD, piece.shape[2]), 0)
    segment = piece[chip, pl.ds(seg_row, 16), :].astype(F32)[:1].astype(jnp.int32)
    return jnp.where((crop != segment) & (crop < crops), masked_value, 0.0)


def load_keys(piece, crops, keys, key_t, value_n):
    chips, _, patches = piece.shape
    for chip in range(chips):
        key = piece[chip, pl.ds(HD, HD), :]
        value = piece[chip, pl.ds(2 * HD, HD), :]
        place = pl.ds(chip * patches, patches)
        both = jnp.concatenate([key.astype(F32), mask_rows(piece, chip, crops)], axis=0)
        keys[place, :] = both.T.astype(BF16)
        key_t[:, place] = key
        value_n[place, :] = value.astype(F32).T.astype(BF16)


def masked_query(query_ref, dtype=BF16):
    query = query_ref[0, pl.ds(0, HD), :].astype(F32) * 0.125
    segment = query_ref[0, pl.ds(seg_row, 16), :].astype(F32)[:1].astype(jnp.int32)
    crop = lax.broadcasted_iota(jnp.int32, query.shape, 0)
    onehot = jnp.where(crop == segment, 1.0, 0.0)
    return jnp.concatenate([query, onehot], axis=0).astype(dtype)


def forward_kernel(
    crops, step, query_ref, own, other, raw_ref, out_ref, logsum_ref, key_t, value_n, scores
):
    @pl.when(pl.program_id(0) == 0)
    def _():
        start = 0
        for piece in (own, other):
            chips, _, patches = piece.shape
            for chip in range(chips):
                place = pl.ds(start, patches)
                key = piece[chip, pl.ds(HD, HD), :].astype(F32)
                key_t[:, place] = jnp.concatenate([key, mask_rows(piece, chip, crops)], axis=0).astype(BF16)
                value = piece[chip, pl.ds(2 * HD, HD), :].astype(F32)
                value = jnp.concatenate([value, jnp.ones_like(value)], axis=0)
                value_n[place, :] = value.T.astype(BF16)
                start += patches

    query = masked_query(query_ref, F32).T.astype(BF16)
    count = query.shape[0]
    top = jnp.full((count, 128), masked_value, F32)
    for start in range(0, key_t.shape[1], step):
        block = product(query, key_t[:, pl.ds(start, step)])
        scores[:, pl.ds(start, step)] = block
        for at in range(0, step, 128):
            top = jnp.maximum(top, block[:, at : at + 128])
    top = jnp.max(top, axis=1, keepdims=True)
    accum = jnp.zeros((count, 2 * HD), F32)
    for start in range(0, key_t.shape[1], step):
        weights = jnp.exp(scores[:, pl.ds(start, step)] - top).astype(BF16)
        accum += product(weights, value_n[pl.ds(start, step), :])
    accum = accum.T
    total = accum[HD : HD + 1]
    raw = accum[:HD] / total
    raw_ref[0] = raw
    out_ref[0] = raw.astype(BF16)
    top = jnp.broadcast_to(top, (count, 128)).T[:1]
    logsum_ref[0] = top + jnp.log(total)


def backward_kernel(
    crops,
    extra,
    query_ref,
    grad_ref,
    raw_ref,
    logsum_ref,
    piece,
    *refs,
):
    extras, refs = refs[:extra], refs[extra:]
    outputs, (keys, key_t, value_n, sums) = refs[:-4], refs[-4:]
    group = pl.program_id(0)

    @pl.when(group == 0)
    def _():
        load_keys(piece, crops, keys, key_t, value_n)
        sums[...] = jnp.zeros_like(sums)

    query = masked_query(query_ref)
    grad = grad_ref[0]
    grad_wide = grad.astype(F32)
    delta = jnp.sum(grad_wide * raw_ref[0], axis=0, keepdims=True)
    scaled = query_ref[0, pl.ds(0, HD), :].astype(F32) * 0.125
    zero = jnp.zeros_like(scaled)
    query_side = jnp.concatenate([scaled, zero], axis=0).T.astype(BF16)
    grad_side = jnp.concatenate([zero, grad_wide], axis=0).T.astype(BF16)
    probs = jnp.exp(product(keys[...], query) - logsum_ref[0])
    dprobs = product(value_n[...], grad)
    dscores = (probs * (dprobs - delta)).astype(BF16)
    sums[...] += product(dscores, query_side) + product(probs.astype(BF16), grad_side)
    dquery = product(key_t[...], dscores) * 0.125
    if extras:
        dquery += extras[0][0]
    if len(outputs) == 1:
        outputs[0][group, pl.ds(0, HD), :] = dquery.astype(BF16)
    else:
        outputs[0][0] = dquery.astype(outputs[0].dtype)

    @pl.when(group == pl.num_programs(0) - 1)
    def _():
        chips, _, patches = piece.shape
        for chip in range(chips):
            total = sums[pl.ds(chip * patches, patches), :].T
            if extra > 1:
                total += extras[1][chip].astype(F32)
            total = total.astype(BF16)
            if len(outputs) == 1:
                outputs[0][chip, pl.ds(HD, 2 * HD), :] = total
            else:
                outputs[1][chip] = total


def key_step(count):
    return 1024 if count % 1024 == 0 else 256


def query_spec(rows, patches):
    return pl.BlockSpec((1, rows, patches), lambda group: (group, 0, 0))


def attention_forward(queries, own, other, crops):
    groups, _, patches = queries.shape
    count = 2 * own.shape[0] * own.shape[2]
    return pl.pallas_call(
        functools.partial(forward_kernel, crops, key_step(count)),
        grid=(groups,),
        in_specs=[
            query_spec(payload_rows, patches),
            whole_spec(own.shape),
            whole_spec(other.shape),
        ],
        out_specs=[query_spec(HD, patches), query_spec(HD, patches), query_spec(1, patches)],
        out_shape=[
            struct((groups, HD, patches), F32),
            struct((groups, HD, patches), BF16),
            struct((groups, 1, patches), F32),
        ],
        scratch_shapes=[
            pltpu.VMEM((2 * HD, count), BF16),
            pltpu.VMEM((count, 2 * HD), BF16),
            pltpu.VMEM((patches, count), F32),
        ],
        compiler_params=streaming,
        cost_estimate=light,
        name="attention_forward",
    )(queries, own, other)


def attention_backward(queries, grads, raw, logsum, keys, extras, crops):
    groups, _, patches = queries.shape
    chips, count = keys.shape[0], keys.shape[0] * keys.shape[2]
    sums_shape = (chips, 2 * HD, keys.shape[2])
    specs = [query_spec(HD, patches), whole_spec(sums_shape)]
    shapes = [
        struct((groups, HD, patches), BF16 if extras else F32),
        struct(sums_shape, BF16),
    ]
    outs = specs
    if extras and (groups, patches) == (chips, keys.shape[2]):
        shapes = [struct((chips, 3 * HD, patches), BF16)]
        outs = [whole_spec(shapes[0].shape)]
    return pl.pallas_call(
        functools.partial(backward_kernel, crops, len(extras)),
        grid=(groups,),
        in_specs=[
            query_spec(payload_rows, patches),
            query_spec(HD, patches),
            query_spec(HD, patches),
            query_spec(1, patches),
            whole_spec(keys.shape),
        ]
        + specs[: len(extras)],
        out_specs=outs,
        out_shape=shapes,
        scratch_shapes=[
            pltpu.VMEM((count, 2 * HD), BF16),
            pltpu.VMEM((HD, count), BF16),
            pltpu.VMEM((count, HD), BF16),
            pltpu.VMEM((count, 2 * HD), F32),
        ],
        compiler_params=params,
        cost_estimate=light,
        name="attention_backward",
    )(queries, grads, raw, logsum, keys, *extras)


def swap_cores(values):
    return lax.ppermute(values, "core", [(0, 1), (1, 0)])


def to_heads(blocks):
    return lax.all_to_all(blocks, "chip", 0, 0, tiled=True)


def scatter_queries(values, heads, split):
    rows, patches = values.shape[0] // heads, values.shape[1]
    if split == 1:
        return to_heads(values.reshape(heads, rows, patches))
    part = patches // split
    blocks = values.reshape(heads, rows, split, part).transpose(0, 2, 1, 3)
    moved = to_heads(blocks.reshape(heads * split, rows, part))
    width = min(256, moved.shape[0] * part)
    joined = moved.transpose(1, 0, 2).reshape(rows, -1, width)
    return joined.transpose(1, 0, 2)


def gather_queries(values, heads, split, patches):
    rows = values.shape[1]
    if split == 1:
        return to_heads(values).reshape(heads * rows, patches)
    part = patches // split
    joined = values.transpose(1, 0, 2).reshape(rows, heads * split, part)
    moved = to_heads(joined.transpose(1, 0, 2)).reshape(heads, split, rows, part)
    return moved.transpose(0, 2, 1, 3).reshape(heads * rows, patches)


def across_heads(part):
    if lax.axis_size("head") == 2:
        return [part, lax.ppermute(part, "head", [(0, 1), (1, 0)])]
    return [lax.psum(part, "head")]


def ring_pairs(direction):
    chips = lax.axis_size("chip")
    order = list(range(0, chips, 2)) + list(range(chips - 1, 0, -2))
    return [(order[at], order[(at + direction) % chips]) for at in range(chips)]


def ring_table():
    chips, chip = lax.axis_size("chip"), lax.axis_index("chip")
    place = jnp.where(chip % 2 == 0, chip // 2, chips - 1 - chip // 2)
    steps = jnp.arange(2 * chips + 2, dtype=jnp.int32)
    places = (place + steps) % chips
    there = jnp.where(places < chips // 2, 2 * places, 2 * (chips - 1 - places) + 1)
    table = jnp.where(steps < chips, places, there)
    table = jnp.where(steps == 2 * chips, lax.axis_index("core"), table)
    return jnp.where(steps == 2 * chips + 1, lax.axis_index("head"), table).astype(jnp.int32)


def visit(streams, values):
    states, values = lax.optimization_barrier(([stream.state for stream in streams], values))
    for stream, state in zip(streams, states):
        stream.advance(state)
    ready, values = lax.optimization_barrier(([stream.ready for stream in streams], values))
    for stream, blocks in zip(streams, ready):
        stream.send(blocks)
    return values


def pieces_of(block):
    return list(block) if isinstance(block, tuple) else [block]


def whole_block(block):
    return jnp.concatenate(pieces_of(block), axis=1)


def join_kernel(counts, *refs):
    output, refs, start = refs[-1], list(refs[:-1]), 0
    for count in counts:
        column = 0
        for _ in range(count):
            piece = refs.pop(0)
            rows, columns = piece.shape
            output[pl.ds(start, rows), pl.ds(column, columns)] = piece[...]
            column += columns
        start += rows


def join(blocks):
    blocks = [pieces_of(block) for block in blocks]
    rows = sum(block[0].shape[0] for block in blocks)
    columns = sum(piece.shape[1] for piece in blocks[0])
    return pl.pallas_call(
        functools.partial(join_kernel, [len(block) for block in blocks]),
        out_shape=struct((rows, columns), blocks[0][0].dtype),
        compiler_params=streaming,
        name="join",
    )(*[piece for block in blocks for piece in block])


def halves_kernel(left, right, left_ref, right_ref):
    left_ref[...] = left[...]
    right_ref[...] = right[...]


def halves(left, right):
    rows, columns = left.shape
    if rows % 16 or columns % 256:
        return [left[:, : columns // 2], right[:, columns // 2 :]]
    out = pl.BlockSpec((rows, columns // 2), lambda at: (0, 0))
    return pl.pallas_call(
        halves_kernel,
        grid=(1,),
        in_specs=[out, pl.BlockSpec((rows, columns // 2), lambda at: (0, 1))],
        out_specs=[out, out],
        out_shape=[struct((rows, columns // 2), left.dtype)] * 2,
        compiler_params=streaming,
        name="halves",
    )(left, right)


class Gather:
    def __init__(self, block, swap=False, take=None):
        self.reach, self.swap, self.take = lax.axis_size("chip") // 2, swap, take
        self.blocks, self.pairs, self.count = [], [], 0
        self.new, self.outputs = [0], []
        self.ready = [block]

    def send(self, ready):
        if len(self.new) < len(ready):
            ready = [tuple(ready)]
        new = list(zip(self.new, ready))
        self.blocks += new
        self.new = new
        self.count += 1
        sides = ready if len(ready) > 1 else ready * 2
        if self.count == self.reach:
            sides = halves(*sides)
        flying = []
        if self.count <= self.reach:
            flying = [
                lax.ppermute(block, "chip", ring_pairs(direction))
                for block, direction in zip(sides, (1, -1))
            ]
        if self.swap and ready:
            pairs = [(step, block, jax.tree.map(swap_cores, block)) for step, block in new]
            self.pairs += pairs
            self.outputs = self.take(self.outputs, pairs)
        self.state = (flying, self.outputs)

    def advance(self, state):
        arrived, self.outputs = state
        self.new = [-self.count, self.count]
        if self.count == self.reach:
            self.new = [self.count]
        self.ready = arrived

    def busy(self):
        return bool(self.state[0])


def add_kernel(wanted, count, _, *refs):
    outputs, refs = refs[-count:], list(refs[:-count])
    keep_in, far_in = refs.pop(0), refs.pop(0)
    at = pl.program_id(0)

    def put(output, total):
        output[...] = total.astype(BF16)

    for places, output in zip(wanted, outputs):
        near, far = refs.pop(0), refs.pop(0)
        total = product(near[...], keep_in[...], 0, 0) + product(far[...], far_in[...], 0, 0)
        arrived = [(place, refs.pop(0)) for place in places]
        if count > len(wanted):
            for place in range(count):
                pl.when(at == place)(functools.partial(put, outputs[place], total))
            return
        for place, part in arrived:
            if place is None:
                total += part[...].astype(F32)
        put(output, total)
        for place, part in arrived:
            if place is not None:
                pl.when(at == place)(lambda: put(output, total + part[...].astype(F32)))


class Reduce:
    def __init__(self, keep, far, keep_in, far_in, table):
        self.chips, self.table = lax.axis_size("chip"), table
        self.operands, self.sides = (keep, far), (keep_in, far_in)
        self.units = keep.shape[1] // self.chips
        self.tiled = self.units % 128 == 0
        self.left, self.rest = self.chips // 2, None
        blocks = self.add([(self.left, [])], True)
        self.send(blocks if len(blocks) > 1 else halves(blocks[0], blocks[0]))

    def send(self, ready):
        self.left -= 1
        self.state = [
            lax.ppermute(block, "chip", ring_pairs(direction))
            for block, direction in zip(ready, (1, -1))
        ]

    def advance(self, state):
        half = self.sides[0].shape[1] // 2
        ahead, behind = state
        places = (0, 1) if ahead.shape[1] == half else (None, None)
        self.ready = self.add(
            [(self.left, [(ahead, places[0])]), (-self.left, [(behind, places[1])])]
        )

    def arrive(self, values):
        self.state, values = lax.optimization_barrier((self.state, values))
        return values

    def finish(self):
        ahead, behind = self.state
        return self.add([(0, [(ahead, None), (behind, None)])])[0]

    def add(self, wanted, split=False):
        (rows, model), units, chips = self.sides[0].shape, self.units, self.chips
        if not self.tiled:
            sums = []
            for step, parts in wanted:
                start = self.table[step % chips] * units
                total = jnp.zeros((units, model), F32)
                for operand, side in zip(self.operands, self.sides):
                    block = lax.dynamic_slice_in_dim(operand, start, units, 1)
                    total += product(block, side, 0, 0)
                for part, place in parts:
                    start = (place or 0) * part.shape[1]
                    total = total.at[:, start : start + part.shape[1]].add(part.astype(F32))
                sums.append(total.astype(BF16))
            return sums
        half = model // 2
        side = pl.BlockSpec((rows, half), lambda at, table: (0, at))
        whole = pl.BlockSpec((units, half), lambda at, table: (0, at))
        fixed = pl.BlockSpec((units, half), lambda at, table: (0, 0))
        specs, arrays = [side] * 2, list(self.sides)
        for step, parts in wanted:
            block = pl.BlockSpec(
                (rows, units), lambda at, table, step=step % chips: (0, table[step])
            )
            specs += [block] * 2 + [whole if place is None else fixed for _, place in parts]
            arrays += list(self.operands) + [part for part, _ in parts]
        places = [[place for _, place in parts] for _, parts in wanted]
        shapes, outs = [struct((units, model), BF16)] * len(wanted), [whole] * len(wanted)
        if split:
            shapes, outs = [struct((units, half), BF16)] * 2, [fixed] * 2
        return pl.pallas_call(
            functools.partial(add_kernel, places, len(shapes)),
            grid_spec=pltpu.PrefetchScalarGridSpec(
                num_scalar_prefetch=1,
                grid=(2,),
                in_specs=specs,
                out_specs=outs,
            ),
            out_shape=shapes,
            compiler_params=streaming,
            cost_estimate=light,
            name="ring_add",
        )(self.table, *arrays)

    def place(self, outputs, pairs):
        units, chips, model = self.units, self.chips, self.sides[0].shape[1]
        size, extra = self.size, self.extra
        shapes = [struct((chips * units, model), F32), struct((model, chips * units), F32)]
        if not self.tiled:
            outputs = outputs or [jnp.zeros(shape.shape, F32) for shape in shapes]
            down, up = outputs
            is_down = self.table[2 * chips] == 0
            for step, near, far in pairs:
                start = self.table[step % chips] * units
                near, far = whole_block(near)[:units], whole_block(far)[:units]
                first = jnp.where(is_down, near, far).astype(F32)
                second = jnp.where(is_down, far, near).astype(F32).T
                down = lax.dynamic_update_slice_in_dim(down, first, start, 0)
                up = lax.dynamic_update_slice_in_dim(up, second, start, 1)
            return [down, up]
        first = pairs[0][0] % chips
        stride = pairs[-1][0] % chips - first
        blocks = [pieces_of(pair[1]) + pieces_of(pair[2]) for pair in pairs]
        flat = [piece for block in blocks for piece in block]

        def place(at, table):
            return table[first + at * stride]

        def chip(at, table):
            return table[chips + first + at * stride]

        column = pl.BlockSpec(
            (model, 2 * HD), lambda at, table: (0, lax.div(chip(at, table), 2))
        )
        columns = [column] * (3 if outputs else 0)
        heads = [[first, first + stride][at] + chips for at in range(len(pairs))]
        return pl.pallas_call(
            functools.partial(place_kernel, heads, len(blocks[0]) // 2, (units, size, extra)),
            grid_spec=pltpu.PrefetchScalarGridSpec(
                num_scalar_prefetch=1,
                grid=(len(pairs),),
                in_specs=[pl.BlockSpec(memory_space=pl.ANY)] * (len(outputs) - len(columns))
                + columns
                + [pl.BlockSpec(piece.shape, lambda at, table: (0, 0)) for piece in flat],
                out_specs=[
                    pl.BlockSpec((units, model), lambda at, table: (place(at, table), 0)),
                    pl.BlockSpec((model, units), lambda at, table: (0, place(at, table))),
                    pl.BlockSpec((2, 1, extra, model), lambda at, table: (0, chip(at, table), 0, 0)),
                    pl.BlockSpec(
                        (1, 2, small_rows, model), lambda at, table: (chip(at, table), 0, 0, 0)
                    ),
                ]
                + [column] * 3,
            ),
            out_shape=shapes
            + [
                struct((2, chips, extra, model), F32),
                struct((chips, 2, small_rows, model), F32),
            ]
            + [struct((model, chips * HD), F32)] * 3,
            input_output_aliases={1 + at: at for at in range(len(outputs))},
            compiler_params=streaming,
            cost_estimate=light,
            name="place",
        )(self.table, *outputs, *flat)


def place_kernel(heads, width, sizes, table, *refs):
    count = len(heads)
    refs, (down, up, weight, small), projections = refs[:-7], refs[-7:-3], refs[-3:]
    blocks, refs = refs[-2 * width * count :], refs[: -2 * width * count]
    core = table[table.shape[0] - 2]
    units, size, extra = sizes
    rows = [pl.ds(0, units), pl.ds(units, size), pl.ds(units + size, extra)]
    rows.append(pl.ds(units + size + extra, small_rows))

    def read(block, which):
        return jnp.concatenate([piece[rows[which], :] for piece in block], axis=1)

    def put(first, second, head):
        down[...] = read(first, 0).astype(F32)
        up[...] = read(second, 0).astype(F32).T
        for side, block in ((0, first), (1, second)):
            weight[side, 0] = read(block, 2).astype(F32)
            small[0, side] = read(block, 3).astype(F32)
        both = jnp.concatenate([read(first, 1), read(second, 1)], axis=0)
        for at, output in enumerate(projections):
            part = both[at * HD : at * HD + HD].astype(F32)
            part = jnp.concatenate([part, part], axis=0).T
            if refs:
                mine = lax.broadcasted_iota(jnp.int32, part.shape, 1) // HD == head % 2
                part = jnp.where(mine, part, refs[at - 3][...])
            output[...] = part

    for at in range(count):
        near, far = (
            blocks[(2 * at + side) * width : (2 * at + side + 1) * width] for side in range(2)
        )
        head = table[heads[at]]
        here = pl.program_id(0) == at
        pl.when(here & (core == 0))(functools.partial(put, near, far, head))
        pl.when(here & (core != 0))(functools.partial(put, far, near, head))


def head_gradient_kernel(steps, chips, table, grads_ref, *refs):
    parts, out_ref = refs[:-1], refs[-1]
    patches = grads_ref.shape[2]
    for at, part in enumerate(parts):

        @pl.when(pl.program_id(0) == at)
        def _(part=part):
            total = jnp.zeros(out_ref.shape, F32)
            for index, step in enumerate(steps):
                chip = table[chips + step % chips]
                total += product(grads_ref[chip], part[pl.ds(index * patches, patches), :])
            out_ref[...] = total.astype(BF16)


def head_gradient(grads, parts, steps, table):
    chips, rows, _ = grads.shape
    columns = parts[0].shape[1]

    def column(at, table):
        mine = table[2 * chips + 1] if len(parts) > 1 else 0
        return (0, jnp.where(at == 0, mine, 1 - mine))

    return pl.pallas_call(
        functools.partial(head_gradient_kernel, steps, chips),
        grid_spec=pltpu.PrefetchScalarGridSpec(
            num_scalar_prefetch=1,
            grid=(len(parts),),
            in_specs=[
                pl.BlockSpec(array.shape, lambda at, table, rank=array.ndim: (0,) * rank)
                for array in (grads, *parts)
            ],
            out_specs=pl.BlockSpec((rows, columns), column),
        ),
        out_shape=struct((rows, columns * len(parts)), BF16),
        compiler_params=streaming,
        cost_estimate=light,
        name="head_gradient",
    )(table, grads, *parts)


def core_half(values, axis, side):
    size = values.shape[axis] // 2
    return lax.dynamic_slice_in_dim(values, side * size, size, axis)


def share_halves(values, axis):
    core = lax.axis_index("core")
    return core_half(values, axis, core), swap_cores(core_half(values, axis, 1 - core))


def local(
    block_input,
    out_grad,
    segments,
    lead_steps,
    gain_attn,
    shift_attn,
    lead_weight,
    query_weight,
    key_weight,
    value_weight,
    output_weight,
    output_bias,
    gain_mlp,
    shift_mlp,
    up_weight,
    up_bias,
    down_weight,
    down_bias,
):
    rows, model = block_input.shape
    heads = query_weight.shape[1] // HD
    width = heads * HD
    chips, core = lax.axis_size("chip"), lax.axis_index("core")
    split = chips // heads
    crops = lead_steps.shape[0]
    table = ring_table()
    weights = (query_weight, key_weight, value_weight)
    cut = model // 2 if lax.axis_size("head") == 2 else model
    payload, attn_in, attn_in_cut = project(
        table, cut, block_input, segments, lead_steps, gain_attn, shift_attn, lead_weight, weights
    )
    if split == 1:
        own = to_heads(payload)
        queries = own
    else:
        queries = scatter_queries(payload.reshape(-1, rows), heads, split)
        own = to_heads(jnp.repeat(payload, split, axis=0))
    own, attn_in_cut = lax.optimization_barrier((own, attn_in_cut))
    inputs = Gather(attn_in_cut)
    inputs.send(inputs.ready)
    other = swap_cores(own)
    raw, out, logsum = attention_forward(queries, own, other, crops)
    inputs.state, out = lax.optimization_barrier((inputs.state, out))
    attn_out = gather_queries(out, heads, split, rows)
    attn_out = visit([inputs], attn_out)
    branches = across_heads(product(attn_out, output_weight, 0, 0).astype(BF16))
    visit([inputs], ())
    keep, give, keep_in, give_in, hidden, dup_bias, mlp_part, d_mlp_part = mlp(
        table,
        block_input,
        out_grad,
        branches,
        output_bias,
        gain_mlp,
        shift_mlp,
        up_weight,
        up_bias,
        down_weight,
    )
    keep, give, keep_in, give_in, d_mlp_part = visit(
        [inputs], (keep, give, keep_in, give_in, d_mlp_part)
    )
    d_mlp = across_heads(d_mlp_part)
    ring = Reduce(keep, swap_cores(give), keep_in, swap_cores(give_in), table)
    mlp_part, d_mlp = lax.optimization_barrier((mlp_part, d_mlp))
    d_hidden, d_branch, d_attn, sums = middle(hidden, out_grad, d_mlp, gain_mlp, output_weight)
    grads = scatter_queries(d_attn, heads, split)
    d_branch, mlp_part = visit([ring, inputs], (d_branch, mlp_part))
    while inputs.busy():
        visit([inputs], ())
    mlp_out = across_heads(mlp_part)
    out_near, out_far = share_halves(attn_out, 0)
    doutput = product(out_near, d_branch) + product(out_far, swap_cores(d_branch))
    doutput = doutput.astype(BF16).reshape(chips, -1, model)
    steps, inputs = zip(*inputs.blocks)
    inputs = join(inputs)
    parts = across_heads(inputs) if cut != model else [inputs]
    grads, doutput = visit([ring], (grads, doutput))
    doutput = to_heads(doutput)
    dquery, far_sums = attention_backward(queries, grads, raw, logsum, other, [], crops)
    far_sums = swap_cores(far_sums)
    grads, dquery = visit([ring], (grads, dquery))
    head_grads = attention_backward(
        queries, grads, raw, logsum, own, [dquery, far_sums], crops
    )
    head_grads = ring.arrive(head_grads)
    doutput, head_grads = lax.optimization_barrier((doutput, head_grads))
    doutput = jnp.sum(doutput.astype(F32), axis=0)
    small = jnp.concatenate([sums.reshape(-1), dup_bias[0]])
    small = jnp.pad(small, (0, small_rows * model - small.shape[0])).reshape(small_rows, model)
    doutput = jnp.concatenate([doutput, small], axis=0).astype(BF16)
    if split == 1:
        (head_grads,) = head_grads
        moved = to_heads(head_grads)
        projections = head_gradient(head_grads, parts, steps, table)
        near, far = share_halves(projections, 0)
        projections = (near.astype(F32) + far.astype(F32)).astype(BF16)
        size = projections.shape[0]
        blocks = jnp.concatenate([projections, doutput], axis=0)
        dquery, dkey, dvalue = (
            moved[:, at * HD : at * HD + HD].reshape(width, rows) for at in range(3)
        )
    else:
        dquery, key_value = head_grads
        dquery = gather_queries(dquery, heads, split, rows)
        moved = to_heads(key_value).reshape(heads, split, 2 * HD, rows).astype(F32)
        moved = jnp.sum(moved, axis=1).astype(BF16)
        dkey, dvalue = (moved[:, at * HD : at * HD + HD].reshape(width, rows) for at in range(2))
        size, blocks = 0, doutput
        projections = [
            lax.psum(product(attn_in, grad, 0, 1).astype(BF16), ("chip", "core")).astype(F32)
            for grad in (dquery, dkey, dvalue)
        ]
    total = ring.finish()
    start = total.shape[0]
    ring.size, ring.extra = size, blocks.shape[0] - size - small_rows
    gathered = Gather(jnp.concatenate([total, blocks], axis=0), True, ring.place)
    gathered.send(gathered.ready)
    d_part = (
        product(dquery, query_weight, 0, 1)
        + product(dkey, key_weight, 0, 1)
        + product(dvalue, value_weight, 0, 1)
    )
    d_in = across_heads(d_part.astype(BF16))
    unit_attn, inverse_attn = normalize(block_input.astype(F32))
    onehot = (segments[:, None] == jnp.arange(crops, dtype=jnp.int32)[None, :]).astype(F32)
    lead = jnp.sum(onehot * lead_steps.astype(F32)[None, :], axis=1) / 12.0
    ends = jnp.stack(
        [
            jnp.sum(d_part * unit_attn, axis=0),
            jnp.sum(d_part, axis=0),
            jnp.sum(lead[:, None] * d_part, axis=0),
        ]
    )
    ends = ends.reshape(-1, 128)
    ends = functools.reduce(jnp.add, across_heads(ends))
    ends = ends + swap_cores(ends)
    moves = [chips >> (at + 1) for at in range(chips.bit_length() - 1)][::-1]

    def step_ends(ends):
        if not moves:
            return [ends]
        reach = moves.pop(0)
        pairs = [(chip, chip ^ reach) for chip in range(chips)]
        return [ends, lax.ppermute(ends, "chip", pairs)]

    ends = step_ends(visit([gathered], ends))
    ends, mlp_out = visit([gathered], (ends, mlp_out))
    ends = step_ends(functools.reduce(jnp.add, ends))
    block_output = hidden + down_bias
    for part in mlp_out:
        block_output += part.astype(F32)
    block_output = block_output.astype(BF16)
    d_in, block_output, ends = visit([gathered], (d_in, block_output, ends))
    ends = step_ends(functools.reduce(jnp.add, ends))
    d_in = functools.reduce(jnp.add, (part.astype(F32) for part in d_in))
    input_grad = (d_hidden + normalize_back(d_in * gain_attn, unit_attn, inverse_attn)).astype(
        BF16
    )
    while gathered.busy() or moves:
        input_grad, ends = visit([gathered], (input_grad, ends))
        ends = step_ends(functools.reduce(jnp.add, ends))
    ends = functools.reduce(jnp.add, ends).reshape(3, model)
    ddown_weight, dup_weight, *rest = gathered.outputs
    if split == 1:
        doutput_weight, small, *projections = rest
        doutput_weight = doutput_weight.reshape(width, model)
    if split != 1:
        blocks = jnp.zeros((2, chips) + blocks.shape, F32)
        for step, near, far in gathered.pairs:
            for side, block in ((core, near), (1 - core, far)):
                at = (side, table[chips + step % chips], 0, 0)
                block = whole_block(block)[None, None, start:].astype(F32)
                blocks = lax.dynamic_update_slice(blocks, block, at)
        doutput_weight = blocks[:, :, :-small_rows].reshape(width, model)
        small = blocks[:, :, -small_rows:]
    small = jnp.sum(small, axis=(0, 1))
    dup_bias = small[4:].reshape(-1)[: dup_bias.shape[1]]
    return (
        block_output,
        input_grad,
        ends[0],
        ends[1],
        ends[2],
        *projections,
        doutput_weight,
        *small[:3],
        dup_weight,
        dup_bias,
        ddown_weight,
        small[3],
    )


def solution(mesh):
    bands, halves = mesh.shape["band"], mesh.shape["head"]
    inner = Mesh(mesh.devices.reshape(bands // 2, 2, halves), ("chip", "core", "head"))
    band = ("chip", "core")
    rows, columns, split_rows = P(band, None), P(None, "head"), P("head", None)
    return jax.shard_map(
        local,
        mesh=inner,
        in_specs=(
            rows,
            rows,
            P(band),
            P(),
            P(),
            P(),
            P(),
            columns,
            columns,
            columns,
            split_rows,
            P(),
            P(),
            P(),
            columns,
            P("head"),
            split_rows,
            P(),
        ),
        out_specs=(
            rows,
            rows,
            P(),
            P(),
            P(),
            columns,
            columns,
            columns,
            split_rows,
            P(),
            P(),
            P(),
            columns,
            P("head"),
            split_rows,
            P(),
        ),
        check_vma=False,
    )
```

```python
import functools
import math

import jax
import jax.numpy as jnp
from jax import lax
from jax.experimental import pallas as pl
from jax.experimental.pallas import tpu as pltpu
from jax.sharding import Mesh, PartitionSpec as P

HD = 64
F32 = jnp.float32
BF16 = jnp.bfloat16
eps = 1e-05
masked_value = -1e30
seg_row = 3 * HD
payload_rows = 3 * HD + 16
small_rows = 16
params = pltpu.CompilerParams(vmem_limit_bytes=48 * 2**20)
streaming = pltpu.CompilerParams(vmem_limit_bytes=63_400_000)


def normalize(values):
    centred = values - jnp.mean(values, axis=-1, keepdims=True)
    inverse = lax.rsqrt(jnp.mean(centred * centred, axis=-1, keepdims=True) + eps)
    return (centred * inverse, inverse)


def normalize_back(grad_unit, unit, inverse):
    return inverse * (
        grad_unit
        - jnp.mean(grad_unit, axis=-1, keepdims=True)
        - unit * jnp.mean(grad_unit * unit, axis=-1, keepdims=True)
    )


def product(first, second, first_axis=1, second_axis=0):
    return lax.dot_general(
        first,
        second,
        (((first_axis,), (second_axis,)), ((), ())),
        preferred_element_type=jnp.float32,
    )


def struct(shape, dtype):
    return jax.ShapeDtypeStruct(shape, dtype)


def whole_spec(shape):
    return pl.BlockSpec(shape, lambda *at: (0,) * len(shape))


light = pl.CostEstimate(flops=1, bytes_accessed=1, transcendentals=0)


def project_kernel(
    table, input_ref, segment_ref, steps_ref, gain, shift, lead_weight, *refs
):
    weights, (payload_ref, attn_in_ref, cut_ref) = refs[:3], refs[3:]
    rows = input_ref.shape[0]

    @pl.when(pl.program_id(0) == 0)
    def _():
        unit, _ = normalize(input_ref[...].astype(F32))
        crops = steps_ref.shape[0]
        crop = lax.broadcasted_iota(jnp.int32, (crops, rows), 0)
        steps = jnp.zeros((crops, rows), jnp.int32)
        for at in range(crops):
            steps = jnp.where(crop == at, steps_ref[at], steps)
        steps = jnp.where(crop == segment_ref[...], steps, 0).astype(F32)
        lead = product(steps, jnp.ones((crops, 128), F32), 0, 0)[:, :1] / 12.0
        attn_in = unit * gain[...] + shift[...] + lead * lead_weight[...]
        attn_in = attn_in.astype(BF16)
        attn_in_ref[...] = attn_in
        columns = cut_ref.shape[1]
        first = table[table.shape[0] - 1] % (attn_in.shape[1] // columns) == 0
        cut_ref[...] = jnp.where(first, attn_in[:, :columns], attn_in[:, -columns:])

    for at, weight in enumerate(weights):
        part = product(attn_in_ref[...], weight[...]).T.astype(BF16)
        for head in range(2):
            payload_ref[head, pl.ds(at * HD, HD), :] = part[head * HD : head * HD + HD]
    segment = jnp.broadcast_to(segment_ref[...].astype(F32), (16, rows)).astype(BF16)
    for head in range(2):
        payload_ref[head, pl.ds(seg_row, 16), :] = segment


def project(table, cut, block_input, segments, lead_steps, gain, shift, lead_weight, weights):
    rows, model = block_input.shape
    heads = weights[0].shape[1] // HD
    line = whole_spec((1, model))
    column = pl.BlockSpec((model, 2 * HD), lambda at, table: (0, at))
    return pl.pallas_call(
        project_kernel,
        grid_spec=pltpu.PrefetchScalarGridSpec(
            num_scalar_prefetch=1,
            grid=(heads // 2,),
            in_specs=[
                whole_spec(block_input.shape),
                whole_spec((1, rows)),
                pl.BlockSpec(memory_space=pltpu.SMEM),
            ]
            + [line] * 3
            + [column] * 3,
            out_specs=[
                pl.BlockSpec((2, payload_rows, rows), lambda at, table: (at, 0, 0)),
                whole_spec((rows, model)),
                whole_spec((rows, cut)),
            ],
        ),
        out_shape=[
            struct((heads, payload_rows, rows), BF16),
            struct((rows, model), BF16),
            struct((rows, cut), BF16),
        ],
        compiler_params=streaming,
        cost_estimate=light,
        name="project",
    )(table, block_input, segments[None], lead_steps, gain[None], shift[None], lead_weight[None], *weights)


def mlp_kernel(count, core_ref, input_ref, grad_ref, *refs):
    branches, refs = refs[:count], refs[count:]
    output_bias, gain, shift, up_weight, up_bias, down_weight = refs[:6]
    keep_ref, give_ref, keep_in_ref, give_in_ref, hidden_ref, bias_ref, forward_ref, back_ref = refs[
        6:14
    ]
    mlp_in_ref, forward, back = refs[14:]
    at = pl.program_id(0)
    is_down = core_ref[core_ref.shape[0] - 2] == 0

    @pl.when(at == 0)
    def _():
        hidden = input_ref[...].astype(F32) + output_bias[...]
        for branch in branches:
            hidden += branch[...].astype(F32)
        hidden_ref[...] = hidden
        unit, _ = normalize(hidden)
        mlp_in = (unit * gain[...] + shift[...]).astype(BF16)
        mlp_in_ref[...] = mlp_in
        keep_in_ref[...] = jnp.where(is_down, grad_ref[...], mlp_in)
        give_in_ref[...] = jnp.where(is_down, mlp_in, grad_ref[...])
        forward[...] = jnp.zeros_like(forward)
        back[...] = jnp.zeros_like(back)

    upper = product(mlp_in_ref[...], up_weight[...]) + up_bias[...]
    share = 0.5 + 0.5 * lax.erf(upper * math.sqrt(0.5))
    slope = share + upper * (jnp.exp(upper * upper * -0.5) * (1.0 / math.sqrt(2.0 * math.pi)))
    active = (upper * share).astype(BF16)
    d_active = product(grad_ref[...], down_weight[...], 1, 1)
    d_upper = (d_active * slope).astype(BF16)
    keep_ref[...] = jnp.where(is_down, active, d_upper)
    give_ref[...] = jnp.where(is_down, d_upper, active)
    bias_ref[...] = jnp.sum(d_upper.astype(F32), axis=0, keepdims=True)
    forward[...] += product(active, down_weight[...])
    back[...] += product(d_upper, up_weight[...], 1, 1)

    @pl.when(at == pl.num_programs(0) - 1)
    def _():
        forward_ref[...] = forward[...].astype(BF16)
        back_ref[...] = back[...].astype(BF16)


def mlp(
    table, block_input, out_grad, branches, output_bias, gain, shift, up_weight, up_bias, down_weight
):
    rows, model = block_input.shape
    units = up_weight.shape[1]
    step = math.gcd(units, 512)
    tile, line = whole_spec((rows, model)), whole_spec((1, model))
    wide = pl.BlockSpec((rows, step), lambda at, table: (0, at))
    bias = pl.BlockSpec((1, step), lambda at, table: (0, at))
    return pl.pallas_call(
        functools.partial(mlp_kernel, len(branches)),
        grid_spec=pltpu.PrefetchScalarGridSpec(
            num_scalar_prefetch=1,
            grid=(units // step,),
            in_specs=[tile] * (2 + len(branches))
            + [line] * 3
            + [
                pl.BlockSpec((model, step), lambda at, table: (0, at)),
                bias,
                pl.BlockSpec((step, model), lambda at, table: (at, 0)),
            ],
            out_specs=[wide, wide, tile, tile, tile, bias, tile, tile],
            scratch_shapes=[pltpu.VMEM((rows, model), BF16)]
            + [pltpu.VMEM((rows, model), F32)] * 2,
        ),
        out_shape=[struct((rows, units), BF16)] * 2
        + [struct((rows, model), BF16)] * 2
        + [
            struct((rows, model), F32),
            struct((1, units), F32),
            struct((rows, model), BF16),
            struct((rows, model), BF16),
        ],
        compiler_params=streaming,
        cost_estimate=light,
        name="mlp",
    )(
        table,
        block_input,
        out_grad,
        *branches,
        output_bias[None],
        gain[None],
        shift[None],
        up_weight,
        up_bias[None],
        down_weight,
    )


def middle_kernel(count, hidden_ref, grad_ref, *refs):
    parts, refs = refs[:count], refs[count:]
    gain, output_weight, d_hidden_ref, d_branch_ref, d_attn_ref, sums_ref = refs
    unit, inverse = normalize(hidden_ref[...])
    d_mlp = parts[0][...].astype(F32)
    for part in parts[1:]:
        d_mlp += part[...].astype(F32)
    grad = grad_ref[...].astype(F32)
    d_hidden = grad + normalize_back(d_mlp * gain[...], unit, inverse)
    d_hidden_ref[...] = d_hidden
    d_branch = d_hidden.astype(BF16)
    d_branch_ref[...] = d_branch
    d_attn_ref[...] = product(output_weight[...], d_branch, 1, 1).astype(BF16)
    for at, values in enumerate((d_hidden, d_mlp * unit, d_mlp, grad)):
        sums_ref[pl.ds(at, 1), :] = jnp.sum(values, axis=0, keepdims=True)


def middle(hidden, out_grad, parts, gain, output_weight):
    rows, model = hidden.shape
    width = output_weight.shape[0]
    return pl.pallas_call(
        functools.partial(middle_kernel, len(parts)),
        out_shape=[
            struct((rows, model), F32),
            struct((rows, model), BF16),
            struct((width, rows), BF16),
            struct((4, model), F32),
        ],
        compiler_params=streaming,
        cost_estimate=light,
        name="middle",
    )(hidden, out_grad, *parts, gain[None], output_weight)


def mask_rows(piece, chip, crops):
    crop = lax.broadcasted_iota(jnp.int32, (HD, piece.shape[2]), 0)
    segment = piece[chip, pl.ds(seg_row, 16), :].astype(F32)[:1].astype(jnp.int32)
    return jnp.where((crop != segment) & (crop < crops), masked_value, 0.0)


def load_keys(piece, crops, keys, key_t, value_n):
    chips, _, patches = piece.shape
    for chip in range(chips):
        key = piece[chip, pl.ds(HD, HD), :]
        value = piece[chip, pl.ds(2 * HD, HD), :]
        place = pl.ds(chip * patches, patches)
        both = jnp.concatenate([key.astype(F32), mask_rows(piece, chip, crops)], axis=0)
        keys[place, :] = both.T.astype(BF16)
        key_t[:, place] = key
        value_n[place, :] = value.astype(F32).T.astype(BF16)


def masked_query(query_ref, dtype=BF16):
    query = query_ref[0, pl.ds(0, HD), :].astype(F32) * 0.125
    segment = query_ref[0, pl.ds(seg_row, 16), :].astype(F32)[:1].astype(jnp.int32)
    crop = lax.broadcasted_iota(jnp.int32, query.shape, 0)
    onehot = jnp.where(crop == segment, 1.0, 0.0)
    return jnp.concatenate([query, onehot], axis=0).astype(dtype)


def forward_kernel(
    crops, step, query_ref, own, other, raw_ref, out_ref, logsum_ref, key_t, value_n, scores
):
    @pl.when(pl.program_id(0) == 0)
    def _():
        start = 0
        for piece in (own, other):
            chips, _, patches = piece.shape
            for chip in range(chips):
                place = pl.ds(start, patches)
                key = piece[chip, pl.ds(HD, HD), :].astype(F32)
                key_t[:, place] = jnp.concatenate([key, mask_rows(piece, chip, crops)], axis=0).astype(BF16)
                value = piece[chip, pl.ds(2 * HD, HD), :].astype(F32)
                value = jnp.concatenate([value, jnp.ones_like(value)], axis=0)
                value_n[place, :] = value.T.astype(BF16)
                start += patches

    query = masked_query(query_ref, F32).T.astype(BF16)
    count = query.shape[0]
    top = jnp.full((count, 128), masked_value, F32)
    for start in range(0, key_t.shape[1], step):
        block = product(query, key_t[:, pl.ds(start, step)])
        scores[:, pl.ds(start, step)] = block
        for at in range(0, step, 128):
            top = jnp.maximum(top, block[:, at : at + 128])
    top = jnp.max(top, axis=1, keepdims=True)
    accum = jnp.zeros((count, 2 * HD), F32)
    for start in range(0, key_t.shape[1], step):
        weights = jnp.exp(scores[:, pl.ds(start, step)] - top).astype(BF16)
        accum += product(weights, value_n[pl.ds(start, step), :])
    accum = accum.T
    total = accum[HD : HD + 1]
    raw = accum[:HD] / total
    raw_ref[0] = raw
    out_ref[0] = raw.astype(BF16)
    top = jnp.broadcast_to(top, (count, 128)).T[:1]
    logsum_ref[0] = top + jnp.log(total)


def backward_kernel(
    crops,
    extra,
    query_ref,
    grad_ref,
    raw_ref,
    logsum_ref,
    piece,
    *refs,
):
    extras, refs = refs[:extra], refs[extra:]
    outputs, (keys, key_t, value_n, sums) = refs[:-4], refs[-4:]
    group = pl.program_id(0)

    @pl.when(group == 0)
    def _():
        load_keys(piece, crops, keys, key_t, value_n)
        sums[...] = jnp.zeros_like(sums)

    query = masked_query(query_ref)
    grad = grad_ref[0]
    grad_wide = grad.astype(F32)
    delta = jnp.sum(grad_wide * raw_ref[0], axis=0, keepdims=True)
    scaled = query_ref[0, pl.ds(0, HD), :].astype(F32) * 0.125
    zero = jnp.zeros_like(scaled)
    query_side = jnp.concatenate([scaled, zero], axis=0).T.astype(BF16)
    grad_side = jnp.concatenate([zero, grad_wide], axis=0).T.astype(BF16)
    probs = jnp.exp(product(keys[...], query) - logsum_ref[0])
    dprobs = product(value_n[...], grad)
    dscores = (probs * (dprobs - delta)).astype(BF16)
    sums[...] += product(dscores, query_side) + product(probs.astype(BF16), grad_side)
    dquery = product(key_t[...], dscores) * 0.125
    if extras:
        dquery += extras[0][0]
    if len(outputs) == 1:
        outputs[0][group, pl.ds(0, HD), :] = dquery.astype(BF16)
    else:
        outputs[0][0] = dquery.astype(outputs[0].dtype)

    @pl.when(group == pl.num_programs(0) - 1)
    def _():
        chips, _, patches = piece.shape
        for chip in range(chips):
            total = sums[pl.ds(chip * patches, patches), :].T
            if extra > 1:
                total += extras[1][chip].astype(F32)
            total = total.astype(BF16)
            if len(outputs) == 1:
                outputs[0][chip, pl.ds(HD, 2 * HD), :] = total
            else:
                outputs[1][chip] = total


def key_step(count):
    return 1024 if count % 1024 == 0 else 256


def query_spec(rows, patches):
    return pl.BlockSpec((1, rows, patches), lambda group: (group, 0, 0))


def attention_forward(queries, own, other, crops):
    groups, _, patches = queries.shape
    count = 2 * own.shape[0] * own.shape[2]
    return pl.pallas_call(
        functools.partial(forward_kernel, crops, key_step(count)),
        grid=(groups,),
        in_specs=[
            query_spec(payload_rows, patches),
            whole_spec(own.shape),
            whole_spec(other.shape),
        ],
        out_specs=[query_spec(HD, patches), query_spec(HD, patches), query_spec(1, patches)],
        out_shape=[
            struct((groups, HD, patches), F32),
            struct((groups, HD, patches), BF16),
            struct((groups, 1, patches), F32),
        ],
        scratch_shapes=[
            pltpu.VMEM((2 * HD, count), BF16),
            pltpu.VMEM((count, 2 * HD), BF16),
            pltpu.VMEM((patches, count), F32),
        ],
        compiler_params=streaming,
        cost_estimate=light,
        name="attention_forward",
    )(queries, own, other)


def attention_backward(queries, grads, raw, logsum, keys, extras, crops):
    groups, _, patches = queries.shape
    chips, count = keys.shape[0], keys.shape[0] * keys.shape[2]
    sums_shape = (chips, 2 * HD, keys.shape[2])
    specs = [query_spec(HD, patches), whole_spec(sums_shape)]
    shapes = [
        struct((groups, HD, patches), BF16 if extras else F32),
        struct(sums_shape, BF16),
    ]
    outs = specs
    if extras and (groups, patches) == (chips, keys.shape[2]):
        shapes = [struct((chips, 3 * HD, patches), BF16)]
        outs = [whole_spec(shapes[0].shape)]
    return pl.pallas_call(
        functools.partial(backward_kernel, crops, len(extras)),
        grid=(groups,),
        in_specs=[
            query_spec(payload_rows, patches),
            query_spec(HD, patches),
            query_spec(HD, patches),
            query_spec(1, patches),
            whole_spec(keys.shape),
        ]
        + specs[: len(extras)],
        out_specs=outs,
        out_shape=shapes,
        scratch_shapes=[
            pltpu.VMEM((count, 2 * HD), BF16),
            pltpu.VMEM((HD, count), BF16),
            pltpu.VMEM((count, HD), BF16),
            pltpu.VMEM((count, 2 * HD), F32),
        ],
        compiler_params=params,
        cost_estimate=light,
        name="attention_backward",
    )(queries, grads, raw, logsum, keys, *extras)


def swap_cores(values):
    return lax.ppermute(values, "core", [(0, 1), (1, 0)])


def to_heads(blocks):
    return lax.all_to_all(blocks, "chip", 0, 0, tiled=True)


def scatter_queries(values, heads, split):
    rows, patches = values.shape[0] // heads, values.shape[1]
    if split == 1:
        return to_heads(values.reshape(heads, rows, patches))
    part = patches // split
    blocks = values.reshape(heads, rows, split, part).transpose(0, 2, 1, 3)
    moved = to_heads(blocks.reshape(heads * split, rows, part))
    width = min(256, moved.shape[0] * part)
    joined = moved.transpose(1, 0, 2).reshape(rows, -1, width)
    return joined.transpose(1, 0, 2)


def gather_queries(values, heads, split, patches):
    rows = values.shape[1]
    if split == 1:
        return to_heads(values).reshape(heads * rows, patches)
    part = patches // split
    joined = values.transpose(1, 0, 2).reshape(rows, heads * split, part)
    moved = to_heads(joined.transpose(1, 0, 2)).reshape(heads, split, rows, part)
    return moved.transpose(0, 2, 1, 3).reshape(heads * rows, patches)


def across_heads(part):
    if lax.axis_size("head") == 2:
        return [part, lax.ppermute(part, "head", [(0, 1), (1, 0)])]
    return [lax.psum(part, "head")]


def ring_pairs(direction):
    chips = lax.axis_size("chip")
    order = list(range(0, chips, 2)) + list(range(chips - 1, 0, -2))
    return [(order[at], order[(at + direction) % chips]) for at in range(chips)]


def ring_table():
    chips, chip = lax.axis_size("chip"), lax.axis_index("chip")
    place = jnp.where(chip % 2 == 0, chip // 2, chips - 1 - chip // 2)
    steps = jnp.arange(2 * chips + 2, dtype=jnp.int32)
    places = (place + steps) % chips
    there = jnp.where(places < chips // 2, 2 * places, 2 * (chips - 1 - places) + 1)
    table = jnp.where(steps < chips, places, there)
    table = jnp.where(steps == 2 * chips, lax.axis_index("core"), table)
    return jnp.where(steps == 2 * chips + 1, lax.axis_index("head"), table).astype(jnp.int32)


def visit(streams, values):
    states, values = lax.optimization_barrier(([stream.state for stream in streams], values))
    for stream, state in zip(streams, states):
        stream.advance(state)
    ready, values = lax.optimization_barrier(([stream.ready for stream in streams], values))
    for stream, blocks in zip(streams, ready):
        stream.send(blocks)
    return values


def pieces_of(block):
    return list(block) if isinstance(block, tuple) else [block]


def whole_block(block):
    return jnp.concatenate(pieces_of(block), axis=1)


def join_kernel(counts, *refs):
    output, refs, start = refs[-1], list(refs[:-1]), 0
    for count in counts:
        column = 0
        for _ in range(count):
            piece = refs.pop(0)
            rows, columns = piece.shape
            output[pl.ds(start, rows), pl.ds(column, columns)] = piece[...]
            column += columns
        start += rows


def join(blocks):
    blocks = [pieces_of(block) for block in blocks]
    rows = sum(block[0].shape[0] for block in blocks)
    columns = sum(piece.shape[1] for piece in blocks[0])
    return pl.pallas_call(
        functools.partial(join_kernel, [len(block) for block in blocks]),
        out_shape=struct((rows, columns), blocks[0][0].dtype),
        compiler_params=streaming,
        name="join",
    )(*[piece for block in blocks for piece in block])


def halves_kernel(left, right, left_ref, right_ref):
    left_ref[...] = left[...]
    right_ref[...] = right[...]


def halves(left, right):
    rows, columns = left.shape
    if rows % 16 or columns % 256:
        return [left[:, : columns // 2], right[:, columns // 2 :]]
    out = pl.BlockSpec((rows, columns // 2), lambda at: (0, 0))
    return pl.pallas_call(
        halves_kernel,
        grid=(1,),
        in_specs=[out, pl.BlockSpec((rows, columns // 2), lambda at: (0, 1))],
        out_specs=[out, out],
        out_shape=[struct((rows, columns // 2), left.dtype)] * 2,
        compiler_params=streaming,
        name="halves",
    )(left, right)


class Gather:
    def __init__(self, block, swap=False, take=None):
        self.reach, self.swap, self.take = lax.axis_size("chip") // 2, swap, take
        self.blocks, self.pairs, self.count = [], [], 0
        self.new, self.outputs = [0], []
        self.ready = [block]

    def send(self, ready):
        if len(self.new) < len(ready):
            ready = [tuple(ready)]
        new = list(zip(self.new, ready))
        self.blocks += new
        self.new = new
        self.count += 1
        sides = ready if len(ready) > 1 else ready * 2
        if self.count == self.reach:
            sides = halves(*sides)
        flying = []
        if self.count <= self.reach:
            flying = [
                lax.ppermute(block, "chip", ring_pairs(direction))
                for block, direction in zip(sides, (1, -1))
            ]
        if self.swap and ready:
            pairs = [(step, block, jax.tree.map(swap_cores, block)) for step, block in new]
            self.pairs += pairs
            self.outputs = self.take(self.outputs, pairs)
        self.state = (flying, self.outputs)

    def advance(self, state):
        arrived, self.outputs = state
        self.new = [-self.count, self.count]
        if self.count == self.reach:
            self.new = [self.count]
        self.ready = arrived

    def busy(self):
        return bool(self.state[0])


def add_kernel(wanted, count, _, *refs):
    outputs, refs = refs[-count:], list(refs[:-count])
    keep_in, far_in = refs.pop(0), refs.pop(0)
    at = pl.program_id(0)

    def put(output, total):
        output[...] = total.astype(BF16)

    for places, output in zip(wanted, outputs):
        near, far = refs.pop(0), refs.pop(0)
        total = product(near[...], keep_in[...], 0, 0) + product(far[...], far_in[...], 0, 0)
        arrived = [(place, refs.pop(0)) for place in places]
        if count > len(wanted):
            for place in range(count):
                pl.when(at == place)(functools.partial(put, outputs[place], total))
            return
        for place, part in arrived:
            if place is None:
                total += part[...].astype(F32)
        put(output, total)
        for place, part in arrived:
            if place is not None:
                pl.when(at == place)(lambda: put(output, total + part[...].astype(F32)))


def finish_kernel(counts, _, keep_in, far_in, near, far, ahead, behind, *refs):
    refs, output = list(refs[:-1]), refs[-1]
    total = product(near[...], keep_in[...], 0, 0) + product(far[...], far_in[...], 0, 0)
    total += ahead[...].astype(F32) + behind[...].astype(F32)
    start = total.shape[0]
    output[pl.ds(0, start), :] = total.astype(BF16)
    for count in counts:
        total = 0.0
        for _ in range(count):
            part = refs.pop(0)[...].astype(F32)
            total += part if part.ndim == 2 else jnp.sum(part, axis=0)
        output[pl.ds(start, total.shape[0]), :] = total.astype(BF16)
        start += total.shape[0]


class Reduce:
    def __init__(self, keep, far, keep_in, far_in, table):
        self.chips, self.table = lax.axis_size("chip"), table
        self.operands, self.sides = (keep, far), (keep_in, far_in)
        self.units = keep.shape[1] // self.chips
        self.tiled = self.units % 128 == 0
        self.left, self.rest = self.chips // 2, None
        blocks = self.add([(self.left, [])], True)
        self.send(blocks if len(blocks) > 1 else halves(blocks[0], blocks[0]))

    def send(self, ready):
        self.left -= 1
        self.state = [
            lax.ppermute(block, "chip", ring_pairs(direction))
            for block, direction in zip(ready, (1, -1))
        ]

    def advance(self, state):
        half = self.sides[0].shape[1] // 2
        ahead, behind = state
        places = (0, 1) if ahead.shape[1] == half else (None, None)
        self.ready = self.add(
            [(self.left, [(ahead, places[0])]), (-self.left, [(behind, places[1])])]
        )

    def arrive(self, values):
        self.state, values = lax.optimization_barrier((self.state, values))
        return values

    def finish(self, below):
        ahead, behind = self.state
        if not self.tiled:
            rows = self.add([(0, [(ahead, None), (behind, None)])])
            for parts in below:
                total = jnp.zeros(parts[0].shape[-2:], F32)
                for part in parts:
                    part = part.astype(F32)
                    total += part if part.ndim == 2 else jnp.sum(part, axis=0)
                rows.append(total.astype(BF16))
            return jnp.concatenate(rows, axis=0)
        (rows, model), units, chips = self.sides[0].shape, self.units, self.chips
        half = model // 2
        arrays = [ahead, behind] + [part for parts in below for part in parts]
        specs = [pl.BlockSpec((rows, half), lambda at, table: (0, at))] * 2
        specs += [pl.BlockSpec((rows, units), lambda at, table: (0, table[0]))] * 2
        for array in arrays:
            shape = array.shape[:-1] + (half,)
            specs.append(
                pl.BlockSpec(shape, lambda at, table, rank=array.ndim: (0,) * (rank - 1) + (at,))
            )
        height = units + sum(parts[0].shape[-2] for parts in below)
        return pl.pallas_call(
            functools.partial(finish_kernel, [len(parts) for parts in below]),
            grid_spec=pltpu.PrefetchScalarGridSpec(
                num_scalar_prefetch=1,
                grid=(2,),
                in_specs=specs,
                out_specs=pl.BlockSpec((height, half), lambda at, table: (0, at)),
            ),
            out_shape=struct((height, model), BF16),
            compiler_params=streaming,
            cost_estimate=light,
            name="ring_finish",
        )(self.table, *self.sides, *self.operands, *arrays)

    def add(self, wanted, split=False):
        (rows, model), units, chips = self.sides[0].shape, self.units, self.chips
        if not self.tiled:
            sums = []
            for step, parts in wanted:
                start = self.table[step % chips] * units
                total = jnp.zeros((units, model), F32)
                for operand, side in zip(self.operands, self.sides):
                    block = lax.dynamic_slice_in_dim(operand, start, units, 1)
                    total += product(block, side, 0, 0)
                for part, place in parts:
                    start = (place or 0) * part.shape[1]
                    total = total.at[:, start : start + part.shape[1]].add(part.astype(F32))
                sums.append(total.astype(BF16))
            return sums
        half = model // 2
        side = pl.BlockSpec((rows, half), lambda at, table: (0, at))
        whole = pl.BlockSpec((units, half), lambda at, table: (0, at))
        fixed = pl.BlockSpec((units, half), lambda at, table: (0, 0))
        specs, arrays = [side] * 2, list(self.sides)
        for step, parts in wanted:
            block = pl.BlockSpec(
                (rows, units), lambda at, table, step=step % chips: (0, table[step])
            )
            specs += [block] * 2 + [whole if place is None else fixed for _, place in parts]
            arrays += list(self.operands) + [part for part, _ in parts]
        places = [[place for _, place in parts] for _, parts in wanted]
        shapes, outs = [struct((units, model), BF16)] * len(wanted), [whole] * len(wanted)
        if split:
            shapes, outs = [struct((units, half), BF16)] * 2, [fixed] * 2
        return pl.pallas_call(
            functools.partial(add_kernel, places, len(shapes)),
            grid_spec=pltpu.PrefetchScalarGridSpec(
                num_scalar_prefetch=1,
                grid=(2,),
                in_specs=specs,
                out_specs=outs,
            ),
            out_shape=shapes,
            compiler_params=streaming,
            cost_estimate=light,
            name="ring_add",
        )(self.table, *arrays)

    def place(self, outputs, pairs):
        units, chips, model = self.units, self.chips, self.sides[0].shape[1]
        size, extra = self.size, self.extra
        shapes = [struct((chips * units, model), F32), struct((model, chips * units), F32)]
        if not self.tiled:
            outputs = outputs or [jnp.zeros(shape.shape, F32) for shape in shapes]
            down, up = outputs
            is_down = self.table[2 * chips] == 0
            for step, near, far in pairs:
                start = self.table[step % chips] * units
                near, far = whole_block(near)[:units], whole_block(far)[:units]
                first = jnp.where(is_down, near, far).astype(F32)
                second = jnp.where(is_down, far, near).astype(F32).T
                down = lax.dynamic_update_slice_in_dim(down, first, start, 0)
                up = lax.dynamic_update_slice_in_dim(up, second, start, 1)
            return [down, up]
        first = pairs[0][0] % chips
        stride = pairs[-1][0] % chips - first
        blocks = [pieces_of(pair[1]) + pieces_of(pair[2]) for pair in pairs]
        flat = [piece for block in blocks for piece in block]

        def place(at, table):
            return table[first + at * stride]

        def chip(at, table):
            return table[chips + first + at * stride]

        column = pl.BlockSpec(
            (model, 2 * HD), lambda at, table: (0, lax.div(chip(at, table), 2))
        )
        columns = [column] * (3 if outputs else 0)
        heads = [[first, first + stride][at] + chips for at in range(len(pairs))]
        return pl.pallas_call(
            functools.partial(place_kernel, heads, len(blocks[0]) // 2, (units, size, extra)),
            grid_spec=pltpu.PrefetchScalarGridSpec(
                num_scalar_prefetch=1,
                grid=(len(pairs),),
                in_specs=[pl.BlockSpec(memory_space=pl.ANY)] * (len(outputs) - len(columns))
                + columns
                + [pl.BlockSpec(piece.shape, lambda at, table: (0, 0)) for piece in flat],
                out_specs=[
                    pl.BlockSpec((units, model), lambda at, table: (place(at, table), 0)),
                    pl.BlockSpec((model, units), lambda at, table: (0, place(at, table))),
                    pl.BlockSpec((2, 1, extra, model), lambda at, table: (0, chip(at, table), 0, 0)),
                    pl.BlockSpec(
                        (1, 2, small_rows, model), lambda at, table: (chip(at, table), 0, 0, 0)
                    ),
                ]
                + [column] * 3,
            ),
            out_shape=shapes
            + [
                struct((2, chips, extra, model), F32),
                struct((chips, 2, small_rows, model), F32),
            ]
            + [struct((model, chips * HD), F32)] * 3,
            input_output_aliases={1 + at: at for at in range(len(outputs))},
            compiler_params=streaming,
            cost_estimate=light,
            name="place",
        )(self.table, *outputs, *flat)


def place_kernel(heads, width, sizes, table, *refs):
    count = len(heads)
    refs, (down, up, weight, small), projections = refs[:-7], refs[-7:-3], refs[-3:]
    blocks, refs = refs[-2 * width * count :], refs[: -2 * width * count]
    core = table[table.shape[0] - 2]
    units, size, extra = sizes
    rows = [pl.ds(0, units), pl.ds(units, size), pl.ds(units + size, extra)]
    rows.append(pl.ds(units + size + extra, small_rows))

    def read(block, which):
        return jnp.concatenate([piece[rows[which], :] for piece in block], axis=1)

    def put(first, second, head):
        down[...] = read(first, 0).astype(F32)
        up[...] = read(second, 0).astype(F32).T
        for side, block in ((0, first), (1, second)):
            weight[side, 0] = read(block, 2).astype(F32)
            small[0, side] = read(block, 3).astype(F32)
        both = jnp.concatenate([read(first, 1), read(second, 1)], axis=0)
        for at, output in enumerate(projections):
            part = both[at * HD : at * HD + HD].astype(F32)
            part = jnp.concatenate([part, part], axis=0).T
            if refs:
                mine = lax.broadcasted_iota(jnp.int32, part.shape, 1) // HD == head % 2
                part = jnp.where(mine, part, refs[at - 3][...])
            output[...] = part

    for at in range(count):
        near, far = (
            blocks[(2 * at + side) * width : (2 * at + side + 1) * width] for side in range(2)
        )
        head = table[heads[at]]
        here = pl.program_id(0) == at
        pl.when(here & (core == 0))(functools.partial(put, near, far, head))
        pl.when(here & (core != 0))(functools.partial(put, far, near, head))


def head_gradient_kernel(steps, chips, table, grads_ref, *refs):
    parts, out_ref = refs[:-1], refs[-1]
    for at, part in enumerate(parts):

        @pl.when(pl.program_id(0) == at)
        def _(part=part):
            chosen = [grads_ref[table[chips + step % chips]] for step in steps]
            total = product(jnp.concatenate(chosen, axis=1), part[...])
            out_ref[...] = total.astype(BF16)


def head_gradient(grads, parts, steps, table):
    chips, rows, _ = grads.shape
    columns = parts[0].shape[1]

    def column(at, table):
        mine = table[2 * chips + 1] if len(parts) > 1 else 0
        return (0, jnp.where(at == 0, mine, 1 - mine))

    return pl.pallas_call(
        functools.partial(head_gradient_kernel, steps, chips),
        grid_spec=pltpu.PrefetchScalarGridSpec(
            num_scalar_prefetch=1,
            grid=(len(parts),),
            in_specs=[
                pl.BlockSpec(array.shape, lambda at, table, rank=array.ndim: (0,) * rank)
                for array in (grads, *parts)
            ],
            out_specs=pl.BlockSpec((rows, columns), column),
        ),
        out_shape=struct((rows, columns * len(parts)), BF16),
        compiler_params=streaming,
        cost_estimate=light,
        name="head_gradient",
    )(table, grads, *parts)


def core_half(values, axis, side):
    size = values.shape[axis] // 2
    return lax.dynamic_slice_in_dim(values, side * size, size, axis)


def share_halves(values, axis):
    core = lax.axis_index("core")
    return core_half(values, axis, core), swap_cores(core_half(values, axis, 1 - core))


def local(
    block_input,
    out_grad,
    segments,
    lead_steps,
    gain_attn,
    shift_attn,
    lead_weight,
    query_weight,
    key_weight,
    value_weight,
    output_weight,
    output_bias,
    gain_mlp,
    shift_mlp,
    up_weight,
    up_bias,
    down_weight,
    down_bias,
):
    rows, model = block_input.shape
    heads = query_weight.shape[1] // HD
    width = heads * HD
    chips, core = lax.axis_size("chip"), lax.axis_index("core")
    split = chips // heads
    crops = lead_steps.shape[0]
    table = ring_table()
    weights = (query_weight, key_weight, value_weight)
    cut = model // 2 if lax.axis_size("head") == 2 else model
    payload, attn_in, attn_in_cut = project(
        table, cut, block_input, segments, lead_steps, gain_attn, shift_attn, lead_weight, weights
    )
    if split == 1:
        own = to_heads(payload)
        queries = own
    else:
        queries = scatter_queries(payload.reshape(-1, rows), heads, split)
        own = to_heads(jnp.repeat(payload, split, axis=0))
    own, attn_in_cut = lax.optimization_barrier((own, attn_in_cut))
    inputs = Gather(attn_in_cut)
    inputs.send(inputs.ready)
    other = swap_cores(own)
    raw, out, logsum = attention_forward(queries, own, other, crops)
    inputs.state, out = lax.optimization_barrier((inputs.state, out))
    attn_out = gather_queries(out, heads, split, rows)
    attn_out = visit([inputs], attn_out)
    branches = across_heads(product(attn_out, output_weight, 0, 0).astype(BF16))
    wide = block_input.astype(F32)
    mean_attn = jnp.mean(wide, axis=-1, keepdims=True)
    centred = wide - mean_attn
    inverse_attn = lax.rsqrt(jnp.mean(centred * centred, axis=-1, keepdims=True) + eps)
    mean_attn, inverse_attn = visit([inputs], (mean_attn, inverse_attn))
    keep, give, keep_in, give_in, hidden, dup_bias, mlp_part, d_mlp_part = mlp(
        table,
        block_input,
        out_grad,
        branches,
        output_bias,
        gain_mlp,
        shift_mlp,
        up_weight,
        up_bias,
        down_weight,
    )
    keep, give, keep_in, give_in, d_mlp_part = visit(
        [inputs], (keep, give, keep_in, give_in, d_mlp_part)
    )
    d_mlp = across_heads(d_mlp_part)
    ring = Reduce(keep, swap_cores(give), keep_in, swap_cores(give_in), table)
    mlp_part, d_mlp = lax.optimization_barrier((mlp_part, d_mlp))
    d_hidden, d_branch, d_attn, sums = middle(hidden, out_grad, d_mlp, gain_mlp, output_weight)
    grads = scatter_queries(d_attn, heads, split)
    d_branch, mlp_part = visit([ring, inputs], (d_branch, mlp_part))
    while inputs.busy():
        visit([inputs], ())
    mlp_out = across_heads(mlp_part)
    out_near, out_far = share_halves(attn_out, 0)
    doutput = product(out_near, d_branch) + product(out_far, swap_cores(d_branch))
    doutput = doutput.astype(BF16).reshape(chips, -1, model)
    steps, inputs = zip(*inputs.blocks)
    inputs = join(inputs)
    parts = across_heads(inputs) if cut != model else [inputs]
    grads, doutput = visit([ring], (grads, doutput))
    doutput = to_heads(doutput)
    dquery, far_sums = attention_backward(queries, grads, raw, logsum, other, [], crops)
    far_sums = swap_cores(far_sums)
    grads, dquery = visit([ring], (grads, dquery))
    head_grads = attention_backward(
        queries, grads, raw, logsum, own, [dquery, far_sums], crops
    )
    head_grads = ring.arrive(head_grads)
    doutput, head_grads = lax.optimization_barrier((doutput, head_grads))
    small = jnp.concatenate([sums.reshape(-1), dup_bias[0]])
    small = jnp.pad(small, (0, small_rows * model - small.shape[0])).reshape(small_rows, model)
    below = [[doutput], [small]]
    if split == 1:
        (head_grads,) = head_grads
        moved = to_heads(head_grads)
        projections = head_gradient(head_grads, parts, steps, table)
        near, far = share_halves(projections, 0)
        size, below = near.shape[0], [[near, far]] + below
        dquery, dkey, dvalue = (
            moved[:, at * HD : at * HD + HD].reshape(width, rows) for at in range(3)
        )
    else:
        dquery, key_value = head_grads
        dquery = gather_queries(dquery, heads, split, rows)
        moved = to_heads(key_value).reshape(heads, split, 2 * HD, rows).astype(F32)
        moved = jnp.sum(moved, axis=1).astype(BF16)
        dkey, dvalue = (moved[:, at * HD : at * HD + HD].reshape(width, rows) for at in range(2))
        size = 0
        projections = [
            lax.psum(product(attn_in, grad, 0, 1).astype(BF16), ("chip", "core")).astype(F32)
            for grad in (dquery, dkey, dvalue)
        ]
    start, ring.size, ring.extra = ring.units, size, doutput.shape[1]
    gathered = Gather(ring.finish(below), True, ring.place)
    gathered.send(gathered.ready)
    d_part = (
        product(dquery, query_weight, 0, 1)
        + product(dkey, key_weight, 0, 1)
        + product(dvalue, value_weight, 0, 1)
    )
    d_in = across_heads(d_part.astype(BF16))
    unit_attn = (block_input.astype(F32) - mean_attn) * inverse_attn
    onehot = (segments[:, None] == jnp.arange(crops, dtype=jnp.int32)[None, :]).astype(F32)
    lead = jnp.sum(onehot * lead_steps.astype(F32)[None, :], axis=1) / 12.0
    ends = jnp.stack(
        [
            jnp.sum(d_part * unit_attn, axis=0),
            jnp.sum(d_part, axis=0),
            jnp.sum(lead[:, None] * d_part, axis=0),
        ]
    )
    ends = ends.reshape(-1, 128)
    ends = functools.reduce(jnp.add, across_heads(ends))
    ends = ends + swap_cores(ends)
    moves = [chips >> (at + 1) for at in range(chips.bit_length() - 1)][::-1]

    def step_ends(ends):
        if not moves:
            return [ends]
        reach = moves.pop(0)
        pairs = [(chip, chip ^ reach) for chip in range(chips)]
        return [ends, lax.ppermute(ends, "chip", pairs)]

    ends = step_ends(visit([gathered], ends))
    ends, mlp_out = visit([gathered], (ends, mlp_out))
    ends = step_ends(functools.reduce(jnp.add, ends))
    block_output = hidden + down_bias
    for part in mlp_out:
        block_output += part.astype(F32)
    block_output = block_output.astype(BF16)
    d_in, block_output, ends = visit([gathered], (d_in, block_output, ends))
    ends = step_ends(functools.reduce(jnp.add, ends))
    d_in = functools.reduce(jnp.add, (part.astype(F32) for part in d_in))
    input_grad = (d_hidden + normalize_back(d_in * gain_attn, unit_attn, inverse_attn)).astype(
        BF16
    )
    while gathered.busy() or moves:
        input_grad, ends = visit([gathered], (input_grad, ends))
        ends = step_ends(functools.reduce(jnp.add, ends))
    ends = functools.reduce(jnp.add, ends).reshape(3, model)
    ddown_weight, dup_weight, *rest = gathered.outputs
    if split == 1:
        doutput_weight, small, *projections = rest
        doutput_weight = doutput_weight.reshape(width, model)
    if split != 1:
        blocks = jnp.zeros((2, chips, ring.extra + small_rows, model), F32)
        for step, near, far in gathered.pairs:
            for side, block in ((core, near), (1 - core, far)):
                at = (side, table[chips + step % chips], 0, 0)
                block = whole_block(block)[None, None, start:].astype(F32)
                blocks = lax.dynamic_update_slice(blocks, block, at)
        doutput_weight = blocks[:, :, :-small_rows].reshape(width, model)
        small = blocks[:, :, -small_rows:]
    small = jnp.sum(small, axis=(0, 1))
    dup_bias = small[4:].reshape(-1)[: dup_bias.shape[1]]
    return (
        block_output,
        input_grad,
        ends[0],
        ends[1],
        ends[2],
        *projections,
        doutput_weight,
        *small[:3],
        dup_weight,
        dup_bias,
        ddown_weight,
        small[3],
    )


def solution(mesh):
    bands, halves = mesh.shape["band"], mesh.shape["head"]
    inner = Mesh(mesh.devices.reshape(bands // 2, 2, halves), ("chip", "core", "head"))
    band = ("chip", "core")
    rows, columns, split_rows = P(band, None), P(None, "head"), P("head", None)
    return jax.shard_map(
        local,
        mesh=inner,
        in_specs=(
            rows,
            rows,
            P(band),
            P(),
            P(),
            P(),
            P(),
            columns,
            columns,
            columns,
            split_rows,
            P(),
            P(),
            P(),
            columns,
            P("head"),
            split_rows,
            P(),
        ),
        out_specs=(
            rows,
            rows,
            P(),
            P(),
            P(),
            columns,
            columns,
            columns,
            split_rows,
            P(),
            P(),
            P(),
            columns,
            P("head"),
            split_rows,
            P(),
        ),
        check_vma=False,
    )
```

```python
import functools
import math

import jax
import jax.numpy as jnp
from jax import lax
from jax.experimental import pallas as pl
from jax.experimental.pallas import tpu as pltpu
from jax.sharding import Mesh, PartitionSpec as P

HD = 64
F32 = jnp.float32
BF16 = jnp.bfloat16
eps = 1e-05
masked_value = -1e30
seg_row = 3 * HD
payload_rows = 3 * HD + 16
small_rows = 16
params = pltpu.CompilerParams(vmem_limit_bytes=48 * 2**20)
streaming = pltpu.CompilerParams(vmem_limit_bytes=63_400_000)


def normalize(values):
    centred = values - jnp.mean(values, axis=-1, keepdims=True)
    inverse = lax.rsqrt(jnp.mean(centred * centred, axis=-1, keepdims=True) + eps)
    return (centred * inverse, inverse)


def normalize_back(grad_unit, unit, inverse):
    return inverse * (
        grad_unit
        - jnp.mean(grad_unit, axis=-1, keepdims=True)
        - unit * jnp.mean(grad_unit * unit, axis=-1, keepdims=True)
    )


def product(first, second, first_axis=1, second_axis=0):
    return lax.dot_general(
        first,
        second,
        (((first_axis,), (second_axis,)), ((), ())),
        preferred_element_type=jnp.float32,
    )


def struct(shape, dtype):
    return jax.ShapeDtypeStruct(shape, dtype)


def whole_spec(shape):
    return pl.BlockSpec(shape, lambda *at: (0,) * len(shape))


light = pl.CostEstimate(flops=1, bytes_accessed=1, transcendentals=0)


def project_kernel(
    table, input_ref, segment_ref, steps_ref, gain, shift, lead_weight, *refs
):
    weights, (payload_ref, attn_in_ref, cut_ref) = refs[:3], refs[3:]
    rows = input_ref.shape[0]

    @pl.when(pl.program_id(0) == 0)
    def _():
        unit, _ = normalize(input_ref[...].astype(F32))
        crops = steps_ref.shape[0]
        crop = lax.broadcasted_iota(jnp.int32, (crops, rows), 0)
        steps = jnp.zeros((crops, rows), jnp.int32)
        for at in range(crops):
            steps = jnp.where(crop == at, steps_ref[at], steps)
        steps = jnp.where(crop == segment_ref[...], steps, 0).astype(F32)
        lead = product(steps, jnp.ones((crops, 128), F32), 0, 0)[:, :1] / 12.0
        attn_in = unit * gain[...] + shift[...] + lead * lead_weight[...]
        attn_in = attn_in.astype(BF16)
        attn_in_ref[...] = attn_in
        columns = cut_ref.shape[1]
        first = table[table.shape[0] - 1] % (attn_in.shape[1] // columns) == 0
        cut_ref[...] = jnp.where(first, attn_in[:, :columns], attn_in[:, -columns:])

    for at, weight in enumerate(weights):
        part = product(attn_in_ref[...], weight[...]).T.astype(BF16)
        for head in range(2):
            payload_ref[head, pl.ds(at * HD, HD), :] = part[head * HD : head * HD + HD]
    segment = jnp.broadcast_to(segment_ref[...].astype(F32), (16, rows)).astype(BF16)
    for head in range(2):
        payload_ref[head, pl.ds(seg_row, 16), :] = segment


def project(table, cut, block_input, segments, lead_steps, gain, shift, lead_weight, weights):
    rows, model = block_input.shape
    heads = weights[0].shape[1] // HD
    line = whole_spec((1, model))
    column = pl.BlockSpec((model, 2 * HD), lambda at, table: (0, at))
    return pl.pallas_call(
        project_kernel,
        grid_spec=pltpu.PrefetchScalarGridSpec(
            num_scalar_prefetch=1,
            grid=(heads // 2,),
            in_specs=[
                whole_spec(block_input.shape),
                whole_spec((1, rows)),
                pl.BlockSpec(memory_space=pltpu.SMEM),
            ]
            + [line] * 3
            + [column] * 3,
            out_specs=[
                pl.BlockSpec((2, payload_rows, rows), lambda at, table: (at, 0, 0)),
                whole_spec((rows, model)),
                whole_spec((rows, cut)),
            ],
        ),
        out_shape=[
            struct((heads, payload_rows, rows), BF16),
            struct((rows, model), BF16),
            struct((rows, cut), BF16),
        ],
        compiler_params=streaming,
        cost_estimate=light,
        name="project",
    )(table, block_input, segments[None], lead_steps, gain[None], shift[None], lead_weight[None], *weights)


def mlp_kernel(count, core_ref, input_ref, grad_ref, *refs):
    branches, refs = refs[:count], refs[count:]
    output_bias, gain, shift, up_weight, up_bias, down_weight = refs[:6]
    keep_ref, give_ref, keep_in_ref, give_in_ref, hidden_ref, bias_ref, forward_ref, back_ref = refs[
        6:14
    ]
    mlp_in_ref, forward, back = refs[14:]
    at = pl.program_id(0)
    is_down = core_ref[core_ref.shape[0] - 2] == 0

    @pl.when(at == 0)
    def _():
        hidden = input_ref[...].astype(F32) + output_bias[...]
        for branch in branches:
            hidden += branch[...].astype(F32)
        hidden_ref[...] = hidden
        unit, _ = normalize(hidden)
        mlp_in = (unit * gain[...] + shift[...]).astype(BF16)
        mlp_in_ref[...] = mlp_in
        keep_in_ref[...] = jnp.where(is_down, grad_ref[...], mlp_in)
        give_in_ref[...] = jnp.where(is_down, mlp_in, grad_ref[...])
        forward[...] = jnp.zeros_like(forward)
        back[...] = jnp.zeros_like(back)

    upper = product(mlp_in_ref[...], up_weight[...]) + up_bias[...]
    share = 0.5 + 0.5 * lax.erf(upper * math.sqrt(0.5))
    slope = share + upper * (jnp.exp(upper * upper * -0.5) * (1.0 / math.sqrt(2.0 * math.pi)))
    active = (upper * share).astype(BF16)
    d_active = product(grad_ref[...], down_weight[...], 1, 1)
    d_upper = (d_active * slope).astype(BF16)
    keep_ref[...] = jnp.where(is_down, active, d_upper)
    give_ref[...] = jnp.where(is_down, d_upper, active)
    bias_ref[...] = jnp.sum(d_upper.astype(F32), axis=0, keepdims=True)
    forward[...] += product(active, down_weight[...])
    back[...] += product(d_upper, up_weight[...], 1, 1)

    @pl.when(at == pl.num_programs(0) - 1)
    def _():
        forward_ref[...] = forward[...].astype(BF16)
        back_ref[...] = back[...].astype(BF16)


def mlp(
    table, block_input, out_grad, branches, output_bias, gain, shift, up_weight, up_bias, down_weight
):
    rows, model = block_input.shape
    units = up_weight.shape[1]
    step = math.gcd(units, 512)
    tile, line = whole_spec((rows, model)), whole_spec((1, model))
    wide = pl.BlockSpec((rows, step), lambda at, table: (0, at))
    bias = pl.BlockSpec((1, step), lambda at, table: (0, at))
    return pl.pallas_call(
        functools.partial(mlp_kernel, len(branches)),
        grid_spec=pltpu.PrefetchScalarGridSpec(
            num_scalar_prefetch=1,
            grid=(units // step,),
            in_specs=[tile] * (2 + len(branches))
            + [line] * 3
            + [
                pl.BlockSpec((model, step), lambda at, table: (0, at)),
                bias,
                pl.BlockSpec((step, model), lambda at, table: (at, 0)),
            ],
            out_specs=[wide, wide, tile, tile, tile, bias, tile, tile],
            scratch_shapes=[pltpu.VMEM((rows, model), BF16)]
            + [pltpu.VMEM((rows, model), F32)] * 2,
        ),
        out_shape=[struct((rows, units), BF16)] * 2
        + [struct((rows, model), BF16)] * 2
        + [
            struct((rows, model), F32),
            struct((1, units), F32),
            struct((rows, model), BF16),
            struct((rows, model), BF16),
        ],
        compiler_params=streaming,
        cost_estimate=light,
        name="mlp",
    )(
        table,
        block_input,
        out_grad,
        *branches,
        output_bias[None],
        gain[None],
        shift[None],
        up_weight,
        up_bias[None],
        down_weight,
    )


def middle_kernel(count, hidden_ref, grad_ref, *refs):
    parts, refs = refs[:count], refs[count:]
    gain, output_weight, d_hidden_ref, d_branch_ref, d_attn_ref, sums_ref = refs
    unit, inverse = normalize(hidden_ref[...])
    d_mlp = parts[0][...].astype(F32)
    for part in parts[1:]:
        d_mlp += part[...].astype(F32)
    grad = grad_ref[...].astype(F32)
    d_hidden = grad + normalize_back(d_mlp * gain[...], unit, inverse)
    d_hidden_ref[...] = d_hidden
    d_branch = d_hidden.astype(BF16)
    d_branch_ref[...] = d_branch
    d_attn_ref[...] = product(output_weight[...], d_branch, 1, 1).astype(BF16)
    for at, values in enumerate((d_hidden, d_mlp * unit, d_mlp, grad)):
        sums_ref[pl.ds(at, 1), :] = jnp.sum(values, axis=0, keepdims=True)


def middle(hidden, out_grad, parts, gain, output_weight):
    rows, model = hidden.shape
    width = output_weight.shape[0]
    return pl.pallas_call(
        functools.partial(middle_kernel, len(parts)),
        out_shape=[
            struct((rows, model), F32),
            struct((rows, model), BF16),
            struct((width, rows), BF16),
            struct((4, model), F32),
        ],
        compiler_params=streaming,
        cost_estimate=light,
        name="middle",
    )(hidden, out_grad, *parts, gain[None], output_weight)


def mask_rows(piece, chip, crops):
    crop = lax.broadcasted_iota(jnp.int32, (HD, piece.shape[2]), 0)
    segment = piece[chip, pl.ds(seg_row, 16), :].astype(F32)[:1].astype(jnp.int32)
    return jnp.where((crop != segment) & (crop < crops), masked_value, 0.0)


def load_keys(piece, crops, keys, key_t, value_n):
    chips, _, patches = piece.shape
    for chip in range(chips):
        key = piece[chip, pl.ds(HD, HD), :]
        value = piece[chip, pl.ds(2 * HD, HD), :]
        place = pl.ds(chip * patches, patches)
        both = jnp.concatenate([key.astype(F32), mask_rows(piece, chip, crops)], axis=0)
        keys[place, :] = both.T.astype(BF16)
        key_t[:, place] = key
        value_n[place, :] = value.astype(F32).T.astype(BF16)


def masked_query(query_ref, dtype=BF16):
    query = query_ref[0, pl.ds(0, HD), :].astype(F32) * 0.125
    segment = query_ref[0, pl.ds(seg_row, 16), :].astype(F32)[:1].astype(jnp.int32)
    crop = lax.broadcasted_iota(jnp.int32, query.shape, 0)
    onehot = jnp.where(crop == segment, 1.0, 0.0)
    return jnp.concatenate([query, onehot], axis=0).astype(dtype)


def forward_kernel(
    crops, step, query_ref, own, other, raw_ref, out_ref, logsum_ref, key_t, value_n, scores
):
    @pl.when(pl.program_id(0) == 0)
    def _():
        start = 0
        for piece in (own, other):
            chips, _, patches = piece.shape
            for chip in range(chips):
                place = pl.ds(start, patches)
                key = piece[chip, pl.ds(HD, HD), :].astype(F32)
                key_t[:, place] = jnp.concatenate([key, mask_rows(piece, chip, crops)], axis=0).astype(BF16)
                value = piece[chip, pl.ds(2 * HD, HD), :].astype(F32)
                value = jnp.concatenate([value, jnp.ones_like(value)], axis=0)
                value_n[place, :] = value.T.astype(BF16)
                start += patches

    query = masked_query(query_ref, F32).T.astype(BF16)
    count = query.shape[0]
    top = jnp.full((count, 128), masked_value, F32)
    for start in range(0, key_t.shape[1], step):
        block = product(query, key_t[:, pl.ds(start, step)])
        scores[:, pl.ds(start, step)] = block
        for at in range(0, step, 128):
            top = jnp.maximum(top, block[:, at : at + 128])
    top = jnp.max(top, axis=1, keepdims=True)
    accum = jnp.zeros((count, 2 * HD), F32)
    for start in range(0, key_t.shape[1], step):
        weights = jnp.exp(scores[:, pl.ds(start, step)] - top).astype(BF16)
        accum += product(weights, value_n[pl.ds(start, step), :])
    accum = accum.T
    total = accum[HD : HD + 1]
    raw = accum[:HD] / total
    raw_ref[0] = raw
    out_ref[0] = raw.astype(BF16)
    top = jnp.broadcast_to(top, (count, 128)).T[:1]
    logsum_ref[0] = top + jnp.log(total)


def backward_kernel(
    crops,
    extra,
    query_ref,
    grad_ref,
    raw_ref,
    logsum_ref,
    piece,
    *refs,
):
    extras, refs = refs[:extra], refs[extra:]
    outputs, (keys, key_t, value_n, sums) = refs[:-4], refs[-4:]
    group = pl.program_id(0)

    @pl.when(group == 0)
    def _():
        load_keys(piece, crops, keys, key_t, value_n)
        sums[...] = jnp.zeros_like(sums)

    query = masked_query(query_ref)
    grad = grad_ref[0]
    grad_wide = grad.astype(F32)
    delta = jnp.sum(grad_wide * raw_ref[0], axis=0, keepdims=True)
    scaled = query_ref[0, pl.ds(0, HD), :].astype(F32) * 0.125
    zero = jnp.zeros_like(scaled)
    query_side = jnp.concatenate([scaled, zero], axis=0).T.astype(BF16)
    grad_side = jnp.concatenate([zero, grad_wide], axis=0).T.astype(BF16)
    probs = jnp.exp(product(keys[...], query) - logsum_ref[0])
    dprobs = product(value_n[...], grad)
    dscores = (probs * (dprobs - delta)).astype(BF16)
    sums[...] += product(dscores, query_side) + product(probs.astype(BF16), grad_side)
    dquery = product(key_t[...], dscores) * 0.125
    if extras:
        dquery += extras[0][0]
    if len(outputs) == 1:
        outputs[0][group, pl.ds(0, HD), :] = dquery.astype(BF16)
    else:
        outputs[0][0] = dquery.astype(outputs[0].dtype)

    @pl.when(group == pl.num_programs(0) - 1)
    def _():
        chips, _, patches = piece.shape
        for chip in range(chips):
            total = sums[pl.ds(chip * patches, patches), :].T
            if extra > 1:
                total += extras[1][chip].astype(F32)
            total = total.astype(BF16)
            if len(outputs) == 1:
                outputs[0][chip, pl.ds(HD, 2 * HD), :] = total
            else:
                outputs[1][chip] = total


def key_step(count):
    return 1024 if count % 1024 == 0 else 256


def query_spec(rows, patches):
    return pl.BlockSpec((1, rows, patches), lambda group: (group, 0, 0))


def attention_forward(queries, own, other, crops):
    groups, _, patches = queries.shape
    count = 2 * own.shape[0] * own.shape[2]
    return pl.pallas_call(
        functools.partial(forward_kernel, crops, key_step(count)),
        grid=(groups,),
        in_specs=[
            query_spec(payload_rows, patches),
            whole_spec(own.shape),
            whole_spec(other.shape),
        ],
        out_specs=[query_spec(HD, patches), query_spec(HD, patches), query_spec(1, patches)],
        out_shape=[
            struct((groups, HD, patches), F32),
            struct((groups, HD, patches), BF16),
            struct((groups, 1, patches), F32),
        ],
        scratch_shapes=[
            pltpu.VMEM((2 * HD, count), BF16),
            pltpu.VMEM((count, 2 * HD), BF16),
            pltpu.VMEM((patches, count), F32),
        ],
        compiler_params=streaming,
        cost_estimate=light,
        name="attention_forward",
    )(queries, own, other)


def attention_backward(queries, grads, raw, logsum, keys, extras, crops):
    groups, _, patches = queries.shape
    chips, count = keys.shape[0], keys.shape[0] * keys.shape[2]
    sums_shape = (chips, 2 * HD, keys.shape[2])
    specs = [query_spec(HD, patches), whole_spec(sums_shape)]
    shapes = [
        struct((groups, HD, patches), BF16 if extras else F32),
        struct(sums_shape, BF16),
    ]
    outs = specs
    if extras and (groups, patches) == (chips, keys.shape[2]):
        shapes = [struct((chips, 3 * HD, patches), BF16)]
        outs = [whole_spec(shapes[0].shape)]
    return pl.pallas_call(
        functools.partial(backward_kernel, crops, len(extras)),
        grid=(groups,),
        in_specs=[
            query_spec(payload_rows, patches),
            query_spec(HD, patches),
            query_spec(HD, patches),
            query_spec(1, patches),
            whole_spec(keys.shape),
        ]
        + specs[: len(extras)],
        out_specs=outs,
        out_shape=shapes,
        scratch_shapes=[
            pltpu.VMEM((count, 2 * HD), BF16),
            pltpu.VMEM((HD, count), BF16),
            pltpu.VMEM((count, HD), BF16),
            pltpu.VMEM((count, 2 * HD), F32),
        ],
        compiler_params=params,
        cost_estimate=light,
        name="attention_backward",
    )(queries, grads, raw, logsum, keys, *extras)


def swap_cores(values):
    return lax.ppermute(values, "core", [(0, 1), (1, 0)])


def to_heads(blocks):
    return lax.all_to_all(blocks, "chip", 0, 0, tiled=True)


def scatter_queries(values, heads, split):
    rows, patches = values.shape[0] // heads, values.shape[1]
    if split == 1:
        return to_heads(values.reshape(heads, rows, patches))
    part = patches // split
    blocks = values.reshape(heads, rows, split, part).transpose(0, 2, 1, 3)
    moved = to_heads(blocks.reshape(heads * split, rows, part))
    width = min(256, moved.shape[0] * part)
    joined = moved.transpose(1, 0, 2).reshape(rows, -1, width)
    return joined.transpose(1, 0, 2)


def gather_queries(values, heads, split, patches):
    rows = values.shape[1]
    if split == 1:
        return to_heads(values).reshape(heads * rows, patches)
    part = patches // split
    joined = values.transpose(1, 0, 2).reshape(rows, heads * split, part)
    moved = to_heads(joined.transpose(1, 0, 2)).reshape(heads, split, rows, part)
    return moved.transpose(0, 2, 1, 3).reshape(heads * rows, patches)


def across_heads(part):
    if lax.axis_size("head") == 2:
        return [part, lax.ppermute(part, "head", [(0, 1), (1, 0)])]
    return [lax.psum(part, "head")]


def ring_pairs(direction):
    chips = lax.axis_size("chip")
    order = list(range(0, chips, 2)) + list(range(chips - 1, 0, -2))
    return [(order[at], order[(at + direction) % chips]) for at in range(chips)]


def ring_table():
    chips, chip = lax.axis_size("chip"), lax.axis_index("chip")
    place = jnp.where(chip % 2 == 0, chip // 2, chips - 1 - chip // 2)
    steps = jnp.arange(2 * chips + 2, dtype=jnp.int32)
    places = (place + steps) % chips
    there = jnp.where(places < chips // 2, 2 * places, 2 * (chips - 1 - places) + 1)
    table = jnp.where(steps < chips, places, there)
    table = jnp.where(steps == 2 * chips, lax.axis_index("core"), table)
    return jnp.where(steps == 2 * chips + 1, lax.axis_index("head"), table).astype(jnp.int32)


def visit(streams, values):
    states, values = lax.optimization_barrier(([stream.state for stream in streams], values))
    for stream, state in zip(streams, states):
        stream.advance(state)
    ready, values = lax.optimization_barrier(([stream.ready for stream in streams], values))
    for stream, blocks in zip(streams, ready):
        stream.send(blocks)
    return values


def pieces_of(block):
    return list(block) if isinstance(block, tuple) else [block]


def whole_block(block):
    return jnp.concatenate(pieces_of(block), axis=1)


def join_kernel(counts, *refs):
    output, refs, start = refs[-1], list(refs[:-1]), 0
    for count in counts:
        column = 0
        for _ in range(count):
            piece = refs.pop(0)
            rows, columns = piece.shape
            output[pl.ds(start, rows), pl.ds(column, columns)] = piece[...]
            column += columns
        start += rows


def join(blocks):
    blocks = [pieces_of(block) for block in blocks]
    rows = sum(block[0].shape[0] for block in blocks)
    columns = sum(piece.shape[1] for piece in blocks[0])
    return pl.pallas_call(
        functools.partial(join_kernel, [len(block) for block in blocks]),
        out_shape=struct((rows, columns), blocks[0][0].dtype),
        compiler_params=streaming,
        name="join",
    )(*[piece for block in blocks for piece in block])


def halves_kernel(left, right, left_ref, right_ref):
    left_ref[...] = left[...]
    right_ref[...] = right[...]


def halves(left, right):
    rows, columns = left.shape
    if rows % 16 or columns % 256:
        return [left[:, : columns // 2], right[:, columns // 2 :]]
    out = pl.BlockSpec((rows, columns // 2), lambda at: (0, 0))
    return pl.pallas_call(
        halves_kernel,
        grid=(1,),
        in_specs=[out, pl.BlockSpec((rows, columns // 2), lambda at: (0, 1))],
        out_specs=[out, out],
        out_shape=[struct((rows, columns // 2), left.dtype)] * 2,
        compiler_params=streaming,
        name="halves",
    )(left, right)


class Gather:
    def __init__(self, block, swap=False, take=None):
        self.reach, self.swap, self.take = lax.axis_size("chip") // 2, swap, take
        self.blocks, self.pairs, self.count = [], [], 0
        self.new, self.outputs = [0], []
        self.ready = [block]

    def send(self, ready):
        if len(self.new) < len(ready):
            ready = [tuple(ready)]
        new = list(zip(self.new, ready))
        self.blocks += new
        self.new = new
        self.count += 1
        sides = ready if len(ready) > 1 else ready * 2
        if self.count == self.reach:
            sides = halves(*sides)
        flying = []
        if self.count <= self.reach:
            flying = [
                lax.ppermute(block, "chip", ring_pairs(direction))
                for block, direction in zip(sides, (1, -1))
            ]
        if self.swap and ready:
            pairs = [(step, block, jax.tree.map(swap_cores, block)) for step, block in new]
            self.pairs += pairs
            self.outputs = self.take(self.outputs, pairs)
        self.state = (flying, self.outputs)

    def advance(self, state):
        arrived, self.outputs = state
        self.new = [-self.count, self.count]
        if self.count == self.reach:
            self.new = [self.count]
        self.ready = arrived

    def busy(self):
        return bool(self.state[0])


def add_kernel(wanted, count, _, *refs):
    outputs, refs = refs[-count:], list(refs[:-count])
    keep_in, far_in = refs.pop(0), refs.pop(0)
    at = pl.program_id(0)

    def put(output, total):
        output[...] = total.astype(BF16)

    for places, output in zip(wanted, outputs):
        near, far = refs.pop(0), refs.pop(0)
        total = product(near[...], keep_in[...], 0, 0) + product(far[...], far_in[...], 0, 0)
        arrived = [(place, refs.pop(0)) for place in places]
        if count > len(wanted):
            for place in range(count):
                pl.when(at == place)(functools.partial(put, outputs[place], total))
            return
        for place, part in arrived:
            if place is None:
                total += part[...].astype(F32)
        put(output, total)
        for place, part in arrived:
            if place is not None:
                pl.when(at == place)(lambda: put(output, total + part[...].astype(F32)))


def finish_kernel(counts, _, keep_in, far_in, near, far, ahead, behind, *refs):
    refs, output = list(refs[:-1]), refs[-1]
    total = product(near[...], keep_in[...], 0, 0) + product(far[...], far_in[...], 0, 0)
    total += ahead[...].astype(F32) + behind[...].astype(F32)
    start = total.shape[0]
    output[pl.ds(0, start), :] = total.astype(BF16)
    for count in counts:
        total = 0.0
        for _ in range(count):
            part = refs.pop(0)[...].astype(F32)
            total += part if part.ndim == 2 else jnp.sum(part, axis=0)
        output[pl.ds(start, total.shape[0]), :] = total.astype(BF16)
        start += total.shape[0]


class Reduce:
    def __init__(self, keep, far, keep_in, far_in, table):
        self.chips, self.table = lax.axis_size("chip"), table
        self.operands, self.sides = (keep, far), (keep_in, far_in)
        self.units = keep.shape[1] // self.chips
        self.tiled = self.units % 128 == 0
        self.left, self.rest = self.chips // 2, None
        blocks = self.add([(self.left, [])], True)
        self.send(blocks if len(blocks) > 1 else halves(blocks[0], blocks[0]))

    def send(self, ready):
        self.left -= 1
        self.state = [
            lax.ppermute(block, "chip", ring_pairs(direction))
            for block, direction in zip(ready, (1, -1))
        ]

    def advance(self, state):
        half = self.sides[0].shape[1] // 2
        ahead, behind = state
        places = (0, 1) if ahead.shape[1] == half else (None, None)
        self.ready = self.add(
            [(self.left, [(ahead, places[0])]), (-self.left, [(behind, places[1])])]
        )

    def arrive(self, values):
        self.state, values = lax.optimization_barrier((self.state, values))
        return values

    def finish(self, below):
        ahead, behind = self.state
        if not self.tiled:
            rows = self.add([(0, [(ahead, None), (behind, None)])])
            for parts in below:
                total = jnp.zeros(parts[0].shape[-2:], F32)
                for part in parts:
                    part = part.astype(F32)
                    total += part if part.ndim == 2 else jnp.sum(part, axis=0)
                rows.append(total.astype(BF16))
            return jnp.concatenate(rows, axis=0)
        (rows, model), units, chips = self.sides[0].shape, self.units, self.chips
        half = model // 2
        arrays = [ahead, behind] + [part for parts in below for part in parts]
        specs = [pl.BlockSpec((rows, half), lambda at, table: (0, at))] * 2
        specs += [pl.BlockSpec((rows, units), lambda at, table: (0, table[0]))] * 2
        for array in arrays:
            shape = array.shape[:-1] + (half,)
            specs.append(
                pl.BlockSpec(shape, lambda at, table, rank=array.ndim: (0,) * (rank - 1) + (at,))
            )
        height = units + sum(parts[0].shape[-2] for parts in below)
        return pl.pallas_call(
            functools.partial(finish_kernel, [len(parts) for parts in below]),
            grid_spec=pltpu.PrefetchScalarGridSpec(
                num_scalar_prefetch=1,
                grid=(2,),
                in_specs=specs,
                out_specs=pl.BlockSpec((height, half), lambda at, table: (0, at)),
            ),
            out_shape=struct((height, model), BF16),
            compiler_params=streaming,
            cost_estimate=light,
            name="ring_finish",
        )(self.table, *self.sides, *self.operands, *arrays)

    def add(self, wanted, split=False):
        (rows, model), units, chips = self.sides[0].shape, self.units, self.chips
        if not self.tiled:
            sums = []
            for step, parts in wanted:
                start = self.table[step % chips] * units
                total = jnp.zeros((units, model), F32)
                for operand, side in zip(self.operands, self.sides):
                    block = lax.dynamic_slice_in_dim(operand, start, units, 1)
                    total += product(block, side, 0, 0)
                for part, place in parts:
                    start = (place or 0) * part.shape[1]
                    total = total.at[:, start : start + part.shape[1]].add(part.astype(F32))
                sums.append(total.astype(BF16))
            return sums
        half = model // 2
        side = pl.BlockSpec((rows, half), lambda at, table: (0, at))
        whole = pl.BlockSpec((units, half), lambda at, table: (0, at))
        fixed = pl.BlockSpec((units, half), lambda at, table: (0, 0))
        specs, arrays = [side] * 2, list(self.sides)
        for step, parts in wanted:
            block = pl.BlockSpec(
                (rows, units), lambda at, table, step=step % chips: (0, table[step])
            )
            specs += [block] * 2 + [whole if place is None else fixed for _, place in parts]
            arrays += list(self.operands) + [part for part, _ in parts]
        places = [[place for _, place in parts] for _, parts in wanted]
        shapes, outs = [struct((units, model), BF16)] * len(wanted), [whole] * len(wanted)
        if split:
            shapes, outs = [struct((units, half), BF16)] * 2, [fixed] * 2
        return pl.pallas_call(
            functools.partial(add_kernel, places, len(shapes)),
            grid_spec=pltpu.PrefetchScalarGridSpec(
                num_scalar_prefetch=1,
                grid=(2,),
                in_specs=specs,
                out_specs=outs,
            ),
            out_shape=shapes,
            compiler_params=streaming,
            cost_estimate=light,
            name="ring_add",
        )(self.table, *arrays)

    def place(self, outputs, pairs):
        units, chips, model = self.units, self.chips, self.sides[0].shape[1]
        size, extra = self.size, self.extra
        shapes = [struct((chips * units, model), F32), struct((model, chips * units), F32)]
        if not self.tiled:
            outputs = outputs or [jnp.zeros(shape.shape, F32) for shape in shapes]
            down, up = outputs
            is_down = self.table[2 * chips] == 0
            for step, near, far in pairs:
                start = self.table[step % chips] * units
                near, far = whole_block(near)[:units], whole_block(far)[:units]
                first = jnp.where(is_down, near, far).astype(F32)
                second = jnp.where(is_down, far, near).astype(F32).T
                down = lax.dynamic_update_slice_in_dim(down, first, start, 0)
                up = lax.dynamic_update_slice_in_dim(up, second, start, 1)
            return [down, up]
        first = pairs[0][0] % chips
        stride = pairs[-1][0] % chips - first
        blocks = [pieces_of(pair[1]) + pieces_of(pair[2]) for pair in pairs]
        flat = [piece for block in blocks for piece in block]

        def place(at, table):
            return table[first + at * stride]

        def chip(at, table):
            return table[chips + first + at * stride]

        column = pl.BlockSpec(
            (model, 2 * HD), lambda at, table: (0, lax.div(chip(at, table), 2))
        )
        columns = [column] * (3 if outputs else 0)
        heads = [[first, first + stride][at] + chips for at in range(len(pairs))]
        return pl.pallas_call(
            functools.partial(place_kernel, heads, len(blocks[0]) // 2, (units, size, extra)),
            grid_spec=pltpu.PrefetchScalarGridSpec(
                num_scalar_prefetch=1,
                grid=(len(pairs),),
                in_specs=[pl.BlockSpec(memory_space=pl.ANY)] * (len(outputs) - len(columns))
                + columns
                + [pl.BlockSpec(piece.shape, lambda at, table: (0, 0)) for piece in flat],
                out_specs=[
                    pl.BlockSpec((units, model), lambda at, table: (place(at, table), 0)),
                    pl.BlockSpec((model, units), lambda at, table: (0, place(at, table))),
                    pl.BlockSpec((2, 1, extra, model), lambda at, table: (0, chip(at, table), 0, 0)),
                    pl.BlockSpec(
                        (1, 2, small_rows, model), lambda at, table: (chip(at, table), 0, 0, 0)
                    ),
                ]
                + [column] * 3,
            ),
            out_shape=shapes
            + [
                struct((2, chips, extra, model), F32),
                struct((chips, 2, small_rows, model), F32),
            ]
            + [struct((model, chips * HD), F32)] * 3,
            input_output_aliases={1 + at: at for at in range(len(outputs))},
            compiler_params=streaming,
            cost_estimate=light,
            name="place",
        )(self.table, *outputs, *flat)


def place_kernel(heads, width, sizes, table, *refs):
    count = len(heads)
    refs, (down, up, weight, small), projections = refs[:-7], refs[-7:-3], refs[-3:]
    blocks, refs = refs[-2 * width * count :], refs[: -2 * width * count]
    core = table[table.shape[0] - 2]
    units, size, extra = sizes
    rows = [pl.ds(0, units), pl.ds(units, size), pl.ds(units + size, extra)]
    rows.append(pl.ds(units + size + extra, small_rows))

    def read(block, which):
        return jnp.concatenate([piece[rows[which], :] for piece in block], axis=1)

    def put(first, second, head):
        down[...] = read(first, 0).astype(F32)
        up[...] = read(second, 0).astype(F32).T
        for side, block in ((0, first), (1, second)):
            weight[side, 0] = read(block, 2).astype(F32)
            small[0, side] = read(block, 3).astype(F32)
        both = jnp.concatenate([read(first, 1), read(second, 1)], axis=0)
        for at, output in enumerate(projections):
            part = both[at * HD : at * HD + HD].astype(F32)
            part = jnp.concatenate([part, part], axis=0).T
            if refs:
                mine = lax.broadcasted_iota(jnp.int32, part.shape, 1) // HD == head % 2
                part = jnp.where(mine, part, refs[at - 3][...])
            output[...] = part

    for at in range(count):
        near, far = (
            blocks[(2 * at + side) * width : (2 * at + side + 1) * width] for side in range(2)
        )
        head = table[heads[at]]
        here = pl.program_id(0) == at
        pl.when(here & (core == 0))(functools.partial(put, near, far, head))
        pl.when(here & (core != 0))(functools.partial(put, far, near, head))


def head_gradient_kernel(steps, chips, table, grads_ref, *refs):
    parts, out_ref = refs[:-1], refs[-1]
    for at, part in enumerate(parts):

        @pl.when(pl.program_id(0) == at)
        def _(part=part):
            chosen = [grads_ref[table[chips + step % chips]] for step in steps]
            total = product(jnp.concatenate(chosen, axis=1), part[...])
            out_ref[...] = total.astype(BF16)


def head_gradient(grads, parts, steps, table):
    chips, rows, _ = grads.shape
    columns = parts[0].shape[1]

    def column(at, table):
        mine = table[2 * chips + 1] if len(parts) > 1 else 0
        return (0, jnp.where(at == 0, mine, 1 - mine))

    return pl.pallas_call(
        functools.partial(head_gradient_kernel, steps, chips),
        grid_spec=pltpu.PrefetchScalarGridSpec(
            num_scalar_prefetch=1,
            grid=(len(parts),),
            in_specs=[
                pl.BlockSpec(array.shape, lambda at, table, rank=array.ndim: (0,) * rank)
                for array in (grads, *parts)
            ],
            out_specs=pl.BlockSpec((rows, columns), column),
        ),
        out_shape=struct((rows, columns * len(parts)), BF16),
        compiler_params=streaming,
        cost_estimate=light,
        name="head_gradient",
    )(table, grads, *parts)


def core_half(values, axis, side):
    size = values.shape[axis] // 2
    return lax.dynamic_slice_in_dim(values, side * size, size, axis)


def share_halves(values, axis):
    core = lax.axis_index("core")
    return core_half(values, axis, core), swap_cores(core_half(values, axis, 1 - core))


def local(
    block_input,
    out_grad,
    segments,
    lead_steps,
    gain_attn,
    shift_attn,
    lead_weight,
    query_weight,
    key_weight,
    value_weight,
    output_weight,
    output_bias,
    gain_mlp,
    shift_mlp,
    up_weight,
    up_bias,
    down_weight,
    down_bias,
):
    rows, model = block_input.shape
    heads = query_weight.shape[1] // HD
    width = heads * HD
    chips, core = lax.axis_size("chip"), lax.axis_index("core")
    split = chips // heads
    crops = lead_steps.shape[0]
    table = ring_table()
    weights = (query_weight, key_weight, value_weight)
    cut = model // 2 if lax.axis_size("head") == 2 else model
    payload, attn_in, attn_in_cut = project(
        table, cut, block_input, segments, lead_steps, gain_attn, shift_attn, lead_weight, weights
    )
    if split == 1:
        own = to_heads(payload)
        queries = own
    else:
        queries = scatter_queries(payload.reshape(-1, rows), heads, split)
        own = to_heads(jnp.repeat(payload, split, axis=0))
    own, attn_in_cut = lax.optimization_barrier((own, attn_in_cut))
    inputs = Gather(attn_in_cut)
    inputs.send(inputs.ready)
    other = swap_cores(own)
    raw, out, logsum = attention_forward(queries, own, other, crops)
    inputs.state, out = lax.optimization_barrier((inputs.state, out))
    attn_out = gather_queries(out, heads, split, rows)
    attn_out = visit([inputs], attn_out)
    branches = across_heads(product(attn_out, output_weight, 0, 0).astype(BF16))
    wide = block_input.astype(F32)
    mean_attn = jnp.mean(wide, axis=-1, keepdims=True)
    centred = wide - mean_attn
    inverse_attn = lax.rsqrt(jnp.mean(centred * centred, axis=-1, keepdims=True) + eps)
    mean_attn, inverse_attn = visit([inputs], (mean_attn, inverse_attn))
    keep, give, keep_in, give_in, hidden, dup_bias, mlp_part, d_mlp_part = mlp(
        table,
        block_input,
        out_grad,
        branches,
        output_bias,
        gain_mlp,
        shift_mlp,
        up_weight,
        up_bias,
        down_weight,
    )
    keep, give, keep_in, give_in, d_mlp_part = visit(
        [inputs], (keep, give, keep_in, give_in, d_mlp_part)
    )
    d_mlp = across_heads(d_mlp_part)
    ring = Reduce(keep, swap_cores(give), keep_in, swap_cores(give_in), table)
    mlp_part, d_mlp = lax.optimization_barrier((mlp_part, d_mlp))
    d_hidden, d_branch, d_attn, sums = middle(hidden, out_grad, d_mlp, gain_mlp, output_weight)
    d_branch, mlp_part = visit([ring, inputs], (d_branch, mlp_part))
    while inputs.busy():
        visit([inputs], ())
    mlp_out = across_heads(mlp_part)
    out_near, out_far = share_halves(attn_out, 0)
    d_attn, d_branch_far = lax.optimization_barrier((d_attn, swap_cores(d_branch)))
    grads = scatter_queries(d_attn, heads, split)
    doutput = product(out_near, d_branch) + product(out_far, d_branch_far)
    doutput = doutput.astype(BF16).reshape(chips, -1, model)
    steps, inputs = zip(*inputs.blocks)
    inputs = join(inputs)
    parts = across_heads(inputs) if cut != model else [inputs]
    doutput = visit([ring], doutput)
    doutput = to_heads(doutput)
    dquery, far_sums = attention_backward(queries, grads, raw, logsum, other, [], crops)
    far_sums = swap_cores(far_sums)
    grads, dquery = visit([ring], (grads, dquery))
    head_grads = attention_backward(
        queries, grads, raw, logsum, own, [dquery, far_sums], crops
    )
    head_grads = ring.arrive(head_grads)
    doutput, head_grads = lax.optimization_barrier((doutput, head_grads))
    small = jnp.concatenate([sums.reshape(-1), dup_bias[0]])
    small = jnp.pad(small, (0, small_rows * model - small.shape[0])).reshape(small_rows, model)
    below = [[doutput], [small]]
    if split == 1:
        (head_grads,) = head_grads
        moved = to_heads(head_grads)
        projections = head_gradient(head_grads, parts, steps, table)
        near, far = share_halves(projections, 0)
        size, below = near.shape[0], [[near, far]] + below
        dquery, dkey, dvalue = (
            moved[:, at * HD : at * HD + HD].reshape(width, rows) for at in range(3)
        )
    else:
        dquery, key_value = head_grads
        dquery = gather_queries(dquery, heads, split, rows)
        moved = to_heads(key_value).reshape(heads, split, 2 * HD, rows).astype(F32)
        moved = jnp.sum(moved, axis=1).astype(BF16)
        dkey, dvalue = (moved[:, at * HD : at * HD + HD].reshape(width, rows) for at in range(2))
        size = 0
        projections = [
            lax.psum(product(attn_in, grad, 0, 1).astype(BF16), ("chip", "core")).astype(F32)
            for grad in (dquery, dkey, dvalue)
        ]
    start, ring.size, ring.extra = ring.units, size, doutput.shape[1]
    gathered = Gather(ring.finish(below), True, ring.place)
    gathered.send(gathered.ready)
    d_part = (
        product(dquery, query_weight, 0, 1)
        + product(dkey, key_weight, 0, 1)
        + product(dvalue, value_weight, 0, 1)
    )
    d_in = across_heads(d_part.astype(BF16))
    unit_attn = (block_input.astype(F32) - mean_attn) * inverse_attn
    onehot = (segments[:, None] == jnp.arange(crops, dtype=jnp.int32)[None, :]).astype(F32)
    lead = jnp.sum(onehot * lead_steps.astype(F32)[None, :], axis=1) / 12.0
    ends = jnp.stack(
        [
            jnp.sum(d_part * unit_attn, axis=0),
            jnp.sum(d_part, axis=0),
            jnp.sum(lead[:, None] * d_part, axis=0),
        ]
    )
    ends = ends.reshape(-1, 128)
    ends = functools.reduce(jnp.add, across_heads(ends))
    ends = ends + swap_cores(ends)
    moves = [chips >> (at + 1) for at in range(chips.bit_length() - 1)][::-1]

    def step_ends(ends):
        if not moves:
            return [ends]
        reach = moves.pop(0)
        pairs = [(chip, chip ^ reach) for chip in range(chips)]
        return [ends, lax.ppermute(ends, "chip", pairs)]

    ends = step_ends(visit([gathered], ends))
    ends, mlp_out = visit([gathered], (ends, mlp_out))
    ends = step_ends(functools.reduce(jnp.add, ends))
    block_output = hidden + down_bias
    for part in mlp_out:
        block_output += part.astype(F32)
    block_output = block_output.astype(BF16)
    d_in, block_output, ends = visit([gathered], (d_in, block_output, ends))
    ends = step_ends(functools.reduce(jnp.add, ends))
    d_in = functools.reduce(jnp.add, (part.astype(F32) for part in d_in))
    input_grad = (d_hidden + normalize_back(d_in * gain_attn, unit_attn, inverse_attn)).astype(
        BF16
    )
    while gathered.busy() or moves:
        input_grad, ends = visit([gathered], (input_grad, ends))
        ends = step_ends(functools.reduce(jnp.add, ends))
    ends = functools.reduce(jnp.add, ends).reshape(3, model)
    ddown_weight, dup_weight, *rest = gathered.outputs
    if split == 1:
        doutput_weight, small, *projections = rest
        doutput_weight = doutput_weight.reshape(width, model)
    if split != 1:
        blocks = jnp.zeros((2, chips, ring.extra + small_rows, model), F32)
        for step, near, far in gathered.pairs:
            for side, block in ((core, near), (1 - core, far)):
                at = (side, table[chips + step % chips], 0, 0)
                block = whole_block(block)[None, None, start:].astype(F32)
                blocks = lax.dynamic_update_slice(blocks, block, at)
        doutput_weight = blocks[:, :, :-small_rows].reshape(width, model)
        small = blocks[:, :, -small_rows:]
    small = jnp.sum(small, axis=(0, 1))
    dup_bias = small[4:].reshape(-1)[: dup_bias.shape[1]]
    return (
        block_output,
        input_grad,
        ends[0],
        ends[1],
        ends[2],
        *projections,
        doutput_weight,
        *small[:3],
        dup_weight,
        dup_bias,
        ddown_weight,
        small[3],
    )


def solution(mesh):
    bands, halves = mesh.shape["band"], mesh.shape["head"]
    inner = Mesh(mesh.devices.reshape(bands // 2, 2, halves), ("chip", "core", "head"))
    band = ("chip", "core")
    rows, columns, split_rows = P(band, None), P(None, "head"), P("head", None)
    return jax.shard_map(
        local,
        mesh=inner,
        in_specs=(
            rows,
            rows,
            P(band),
            P(),
            P(),
            P(),
            P(),
            columns,
            columns,
            columns,
            split_rows,
            P(),
            P(),
            P(),
            columns,
            P("head"),
            split_rows,
            P(),
        ),
        out_specs=(
            rows,
            rows,
            P(),
            P(),
            P(),
            columns,
            columns,
            columns,
            split_rows,
            P(),
            P(),
            P(),
            columns,
            P("head"),
            split_rows,
            P(),
        ),
        check_vma=False,
    )
```

```python
import functools
import math

import jax
import jax.numpy as jnp
from jax import lax
from jax.experimental import pallas as pl
from jax.experimental.pallas import tpu as pltpu
from jax.sharding import Mesh, PartitionSpec as P

HD = 64
F32 = jnp.float32
BF16 = jnp.bfloat16
eps = 1e-05
masked_value = -1e30
seg_row = 3 * HD
payload_rows = 3 * HD + 16
small_rows = 16
params = pltpu.CompilerParams(vmem_limit_bytes=48 * 2**20)
streaming = pltpu.CompilerParams(vmem_limit_bytes=63_400_000)


def normalize(values):
    centred = values - jnp.mean(values, axis=-1, keepdims=True)
    inverse = lax.rsqrt(jnp.mean(centred * centred, axis=-1, keepdims=True) + eps)
    return (centred * inverse, inverse)


def normalize_back(grad_unit, unit, inverse):
    return inverse * (
        grad_unit
        - jnp.mean(grad_unit, axis=-1, keepdims=True)
        - unit * jnp.mean(grad_unit * unit, axis=-1, keepdims=True)
    )


def product(first, second, first_axis=1, second_axis=0):
    return lax.dot_general(
        first,
        second,
        (((first_axis,), (second_axis,)), ((), ())),
        preferred_element_type=jnp.float32,
    )


def struct(shape, dtype):
    return jax.ShapeDtypeStruct(shape, dtype)


def whole_spec(shape):
    return pl.BlockSpec(shape, lambda *at: (0,) * len(shape))


light = pl.CostEstimate(flops=1, bytes_accessed=1, transcendentals=0)


def project_kernel(
    table, input_ref, segment_ref, steps_ref, gain, shift, lead_weight, *refs
):
    weights, (payload_ref, attn_in_ref, cut_ref) = refs[:3], refs[3:]
    rows = input_ref.shape[0]

    @pl.when(pl.program_id(0) == 0)
    def _():
        unit, _ = normalize(input_ref[...].astype(F32))
        crops = steps_ref.shape[0]
        crop = lax.broadcasted_iota(jnp.int32, (crops, rows), 0)
        steps = jnp.zeros((crops, rows), jnp.int32)
        for at in range(crops):
            steps = jnp.where(crop == at, steps_ref[at], steps)
        steps = jnp.where(crop == segment_ref[...], steps, 0).astype(F32)
        lead = product(steps, jnp.ones((crops, 128), F32), 0, 0)[:, :1] / 12.0
        attn_in = unit * gain[...] + shift[...] + lead * lead_weight[...]
        attn_in = attn_in.astype(BF16)
        attn_in_ref[...] = attn_in
        columns = cut_ref.shape[1]
        first = table[table.shape[0] - 1] % (attn_in.shape[1] // columns) == 0
        cut_ref[...] = jnp.where(first, attn_in[:, :columns], attn_in[:, -columns:])

    for at, weight in enumerate(weights):
        part = product(attn_in_ref[...], weight[...]).T.astype(BF16)
        for head in range(2):
            payload_ref[head, pl.ds(at * HD, HD), :] = part[head * HD : head * HD + HD]
    segment = jnp.broadcast_to(segment_ref[...].astype(F32), (16, rows)).astype(BF16)
    for head in range(2):
        payload_ref[head, pl.ds(seg_row, 16), :] = segment


def project(table, cut, block_input, segments, lead_steps, gain, shift, lead_weight, weights):
    rows, model = block_input.shape
    heads = weights[0].shape[1] // HD
    line = whole_spec((1, model))
    column = pl.BlockSpec((model, 2 * HD), lambda at, table: (0, at))
    return pl.pallas_call(
        project_kernel,
        grid_spec=pltpu.PrefetchScalarGridSpec(
            num_scalar_prefetch=1,
            grid=(heads // 2,),
            in_specs=[
                whole_spec(block_input.shape),
                whole_spec((1, rows)),
                pl.BlockSpec(memory_space=pltpu.SMEM),
            ]
            + [line] * 3
            + [column] * 3,
            out_specs=[
                pl.BlockSpec((2, payload_rows, rows), lambda at, table: (at, 0, 0)),
                whole_spec((rows, model)),
                whole_spec((rows, cut)),
            ],
        ),
        out_shape=[
            struct((heads, payload_rows, rows), BF16),
            struct((rows, model), BF16),
            struct((rows, cut), BF16),
        ],
        compiler_params=streaming,
        cost_estimate=light,
        name="project",
    )(table, block_input, segments[None], lead_steps, gain[None], shift[None], lead_weight[None], *weights)


def mlp_kernel(count, core_ref, input_ref, grad_ref, *refs):
    branches, refs = refs[:count], refs[count:]
    output_bias, gain, shift, up_weight, up_bias, down_weight = refs[:6]
    keep_ref, give_ref, keep_in_ref, give_in_ref, hidden_ref, bias_ref, forward_ref, back_ref = refs[
        6:14
    ]
    mlp_in_ref, forward, back = refs[14:]
    at = pl.program_id(0)
    is_down = core_ref[core_ref.shape[0] - 2] == 0

    @pl.when(at == 0)
    def _():
        hidden = input_ref[...].astype(F32) + output_bias[...]
        for branch in branches:
            hidden += branch[...].astype(F32)
        hidden_ref[...] = hidden
        unit, _ = normalize(hidden)
        mlp_in = (unit * gain[...] + shift[...]).astype(BF16)
        mlp_in_ref[...] = mlp_in
        keep_in_ref[...] = jnp.where(is_down, grad_ref[...], mlp_in)
        give_in_ref[...] = jnp.where(is_down, mlp_in, grad_ref[...])
        forward[...] = jnp.zeros_like(forward)
        back[...] = jnp.zeros_like(back)

    upper = product(mlp_in_ref[...], up_weight[...]) + up_bias[...]
    share = 0.5 + 0.5 * lax.erf(upper * math.sqrt(0.5))
    slope = share + upper * (jnp.exp(upper * upper * -0.5) * (1.0 / math.sqrt(2.0 * math.pi)))
    active = (upper * share).astype(BF16)
    d_active = product(grad_ref[...], down_weight[...], 1, 1)
    d_upper = (d_active * slope).astype(BF16)
    keep_ref[...] = jnp.where(is_down, active, d_upper)
    give_ref[...] = jnp.where(is_down, d_upper, active)
    bias_ref[...] = jnp.sum(d_upper.astype(F32), axis=0, keepdims=True)
    forward[...] += product(active, down_weight[...])
    back[...] += product(d_upper, up_weight[...], 1, 1)

    @pl.when(at == pl.num_programs(0) - 1)
    def _():
        forward_ref[...] = forward[...].astype(BF16)
        back_ref[...] = back[...].astype(BF16)


def mlp(
    table, block_input, out_grad, branches, output_bias, gain, shift, up_weight, up_bias, down_weight
):
    rows, model = block_input.shape
    units = up_weight.shape[1]
    step = math.gcd(units, 1024)
    tile, line = whole_spec((rows, model)), whole_spec((1, model))
    wide = pl.BlockSpec((rows, step), lambda at, table: (0, at))
    bias = pl.BlockSpec((1, step), lambda at, table: (0, at))
    return pl.pallas_call(
        functools.partial(mlp_kernel, len(branches)),
        grid_spec=pltpu.PrefetchScalarGridSpec(
            num_scalar_prefetch=1,
            grid=(units // step,),
            in_specs=[tile] * (2 + len(branches))
            + [line] * 3
            + [
                pl.BlockSpec((model, step), lambda at, table: (0, at)),
                bias,
                pl.BlockSpec((step, model), lambda at, table: (at, 0)),
            ],
            out_specs=[wide, wide, tile, tile, tile, bias, tile, tile],
            scratch_shapes=[pltpu.VMEM((rows, model), BF16)]
            + [pltpu.VMEM((rows, model), F32)] * 2,
        ),
        out_shape=[struct((rows, units), BF16)] * 2
        + [struct((rows, model), BF16)] * 2
        + [
            struct((rows, model), F32),
            struct((1, units), F32),
            struct((rows, model), BF16),
            struct((rows, model), BF16),
        ],
        compiler_params=streaming,
        cost_estimate=light,
        name="mlp",
    )(
        table,
        block_input,
        out_grad,
        *branches,
        output_bias[None],
        gain[None],
        shift[None],
        up_weight,
        up_bias[None],
        down_weight,
    )


def middle_kernel(count, hidden_ref, grad_ref, *refs):
    parts, refs = refs[:count], refs[count:]
    gain, output_weight, d_hidden_ref, d_branch_ref, d_attn_ref, sums_ref = refs
    unit, inverse = normalize(hidden_ref[...])
    d_mlp = parts[0][...].astype(F32)
    for part in parts[1:]:
        d_mlp += part[...].astype(F32)
    grad = grad_ref[...].astype(F32)
    d_hidden = grad + normalize_back(d_mlp * gain[...], unit, inverse)
    d_hidden_ref[...] = d_hidden
    d_branch = d_hidden.astype(BF16)
    d_branch_ref[...] = d_branch
    d_attn_ref[...] = product(output_weight[...], d_branch, 1, 1).astype(BF16)
    for at, values in enumerate((d_hidden, d_mlp * unit, d_mlp, grad)):
        sums_ref[pl.ds(at, 1), :] = jnp.sum(values, axis=0, keepdims=True)


def middle(hidden, out_grad, parts, gain, output_weight):
    rows, model = hidden.shape
    width = output_weight.shape[0]
    return pl.pallas_call(
        functools.partial(middle_kernel, len(parts)),
        out_shape=[
            struct((rows, model), F32),
            struct((rows, model), BF16),
            struct((width, rows), BF16),
            struct((4, model), F32),
        ],
        compiler_params=streaming,
        cost_estimate=light,
        name="middle",
    )(hidden, out_grad, *parts, gain[None], output_weight)


def mask_rows(piece, chip, crops):
    crop = lax.broadcasted_iota(jnp.int32, (HD, piece.shape[2]), 0)
    segment = piece[chip, pl.ds(seg_row, 16), :].astype(F32)[:1].astype(jnp.int32)
    return jnp.where((crop != segment) & (crop < crops), masked_value, 0.0)


def load_keys(piece, crops, keys, key_t, value_n):
    chips, _, patches = piece.shape
    for chip in range(chips):
        key = piece[chip, pl.ds(HD, HD), :]
        value = piece[chip, pl.ds(2 * HD, HD), :]
        place = pl.ds(chip * patches, patches)
        both = jnp.concatenate([key.astype(F32), mask_rows(piece, chip, crops)], axis=0)
        keys[place, :] = both.T.astype(BF16)
        key_t[:, place] = key
        value_n[place, :] = value.astype(F32).T.astype(BF16)


def masked_query(query_ref, dtype=BF16):
    query = query_ref[0, pl.ds(0, HD), :].astype(F32) * 0.125
    segment = query_ref[0, pl.ds(seg_row, 16), :].astype(F32)[:1].astype(jnp.int32)
    crop = lax.broadcasted_iota(jnp.int32, query.shape, 0)
    onehot = jnp.where(crop == segment, 1.0, 0.0)
    return jnp.concatenate([query, onehot], axis=0).astype(dtype)


def forward_kernel(
    crops, step, query_ref, own, other, raw_ref, out_ref, logsum_ref, key_t, value_n, scores
):
    @pl.when(pl.program_id(0) == 0)
    def _():
        start = 0
        for piece in (own, other):
            chips, _, patches = piece.shape
            for chip in range(chips):
                place = pl.ds(start, patches)
                key = piece[chip, pl.ds(HD, HD), :].astype(F32)
                key_t[:, place] = jnp.concatenate([key, mask_rows(piece, chip, crops)], axis=0).astype(BF16)
                value = piece[chip, pl.ds(2 * HD, HD), :].astype(F32)
                value = jnp.concatenate([value, jnp.ones_like(value)], axis=0)
                value_n[place, :] = value.T.astype(BF16)
                start += patches

    query = masked_query(query_ref, F32).T.astype(BF16)
    count = query.shape[0]
    top = jnp.full((count, 128), masked_value, F32)
    for start in range(0, key_t.shape[1], step):
        block = product(query, key_t[:, pl.ds(start, step)])
        scores[:, pl.ds(start, step)] = block
        for at in range(0, step, 128):
            top = jnp.maximum(top, block[:, at : at + 128])
    top = jnp.max(top, axis=1, keepdims=True)
    accum = jnp.zeros((count, 2 * HD), F32)
    for start in range(0, key_t.shape[1], step):
        weights = jnp.exp(scores[:, pl.ds(start, step)] - top).astype(BF16)
        accum += product(weights, value_n[pl.ds(start, step), :])
    accum = accum.T
    total = accum[HD : HD + 1]
    raw = accum[:HD] / total
    raw_ref[0] = raw
    out_ref[0] = raw.astype(BF16)
    top = jnp.broadcast_to(top, (count, 128)).T[:1]
    logsum_ref[0] = top + jnp.log(total)


def backward_kernel(
    crops,
    extra,
    query_ref,
    grad_ref,
    raw_ref,
    logsum_ref,
    piece,
    *refs,
):
    extras, refs = refs[:extra], refs[extra:]
    outputs, (keys, key_t, value_n, sums) = refs[:-4], refs[-4:]
    group = pl.program_id(0)

    @pl.when(group == 0)
    def _():
        load_keys(piece, crops, keys, key_t, value_n)
        sums[...] = jnp.zeros_like(sums)

    query = masked_query(query_ref)
    grad = grad_ref[0]
    grad_wide = grad.astype(F32)
    delta = jnp.sum(grad_wide * raw_ref[0], axis=0, keepdims=True)
    scaled = query_ref[0, pl.ds(0, HD), :].astype(F32) * 0.125
    zero = jnp.zeros_like(scaled)
    query_side = jnp.concatenate([scaled, zero], axis=0).T.astype(BF16)
    grad_side = jnp.concatenate([zero, grad_wide], axis=0).T.astype(BF16)
    probs = jnp.exp(product(keys[...], query) - logsum_ref[0])
    dprobs = product(value_n[...], grad)
    dscores = (probs * (dprobs - delta)).astype(BF16)
    sums[...] += product(dscores, query_side) + product(probs.astype(BF16), grad_side)
    dquery = product(key_t[...], dscores) * 0.125
    if extras:
        dquery += extras[0][0]
    if len(outputs) == 1:
        outputs[0][group, pl.ds(0, HD), :] = dquery.astype(BF16)
    else:
        outputs[0][0] = dquery.astype(outputs[0].dtype)

    @pl.when(group == pl.num_programs(0) - 1)
    def _():
        chips, _, patches = piece.shape
        for chip in range(chips):
            total = sums[pl.ds(chip * patches, patches), :].T
            if extra > 1:
                total += extras[1][chip].astype(F32)
            total = total.astype(BF16)
            if len(outputs) == 1:
                outputs[0][chip, pl.ds(HD, 2 * HD), :] = total
            else:
                outputs[1][chip] = total


def key_step(count):
    return 1024 if count % 1024 == 0 else 256


def query_spec(rows, patches):
    return pl.BlockSpec((1, rows, patches), lambda group: (group, 0, 0))


def attention_forward(queries, own, other, crops):
    groups, _, patches = queries.shape
    count = 2 * own.shape[0] * own.shape[2]
    return pl.pallas_call(
        functools.partial(forward_kernel, crops, key_step(count)),
        grid=(groups,),
        in_specs=[
            query_spec(payload_rows, patches),
            whole_spec(own.shape),
            whole_spec(other.shape),
        ],
        out_specs=[query_spec(HD, patches), query_spec(HD, patches), query_spec(1, patches)],
        out_shape=[
            struct((groups, HD, patches), F32),
            struct((groups, HD, patches), BF16),
            struct((groups, 1, patches), F32),
        ],
        scratch_shapes=[
            pltpu.VMEM((2 * HD, count), BF16),
            pltpu.VMEM((count, 2 * HD), BF16),
            pltpu.VMEM((patches, count), F32),
        ],
        compiler_params=streaming,
        cost_estimate=light,
        name="attention_forward",
    )(queries, own, other)


def attention_backward(queries, grads, raw, logsum, keys, extras, crops):
    groups, _, patches = queries.shape
    chips, count = keys.shape[0], keys.shape[0] * keys.shape[2]
    sums_shape = (chips, 2 * HD, keys.shape[2])
    specs = [query_spec(HD, patches), whole_spec(sums_shape)]
    shapes = [
        struct((groups, HD, patches), BF16 if extras else F32),
        struct(sums_shape, BF16),
    ]
    outs = specs
    if extras and (groups, patches) == (chips, keys.shape[2]):
        shapes = [struct((chips, 3 * HD, patches), BF16)]
        outs = [whole_spec(shapes[0].shape)]
    return pl.pallas_call(
        functools.partial(backward_kernel, crops, len(extras)),
        grid=(groups,),
        in_specs=[
            query_spec(payload_rows, patches),
            query_spec(HD, patches),
            query_spec(HD, patches),
            query_spec(1, patches),
            whole_spec(keys.shape),
        ]
        + specs[: len(extras)],
        out_specs=outs,
        out_shape=shapes,
        scratch_shapes=[
            pltpu.VMEM((count, 2 * HD), BF16),
            pltpu.VMEM((HD, count), BF16),
            pltpu.VMEM((count, HD), BF16),
            pltpu.VMEM((count, 2 * HD), F32),
        ],
        compiler_params=params,
        cost_estimate=light,
        name="attention_backward",
    )(queries, grads, raw, logsum, keys, *extras)


def swap_cores(values):
    return lax.ppermute(values, "core", [(0, 1), (1, 0)])


def to_heads(blocks):
    return lax.all_to_all(blocks, "chip", 0, 0, tiled=True)


def scatter_queries(values, heads, split):
    rows, patches = values.shape[0] // heads, values.shape[1]
    if split == 1:
        return to_heads(values.reshape(heads, rows, patches))
    part = patches // split
    blocks = values.reshape(heads, rows, split, part).transpose(0, 2, 1, 3)
    moved = to_heads(blocks.reshape(heads * split, rows, part))
    width = min(256, moved.shape[0] * part)
    joined = moved.transpose(1, 0, 2).reshape(rows, -1, width)
    return joined.transpose(1, 0, 2)


def gather_queries(values, heads, split, patches):
    rows = values.shape[1]
    if split == 1:
        return to_heads(values).reshape(heads * rows, patches)
    part = patches // split
    joined = values.transpose(1, 0, 2).reshape(rows, heads * split, part)
    moved = to_heads(joined.transpose(1, 0, 2)).reshape(heads, split, rows, part)
    return moved.transpose(0, 2, 1, 3).reshape(heads * rows, patches)


def across_heads(part):
    if lax.axis_size("head") == 2:
        return [part, lax.ppermute(part, "head", [(0, 1), (1, 0)])]
    return [lax.psum(part, "head")]


def ring_pairs(direction):
    chips = lax.axis_size("chip")
    order = list(range(0, chips, 2)) + list(range(chips - 1, 0, -2))
    return [(order[at], order[(at + direction) % chips]) for at in range(chips)]


def ring_table():
    chips, chip = lax.axis_size("chip"), lax.axis_index("chip")
    place = jnp.where(chip % 2 == 0, chip // 2, chips - 1 - chip // 2)
    steps = jnp.arange(2 * chips + 2, dtype=jnp.int32)
    places = (place + steps) % chips
    there = jnp.where(places < chips // 2, 2 * places, 2 * (chips - 1 - places) + 1)
    table = jnp.where(steps < chips, places, there)
    table = jnp.where(steps == 2 * chips, lax.axis_index("core"), table)
    return jnp.where(steps == 2 * chips + 1, lax.axis_index("head"), table).astype(jnp.int32)


def visit(streams, values):
    states, values = lax.optimization_barrier(([stream.state for stream in streams], values))
    for stream, state in zip(streams, states):
        stream.advance(state)
    ready, values = lax.optimization_barrier(([stream.ready for stream in streams], values))
    for stream, blocks in zip(streams, ready):
        stream.send(blocks)
    return values


def pieces_of(block):
    return list(block) if isinstance(block, tuple) else [block]


def whole_block(block):
    return jnp.concatenate(pieces_of(block), axis=1)


def join_kernel(counts, *refs):
    output, refs, start = refs[-1], list(refs[:-1]), 0
    for count in counts:
        column = 0
        for _ in range(count):
            piece = refs.pop(0)
            rows, columns = piece.shape
            output[pl.ds(start, rows), pl.ds(column, columns)] = piece[...]
            column += columns
        start += rows


def join(blocks):
    blocks = [pieces_of(block) for block in blocks]
    rows = sum(block[0].shape[0] for block in blocks)
    columns = sum(piece.shape[1] for piece in blocks[0])
    return pl.pallas_call(
        functools.partial(join_kernel, [len(block) for block in blocks]),
        out_shape=struct((rows, columns), blocks[0][0].dtype),
        compiler_params=streaming,
        name="join",
    )(*[piece for block in blocks for piece in block])


def halves_kernel(left, right, left_ref, right_ref):
    left_ref[...] = left[...]
    right_ref[...] = right[...]


def halves(left, right):
    rows, columns = left.shape
    if rows % 16 or columns % 256:
        return [left[:, : columns // 2], right[:, columns // 2 :]]
    out = pl.BlockSpec((rows, columns // 2), lambda at: (0, 0))
    return pl.pallas_call(
        halves_kernel,
        grid=(1,),
        in_specs=[out, pl.BlockSpec((rows, columns // 2), lambda at: (0, 1))],
        out_specs=[out, out],
        out_shape=[struct((rows, columns // 2), left.dtype)] * 2,
        compiler_params=streaming,
        name="halves",
    )(left, right)


class Gather:
    def __init__(self, block, swap=False, take=None):
        self.reach, self.swap, self.take = lax.axis_size("chip") // 2, swap, take
        self.blocks, self.pairs, self.count = [], [], 0
        self.new, self.outputs = [0], []
        self.ready = [block]

    def send(self, ready):
        if len(self.new) < len(ready):
            ready = [tuple(ready)]
        new = list(zip(self.new, ready))
        self.blocks += new
        self.new = new
        self.count += 1
        sides = ready if len(ready) > 1 else ready * 2
        if self.count == self.reach:
            sides = halves(*sides)
        flying = []
        if self.count <= self.reach:
            flying = [
                lax.ppermute(block, "chip", ring_pairs(direction))
                for block, direction in zip(sides, (1, -1))
            ]
        if self.swap and ready:
            pairs = [(step, block, jax.tree.map(swap_cores, block)) for step, block in new]
            self.pairs += pairs
            self.outputs = self.take(self.outputs, pairs)
        self.state = (flying, self.outputs)

    def advance(self, state):
        arrived, self.outputs = state
        self.new = [-self.count, self.count]
        if self.count == self.reach:
            self.new = [self.count]
        self.ready = arrived

    def busy(self):
        return bool(self.state[0])


def add_kernel(wanted, count, _, *refs):
    outputs, refs = refs[-count:], list(refs[:-count])
    keep_in, far_in = refs.pop(0), refs.pop(0)
    at = pl.program_id(0)

    def put(output, total):
        output[...] = total.astype(BF16)

    for places, output in zip(wanted, outputs):
        near, far = refs.pop(0), refs.pop(0)
        total = product(near[...], keep_in[...], 0, 0) + product(far[...], far_in[...], 0, 0)
        arrived = [(place, refs.pop(0)) for place in places]
        if count > len(wanted):
            for place in range(count):
                pl.when(at == place)(functools.partial(put, outputs[place], total))
            return
        for place, part in arrived:
            if place is None:
                total += part[...].astype(F32)
        put(output, total)
        for place, part in arrived:
            if place is not None:
                pl.when(at == place)(lambda: put(output, total + part[...].astype(F32)))


def finish_kernel(counts, _, keep_in, far_in, near, far, ahead, behind, *refs):
    refs, output = list(refs[:-1]), refs[-1]
    total = product(near[...], keep_in[...], 0, 0) + product(far[...], far_in[...], 0, 0)
    total += ahead[...].astype(F32) + behind[...].astype(F32)
    start = total.shape[0]
    output[pl.ds(0, start), :] = total.astype(BF16)
    for count in counts:
        total = 0.0
        for _ in range(count):
            part = refs.pop(0)[...].astype(F32)
            total += part if part.ndim == 2 else jnp.sum(part, axis=0)
        output[pl.ds(start, total.shape[0]), :] = total.astype(BF16)
        start += total.shape[0]


class Reduce:
    def __init__(self, keep, far, keep_in, far_in, table):
        self.chips, self.table = lax.axis_size("chip"), table
        self.operands, self.sides = (keep, far), (keep_in, far_in)
        self.units = keep.shape[1] // self.chips
        self.tiled = self.units % 128 == 0
        self.left, self.rest = self.chips // 2, None
        blocks = self.add([(self.left, [])], True)
        self.send(blocks if len(blocks) > 1 else halves(blocks[0], blocks[0]))

    def send(self, ready):
        self.left -= 1
        self.state = [
            lax.ppermute(block, "chip", ring_pairs(direction))
            for block, direction in zip(ready, (1, -1))
        ]

    def advance(self, state):
        half = self.sides[0].shape[1] // 2
        ahead, behind = state
        places = (0, 1) if ahead.shape[1] == half else (None, None)
        self.ready = self.add(
            [(self.left, [(ahead, places[0])]), (-self.left, [(behind, places[1])])]
        )

    def arrive(self, values):
        self.state, values = lax.optimization_barrier((self.state, values))
        return values

    def finish(self, below):
        ahead, behind = self.state
        if not self.tiled:
            rows = self.add([(0, [(ahead, None), (behind, None)])])
            for parts in below:
                total = jnp.zeros(parts[0].shape[-2:], F32)
                for part in parts:
                    part = part.astype(F32)
                    total += part if part.ndim == 2 else jnp.sum(part, axis=0)
                rows.append(total.astype(BF16))
            return jnp.concatenate(rows, axis=0)
        (rows, model), units, chips = self.sides[0].shape, self.units, self.chips
        half = model // 2
        arrays = [ahead, behind] + [part for parts in below for part in parts]
        specs = [pl.BlockSpec((rows, half), lambda at, table: (0, at))] * 2
        specs += [pl.BlockSpec((rows, units), lambda at, table: (0, table[0]))] * 2
        for array in arrays:
            shape = array.shape[:-1] + (half,)
            specs.append(
                pl.BlockSpec(shape, lambda at, table, rank=array.ndim: (0,) * (rank - 1) + (at,))
            )
        height = units + sum(parts[0].shape[-2] for parts in below)
        return pl.pallas_call(
            functools.partial(finish_kernel, [len(parts) for parts in below]),
            grid_spec=pltpu.PrefetchScalarGridSpec(
                num_scalar_prefetch=1,
                grid=(2,),
                in_specs=specs,
                out_specs=pl.BlockSpec((height, half), lambda at, table: (0, at)),
            ),
            out_shape=struct((height, model), BF16),
            compiler_params=streaming,
            cost_estimate=light,
            name="ring_finish",
        )(self.table, *self.sides, *self.operands, *arrays)

    def add(self, wanted, split=False):
        (rows, model), units, chips = self.sides[0].shape, self.units, self.chips
        if not self.tiled:
            sums = []
            for step, parts in wanted:
                start = self.table[step % chips] * units
                total = jnp.zeros((units, model), F32)
                for operand, side in zip(self.operands, self.sides):
                    block = lax.dynamic_slice_in_dim(operand, start, units, 1)
                    total += product(block, side, 0, 0)
                for part, place in parts:
                    start = (place or 0) * part.shape[1]
                    total = total.at[:, start : start + part.shape[1]].add(part.astype(F32))
                sums.append(total.astype(BF16))
            return sums
        half = model // 2
        side = pl.BlockSpec((rows, half), lambda at, table: (0, at))
        whole = pl.BlockSpec((units, half), lambda at, table: (0, at))
        fixed = pl.BlockSpec((units, half), lambda at, table: (0, 0))
        specs, arrays = [side] * 2, list(self.sides)
        for step, parts in wanted:
            block = pl.BlockSpec(
                (rows, units), lambda at, table, step=step % chips: (0, table[step])
            )
            specs += [block] * 2 + [whole if place is None else fixed for _, place in parts]
            arrays += list(self.operands) + [part for part, _ in parts]
        places = [[place for _, place in parts] for _, parts in wanted]
        shapes, outs = [struct((units, model), BF16)] * len(wanted), [whole] * len(wanted)
        if split:
            shapes, outs = [struct((units, half), BF16)] * 2, [fixed] * 2
        return pl.pallas_call(
            functools.partial(add_kernel, places, len(shapes)),
            grid_spec=pltpu.PrefetchScalarGridSpec(
                num_scalar_prefetch=1,
                grid=(2,),
                in_specs=specs,
                out_specs=outs,
            ),
            out_shape=shapes,
            compiler_params=streaming,
            cost_estimate=light,
            name="ring_add",
        )(self.table, *arrays)

    def place(self, outputs, pairs):
        units, chips, model = self.units, self.chips, self.sides[0].shape[1]
        size, extra = self.size, self.extra
        shapes = [struct((chips * units, model), F32), struct((model, chips * units), F32)]
        if not self.tiled:
            outputs = outputs or [jnp.zeros(shape.shape, F32) for shape in shapes]
            down, up = outputs
            is_down = self.table[2 * chips] == 0
            for step, near, far in pairs:
                start = self.table[step % chips] * units
                near, far = whole_block(near)[:units], whole_block(far)[:units]
                first = jnp.where(is_down, near, far).astype(F32)
                second = jnp.where(is_down, far, near).astype(F32).T
                down = lax.dynamic_update_slice_in_dim(down, first, start, 0)
                up = lax.dynamic_update_slice_in_dim(up, second, start, 1)
            return [down, up]
        first = pairs[0][0] % chips
        stride = pairs[-1][0] % chips - first
        blocks = [pieces_of(pair[1]) + pieces_of(pair[2]) for pair in pairs]
        flat = [piece for block in blocks for piece in block]

        def place(at, table):
            return table[first + at * stride]

        def chip(at, table):
            return table[chips + first + at * stride]

        column = pl.BlockSpec(
            (model, 2 * HD), lambda at, table: (0, lax.div(chip(at, table), 2))
        )
        columns = [column] * (3 if outputs else 0)
        heads = [[first, first + stride][at] + chips for at in range(len(pairs))]
        return pl.pallas_call(
            functools.partial(place_kernel, heads, len(blocks[0]) // 2, (units, size, extra)),
            grid_spec=pltpu.PrefetchScalarGridSpec(
                num_scalar_prefetch=1,
                grid=(len(pairs),),
                in_specs=[pl.BlockSpec(memory_space=pl.ANY)] * (len(outputs) - len(columns))
                + columns
                + [pl.BlockSpec(piece.shape, lambda at, table: (0, 0)) for piece in flat],
                out_specs=[
                    pl.BlockSpec((units, model), lambda at, table: (place(at, table), 0)),
                    pl.BlockSpec((model, units), lambda at, table: (0, place(at, table))),
                    pl.BlockSpec((2, 1, extra, model), lambda at, table: (0, chip(at, table), 0, 0)),
                    pl.BlockSpec(
                        (1, 2, small_rows, model), lambda at, table: (chip(at, table), 0, 0, 0)
                    ),
                ]
                + [column] * 3,
            ),
            out_shape=shapes
            + [
                struct((2, chips, extra, model), F32),
                struct((chips, 2, small_rows, model), F32),
            ]
            + [struct((model, chips * HD), F32)] * 3,
            input_output_aliases={1 + at: at for at in range(len(outputs))},
            compiler_params=streaming,
            cost_estimate=light,
            name="place",
        )(self.table, *outputs, *flat)


def place_kernel(heads, width, sizes, table, *refs):
    count = len(heads)
    refs, (down, up, weight, small), projections = refs[:-7], refs[-7:-3], refs[-3:]
    blocks, refs = refs[-2 * width * count :], refs[: -2 * width * count]
    core = table[table.shape[0] - 2]
    units, size, extra = sizes
    rows = [pl.ds(0, units), pl.ds(units, size), pl.ds(units + size, extra)]
    rows.append(pl.ds(units + size + extra, small_rows))

    def read(block, which):
        return jnp.concatenate([piece[rows[which], :] for piece in block], axis=1)

    def put(first, second, head):
        down[...] = read(first, 0).astype(F32)
        up[...] = read(second, 0).astype(F32).T
        for side, block in ((0, first), (1, second)):
            weight[side, 0] = read(block, 2).astype(F32)
            small[0, side] = read(block, 3).astype(F32)
        both = jnp.concatenate([read(first, 1), read(second, 1)], axis=0)
        for at, output in enumerate(projections):
            part = both[at * HD : at * HD + HD].astype(F32)
            part = jnp.concatenate([part, part], axis=0).T
            if refs:
                mine = lax.broadcasted_iota(jnp.int32, part.shape, 1) // HD == head % 2
                part = jnp.where(mine, part, refs[at - 3][...])
            output[...] = part

    for at in range(count):
        near, far = (
            blocks[(2 * at + side) * width : (2 * at + side + 1) * width] for side in range(2)
        )
        head = table[heads[at]]
        here = pl.program_id(0) == at
        pl.when(here & (core == 0))(functools.partial(put, near, far, head))
        pl.when(here & (core != 0))(functools.partial(put, far, near, head))


def head_gradient_kernel(steps, chips, table, grads_ref, *refs):
    parts, out_ref = refs[:-1], refs[-1]
    for at, part in enumerate(parts):

        @pl.when(pl.program_id(0) == at)
        def _(part=part):
            chosen = [grads_ref[table[chips + step % chips]] for step in steps]
            total = product(jnp.concatenate(chosen, axis=1), part[...])
            out_ref[...] = total.astype(BF16)


def head_gradient(grads, parts, steps, table):
    chips, rows, _ = grads.shape
    columns = parts[0].shape[1]

    def column(at, table):
        mine = table[2 * chips + 1] if len(parts) > 1 else 0
        return (0, jnp.where(at == 0, mine, 1 - mine))

    return pl.pallas_call(
        functools.partial(head_gradient_kernel, steps, chips),
        grid_spec=pltpu.PrefetchScalarGridSpec(
            num_scalar_prefetch=1,
            grid=(len(parts),),
            in_specs=[
                pl.BlockSpec(array.shape, lambda at, table, rank=array.ndim: (0,) * rank)
                for array in (grads, *parts)
            ],
            out_specs=pl.BlockSpec((rows, columns), column),
        ),
        out_shape=struct((rows, columns * len(parts)), BF16),
        compiler_params=streaming,
        cost_estimate=light,
        name="head_gradient",
    )(table, grads, *parts)


def core_half(values, axis, side):
    size = values.shape[axis] // 2
    return lax.dynamic_slice_in_dim(values, side * size, size, axis)


def share_halves(values, axis):
    core = lax.axis_index("core")
    return core_half(values, axis, core), swap_cores(core_half(values, axis, 1 - core))


def local(
    block_input,
    out_grad,
    segments,
    lead_steps,
    gain_attn,
    shift_attn,
    lead_weight,
    query_weight,
    key_weight,
    value_weight,
    output_weight,
    output_bias,
    gain_mlp,
    shift_mlp,
    up_weight,
    up_bias,
    down_weight,
    down_bias,
):
    rows, model = block_input.shape
    heads = query_weight.shape[1] // HD
    width = heads * HD
    chips, core = lax.axis_size("chip"), lax.axis_index("core")
    split = chips // heads
    crops = lead_steps.shape[0]
    table = ring_table()
    weights = (query_weight, key_weight, value_weight)
    cut = model // 2 if lax.axis_size("head") == 2 else model
    payload, attn_in, attn_in_cut = project(
        table, cut, block_input, segments, lead_steps, gain_attn, shift_attn, lead_weight, weights
    )
    if split == 1:
        own = to_heads(payload)
        queries = own
    else:
        queries = scatter_queries(payload.reshape(-1, rows), heads, split)
        own = to_heads(jnp.repeat(payload, split, axis=0))
    own, attn_in_cut = lax.optimization_barrier((own, attn_in_cut))
    inputs = Gather(attn_in_cut)
    inputs.send(inputs.ready)
    other = swap_cores(own)
    raw, out, logsum = attention_forward(queries, own, other, crops)
    inputs.state, out = lax.optimization_barrier((inputs.state, out))
    attn_out = gather_queries(out, heads, split, rows)
    attn_out = visit([inputs], attn_out)
    branches = across_heads(product(attn_out, output_weight, 0, 0).astype(BF16))
    wide = block_input.astype(F32)
    mean_attn = jnp.mean(wide, axis=-1, keepdims=True)
    centred = wide - mean_attn
    inverse_attn = lax.rsqrt(jnp.mean(centred * centred, axis=-1, keepdims=True) + eps)
    mean_attn, inverse_attn = visit([inputs], (mean_attn, inverse_attn))
    keep, give, keep_in, give_in, hidden, dup_bias, mlp_part, d_mlp_part = mlp(
        table,
        block_input,
        out_grad,
        branches,
        output_bias,
        gain_mlp,
        shift_mlp,
        up_weight,
        up_bias,
        down_weight,
    )
    keep, give, keep_in, give_in, d_mlp_part = visit(
        [inputs], (keep, give, keep_in, give_in, d_mlp_part)
    )
    d_mlp = across_heads(d_mlp_part)
    ring = Reduce(keep, swap_cores(give), keep_in, swap_cores(give_in), table)
    mlp_part, d_mlp = lax.optimization_barrier((mlp_part, d_mlp))
    d_hidden, d_branch, d_attn, sums = middle(hidden, out_grad, d_mlp, gain_mlp, output_weight)
    d_branch, mlp_part = visit([ring, inputs], (d_branch, mlp_part))
    while inputs.busy():
        visit([inputs], ())
    mlp_out = across_heads(mlp_part)
    out_near, out_far = share_halves(attn_out, 0)
    d_attn, d_branch_far = lax.optimization_barrier((d_attn, swap_cores(d_branch)))
    grads = scatter_queries(d_attn, heads, split)
    doutput = product(out_near, d_branch) + product(out_far, d_branch_far)
    doutput = doutput.astype(BF16).reshape(chips, -1, model)
    steps, inputs = zip(*inputs.blocks)
    inputs = join(inputs)
    parts = across_heads(inputs) if cut != model else [inputs]
    doutput = visit([ring], doutput)
    doutput = to_heads(doutput)
    dquery, far_sums = attention_backward(queries, grads, raw, logsum, other, [], crops)
    far_sums = swap_cores(far_sums)
    grads, dquery = visit([ring], (grads, dquery))
    head_grads = attention_backward(
        queries, grads, raw, logsum, own, [dquery, far_sums], crops
    )
    head_grads = ring.arrive(head_grads)
    doutput, head_grads = lax.optimization_barrier((doutput, head_grads))
    small = jnp.concatenate([sums.reshape(-1), dup_bias[0]])
    small = jnp.pad(small, (0, small_rows * model - small.shape[0])).reshape(small_rows, model)
    below = [[doutput], [small]]
    if split == 1:
        (head_grads,) = head_grads
        moved = to_heads(head_grads)
        projections = head_gradient(head_grads, parts, steps, table)
        near, far = share_halves(projections, 0)
        size, below = near.shape[0], [[near, far]] + below
        dquery, dkey, dvalue = (
            moved[:, at * HD : at * HD + HD].reshape(width, rows) for at in range(3)
        )
    else:
        dquery, key_value = head_grads
        dquery = gather_queries(dquery, heads, split, rows)
        moved = to_heads(key_value).reshape(heads, split, 2 * HD, rows).astype(F32)
        moved = jnp.sum(moved, axis=1).astype(BF16)
        dkey, dvalue = (moved[:, at * HD : at * HD + HD].reshape(width, rows) for at in range(2))
        size = 0
        projections = [
            lax.psum(product(attn_in, grad, 0, 1).astype(BF16), ("chip", "core")).astype(F32)
            for grad in (dquery, dkey, dvalue)
        ]
    start, ring.size, ring.extra = ring.units, size, doutput.shape[1]
    gathered = Gather(ring.finish(below), True, ring.place)
    gathered.send(gathered.ready)
    d_part = (
        product(dquery, query_weight, 0, 1)
        + product(dkey, key_weight, 0, 1)
        + product(dvalue, value_weight, 0, 1)
    )
    d_in = across_heads(d_part.astype(BF16))
    unit_attn = (block_input.astype(F32) - mean_attn) * inverse_attn
    onehot = (segments[:, None] == jnp.arange(crops, dtype=jnp.int32)[None, :]).astype(F32)
    lead = jnp.sum(onehot * lead_steps.astype(F32)[None, :], axis=1) / 12.0
    ends = jnp.stack(
        [
            jnp.sum(d_part * unit_attn, axis=0),
            jnp.sum(d_part, axis=0),
            jnp.sum(lead[:, None] * d_part, axis=0),
        ]
    )
    ends = ends.reshape(-1, 128)
    ends = functools.reduce(jnp.add, across_heads(ends))
    ends = ends + swap_cores(ends)
    moves = [chips >> (at + 1) for at in range(chips.bit_length() - 1)][::-1]

    def step_ends(ends):
        if not moves:
            return [ends]
        reach = moves.pop(0)
        pairs = [(chip, chip ^ reach) for chip in range(chips)]
        return [ends, lax.ppermute(ends, "chip", pairs)]

    ends = step_ends(visit([gathered], ends))
    ends, mlp_out = visit([gathered], (ends, mlp_out))
    ends = step_ends(functools.reduce(jnp.add, ends))
    block_output = hidden + down_bias
    for part in mlp_out:
        block_output += part.astype(F32)
    block_output = block_output.astype(BF16)
    d_in, block_output, ends = visit([gathered], (d_in, block_output, ends))
    ends = step_ends(functools.reduce(jnp.add, ends))
    d_in = functools.reduce(jnp.add, (part.astype(F32) for part in d_in))
    input_grad = (d_hidden + normalize_back(d_in * gain_attn, unit_attn, inverse_attn)).astype(
        BF16
    )
    while gathered.busy() or moves:
        input_grad, ends = visit([gathered], (input_grad, ends))
        ends = step_ends(functools.reduce(jnp.add, ends))
    ends = functools.reduce(jnp.add, ends).reshape(3, model)
    ddown_weight, dup_weight, *rest = gathered.outputs
    if split == 1:
        doutput_weight, small, *projections = rest
        doutput_weight = doutput_weight.reshape(width, model)
    if split != 1:
        blocks = jnp.zeros((2, chips, ring.extra + small_rows, model), F32)
        for step, near, far in gathered.pairs:
            for side, block in ((core, near), (1 - core, far)):
                at = (side, table[chips + step % chips], 0, 0)
                block = whole_block(block)[None, None, start:].astype(F32)
                blocks = lax.dynamic_update_slice(blocks, block, at)
        doutput_weight = blocks[:, :, :-small_rows].reshape(width, model)
        small = blocks[:, :, -small_rows:]
    small = jnp.sum(small, axis=(0, 1))
    dup_bias = small[4:].reshape(-1)[: dup_bias.shape[1]]
    return (
        block_output,
        input_grad,
        ends[0],
        ends[1],
        ends[2],
        *projections,
        doutput_weight,
        *small[:3],
        dup_weight,
        dup_bias,
        ddown_weight,
        small[3],
    )


def solution(mesh):
    bands, halves = mesh.shape["band"], mesh.shape["head"]
    inner = Mesh(mesh.devices.reshape(bands // 2, 2, halves), ("chip", "core", "head"))
    band = ("chip", "core")
    rows, columns, split_rows = P(band, None), P(None, "head"), P("head", None)
    return jax.shard_map(
        local,
        mesh=inner,
        in_specs=(
            rows,
            rows,
            P(band),
            P(),
            P(),
            P(),
            P(),
            columns,
            columns,
            columns,
            split_rows,
            P(),
            P(),
            P(),
            columns,
            P("head"),
            split_rows,
            P(),
        ),
        out_specs=(
            rows,
            rows,
            P(),
            P(),
            P(),
            columns,
            columns,
            columns,
            split_rows,
            P(),
            P(),
            P(),
            columns,
            P("head"),
            split_rows,
            P(),
        ),
        check_vma=False,
    )
```

```python
import functools
import math

import jax
import jax.numpy as jnp
from jax import lax
from jax.experimental import pallas as pl
from jax.experimental.pallas import tpu as pltpu
from jax.sharding import Mesh, PartitionSpec as P

HD = 64
F32 = jnp.float32
BF16 = jnp.bfloat16
eps = 1e-05
masked_value = -1e30
seg_row = 3 * HD
payload_rows = 3 * HD + 16
small_rows = 16
params = pltpu.CompilerParams(vmem_limit_bytes=48 * 2**20)
streaming = pltpu.CompilerParams(vmem_limit_bytes=63_400_000)


def normalize(values):
    centred = values - jnp.mean(values, axis=-1, keepdims=True)
    inverse = lax.rsqrt(jnp.mean(centred * centred, axis=-1, keepdims=True) + eps)
    return (centred * inverse, inverse)


def normalize_back(grad_unit, unit, inverse):
    return inverse * (
        grad_unit
        - jnp.mean(grad_unit, axis=-1, keepdims=True)
        - unit * jnp.mean(grad_unit * unit, axis=-1, keepdims=True)
    )


def product(first, second, first_axis=1, second_axis=0):
    return lax.dot_general(
        first,
        second,
        (((first_axis,), (second_axis,)), ((), ())),
        preferred_element_type=jnp.float32,
    )


def struct(shape, dtype):
    return jax.ShapeDtypeStruct(shape, dtype)


def whole_spec(shape):
    return pl.BlockSpec(shape, lambda *at: (0,) * len(shape))


light = pl.CostEstimate(flops=1, bytes_accessed=1, transcendentals=0)


def project_kernel(
    table, input_ref, segment_ref, steps_ref, gain, shift, lead_weight, *refs
):
    weights, (payload_ref, attn_in_ref, cut_ref) = refs[:3], refs[3:]
    rows = input_ref.shape[0]

    @pl.when(pl.program_id(0) == 0)
    def _():
        unit, _ = normalize(input_ref[...].astype(F32))
        crops = steps_ref.shape[0]
        crop = lax.broadcasted_iota(jnp.int32, (crops, rows), 0)
        steps = jnp.zeros((crops, rows), jnp.int32)
        for at in range(crops):
            steps = jnp.where(crop == at, steps_ref[at], steps)
        steps = jnp.where(crop == segment_ref[...], steps, 0).astype(F32)
        lead = product(steps, jnp.ones((crops, 128), F32), 0, 0)[:, :1] / 12.0
        attn_in = unit * gain[...] + shift[...] + lead * lead_weight[...]
        attn_in = attn_in.astype(BF16)
        attn_in_ref[...] = attn_in
        columns = cut_ref.shape[1]
        first = table[table.shape[0] - 1] % (attn_in.shape[1] // columns) == 0
        cut_ref[...] = jnp.where(first, attn_in[:, :columns], attn_in[:, -columns:])

    for at, weight in enumerate(weights):
        part = product(attn_in_ref[...], weight[...]).T.astype(BF16)
        for head in range(2):
            payload_ref[head, pl.ds(at * HD, HD), :] = part[head * HD : head * HD + HD]
    segment = jnp.broadcast_to(segment_ref[...].astype(F32), (16, rows)).astype(BF16)
    for head in range(2):
        payload_ref[head, pl.ds(seg_row, 16), :] = segment


def project(table, cut, block_input, segments, lead_steps, gain, shift, lead_weight, weights):
    rows, model = block_input.shape
    heads = weights[0].shape[1] // HD
    line = whole_spec((1, model))
    column = pl.BlockSpec((model, 2 * HD), lambda at, table: (0, at))
    return pl.pallas_call(
        project_kernel,
        grid_spec=pltpu.PrefetchScalarGridSpec(
            num_scalar_prefetch=1,
            grid=(heads // 2,),
            in_specs=[
                whole_spec(block_input.shape),
                whole_spec((1, rows)),
                pl.BlockSpec(memory_space=pltpu.SMEM),
            ]
            + [line] * 3
            + [column] * 3,
            out_specs=[
                pl.BlockSpec((2, payload_rows, rows), lambda at, table: (at, 0, 0)),
                whole_spec((rows, model)),
                whole_spec((rows, cut)),
            ],
        ),
        out_shape=[
            struct((heads, payload_rows, rows), BF16),
            struct((rows, model), BF16),
            struct((rows, cut), BF16),
        ],
        compiler_params=streaming,
        cost_estimate=light,
        name="project",
    )(table, block_input, segments[None], lead_steps, gain[None], shift[None], lead_weight[None], *weights)


def mlp_kernel(count, core_ref, input_ref, grad_ref, *refs):
    branches, refs = refs[:count], refs[count:]
    output_bias, gain, shift, up_weight, up_bias, down_weight = refs[:6]
    keep_ref, give_ref, keep_in_ref, give_in_ref, hidden_ref, bias_ref, forward_ref, back_ref = refs[
        6:14
    ]
    mlp_in_ref, forward, back = refs[14:]
    at = pl.program_id(0)
    is_down = core_ref[core_ref.shape[0] - 2] == 0

    @pl.when(at == 0)
    def _():
        hidden = input_ref[...].astype(F32) + output_bias[...]
        for branch in branches:
            hidden += branch[...].astype(F32)
        hidden_ref[...] = hidden
        unit, _ = normalize(hidden)
        mlp_in = (unit * gain[...] + shift[...]).astype(BF16)
        mlp_in_ref[...] = mlp_in
        keep_in_ref[...] = jnp.where(is_down, grad_ref[...], mlp_in)
        give_in_ref[...] = jnp.where(is_down, mlp_in, grad_ref[...])
        forward[...] = jnp.zeros_like(forward)
        back[...] = jnp.zeros_like(back)

    upper = product(mlp_in_ref[...], up_weight[...]) + up_bias[...]
    share = 0.5 + 0.5 * lax.erf(upper * math.sqrt(0.5))
    slope = share + upper * (jnp.exp(upper * upper * -0.5) * (1.0 / math.sqrt(2.0 * math.pi)))
    active = (upper * share).astype(BF16)
    d_active = product(grad_ref[...], down_weight[...], 1, 1)
    d_upper = (d_active * slope).astype(BF16)
    keep_ref[...] = jnp.where(is_down, active, d_upper)
    give_ref[...] = jnp.where(is_down, d_upper, active)
    bias_ref[...] = jnp.sum(d_upper.astype(F32), axis=0, keepdims=True)
    forward[...] += product(active, down_weight[...])
    back[...] += product(d_upper, up_weight[...], 1, 1)

    @pl.when(at == pl.num_programs(0) - 1)
    def _():
        forward_ref[...] = forward[...].astype(BF16)
        back_ref[...] = back[...].astype(BF16)


def mlp(
    table, block_input, out_grad, branches, output_bias, gain, shift, up_weight, up_bias, down_weight
):
    rows, model = block_input.shape
    units = up_weight.shape[1]
    step = math.gcd(units, 512)
    tile, line = whole_spec((rows, model)), whole_spec((1, model))
    wide = pl.BlockSpec((rows, step), lambda at, table: (0, at))
    bias = pl.BlockSpec((1, step), lambda at, table: (0, at))
    return pl.pallas_call(
        functools.partial(mlp_kernel, len(branches)),
        grid_spec=pltpu.PrefetchScalarGridSpec(
            num_scalar_prefetch=1,
            grid=(units // step,),
            in_specs=[tile] * (2 + len(branches))
            + [line] * 3
            + [
                pl.BlockSpec((model, step), lambda at, table: (0, at)),
                bias,
                pl.BlockSpec((step, model), lambda at, table: (at, 0)),
            ],
            out_specs=[wide, wide, tile, tile, tile, bias, tile, tile],
            scratch_shapes=[pltpu.VMEM((rows, model), BF16)]
            + [pltpu.VMEM((rows, model), F32)] * 2,
        ),
        out_shape=[struct((rows, units), BF16)] * 2
        + [struct((rows, model), BF16)] * 2
        + [
            struct((rows, model), F32),
            struct((1, units), F32),
            struct((rows, model), BF16),
            struct((rows, model), BF16),
        ],
        compiler_params=streaming,
        cost_estimate=light,
        name="mlp",
    )(
        table,
        block_input,
        out_grad,
        *branches,
        output_bias[None],
        gain[None],
        shift[None],
        up_weight,
        up_bias[None],
        down_weight,
    )


def middle_kernel(count, hidden_ref, grad_ref, *refs):
    parts, refs = refs[:count], refs[count:]
    gain, output_weight, d_hidden_ref, d_branch_ref, d_attn_ref, sums_ref = refs
    unit, inverse = normalize(hidden_ref[...])
    d_mlp = parts[0][...].astype(F32)
    for part in parts[1:]:
        d_mlp += part[...].astype(F32)
    grad = grad_ref[...].astype(F32)
    d_hidden = grad + normalize_back(d_mlp * gain[...], unit, inverse)
    d_hidden_ref[...] = d_hidden
    d_branch = d_hidden.astype(BF16)
    d_branch_ref[...] = d_branch
    d_attn_ref[...] = product(output_weight[...], d_branch, 1, 1).astype(BF16)
    for at, values in enumerate((d_hidden, d_mlp * unit, d_mlp, grad)):
        sums_ref[pl.ds(at, 1), :] = jnp.sum(values, axis=0, keepdims=True)


def middle(hidden, out_grad, parts, gain, output_weight):
    rows, model = hidden.shape
    width = output_weight.shape[0]
    return pl.pallas_call(
        functools.partial(middle_kernel, len(parts)),
        out_shape=[
            struct((rows, model), F32),
            struct((rows, model), BF16),
            struct((width, rows), BF16),
            struct((4, model), F32),
        ],
        compiler_params=streaming,
        cost_estimate=light,
        name="middle",
    )(hidden, out_grad, *parts, gain[None], output_weight)


def mask_rows(piece, chip, crops):
    crop = lax.broadcasted_iota(jnp.int32, (HD, piece.shape[2]), 0)
    segment = piece[chip, pl.ds(seg_row, 16), :].astype(F32)[:1].astype(jnp.int32)
    return jnp.where((crop != segment) & (crop < crops), masked_value, 0.0)


def load_keys(piece, crops, keys, key_t, value_n):
    chips, _, patches = piece.shape
    for chip in range(chips):
        key = piece[chip, pl.ds(HD, HD), :]
        value = piece[chip, pl.ds(2 * HD, HD), :]
        place = pl.ds(chip * patches, patches)
        both = jnp.concatenate([key.astype(F32), mask_rows(piece, chip, crops)], axis=0)
        keys[place, :] = both.T.astype(BF16)
        key_t[:, place] = key
        value_n[place, :] = value.astype(F32).T.astype(BF16)


def masked_query(query_ref, dtype=BF16):
    query = query_ref[0, pl.ds(0, HD), :].astype(F32) * 0.125
    segment = query_ref[0, pl.ds(seg_row, 16), :].astype(F32)[:1].astype(jnp.int32)
    crop = lax.broadcasted_iota(jnp.int32, query.shape, 0)
    onehot = jnp.where(crop == segment, 1.0, 0.0)
    return jnp.concatenate([query, onehot], axis=0).astype(dtype)


def forward_kernel(
    crops, step, query_ref, own, other, raw_ref, out_ref, logsum_ref, key_t, value_n, scores
):
    @pl.when(pl.program_id(0) == 0)
    def _():
        start = 0
        for piece in (own, other):
            chips, _, patches = piece.shape
            for chip in range(chips):
                place = pl.ds(start, patches)
                key = piece[chip, pl.ds(HD, HD), :].astype(F32)
                key_t[:, place] = jnp.concatenate([key, mask_rows(piece, chip, crops)], axis=0).astype(BF16)
                value = piece[chip, pl.ds(2 * HD, HD), :].astype(F32)
                value = jnp.concatenate([value, jnp.ones_like(value)], axis=0)
                value_n[place, :] = value.T.astype(BF16)
                start += patches

    query = masked_query(query_ref, F32).T.astype(BF16)
    count = query.shape[0]
    top = jnp.full((count, 128), masked_value, F32)
    for start in range(0, key_t.shape[1], step):
        block = product(query, key_t[:, pl.ds(start, step)])
        scores[:, pl.ds(start, step)] = block
        for at in range(0, step, 128):
            top = jnp.maximum(top, block[:, at : at + 128])
    top = jnp.max(top, axis=1, keepdims=True)
    accum = jnp.zeros((count, 2 * HD), F32)
    for start in range(0, key_t.shape[1], step):
        weights = jnp.exp(scores[:, pl.ds(start, step)] - top).astype(BF16)
        accum += product(weights, value_n[pl.ds(start, step), :])
    accum = accum.T
    total = accum[HD : HD + 1]
    raw = accum[:HD] / total
    raw_ref[0] = raw
    out_ref[0] = raw.astype(BF16)
    top = jnp.broadcast_to(top, (count, 128)).T[:1]
    logsum_ref[0] = top + jnp.log(total)


def backward_kernel(
    crops,
    extra,
    query_ref,
    grad_ref,
    raw_ref,
    logsum_ref,
    piece,
    *refs,
):
    extras, refs = refs[:extra], refs[extra:]
    outputs, (keys, key_t, value_n, sums) = refs[:-4], refs[-4:]
    group = pl.program_id(0)

    @pl.when(group == 0)
    def _():
        load_keys(piece, crops, keys, key_t, value_n)
        sums[...] = jnp.zeros_like(sums)

    query = masked_query(query_ref)
    grad = grad_ref[0]
    grad_wide = grad.astype(F32)
    delta = jnp.sum(grad_wide * raw_ref[0], axis=0, keepdims=True)
    scaled = query_ref[0, pl.ds(0, HD), :].astype(F32) * 0.125
    zero = jnp.zeros_like(scaled)
    query_side = jnp.concatenate([scaled, zero], axis=0).T.astype(BF16)
    grad_side = jnp.concatenate([zero, grad_wide], axis=0).T.astype(BF16)
    probs = jnp.exp(product(keys[...], query) - logsum_ref[0])
    dprobs = product(value_n[...], grad)
    dscores = (probs * (dprobs - delta)).astype(BF16)
    sums[...] += product(dscores, query_side) + product(probs.astype(BF16), grad_side)
    dquery = product(key_t[...], dscores) * 0.125
    if extras:
        dquery += extras[0][0]
    if len(outputs) == 1:
        outputs[0][group, pl.ds(0, HD), :] = dquery.astype(BF16)
    else:
        outputs[0][0] = dquery.astype(outputs[0].dtype)

    @pl.when(group == pl.num_programs(0) - 1)
    def _():
        chips, _, patches = piece.shape
        for chip in range(chips):
            total = sums[pl.ds(chip * patches, patches), :].T
            if extra > 1:
                total += extras[1][chip].astype(F32)
            total = total.astype(BF16)
            if len(outputs) == 1:
                outputs[0][chip, pl.ds(HD, 2 * HD), :] = total
            else:
                outputs[1][chip] = total


def key_step(count):
    return 1024 if count % 1024 == 0 else 256


def query_spec(rows, patches):
    return pl.BlockSpec((1, rows, patches), lambda group: (group, 0, 0))


def attention_forward(queries, own, other, crops):
    groups, _, patches = queries.shape
    count = 2 * own.shape[0] * own.shape[2]
    return pl.pallas_call(
        functools.partial(forward_kernel, crops, key_step(count)),
        grid=(groups,),
        in_specs=[
            query_spec(payload_rows, patches),
            whole_spec(own.shape),
            whole_spec(other.shape),
        ],
        out_specs=[query_spec(HD, patches), query_spec(HD, patches), query_spec(1, patches)],
        out_shape=[
            struct((groups, HD, patches), F32),
            struct((groups, HD, patches), BF16),
            struct((groups, 1, patches), F32),
        ],
        scratch_shapes=[
            pltpu.VMEM((2 * HD, count), BF16),
            pltpu.VMEM((count, 2 * HD), BF16),
            pltpu.VMEM((patches, count), F32),
        ],
        compiler_params=streaming,
        cost_estimate=light,
        name="attention_forward",
    )(queries, own, other)


def attention_backward(queries, grads, raw, logsum, keys, extras, crops):
    groups, _, patches = queries.shape
    chips, count = keys.shape[0], keys.shape[0] * keys.shape[2]
    sums_shape = (chips, 2 * HD, keys.shape[2])
    specs = [query_spec(HD, patches), whole_spec(sums_shape)]
    shapes = [
        struct((groups, HD, patches), BF16 if extras else F32),
        struct(sums_shape, BF16),
    ]
    outs = specs
    if extras and (groups, patches) == (chips, keys.shape[2]):
        shapes = [struct((chips, 3 * HD, patches), BF16)]
        outs = [whole_spec(shapes[0].shape)]
    return pl.pallas_call(
        functools.partial(backward_kernel, crops, len(extras)),
        grid=(groups,),
        in_specs=[
            query_spec(payload_rows, patches),
            query_spec(HD, patches),
            query_spec(HD, patches),
            query_spec(1, patches),
            whole_spec(keys.shape),
        ]
        + specs[: len(extras)],
        out_specs=outs,
        out_shape=shapes,
        scratch_shapes=[
            pltpu.VMEM((count, 2 * HD), BF16),
            pltpu.VMEM((HD, count), BF16),
            pltpu.VMEM((count, HD), BF16),
            pltpu.VMEM((count, 2 * HD), F32),
        ],
        compiler_params=params,
        cost_estimate=light,
        name="attention_backward",
    )(queries, grads, raw, logsum, keys, *extras)


def swap_cores(values):
    return lax.ppermute(values, "core", [(0, 1), (1, 0)])


def to_heads(blocks):
    return lax.all_to_all(blocks, "chip", 0, 0, tiled=True)


def scatter_queries(values, heads, split):
    rows, patches = values.shape[0] // heads, values.shape[1]
    if split == 1:
        return to_heads(values.reshape(heads, rows, patches))
    part = patches // split
    blocks = values.reshape(heads, rows, split, part).transpose(0, 2, 1, 3)
    moved = to_heads(blocks.reshape(heads * split, rows, part))
    width = min(256, moved.shape[0] * part)
    joined = moved.transpose(1, 0, 2).reshape(rows, -1, width)
    return joined.transpose(1, 0, 2)


def gather_queries(values, heads, split, patches):
    rows = values.shape[1]
    if split == 1:
        return to_heads(values).reshape(heads * rows, patches)
    part = patches // split
    joined = values.transpose(1, 0, 2).reshape(rows, heads * split, part)
    moved = to_heads(joined.transpose(1, 0, 2)).reshape(heads, split, rows, part)
    return moved.transpose(0, 2, 1, 3).reshape(heads * rows, patches)


def across_heads(part):
    if lax.axis_size("head") == 2:
        return [part, lax.ppermute(part, "head", [(0, 1), (1, 0)])]
    return [lax.psum(part, "head")]


def ring_pairs(direction):
    chips = lax.axis_size("chip")
    order = list(range(0, chips, 2)) + list(range(chips - 1, 0, -2))
    return [(order[at], order[(at + direction) % chips]) for at in range(chips)]


def ring_table():
    chips, chip = lax.axis_size("chip"), lax.axis_index("chip")
    place = jnp.where(chip % 2 == 0, chip // 2, chips - 1 - chip // 2)
    steps = jnp.arange(2 * chips + 2, dtype=jnp.int32)
    places = (place + steps) % chips
    there = jnp.where(places < chips // 2, 2 * places, 2 * (chips - 1 - places) + 1)
    table = jnp.where(steps < chips, places, there)
    table = jnp.where(steps == 2 * chips, lax.axis_index("core"), table)
    return jnp.where(steps == 2 * chips + 1, lax.axis_index("head"), table).astype(jnp.int32)


def visit(streams, values):
    states, values = lax.optimization_barrier(([stream.state for stream in streams], values))
    for stream, state in zip(streams, states):
        stream.advance(state)
    ready, values = lax.optimization_barrier(([stream.ready for stream in streams], values))
    for stream, blocks in zip(streams, ready):
        stream.send(blocks)
    return values


def pieces_of(block):
    return list(block) if isinstance(block, tuple) else [block]


def whole_block(block):
    return jnp.concatenate(pieces_of(block), axis=1)


def join_kernel(counts, *refs):
    output, refs, start = refs[-1], list(refs[:-1]), 0
    for count in counts:
        column = 0
        for _ in range(count):
            piece = refs.pop(0)
            rows, columns = piece.shape
            output[pl.ds(start, rows), pl.ds(column, columns)] = piece[...]
            column += columns
        start += rows


def join(blocks):
    blocks = [pieces_of(block) for block in blocks]
    rows = sum(block[0].shape[0] for block in blocks)
    columns = sum(piece.shape[1] for piece in blocks[0])
    return pl.pallas_call(
        functools.partial(join_kernel, [len(block) for block in blocks]),
        out_shape=struct((rows, columns), blocks[0][0].dtype),
        compiler_params=streaming,
        name="join",
    )(*[piece for block in blocks for piece in block])


def halves_kernel(left, right, left_ref, right_ref):
    left_ref[...] = left[...]
    right_ref[...] = right[...]


def halves(left, right):
    rows, columns = left.shape
    if rows % 16 or columns % 256:
        return [left[:, : columns // 2], right[:, columns // 2 :]]
    out = pl.BlockSpec((rows, columns // 2), lambda at: (0, 0))
    return pl.pallas_call(
        halves_kernel,
        grid=(1,),
        in_specs=[out, pl.BlockSpec((rows, columns // 2), lambda at: (0, 1))],
        out_specs=[out, out],
        out_shape=[struct((rows, columns // 2), left.dtype)] * 2,
        compiler_params=streaming,
        name="halves",
    )(left, right)


class Gather:
    def __init__(self, block, swap=False, take=None):
        self.reach, self.swap, self.take = lax.axis_size("chip") // 2, swap, take
        self.blocks, self.pairs, self.count = [], [], 0
        self.new, self.outputs = [0], []
        self.ready = [block]

    def send(self, ready):
        if len(self.new) < len(ready):
            ready = [tuple(ready)]
        new = list(zip(self.new, ready))
        self.blocks += new
        self.new = new
        self.count += 1
        sides = ready if len(ready) > 1 else ready * 2
        if self.count == self.reach:
            sides = halves(*sides)
        flying = []
        if self.count <= self.reach:
            flying = [
                lax.ppermute(block, "chip", ring_pairs(direction))
                for block, direction in zip(sides, (1, -1))
            ]
        if self.swap and ready:
            pairs = [(step, block, jax.tree.map(swap_cores, block)) for step, block in new]
            self.pairs += pairs
            self.outputs = self.take(self.outputs, pairs)
        self.state = (flying, self.outputs)

    def advance(self, state):
        arrived, self.outputs = state
        self.new = [-self.count, self.count]
        if self.count == self.reach:
            self.new = [self.count]
        self.ready = arrived

    def busy(self):
        return bool(self.state[0])


def add_kernel(wanted, count, _, *refs):
    outputs, refs = refs[-count:], list(refs[:-count])
    keep_in, far_in = refs.pop(0), refs.pop(0)
    at = pl.program_id(0)

    def put(output, total):
        output[...] = total.astype(BF16)

    for places, output in zip(wanted, outputs):
        near, far = refs.pop(0), refs.pop(0)
        total = product(near[...], keep_in[...], 0, 0) + product(far[...], far_in[...], 0, 0)
        arrived = [(place, refs.pop(0)) for place in places]
        if count > len(wanted):
            for place in range(count):
                pl.when(at == place)(functools.partial(put, outputs[place], total))
            return
        for place, part in arrived:
            if place is None:
                total += part[...].astype(F32)
        put(output, total)
        for place, part in arrived:
            if place is not None:
                pl.when(at == place)(lambda: put(output, total + part[...].astype(F32)))


def finish_kernel(counts, _, keep_in, far_in, near, far, ahead, behind, *refs):
    refs, output = list(refs[:-1]), refs[-1]
    total = product(near[...], keep_in[...], 0, 0) + product(far[...], far_in[...], 0, 0)
    total += ahead[...].astype(F32) + behind[...].astype(F32)
    start = total.shape[0]
    output[pl.ds(0, start), :] = total.astype(BF16)
    for count in counts:
        total = 0.0
        for _ in range(count):
            part = refs.pop(0)[...].astype(F32)
            total += part if part.ndim == 2 else jnp.sum(part, axis=0)
        output[pl.ds(start, total.shape[0]), :] = total.astype(BF16)
        start += total.shape[0]


class Reduce:
    def __init__(self, keep, far, keep_in, far_in, table):
        self.chips, self.table = lax.axis_size("chip"), table
        self.operands, self.sides = (keep, far), (keep_in, far_in)
        self.units = keep.shape[1] // self.chips
        self.tiled = self.units % 128 == 0
        self.left, self.rest = self.chips // 2, None
        blocks = self.add([(self.left, [])], True)
        self.send(blocks if len(blocks) > 1 else halves(blocks[0], blocks[0]))

    def send(self, ready):
        self.left -= 1
        self.state = [
            lax.ppermute(block, "chip", ring_pairs(direction))
            for block, direction in zip(ready, (1, -1))
        ]

    def advance(self, state):
        half = self.sides[0].shape[1] // 2
        ahead, behind = state
        places = (0, 1) if ahead.shape[1] == half else (None, None)
        self.ready = self.add(
            [(self.left, [(ahead, places[0])]), (-self.left, [(behind, places[1])])]
        )

    def arrive(self, values):
        self.state, values = lax.optimization_barrier((self.state, values))
        return values

    def finish(self, below):
        ahead, behind = self.state
        if not self.tiled:
            rows = self.add([(0, [(ahead, None), (behind, None)])])
            for parts in below:
                total = jnp.zeros(parts[0].shape[-2:], F32)
                for part in parts:
                    part = part.astype(F32)
                    total += part if part.ndim == 2 else jnp.sum(part, axis=0)
                rows.append(total.astype(BF16))
            return jnp.concatenate(rows, axis=0)
        (rows, model), units, chips = self.sides[0].shape, self.units, self.chips
        half = model // 2
        arrays = [ahead, behind] + [part for parts in below for part in parts]
        specs = [pl.BlockSpec((rows, half), lambda at, table: (0, at))] * 2
        specs += [pl.BlockSpec((rows, units), lambda at, table: (0, table[0]))] * 2
        for array in arrays:
            shape = array.shape[:-1] + (half,)
            specs.append(
                pl.BlockSpec(shape, lambda at, table, rank=array.ndim: (0,) * (rank - 1) + (at,))
            )
        height = units + sum(parts[0].shape[-2] for parts in below)
        return pl.pallas_call(
            functools.partial(finish_kernel, [len(parts) for parts in below]),
            grid_spec=pltpu.PrefetchScalarGridSpec(
                num_scalar_prefetch=1,
                grid=(2,),
                in_specs=specs,
                out_specs=pl.BlockSpec((height, half), lambda at, table: (0, at)),
            ),
            out_shape=struct((height, model), BF16),
            compiler_params=streaming,
            cost_estimate=light,
            name="ring_finish",
        )(self.table, *self.sides, *self.operands, *arrays)

    def add(self, wanted, split=False):
        (rows, model), units, chips = self.sides[0].shape, self.units, self.chips
        if not self.tiled:
            sums = []
            for step, parts in wanted:
                start = self.table[step % chips] * units
                total = jnp.zeros((units, model), F32)
                for operand, side in zip(self.operands, self.sides):
                    block = lax.dynamic_slice_in_dim(operand, start, units, 1)
                    total += product(block, side, 0, 0)
                for part, place in parts:
                    start = (place or 0) * part.shape[1]
                    total = total.at[:, start : start + part.shape[1]].add(part.astype(F32))
                sums.append(total.astype(BF16))
            return sums
        half = model // 2
        side = pl.BlockSpec((rows, half), lambda at, table: (0, at))
        whole = pl.BlockSpec((units, half), lambda at, table: (0, at))
        fixed = pl.BlockSpec((units, half), lambda at, table: (0, 0))
        specs, arrays = [side] * 2, list(self.sides)
        for step, parts in wanted:
            block = pl.BlockSpec(
                (rows, units), lambda at, table, step=step % chips: (0, table[step])
            )
            specs += [block] * 2 + [whole if place is None else fixed for _, place in parts]
            arrays += list(self.operands) + [part for part, _ in parts]
        places = [[place for _, place in parts] for _, parts in wanted]
        shapes, outs = [struct((units, model), BF16)] * len(wanted), [whole] * len(wanted)
        if split:
            shapes, outs = [struct((units, half), BF16)] * 2, [fixed] * 2
        return pl.pallas_call(
            functools.partial(add_kernel, places, len(shapes)),
            grid_spec=pltpu.PrefetchScalarGridSpec(
                num_scalar_prefetch=1,
                grid=(2,),
                in_specs=specs,
                out_specs=outs,
            ),
            out_shape=shapes,
            compiler_params=streaming,
            cost_estimate=light,
            name="ring_add",
        )(self.table, *arrays)

    def place(self, outputs, pairs):
        units, chips, model = self.units, self.chips, self.sides[0].shape[1]
        size, extra = self.size, self.extra
        shapes = [struct((chips * units, model), F32), struct((model, chips * units), F32)]
        if not self.tiled:
            outputs = outputs or [jnp.zeros(shape.shape, F32) for shape in shapes]
            down, up = outputs
            is_down = self.table[2 * chips] == 0
            for step, near, far in pairs:
                start = self.table[step % chips] * units
                near, far = whole_block(near)[:units], whole_block(far)[:units]
                first = jnp.where(is_down, near, far).astype(F32)
                second = jnp.where(is_down, far, near).astype(F32).T
                down = lax.dynamic_update_slice_in_dim(down, first, start, 0)
                up = lax.dynamic_update_slice_in_dim(up, second, start, 1)
            return [down, up]
        first = pairs[0][0] % chips
        stride = pairs[-1][0] % chips - first
        blocks = [pieces_of(pair[1]) + pieces_of(pair[2]) for pair in pairs]
        flat = [piece for block in blocks for piece in block]

        def place(at, table):
            return table[first + at * stride]

        def chip(at, table):
            return table[chips + first + at * stride]

        column = pl.BlockSpec(
            (model, 2 * HD), lambda at, table: (0, lax.div(chip(at, table), 2))
        )
        columns = [column] * (3 if outputs else 0)
        heads = [[first, first + stride][at] + chips for at in range(len(pairs))]
        return pl.pallas_call(
            functools.partial(place_kernel, heads, len(blocks[0]) // 2, (units, size, extra)),
            grid_spec=pltpu.PrefetchScalarGridSpec(
                num_scalar_prefetch=1,
                grid=(len(pairs),),
                in_specs=[pl.BlockSpec(memory_space=pl.ANY)] * (len(outputs) - len(columns))
                + columns
                + [pl.BlockSpec(piece.shape, lambda at, table: (0, 0)) for piece in flat],
                out_specs=[
                    pl.BlockSpec((units, model), lambda at, table: (place(at, table), 0)),
                    pl.BlockSpec((model, units), lambda at, table: (0, place(at, table))),
                    pl.BlockSpec((2, 1, extra, model), lambda at, table: (0, chip(at, table), 0, 0)),
                    pl.BlockSpec(
                        (1, 2, small_rows, model), lambda at, table: (chip(at, table), 0, 0, 0)
                    ),
                ]
                + [column] * 3,
            ),
            out_shape=shapes
            + [
                struct((2, chips, extra, model), F32),
                struct((chips, 2, small_rows, model), F32),
            ]
            + [struct((model, chips * HD), F32)] * 3,
            input_output_aliases={1 + at: at for at in range(len(outputs))},
            compiler_params=streaming,
            cost_estimate=light,
            name="place",
        )(self.table, *outputs, *flat)


def place_kernel(heads, width, sizes, table, *refs):
    count = len(heads)
    refs, (down, up, weight, small), projections = refs[:-7], refs[-7:-3], refs[-3:]
    blocks, refs = refs[-2 * width * count :], refs[: -2 * width * count]
    core = table[table.shape[0] - 2]
    units, size, extra = sizes
    rows = [pl.ds(0, units), pl.ds(units, size), pl.ds(units + size, extra)]
    rows.append(pl.ds(units + size + extra, small_rows))

    def read(block, which):
        return jnp.concatenate([piece[rows[which], :] for piece in block], axis=1)

    def put(first, second, head):
        down[...] = read(first, 0).astype(F32)
        up[...] = read(second, 0).astype(F32).T
        for side, block in ((0, first), (1, second)):
            weight[side, 0] = read(block, 2).astype(F32)
            small[0, side] = read(block, 3).astype(F32)
        both = jnp.concatenate([read(first, 1), read(second, 1)], axis=0)
        for at, output in enumerate(projections):
            part = both[at * HD : at * HD + HD].astype(F32)
            part = jnp.concatenate([part, part], axis=0).T
            if refs:
                mine = lax.broadcasted_iota(jnp.int32, part.shape, 1) // HD == head % 2
                part = jnp.where(mine, part, refs[at - 3][...])
            output[...] = part

    for at in range(count):
        near, far = (
            blocks[(2 * at + side) * width : (2 * at + side + 1) * width] for side in range(2)
        )
        head = table[heads[at]]
        here = pl.program_id(0) == at
        pl.when(here & (core == 0))(functools.partial(put, near, far, head))
        pl.when(here & (core != 0))(functools.partial(put, far, near, head))


def head_gradient_kernel(steps, chips, table, grads_ref, *refs):
    parts, out_ref = refs[:-1], refs[-1]
    for at, part in enumerate(parts):

        @pl.when(pl.program_id(0) == at)
        def _(part=part):
            chosen = [grads_ref[table[chips + step % chips]] for step in steps]
            total = product(jnp.concatenate(chosen, axis=1), part[...])
            out_ref[...] = total.astype(BF16)


def head_gradient(grads, parts, steps, table):
    chips, rows, _ = grads.shape
    columns = parts[0].shape[1]

    def column(at, table):
        mine = table[2 * chips + 1] if len(parts) > 1 else 0
        return (0, jnp.where(at == 0, mine, 1 - mine))

    return pl.pallas_call(
        functools.partial(head_gradient_kernel, steps, chips),
        grid_spec=pltpu.PrefetchScalarGridSpec(
            num_scalar_prefetch=1,
            grid=(len(parts),),
            in_specs=[
                pl.BlockSpec(array.shape, lambda at, table, rank=array.ndim: (0,) * rank)
                for array in (grads, *parts)
            ],
            out_specs=pl.BlockSpec((rows, columns), column),
        ),
        out_shape=struct((rows, columns * len(parts)), BF16),
        compiler_params=streaming,
        cost_estimate=light,
        name="head_gradient",
    )(table, grads, *parts)


def core_half(values, axis, side):
    size = values.shape[axis] // 2
    return lax.dynamic_slice_in_dim(values, side * size, size, axis)


def share_halves(values, axis):
    core = lax.axis_index("core")
    return core_half(values, axis, core), swap_cores(core_half(values, axis, 1 - core))


def local(
    block_input,
    out_grad,
    segments,
    lead_steps,
    gain_attn,
    shift_attn,
    lead_weight,
    query_weight,
    key_weight,
    value_weight,
    output_weight,
    output_bias,
    gain_mlp,
    shift_mlp,
    up_weight,
    up_bias,
    down_weight,
    down_bias,
):
    rows, model = block_input.shape
    heads = query_weight.shape[1] // HD
    width = heads * HD
    chips, core = lax.axis_size("chip"), lax.axis_index("core")
    split = chips // heads
    crops = lead_steps.shape[0]
    table = ring_table()
    weights = (query_weight, key_weight, value_weight)
    cut = model // 2 if lax.axis_size("head") == 2 else model
    payload, attn_in, attn_in_cut = project(
        table, cut, block_input, segments, lead_steps, gain_attn, shift_attn, lead_weight, weights
    )
    if split == 1:
        own = to_heads(payload)
        queries = own
    else:
        queries = scatter_queries(payload.reshape(-1, rows), heads, split)
        own = to_heads(jnp.repeat(payload, split, axis=0))
    own, attn_in_cut = lax.optimization_barrier((own, attn_in_cut))
    inputs = Gather(attn_in_cut)
    inputs.send(inputs.ready)
    other = swap_cores(own)
    raw, out, logsum = attention_forward(queries, own, other, crops)
    inputs.state, out = lax.optimization_barrier((inputs.state, out))
    attn_out = gather_queries(out, heads, split, rows)
    attn_out = visit([inputs], attn_out)
    branches = across_heads(product(attn_out, output_weight, 0, 0).astype(BF16))
    wide = block_input.astype(F32)
    mean_attn = jnp.mean(wide, axis=-1, keepdims=True)
    centred = wide - mean_attn
    inverse_attn = lax.rsqrt(jnp.mean(centred * centred, axis=-1, keepdims=True) + eps)
    mean_attn, inverse_attn = visit([inputs], (mean_attn, inverse_attn))
    keep, give, keep_in, give_in, hidden, dup_bias, mlp_part, d_mlp_part = mlp(
        table,
        block_input,
        out_grad,
        branches,
        output_bias,
        gain_mlp,
        shift_mlp,
        up_weight,
        up_bias,
        down_weight,
    )
    keep, give, keep_in, give_in, d_mlp_part = visit(
        [inputs], (keep, give, keep_in, give_in, d_mlp_part)
    )
    d_mlp = across_heads(d_mlp_part)
    ring = Reduce(keep, swap_cores(give), keep_in, swap_cores(give_in), table)
    mlp_part, d_mlp = lax.optimization_barrier((mlp_part, d_mlp))
    d_hidden, d_branch, d_attn, sums = middle(hidden, out_grad, d_mlp, gain_mlp, output_weight)
    d_branch, mlp_part = visit([ring, inputs], (d_branch, mlp_part))
    while inputs.busy():
        visit([inputs], ())
    mlp_out = across_heads(mlp_part)
    out_near, out_far = share_halves(attn_out, 0)
    d_attn, d_branch_far = lax.optimization_barrier((d_attn, swap_cores(d_branch)))
    grads = scatter_queries(d_attn, heads, split)
    doutput = product(out_near, d_branch) + product(out_far, d_branch_far)
    doutput = doutput.astype(BF16).reshape(chips, -1, model)
    steps, inputs = zip(*inputs.blocks)
    inputs = join(inputs)
    parts = across_heads(inputs) if cut != model else [inputs]
    doutput = visit([ring], doutput)
    doutput = to_heads(doutput)
    dquery, far_sums = attention_backward(queries, grads, raw, logsum, other, [], crops)
    far_sums = swap_cores(far_sums)
    grads, dquery = visit([ring], (grads, dquery))
    head_grads = attention_backward(
        queries, grads, raw, logsum, own, [dquery, far_sums], crops
    )
    head_grads = ring.arrive(head_grads)
    doutput, head_grads = lax.optimization_barrier((doutput, head_grads))
    small = jnp.concatenate([sums.reshape(-1), dup_bias[0]])
    small = jnp.pad(small, (0, small_rows * model - small.shape[0])).reshape(small_rows, model)
    below = [[doutput], [small]]
    if split == 1:
        (head_grads,) = head_grads
        moved = to_heads(head_grads)
        projections = head_gradient(head_grads, parts, steps, table)
        near, far = share_halves(projections, 0)
        size, below = near.shape[0], [[near, far]] + below
        dquery, dkey, dvalue = (
            moved[:, at * HD : at * HD + HD].reshape(width, rows) for at in range(3)
        )
    else:
        dquery, key_value = head_grads
        dquery = gather_queries(dquery, heads, split, rows)
        moved = to_heads(key_value).reshape(heads, split, 2 * HD, rows).astype(F32)
        moved = jnp.sum(moved, axis=1).astype(BF16)
        dkey, dvalue = (moved[:, at * HD : at * HD + HD].reshape(width, rows) for at in range(2))
        size = 0
        projections = [
            lax.psum(product(attn_in, grad, 0, 1).astype(BF16), ("chip", "core")).astype(F32)
            for grad in (dquery, dkey, dvalue)
        ]
    start, ring.size, ring.extra = ring.units, size, doutput.shape[1]
    gathered = Gather(ring.finish(below), True, ring.place)
    gathered.send(gathered.ready)
    d_part = (
        product(dquery, query_weight, 0, 1)
        + product(dkey, key_weight, 0, 1)
        + product(dvalue, value_weight, 0, 1)
    )
    d_in = across_heads(d_part.astype(BF16))
    unit_attn = (block_input.astype(F32) - mean_attn) * inverse_attn
    onehot = (segments[:, None] == jnp.arange(crops, dtype=jnp.int32)[None, :]).astype(F32)
    lead = jnp.sum(onehot * lead_steps.astype(F32)[None, :], axis=1) / 12.0
    ends = jnp.stack(
        [
            jnp.sum(d_part * unit_attn, axis=0),
            jnp.sum(d_part, axis=0),
            jnp.sum(lead[:, None] * d_part, axis=0),
        ]
    )
    ends = ends.reshape(-1, 128)
    ends = functools.reduce(jnp.add, across_heads(ends))
    ends = ends + swap_cores(ends)
    moves = [chips >> (at + 1) for at in range(chips.bit_length() - 1)][::-1]

    def step_ends(ends):
        if not moves:
            return [ends]
        reach = moves.pop(0)
        pairs = [(chip, chip ^ reach) for chip in range(chips)]
        return [ends, lax.ppermute(ends, "chip", pairs)]

    ends = visit([gathered], step_ends(ends))
    ends = step_ends(functools.reduce(jnp.add, ends))
    ends, mlp_out = visit([gathered], (ends, mlp_out))
    ends = step_ends(functools.reduce(jnp.add, ends))
    block_output = hidden + down_bias
    for part in mlp_out:
        block_output += part.astype(F32)
    block_output = block_output.astype(BF16)
    d_in, block_output, ends = visit([gathered], (d_in, block_output, ends))
    ends = step_ends(functools.reduce(jnp.add, ends))
    d_in = functools.reduce(jnp.add, (part.astype(F32) for part in d_in))
    input_grad = (d_hidden + normalize_back(d_in * gain_attn, unit_attn, inverse_attn)).astype(
        BF16
    )
    while gathered.busy() or moves:
        input_grad, ends = visit([gathered], (input_grad, ends))
        ends = step_ends(functools.reduce(jnp.add, ends))
    ends = functools.reduce(jnp.add, ends).reshape(3, model)
    ddown_weight, dup_weight, *rest = gathered.outputs
    if split == 1:
        doutput_weight, small, *projections = rest
        doutput_weight = doutput_weight.reshape(width, model)
    if split != 1:
        blocks = jnp.zeros((2, chips, ring.extra + small_rows, model), F32)
        for step, near, far in gathered.pairs:
            for side, block in ((core, near), (1 - core, far)):
                at = (side, table[chips + step % chips], 0, 0)
                block = whole_block(block)[None, None, start:].astype(F32)
                blocks = lax.dynamic_update_slice(blocks, block, at)
        doutput_weight = blocks[:, :, :-small_rows].reshape(width, model)
        small = blocks[:, :, -small_rows:]
    lines = 4 - (-dup_bias.shape[1] // model)
    small = jnp.sum(small[:, :, :lines], axis=(0, 1))
    dup_bias = small[4:].reshape(-1)[: dup_bias.shape[1]]
    return (
        block_output,
        input_grad,
        ends[0],
        ends[1],
        ends[2],
        *projections,
        doutput_weight,
        *small[:3],
        dup_weight,
        dup_bias,
        ddown_weight,
        small[3],
    )


def solution(mesh):
    bands, halves = mesh.shape["band"], mesh.shape["head"]
    inner = Mesh(mesh.devices.reshape(bands // 2, 2, halves), ("chip", "core", "head"))
    band = ("chip", "core")
    rows, columns, split_rows = P(band, None), P(None, "head"), P("head", None)
    return jax.shard_map(
        local,
        mesh=inner,
        in_specs=(
            rows,
            rows,
            P(band),
            P(),
            P(),
            P(),
            P(),
            columns,
            columns,
            columns,
            split_rows,
            P(),
            P(),
            P(),
            columns,
            P("head"),
            split_rows,
            P(),
        ),
        out_specs=(
            rows,
            rows,
            P(),
            P(),
            P(),
            columns,
            columns,
            columns,
            split_rows,
            P(),
            P(),
            P(),
            columns,
            P("head"),
            split_rows,
            P(),
        ),
        check_vma=False,
    )
```

```python
import functools
import math

import jax
import jax.numpy as jnp
from jax import lax
from jax.experimental import pallas as pl
from jax.experimental.pallas import tpu as pltpu
from jax.sharding import Mesh, PartitionSpec as P

HD = 64
F32 = jnp.float32
BF16 = jnp.bfloat16
eps = 1e-05
masked_value = -1e30
seg_row = 3 * HD
payload_rows = 3 * HD + 16
small_rows = 16
params = pltpu.CompilerParams(vmem_limit_bytes=48 * 2**20)
streaming = pltpu.CompilerParams(vmem_limit_bytes=63_400_000)


def normalize(values):
    centred = values - jnp.mean(values, axis=-1, keepdims=True)
    inverse = lax.rsqrt(jnp.mean(centred * centred, axis=-1, keepdims=True) + eps)
    return (centred * inverse, inverse)


def normalize_back(grad_unit, unit, inverse):
    return inverse * (
        grad_unit
        - jnp.mean(grad_unit, axis=-1, keepdims=True)
        - unit * jnp.mean(grad_unit * unit, axis=-1, keepdims=True)
    )


def product(first, second, first_axis=1, second_axis=0):
    return lax.dot_general(
        first,
        second,
        (((first_axis,), (second_axis,)), ((), ())),
        preferred_element_type=jnp.float32,
    )


def struct(shape, dtype):
    return jax.ShapeDtypeStruct(shape, dtype)


def whole_spec(shape):
    return pl.BlockSpec(shape, lambda *at: (0,) * len(shape))


light = pl.CostEstimate(flops=1, bytes_accessed=1, transcendentals=0)


def project_kernel(
    table, input_ref, segment_ref, steps_ref, gain, shift, lead_weight, *refs
):
    weights, (payload_ref, attn_in_ref, cut_ref) = refs[:3], refs[3:]
    rows = input_ref.shape[0]

    @pl.when(pl.program_id(0) == 0)
    def _():
        unit, _ = normalize(input_ref[...].astype(F32))
        crops = steps_ref.shape[0]
        crop = lax.broadcasted_iota(jnp.int32, (crops, rows), 0)
        steps = jnp.zeros((crops, rows), jnp.int32)
        for at in range(crops):
            steps = jnp.where(crop == at, steps_ref[at], steps)
        steps = jnp.where(crop == segment_ref[...], steps, 0).astype(F32)
        lead = product(steps, jnp.ones((crops, 128), F32), 0, 0)[:, :1] / 12.0
        attn_in = unit * gain[...] + shift[...] + lead * lead_weight[...]
        attn_in = attn_in.astype(BF16)
        attn_in_ref[...] = attn_in
        columns = cut_ref.shape[1]
        first = table[table.shape[0] - 1] % (attn_in.shape[1] // columns) == 0
        cut_ref[...] = jnp.where(first, attn_in[:, :columns], attn_in[:, -columns:])

    for at, weight in enumerate(weights):
        part = product(attn_in_ref[...], weight[...]).T.astype(BF16)
        for head in range(2):
            payload_ref[head, pl.ds(at * HD, HD), :] = part[head * HD : head * HD + HD]
    segment = jnp.broadcast_to(segment_ref[...].astype(F32), (16, rows)).astype(BF16)
    for head in range(2):
        payload_ref[head, pl.ds(seg_row, 16), :] = segment


def project(table, cut, block_input, segments, lead_steps, gain, shift, lead_weight, weights):
    rows, model = block_input.shape
    heads = weights[0].shape[1] // HD
    line = whole_spec((1, model))
    column = pl.BlockSpec((model, 2 * HD), lambda at, table: (0, at))
    return pl.pallas_call(
        project_kernel,
        grid_spec=pltpu.PrefetchScalarGridSpec(
            num_scalar_prefetch=1,
            grid=(heads // 2,),
            in_specs=[
                whole_spec(block_input.shape),
                whole_spec((1, rows)),
                pl.BlockSpec(memory_space=pltpu.SMEM),
            ]
            + [line] * 3
            + [column] * 3,
            out_specs=[
                pl.BlockSpec((2, payload_rows, rows), lambda at, table: (at, 0, 0)),
                whole_spec((rows, model)),
                whole_spec((rows, cut)),
            ],
        ),
        out_shape=[
            struct((heads, payload_rows, rows), BF16),
            struct((rows, model), BF16),
            struct((rows, cut), BF16),
        ],
        compiler_params=streaming,
        cost_estimate=light,
        name="project",
    )(table, block_input, segments[None], lead_steps, gain[None], shift[None], lead_weight[None], *weights)


def mlp_kernel(count, core_ref, input_ref, grad_ref, *refs):
    branches, refs = refs[:count], refs[count:]
    output_bias, gain, shift, up_weight, up_bias, down_weight = refs[:6]
    keep_ref, give_ref, keep_in_ref, give_in_ref, hidden_ref, bias_ref, forward_ref, back_ref = refs[
        6:14
    ]
    mlp_in_ref, forward, back = refs[14:]
    at = pl.program_id(0)
    is_down = core_ref[core_ref.shape[0] - 2] == 0

    @pl.when(at == 0)
    def _():
        hidden = input_ref[...].astype(F32) + output_bias[...]
        for branch in branches:
            hidden += branch[...].astype(F32)
        hidden_ref[...] = hidden
        unit, _ = normalize(hidden)
        mlp_in = (unit * gain[...] + shift[...]).astype(BF16)
        mlp_in_ref[...] = mlp_in
        keep_in_ref[...] = jnp.where(is_down, grad_ref[...], mlp_in)
        give_in_ref[...] = jnp.where(is_down, mlp_in, grad_ref[...])
        forward[...] = jnp.zeros_like(forward)
        back[...] = jnp.zeros_like(back)

    upper = product(mlp_in_ref[...], up_weight[...]) + up_bias[...]
    share = 0.5 + 0.5 * lax.erf(upper * math.sqrt(0.5))
    slope = share + upper * (jnp.exp(upper * upper * -0.5) * (1.0 / math.sqrt(2.0 * math.pi)))
    active = (upper * share).astype(BF16)
    d_active = product(grad_ref[...], down_weight[...], 1, 1)
    d_upper = (d_active * slope).astype(BF16)
    keep_ref[...] = jnp.where(is_down, active, d_upper)
    give_ref[...] = jnp.where(is_down, d_upper, active)
    bias_ref[...] = jnp.sum(d_upper.astype(F32), axis=0, keepdims=True)
    forward[...] += product(active, down_weight[...])
    back[...] += product(d_upper, up_weight[...], 1, 1)

    @pl.when(at == pl.num_programs(0) - 1)
    def _():
        forward_ref[...] = forward[...].astype(BF16)
        back_ref[...] = back[...].astype(BF16)


def mlp(
    table, block_input, out_grad, branches, output_bias, gain, shift, up_weight, up_bias, down_weight
):
    rows, model = block_input.shape
    units = up_weight.shape[1]
    step = math.gcd(units, 512)
    tile, line = whole_spec((rows, model)), whole_spec((1, model))
    wide = pl.BlockSpec((rows, step), lambda at, table: (0, at))
    bias = pl.BlockSpec((1, step), lambda at, table: (0, at))
    return pl.pallas_call(
        functools.partial(mlp_kernel, len(branches)),
        grid_spec=pltpu.PrefetchScalarGridSpec(
            num_scalar_prefetch=1,
            grid=(units // step,),
            in_specs=[tile] * (2 + len(branches))
            + [line] * 3
            + [
                pl.BlockSpec((model, step), lambda at, table: (0, at)),
                bias,
                pl.BlockSpec((step, model), lambda at, table: (at, 0)),
            ],
            out_specs=[wide, wide, tile, tile, tile, bias, tile, tile],
            scratch_shapes=[pltpu.VMEM((rows, model), BF16)]
            + [pltpu.VMEM((rows, model), F32)] * 2,
        ),
        out_shape=[struct((rows, units), BF16)] * 2
        + [struct((rows, model), BF16)] * 2
        + [
            struct((rows, model), F32),
            struct((1, units), F32),
            struct((rows, model), BF16),
            struct((rows, model), BF16),
        ],
        compiler_params=streaming,
        cost_estimate=light,
        name="mlp",
    )(
        table,
        block_input,
        out_grad,
        *branches,
        output_bias[None],
        gain[None],
        shift[None],
        up_weight,
        up_bias[None],
        down_weight,
    )


def middle_kernel(count, hidden_ref, grad_ref, *refs):
    parts, refs = refs[:count], refs[count:]
    gain, output_weight, d_hidden_ref, d_branch_ref, d_attn_ref, sums_ref = refs
    unit, inverse = normalize(hidden_ref[...])
    d_mlp = parts[0][...].astype(F32)
    for part in parts[1:]:
        d_mlp += part[...].astype(F32)
    grad = grad_ref[...].astype(F32)
    d_hidden = grad + normalize_back(d_mlp * gain[...], unit, inverse)
    d_hidden_ref[...] = d_hidden
    d_branch = d_hidden.astype(BF16)
    d_branch_ref[...] = d_branch
    d_attn_ref[...] = product(output_weight[...], d_branch, 1, 1).astype(BF16)
    for at, values in enumerate((d_hidden, d_mlp * unit, d_mlp, grad)):
        sums_ref[pl.ds(at, 1), :] = jnp.sum(values, axis=0, keepdims=True)


def middle(hidden, out_grad, parts, gain, output_weight):
    rows, model = hidden.shape
    width = output_weight.shape[0]
    return pl.pallas_call(
        functools.partial(middle_kernel, len(parts)),
        out_shape=[
            struct((rows, model), F32),
            struct((rows, model), BF16),
            struct((width, rows), BF16),
            struct((4, model), F32),
        ],
        compiler_params=streaming,
        cost_estimate=light,
        name="middle",
    )(hidden, out_grad, *parts, gain[None], output_weight)


def mask_rows(piece, chip, crops):
    crop = lax.broadcasted_iota(jnp.int32, (HD, piece.shape[2]), 0)
    segment = piece[chip, pl.ds(seg_row, 16), :].astype(F32)[:1].astype(jnp.int32)
    return jnp.where((crop != segment) & (crop < crops), masked_value, 0.0)


def load_keys(piece, crops, keys, key_t, value_n):
    chips, _, patches = piece.shape
    for chip in range(chips):
        key = piece[chip, pl.ds(HD, HD), :]
        value = piece[chip, pl.ds(2 * HD, HD), :]
        place = pl.ds(chip * patches, patches)
        both = jnp.concatenate([key.astype(F32), mask_rows(piece, chip, crops)], axis=0)
        keys[place, :] = both.T.astype(BF16)
        key_t[:, place] = key
        value_n[place, :] = value.astype(F32).T.astype(BF16)


def masked_query(query_ref, dtype=BF16):
    query = query_ref[0, pl.ds(0, HD), :].astype(F32) * 0.125
    segment = query_ref[0, pl.ds(seg_row, 16), :].astype(F32)[:1].astype(jnp.int32)
    crop = lax.broadcasted_iota(jnp.int32, query.shape, 0)
    onehot = jnp.where(crop == segment, 1.0, 0.0)
    return jnp.concatenate([query, onehot], axis=0).astype(dtype)


def forward_kernel(
    crops, step, query_ref, own, other, raw_ref, out_ref, logsum_ref, key_t, value_n, scores
):
    @pl.when(pl.program_id(0) == 0)
    def _():
        start = 0
        for piece in (own, other):
            chips, _, patches = piece.shape
            for chip in range(chips):
                place = pl.ds(start, patches)
                key = piece[chip, pl.ds(HD, HD), :].astype(F32)
                key_t[:, place] = jnp.concatenate([key, mask_rows(piece, chip, crops)], axis=0).astype(BF16)
                value = piece[chip, pl.ds(2 * HD, HD), :].astype(F32)
                value = jnp.concatenate([value, jnp.ones_like(value)], axis=0)
                value_n[place, :] = value.T.astype(BF16)
                start += patches

    query = masked_query(query_ref, F32).T.astype(BF16)
    count = query.shape[0]
    top = jnp.full((count, 128), masked_value, F32)
    for start in range(0, key_t.shape[1], step):
        block = product(query, key_t[:, pl.ds(start, step)])
        scores[:, pl.ds(start, step)] = block
        for at in range(0, step, 128):
            top = jnp.maximum(top, block[:, at : at + 128])
    top = jnp.max(top, axis=1, keepdims=True)
    accum = jnp.zeros((count, 2 * HD), F32)
    for start in range(0, key_t.shape[1], step):
        weights = jnp.exp(scores[:, pl.ds(start, step)] - top).astype(BF16)
        accum += product(weights, value_n[pl.ds(start, step), :])
    accum = accum.T
    total = accum[HD : HD + 1]
    raw = accum[:HD] / total
    raw_ref[0] = raw
    out_ref[0] = raw.astype(BF16)
    top = jnp.broadcast_to(top, (count, 128)).T[:1]
    logsum_ref[0] = top + jnp.log(total)


def backward_kernel(
    crops,
    extra,
    query_ref,
    grad_ref,
    raw_ref,
    logsum_ref,
    piece,
    *refs,
):
    extras, refs = refs[:extra], refs[extra:]
    outputs, (keys, key_t, value_n, sums) = refs[:-4], refs[-4:]
    group = pl.program_id(0)

    @pl.when(group == 0)
    def _():
        load_keys(piece, crops, keys, key_t, value_n)
        sums[...] = jnp.zeros_like(sums)

    query = masked_query(query_ref)
    grad = grad_ref[0]
    grad_wide = grad.astype(F32)
    delta = jnp.sum(grad_wide * raw_ref[0], axis=0, keepdims=True)
    scaled = query_ref[0, pl.ds(0, HD), :].astype(F32) * 0.125
    zero = jnp.zeros_like(scaled)
    query_side = jnp.concatenate([scaled, zero], axis=0).T.astype(BF16)
    grad_side = jnp.concatenate([zero, grad_wide], axis=0).T.astype(BF16)
    probs = jnp.exp(product(keys[...], query) - logsum_ref[0])
    dprobs = product(value_n[...], grad)
    dscores = (probs * (dprobs - delta)).astype(BF16)
    sums[...] += product(dscores, query_side) + product(probs.astype(BF16), grad_side)
    dquery = product(key_t[...], dscores) * 0.125
    if extras:
        dquery += extras[0][0]
    if len(outputs) == 1:
        outputs[0][group, pl.ds(0, HD), :] = dquery.astype(BF16)
    else:
        outputs[0][0] = dquery.astype(outputs[0].dtype)

    @pl.when(group == pl.num_programs(0) - 1)
    def _():
        chips, _, patches = piece.shape
        for chip in range(chips):
            total = sums[pl.ds(chip * patches, patches), :].T
            if extra > 1:
                total += extras[1][chip].astype(F32)
            total = total.astype(BF16)
            if len(outputs) == 1:
                outputs[0][chip, pl.ds(HD, 2 * HD), :] = total
            else:
                outputs[1][chip] = total


def key_step(count):
    return 1024 if count % 1024 == 0 else 256


def query_spec(rows, patches):
    return pl.BlockSpec((1, rows, patches), lambda group: (group, 0, 0))


def attention_forward(queries, own, other, crops):
    groups, _, patches = queries.shape
    count = 2 * own.shape[0] * own.shape[2]
    return pl.pallas_call(
        functools.partial(forward_kernel, crops, key_step(count)),
        grid=(groups,),
        in_specs=[
            query_spec(payload_rows, patches),
            whole_spec(own.shape),
            whole_spec(other.shape),
        ],
        out_specs=[query_spec(HD, patches), query_spec(HD, patches), query_spec(1, patches)],
        out_shape=[
            struct((groups, HD, patches), F32),
            struct((groups, HD, patches), BF16),
            struct((groups, 1, patches), F32),
        ],
        scratch_shapes=[
            pltpu.VMEM((2 * HD, count), BF16),
            pltpu.VMEM((count, 2 * HD), BF16),
            pltpu.VMEM((patches, count), F32),
        ],
        compiler_params=streaming,
        cost_estimate=light,
        name="attention_forward",
    )(queries, own, other)


def attention_backward(queries, grads, raw, logsum, keys, extras, crops):
    groups, _, patches = queries.shape
    chips, count = keys.shape[0], keys.shape[0] * keys.shape[2]
    sums_shape = (chips, 2 * HD, keys.shape[2])
    specs = [query_spec(HD, patches), whole_spec(sums_shape)]
    shapes = [
        struct((groups, HD, patches), BF16 if extras else F32),
        struct(sums_shape, BF16),
    ]
    outs = specs
    if extras and (groups, patches) == (chips, keys.shape[2]):
        shapes = [struct((chips, 3 * HD, patches), BF16)]
        outs = [whole_spec(shapes[0].shape)]
    return pl.pallas_call(
        functools.partial(backward_kernel, crops, len(extras)),
        grid=(groups,),
        in_specs=[
            query_spec(payload_rows, patches),
            query_spec(HD, patches),
            query_spec(HD, patches),
            query_spec(1, patches),
            whole_spec(keys.shape),
        ]
        + specs[: len(extras)],
        out_specs=outs,
        out_shape=shapes,
        scratch_shapes=[
            pltpu.VMEM((count, 2 * HD), BF16),
            pltpu.VMEM((HD, count), BF16),
            pltpu.VMEM((count, HD), BF16),
            pltpu.VMEM((count, 2 * HD), F32),
        ],
        compiler_params=params,
        cost_estimate=light,
        name="attention_backward",
    )(queries, grads, raw, logsum, keys, *extras)


def swap_cores(values):
    return lax.ppermute(values, "core", [(0, 1), (1, 0)])


def to_heads(blocks):
    return lax.all_to_all(blocks, "chip", 0, 0, tiled=True)


def scatter_queries(values, heads, split):
    rows, patches = values.shape[0] // heads, values.shape[1]
    if split == 1:
        return to_heads(values.reshape(heads, rows, patches))
    part = patches // split
    blocks = values.reshape(heads, rows, split, part).transpose(0, 2, 1, 3)
    moved = to_heads(blocks.reshape(heads * split, rows, part))
    width = min(256, moved.shape[0] * part)
    joined = moved.transpose(1, 0, 2).reshape(rows, -1, width)
    return joined.transpose(1, 0, 2)


def gather_queries(values, heads, split, patches):
    rows = values.shape[1]
    if split == 1:
        return to_heads(values).reshape(heads * rows, patches)
    part = patches // split
    joined = values.transpose(1, 0, 2).reshape(rows, heads * split, part)
    moved = to_heads(joined.transpose(1, 0, 2)).reshape(heads, split, rows, part)
    return moved.transpose(0, 2, 1, 3).reshape(heads * rows, patches)


def across_heads(part):
    if lax.axis_size("head") == 2:
        return [part, lax.ppermute(part, "head", [(0, 1), (1, 0)])]
    return [lax.psum(part, "head")]


def ring_pairs(direction):
    chips = lax.axis_size("chip")
    order = list(range(0, chips, 2)) + list(range(chips - 1, 0, -2))
    return [(order[at], order[(at + direction) % chips]) for at in range(chips)]


def ring_table():
    chips, chip = lax.axis_size("chip"), lax.axis_index("chip")
    place = jnp.where(chip % 2 == 0, chip // 2, chips - 1 - chip // 2)
    steps = jnp.arange(2 * chips + 2, dtype=jnp.int32)
    places = (place + steps) % chips
    there = jnp.where(places < chips // 2, 2 * places, 2 * (chips - 1 - places) + 1)
    table = jnp.where(steps < chips, places, there)
    table = jnp.where(steps == 2 * chips, lax.axis_index("core"), table)
    return jnp.where(steps == 2 * chips + 1, lax.axis_index("head"), table).astype(jnp.int32)


def visit(streams, values):
    states, values = lax.optimization_barrier(([stream.state for stream in streams], values))
    for stream, state in zip(streams, states):
        stream.advance(state)
    ready, values = lax.optimization_barrier(([stream.ready for stream in streams], values))
    for stream, blocks in zip(streams, ready):
        stream.send(blocks)
    return values


def pieces_of(block):
    return list(block) if isinstance(block, tuple) else [block]


def whole_block(block):
    return jnp.concatenate(pieces_of(block), axis=1)


def join_kernel(counts, *refs):
    output, refs, start = refs[-1], list(refs[:-1]), 0
    for count in counts:
        column = 0
        for _ in range(count):
            piece = refs.pop(0)
            rows, columns = piece.shape
            output[pl.ds(start, rows), pl.ds(column, columns)] = piece[...]
            column += columns
        start += rows


def join(blocks):
    blocks = [pieces_of(block) for block in blocks]
    rows = sum(block[0].shape[0] for block in blocks)
    columns = sum(piece.shape[1] for piece in blocks[0])
    return pl.pallas_call(
        functools.partial(join_kernel, [len(block) for block in blocks]),
        out_shape=struct((rows, columns), blocks[0][0].dtype),
        compiler_params=streaming,
        name="join",
    )(*[piece for block in blocks for piece in block])


def halves_kernel(left, right, left_ref, right_ref):
    left_ref[...] = left[...]
    right_ref[...] = right[...]


def halves(left, right):
    rows, columns = left.shape
    if rows % 16 or columns % 256:
        return [left[:, : columns // 2], right[:, columns // 2 :]]
    out = pl.BlockSpec((rows, columns // 2), lambda at: (0, 0))
    return pl.pallas_call(
        halves_kernel,
        grid=(1,),
        in_specs=[out, pl.BlockSpec((rows, columns // 2), lambda at: (0, 1))],
        out_specs=[out, out],
        out_shape=[struct((rows, columns // 2), left.dtype)] * 2,
        compiler_params=streaming,
        name="halves",
    )(left, right)


class Gather:
    def __init__(self, block, swap=False, take=None):
        self.reach, self.swap, self.take = lax.axis_size("chip") // 2, swap, take
        self.blocks, self.pairs, self.count = [], [], 0
        self.new, self.outputs = [0], []
        self.ready = [block]

    def send(self, ready):
        if len(self.new) < len(ready):
            ready = [tuple(ready)]
        new = list(zip(self.new, ready))
        self.blocks += new
        self.new = new
        self.count += 1
        sides = ready if len(ready) > 1 else ready * 2
        if self.count == self.reach:
            sides = halves(*sides)
        flying = []
        if self.count <= self.reach:
            flying = [
                lax.ppermute(block, "chip", ring_pairs(direction))
                for block, direction in zip(sides, (1, -1))
            ]
        if self.swap and ready:
            pairs = [(step, block, jax.tree.map(swap_cores, block)) for step, block in new]
            self.pairs += pairs
            self.outputs = self.take(self.outputs, pairs)
        self.state = (flying, self.outputs)

    def advance(self, state):
        arrived, self.outputs = state
        self.new = [-self.count, self.count]
        if self.count == self.reach:
            self.new = [self.count]
        self.ready = arrived

    def busy(self):
        return bool(self.state[0])


def add_kernel(wanted, count, _, *refs):
    outputs, refs = refs[-count:], list(refs[:-count])
    keep_in, far_in = refs.pop(0), refs.pop(0)
    at = pl.program_id(0)

    def put(output, total):
        output[...] = total.astype(BF16)

    for places, output in zip(wanted, outputs):
        near, far = refs.pop(0), refs.pop(0)
        total = product(near[...], keep_in[...], 0, 0) + product(far[...], far_in[...], 0, 0)
        arrived = [(place, refs.pop(0)) for place in places]
        if count > len(wanted):
            for place in range(count):
                pl.when(at == place)(functools.partial(put, outputs[place], total))
            return
        for place, part in arrived:
            if place is None:
                total += part[...].astype(F32)
        put(output, total)
        for place, part in arrived:
            if place is not None:
                pl.when(at == place)(lambda: put(output, total + part[...].astype(F32)))


def finish_kernel(counts, _, keep_in, far_in, near, far, ahead, behind, *refs):
    refs, output = list(refs[:-1]), refs[-1]
    total = product(near[...], keep_in[...], 0, 0) + product(far[...], far_in[...], 0, 0)
    total += ahead[...].astype(F32) + behind[...].astype(F32)
    start = total.shape[0]
    output[pl.ds(0, start), :] = total.astype(BF16)
    for count in counts:
        total = 0.0
        for _ in range(count):
            part = refs.pop(0)[...].astype(F32)
            total += part if part.ndim == 2 else jnp.sum(part, axis=0)
        output[pl.ds(start, total.shape[0]), :] = total.astype(BF16)
        start += total.shape[0]


class Reduce:
    def __init__(self, keep, far, keep_in, far_in, table):
        self.chips, self.table = lax.axis_size("chip"), table
        self.operands, self.sides = (keep, far), (keep_in, far_in)
        self.units = keep.shape[1] // self.chips
        self.tiled = self.units % 128 == 0
        self.left, self.rest = self.chips // 2, None
        blocks = self.add([(self.left, [])], True)
        self.send(blocks if len(blocks) > 1 else halves(blocks[0], blocks[0]))

    def send(self, ready):
        self.left -= 1
        self.state = [
            lax.ppermute(block, "chip", ring_pairs(direction))
            for block, direction in zip(ready, (1, -1))
        ]

    def advance(self, state):
        half = self.sides[0].shape[1] // 2
        ahead, behind = state
        places = (0, 1) if ahead.shape[1] == half else (None, None)
        self.ready = self.add(
            [(self.left, [(ahead, places[0])]), (-self.left, [(behind, places[1])])]
        )

    def arrive(self, values):
        self.state, values = lax.optimization_barrier((self.state, values))
        return values

    def finish(self, below):
        ahead, behind = self.state
        if not self.tiled:
            rows = self.add([(0, [(ahead, None), (behind, None)])])
            for parts in below:
                total = jnp.zeros(parts[0].shape[-2:], F32)
                for part in parts:
                    part = part.astype(F32)
                    total += part if part.ndim == 2 else jnp.sum(part, axis=0)
                rows.append(total.astype(BF16))
            return jnp.concatenate(rows, axis=0)
        (rows, model), units, chips = self.sides[0].shape, self.units, self.chips
        half = model // 2
        arrays = [ahead, behind] + [part for parts in below for part in parts]
        specs = [pl.BlockSpec((rows, half), lambda at, table: (0, at))] * 2
        specs += [pl.BlockSpec((rows, units), lambda at, table: (0, table[0]))] * 2
        for array in arrays:
            shape = array.shape[:-1] + (half,)
            specs.append(
                pl.BlockSpec(shape, lambda at, table, rank=array.ndim: (0,) * (rank - 1) + (at,))
            )
        height = units + sum(parts[0].shape[-2] for parts in below)
        return pl.pallas_call(
            functools.partial(finish_kernel, [len(parts) for parts in below]),
            grid_spec=pltpu.PrefetchScalarGridSpec(
                num_scalar_prefetch=1,
                grid=(2,),
                in_specs=specs,
                out_specs=pl.BlockSpec((height, half), lambda at, table: (0, at)),
            ),
            out_shape=struct((height, model), BF16),
            compiler_params=streaming,
            cost_estimate=light,
            name="ring_finish",
        )(self.table, *self.sides, *self.operands, *arrays)

    def add(self, wanted, split=False):
        (rows, model), units, chips = self.sides[0].shape, self.units, self.chips
        if not self.tiled:
            sums = []
            for step, parts in wanted:
                start = self.table[step % chips] * units
                total = jnp.zeros((units, model), F32)
                for operand, side in zip(self.operands, self.sides):
                    block = lax.dynamic_slice_in_dim(operand, start, units, 1)
                    total += product(block, side, 0, 0)
                for part, place in parts:
                    start = (place or 0) * part.shape[1]
                    total = total.at[:, start : start + part.shape[1]].add(part.astype(F32))
                sums.append(total.astype(BF16))
            return sums
        half = model // 2
        side = pl.BlockSpec((rows, half), lambda at, table: (0, at))
        whole = pl.BlockSpec((units, half), lambda at, table: (0, at))
        fixed = pl.BlockSpec((units, half), lambda at, table: (0, 0))
        specs, arrays = [side] * 2, list(self.sides)
        for step, parts in wanted:
            block = pl.BlockSpec(
                (rows, units), lambda at, table, step=step % chips: (0, table[step])
            )
            specs += [block] * 2 + [whole if place is None else fixed for _, place in parts]
            arrays += list(self.operands) + [part for part, _ in parts]
        places = [[place for _, place in parts] for _, parts in wanted]
        shapes, outs = [struct((units, model), BF16)] * len(wanted), [whole] * len(wanted)
        if split:
            shapes, outs = [struct((units, half), BF16)] * 2, [fixed] * 2
        return pl.pallas_call(
            functools.partial(add_kernel, places, len(shapes)),
            grid_spec=pltpu.PrefetchScalarGridSpec(
                num_scalar_prefetch=1,
                grid=(2,),
                in_specs=specs,
                out_specs=outs,
            ),
            out_shape=shapes,
            compiler_params=streaming,
            cost_estimate=light,
            name="ring_add",
        )(self.table, *arrays)

    def place(self, outputs, pairs):
        units, chips, model = self.units, self.chips, self.sides[0].shape[1]
        size, extra = self.size, self.extra
        shapes = [struct((chips * units, model), F32), struct((model, chips * units), F32)]
        if not self.tiled:
            outputs = outputs or [jnp.zeros(shape.shape, F32) for shape in shapes]
            down, up = outputs
            is_down = self.table[2 * chips] == 0
            for step, near, far in pairs:
                start = self.table[step % chips] * units
                near, far = whole_block(near)[:units], whole_block(far)[:units]
                first = jnp.where(is_down, near, far).astype(F32)
                second = jnp.where(is_down, far, near).astype(F32).T
                down = lax.dynamic_update_slice_in_dim(down, first, start, 0)
                up = lax.dynamic_update_slice_in_dim(up, second, start, 1)
            return [down, up]
        first = pairs[0][0] % chips
        stride = pairs[-1][0] % chips - first
        blocks = [pieces_of(pair[1]) + pieces_of(pair[2]) for pair in pairs]
        flat = [piece for block in blocks for piece in block]

        def place(at, table):
            return table[first + at * stride]

        def chip(at, table):
            return table[chips + first + at * stride]

        column = pl.BlockSpec(
            (model, 2 * HD), lambda at, table: (0, lax.div(chip(at, table), 2))
        )
        columns = [column] * (3 if outputs else 0)
        heads = [[first, first + stride][at] + chips for at in range(len(pairs))]
        return pl.pallas_call(
            functools.partial(place_kernel, heads, len(blocks[0]) // 2, (units, size, extra)),
            grid_spec=pltpu.PrefetchScalarGridSpec(
                num_scalar_prefetch=1,
                grid=(len(pairs),),
                in_specs=[pl.BlockSpec(memory_space=pl.ANY)] * (len(outputs) - len(columns))
                + columns
                + [pl.BlockSpec(piece.shape, lambda at, table: (0, 0)) for piece in flat],
                out_specs=[
                    pl.BlockSpec((units, model), lambda at, table: (place(at, table), 0)),
                    pl.BlockSpec((model, units), lambda at, table: (0, place(at, table))),
                    pl.BlockSpec((2, 1, extra, model), lambda at, table: (0, chip(at, table), 0, 0)),
                    pl.BlockSpec(
                        (1, 2, small_rows, model), lambda at, table: (chip(at, table), 0, 0, 0)
                    ),
                ]
                + [column] * 3,
            ),
            out_shape=shapes
            + [
                struct((2, chips, extra, model), F32),
                struct((chips, 2, small_rows, model), F32),
            ]
            + [struct((model, chips * HD), F32)] * 3,
            input_output_aliases={1 + at: at for at in range(len(outputs))},
            compiler_params=streaming,
            cost_estimate=light,
            name="place",
        )(self.table, *outputs, *flat)


def place_kernel(heads, width, sizes, table, *refs):
    count = len(heads)
    refs, (down, up, weight, small), projections = refs[:-7], refs[-7:-3], refs[-3:]
    blocks, refs = refs[-2 * width * count :], refs[: -2 * width * count]
    core = table[table.shape[0] - 2]
    units, size, extra = sizes
    rows = [pl.ds(0, units), pl.ds(units, size), pl.ds(units + size, extra)]
    rows.append(pl.ds(units + size + extra, small_rows))

    def read(block, which):
        return jnp.concatenate([piece[rows[which], :] for piece in block], axis=1)

    def put(first, second, head):
        down[...] = read(first, 0).astype(F32)
        up[...] = read(second, 0).astype(F32).T
        for side, block in ((0, first), (1, second)):
            weight[side, 0] = read(block, 2).astype(F32)
            small[0, side] = read(block, 3).astype(F32)
        both = jnp.concatenate([read(first, 1), read(second, 1)], axis=0)
        for at, output in enumerate(projections):
            part = both[at * HD : at * HD + HD].astype(F32)
            part = jnp.concatenate([part, part], axis=0).T
            if refs:
                mine = lax.broadcasted_iota(jnp.int32, part.shape, 1) // HD == head % 2
                part = jnp.where(mine, part, refs[at - 3][...])
            output[...] = part

    for at in range(count):
        near, far = (
            blocks[(2 * at + side) * width : (2 * at + side + 1) * width] for side in range(2)
        )
        head = table[heads[at]]
        here = pl.program_id(0) == at
        pl.when(here & (core == 0))(functools.partial(put, near, far, head))
        pl.when(here & (core != 0))(functools.partial(put, far, near, head))


def head_gradient_kernel(steps, chips, table, grads_ref, *refs):
    parts, out_ref = refs[:-1], refs[-1]
    for at, part in enumerate(parts):

        @pl.when(pl.program_id(0) == at)
        def _(part=part):
            chosen = [grads_ref[table[chips + step % chips]] for step in steps]
            total = product(jnp.concatenate(chosen, axis=1), part[...])
            out_ref[...] = total.astype(BF16)


def head_gradient(grads, parts, steps, table):
    chips, rows, _ = grads.shape
    columns = parts[0].shape[1]

    def column(at, table):
        mine = table[2 * chips + 1] if len(parts) > 1 else 0
        return (0, jnp.where(at == 0, mine, 1 - mine))

    return pl.pallas_call(
        functools.partial(head_gradient_kernel, steps, chips),
        grid_spec=pltpu.PrefetchScalarGridSpec(
            num_scalar_prefetch=1,
            grid=(len(parts),),
            in_specs=[
                pl.BlockSpec(array.shape, lambda at, table, rank=array.ndim: (0,) * rank)
                for array in (grads, *parts)
            ],
            out_specs=pl.BlockSpec((rows, columns), column),
        ),
        out_shape=struct((rows, columns * len(parts)), BF16),
        compiler_params=streaming,
        cost_estimate=light,
        name="head_gradient",
    )(table, grads, *parts)


def core_half(values, axis, side):
    size = values.shape[axis] // 2
    return lax.dynamic_slice_in_dim(values, side * size, size, axis)


def share_halves(values, axis):
    core = lax.axis_index("core")
    return core_half(values, axis, core), swap_cores(core_half(values, axis, 1 - core))


def local(
    block_input,
    out_grad,
    segments,
    lead_steps,
    gain_attn,
    shift_attn,
    lead_weight,
    query_weight,
    key_weight,
    value_weight,
    output_weight,
    output_bias,
    gain_mlp,
    shift_mlp,
    up_weight,
    up_bias,
    down_weight,
    down_bias,
):
    rows, model = block_input.shape
    heads = query_weight.shape[1] // HD
    width = heads * HD
    chips, core = lax.axis_size("chip"), lax.axis_index("core")
    split = chips // heads
    crops = lead_steps.shape[0]
    table = ring_table()
    weights = (query_weight, key_weight, value_weight)
    cut = model // 2 if lax.axis_size("head") == 2 else model
    payload, attn_in, attn_in_cut = project(
        table, cut, block_input, segments, lead_steps, gain_attn, shift_attn, lead_weight, weights
    )
    if split == 1:
        own = to_heads(payload)
        queries = own
    else:
        queries = scatter_queries(payload.reshape(-1, rows), heads, split)
        own = to_heads(jnp.repeat(payload, split, axis=0))
    own, attn_in_cut = lax.optimization_barrier((own, attn_in_cut))
    inputs = Gather(attn_in_cut)
    inputs.send(inputs.ready)
    other = swap_cores(own)
    raw, out, logsum = attention_forward(queries, own, other, crops)
    inputs.state, out = lax.optimization_barrier((inputs.state, out))
    attn_out = gather_queries(out, heads, split, rows)
    attn_out = visit([inputs], attn_out)
    branches = across_heads(product(attn_out, output_weight, 0, 0).astype(BF16))
    wide = block_input.astype(F32)
    mean_attn = jnp.mean(wide, axis=-1, keepdims=True)
    centred = wide - mean_attn
    inverse_attn = lax.rsqrt(jnp.mean(centred * centred, axis=-1, keepdims=True) + eps)
    mean_attn, inverse_attn = visit([inputs], (mean_attn, inverse_attn))
    keep, give, keep_in, give_in, hidden, dup_bias, mlp_part, d_mlp_part = mlp(
        table,
        block_input,
        out_grad,
        branches,
        output_bias,
        gain_mlp,
        shift_mlp,
        up_weight,
        up_bias,
        down_weight,
    )
    keep, give, keep_in, give_in, d_mlp_part = visit(
        [inputs], (keep, give, keep_in, give_in, d_mlp_part)
    )
    d_mlp = across_heads(d_mlp_part)
    ring = Reduce(keep, swap_cores(give), keep_in, swap_cores(give_in), table)
    mlp_part, d_mlp = lax.optimization_barrier((mlp_part, d_mlp))
    d_hidden, d_branch, d_attn, sums = middle(hidden, out_grad, d_mlp, gain_mlp, output_weight)
    d_branch, mlp_part = visit([ring, inputs], (d_branch, mlp_part))
    while inputs.busy():
        visit([inputs], ())
    mlp_out = across_heads(mlp_part)
    out_near, out_far = share_halves(attn_out, 0)
    d_attn, d_branch_far = lax.optimization_barrier((d_attn, swap_cores(d_branch)))
    grads = scatter_queries(d_attn, heads, split)
    doutput = product(out_near, d_branch) + product(out_far, d_branch_far)
    doutput = doutput.astype(BF16).reshape(chips, -1, model)
    steps, inputs = zip(*inputs.blocks)
    inputs = join(inputs)
    parts = across_heads(inputs) if cut != model else [inputs]
    doutput = visit([ring], doutput)
    doutput = to_heads(doutput)
    dquery, far_sums = attention_backward(queries, grads, raw, logsum, other, [], crops)
    far_sums = swap_cores(far_sums)
    grads, dquery = visit([ring], (grads, dquery))
    head_grads = attention_backward(
        queries, grads, raw, logsum, own, [dquery, far_sums], crops
    )
    head_grads = ring.arrive(head_grads)
    doutput, head_grads = lax.optimization_barrier((doutput, head_grads))
    small = jnp.concatenate([sums.reshape(-1), dup_bias[0]])
    small = jnp.pad(small, (0, small_rows * model - small.shape[0])).reshape(small_rows, model)
    below = [[doutput], [small]]
    if split == 1:
        (head_grads,) = head_grads
        moved = to_heads(head_grads)
        projections = head_gradient(head_grads, parts, steps, table)
        near, far = share_halves(projections, 0)
        size, below = near.shape[0], [[near, far]] + below
        dquery, dkey, dvalue = (
            moved[:, at * HD : at * HD + HD].reshape(width, rows) for at in range(3)
        )
    else:
        dquery, key_value = head_grads
        dquery = gather_queries(dquery, heads, split, rows)
        moved = to_heads(key_value).reshape(heads, split, 2 * HD, rows).astype(F32)
        moved = jnp.sum(moved, axis=1).astype(BF16)
        dkey, dvalue = (moved[:, at * HD : at * HD + HD].reshape(width, rows) for at in range(2))
        size = 0
        projections = [
            lax.psum(product(attn_in, grad, 0, 1).astype(BF16), ("chip", "core")).astype(F32)
            for grad in (dquery, dkey, dvalue)
        ]
    start, ring.size, ring.extra = ring.units, size, doutput.shape[1]
    gathered = Gather(ring.finish(below), True, ring.place)
    gathered.send(gathered.ready)
    d_part = (
        product(dquery, query_weight, 0, 1)
        + product(dkey, key_weight, 0, 1)
        + product(dvalue, value_weight, 0, 1)
    )
    d_in = across_heads(d_part.astype(BF16))
    unit_attn = (block_input.astype(F32) - mean_attn) * inverse_attn
    onehot = (segments[:, None] == jnp.arange(crops, dtype=jnp.int32)[None, :]).astype(F32)
    lead = jnp.sum(onehot * lead_steps.astype(F32)[None, :], axis=1) / 12.0
    ends = jnp.stack(
        [
            jnp.sum(d_part * unit_attn, axis=0),
            jnp.sum(d_part, axis=0),
            jnp.sum(lead[:, None] * d_part, axis=0),
        ]
    )
    ends = ends.reshape(-1, 128)
    ends = functools.reduce(jnp.add, across_heads(ends))
    ends = ends + swap_cores(ends)
    moves = [chips >> (at + 1) for at in range(chips.bit_length() - 1)]

    def step_ends(ends):
        if not moves:
            return [ends]
        reach = moves.pop(0)
        pairs = [(chip, chip ^ reach) for chip in range(chips)]
        return [ends, lax.ppermute(ends, "chip", pairs)]

    ends = step_ends(visit([gathered], ends))
    ends, mlp_out = visit([gathered], (ends, mlp_out))
    ends = step_ends(functools.reduce(jnp.add, ends))
    block_output = hidden + down_bias
    for part in mlp_out:
        block_output += part.astype(F32)
    block_output = block_output.astype(BF16)
    d_in, block_output, ends = visit([gathered], (d_in, block_output, ends))
    ends = step_ends(functools.reduce(jnp.add, ends))
    d_in = functools.reduce(jnp.add, (part.astype(F32) for part in d_in))
    input_grad = (d_hidden + normalize_back(d_in * gain_attn, unit_attn, inverse_attn)).astype(
        BF16
    )
    while gathered.busy() or moves:
        input_grad, ends = visit([gathered], (input_grad, ends))
        ends = step_ends(functools.reduce(jnp.add, ends))
    ends = functools.reduce(jnp.add, ends).reshape(3, model)
    ddown_weight, dup_weight, *rest = gathered.outputs
    if split == 1:
        doutput_weight, small, *projections = rest
        doutput_weight = doutput_weight.reshape(width, model)
    if split != 1:
        blocks = jnp.zeros((2, chips, ring.extra + small_rows, model), F32)
        for step, near, far in gathered.pairs:
            for side, block in ((core, near), (1 - core, far)):
                at = (side, table[chips + step % chips], 0, 0)
                block = whole_block(block)[None, None, start:].astype(F32)
                blocks = lax.dynamic_update_slice(blocks, block, at)
        doutput_weight = blocks[:, :, :-small_rows].reshape(width, model)
        small = blocks[:, :, -small_rows:]
    small = jnp.sum(small, axis=(0, 1))
    dup_bias = small[4:].reshape(-1)[: dup_bias.shape[1]]
    return (
        block_output,
        input_grad,
        ends[0],
        ends[1],
        ends[2],
        *projections,
        doutput_weight,
        *small[:3],
        dup_weight,
        dup_bias,
        ddown_weight,
        small[3],
    )


def solution(mesh):
    bands, halves = mesh.shape["band"], mesh.shape["head"]
    inner = Mesh(mesh.devices.reshape(bands // 2, 2, halves), ("chip", "core", "head"))
    band = ("chip", "core")
    rows, columns, split_rows = P(band, None), P(None, "head"), P("head", None)
    return jax.shard_map(
        local,
        mesh=inner,
        in_specs=(
            rows,
            rows,
            P(band),
            P(),
            P(),
            P(),
            P(),
            columns,
            columns,
            columns,
            split_rows,
            P(),
            P(),
            P(),
            columns,
            P("head"),
            split_rows,
            P(),
        ),
        out_specs=(
            rows,
            rows,
            P(),
            P(),
            P(),
            columns,
            columns,
            columns,
            split_rows,
            P(),
            P(),
            P(),
            columns,
            P("head"),
            split_rows,
            P(),
        ),
        check_vma=False,
    )
```
